32 devices in a mesh: dp: 16 (over z, x, core), seq: 2 (over y).
Axes of the slice: x: 2, y: 2, z: 4, core: 2. Of those that a mesh axis runs over, the one named last changes fastest.
Arguments:
- tokens: bfloat16 [32, 512, 1024], P('dp', 'seq'), may hold values from -6 to 6
- lengths: int32 [32], P('dp'), may hold values from 128 to 512, as said below
- cotangent: bfloat16 [32, 512, 1024], P('dp', 'seq'), may hold values from -6 to 6
- query_weight: bfloat16 [1024, 1024], P('dp', 'seq'), may hold values from -0.1875 to 0.1875
- key_weight: bfloat16 [1024, 1024], P('dp', 'seq'), may hold values from -0.1875 to 0.1875
- value_weight: bfloat16 [1024, 1024], P('dp', 'seq'), may hold values from -0.1875 to 0.1875
- out_weight: bfloat16 [1024, 1024], P('dp', 'seq'), may hold values from -1 to 1
- up_weight: bfloat16 [1024, 4096], P('dp', 'seq'), may hold values from -0.1875 to 0.1875
- down_weight: bfloat16 [4096, 1024], P('dp', 'seq'), may hold values from -0.09375 to 0.09375
- query_bias: float32 [1024], replicated, may hold values from -1.75 to 1.75
- value_bias: float32 [1024], replicated, may hold values from -0.625 to 0.625
- out_bias: float32 [1024], replicated, may hold values from -1.25 to 1.25
- attn_gain: float32 [1024], replicated, may hold values from 0.5 to 1.5
- attn_shift: float32 [1024], replicated, may hold values from -1.25 to 1.25
- up_bias: float32 [4096], replicated, may hold values from -1.75 to 1.75
- down_bias: float32 [1024], replicated, may hold values from -1.25 to 1.25
- feed_gain: float32 [1024], replicated, may hold values from 0.5 to 1.5
- feed_shift: float32 [1024], replicated, may hold values from -1.25 to 1.25
Outputs:
- mixed: bfloat16 [32, 512, 1024], P('dp', 'seq')
- tokens_grad: bfloat16 [32, 512, 1024], P('dp', 'seq')
- query_weight_grad: float32 [1024, 1024], P('dp', 'seq')
- key_weight_grad: float32 [1024, 1024], P('dp', 'seq')
- value_weight_grad: float32 [1024, 1024], P('dp', 'seq')
- out_weight_grad: float32 [1024, 1024], P('dp', 'seq')
- up_weight_grad: float32 [1024, 4096], P('dp', 'seq')
- down_weight_grad: float32 [4096, 1024], P('dp', 'seq')
- query_bias_grad: float32 [1024], replicated
- value_bias_gradient: float32 [1024], replicated
- out_bias_grad: float32 [1024], replicated
- attn_gain_grad: float32 [1024], replicated
- attn_shift_grad: float32 [1024], replicated
- up_bias_grad: float32 [4096], replicated
- down_bias_grad: float32 [1024], replicated
- feed_gain_grad: float32 [1024], replicated
- feed_shift_grad: float32 [1024], replicated
- stream_rms: float32 [3], replicated
The draws below stay inside these ranges and needn't reach their ends.
Inputs may be any that keep to these rules, and one draw needn't show every extreme that they name: `lengths`: in each block of 2 sequences held by one index of dp, at least one has length 512.
All inputs are finite; a program needn't handle non-finite values.
Results may differ from the reference program's by a relative error of at most 0.02.
Values may be sent and summed in bfloat16 or wider, within the bound.
No kernel may reach another device: no remote copies, remote signals or barrier semaphores. Data moves between devices by JAX's collectives and lax.ppermute only.
A program may use at most 192 MiB of HBM per device.

```python
import math
import jax
import jax.numpy as jnp
from jax import lax

D = 1024
HEADS = 16
HD = 64
FF = 4096
SEQS = 2
LEN = 512
SEQ_ALL = 32


def draw_lengths(key, part):
    key = jax.random.fold_in(key, 7)
    first_key, second_key = jax.random.split(key)
    group_count = SEQ_ALL // SEQS
    drawn = jax.random.randint(first_key, (group_count, SEQS), LEN // 4, LEN + 1)
    chosen = jax.random.randint(second_key, (group_count,), 0, SEQS)
    places = jnp.arange(SEQS)[None, :]
    drawn = jnp.where(places == chosen[:, None], LEN, drawn)
    shortest = jnp.logical_and(places == (chosen[:, None] + 1) % SEQS, jnp.arange(group_count)[:, None] == 0)
    drawn = jnp.where(shortest, LEN // 4, drawn)
    return drawn.reshape(SEQ_ALL).astype(jnp.int32)


def with_spikes(entries, rng, source, target, parts, factor):
    def block_of(dim):
        return (jnp.arange(entries.shape[dim]) // (entries.shape[dim] // parts)).reshape((-1,) + (1,) * (entries.ndim - 1 - dim))

    first = jax.random.permutation(rng, parts)[block_of(target)]
    other_side = (block_of(target) + parts // 2) % parts
    return jnp.where((block_of(source) == first) | (block_of(source) == other_side), factor * entries, entries)


def level_of(key, dims, pieces, least, top_value):
    factor_of = 1.0
    for axis_at, shards_of in pieces:
        heights = jax.random.uniform(jax.random.fold_in(jax.random.fold_in(key, 6), axis_at), (shards_of,), jnp.float32, least / len(pieces), top_value / len(pieces))
        factor_of = factor_of * jnp.repeat(jnp.exp(heights), dims[axis_at] // shards_of).reshape((-1,) + (1,) * (len(dims) - 1 - axis_at))
    return factor_of


def gaussian(key, dims, spread, reach, shards=(), kind=jnp.bfloat16):
    factor_of = level_of(key, dims, shards, -0.22, 0.18) if shards else 1.0
    values = jax.random.normal(key, dims, jnp.float32) * spread * factor_of
    return jnp.minimum(jnp.maximum(values, -reach), reach).astype(kind)


def bell_draw_with(rng, extent, deviation, reach, cuts, heavy, dtype=jnp.bfloat16):
    array = deviation * jax.random.normal(rng, extent, jnp.float32)
    if cuts:
        array = array * level_of(rng, extent, cuts, -0.22, 0.18)
    return jnp.clip(with_spikes(array, jax.random.fold_in(rng, 3), *heavy), -reach, reach).astype(dtype)


def setup_inputs(seed: int = 0) -> dict:
    splits = jax.random.split(jax.random.key(seed), 19)
    tokens = bell_draw_with(splits[0], (SEQ_ALL, LEN, D), 1.0, 6.0, ((0, 16), (1, 2)), (0, 2, 16, 2.0))
    lengths = draw_lengths(jax.random.fold_in(splits[18], 71), 0)
    cotangent = bell_draw_with(splits[2], (SEQ_ALL, LEN, D), 1.0, 6.0, ((0, 16), (1, 2)), (0, 2, 16, 2.0))
    query_weight = gaussian(splits[3], (D, D), D ** -0.5, 0.1875, ((0, 16), (1, 2)))
    key_weight = gaussian(splits[4], (D, D), D ** -0.5, 0.1875, ((0, 16), (1, 2)))
    value_weight = gaussian(splits[5], (D, D), D ** -0.5, 0.1875, ((0, 16), (1, 2)))
    out_weight = gaussian(splits[6], (D, D), (D // 32) ** -0.5, 1.0, ((0, 16), (1, 2)))
    up_weight = gaussian(splits[7], (D, FF), D ** -0.5, 0.1875, ((0, 16), (1, 2)))
    down_weight = gaussian(splits[8], (FF, D), FF ** -0.5, 0.09375, ((0, 16), (1, 2)))
    query_bias = gaussian(splits[9], (D,), 0.3, 1.75, (), jnp.float32)
    value_bias = gaussian(splits[10], (D,), 0.1, 0.625, (), jnp.float32)
    out_bias = gaussian(splits[11], (D,), 0.2, 1.25, (), jnp.float32)
    attn_gain = jnp.clip(1.0 + 0.1 * jax.random.normal(splits[12], (D,), jnp.float32), 0.5, 1.5)
    attn_shift = gaussian(splits[13], (D,), 0.2, 1.25, (), jnp.float32)
    up_bias = gaussian(splits[14], (FF,), 0.3, 1.75, (), jnp.float32)
    down_bias = gaussian(splits[15], (D,), 0.2, 1.25, (), jnp.float32)
    feed_gain = jnp.clip(1.0 + 0.1 * jax.random.normal(splits[16], (D,), jnp.float32), 0.5, 1.5)
    feed_shift = gaussian(splits[17], (D,), 0.2, 1.25, (), jnp.float32)
    return {"tokens": tokens, "lengths": lengths, "cotangent": cotangent, "query_weight": query_weight, "key_weight": key_weight, "value_weight": value_weight, "out_weight": out_weight, "up_weight": up_weight, "down_weight": down_weight, "query_bias": query_bias, "value_bias": value_bias, "out_bias": out_bias, "attn_gain": attn_gain, "attn_shift": attn_shift, "up_bias": up_bias, "down_bias": down_bias, "feed_gain": feed_gain, "feed_shift": feed_shift}


@jax.custom_vjp
def low(v):
    return lax.optimization_barrier(v.astype(jnp.bfloat16)).astype(jnp.float32)

@jax.custom_vjp
def low_back(v):
    return v

def low_keep(v):
    return (low(v), None)

def low_pass(kept, grad):
    return (grad,)

def back_keep(v):
    return (v, None)

def back_low(kept, grad):
    return (low(grad),)
low.defvjp(low_keep, low_pass)
low_back.defvjp(back_keep, back_low)

def layer_norm(values_in, gain_vector, shift_vector):
    mean_value = lax.optimization_barrier(jnp.mean(values_in, axis=-1, keepdims=True))
    centered = values_in - mean_value
    variance = lax.optimization_barrier(jnp.mean(centered * centered, axis=-1, keepdims=True))
    return centered * lax.rsqrt(variance + 1e-05) * gain_vector + shift_vector

def product(left_operand, right_operand):
    return jnp.einsum('yif,fa->yia', left_operand, right_operand, precision=lax.Precision.HIGHEST)

def block_forward(inputs, params, seq_lengths):
    query_weight, key_weight, value_weight, out_weight, up_weight, down_weight, query_bias, value_bias, out_bias, attn_gain, attn_shift, up_bias, down_bias, feed_gain, feed_shift = params
    seq_count, slot_count, feature_total = inputs.shape
    queries = low(low_back(product(inputs, query_weight) + query_bias)).reshape(seq_count, slot_count, HEADS, HD)
    key_rows = low(low_back(product(inputs, key_weight))).reshape(seq_count, slot_count, HEADS, HD)
    value_rows = low(low_back(product(inputs, value_weight) + value_bias)).reshape(seq_count, slot_count, HEADS, HD)
    scores = low_back(jnp.einsum('sqhd,skhd->shqk', queries, key_rows, precision=lax.Precision.HIGHEST) * 0.125)
    key_valid = jnp.arange(slot_count)[None, :] < seq_lengths[:, None]
    scores = jnp.where(key_valid[:, None, None, :], scores, -1e+30)
    shifted = scores - lax.optimization_barrier(jnp.max(scores, axis=-1, keepdims=True))
    exponent = jnp.exp(shifted)
    soft_probs = low(exponent / lax.optimization_barrier(jnp.sum(exponent, axis=-1, keepdims=True)))
    heads_out = jnp.einsum('shqk,skhd->sqhd', soft_probs, value_rows, precision=lax.Precision.HIGHEST)
    heads_out = low(low_back(heads_out.reshape(seq_count, slot_count, feature_total)))
    attention_out = low_back(product(heads_out, out_weight) + out_bias)
    hidden = layer_norm(inputs + attention_out, attn_gain, attn_shift)
    pre_act = low_back(product(low(hidden), up_weight) + up_bias)
    activation = low(low_back(jax.nn.gelu(pre_act, approximate=False)))
    feed_out = low_back(product(activation, down_weight) + down_bias)
    result = layer_norm(hidden + feed_out, feed_gain, feed_shift)
    return (result, (attention_out, feed_out))

def reference(tokens, lengths, cotangent, query_weight, key_weight, value_weight, out_weight, up_weight, down_weight, query_bias, value_bias, out_bias, attn_gain, attn_shift, up_bias, down_bias, feed_gain, feed_shift):
    group_length = math.gcd(SEQ_ALL, max(1, 4096 // LEN))
    step_count = SEQ_ALL // group_length
    matrices = tuple((weight.astype(jnp.float32) for weight in (query_weight, key_weight, value_weight, out_weight, up_weight, down_weight)))
    params = matrices + (query_bias, value_bias, out_bias, attn_gain, attn_shift, up_bias, down_bias, feed_gain, feed_shift)
    token_groups = tokens.reshape(step_count, group_length, LEN, D)
    cotangent_groups = cotangent.reshape(step_count, group_length, LEN, D)
    length_groups = lengths.reshape(step_count, group_length)

    def run_group(carry, inputs):
        gradients, statistics = carry
        token_part, cotangent_part, length_part = inputs
        tokens_f32 = token_part.astype(jnp.float32)

        def forward(inputs_f32, weights):
            return block_forward(inputs_f32, weights, length_part)
        result, pull_back, branches = jax.vjp(forward, tokens_f32, params, has_aux=True)
        valid_rows = (jnp.arange(LEN)[None, :] < length_part[:, None]).astype(jnp.float32)[..., None]
        input_grad, param_grads = pull_back(cotangent_part.astype(jnp.float32) * valid_rows)
        attention_out, feed_out = branches
        statistics = statistics + jnp.stack([jnp.sum(valid_rows * tokens_f32 * tokens_f32), jnp.sum(valid_rows * attention_out * attention_out), jnp.sum(valid_rows * feed_out * feed_out), jnp.sum(valid_rows) * D])
        gradients = jax.tree.map(lambda first, second: first + second, gradients, param_grads)
        return ((gradients, statistics), (result.astype(jnp.bfloat16), input_grad.astype(jnp.bfloat16)))
    zero_grads = jax.tree.map(jnp.zeros_like, params)
    (gradients, statistics), (results, input_grads) = lax.scan(run_group, (zero_grads, jnp.zeros((4,), jnp.float32)), (token_groups, cotangent_groups, length_groups))
    stream_rms = jnp.sqrt(statistics[:3] / statistics[3])
    return (results.reshape(SEQ_ALL, LEN, D), input_grads.reshape(SEQ_ALL, LEN, D), gradients[0], gradients[1], gradients[2], gradients[3], gradients[4], gradients[5], gradients[6], gradients[7], gradients[8], gradients[9], gradients[10], gradients[11], gradients[12], gradients[13], gradients[14], stream_rms)
```

```python
from functools import partial
import math

import jax
import jax.numpy as jnp
from jax import lax
from jax.sharding import PartitionSpec as P

HD = 64


def layer_norm(values_in, gain_vector, shift_vector):
    mean_value = jnp.mean(values_in, axis=-1, keepdims=True)
    centered = values_in - mean_value
    variance = jnp.mean(centered * centered, axis=-1, keepdims=True)
    return centered * lax.rsqrt(variance + 1e-05) * gain_vector + shift_vector


def gather_weights(first, second, third, fourth, fifth, sixth):
    part = (
        lax.all_gather(first, "dp", axis=0, tiled=True),
        lax.all_gather(second, "dp", axis=0, tiled=True),
        lax.all_gather(third, "dp", axis=0, tiled=True),
        lax.all_gather(fourth, "dp", axis=0, tiled=True),
        lax.all_gather(fifth, "dp", axis=0, tiled=True),
        lax.all_gather(sixth, "dp", axis=0, tiled=True),
    )
    return (
        lax.all_gather(part[0], "seq", axis=1, tiled=True),
        lax.all_gather(part[1], "seq", axis=1, tiled=True),
        lax.all_gather(part[2], "seq", axis=1, tiled=True),
        lax.all_gather(part[3], "seq", axis=1, tiled=True),
        lax.all_gather(part[4], "seq", axis=1, tiled=True),
        lax.all_gather(part[5], "seq", axis=1, tiled=True),
    )


def reduce_grads(first, second, third, fourth, fifth, sixth):
    part = (
        lax.psum_scatter(first.astype(jnp.bfloat16), "seq", scatter_dimension=1, tiled=True).astype(
            jnp.float32
        ),
        lax.psum_scatter(
            second.astype(jnp.bfloat16), "seq", scatter_dimension=1, tiled=True
        ).astype(jnp.float32),
        lax.psum_scatter(third.astype(jnp.bfloat16), "seq", scatter_dimension=1, tiled=True).astype(
            jnp.float32
        ),
        lax.psum_scatter(
            fourth.astype(jnp.bfloat16), "seq", scatter_dimension=1, tiled=True
        ).astype(jnp.float32),
        lax.psum_scatter(fifth.astype(jnp.bfloat16), "seq", scatter_dimension=1, tiled=True).astype(
            jnp.float32
        ),
        lax.psum_scatter(sixth.astype(jnp.bfloat16), "seq", scatter_dimension=1, tiled=True).astype(
            jnp.float32
        ),
    )
    return (
        lax.psum_scatter(
            part[0].astype(jnp.bfloat16), "dp", scatter_dimension=0, tiled=True
        ).astype(jnp.float32),
        lax.psum_scatter(
            part[1].astype(jnp.bfloat16), "dp", scatter_dimension=0, tiled=True
        ).astype(jnp.float32),
        lax.psum_scatter(
            part[2].astype(jnp.bfloat16), "dp", scatter_dimension=0, tiled=True
        ).astype(jnp.float32),
        lax.psum_scatter(
            part[3].astype(jnp.bfloat16), "dp", scatter_dimension=0, tiled=True
        ).astype(jnp.float32),
        lax.psum_scatter(
            part[4].astype(jnp.bfloat16), "dp", scatter_dimension=0, tiled=True
        ).astype(jnp.float32),
        lax.psum_scatter(
            part[5].astype(jnp.bfloat16), "dp", scatter_dimension=0, tiled=True
        ).astype(jnp.float32),
    )


def block_layout(seq_count, row_count, head_count):
    block_seqs = math.gcd(seq_count, max(1, 512 // row_count))
    group_heads = math.gcd(head_count, 4)
    return (block_seqs, seq_count // block_seqs, group_heads, head_count // group_heads)


def head_slice(block_part, offset, group_width, group_heads):
    sliced = lax.dynamic_slice_in_dim(block_part, offset, group_width, 2)
    return sliced.reshape(sliced.shape[0], sliced.shape[1], group_heads, HD)


def attention_forward(queries, key_all, value_all, key_mask):
    seq_count, row_count, feature_total = queries.shape
    slot_count = key_all.shape[1]
    block_seqs, block_count, group_heads, group_count = block_layout(
        seq_count, row_count, feature_total // HD
    )
    group_width = group_heads * HD

    def seq_block(inputs):
        query_part, key_part, value_part, mask_part = inputs

        def head_block(group_index):
            offset = group_index * group_width
            query_heads = head_slice(query_part, offset, group_width, group_heads)
            key_heads = head_slice(key_part, offset, group_width, group_heads)
            value_heads = head_slice(value_part, offset, group_width, group_heads)
            scores = (
                jnp.einsum(
                    "brhd,bkhd->bhrk", query_heads, key_heads, preferred_element_type=jnp.float32
                )
                * 0.125
            )
            scores = jnp.where(mask_part[:, None, None, :], scores, -1e30)
            row_max = jnp.max(scores, axis=-1, keepdims=True)
            exponent = jnp.exp(scores - row_max)
            row_total = jnp.sum(exponent, axis=-1, keepdims=True)
            soft_probs = (exponent / row_total).astype(jnp.bfloat16)
            heads_out = jnp.einsum(
                "bhrk,bkhd->brhd", soft_probs, value_heads, preferred_element_type=jnp.float32
            )
            log_total = (row_max + jnp.log(row_total))[..., 0]
            return (heads_out.reshape(block_seqs, row_count, group_width), log_total)

        return lax.map(head_block, jnp.arange(group_count))

    outputs, log_totals = lax.map(
        seq_block,
        (
            queries.reshape(block_count, block_seqs, row_count, feature_total),
            key_all.reshape(block_count, block_seqs, slot_count, feature_total),
            value_all.reshape(block_count, block_seqs, slot_count, feature_total),
            key_mask.reshape(block_count, block_seqs, slot_count),
        ),
    )
    mixed_heads = outputs.transpose(0, 2, 3, 1, 4).reshape(seq_count, row_count, feature_total)
    return (mixed_heads, log_totals)


def attention_backward(queries, key_all, value_all, key_mask, heads_grad, log_totals):
    seq_count, row_count, feature_total = queries.shape
    slot_count = key_all.shape[1]
    block_seqs, block_count, group_heads, group_count = block_layout(
        seq_count, row_count, feature_total // HD
    )
    group_width = group_heads * HD

    def seq_block(inputs):
        query_part, key_part, value_part, mask_part, grad_part, total_part = inputs

        def head_block(group_index):
            offset = group_index * group_width
            query_heads = head_slice(query_part, offset, group_width, group_heads)
            key_heads = head_slice(key_part, offset, group_width, group_heads)
            value_heads = head_slice(value_part, offset, group_width, group_heads)
            grad_heads = head_slice(grad_part, offset, group_width, group_heads)
            log_total = lax.dynamic_index_in_dim(total_part, group_index, 0, keepdims=False)
            scores = (
                jnp.einsum(
                    "brhd,bkhd->bhrk", query_heads, key_heads, preferred_element_type=jnp.float32
                )
                * 0.125
            )
            scores = jnp.where(mask_part[:, None, None, :], scores, -1e30)
            soft_probs = jnp.exp(scores - log_total[..., None])
            value_grad = jnp.einsum(
                "bhrk,brhd->bkhd",
                soft_probs.astype(jnp.bfloat16),
                grad_heads,
                preferred_element_type=jnp.float32,
            )
            prob_grad = jnp.einsum(
                "brhd,bkhd->bhrk", grad_heads, value_heads, preferred_element_type=jnp.float32
            )
            inner = jnp.sum(soft_probs * prob_grad, axis=-1, keepdims=True)
            score_grad = (soft_probs * (prob_grad - inner)).astype(jnp.bfloat16)
            query_grad = (
                jnp.einsum(
                    "bhrk,bkhd->brhd", score_grad, key_heads, preferred_element_type=jnp.float32
                )
                * 0.125
            )
            key_grad = (
                jnp.einsum(
                    "bhrk,brhd->bkhd", score_grad, query_heads, preferred_element_type=jnp.float32
                )
                * 0.125
            )
            return (
                query_grad.reshape(block_seqs, row_count, group_width),
                key_grad.reshape(block_seqs, slot_count, group_width),
                value_grad.reshape(block_seqs, slot_count, group_width),
            )

        return lax.map(head_block, jnp.arange(group_count))

    query_blocks, key_blocks, value_block_list = lax.map(
        seq_block,
        (
            queries.reshape(block_count, block_seqs, row_count, feature_total),
            key_all.reshape(block_count, block_seqs, slot_count, feature_total),
            value_all.reshape(block_count, block_seqs, slot_count, feature_total),
            key_mask.reshape(block_count, block_seqs, slot_count),
            heads_grad.reshape(block_count, block_seqs, row_count, feature_total),
            log_totals,
        ),
    )
    query_grad = query_blocks.transpose(0, 2, 3, 1, 4).reshape(seq_count, row_count, feature_total)
    key_grad = key_blocks.transpose(0, 2, 3, 1, 4).reshape(seq_count, slot_count, feature_total)
    value_grad = value_block_list.transpose(0, 2, 3, 1, 4).reshape(
        seq_count, slot_count, feature_total
    )
    return (query_grad, key_grad, value_grad)


def general_body(
    tokens,
    lengths,
    cotangent,
    query_weight,
    key_weight,
    value_weight,
    out_weight,
    up_weight,
    down_weight,
    query_bias,
    value_bias,
    out_bias,
    attn_gain,
    attn_shift,
    up_bias,
    down_bias,
    feed_gain,
    feed_shift,
):
    seq_count, row_count, feature_total = tokens.shape
    slot_count = row_count * lax.axis_size("seq")
    token_count = seq_count * row_count
    whole = gather_weights(
        query_weight, key_weight, value_weight, out_weight, up_weight, down_weight
    )
    full_query, full_key, full_value, full_out, full_up, full_down = whole
    flat_tokens = tokens.reshape(token_count, feature_total)
    queries = (
        jnp.dot(flat_tokens, full_query, preferred_element_type=jnp.float32) + query_bias
    ).astype(jnp.bfloat16)
    key_rows = jnp.dot(flat_tokens, full_key, preferred_element_type=jnp.float32).astype(
        jnp.bfloat16
    )
    value_rows = (
        jnp.dot(flat_tokens, full_value, preferred_element_type=jnp.float32) + value_bias
    ).astype(jnp.bfloat16)
    first_slot = lax.axis_index("seq") * row_count
    key_mask = jnp.arange(slot_count)[None, :] < lengths[:, None]
    row_valid = ((first_slot + jnp.arange(row_count))[None, :] < lengths[:, None]).astype(
        jnp.float32
    )
    row_valid = row_valid.reshape(token_count, 1)
    query_blocks = queries.reshape(seq_count, row_count, feature_total)
    key_blocks = key_rows.reshape(seq_count, row_count, feature_total)
    value_block_list = value_rows.reshape(seq_count, row_count, feature_total)
    key_all, value_all = (
        lax.all_gather(key_blocks, "seq", axis=1, tiled=True),
        lax.all_gather(value_block_list, "seq", axis=1, tiled=True),
    )
    mixed_heads, log_totals = attention_forward(query_blocks, key_all, value_all, key_mask)
    heads_low = mixed_heads.reshape(token_count, feature_total).astype(jnp.bfloat16)
    attention_out = jnp.dot(heads_low, full_out, preferred_element_type=jnp.float32) + out_bias
    tokens_f32 = flat_tokens.astype(jnp.float32)
    first_sum = tokens_f32 + attention_out
    hidden, first_pull = jax.vjp(layer_norm, first_sum, attn_gain, attn_shift)
    hidden_low = hidden.astype(jnp.bfloat16)
    pre_act = jnp.dot(hidden_low, full_up, preferred_element_type=jnp.float32) + up_bias
    gelu_out, gelu_pull = jax.vjp(partial(jax.nn.gelu, approximate=False), pre_act)
    activation = gelu_out.astype(jnp.bfloat16)
    feed_out = jnp.dot(activation, full_down, preferred_element_type=jnp.float32) + down_bias
    result, second_pull = jax.vjp(layer_norm, hidden + feed_out, feed_gain, feed_shift)
    mixed = result.astype(jnp.bfloat16).reshape(seq_count, row_count, feature_total)
    partial_stats = jnp.stack(
        [
            jnp.sum(row_valid * tokens_f32 * tokens_f32),
            jnp.sum(row_valid * attention_out * attention_out),
            jnp.sum(row_valid * feed_out * feed_out),
            jnp.sum(row_valid) * feature_total,
        ]
    )
    back_weights = gather_weights(
        query_weight, key_weight, value_weight, out_weight, up_weight, down_weight
    )
    back_query, back_key, back_value, back_out, back_up, back_down = back_weights
    out_grad = cotangent.reshape(token_count, feature_total).astype(jnp.float32) * row_valid
    second_grad, feed_gain_grad, feed_shift_grad = second_pull(out_grad)
    feed_low = second_grad.astype(jnp.bfloat16)
    down_weight_grad = jnp.einsum(
        "nf,nd->fd", activation, feed_low, preferred_element_type=jnp.float32
    )
    down_bias_grad = jnp.sum(feed_low, axis=0, dtype=jnp.float32)
    act_grad = jnp.einsum(
        "nd,fd->nf", feed_low, back_down, preferred_element_type=jnp.float32
    ).astype(jnp.bfloat16)
    pre_grad = gelu_pull(act_grad.astype(jnp.float32))[0].astype(jnp.bfloat16)
    up_weight_grad = jnp.einsum(
        "nd,nf->df", hidden_low, pre_grad, preferred_element_type=jnp.float32
    )
    up_bias_grad = jnp.sum(pre_grad, axis=0, dtype=jnp.float32)
    hidden_grad = (
        jnp.einsum("nf,df->nd", pre_grad, back_up, preferred_element_type=jnp.float32) + second_grad
    )
    first_grad, attn_gain_grad, attn_shift_grad = first_pull(hidden_grad)
    attn_low = first_grad.astype(jnp.bfloat16)
    out_weight_grad = jnp.einsum(
        "nd,ne->de", heads_low, attn_low, preferred_element_type=jnp.float32
    )
    out_bias_grad = jnp.sum(attn_low, axis=0, dtype=jnp.float32)
    heads_grad = jnp.einsum(
        "ne,de->nd", attn_low, back_out, preferred_element_type=jnp.float32
    ).astype(jnp.bfloat16)
    heads_grad = heads_grad.reshape(seq_count, row_count, feature_total)
    query_grad, key_part_grad, value_part_grad = attention_backward(
        query_blocks, key_all, value_all, key_mask, heads_grad, log_totals
    )
    key_sum, value_sum = (
        lax.psum_scatter(
            key_part_grad.astype(jnp.bfloat16), "seq", scatter_dimension=1, tiled=True
        ).astype(jnp.float32),
        lax.psum_scatter(
            value_part_grad.astype(jnp.bfloat16), "seq", scatter_dimension=1, tiled=True
        ).astype(jnp.float32),
    )
    query_low = query_grad.reshape(token_count, feature_total).astype(jnp.bfloat16)
    key_low = key_sum.reshape(token_count, feature_total).astype(jnp.bfloat16)
    value_low = value_sum.reshape(token_count, feature_total).astype(jnp.bfloat16)
    query_weight_grad = jnp.einsum(
        "nd,ne->de", flat_tokens, query_low, preferred_element_type=jnp.float32
    )
    key_weight_grad = jnp.einsum(
        "nd,ne->de", flat_tokens, key_low, preferred_element_type=jnp.float32
    )
    value_weight_grad = jnp.einsum(
        "nd,ne->de", flat_tokens, value_low, preferred_element_type=jnp.float32
    )
    query_bias_grad = jnp.sum(query_low, axis=0, dtype=jnp.float32)
    value_bias_gradient = jnp.sum(value_low, axis=0, dtype=jnp.float32)
    tokens_grad = (
        jnp.einsum("ne,de->nd", query_low, back_query, preferred_element_type=jnp.float32)
        + jnp.einsum("ne,de->nd", key_low, back_key, preferred_element_type=jnp.float32)
        + jnp.einsum("ne,de->nd", value_low, back_value, preferred_element_type=jnp.float32)
        + first_grad
    )
    tokens_grad = tokens_grad.astype(jnp.bfloat16).reshape(seq_count, row_count, feature_total)
    matrix_grads = reduce_grads(
        query_weight_grad,
        key_weight_grad,
        value_weight_grad,
        out_weight_grad,
        up_weight_grad,
        down_weight_grad,
    )
    totals = lax.psum(
        (
            partial_stats,
            query_bias_grad,
            value_bias_gradient,
            out_bias_grad,
            attn_gain_grad,
            attn_shift_grad,
            up_bias_grad,
            down_bias_grad,
            feed_gain_grad,
            feed_shift_grad,
        ),
        ("dp", "seq"),
    )
    stream_rms = jnp.sqrt(totals[0][:3] / totals[0][3])
    return (
        mixed,
        tokens_grad,
        matrix_grads[0],
        matrix_grads[1],
        matrix_grads[2],
        matrix_grads[3],
        matrix_grads[4],
        matrix_grads[5],
        totals[1],
        totals[2],
        totals[3],
        totals[4],
        totals[5],
        totals[6],
        totals[7],
        totals[8],
        totals[9],
        stream_rms,
    )


def swap(value, axis):
    return lax.ppermute(value, axis, [(0, 1), (1, 0)])


def both(value, axis):
    return jnp.concatenate([value, swap(value, axis)], axis=0)


def dot(left, right, dims):
    return lax.dot_general(left, right, (dims, ((), ())), preferred_element_type=jnp.float32)


def in_order(own, other, core):
    first = jnp.where(core == 0, own, other)
    second = jnp.where(core == 0, other, own)
    return jnp.concatenate([first, second], axis=0)


def split_columns(weight, width, core):
    rows = weight.shape[0]
    blocks = weight.reshape(rows, -1, 2, width)
    own = lax.dynamic_index_in_dim(blocks, core, 2, keepdims=False).reshape(rows, -1)
    sent = lax.dynamic_index_in_dim(blocks, 1 - core, 2, keepdims=False).reshape(rows, -1)
    return own, sent


def spread(matrix, chips, halves):
    rows, columns = matrix.shape
    return matrix.reshape(chips, rows // chips, halves, columns // halves).transpose(0, 2, 1, 3)


def unspread(parts):
    chips, halves, rows, columns = parts.shape
    return parts.transpose(0, 2, 1, 3).reshape(chips * rows, halves * columns)


def norm_parts(values_in):
    mean_value = jnp.mean(values_in, axis=-1, keepdims=True)
    centered = values_in - mean_value
    variance = jnp.mean(centered * centered, axis=-1, keepdims=True)
    rstd = lax.rsqrt(variance + 1e-05)
    return centered * rstd, rstd


def norm_back(grad, xhat, rstd, gain):
    scaled = grad * gain
    inner = jnp.mean(scaled * xhat, axis=-1, keepdims=True)
    result = rstd * (scaled - jnp.mean(scaled, axis=-1, keepdims=True) - xhat * inner)
    return result, jnp.sum(grad * xhat, axis=0), jnp.sum(grad, axis=0)


def total_over(vector, chips):
    vector = vector + swap(vector, "s")
    step = 1
    while step < chips:
        vector = vector + lax.ppermute(vector, "p", [(i, i ^ step) for i in range(chips)])
        step *= 2
    return vector


def split_body(
    tokens,
    lengths,
    cotangent,
    query_weight,
    key_weight,
    value_weight,
    out_weight,
    up_weight,
    down_weight,
    query_bias,
    value_bias,
    out_bias,
    attn_gain,
    attn_shift,
    up_bias,
    down_bias,
    feed_gain,
    feed_shift,
):
    chips = lax.axis_size("p")
    core = lax.axis_index("c")
    half = lax.axis_index("s")
    row_count, width = tokens.shape[1:]
    slots = 2 * row_count
    unit_block = down_weight.shape[0]
    units = up_bias.shape[0] // 2
    cols = width // 2
    heads = cols // HD

    small = [
        split_columns(weight, HD, core) for weight in (query_weight, key_weight, value_weight)
    ]
    large = split_columns(up_weight, unit_block, core)
    sent = swap(jnp.concatenate([part[1] for part in small] + [large[1]], axis=1), "c")
    kept = jnp.concatenate([part[0] for part in small] + [large[0]], axis=1)
    mine = in_order(kept, sent, core)
    rows = mine.shape[0]
    wide = cols // 2
    near = 3 * wide
    up_cols = large[0].shape[1]
    cut = up_cols // 2
    first_send = jnp.concatenate(
        [
            mine[:, :near].reshape(-1, 512),
            out_weight.reshape(-1, 512),
            mine[:, near : near + cut].reshape(-1, 512),
        ],
        axis=0,
    )
    second_send = jnp.concatenate(
        [mine[:, near + cut :].reshape(-1, 512), down_weight.reshape(-1, 512)], axis=0
    )
    near_rows = rows * near // 512
    out_rows = out_weight.size // 512
    cut_rows = rows * cut // 512
    first_all = lax.all_gather(first_send, ("p", "s"), axis=0, tiled=False)
    second_all = lax.all_gather(second_send, ("p", "s"), axis=0, tiled=False)
    first_all = first_all.reshape(chips, 2, -1, 512)
    second_all = second_all.reshape(chips, 2, -1, 512)
    near_all = first_all[:, :, :near_rows].reshape(chips, 2, rows, 3, wide)
    in_weight = near_all.transpose(0, 2, 3, 1, 4).reshape(width, 3 * cols)
    out_own = unspread(first_all[:, :, near_rows : near_rows + out_rows].reshape((chips, 2) + out_weight.shape))
    up_first = first_all[:, :, near_rows + out_rows :].reshape(chips, 2, rows, cut)
    up_second = second_all[:, :, :cut_rows].reshape(chips, 2, rows, cut)
    up_own = unspread(jnp.concatenate([up_first, up_second], axis=3))
    down_own = unspread(second_all[:, :, cut_rows:].reshape((chips, 2) + down_weight.shape))

    def to_sequence(values):
        own = lax.dynamic_index_in_dim(values, half, 0, keepdims=False)
        other = lax.dynamic_index_in_dim(values, 1 - half, 0, keepdims=False)
        return jnp.concatenate([own, swap(other, "s")], axis=0)

    def from_sequence(values):
        own = values[:row_count]
        other = swap(values[row_count:], "s")
        first = jnp.where(half == 0, own, other)
        second = jnp.where(half == 0, other, own)
        return jnp.stack([first, second], axis=0)

    tokens_own = to_sequence(tokens)
    cotangent_own = to_sequence(cotangent)
    tokens_both = both(tokens_own, "c")
    place = jnp.concatenate(
        [half * row_count + jnp.arange(row_count), (1 - half) * row_count + jnp.arange(row_count)]
    )
    length_own = lax.dynamic_slice_in_dim(lengths, half, 1, 0)
    length_both = both(length_own, "c")
    key_mask = place[None, :] < length_both[:, None]
    row_valid = (place < length_own[0]).astype(jnp.float32)[:, None]

    def halves_of(vector, block):
        return lax.dynamic_index_in_dim(vector.reshape(-1, 2, block), core, 1, keepdims=False).reshape(-1)

    in_bias = jnp.concatenate(
        [halves_of(query_bias, HD), jnp.zeros((cols,), jnp.float32), halves_of(value_bias, HD)]
    )
    projected = (dot(tokens_both, in_weight, ((1,), (0,))) + in_bias).astype(jnp.bfloat16)
    queries, keys, values = [
        projected[:, i * cols : (i + 1) * cols].reshape(2, slots, heads, HD) for i in range(3)
    ]
    scores = jnp.einsum("sqhd,skhd->shqk", queries, keys, preferred_element_type=jnp.float32) * 0.125
    scores = jnp.where(key_mask[:, None, None, :], scores, -1e30)
    exponent = jnp.exp(scores - jnp.max(scores, axis=-1, keepdims=True))
    soft_probs = exponent / jnp.sum(exponent, axis=-1, keepdims=True)
    probs_low = soft_probs.astype(jnp.bfloat16)
    heads_out = jnp.einsum("shqk,skhd->sqhd", probs_low, values, preferred_element_type=jnp.float32)
    heads_out = heads_out.reshape(2 * slots, cols).astype(jnp.bfloat16)
    heads_own = jnp.concatenate([heads_out[:slots], swap(heads_out[slots:], "c")], axis=1)
    out_both = both(out_own, "c")
    attention_out = dot(heads_own, out_both, ((1,), (0,))) + out_bias
    tokens_f32 = tokens_own.astype(jnp.float32)
    first_hat, first_rstd = norm_parts(tokens_f32 + attention_out)
    hidden = first_hat * attn_gain + attn_shift
    hidden_both = both(hidden.astype(jnp.bfloat16), "c")
    pre_act = dot(hidden_both, up_own, ((1,), (0,))) + halves_of(up_bias, unit_block)
    below = 0.5 * (1.0 + lax.erf(pre_act * 0.7071067811865476))
    slope = below + pre_act * (0.3989422804014327 * jnp.exp(-0.5 * pre_act * pre_act))
    slope = slope.astype(jnp.bfloat16)
    activation = (pre_act * below).astype(jnp.bfloat16)
    feed_part = dot(activation, down_own, ((1,), (0,)))
    feed_out = (
        feed_part[:slots]
        + swap(feed_part[slots:].astype(jnp.bfloat16), "c").astype(jnp.float32)
        + down_bias
    )
    second_hat, second_rstd = norm_parts(hidden + feed_out)
    mixed = from_sequence((second_hat * feed_gain + feed_shift).astype(jnp.bfloat16))
    stats = jnp.stack(
        [
            jnp.sum(row_valid * tokens_f32 * tokens_f32),
            jnp.sum(row_valid * attention_out * attention_out),
            jnp.sum(row_valid * feed_out * feed_out),
            jnp.sum(row_valid) * width,
        ]
    )

    out_grad = cotangent_own.astype(jnp.float32) * row_valid
    second_grad, feed_gain_grad, feed_shift_grad = norm_back(
        out_grad, second_hat, second_rstd, feed_gain
    )
    feed_low = second_grad.astype(jnp.bfloat16)
    down_bias_grad = jnp.sum(feed_low, axis=0, dtype=jnp.float32)
    feed_both = both(feed_low, "c")
    down_grad = dot(activation, feed_both, ((0,), (0,))).astype(jnp.bfloat16)
    act_grad = dot(feed_both, down_own, ((1,), (1,))).astype(jnp.bfloat16)
    pre_grad = (act_grad.astype(jnp.float32) * slope.astype(jnp.float32)).astype(jnp.bfloat16)
    up_grad = dot(hidden_both, pre_grad, ((0,), (0,))).astype(jnp.bfloat16)
    up_bias_grad = jnp.sum(pre_grad, axis=0, dtype=jnp.float32)
    up_parts = spread(up_grad, chips, 2)
    first_back = jnp.concatenate(
        [
            spread(down_grad, chips, 2).reshape(2 * chips, -1, 512),
            up_parts[..., cut:].reshape(2 * chips, -1, 512),
        ],
        axis=1,
    )
    first_sum = lax.psum_scatter(first_back, ("p", "s"), scatter_dimension=0, tiled=False)
    hidden_part = dot(pre_grad, up_own, ((1,), (1,)))
    hidden_grad = (
        hidden_part[:slots]
        + swap(hidden_part[slots:].astype(jnp.bfloat16), "c").astype(jnp.float32)
        + second_grad
    )
    first_grad, attn_gain_grad, attn_shift_grad = norm_back(
        hidden_grad, first_hat, first_rstd, attn_gain
    )
    attn_low = first_grad.astype(jnp.bfloat16)
    out_bias_grad = jnp.sum(attn_low, axis=0, dtype=jnp.float32)
    heads_grad = dot(attn_low, out_both, ((1,), (1,))).astype(jnp.bfloat16)
    heads_grad = jnp.concatenate([heads_grad[:, :cols], swap(heads_grad[:, cols:], "c")], axis=0)
    heads_grad = heads_grad.reshape(2, slots, heads, HD)
    out_grad_part = dot(heads_own, attn_low, ((0,), (0,)))
    out_grad_own = (
        out_grad_part[:cols]
        + swap(out_grad_part[cols:].astype(jnp.bfloat16), "c").astype(jnp.float32)
    ).astype(jnp.bfloat16)
    value_low = jnp.einsum(
        "shqk,sqhd->skhd", probs_low, heads_grad, preferred_element_type=jnp.float32
    )
    prob_grad = jnp.einsum(
        "sqhd,skhd->shqk", heads_grad, values, preferred_element_type=jnp.float32
    )
    inner = jnp.sum(soft_probs * prob_grad, axis=-1, keepdims=True)
    score_grad = (soft_probs * (prob_grad - inner)).astype(jnp.bfloat16)
    query_low = 0.125 * jnp.einsum(
        "shqk,skhd->sqhd", score_grad, keys, preferred_element_type=jnp.float32
    )
    key_low = 0.125 * jnp.einsum(
        "shqk,sqhd->skhd", score_grad, queries, preferred_element_type=jnp.float32
    )
    in_low = jnp.concatenate(
        [part.reshape(2 * slots, cols).astype(jnp.bfloat16) for part in (query_low, key_low, value_low)],
        axis=1,
    )
    in_grad = dot(tokens_both, in_low, ((0,), (0,))).astype(jnp.bfloat16)
    in_parts = in_grad.reshape(chips, rows, 3, 2, wide).transpose(0, 3, 1, 2, 4)
    second_back = jnp.concatenate(
        [
            in_parts.reshape(2 * chips, -1, 512),
            spread(out_grad_own, chips, 2).reshape(2 * chips, -1, 512),
            up_parts[..., :cut].reshape(2 * chips, -1, 512),
        ],
        axis=1,
    )
    second_sum = lax.psum_scatter(second_back, ("p", "s"), scatter_dimension=0, tiled=False)
    in_bias_grad = jnp.sum(in_low, axis=0, dtype=jnp.float32)
    tokens_part = dot(in_low, in_weight, ((1,), (1,)))
    tokens_grad = (
        tokens_part[:slots]
        + swap(tokens_part[slots:].astype(jnp.bfloat16), "c").astype(jnp.float32)
        + first_grad
    )
    tokens_grad = from_sequence(tokens_grad.astype(jnp.bfloat16))

    shared = jnp.concatenate(
        [
            down_bias_grad,
            feed_gain_grad,
            feed_shift_grad,
            out_bias_grad,
            attn_gain_grad,
            attn_shift_grad,
            jnp.pad(stats, (0, 124)),
        ]
    )
    own_sums = total_over(
        jnp.concatenate([shared, up_bias_grad, in_bias_grad[:cols], in_bias_grad[2 * cols :]]), chips
    )
    other_sums = swap(own_sums, "c")
    count = shared.shape[0]
    shared = own_sums[:count] + other_sums[:count]
    down_bias_grad, feed_gain_grad, feed_shift_grad, out_bias_grad, attn_gain_grad, attn_shift_grad = [
        shared[i * width : (i + 1) * width] for i in range(6)
    ]
    stats = shared[6 * width : 6 * width + 4]

    def interleave(start, size, block):
        own = own_sums[start : start + size].reshape(-1, block)
        other = other_sums[start : start + size].reshape(-1, block)
        first = jnp.where(core == 0, own, other)
        second = jnp.where(core == 0, other, own)
        return jnp.stack([first, second], axis=1).reshape(-1)

    up_bias_grad = interleave(count, units, unit_block)
    query_bias_grad = interleave(count + units, cols, HD)
    value_bias_gradient = interleave(count + units + cols, cols, HD)
    stream_rms = jnp.sqrt(stats[:3] / stats[3])

    down_count = down_weight.size // 512
    down_weight_grad = first_sum[:down_count].reshape(down_weight.shape).astype(jnp.float32)
    up_second = first_sum[down_count:].reshape(rows, cut)
    in_sum = second_sum[:near_rows].reshape(rows, near)
    out_weight_grad = (
        second_sum[near_rows : near_rows + out_rows].reshape(out_weight.shape).astype(jnp.float32)
    )
    up_first = second_sum[near_rows + out_rows :].reshape(rows, cut)
    joined = jnp.concatenate([in_sum, up_first, up_second], axis=1)
    own = lax.dynamic_slice_in_dim(joined, core * (rows // 2), rows // 2, 0)
    sent = lax.dynamic_slice_in_dim(joined, (1 - core) * (rows // 2), rows // 2, 0)
    other = swap(sent, "c")

    def merge(start, size, block):
        one = own[:, start : start + size].reshape(rows // 2, -1, block)
        two = other[:, start : start + size].reshape(rows // 2, -1, block)
        first = jnp.where(core == 0, one, two)
        second = jnp.where(core == 0, two, one)
        return jnp.stack([first, second], axis=2).reshape(rows // 2, -1).astype(jnp.float32)

    query_weight_grad = merge(0, wide, HD)
    key_weight_grad = merge(wide, wide, HD)
    value_weight_grad = merge(2 * wide, wide, HD)
    up_weight_grad = merge(near, up_cols, unit_block)
    return (
        mixed,
        tokens_grad,
        query_weight_grad,
        key_weight_grad,
        value_weight_grad,
        out_weight_grad,
        up_weight_grad,
        down_weight_grad,
        query_bias_grad,
        value_bias_gradient,
        out_bias_grad,
        attn_gain_grad,
        attn_shift_grad,
        up_bias_grad,
        down_bias_grad,
        feed_gain_grad,
        feed_shift_grad,
        stream_rms,
    )


def solution(mesh):
    devices = mesh.devices
    dp_count, seq_count = devices.shape
    split = seq_count == 2 and dp_count == 16
    if split:
        inner = jax.sharding.Mesh(devices.reshape(dp_count // 2, 2, seq_count), ("p", "c", "s"))
        dp, seq, body = ("p", "c"), "s", split_body
    else:
        inner, dp, seq, body = mesh, "dp", "seq", general_body
    weights = (P(dp, seq),) * 6
    vectors = (P(),) * 9
    rows = P(dp, seq, None)
    in_specs = (rows, P(dp), rows) + weights + vectors
    out_specs = (rows, rows) + weights + vectors + (P(),)
    return jax.shard_map(body, mesh=inner, in_specs=in_specs, out_specs=out_specs, check_vma=False)
```

```python
from functools import partial
import math

import jax
import jax.numpy as jnp
from jax import lax
from jax.sharding import PartitionSpec as P

HD = 64


def layer_norm(values_in, gain_vector, shift_vector):
    mean_value = jnp.mean(values_in, axis=-1, keepdims=True)
    centered = values_in - mean_value
    variance = jnp.mean(centered * centered, axis=-1, keepdims=True)
    return centered * lax.rsqrt(variance + 1e-05) * gain_vector + shift_vector


def gather_weights(first, second, third, fourth, fifth, sixth):
    part = (
        lax.all_gather(first, "dp", axis=0, tiled=True),
        lax.all_gather(second, "dp", axis=0, tiled=True),
        lax.all_gather(third, "dp", axis=0, tiled=True),
        lax.all_gather(fourth, "dp", axis=0, tiled=True),
        lax.all_gather(fifth, "dp", axis=0, tiled=True),
        lax.all_gather(sixth, "dp", axis=0, tiled=True),
    )
    return (
        lax.all_gather(part[0], "seq", axis=1, tiled=True),
        lax.all_gather(part[1], "seq", axis=1, tiled=True),
        lax.all_gather(part[2], "seq", axis=1, tiled=True),
        lax.all_gather(part[3], "seq", axis=1, tiled=True),
        lax.all_gather(part[4], "seq", axis=1, tiled=True),
        lax.all_gather(part[5], "seq", axis=1, tiled=True),
    )


def reduce_grads(first, second, third, fourth, fifth, sixth):
    part = (
        lax.psum_scatter(first.astype(jnp.bfloat16), "seq", scatter_dimension=1, tiled=True).astype(
            jnp.float32
        ),
        lax.psum_scatter(
            second.astype(jnp.bfloat16), "seq", scatter_dimension=1, tiled=True
        ).astype(jnp.float32),
        lax.psum_scatter(third.astype(jnp.bfloat16), "seq", scatter_dimension=1, tiled=True).astype(
            jnp.float32
        ),
        lax.psum_scatter(
            fourth.astype(jnp.bfloat16), "seq", scatter_dimension=1, tiled=True
        ).astype(jnp.float32),
        lax.psum_scatter(fifth.astype(jnp.bfloat16), "seq", scatter_dimension=1, tiled=True).astype(
            jnp.float32
        ),
        lax.psum_scatter(sixth.astype(jnp.bfloat16), "seq", scatter_dimension=1, tiled=True).astype(
            jnp.float32
        ),
    )
    return (
        lax.psum_scatter(
            part[0].astype(jnp.bfloat16), "dp", scatter_dimension=0, tiled=True
        ).astype(jnp.float32),
        lax.psum_scatter(
            part[1].astype(jnp.bfloat16), "dp", scatter_dimension=0, tiled=True
        ).astype(jnp.float32),
        lax.psum_scatter(
            part[2].astype(jnp.bfloat16), "dp", scatter_dimension=0, tiled=True
        ).astype(jnp.float32),
        lax.psum_scatter(
            part[3].astype(jnp.bfloat16), "dp", scatter_dimension=0, tiled=True
        ).astype(jnp.float32),
        lax.psum_scatter(
            part[4].astype(jnp.bfloat16), "dp", scatter_dimension=0, tiled=True
        ).astype(jnp.float32),
        lax.psum_scatter(
            part[5].astype(jnp.bfloat16), "dp", scatter_dimension=0, tiled=True
        ).astype(jnp.float32),
    )


def block_layout(seq_count, row_count, head_count):
    block_seqs = math.gcd(seq_count, max(1, 512 // row_count))
    group_heads = math.gcd(head_count, 4)
    return (block_seqs, seq_count // block_seqs, group_heads, head_count // group_heads)


def head_slice(block_part, offset, group_width, group_heads):
    sliced = lax.dynamic_slice_in_dim(block_part, offset, group_width, 2)
    return sliced.reshape(sliced.shape[0], sliced.shape[1], group_heads, HD)


def attention_forward(queries, key_all, value_all, key_mask):
    seq_count, row_count, feature_total = queries.shape
    slot_count = key_all.shape[1]
    block_seqs, block_count, group_heads, group_count = block_layout(
        seq_count, row_count, feature_total // HD
    )
    group_width = group_heads * HD

    def seq_block(inputs):
        query_part, key_part, value_part, mask_part = inputs

        def head_block(group_index):
            offset = group_index * group_width
            query_heads = head_slice(query_part, offset, group_width, group_heads)
            key_heads = head_slice(key_part, offset, group_width, group_heads)
            value_heads = head_slice(value_part, offset, group_width, group_heads)
            scores = (
                jnp.einsum(
                    "brhd,bkhd->bhrk", query_heads, key_heads, preferred_element_type=jnp.float32
                )
                * 0.125
            )
            scores = jnp.where(mask_part[:, None, None, :], scores, -1e30)
            row_max = jnp.max(scores, axis=-1, keepdims=True)
            exponent = jnp.exp(scores - row_max)
            row_total = jnp.sum(exponent, axis=-1, keepdims=True)
            soft_probs = (exponent / row_total).astype(jnp.bfloat16)
            heads_out = jnp.einsum(
                "bhrk,bkhd->brhd", soft_probs, value_heads, preferred_element_type=jnp.float32
            )
            log_total = (row_max + jnp.log(row_total))[..., 0]
            return (heads_out.reshape(block_seqs, row_count, group_width), log_total)

        return lax.map(head_block, jnp.arange(group_count))

    outputs, log_totals = lax.map(
        seq_block,
        (
            queries.reshape(block_count, block_seqs, row_count, feature_total),
            key_all.reshape(block_count, block_seqs, slot_count, feature_total),
            value_all.reshape(block_count, block_seqs, slot_count, feature_total),
            key_mask.reshape(block_count, block_seqs, slot_count),
        ),
    )
    mixed_heads = outputs.transpose(0, 2, 3, 1, 4).reshape(seq_count, row_count, feature_total)
    return (mixed_heads, log_totals)


def attention_backward(queries, key_all, value_all, key_mask, heads_grad, log_totals):
    seq_count, row_count, feature_total = queries.shape
    slot_count = key_all.shape[1]
    block_seqs, block_count, group_heads, group_count = block_layout(
        seq_count, row_count, feature_total // HD
    )
    group_width = group_heads * HD

    def seq_block(inputs):
        query_part, key_part, value_part, mask_part, grad_part, total_part = inputs

        def head_block(group_index):
            offset = group_index * group_width
            query_heads = head_slice(query_part, offset, group_width, group_heads)
            key_heads = head_slice(key_part, offset, group_width, group_heads)
            value_heads = head_slice(value_part, offset, group_width, group_heads)
            grad_heads = head_slice(grad_part, offset, group_width, group_heads)
            log_total = lax.dynamic_index_in_dim(total_part, group_index, 0, keepdims=False)
            scores = (
                jnp.einsum(
                    "brhd,bkhd->bhrk", query_heads, key_heads, preferred_element_type=jnp.float32
                )
                * 0.125
            )
            scores = jnp.where(mask_part[:, None, None, :], scores, -1e30)
            soft_probs = jnp.exp(scores - log_total[..., None])
            value_grad = jnp.einsum(
                "bhrk,brhd->bkhd",
                soft_probs.astype(jnp.bfloat16),
                grad_heads,
                preferred_element_type=jnp.float32,
            )
            prob_grad = jnp.einsum(
                "brhd,bkhd->bhrk", grad_heads, value_heads, preferred_element_type=jnp.float32
            )
            inner = jnp.sum(soft_probs * prob_grad, axis=-1, keepdims=True)
            score_grad = (soft_probs * (prob_grad - inner)).astype(jnp.bfloat16)
            query_grad = (
                jnp.einsum(
                    "bhrk,bkhd->brhd", score_grad, key_heads, preferred_element_type=jnp.float32
                )
                * 0.125
            )
            key_grad = (
                jnp.einsum(
                    "bhrk,brhd->bkhd", score_grad, query_heads, preferred_element_type=jnp.float32
                )
                * 0.125
            )
            return (
                query_grad.reshape(block_seqs, row_count, group_width),
                key_grad.reshape(block_seqs, slot_count, group_width),
                value_grad.reshape(block_seqs, slot_count, group_width),
            )

        return lax.map(head_block, jnp.arange(group_count))

    query_blocks, key_blocks, value_block_list = lax.map(
        seq_block,
        (
            queries.reshape(block_count, block_seqs, row_count, feature_total),
            key_all.reshape(block_count, block_seqs, slot_count, feature_total),
            value_all.reshape(block_count, block_seqs, slot_count, feature_total),
            key_mask.reshape(block_count, block_seqs, slot_count),
            heads_grad.reshape(block_count, block_seqs, row_count, feature_total),
            log_totals,
        ),
    )
    query_grad = query_blocks.transpose(0, 2, 3, 1, 4).reshape(seq_count, row_count, feature_total)
    key_grad = key_blocks.transpose(0, 2, 3, 1, 4).reshape(seq_count, slot_count, feature_total)
    value_grad = value_block_list.transpose(0, 2, 3, 1, 4).reshape(
        seq_count, slot_count, feature_total
    )
    return (query_grad, key_grad, value_grad)


def general_body(
    tokens,
    lengths,
    cotangent,
    query_weight,
    key_weight,
    value_weight,
    out_weight,
    up_weight,
    down_weight,
    query_bias,
    value_bias,
    out_bias,
    attn_gain,
    attn_shift,
    up_bias,
    down_bias,
    feed_gain,
    feed_shift,
):
    seq_count, row_count, feature_total = tokens.shape
    slot_count = row_count * lax.axis_size("seq")
    token_count = seq_count * row_count
    whole = gather_weights(
        query_weight, key_weight, value_weight, out_weight, up_weight, down_weight
    )
    full_query, full_key, full_value, full_out, full_up, full_down = whole
    flat_tokens = tokens.reshape(token_count, feature_total)
    queries = (
        jnp.dot(flat_tokens, full_query, preferred_element_type=jnp.float32) + query_bias
    ).astype(jnp.bfloat16)
    key_rows = jnp.dot(flat_tokens, full_key, preferred_element_type=jnp.float32).astype(
        jnp.bfloat16
    )
    value_rows = (
        jnp.dot(flat_tokens, full_value, preferred_element_type=jnp.float32) + value_bias
    ).astype(jnp.bfloat16)
    first_slot = lax.axis_index("seq") * row_count
    key_mask = jnp.arange(slot_count)[None, :] < lengths[:, None]
    row_valid = ((first_slot + jnp.arange(row_count))[None, :] < lengths[:, None]).astype(
        jnp.float32
    )
    row_valid = row_valid.reshape(token_count, 1)
    query_blocks = queries.reshape(seq_count, row_count, feature_total)
    key_blocks = key_rows.reshape(seq_count, row_count, feature_total)
    value_block_list = value_rows.reshape(seq_count, row_count, feature_total)
    key_all, value_all = (
        lax.all_gather(key_blocks, "seq", axis=1, tiled=True),
        lax.all_gather(value_block_list, "seq", axis=1, tiled=True),
    )
    mixed_heads, log_totals = attention_forward(query_blocks, key_all, value_all, key_mask)
    heads_low = mixed_heads.reshape(token_count, feature_total).astype(jnp.bfloat16)
    attention_out = jnp.dot(heads_low, full_out, preferred_element_type=jnp.float32) + out_bias
    tokens_f32 = flat_tokens.astype(jnp.float32)
    first_sum = tokens_f32 + attention_out
    hidden, first_pull = jax.vjp(layer_norm, first_sum, attn_gain, attn_shift)
    hidden_low = hidden.astype(jnp.bfloat16)
    pre_act = jnp.dot(hidden_low, full_up, preferred_element_type=jnp.float32) + up_bias
    gelu_out, gelu_pull = jax.vjp(partial(jax.nn.gelu, approximate=False), pre_act)
    activation = gelu_out.astype(jnp.bfloat16)
    feed_out = jnp.dot(activation, full_down, preferred_element_type=jnp.float32) + down_bias
    result, second_pull = jax.vjp(layer_norm, hidden + feed_out, feed_gain, feed_shift)
    mixed = result.astype(jnp.bfloat16).reshape(seq_count, row_count, feature_total)
    partial_stats = jnp.stack(
        [
            jnp.sum(row_valid * tokens_f32 * tokens_f32),
            jnp.sum(row_valid * attention_out * attention_out),
            jnp.sum(row_valid * feed_out * feed_out),
            jnp.sum(row_valid) * feature_total,
        ]
    )
    back_weights = gather_weights(
        query_weight, key_weight, value_weight, out_weight, up_weight, down_weight
    )
    back_query, back_key, back_value, back_out, back_up, back_down = back_weights
    out_grad = cotangent.reshape(token_count, feature_total).astype(jnp.float32) * row_valid
    second_grad, feed_gain_grad, feed_shift_grad = second_pull(out_grad)
    feed_low = second_grad.astype(jnp.bfloat16)
    down_weight_grad = jnp.einsum(
        "nf,nd->fd", activation, feed_low, preferred_element_type=jnp.float32
    )
    down_bias_grad = jnp.sum(feed_low, axis=0, dtype=jnp.float32)
    act_grad = jnp.einsum(
        "nd,fd->nf", feed_low, back_down, preferred_element_type=jnp.float32
    ).astype(jnp.bfloat16)
    pre_grad = gelu_pull(act_grad.astype(jnp.float32))[0].astype(jnp.bfloat16)
    up_weight_grad = jnp.einsum(
        "nd,nf->df", hidden_low, pre_grad, preferred_element_type=jnp.float32
    )
    up_bias_grad = jnp.sum(pre_grad, axis=0, dtype=jnp.float32)
    hidden_grad = (
        jnp.einsum("nf,df->nd", pre_grad, back_up, preferred_element_type=jnp.float32) + second_grad
    )
    first_grad, attn_gain_grad, attn_shift_grad = first_pull(hidden_grad)
    attn_low = first_grad.astype(jnp.bfloat16)
    out_weight_grad = jnp.einsum(
        "nd,ne->de", heads_low, attn_low, preferred_element_type=jnp.float32
    )
    out_bias_grad = jnp.sum(attn_low, axis=0, dtype=jnp.float32)
    heads_grad = jnp.einsum(
        "ne,de->nd", attn_low, back_out, preferred_element_type=jnp.float32
    ).astype(jnp.bfloat16)
    heads_grad = heads_grad.reshape(seq_count, row_count, feature_total)
    query_grad, key_part_grad, value_part_grad = attention_backward(
        query_blocks, key_all, value_all, key_mask, heads_grad, log_totals
    )
    key_sum, value_sum = (
        lax.psum_scatter(
            key_part_grad.astype(jnp.bfloat16), "seq", scatter_dimension=1, tiled=True
        ).astype(jnp.float32),
        lax.psum_scatter(
            value_part_grad.astype(jnp.bfloat16), "seq", scatter_dimension=1, tiled=True
        ).astype(jnp.float32),
    )
    query_low = query_grad.reshape(token_count, feature_total).astype(jnp.bfloat16)
    key_low = key_sum.reshape(token_count, feature_total).astype(jnp.bfloat16)
    value_low = value_sum.reshape(token_count, feature_total).astype(jnp.bfloat16)
    query_weight_grad = jnp.einsum(
        "nd,ne->de", flat_tokens, query_low, preferred_element_type=jnp.float32
    )
    key_weight_grad = jnp.einsum(
        "nd,ne->de", flat_tokens, key_low, preferred_element_type=jnp.float32
    )
    value_weight_grad = jnp.einsum(
        "nd,ne->de", flat_tokens, value_low, preferred_element_type=jnp.float32
    )
    query_bias_grad = jnp.sum(query_low, axis=0, dtype=jnp.float32)
    value_bias_gradient = jnp.sum(value_low, axis=0, dtype=jnp.float32)
    tokens_grad = (
        jnp.einsum("ne,de->nd", query_low, back_query, preferred_element_type=jnp.float32)
        + jnp.einsum("ne,de->nd", key_low, back_key, preferred_element_type=jnp.float32)
        + jnp.einsum("ne,de->nd", value_low, back_value, preferred_element_type=jnp.float32)
        + first_grad
    )
    tokens_grad = tokens_grad.astype(jnp.bfloat16).reshape(seq_count, row_count, feature_total)
    matrix_grads = reduce_grads(
        query_weight_grad,
        key_weight_grad,
        value_weight_grad,
        out_weight_grad,
        up_weight_grad,
        down_weight_grad,
    )
    totals = lax.psum(
        (
            partial_stats,
            query_bias_grad,
            value_bias_gradient,
            out_bias_grad,
            attn_gain_grad,
            attn_shift_grad,
            up_bias_grad,
            down_bias_grad,
            feed_gain_grad,
            feed_shift_grad,
        ),
        ("dp", "seq"),
    )
    stream_rms = jnp.sqrt(totals[0][:3] / totals[0][3])
    return (
        mixed,
        tokens_grad,
        matrix_grads[0],
        matrix_grads[1],
        matrix_grads[2],
        matrix_grads[3],
        matrix_grads[4],
        matrix_grads[5],
        totals[1],
        totals[2],
        totals[3],
        totals[4],
        totals[5],
        totals[6],
        totals[7],
        totals[8],
        totals[9],
        stream_rms,
    )


def swap(value, axis):
    return lax.ppermute(value, axis, [(0, 1), (1, 0)])


def both(value, axis):
    return jnp.concatenate([value, swap(value, axis)], axis=0)


def dot(left, right, dims):
    return lax.dot_general(left, right, (dims, ((), ())), preferred_element_type=jnp.float32)


def in_order(own, other, core):
    first = jnp.where(core == 0, own, other)
    second = jnp.where(core == 0, other, own)
    return jnp.concatenate([first, second], axis=0)


def split_columns(weight, width, core):
    rows = weight.shape[0]
    blocks = weight.reshape(rows, -1, 2, width)
    own = lax.dynamic_index_in_dim(blocks, core, 2, keepdims=False).reshape(rows, -1)
    sent = lax.dynamic_index_in_dim(blocks, 1 - core, 2, keepdims=False).reshape(rows, -1)
    return own, sent


def spread(matrix, chips, halves):
    rows, columns = matrix.shape
    return matrix.reshape(chips, rows // chips, halves, columns // halves).transpose(0, 2, 1, 3)


def unspread(parts):
    chips, halves, rows, columns = parts.shape
    return parts.transpose(0, 2, 1, 3).reshape(chips * rows, halves * columns)


def norm_parts(values_in):
    mean_value = jnp.mean(values_in, axis=-1, keepdims=True)
    centered = values_in - mean_value
    variance = jnp.mean(centered * centered, axis=-1, keepdims=True)
    rstd = lax.rsqrt(variance + 1e-05)
    return centered * rstd, rstd


def norm_back(grad, xhat, rstd, gain):
    scaled = grad * gain
    inner = jnp.mean(scaled * xhat, axis=-1, keepdims=True)
    result = rstd * (scaled - jnp.mean(scaled, axis=-1, keepdims=True) - xhat * inner)
    return result, jnp.sum(grad * xhat, axis=0), jnp.sum(grad, axis=0)


def total_over(vector):
    vector = vector + swap(vector, "s")
    vector = vector + swap(vector, "x")
    vector = vector + lax.ppermute(vector, "z", [(0, 1), (1, 0), (2, 3), (3, 2)])
    return vector + lax.ppermute(vector, "z", [(0, 2), (2, 0), (1, 3), (3, 1)])


def pick(values, index, axis):
    return lax.dynamic_index_in_dim(values, index, axis, keepdims=False)


def add(left, right):
    return (left.astype(jnp.float32) + right.astype(jnp.float32)).astype(jnp.bfloat16)


def fold(values, axis, dim):
    index = lax.axis_index(axis)
    return add(pick(values, index, dim), swap(pick(values, 1 - index, dim), axis))


def fold_line(values):
    place = lax.axis_index("z")
    upper = (place >= 2).astype(jnp.int32)
    pairs = values.reshape((2, 2) + values.shape[1:])
    far = pick(pairs, 1 - upper, 0)
    far = add(far, lax.ppermute(far, "z", [(0, 1), (3, 2)]))
    near = add(pick(pairs, upper, 0), lax.ppermute(far, "z", [(1, 2), (2, 1)]))
    odd = place % 2
    other = lax.ppermute(pick(near, 1 - odd, 0), "z", [(0, 1), (1, 0), (2, 3), (3, 2)])
    return add(pick(near, odd, 0), other)


def scatter_sum(matrix, rows):
    columns = matrix.shape[1] // 2
    parts = matrix.reshape(4, 2, rows, 2 * columns)
    half = lax.axis_index("s")
    top = parts[:, :, : rows // 2]
    low = parts[:, :, rows // 2 :]
    kept = lax.dynamic_slice_in_dim(top, half * columns, columns, 3)
    sent = lax.dynamic_slice_in_dim(top, (1 - half) * columns, columns, 3)
    top = fold_line(fold(add(kept, swap(sent, "s")), "x", 1))
    low = fold_line(fold(low, "x", 1))
    kept = lax.dynamic_slice_in_dim(low, half * columns, columns, 1)
    sent = lax.dynamic_slice_in_dim(low, (1 - half) * columns, columns, 1)
    return top, add(kept, swap(sent, "s"))


def split_body(
    tokens,
    lengths,
    cotangent,
    query_weight,
    key_weight,
    value_weight,
    out_weight,
    up_weight,
    down_weight,
    query_bias,
    value_bias,
    out_bias,
    attn_gain,
    attn_shift,
    up_bias,
    down_bias,
    feed_gain,
    feed_shift,
):
    chips = lax.axis_size("z") * lax.axis_size("x")
    core = lax.axis_index("c")
    half = lax.axis_index("s")
    row_count, width = tokens.shape[1:]
    slots = 2 * row_count
    unit_block = down_weight.shape[0]
    units = up_bias.shape[0] // 2
    cols = width // 2
    heads = cols // HD

    small = [
        split_columns(weight, HD, core) for weight in (query_weight, key_weight, value_weight)
    ]
    large = split_columns(up_weight, unit_block, core)
    sent = swap(jnp.concatenate([part[1] for part in small] + [large[1]], axis=1), "c")
    kept = jnp.concatenate([part[0] for part in small] + [large[0]], axis=1)
    mine = in_order(kept, sent, core)
    rows = mine.shape[0]
    wide = cols // 2
    near = 3 * wide
    up_cols = large[0].shape[1]
    cut = up_cols // 2
    first_send = jnp.concatenate(
        [
            mine[:, :near].reshape(-1, 512),
            out_weight.reshape(-1, 512),
            mine[:, near : near + cut].reshape(-1, 512),
        ],
        axis=0,
    )
    second_send = jnp.concatenate(
        [mine[:, near + cut :].reshape(-1, 512), down_weight.reshape(-1, 512)], axis=0
    )
    near_rows = rows * near // 512
    out_rows = out_weight.size // 512
    cut_rows = rows * cut // 512
    first_all = lax.all_gather(first_send, ("z", "x", "s"), axis=0, tiled=False)
    second_all = lax.all_gather(second_send, ("z", "x", "s"), axis=0, tiled=False)
    first_all = first_all.reshape(chips, 2, -1, 512)
    second_all = second_all.reshape(chips, 2, -1, 512)
    near_all = first_all[:, :, :near_rows].reshape(chips, 2, rows, 3, wide)
    in_weight = near_all.transpose(0, 2, 1, 3, 4).reshape(width, 3 * cols)
    out_own = unspread(first_all[:, :, near_rows : near_rows + out_rows].reshape((chips, 2) + out_weight.shape))
    up_first = first_all[:, :, near_rows + out_rows :].reshape(chips, 2, rows, cut)
    up_second = second_all[:, :, :cut_rows].reshape(chips, 2, rows, cut)
    up_own = unspread(jnp.concatenate([up_first, up_second], axis=3))
    down_own = unspread(second_all[:, :, cut_rows:].reshape((chips, 2) + down_weight.shape))

    def to_sequence(values):
        own = lax.dynamic_index_in_dim(values, half, 0, keepdims=False)
        other = lax.dynamic_index_in_dim(values, 1 - half, 0, keepdims=False)
        return jnp.concatenate([own, swap(other, "s")], axis=0)

    def from_sequence(values):
        own = values[:row_count]
        other = swap(values[row_count:], "s")
        first = jnp.where(half == 0, own, other)
        second = jnp.where(half == 0, other, own)
        return jnp.stack([first, second], axis=0)

    tokens_own = to_sequence(tokens)
    cotangent_own = to_sequence(cotangent)
    tokens_both = both(tokens_own, "c")
    place = jnp.concatenate(
        [half * row_count + jnp.arange(row_count), (1 - half) * row_count + jnp.arange(row_count)]
    )
    length_own = lax.dynamic_slice_in_dim(lengths, half, 1, 0)
    length_both = both(length_own, "c")
    key_mask = place[None, :] < length_both[:, None]
    row_valid = (place < length_own[0]).astype(jnp.float32)[:, None]

    def halves_of(vector, block):
        return lax.dynamic_index_in_dim(vector.reshape(-1, 2, block), core, 1, keepdims=False).reshape(-1)

    query_part = halves_of(query_bias, HD).reshape(2, wide)
    value_part = halves_of(value_bias, HD).reshape(2, wide)
    in_bias = jnp.stack([query_part, jnp.zeros_like(query_part), value_part], axis=1).reshape(-1)
    projected = (dot(tokens_both, in_weight, ((1,), (0,))) + in_bias).astype(jnp.bfloat16)
    queries, keys, values = [
        jnp.concatenate(
            [projected[:, j * wide : (j + 1) * wide] for j in (i, i + 3)], axis=1
        ).reshape(2, slots, heads, HD)
        for i in range(3)
    ]
    scores = jnp.einsum("sqhd,skhd->shqk", queries, keys, preferred_element_type=jnp.float32) * 0.125
    scores = jnp.where(key_mask[:, None, None, :], scores, -1e30)
    exponent = jnp.exp(scores - jnp.max(scores, axis=-1, keepdims=True))
    soft_probs = exponent / jnp.sum(exponent, axis=-1, keepdims=True)
    probs_low = soft_probs.astype(jnp.bfloat16)
    heads_out = jnp.einsum("shqk,skhd->sqhd", probs_low, values, preferred_element_type=jnp.float32)
    heads_out = heads_out.reshape(2 * slots, cols).astype(jnp.bfloat16)
    heads_own = jnp.concatenate([heads_out[:slots], swap(heads_out[slots:], "c")], axis=1)
    out_both = both(out_own, "c")
    attention_out = dot(heads_own, out_both, ((1,), (0,))) + out_bias
    tokens_f32 = tokens_own.astype(jnp.float32)
    first_hat, first_rstd = norm_parts(tokens_f32 + attention_out)
    hidden = first_hat * attn_gain + attn_shift
    hidden_both = both(hidden.astype(jnp.bfloat16), "c")
    pre_act = dot(hidden_both, up_own, ((1,), (0,))) + halves_of(up_bias, unit_block)
    below = 0.5 * (1.0 + lax.erf(pre_act * 0.7071067811865476))
    slope = below + pre_act * (0.3989422804014327 * jnp.exp(-0.5 * pre_act * pre_act))
    slope = slope.astype(jnp.bfloat16)
    activation = (pre_act * below).astype(jnp.bfloat16)
    feed_part = dot(activation, down_own, ((1,), (0,)))
    feed_out = (
        feed_part[:slots]
        + swap(feed_part[slots:].astype(jnp.bfloat16), "c").astype(jnp.float32)
        + down_bias
    )
    second_hat, second_rstd = norm_parts(hidden + feed_out)
    mixed = from_sequence((second_hat * feed_gain + feed_shift).astype(jnp.bfloat16))
    stats = jnp.stack(
        [
            jnp.sum(row_valid * tokens_f32 * tokens_f32),
            jnp.sum(row_valid * attention_out * attention_out),
            jnp.sum(row_valid * feed_out * feed_out),
            jnp.sum(row_valid) * width,
        ]
    )

    out_grad = cotangent_own.astype(jnp.float32) * row_valid
    second_grad, feed_gain_grad, feed_shift_grad = norm_back(
        out_grad, second_hat, second_rstd, feed_gain
    )
    feed_low = second_grad.astype(jnp.bfloat16)
    down_bias_grad = jnp.sum(feed_low, axis=0, dtype=jnp.float32)
    feed_both = both(feed_low, "c")
    down_grad = dot(activation, feed_both, ((0,), (0,))).astype(jnp.bfloat16)
    act_grad = dot(feed_both, down_own, ((1,), (1,))).astype(jnp.bfloat16)
    pre_grad = (act_grad.astype(jnp.float32) * slope.astype(jnp.float32)).astype(jnp.bfloat16)
    up_grad = dot(hidden_both, pre_grad, ((0,), (0,))).astype(jnp.bfloat16)
    up_bias_grad = jnp.sum(pre_grad, axis=0, dtype=jnp.float32)
    down_top, down_low = scatter_sum(down_grad, down_weight.shape[0])
    up_top, up_low = scatter_sum(up_grad, rows)
    hidden_part = dot(pre_grad, up_own, ((1,), (1,)))
    hidden_grad = (
        hidden_part[:slots]
        + swap(hidden_part[slots:].astype(jnp.bfloat16), "c").astype(jnp.float32)
        + second_grad
    )
    first_grad, attn_gain_grad, attn_shift_grad = norm_back(
        hidden_grad, first_hat, first_rstd, attn_gain
    )
    attn_low = first_grad.astype(jnp.bfloat16)
    out_bias_grad = jnp.sum(attn_low, axis=0, dtype=jnp.float32)
    heads_grad = dot(attn_low, out_both, ((1,), (1,))).astype(jnp.bfloat16)
    heads_grad = jnp.concatenate([heads_grad[:, :cols], swap(heads_grad[:, cols:], "c")], axis=0)
    heads_grad = heads_grad.reshape(2, slots, heads, HD)
    out_grad_part = dot(heads_own, attn_low, ((0,), (0,)))
    out_grad_own = (
        out_grad_part[:cols]
        + swap(out_grad_part[cols:].astype(jnp.bfloat16), "c").astype(jnp.float32)
    ).astype(jnp.bfloat16)
    value_low = jnp.einsum(
        "shqk,sqhd->skhd", probs_low, heads_grad, preferred_element_type=jnp.float32
    )
    prob_grad = jnp.einsum(
        "sqhd,skhd->shqk", heads_grad, values, preferred_element_type=jnp.float32
    )
    inner = jnp.sum(soft_probs * prob_grad, axis=-1, keepdims=True)
    score_grad = (soft_probs * (prob_grad - inner)).astype(jnp.bfloat16)
    query_low = 0.125 * jnp.einsum(
        "shqk,skhd->sqhd", score_grad, keys, preferred_element_type=jnp.float32
    )
    key_low = 0.125 * jnp.einsum(
        "shqk,sqhd->skhd", score_grad, queries, preferred_element_type=jnp.float32
    )
    low_parts = [
        part.reshape(2 * slots, cols).astype(jnp.bfloat16) for part in (query_low, key_low, value_low)
    ]
    in_low = jnp.concatenate(
        [part[:, i * wide : (i + 1) * wide] for i in range(2) for part in low_parts], axis=1
    )
    in_grad = dot(tokens_both, in_low, ((0,), (0,))).astype(jnp.bfloat16)
    out_top, out_low = scatter_sum(out_grad_own, out_weight.shape[0])
    in_top, in_below = scatter_sum(in_grad, rows)
    in_bias_grad = jnp.sum(in_low, axis=0, dtype=jnp.float32)
    tokens_part = dot(in_low, in_weight, ((1,), (1,)))
    tokens_grad = (
        tokens_part[:slots]
        + swap(tokens_part[slots:].astype(jnp.bfloat16), "c").astype(jnp.float32)
        + first_grad
    )
    tokens_grad = from_sequence(tokens_grad.astype(jnp.bfloat16))

    shared = jnp.concatenate(
        [
            down_bias_grad,
            feed_gain_grad,
            feed_shift_grad,
            out_bias_grad,
            attn_gain_grad,
            attn_shift_grad,
            jnp.pad(stats, (0, 124)),
        ]
    )
    own_sums = total_over(
        jnp.concatenate(
            [
                shared,
                up_bias_grad,
                in_bias_grad[:wide],
                in_bias_grad[3 * wide : 4 * wide],
                in_bias_grad[2 * wide : 3 * wide],
                in_bias_grad[5 * wide :],
            ]
        )
    )
    other_sums = swap(own_sums, "c")
    count = shared.shape[0]
    shared = own_sums[:count] + other_sums[:count]
    down_bias_grad, feed_gain_grad, feed_shift_grad, out_bias_grad, attn_gain_grad, attn_shift_grad = [
        shared[i * width : (i + 1) * width] for i in range(6)
    ]
    stats = shared[6 * width : 6 * width + 4]

    def interleave(start, size, block):
        own = own_sums[start : start + size].reshape(-1, block)
        other = other_sums[start : start + size].reshape(-1, block)
        first = jnp.where(core == 0, own, other)
        second = jnp.where(core == 0, other, own)
        return jnp.stack([first, second], axis=1).reshape(-1)

    up_bias_grad = interleave(count, units, unit_block)
    query_bias_grad = interleave(count + units, cols, HD)
    value_bias_gradient = interleave(count + units + cols, cols, HD)
    stream_rms = jnp.sqrt(stats[:3] / stats[3])

    down_weight_grad = jnp.concatenate([down_top, down_low], axis=0).astype(jnp.float32)
    out_weight_grad = jnp.concatenate([out_top, out_low], axis=0).astype(jnp.float32)
    top = jnp.concatenate([in_top, up_top], axis=1)
    low = jnp.concatenate([in_below, up_low], axis=1)
    own = jnp.where(core == 0, top, low)
    other = swap(jnp.where(core == 0, low, top), "c")

    def merge(start, size, block):
        one = own[:, start : start + size].reshape(rows // 2, -1, block)
        two = other[:, start : start + size].reshape(rows // 2, -1, block)
        first = jnp.where(core == 0, one, two)
        second = jnp.where(core == 0, two, one)
        return jnp.stack([first, second], axis=2).reshape(rows // 2, -1).astype(jnp.float32)

    query_weight_grad = merge(0, wide, HD)
    key_weight_grad = merge(wide, wide, HD)
    value_weight_grad = merge(2 * wide, wide, HD)
    up_weight_grad = merge(near, up_cols, unit_block)
    return (
        mixed,
        tokens_grad,
        query_weight_grad,
        key_weight_grad,
        value_weight_grad,
        out_weight_grad,
        up_weight_grad,
        down_weight_grad,
        query_bias_grad,
        value_bias_gradient,
        out_bias_grad,
        attn_gain_grad,
        attn_shift_grad,
        up_bias_grad,
        down_bias_grad,
        feed_gain_grad,
        feed_shift_grad,
        stream_rms,
    )


def solution(mesh):
    devices = mesh.devices
    dp_count, seq_count = devices.shape
    split = seq_count == 2 and dp_count == 16
    if split:
        inner = jax.sharding.Mesh(devices.reshape(4, 2, 2, seq_count), ("z", "x", "c", "s"))
        dp, seq, body = ("z", "x", "c"), "s", split_body
    else:
        inner, dp, seq, body = mesh, "dp", "seq", general_body
    weights = (P(dp, seq),) * 6
    vectors = (P(),) * 9
    rows = P(dp, seq, None)
    in_specs = (rows, P(dp), rows) + weights + vectors
    out_specs = (rows, rows) + weights + vectors + (P(),)
    return jax.shard_map(body, mesh=inner, in_specs=in_specs, out_specs=out_specs, check_vma=False)
```

```python
from functools import partial
import math

import jax
import jax.numpy as jnp
from jax import lax
from jax.experimental import pallas as pl
from jax.experimental.pallas import tpu as pltpu
from jax.sharding import PartitionSpec as P

HD = 64


def layer_norm(values_in, gain_vector, shift_vector):
    mean_value = jnp.mean(values_in, axis=-1, keepdims=True)
    centered = values_in - mean_value
    variance = jnp.mean(centered * centered, axis=-1, keepdims=True)
    return centered * lax.rsqrt(variance + 1e-05) * gain_vector + shift_vector


def gather_weights(first, second, third, fourth, fifth, sixth):
    part = (
        lax.all_gather(first, "dp", axis=0, tiled=True),
        lax.all_gather(second, "dp", axis=0, tiled=True),
        lax.all_gather(third, "dp", axis=0, tiled=True),
        lax.all_gather(fourth, "dp", axis=0, tiled=True),
        lax.all_gather(fifth, "dp", axis=0, tiled=True),
        lax.all_gather(sixth, "dp", axis=0, tiled=True),
    )
    return (
        lax.all_gather(part[0], "seq", axis=1, tiled=True),
        lax.all_gather(part[1], "seq", axis=1, tiled=True),
        lax.all_gather(part[2], "seq", axis=1, tiled=True),
        lax.all_gather(part[3], "seq", axis=1, tiled=True),
        lax.all_gather(part[4], "seq", axis=1, tiled=True),
        lax.all_gather(part[5], "seq", axis=1, tiled=True),
    )


def reduce_grads(first, second, third, fourth, fifth, sixth):
    part = (
        lax.psum_scatter(first.astype(jnp.bfloat16), "seq", scatter_dimension=1, tiled=True).astype(
            jnp.float32
        ),
        lax.psum_scatter(
            second.astype(jnp.bfloat16), "seq", scatter_dimension=1, tiled=True
        ).astype(jnp.float32),
        lax.psum_scatter(third.astype(jnp.bfloat16), "seq", scatter_dimension=1, tiled=True).astype(
            jnp.float32
        ),
        lax.psum_scatter(
            fourth.astype(jnp.bfloat16), "seq", scatter_dimension=1, tiled=True
        ).astype(jnp.float32),
        lax.psum_scatter(fifth.astype(jnp.bfloat16), "seq", scatter_dimension=1, tiled=True).astype(
            jnp.float32
        ),
        lax.psum_scatter(sixth.astype(jnp.bfloat16), "seq", scatter_dimension=1, tiled=True).astype(
            jnp.float32
        ),
    )
    return (
        lax.psum_scatter(
            part[0].astype(jnp.bfloat16), "dp", scatter_dimension=0, tiled=True
        ).astype(jnp.float32),
        lax.psum_scatter(
            part[1].astype(jnp.bfloat16), "dp", scatter_dimension=0, tiled=True
        ).astype(jnp.float32),
        lax.psum_scatter(
            part[2].astype(jnp.bfloat16), "dp", scatter_dimension=0, tiled=True
        ).astype(jnp.float32),
        lax.psum_scatter(
            part[3].astype(jnp.bfloat16), "dp", scatter_dimension=0, tiled=True
        ).astype(jnp.float32),
        lax.psum_scatter(
            part[4].astype(jnp.bfloat16), "dp", scatter_dimension=0, tiled=True
        ).astype(jnp.float32),
        lax.psum_scatter(
            part[5].astype(jnp.bfloat16), "dp", scatter_dimension=0, tiled=True
        ).astype(jnp.float32),
    )


def block_layout(seq_count, row_count, head_count):
    block_seqs = math.gcd(seq_count, max(1, 512 // row_count))
    group_heads = math.gcd(head_count, 4)
    return (block_seqs, seq_count // block_seqs, group_heads, head_count // group_heads)


def head_slice(block_part, offset, group_width, group_heads):
    sliced = lax.dynamic_slice_in_dim(block_part, offset, group_width, 2)
    return sliced.reshape(sliced.shape[0], sliced.shape[1], group_heads, HD)


def attention_forward(queries, key_all, value_all, key_mask):
    seq_count, row_count, feature_total = queries.shape
    slot_count = key_all.shape[1]
    block_seqs, block_count, group_heads, group_count = block_layout(
        seq_count, row_count, feature_total // HD
    )
    group_width = group_heads * HD

    def seq_block(inputs):
        query_part, key_part, value_part, mask_part = inputs

        def head_block(group_index):
            offset = group_index * group_width
            query_heads = head_slice(query_part, offset, group_width, group_heads)
            key_heads = head_slice(key_part, offset, group_width, group_heads)
            value_heads = head_slice(value_part, offset, group_width, group_heads)
            scores = (
                jnp.einsum(
                    "brhd,bkhd->bhrk", query_heads, key_heads, preferred_element_type=jnp.float32
                )
                * 0.125
            )
            scores = jnp.where(mask_part[:, None, None, :], scores, -1e30)
            row_max = jnp.max(scores, axis=-1, keepdims=True)
            exponent = jnp.exp(scores - row_max)
            row_total = jnp.sum(exponent, axis=-1, keepdims=True)
            soft_probs = (exponent / row_total).astype(jnp.bfloat16)
            heads_out = jnp.einsum(
                "bhrk,bkhd->brhd", soft_probs, value_heads, preferred_element_type=jnp.float32
            )
            log_total = (row_max + jnp.log(row_total))[..., 0]
            return (heads_out.reshape(block_seqs, row_count, group_width), log_total)

        return lax.map(head_block, jnp.arange(group_count))

    outputs, log_totals = lax.map(
        seq_block,
        (
            queries.reshape(block_count, block_seqs, row_count, feature_total),
            key_all.reshape(block_count, block_seqs, slot_count, feature_total),
            value_all.reshape(block_count, block_seqs, slot_count, feature_total),
            key_mask.reshape(block_count, block_seqs, slot_count),
        ),
    )
    mixed_heads = outputs.transpose(0, 2, 3, 1, 4).reshape(seq_count, row_count, feature_total)
    return (mixed_heads, log_totals)


def attention_backward(queries, key_all, value_all, key_mask, heads_grad, log_totals):
    seq_count, row_count, feature_total = queries.shape
    slot_count = key_all.shape[1]
    block_seqs, block_count, group_heads, group_count = block_layout(
        seq_count, row_count, feature_total // HD
    )
    group_width = group_heads * HD

    def seq_block(inputs):
        query_part, key_part, value_part, mask_part, grad_part, total_part = inputs

        def head_block(group_index):
            offset = group_index * group_width
            query_heads = head_slice(query_part, offset, group_width, group_heads)
            key_heads = head_slice(key_part, offset, group_width, group_heads)
            value_heads = head_slice(value_part, offset, group_width, group_heads)
            grad_heads = head_slice(grad_part, offset, group_width, group_heads)
            log_total = lax.dynamic_index_in_dim(total_part, group_index, 0, keepdims=False)
            scores = (
                jnp.einsum(
                    "brhd,bkhd->bhrk", query_heads, key_heads, preferred_element_type=jnp.float32
                )
                * 0.125
            )
            scores = jnp.where(mask_part[:, None, None, :], scores, -1e30)
            soft_probs = jnp.exp(scores - log_total[..., None])
            value_grad = jnp.einsum(
                "bhrk,brhd->bkhd",
                soft_probs.astype(jnp.bfloat16),
                grad_heads,
                preferred_element_type=jnp.float32,
            )
            prob_grad = jnp.einsum(
                "brhd,bkhd->bhrk", grad_heads, value_heads, preferred_element_type=jnp.float32
            )
            inner = jnp.sum(soft_probs * prob_grad, axis=-1, keepdims=True)
            score_grad = (soft_probs * (prob_grad - inner)).astype(jnp.bfloat16)
            query_grad = (
                jnp.einsum(
                    "bhrk,bkhd->brhd", score_grad, key_heads, preferred_element_type=jnp.float32
                )
                * 0.125
            )
            key_grad = (
                jnp.einsum(
                    "bhrk,brhd->bkhd", score_grad, query_heads, preferred_element_type=jnp.float32
                )
                * 0.125
            )
            return (
                query_grad.reshape(block_seqs, row_count, group_width),
                key_grad.reshape(block_seqs, slot_count, group_width),
                value_grad.reshape(block_seqs, slot_count, group_width),
            )

        return lax.map(head_block, jnp.arange(group_count))

    query_blocks, key_blocks, value_block_list = lax.map(
        seq_block,
        (
            queries.reshape(block_count, block_seqs, row_count, feature_total),
            key_all.reshape(block_count, block_seqs, slot_count, feature_total),
            value_all.reshape(block_count, block_seqs, slot_count, feature_total),
            key_mask.reshape(block_count, block_seqs, slot_count),
            heads_grad.reshape(block_count, block_seqs, row_count, feature_total),
            log_totals,
        ),
    )
    query_grad = query_blocks.transpose(0, 2, 3, 1, 4).reshape(seq_count, row_count, feature_total)
    key_grad = key_blocks.transpose(0, 2, 3, 1, 4).reshape(seq_count, slot_count, feature_total)
    value_grad = value_block_list.transpose(0, 2, 3, 1, 4).reshape(
        seq_count, slot_count, feature_total
    )
    return (query_grad, key_grad, value_grad)


def general_body(
    tokens,
    lengths,
    cotangent,
    query_weight,
    key_weight,
    value_weight,
    out_weight,
    up_weight,
    down_weight,
    query_bias,
    value_bias,
    out_bias,
    attn_gain,
    attn_shift,
    up_bias,
    down_bias,
    feed_gain,
    feed_shift,
):
    seq_count, row_count, feature_total = tokens.shape
    slot_count = row_count * lax.axis_size("seq")
    token_count = seq_count * row_count
    whole = gather_weights(
        query_weight, key_weight, value_weight, out_weight, up_weight, down_weight
    )
    full_query, full_key, full_value, full_out, full_up, full_down = whole
    flat_tokens = tokens.reshape(token_count, feature_total)
    queries = (
        jnp.dot(flat_tokens, full_query, preferred_element_type=jnp.float32) + query_bias
    ).astype(jnp.bfloat16)
    key_rows = jnp.dot(flat_tokens, full_key, preferred_element_type=jnp.float32).astype(
        jnp.bfloat16
    )
    value_rows = (
        jnp.dot(flat_tokens, full_value, preferred_element_type=jnp.float32) + value_bias
    ).astype(jnp.bfloat16)
    first_slot = lax.axis_index("seq") * row_count
    key_mask = jnp.arange(slot_count)[None, :] < lengths[:, None]
    row_valid = ((first_slot + jnp.arange(row_count))[None, :] < lengths[:, None]).astype(
        jnp.float32
    )
    row_valid = row_valid.reshape(token_count, 1)
    query_blocks = queries.reshape(seq_count, row_count, feature_total)
    key_blocks = key_rows.reshape(seq_count, row_count, feature_total)
    value_block_list = value_rows.reshape(seq_count, row_count, feature_total)
    key_all, value_all = (
        lax.all_gather(key_blocks, "seq", axis=1, tiled=True),
        lax.all_gather(value_block_list, "seq", axis=1, tiled=True),
    )
    mixed_heads, log_totals = attention_forward(query_blocks, key_all, value_all, key_mask)
    heads_low = mixed_heads.reshape(token_count, feature_total).astype(jnp.bfloat16)
    attention_out = jnp.dot(heads_low, full_out, preferred_element_type=jnp.float32) + out_bias
    tokens_f32 = flat_tokens.astype(jnp.float32)
    first_sum = tokens_f32 + attention_out
    hidden, first_pull = jax.vjp(layer_norm, first_sum, attn_gain, attn_shift)
    hidden_low = hidden.astype(jnp.bfloat16)
    pre_act = jnp.dot(hidden_low, full_up, preferred_element_type=jnp.float32) + up_bias
    gelu_out, gelu_pull = jax.vjp(partial(jax.nn.gelu, approximate=False), pre_act)
    activation = gelu_out.astype(jnp.bfloat16)
    feed_out = jnp.dot(activation, full_down, preferred_element_type=jnp.float32) + down_bias
    result, second_pull = jax.vjp(layer_norm, hidden + feed_out, feed_gain, feed_shift)
    mixed = result.astype(jnp.bfloat16).reshape(seq_count, row_count, feature_total)
    partial_stats = jnp.stack(
        [
            jnp.sum(row_valid * tokens_f32 * tokens_f32),
            jnp.sum(row_valid * attention_out * attention_out),
            jnp.sum(row_valid * feed_out * feed_out),
            jnp.sum(row_valid) * feature_total,
        ]
    )
    back_weights = gather_weights(
        query_weight, key_weight, value_weight, out_weight, up_weight, down_weight
    )
    back_query, back_key, back_value, back_out, back_up, back_down = back_weights
    out_grad = cotangent.reshape(token_count, feature_total).astype(jnp.float32) * row_valid
    second_grad, feed_gain_grad, feed_shift_grad = second_pull(out_grad)
    feed_low = second_grad.astype(jnp.bfloat16)
    down_weight_grad = jnp.einsum(
        "nf,nd->fd", activation, feed_low, preferred_element_type=jnp.float32
    )
    down_bias_grad = jnp.sum(feed_low, axis=0, dtype=jnp.float32)
    act_grad = jnp.einsum(
        "nd,fd->nf", feed_low, back_down, preferred_element_type=jnp.float32
    ).astype(jnp.bfloat16)
    pre_grad = gelu_pull(act_grad.astype(jnp.float32))[0].astype(jnp.bfloat16)
    up_weight_grad = jnp.einsum(
        "nd,nf->df", hidden_low, pre_grad, preferred_element_type=jnp.float32
    )
    up_bias_grad = jnp.sum(pre_grad, axis=0, dtype=jnp.float32)
    hidden_grad = (
        jnp.einsum("nf,df->nd", pre_grad, back_up, preferred_element_type=jnp.float32) + second_grad
    )
    first_grad, attn_gain_grad, attn_shift_grad = first_pull(hidden_grad)
    attn_low = first_grad.astype(jnp.bfloat16)
    out_weight_grad = jnp.einsum(
        "nd,ne->de", heads_low, attn_low, preferred_element_type=jnp.float32
    )
    out_bias_grad = jnp.sum(attn_low, axis=0, dtype=jnp.float32)
    heads_grad = jnp.einsum(
        "ne,de->nd", attn_low, back_out, preferred_element_type=jnp.float32
    ).astype(jnp.bfloat16)
    heads_grad = heads_grad.reshape(seq_count, row_count, feature_total)
    query_grad, key_part_grad, value_part_grad = attention_backward(
        query_blocks, key_all, value_all, key_mask, heads_grad, log_totals
    )
    key_sum, value_sum = (
        lax.psum_scatter(
            key_part_grad.astype(jnp.bfloat16), "seq", scatter_dimension=1, tiled=True
        ).astype(jnp.float32),
        lax.psum_scatter(
            value_part_grad.astype(jnp.bfloat16), "seq", scatter_dimension=1, tiled=True
        ).astype(jnp.float32),
    )
    query_low = query_grad.reshape(token_count, feature_total).astype(jnp.bfloat16)
    key_low = key_sum.reshape(token_count, feature_total).astype(jnp.bfloat16)
    value_low = value_sum.reshape(token_count, feature_total).astype(jnp.bfloat16)
    query_weight_grad = jnp.einsum(
        "nd,ne->de", flat_tokens, query_low, preferred_element_type=jnp.float32
    )
    key_weight_grad = jnp.einsum(
        "nd,ne->de", flat_tokens, key_low, preferred_element_type=jnp.float32
    )
    value_weight_grad = jnp.einsum(
        "nd,ne->de", flat_tokens, value_low, preferred_element_type=jnp.float32
    )
    query_bias_grad = jnp.sum(query_low, axis=0, dtype=jnp.float32)
    value_bias_gradient = jnp.sum(value_low, axis=0, dtype=jnp.float32)
    tokens_grad = (
        jnp.einsum("ne,de->nd", query_low, back_query, preferred_element_type=jnp.float32)
        + jnp.einsum("ne,de->nd", key_low, back_key, preferred_element_type=jnp.float32)
        + jnp.einsum("ne,de->nd", value_low, back_value, preferred_element_type=jnp.float32)
        + first_grad
    )
    tokens_grad = tokens_grad.astype(jnp.bfloat16).reshape(seq_count, row_count, feature_total)
    matrix_grads = reduce_grads(
        query_weight_grad,
        key_weight_grad,
        value_weight_grad,
        out_weight_grad,
        up_weight_grad,
        down_weight_grad,
    )
    totals = lax.psum(
        (
            partial_stats,
            query_bias_grad,
            value_bias_gradient,
            out_bias_grad,
            attn_gain_grad,
            attn_shift_grad,
            up_bias_grad,
            down_bias_grad,
            feed_gain_grad,
            feed_shift_grad,
        ),
        ("dp", "seq"),
    )
    stream_rms = jnp.sqrt(totals[0][:3] / totals[0][3])
    return (
        mixed,
        tokens_grad,
        matrix_grads[0],
        matrix_grads[1],
        matrix_grads[2],
        matrix_grads[3],
        matrix_grads[4],
        matrix_grads[5],
        totals[1],
        totals[2],
        totals[3],
        totals[4],
        totals[5],
        totals[6],
        totals[7],
        totals[8],
        totals[9],
        stream_rms,
    )


def swap(value, axis):
    return lax.ppermute(value, axis, [(0, 1), (1, 0)])


def both(value, axis):
    return jnp.concatenate([value, swap(value, axis)], axis=0)


def in_order(own, other, index):
    return jnp.where(index == 0, jnp.stack([own, other]), jnp.stack([other, own]))


def split_columns(weight, width, core):
    rows = weight.shape[0]
    blocks = weight.reshape(rows, -1, 2, width)
    return pick(blocks, core, 2).reshape(rows, -1), pick(blocks, 1 - core, 2).reshape(rows, -1)


def pick(values, index, axis):
    return lax.dynamic_index_in_dim(values, index, axis, keepdims=False)


def add(left, right):
    return (left.astype(jnp.float32) + right.astype(jnp.float32)).astype(jnp.bfloat16)


def total_over(vector):
    vector = vector + swap(vector, "s")
    vector = vector + swap(vector, "x")
    vector = vector + lax.ppermute(vector, "z", [(0, 1), (1, 0), (2, 3), (3, 2)])
    return vector + lax.ppermute(vector, "z", [(0, 2), (2, 0), (1, 3), (3, 1)])


def fold(values, axis, dim):
    index = lax.axis_index(axis)
    return add(pick(values, index, dim), swap(pick(values, 1 - index, dim), axis))


def fold_line(values):
    place = lax.axis_index("z")
    upper = (place >= 2).astype(jnp.int32)
    pairs = values.reshape((2, 2) + values.shape[1:])
    far = pick(pairs, 1 - upper, 0)
    far = add(far, lax.ppermute(far, "z", [(0, 1), (3, 2)]))
    near = add(pick(pairs, upper, 0), lax.ppermute(far, "z", [(1, 2), (2, 1)]))
    odd = place % 2
    other = lax.ppermute(pick(near, 1 - odd, 0), "z", [(0, 1), (1, 0), (2, 3), (3, 2)])
    return add(pick(near, odd, 0), other)


def gather_line(value):
    place = lax.axis_index("z")
    other = lax.ppermute(value, "z", [(0, 1), (1, 0), (2, 3), (3, 2)])
    pair = in_order(value, other, place % 2)
    crossed = lax.ppermute(pair, "z", [(1, 2), (2, 1)])
    handed = lax.ppermute(crossed, "z", [(1, 0), (2, 3)])
    far = jnp.where((place == 1) | (place == 2), crossed, handed)
    whole = in_order(pair, far, (place >= 2).astype(jnp.int32))
    return whole.reshape((4,) + value.shape)


def gather_two(value, axis):
    return in_order(value, swap(value, axis), lax.axis_index(axis))


def scatter_sum(send, keep):
    top = add(keep[0], swap(send[0], "s"))
    low = add(keep[1], swap(send[1], "x"))
    top = fold_line(fold(top, "x", 1))
    low = fold(fold_line(low), "s", 0)
    return jnp.concatenate([top, low], axis=-1)


PAIR = 2 * HD
LIMIT = 56 * 1024 * 1024


def kernel_params(steps):
    return pltpu.CompilerParams(
        dimension_semantics=("arbitrary",) * steps, vmem_limit_bytes=LIMIT
    )


def product(left, right, left_dim, right_dim):
    return lax.dot_general(
        left, right, (((left_dim,), (right_dim,)), ((), ())), preferred_element_type=jnp.float32
    )


def key_bias(facts_ref, slots):
    place = lax.broadcasted_iota(jnp.int32, (slots, 1), 0) + facts_ref[2]
    place = jnp.where(place >= slots, place - slots, place)
    return jnp.where(place < facts_ref[pl.program_id(0)], 0.0, -1e30)


def head_lanes(value, head):
    lane = lax.broadcasted_iota(jnp.int32, value.shape, 1)
    return jnp.where((lane >= HD) == (head == 1), value, jnp.zeros_like(value))


def turned(value):
    return value.astype(jnp.float32).T


def attend_kernel(facts_ref, query_ref, key_ref, value_ref, out_ref, total_ref):
    slots = key_ref.shape[0]
    bias = key_bias(facts_ref, slots)
    query = query_ref[...] * jnp.bfloat16(0.125)
    key = key_ref[...]
    value_t = turned(value_ref[...]).astype(jnp.bfloat16)
    outs = []
    for head in range(2):
        scores = product(key, head_lanes(query, head), 1, 1) + bias
        peak = jnp.max(scores, axis=0, keepdims=True)
        weight = jnp.exp(scores - peak)
        total = jnp.sum(weight, axis=0, keepdims=True)
        part = product(value_t[head * HD : (head + 1) * HD], weight.astype(jnp.bfloat16), 1, 0)
        outs.append(part * (1.0 / total))
        total_ref[0, 0, head : head + 1, :] = peak + jnp.log(total)
    out_ref[...] = jnp.concatenate(outs, axis=0).T.astype(jnp.bfloat16)


def attend_back_kernel(
    facts_ref, query_ref, key_ref, value_ref, grad_ref, total_ref, low_ref, sums_ref
):
    slots = key_ref.shape[0]
    bias = key_bias(facts_ref, slots)
    query = query_ref[...] * jnp.bfloat16(0.125)
    key = key_ref[...]
    value = value_ref[...]
    grad = grad_ref[...]
    key_t = turned(key).astype(jnp.bfloat16)
    lane = lax.broadcasted_iota(jnp.int32, (slots, PAIR), 1)
    query_parts, key_parts, value_parts = [], [], []
    for head in range(2):
        scores = product(key, head_lanes(query, head), 1, 1) + bias
        soft = jnp.exp(scores - total_ref[0, 0, head : head + 1, :])
        value_parts.append(product(soft.astype(jnp.bfloat16), grad, 1, 0))
        change = product(value, head_lanes(grad, head), 1, 1)
        inner = jnp.sum(soft * change, axis=0, keepdims=True)
        change = (soft * (change - inner)).astype(jnp.bfloat16)
        key_parts.append(product(change, query, 1, 0))
        query_parts.append(product(key_t[head * HD : (head + 1) * HD], change, 1, 0))
    pair = pl.program_id(2)
    groups = low_ref.shape[1] // 3
    query_low = (jnp.concatenate(query_parts, axis=0) * 0.125).T
    key_low = jnp.where(lane < HD, key_parts[0], key_parts[1])
    value_low = jnp.where(lane < HD, value_parts[0], value_parts[1])
    for place, part in enumerate((query_low, key_low, value_low)):
        start = pl.multiple_of(place * groups + pair * PAIR, PAIR)
        low = part.astype(jnp.bfloat16)
        low_ref[:, pl.ds(start, PAIR)] = low
        sums_ref[0, :, pl.ds(start, PAIR)] = jnp.sum(
            low.astype(jnp.float32), axis=0, keepdims=True
        )


def attention_specs(slots, pairs):
    def at(part):
        return pl.BlockSpec(
            (slots, PAIR), lambda b, g, p, *_: (b, g * 3 * pairs + part * pairs + p)
        )

    heads = pl.BlockSpec((slots, PAIR), lambda b, g, p, *_: (b, g * pairs + p))
    totals = pl.BlockSpec((1, 1, 2, slots), lambda b, g, p, *_: (b, g * pairs + p, 0, 0))
    return [at(0), at(1), at(2)], heads, totals


def attend(facts, projected, slots):
    pairs = projected.shape[1] // (6 * PAIR)
    inputs, heads, totals = attention_specs(slots, pairs)
    rows = projected.shape[0]
    return pl.pallas_call(
        attend_kernel,
        grid_spec=pltpu.PrefetchScalarGridSpec(
            num_scalar_prefetch=1,
            grid=(2, 2, pairs),
            in_specs=inputs,
            out_specs=[heads, totals],
        ),
        out_shape=[
            jax.ShapeDtypeStruct((rows, 2 * pairs * PAIR), jnp.bfloat16),
            jax.ShapeDtypeStruct((2, 2 * pairs, 2, slots), jnp.float32),
        ],
        compiler_params=kernel_params(3),
        name="attend",
    )(facts, projected, projected, projected)


def attend_back(facts, projected, heads_grad, totals_in, slots):
    pairs = projected.shape[1] // (6 * PAIR)
    inputs, heads, totals = attention_specs(slots, pairs)
    return pl.pallas_call(
        attend_back_kernel,
        grid_spec=pltpu.PrefetchScalarGridSpec(
            num_scalar_prefetch=1,
            grid=(2, 2, pairs),
            in_specs=inputs + [heads, totals],
            out_specs=[
                pl.BlockSpec((slots, 3 * pairs * PAIR), lambda b, g, p, *_: (b, g)),
                pl.BlockSpec((1, 1, 3 * pairs * PAIR), lambda b, g, p, *_: (b, 0, g)),
            ],
        ),
        out_shape=[
            jax.ShapeDtypeStruct(projected.shape, jnp.bfloat16),
            jax.ShapeDtypeStruct((2, 1, projected.shape[1]), jnp.float32),
        ],
        compiler_params=kernel_params(3),
        name="attend_back",
    )(facts, projected, projected, projected, heads_grad, totals_in)


def call(kernel, name, grid, inputs, outputs, shapes, facts, *args):
    return pl.pallas_call(
        kernel,
        grid_spec=pltpu.PrefetchScalarGridSpec(
            num_scalar_prefetch=1, grid=grid, in_specs=inputs, out_specs=outputs
        ),
        out_shape=shapes,
        compiler_params=kernel_params(len(grid)),
        name=name,
    )(facts, *args)


def block(shape, *index):
    def at(*grid_and_facts):
        return tuple(entry(*grid_and_facts) if callable(entry) else entry for entry in index)

    return pl.BlockSpec(shape, at)


def whole(array):
    zeros = (0,) * array.ndim
    return pl.BlockSpec(array.shape, lambda *_: zeros)


def first(i, *_):
    return i


def like(shape, dtype):
    return jax.ShapeDtypeStruct(shape, dtype)


def near_rows(top, low):
    pieces = []
    for z in range(top.shape[2]):
        for x in range(2):
            pieces += [top[0, x, z], low[x, z, 0]]
    return jnp.concatenate(pieces, axis=0)


def project_kernel(facts_ref, rows_ref, top_ref, low_ref, bias_ref, out_ref):
    weight = near_rows(top_ref[...], low_ref[...])
    out_ref[...] = (product(rows_ref[...], weight, 1, 0) + bias_ref[...]).astype(jnp.bfloat16)


def project(facts, rows, top, low, bias, wide):
    count, width = rows.shape
    steps = 3
    return call(
        project_kernel,
        "project",
        (2 * steps,),
        [
            whole(rows),
            block((1,) + top.shape[1:4] + (wide,), lambda i, *_: i // steps, 0, 0, 0, lambda i, *_: i % steps),
            block(low.shape[:2] + (1, low.shape[3], wide), 0, 0, lambda i, *_: i // steps, 0, lambda i, *_: i % steps),
            block((1, wide), 0, first),
        ],
        block((count, wide), 0, first),
        like((count, 2 * steps * wide), jnp.bfloat16),
        facts,
        rows,
        top,
        low,
        bias[None],
    )


def valid_rows(facts_ref, count, slots):
    place = lax.broadcasted_iota(jnp.int32, (count, 1), 0) + pl.program_id(0) * count + facts_ref[2]
    place = jnp.where(place >= slots, place - slots, place)
    return (place < facts_ref[0]).astype(jnp.float32)


def add_rows(sums_ref, rows):
    total = jnp.concatenate([jnp.sum(part, axis=0, keepdims=True) for part in rows], axis=0)
    total = jnp.concatenate([total, jnp.zeros((8 - len(rows), total.shape[1]), jnp.float32)], axis=0)

    @pl.when(pl.program_id(0) == 0)
    def _():
        sums_ref[...] = total

    @pl.when(pl.program_id(0) > 0)
    def _():
        sums_ref[...] += total


def mean_of(values):
    return jnp.mean(values, axis=-1, keepdims=True)


def out_rows(weight, half, column):
    rows = weight.shape[3] // 2
    part = weight[:, half, :, column * rows : (column + 1) * rows, :]
    return part.reshape(-1, weight.shape[4])


def attend_out_kernel(
    slots, facts_ref, own_ref, other_ref, own_weight_ref, other_weight_ref, tokens_ref, vectors_ref,
    hat_ref, rstd_ref, low_ref, sums_ref,
):
    own, other = own_ref[...], other_ref[...]
    own_weight, other_weight = own_weight_ref[...], other_weight_ref[...]
    parts = []
    for half in range(2):
        for column in range(2):
            parts.append(
                product(own, out_rows(own_weight, half, column), 1, 0)
                + product(other, out_rows(other_weight, half, column), 1, 0)
            )
    branch = jnp.concatenate(parts, axis=1) + vectors_ref[0:1]
    tokens = tokens_ref[...].astype(jnp.float32)
    total = tokens + branch
    centered = total - mean_of(total)
    rstd = lax.rsqrt(mean_of(centered * centered) + 1e-05)
    hat = centered * rstd
    hat_ref[...] = hat
    rstd_ref[...] = rstd
    low_ref[...] = (hat * vectors_ref[1:2] + vectors_ref[2:3]).astype(jnp.bfloat16)
    valid = valid_rows(facts_ref, tokens.shape[0], slots)
    add_rows(sums_ref, [valid * tokens * tokens, valid * branch * branch])


def attend_out(facts, own, other, own_weight, other_weight, tokens, vectors):
    slots, width = tokens.shape
    step = slots // 2
    rows = lambda array: block((step, array.shape[1]), first, 0)
    return call(
        partial(attend_out_kernel, slots),
        "attend_out",
        (2,),
        [rows(own), rows(other), whole(own_weight), whole(other_weight), rows(tokens), whole(vectors)],
        [block((step, width), first, 0), block((step, 1), first, 0), block((step, width), first, 0), block((8, width), 0, 0)],
        [
            like((slots, width), jnp.float32),
            like((slots, 1), jnp.float32),
            like((slots, width), jnp.bfloat16),
            like((8, width), jnp.float32),
        ],
        facts,
        own,
        other,
        own_weight,
        other_weight,
        tokens,
        vectors,
    )


def up_kernel(facts_ref, rows_ref, weight_ref, bias_ref, act_ref, slope_ref):
    weight = weight_ref[...].reshape(rows_ref.shape[1], weight_ref.shape[3])
    pre_act = product(rows_ref[...], weight, 1, 0) + bias_ref[...]
    below = 0.5 + 0.5 * lax.erf(pre_act * 0.7071067811865476)
    act_ref[...] = (pre_act * below).astype(jnp.bfloat16)
    slope = below + pre_act * (0.3989422804014327 * jnp.exp(-0.5 * pre_act * pre_act))
    slope_ref[...] = slope.astype(jnp.bfloat16)


def feed_up(facts, rows, weights, bias):
    count, width = rows.shape
    chips, wide = weights.shape[0], weights.shape[3]
    shape = like((count, 4 * wide), jnp.bfloat16)
    out = block((count, wide), 0, first)
    return call(
        up_kernel,
        "feed_up",
        (4,),
        [
            whole(rows),
            block((chips, 1, width // chips, wide), 0, lambda i, *_: i // 2, lambda i, *_: i % 2, 0),
            block((1, wide), 0, first),
        ],
        [out, out],
        [shape, shape],
        facts,
        rows,
        weights,
        bias[None],
    )


def down_kernel(facts_ref, rows_ref, weight_ref, out_ref):
    weight = weight_ref[...].reshape(rows_ref.shape[1], weight_ref.shape[3])
    out_ref[...] = product(rows_ref[...], weight, 1, 0).astype(out_ref.dtype)


def feed_down(facts, rows, part, weights, dtype):
    count, units = rows.shape
    chips, wide = weights.shape[0], weights.shape[3]
    return call(
        down_kernel,
        "feed_down",
        (2,),
        [
            block((count // 2, units), part, 0),
            block((chips, 1, units // chips, wide), 0, first, 1, 0),
        ],
        block((count // 2, wide), 0, first),
        like((count // 2, 2 * wide), dtype),
        facts,
        rows,
        weights,
    )


def second_norm_kernel(
    slots, facts_ref, part_ref, other_ref, hat_ref, cotangent_ref, vectors_ref,
    mixed_ref, grad_ref, low_ref, sums_ref,
):
    branch = part_ref[...] + other_ref[...].astype(jnp.float32) + vectors_ref[0:1]
    hidden = hat_ref[...] * vectors_ref[1:2] + vectors_ref[2:3]
    gain = vectors_ref[3:4]
    total = hidden + branch
    centered = total - mean_of(total)
    rstd = lax.rsqrt(mean_of(centered * centered) + 1e-05)
    hat = centered * rstd
    mixed_ref[...] = (hat * gain + vectors_ref[4:5]).astype(jnp.bfloat16)
    valid = valid_rows(facts_ref, branch.shape[0], slots)
    grad = cotangent_ref[...].astype(jnp.float32) * valid
    scaled = grad * gain
    result = rstd * (scaled - mean_of(scaled) - hat * mean_of(scaled * hat))
    low = result.astype(jnp.bfloat16)
    grad_ref[...] = result
    low_ref[...] = low
    add_rows(sums_ref, [low.astype(jnp.float32), grad * hat, grad, valid * branch * branch])


def second_norm(facts, part, other, hat, cotangent, vectors):
    slots, width = part.shape
    step = slots // 2
    rows = block((step, width), first, 0)
    return call(
        partial(second_norm_kernel, slots),
        "second_norm",
        (2,),
        [rows, rows, rows, rows, whole(vectors)],
        [rows, rows, rows, block((8, width), 0, 0)],
        [
            like((slots, width), jnp.bfloat16),
            like((slots, width), jnp.float32),
            like((slots, width), jnp.bfloat16),
            like((8, width), jnp.float32),
        ],
        facts,
        part,
        other,
        hat,
        cotangent,
        vectors,
    )


def first_norm_kernel(
    facts_ref, part_ref, other_ref, second_ref, hat_ref, rstd_ref, vectors_ref,
    grad_ref, low_ref, sums_ref,
):
    grad = part_ref[...] + other_ref[...].astype(jnp.float32) + second_ref[...]
    hat = hat_ref[...]
    scaled = grad * vectors_ref[1:2]
    result = rstd_ref[...] * (scaled - mean_of(scaled) - hat * mean_of(scaled * hat))
    low = result.astype(jnp.bfloat16)
    grad_ref[...] = result
    low_ref[...] = low
    add_rows(sums_ref, [low.astype(jnp.float32), grad * hat, grad])


def first_norm(facts, part, other, second, hat, rstd, vectors):
    slots, width = part.shape
    step = slots // 2
    rows = block((step, width), first, 0)
    return call(
        first_norm_kernel,
        "first_norm",
        (2,),
        [rows, rows, rows, rows, block((step, 1), first, 0), whole(vectors)],
        [rows, rows, block((8, width), 0, 0)],
        [
            like((slots, width), jnp.float32),
            like((slots, width), jnp.bfloat16),
            like((8, width), jnp.float32),
        ],
        facts,
        part,
        other,
        second,
        hat,
        rstd,
        vectors,
    )


def grad_kernel(keep, facts_ref, left_ref, right_ref, top_ref, low_ref):
    rows, wide = top_ref.shape[2:]
    half = facts_ref[3] if keep else 1 - facts_ref[3]
    row = facts_ref[4] if keep else 1 - facts_ref[4]
    start = pl.multiple_of(half * (2 * wide), 128)
    value = product(left_ref[...], right_ref[:, pl.ds(start, wide)], 0, 0)
    top_ref[...] = value.astype(jnp.bfloat16).reshape(top_ref.shape)
    left = left_ref[:, pl.ds(pl.multiple_of(row * rows, 128), rows)]
    for column in range(2):
        right = right_ref[:, (2 * column + 1) * wide : (2 * column + 2) * wide]
        low_ref[0, column] = product(left, right, 0, 0).astype(jnp.bfloat16)


def grad_parts(facts, left, right, rows, keep):
    count = left.shape[0]
    wide = right.shape[1] // 4
    out = block((1, 2, rows, wide), first, 0, 0, 0)
    shape = like((4, 2, rows, wide), jnp.bfloat16)
    return call(
        partial(grad_kernel, keep),
        "weight_grad",
        (4,),
        [block((count, 2 * rows), 0, first), whole(right)],
        [out, out],
        [shape, shape],
        facts,
        left,
        right,
    )


def act_grad_kernel(facts_ref, rows_ref, weight_ref, slope_ref, out_ref, sums_ref):
    wide = weight_ref.shape[3]
    total = 0.0
    for half in range(2):
        weight = weight_ref[:, half].reshape(-1, wide)
        total = total + product(rows_ref[:, half * wide : (half + 1) * wide], weight, 1, 1)
    grad = total.astype(jnp.bfloat16).astype(jnp.float32) * slope_ref[...].astype(jnp.float32)
    low = grad.astype(jnp.bfloat16)
    out_ref[...] = low
    sums_ref[...] = jnp.sum(low.astype(jnp.float32), axis=0, keepdims=True)


def act_grad(facts, rows, weights, slope):
    count, units = slope.shape
    chips, wide = weights.shape[0], weights.shape[3]
    step = units // 4
    out = block((count, step), 0, first)
    return call(
        act_grad_kernel,
        "act_grad",
        (4,),
        [whole(rows), block((chips // 4, 2, units // chips, wide), first, 0, 1, 0), out],
        [out, block((1, step), 0, first)],
        [like((count, units), jnp.bfloat16), like((1, units), jnp.float32)],
        facts,
        rows,
        weights,
        slope,
    )


def hidden_grad_kernel(facts_ref, rows_ref, weight_ref, out_ref):
    chips, _, rows, wide = weight_ref.shape
    rows = rows // 2
    total = 0.0
    for half in range(2):
        for column in range(2):
            weight = weight_ref[:, half, column * rows : (column + 1) * rows].reshape(-1, wide)
            start = (2 * half + column) * wide
            total = total + product(rows_ref[:, start : start + wide], weight, 1, 1)
    out_ref[...] = total.astype(out_ref.dtype)


def hidden_grad_part(facts, rows, part, weights, width, dtype):
    count, units = rows.shape
    chips, wide = weights.shape[0], weights.shape[3]
    return call(
        hidden_grad_kernel,
        "hidden_grad",
        (2,),
        [
            block((count // 2, units), part, 0),
            block((chips // 2, 2, 2 * width // chips, wide), first, 0, 0, 0),
        ],
        block((count // 2, width // 2), 0, first),
        like((count // 2, width), dtype),
        facts,
        rows,
        weights,
    )


def heads_grad_kernel(facts_ref, rows_ref, own_ref, other_ref, out_own_ref, out_other_ref):
    for weight_ref, out_ref in ((own_ref, out_own_ref), (other_ref, out_other_ref)):
        weight = weight_ref[...]
        wide = weight.shape[4]
        total = 0.0
        for half in range(2):
            for column in range(2):
                start = (2 * half + column) * wide
                total = total + product(
                    rows_ref[:, start : start + wide], out_rows(weight, half, column), 1, 1
                )
        out_ref[...] = total.astype(jnp.bfloat16)


def heads_grads(facts, rows, own, other):
    count, width = rows.shape
    step = count // 2
    out = block((step, width // 2), first, 0)
    shape = like((count, width // 2), jnp.bfloat16)
    return call(
        heads_grad_kernel,
        "heads_grad",
        (2,),
        [block((step, width), first, 0), whole(own), whole(other)],
        [out, out],
        [shape, shape],
        facts,
        rows,
        own,
        other,
    )


def tokens_grad_kernel(wide, facts_ref, rows_ref, top_ref, low_ref, out_ref):
    total = 0.0
    for half in range(2):
        weight = near_rows(top_ref[half : half + 1], low_ref[:, :, half : half + 1])
        start = half * 3 * wide
        total = total + product(
            rows_ref[:, start : start + 3 * wide], weight[:, : 3 * wide], 1, 1
        )
    out_ref[...] = total.astype(out_ref.dtype)


def tokens_grad_part(facts, rows, part, top, low, wide, dtype):
    count, columns = rows.shape
    width = top.shape[1] * top.shape[2] * 2 * top.shape[3]
    return call(
        partial(tokens_grad_kernel, wide),
        "tokens_grad",
        (2,),
        [
            block((count // 2, columns), part, 0),
            block((2, 2, 2) + top.shape[3:], 0, 0, first, 0, 0),
            block((2, 2, 2) + low.shape[3:], 0, first, 0, 0, 0),
        ],
        block((count // 2, width // 2), 0, first),
        like((count // 2, width), dtype),
        facts,
        rows,
        top,
        low,
    )


def split_body(
    tokens,
    lengths,
    cotangent,
    query_weight,
    key_weight,
    value_weight,
    out_weight,
    up_weight,
    down_weight,
    query_bias,
    value_bias,
    out_bias,
    attn_gain,
    attn_shift,
    up_bias,
    down_bias,
    feed_gain,
    feed_shift,
):
    core = lax.axis_index("c")
    half = lax.axis_index("s")
    row_count, width = tokens.shape[1:]
    slots = 2 * row_count
    unit_block = down_weight.shape[0]
    units = up_bias.shape[0] // 2
    cols = width // 2
    wide = cols // 2

    small = [
        split_columns(weight, HD, core) for weight in (query_weight, key_weight, value_weight)
    ]
    large = split_columns(up_weight, unit_block, core)
    up_pair = in_order(large[0], swap(large[1], "c"), core)
    up_cols = up_pair.shape[2]
    up_mine = up_pair.reshape(-1, up_cols)
    rows = up_mine.shape[0]
    feed_send = jnp.concatenate(
        [up_mine[:, : up_cols // 2], up_mine[:, up_cols // 2 :], down_weight], axis=0
    )
    feed_all = lax.all_gather(feed_send, ("z", "x", "s"), axis=0, tiled=False)
    feed_all = feed_all.reshape((-1, 2) + feed_send.shape)
    near_kept = jnp.concatenate([part[0] for part in small], axis=1)
    near_sent = jnp.concatenate([part[1] for part in small], axis=1)
    near_pair = in_order(near_kept, swap(near_sent, "c"), core)
    out_pair = out_weight.reshape(2, -1, 2, wide).transpose(0, 2, 1, 3)
    out_pair = out_pair.reshape(2, out_weight.shape[0], wide)
    near_pair = jnp.concatenate([near_pair, out_pair], axis=2)
    near_top = gather_two(gather_two(gather_line(near_pair[0]), "x"), "s")
    near_low = gather_two(gather_line(gather_two(near_pair[1], "s")), "x")
    out_own = jnp.stack(
        [
            near_top[..., 3 * wide :].transpose(2, 1, 0, 3, 4),
            near_low[..., 3 * wide :].transpose(1, 0, 2, 3, 4),
        ],
        axis=3,
    )
    out_own = out_own.reshape((-1,) + out_own.shape[2:])
    out_other = swap(out_own, "c")

    def to_sequence(values):
        return jnp.concatenate([pick(values, half, 0), swap(pick(values, 1 - half, 0), "s")], axis=0)

    def from_sequence(values):
        return in_order(values[:row_count], swap(values[row_count:], "s"), half)

    tokens_own = to_sequence(tokens)
    tokens_both = both(tokens_own, "c")
    length_own = lax.dynamic_slice_in_dim(lengths, half, 1, 0)
    facts = jnp.concatenate(
        [
            both(length_own, "c"),
            jnp.stack([half * row_count, half, lax.axis_index("x")]).astype(jnp.int32),
        ]
    )

    def halves_of(vector, size):
        return pick(vector.reshape(-1, 2, size), core, 1).reshape(-1)

    query_part = halves_of(query_bias, HD).reshape(2, wide)
    value_part = halves_of(value_bias, HD).reshape(2, wide)
    in_bias = jnp.stack([query_part, jnp.zeros_like(query_part), value_part], axis=1).reshape(-1)
    projected = project(facts, tokens_both, near_top, near_low, in_bias, wide)
    heads_out, totals = attend(facts, projected, slots)
    heads_other = swap(heads_out[slots:], "c")
    vectors = jnp.stack(
        [out_bias, attn_gain, attn_shift, down_bias, feed_gain, feed_shift, out_bias, out_bias]
    )
    first_hat, first_rstd, hidden_low, first_sums = attend_out(
        facts, heads_out, heads_other, out_own, out_other, tokens_own, vectors
    )
    hidden_both = both(hidden_low, "c")
    activation, slope = feed_up(facts, hidden_both, feed_all, halves_of(up_bias, unit_block))
    feed_other = swap(feed_down(facts, activation, 1, feed_all, jnp.bfloat16), "c")
    feed_part = feed_down(facts, activation, 0, feed_all, jnp.float32)
    cotangent_own = to_sequence(cotangent)
    feed_vectors = jnp.stack(
        [down_bias, attn_gain, attn_shift, feed_gain, feed_shift, out_bias, out_bias, out_bias]
    )
    mixed, second_grad, feed_low, second_sums = second_norm(
        facts, feed_part, feed_other, first_hat, cotangent_own, feed_vectors
    )
    mixed = from_sequence(mixed)

    feed_both = both(feed_low, "c")
    down_send = grad_parts(facts, activation, feed_both, unit_block, False)
    down_keep = grad_parts(facts, activation, feed_both, unit_block, True)
    down_sum = scatter_sum(down_send, down_keep)
    pre_grad, up_bias_grad = act_grad(facts, feed_both, feed_all, slope)
    hidden_other = swap(hidden_grad_part(facts, pre_grad, 1, feed_all, width, jnp.bfloat16), "c")
    hidden_part = hidden_grad_part(facts, pre_grad, 0, feed_all, width, jnp.float32)
    up_send = grad_parts(facts, hidden_both, pre_grad, rows, False)
    up_keep = grad_parts(facts, hidden_both, pre_grad, rows, True)
    up_sum = scatter_sum(up_send, up_keep)
    first_grad, attn_low, third_sums = first_norm(
        facts, hidden_part, hidden_other, second_grad, first_hat, first_rstd, vectors
    )
    grad_own, grad_sent = heads_grads(facts, attn_low, out_own, out_other)
    heads_grad = jnp.concatenate([grad_own, swap(grad_sent, "c")], axis=0)
    out_part = product(heads_out[:slots], attn_low, 0, 0)
    out_sent = product(heads_other, attn_low, 0, 0).astype(jnp.bfloat16)
    out_grad = (out_part + swap(out_sent, "c").astype(jnp.float32)).astype(jnp.bfloat16)
    in_low, in_sums = attend_back(facts, projected, heads_grad, totals, slots)
    out_grad = out_grad.reshape(4, 2, -1, 2, 2, wide).transpose(4, 0, 1, 3, 2, 5)
    out_top = out_grad[0].transpose(2, 0, 1, 3, 4)
    out_low = out_grad[1].transpose(1, 0, 2, 3, 4)
    column = lax.axis_index("x")
    out_sum = scatter_sum(
        (pick(out_top, 1 - half, 0), pick(out_low, 1 - column, 0)),
        (pick(out_top, half, 0), pick(out_low, column, 0)),
    )
    in_send = grad_parts(facts, tokens_both, in_low, rows, False)
    in_keep = grad_parts(facts, tokens_both, in_low, rows, True)
    in_sum = scatter_sum(in_send, in_keep)
    tokens_other = swap(
        tokens_grad_part(facts, in_low, 1, near_top, near_low, wide, jnp.bfloat16), "c"
    )
    tokens_part = tokens_grad_part(facts, in_low, 0, near_top, near_low, wide, jnp.float32)
    tokens_grad = tokens_part + tokens_other.astype(jnp.float32) + first_grad
    tokens_grad = from_sequence(tokens_grad.astype(jnp.bfloat16))

    in_bias_grad = jnp.sum(in_sums, axis=(0, 1))
    valid_count = length_own[0].astype(jnp.float32) * width
    stats = jnp.stack(
        [jnp.sum(first_sums[0]), jnp.sum(first_sums[1]), jnp.sum(second_sums[3]), valid_count]
    )
    shared = jnp.concatenate(
        [second_sums[:3].reshape(-1), third_sums[:3].reshape(-1), jnp.pad(stats, (0, 124))]
    )
    own_sums = total_over(
        jnp.concatenate(
            [
                shared,
                up_bias_grad[0],
                in_bias_grad[:wide],
                in_bias_grad[3 * wide : 4 * wide],
                in_bias_grad[2 * wide : 3 * wide],
                in_bias_grad[5 * wide :],
            ]
        )
    )
    other_sums = swap(own_sums, "c")
    count = shared.shape[0]
    shared = own_sums[:count] + other_sums[:count]
    down_bias_grad, feed_gain_grad, feed_shift_grad, out_bias_grad, attn_gain_grad, attn_shift_grad = [
        shared[i * width : (i + 1) * width] for i in range(6)
    ]
    stats = shared[6 * width : 6 * width + 4]

    def interleave(start, size, block):
        own = own_sums[start : start + size].reshape(-1, block)
        other = other_sums[start : start + size].reshape(-1, block)
        first = jnp.where(core == 0, own, other)
        second = jnp.where(core == 0, other, own)
        return jnp.stack([first, second], axis=1).reshape(-1)

    up_bias_grad = interleave(count, units, unit_block)
    query_bias_grad = interleave(count + units, cols, HD)
    value_bias_gradient = interleave(count + units + cols, cols, HD)
    stream_rms = jnp.sqrt(stats[:3] / stats[3])

    joined = jnp.concatenate([in_sum, up_sum], axis=1)
    joined = joined.reshape((2, rows // 2) + joined.shape[1:])
    own = pick(joined, core, 0)
    other = swap(pick(joined, 1 - core, 0), "c")
    down_weight_grad = down_sum.astype(jnp.float32)
    out_weight_grad = out_sum.astype(jnp.float32)

    def merge(start, size, block):
        one = own[:, start : start + size].reshape(rows // 2, -1, block)
        two = other[:, start : start + size].reshape(rows // 2, -1, block)
        first = jnp.where(core == 0, one, two)
        second = jnp.where(core == 0, two, one)
        return jnp.stack([first, second], axis=2).reshape(rows // 2, -1).astype(jnp.float32)

    query_weight_grad = merge(0, wide, HD)
    key_weight_grad = merge(wide, wide, HD)
    value_weight_grad = merge(2 * wide, wide, HD)
    up_weight_grad = merge(3 * wide, up_cols, unit_block)
    return (
        mixed,
        tokens_grad,
        query_weight_grad,
        key_weight_grad,
        value_weight_grad,
        out_weight_grad,
        up_weight_grad,
        down_weight_grad,
        query_bias_grad,
        value_bias_gradient,
        out_bias_grad,
        attn_gain_grad,
        attn_shift_grad,
        up_bias_grad,
        down_bias_grad,
        feed_gain_grad,
        feed_shift_grad,
        stream_rms,
    )


def solution(mesh):
    devices = mesh.devices
    dp_count, seq_count = devices.shape
    split = seq_count == 2 and dp_count == 16
    if split:
        inner = jax.sharding.Mesh(devices.reshape(4, 2, 2, seq_count), ("z", "x", "c", "s"))
        dp, seq, body = ("z", "x", "c"), "s", split_body
    else:
        inner, dp, seq, body = mesh, "dp", "seq", general_body
    weights = (P(dp, seq),) * 6
    vectors = (P(),) * 9
    rows = P(dp, seq, None)
    in_specs = (rows, P(dp), rows) + weights + vectors
    out_specs = (rows, rows) + weights + vectors + (P(),)
    return jax.shard_map(body, mesh=inner, in_specs=in_specs, out_specs=out_specs, check_vma=False)
```

```python
from functools import partial
import math

import jax
import jax.numpy as jnp
from jax import lax
from jax.experimental import pallas as pl
from jax.experimental.pallas import tpu as pltpu
from jax.sharding import PartitionSpec as P

HD = 64


def layer_norm(values_in, gain_vector, shift_vector):
    mean_value = jnp.mean(values_in, axis=-1, keepdims=True)
    centered = values_in - mean_value
    variance = jnp.mean(centered * centered, axis=-1, keepdims=True)
    return centered * lax.rsqrt(variance + 1e-05) * gain_vector + shift_vector


def gather_weights(first, second, third, fourth, fifth, sixth):
    part = (
        lax.all_gather(first, "dp", axis=0, tiled=True),
        lax.all_gather(second, "dp", axis=0, tiled=True),
        lax.all_gather(third, "dp", axis=0, tiled=True),
        lax.all_gather(fourth, "dp", axis=0, tiled=True),
        lax.all_gather(fifth, "dp", axis=0, tiled=True),
        lax.all_gather(sixth, "dp", axis=0, tiled=True),
    )
    return (
        lax.all_gather(part[0], "seq", axis=1, tiled=True),
        lax.all_gather(part[1], "seq", axis=1, tiled=True),
        lax.all_gather(part[2], "seq", axis=1, tiled=True),
        lax.all_gather(part[3], "seq", axis=1, tiled=True),
        lax.all_gather(part[4], "seq", axis=1, tiled=True),
        lax.all_gather(part[5], "seq", axis=1, tiled=True),
    )


def reduce_grads(first, second, third, fourth, fifth, sixth):
    part = (
        lax.psum_scatter(first.astype(jnp.bfloat16), "seq", scatter_dimension=1, tiled=True).astype(
            jnp.float32
        ),
        lax.psum_scatter(
            second.astype(jnp.bfloat16), "seq", scatter_dimension=1, tiled=True
        ).astype(jnp.float32),
        lax.psum_scatter(third.astype(jnp.bfloat16), "seq", scatter_dimension=1, tiled=True).astype(
            jnp.float32
        ),
        lax.psum_scatter(
            fourth.astype(jnp.bfloat16), "seq", scatter_dimension=1, tiled=True
        ).astype(jnp.float32),
        lax.psum_scatter(fifth.astype(jnp.bfloat16), "seq", scatter_dimension=1, tiled=True).astype(
            jnp.float32
        ),
        lax.psum_scatter(sixth.astype(jnp.bfloat16), "seq", scatter_dimension=1, tiled=True).astype(
            jnp.float32
        ),
    )
    return (
        lax.psum_scatter(
            part[0].astype(jnp.bfloat16), "dp", scatter_dimension=0, tiled=True
        ).astype(jnp.float32),
        lax.psum_scatter(
            part[1].astype(jnp.bfloat16), "dp", scatter_dimension=0, tiled=True
        ).astype(jnp.float32),
        lax.psum_scatter(
            part[2].astype(jnp.bfloat16), "dp", scatter_dimension=0, tiled=True
        ).astype(jnp.float32),
        lax.psum_scatter(
            part[3].astype(jnp.bfloat16), "dp", scatter_dimension=0, tiled=True
        ).astype(jnp.float32),
        lax.psum_scatter(
            part[4].astype(jnp.bfloat16), "dp", scatter_dimension=0, tiled=True
        ).astype(jnp.float32),
        lax.psum_scatter(
            part[5].astype(jnp.bfloat16), "dp", scatter_dimension=0, tiled=True
        ).astype(jnp.float32),
    )


def block_layout(seq_count, row_count, head_count):
    block_seqs = math.gcd(seq_count, max(1, 512 // row_count))
    group_heads = math.gcd(head_count, 4)
    return (block_seqs, seq_count // block_seqs, group_heads, head_count // group_heads)


def head_slice(block_part, offset, group_width, group_heads):
    sliced = lax.dynamic_slice_in_dim(block_part, offset, group_width, 2)
    return sliced.reshape(sliced.shape[0], sliced.shape[1], group_heads, HD)


def attention_forward(queries, key_all, value_all, key_mask):
    seq_count, row_count, feature_total = queries.shape
    slot_count = key_all.shape[1]
    block_seqs, block_count, group_heads, group_count = block_layout(
        seq_count, row_count, feature_total // HD
    )
    group_width = group_heads * HD

    def seq_block(inputs):
        query_part, key_part, value_part, mask_part = inputs

        def head_block(group_index):
            offset = group_index * group_width
            query_heads = head_slice(query_part, offset, group_width, group_heads)
            key_heads = head_slice(key_part, offset, group_width, group_heads)
            value_heads = head_slice(value_part, offset, group_width, group_heads)
            scores = (
                jnp.einsum(
                    "brhd,bkhd->bhrk", query_heads, key_heads, preferred_element_type=jnp.float32
                )
                * 0.125
            )
            scores = jnp.where(mask_part[:, None, None, :], scores, -1e30)
            row_max = jnp.max(scores, axis=-1, keepdims=True)
            exponent = jnp.exp(scores - row_max)
            row_total = jnp.sum(exponent, axis=-1, keepdims=True)
            soft_probs = (exponent / row_total).astype(jnp.bfloat16)
            heads_out = jnp.einsum(
                "bhrk,bkhd->brhd", soft_probs, value_heads, preferred_element_type=jnp.float32
            )
            log_total = (row_max + jnp.log(row_total))[..., 0]
            return (heads_out.reshape(block_seqs, row_count, group_width), log_total)

        return lax.map(head_block, jnp.arange(group_count))

    outputs, log_totals = lax.map(
        seq_block,
        (
            queries.reshape(block_count, block_seqs, row_count, feature_total),
            key_all.reshape(block_count, block_seqs, slot_count, feature_total),
            value_all.reshape(block_count, block_seqs, slot_count, feature_total),
            key_mask.reshape(block_count, block_seqs, slot_count),
        ),
    )
    mixed_heads = outputs.transpose(0, 2, 3, 1, 4).reshape(seq_count, row_count, feature_total)
    return (mixed_heads, log_totals)


def attention_backward(queries, key_all, value_all, key_mask, heads_grad, log_totals):
    seq_count, row_count, feature_total = queries.shape
    slot_count = key_all.shape[1]
    block_seqs, block_count, group_heads, group_count = block_layout(
        seq_count, row_count, feature_total // HD
    )
    group_width = group_heads * HD

    def seq_block(inputs):
        query_part, key_part, value_part, mask_part, grad_part, total_part = inputs

        def head_block(group_index):
            offset = group_index * group_width
            query_heads = head_slice(query_part, offset, group_width, group_heads)
            key_heads = head_slice(key_part, offset, group_width, group_heads)
            value_heads = head_slice(value_part, offset, group_width, group_heads)
            grad_heads = head_slice(grad_part, offset, group_width, group_heads)
            log_total = lax.dynamic_index_in_dim(total_part, group_index, 0, keepdims=False)
            scores = (
                jnp.einsum(
                    "brhd,bkhd->bhrk", query_heads, key_heads, preferred_element_type=jnp.float32
                )
                * 0.125
            )
            scores = jnp.where(mask_part[:, None, None, :], scores, -1e30)
            soft_probs = jnp.exp(scores - log_total[..., None])
            value_grad = jnp.einsum(
                "bhrk,brhd->bkhd",
                soft_probs.astype(jnp.bfloat16),
                grad_heads,
                preferred_element_type=jnp.float32,
            )
            prob_grad = jnp.einsum(
                "brhd,bkhd->bhrk", grad_heads, value_heads, preferred_element_type=jnp.float32
            )
            inner = jnp.sum(soft_probs * prob_grad, axis=-1, keepdims=True)
            score_grad = (soft_probs * (prob_grad - inner)).astype(jnp.bfloat16)
            query_grad = (
                jnp.einsum(
                    "bhrk,bkhd->brhd", score_grad, key_heads, preferred_element_type=jnp.float32
                )
                * 0.125
            )
            key_grad = (
                jnp.einsum(
                    "bhrk,brhd->bkhd", score_grad, query_heads, preferred_element_type=jnp.float32
                )
                * 0.125
            )
            return (
                query_grad.reshape(block_seqs, row_count, group_width),
                key_grad.reshape(block_seqs, slot_count, group_width),
                value_grad.reshape(block_seqs, slot_count, group_width),
            )

        return lax.map(head_block, jnp.arange(group_count))

    query_blocks, key_blocks, value_block_list = lax.map(
        seq_block,
        (
            queries.reshape(block_count, block_seqs, row_count, feature_total),
            key_all.reshape(block_count, block_seqs, slot_count, feature_total),
            value_all.reshape(block_count, block_seqs, slot_count, feature_total),
            key_mask.reshape(block_count, block_seqs, slot_count),
            heads_grad.reshape(block_count, block_seqs, row_count, feature_total),
            log_totals,
        ),
    )
    query_grad = query_blocks.transpose(0, 2, 3, 1, 4).reshape(seq_count, row_count, feature_total)
    key_grad = key_blocks.transpose(0, 2, 3, 1, 4).reshape(seq_count, slot_count, feature_total)
    value_grad = value_block_list.transpose(0, 2, 3, 1, 4).reshape(
        seq_count, slot_count, feature_total
    )
    return (query_grad, key_grad, value_grad)


def general_body(
    tokens,
    lengths,
    cotangent,
    query_weight,
    key_weight,
    value_weight,
    out_weight,
    up_weight,
    down_weight,
    query_bias,
    value_bias,
    out_bias,
    attn_gain,
    attn_shift,
    up_bias,
    down_bias,
    feed_gain,
    feed_shift,
):
    seq_count, row_count, feature_total = tokens.shape
    slot_count = row_count * lax.axis_size("seq")
    token_count = seq_count * row_count
    whole = gather_weights(
        query_weight, key_weight, value_weight, out_weight, up_weight, down_weight
    )
    full_query, full_key, full_value, full_out, full_up, full_down = whole
    flat_tokens = tokens.reshape(token_count, feature_total)
    queries = (
        jnp.dot(flat_tokens, full_query, preferred_element_type=jnp.float32) + query_bias
    ).astype(jnp.bfloat16)
    key_rows = jnp.dot(flat_tokens, full_key, preferred_element_type=jnp.float32).astype(
        jnp.bfloat16
    )
    value_rows = (
        jnp.dot(flat_tokens, full_value, preferred_element_type=jnp.float32) + value_bias
    ).astype(jnp.bfloat16)
    first_slot = lax.axis_index("seq") * row_count
    key_mask = jnp.arange(slot_count)[None, :] < lengths[:, None]
    row_valid = ((first_slot + jnp.arange(row_count))[None, :] < lengths[:, None]).astype(
        jnp.float32
    )
    row_valid = row_valid.reshape(token_count, 1)
    query_blocks = queries.reshape(seq_count, row_count, feature_total)
    key_blocks = key_rows.reshape(seq_count, row_count, feature_total)
    value_block_list = value_rows.reshape(seq_count, row_count, feature_total)
    key_all, value_all = (
        lax.all_gather(key_blocks, "seq", axis=1, tiled=True),
        lax.all_gather(value_block_list, "seq", axis=1, tiled=True),
    )
    mixed_heads, log_totals = attention_forward(query_blocks, key_all, value_all, key_mask)
    heads_low = mixed_heads.reshape(token_count, feature_total).astype(jnp.bfloat16)
    attention_out = jnp.dot(heads_low, full_out, preferred_element_type=jnp.float32) + out_bias
    tokens_f32 = flat_tokens.astype(jnp.float32)
    first_sum = tokens_f32 + attention_out
    hidden, first_pull = jax.vjp(layer_norm, first_sum, attn_gain, attn_shift)
    hidden_low = hidden.astype(jnp.bfloat16)
    pre_act = jnp.dot(hidden_low, full_up, preferred_element_type=jnp.float32) + up_bias
    gelu_out, gelu_pull = jax.vjp(partial(jax.nn.gelu, approximate=False), pre_act)
    activation = gelu_out.astype(jnp.bfloat16)
    feed_out = jnp.dot(activation, full_down, preferred_element_type=jnp.float32) + down_bias
    result, second_pull = jax.vjp(layer_norm, hidden + feed_out, feed_gain, feed_shift)
    mixed = result.astype(jnp.bfloat16).reshape(seq_count, row_count, feature_total)
    partial_stats = jnp.stack(
        [
            jnp.sum(row_valid * tokens_f32 * tokens_f32),
            jnp.sum(row_valid * attention_out * attention_out),
            jnp.sum(row_valid * feed_out * feed_out),
            jnp.sum(row_valid) * feature_total,
        ]
    )
    back_weights = gather_weights(
        query_weight, key_weight, value_weight, out_weight, up_weight, down_weight
    )
    back_query, back_key, back_value, back_out, back_up, back_down = back_weights
    out_grad = cotangent.reshape(token_count, feature_total).astype(jnp.float32) * row_valid
    second_grad, feed_gain_grad, feed_shift_grad = second_pull(out_grad)
    feed_low = second_grad.astype(jnp.bfloat16)
    down_weight_grad = jnp.einsum(
        "nf,nd->fd", activation, feed_low, preferred_element_type=jnp.float32
    )
    down_bias_grad = jnp.sum(feed_low, axis=0, dtype=jnp.float32)
    act_grad = jnp.einsum(
        "nd,fd->nf", feed_low, back_down, preferred_element_type=jnp.float32
    ).astype(jnp.bfloat16)
    pre_grad = gelu_pull(act_grad.astype(jnp.float32))[0].astype(jnp.bfloat16)
    up_weight_grad = jnp.einsum(
        "nd,nf->df", hidden_low, pre_grad, preferred_element_type=jnp.float32
    )
    up_bias_grad = jnp.sum(pre_grad, axis=0, dtype=jnp.float32)
    hidden_grad = (
        jnp.einsum("nf,df->nd", pre_grad, back_up, preferred_element_type=jnp.float32) + second_grad
    )
    first_grad, attn_gain_grad, attn_shift_grad = first_pull(hidden_grad)
    attn_low = first_grad.astype(jnp.bfloat16)
    out_weight_grad = jnp.einsum(
        "nd,ne->de", heads_low, attn_low, preferred_element_type=jnp.float32
    )
    out_bias_grad = jnp.sum(attn_low, axis=0, dtype=jnp.float32)
    heads_grad = jnp.einsum(
        "ne,de->nd", attn_low, back_out, preferred_element_type=jnp.float32
    ).astype(jnp.bfloat16)
    heads_grad = heads_grad.reshape(seq_count, row_count, feature_total)
    query_grad, key_part_grad, value_part_grad = attention_backward(
        query_blocks, key_all, value_all, key_mask, heads_grad, log_totals
    )
    key_sum, value_sum = (
        lax.psum_scatter(
            key_part_grad.astype(jnp.bfloat16), "seq", scatter_dimension=1, tiled=True
        ).astype(jnp.float32),
        lax.psum_scatter(
            value_part_grad.astype(jnp.bfloat16), "seq", scatter_dimension=1, tiled=True
        ).astype(jnp.float32),
    )
    query_low = query_grad.reshape(token_count, feature_total).astype(jnp.bfloat16)
    key_low = key_sum.reshape(token_count, feature_total).astype(jnp.bfloat16)
    value_low = value_sum.reshape(token_count, feature_total).astype(jnp.bfloat16)
    query_weight_grad = jnp.einsum(
        "nd,ne->de", flat_tokens, query_low, preferred_element_type=jnp.float32
    )
    key_weight_grad = jnp.einsum(
        "nd,ne->de", flat_tokens, key_low, preferred_element_type=jnp.float32
    )
    value_weight_grad = jnp.einsum(
        "nd,ne->de", flat_tokens, value_low, preferred_element_type=jnp.float32
    )
    query_bias_grad = jnp.sum(query_low, axis=0, dtype=jnp.float32)
    value_bias_gradient = jnp.sum(value_low, axis=0, dtype=jnp.float32)
    tokens_grad = (
        jnp.einsum("ne,de->nd", query_low, back_query, preferred_element_type=jnp.float32)
        + jnp.einsum("ne,de->nd", key_low, back_key, preferred_element_type=jnp.float32)
        + jnp.einsum("ne,de->nd", value_low, back_value, preferred_element_type=jnp.float32)
        + first_grad
    )
    tokens_grad = tokens_grad.astype(jnp.bfloat16).reshape(seq_count, row_count, feature_total)
    matrix_grads = reduce_grads(
        query_weight_grad,
        key_weight_grad,
        value_weight_grad,
        out_weight_grad,
        up_weight_grad,
        down_weight_grad,
    )
    totals = lax.psum(
        (
            partial_stats,
            query_bias_grad,
            value_bias_gradient,
            out_bias_grad,
            attn_gain_grad,
            attn_shift_grad,
            up_bias_grad,
            down_bias_grad,
            feed_gain_grad,
            feed_shift_grad,
        ),
        ("dp", "seq"),
    )
    stream_rms = jnp.sqrt(totals[0][:3] / totals[0][3])
    return (
        mixed,
        tokens_grad,
        matrix_grads[0],
        matrix_grads[1],
        matrix_grads[2],
        matrix_grads[3],
        matrix_grads[4],
        matrix_grads[5],
        totals[1],
        totals[2],
        totals[3],
        totals[4],
        totals[5],
        totals[6],
        totals[7],
        totals[8],
        totals[9],
        stream_rms,
    )


def swap(value, axis):
    return lax.ppermute(value, axis, [(0, 1), (1, 0)])


def both(value, axis):
    return jnp.concatenate([value, swap(value, axis)], axis=0)


def in_order(own, other, index, axis=0):
    return jnp.where(
        index == 0, jnp.stack([own, other], axis=axis), jnp.stack([other, own], axis=axis)
    )


def split_columns(weight, width, core):
    rows = weight.shape[0]
    blocks = weight.reshape(rows, -1, 2, width)
    return pick(blocks, core, 2).reshape(rows, -1), pick(blocks, 1 - core, 2).reshape(rows, -1)


def pick(values, index, axis):
    return lax.dynamic_index_in_dim(values, index, axis, keepdims=False)


def add(left, right):
    return (left.astype(jnp.float32) + right.astype(jnp.float32)).astype(jnp.bfloat16)


def total_over(vector):
    vector = vector + swap(vector, "s")
    vector = vector + swap(vector, "x")
    vector = vector + lax.ppermute(vector, "z", [(0, 1), (1, 0), (2, 3), (3, 2)])
    return vector + lax.ppermute(vector, "z", [(0, 2), (2, 0), (1, 3), (3, 1)])


def fold(values, axis, dim):
    index = lax.axis_index(axis)
    return add(pick(values, index, dim), swap(pick(values, 1 - index, dim), axis))


NEXT = [(0, 1), (1, 0), (2, 3), (3, 2)]
CROSS = [(0, 2), (2, 0), (1, 3), (3, 1)]


def fold_line(values):
    place = lax.axis_index("z")
    odd, upper = place % 2, place // 2
    pairs = values.reshape((2, 2) + values.shape[1:])
    pairs = add(pick(pairs, odd, 1), lax.ppermute(pick(pairs, 1 - odd, 1), "z", NEXT))
    return add(pick(pairs, upper, 0), lax.ppermute(pick(pairs, 1 - upper, 0), "z", CROSS))


def gather_line(value):
    place = lax.axis_index("z")
    pair = in_order(value, lax.ppermute(value, "z", CROSS), place // 2)
    whole = in_order(pair, lax.ppermute(pair, "z", NEXT), place % 2, 1)
    return whole.reshape((4,) + value.shape)


def gather_two(value, axis, dim=0):
    return in_order(value, swap(value, axis), lax.axis_index(axis), dim)


def gather_top(value):
    whole = gather_two(gather_line(value), "x", 1)
    return gather_two(whole.reshape((8,) + value.shape), "s")


def gather_low(value):
    whole = gather_two(gather_line(gather_two(value, "s")), "x", 1)
    return whole.reshape((8, 2) + value.shape)


def scatter_top(send, keep):
    total = add(keep, swap(send, "s"))
    total = total.reshape((4, 2) + total.shape[1:])
    return fold_line(fold(total, "x", 1))


def scatter_low(send, keep):
    total = fold_line(add(keep, swap(send, "x")))
    columns = total.shape[1] // 2
    half = lax.axis_index("s")
    kept = lax.dynamic_slice_in_dim(total, half * columns, columns, 1)
    sent = lax.dynamic_slice_in_dim(total, (1 - half) * columns, columns, 1)
    return add(kept, swap(sent, "s"))


def grad_top(left, right, rows, half):
    columns = right.shape[1] // 2
    right = lax.dynamic_slice_in_dim(right, half * columns, columns, 1)
    return product(left, right, 0, 0).astype(jnp.bfloat16).reshape(-1, rows, columns)


def rows_of(left, rows, index):
    return pick(left.reshape(left.shape[0], 4, 2, rows), index, 2).reshape(left.shape[0], -1)


def grad_low(left, right, rows):
    return product(left, right, 0, 0).astype(jnp.bfloat16).reshape(4, rows, right.shape[1])


PAIR = 2 * HD
LIMIT = 56 * 1024 * 1024


def kernel_params(steps):
    return pltpu.CompilerParams(
        dimension_semantics=("arbitrary",) * steps, vmem_limit_bytes=LIMIT
    )


def product(left, right, left_dim, right_dim):
    return lax.dot_general(
        left, right, (((left_dim,), (right_dim,)), ((), ())), preferred_element_type=jnp.float32
    )


def key_bias(facts_ref, slots):
    place = lax.broadcasted_iota(jnp.int32, (slots, 1), 0) + facts_ref[2]
    place = jnp.where(place >= slots, place - slots, place)
    return jnp.where(place < facts_ref[pl.program_id(0)], 0.0, -1e30)


def head_lanes(value, head):
    lane = lax.broadcasted_iota(jnp.int32, value.shape, 1)
    return jnp.where((lane >= HD) == (head == 1), value, jnp.zeros_like(value))


def turned(value):
    return value.astype(jnp.float32).T


def attend_kernel(facts_ref, query_ref, key_ref, value_ref, out_ref, total_ref):
    slots = key_ref.shape[0]
    bias = key_bias(facts_ref, slots)
    query = query_ref[...] * jnp.bfloat16(0.125)
    key = key_ref[...]
    value_t = turned(value_ref[...]).astype(jnp.bfloat16)
    outs = []
    for head in range(2):
        scores = product(key, head_lanes(query, head), 1, 1) + bias
        peak = jnp.max(scores, axis=0, keepdims=True)
        weight = jnp.exp(scores - peak)
        total = jnp.sum(weight, axis=0, keepdims=True)
        part = product(value_t[head * HD : (head + 1) * HD], weight.astype(jnp.bfloat16), 1, 0)
        outs.append(part * (1.0 / total))
        total_ref[0, 0, head : head + 1, :] = peak + jnp.log(total)
    out_ref[...] = jnp.concatenate(outs, axis=0).T.astype(jnp.bfloat16)


def attend_back_kernel(
    facts_ref, query_ref, key_ref, value_ref, grad_ref, total_ref, low_ref, sums_ref
):
    slots = key_ref.shape[0]
    bias = key_bias(facts_ref, slots)
    query = query_ref[...] * jnp.bfloat16(0.125)
    key = key_ref[...]
    value = value_ref[...]
    grad = grad_ref[...]
    key_t = turned(key).astype(jnp.bfloat16)
    lane = lax.broadcasted_iota(jnp.int32, (slots, PAIR), 1)
    query_parts, key_parts, value_parts = [], [], []
    for head in range(2):
        scores = product(key, head_lanes(query, head), 1, 1) + bias
        soft = jnp.exp(scores - total_ref[0, 0, head : head + 1, :])
        value_parts.append(product(soft.astype(jnp.bfloat16), grad, 1, 0))
        change = product(value, head_lanes(grad, head), 1, 1)
        inner = jnp.sum(soft * change, axis=0, keepdims=True)
        change = (soft * (change - inner)).astype(jnp.bfloat16)
        key_parts.append(product(change, query, 1, 0))
        query_parts.append(product(key_t[head * HD : (head + 1) * HD], change, 1, 0))
    pair = pl.program_id(2)
    groups = low_ref.shape[1] // 3
    query_low = (jnp.concatenate(query_parts, axis=0) * 0.125).T
    key_low = jnp.where(lane < HD, key_parts[0], key_parts[1])
    value_low = jnp.where(lane < HD, value_parts[0], value_parts[1])
    for place, part in enumerate((query_low, key_low, value_low)):
        start = pl.multiple_of(place * groups + pair * PAIR, PAIR)
        low = part.astype(jnp.bfloat16)
        low_ref[:, pl.ds(start, PAIR)] = low
        sums_ref[0, :, pl.ds(start, PAIR)] = jnp.sum(
            low.astype(jnp.float32), axis=0, keepdims=True
        )


def attention_specs(slots, pairs):
    def at(part):
        return pl.BlockSpec(
            (slots, PAIR), lambda b, g, p, *_: (b, g * 3 * pairs + part * pairs + p)
        )

    heads = pl.BlockSpec((slots, PAIR), lambda b, g, p, *_: (b, g * pairs + p))
    totals = pl.BlockSpec((1, 1, 2, slots), lambda b, g, p, *_: (b, g * pairs + p, 0, 0))
    return [at(0), at(1), at(2)], heads, totals


def attend(facts, projected, slots):
    pairs = projected.shape[1] // (6 * PAIR)
    inputs, heads, totals = attention_specs(slots, pairs)
    rows = projected.shape[0]
    return pl.pallas_call(
        attend_kernel,
        grid_spec=pltpu.PrefetchScalarGridSpec(
            num_scalar_prefetch=1,
            grid=(2, 2, pairs),
            in_specs=inputs,
            out_specs=[heads, totals],
        ),
        out_shape=[
            jax.ShapeDtypeStruct((rows, 2 * pairs * PAIR), jnp.bfloat16),
            jax.ShapeDtypeStruct((2, 2 * pairs, 2, slots), jnp.float32),
        ],
        compiler_params=kernel_params(3),
        name="attend",
    )(facts, projected, projected, projected)


def attend_back(facts, projected, heads_grad, totals_in, slots):
    pairs = projected.shape[1] // (6 * PAIR)
    inputs, heads, totals = attention_specs(slots, pairs)
    return pl.pallas_call(
        attend_back_kernel,
        grid_spec=pltpu.PrefetchScalarGridSpec(
            num_scalar_prefetch=1,
            grid=(2, 2, pairs),
            in_specs=inputs + [heads, totals],
            out_specs=[
                pl.BlockSpec((slots, 3 * pairs * PAIR), lambda b, g, p, *_: (b, g)),
                pl.BlockSpec((1, 1, 3 * pairs * PAIR), lambda b, g, p, *_: (b, 0, g)),
            ],
        ),
        out_shape=[
            jax.ShapeDtypeStruct(projected.shape, jnp.bfloat16),
            jax.ShapeDtypeStruct((2, 1, projected.shape[1]), jnp.float32),
        ],
        compiler_params=kernel_params(3),
        name="attend_back",
    )(facts, projected, projected, projected, heads_grad, totals_in)


def call(kernel, name, grid, inputs, outputs, shapes, facts, *args):
    return pl.pallas_call(
        kernel,
        grid_spec=pltpu.PrefetchScalarGridSpec(
            num_scalar_prefetch=1, grid=grid, in_specs=inputs, out_specs=outputs
        ),
        out_shape=shapes,
        compiler_params=kernel_params(len(grid)),
        name=name,
    )(facts, *args)


def block(shape, *index):
    def at(*grid_and_facts):
        return tuple(entry(*grid_and_facts) if callable(entry) else entry for entry in index)

    return pl.BlockSpec(shape, at)


def whole(array):
    zeros = (0,) * array.ndim
    return pl.BlockSpec(array.shape, lambda *_: zeros)


def first(i, *_):
    return i


def like(shape, dtype):
    return jax.ShapeDtypeStruct(shape, dtype)


def near_rows(top, low):
    pieces = []
    for chip in range(top.shape[0]):
        pieces += [top[chip], low[chip]]
    return jnp.concatenate(pieces, axis=0)


def project_kernel(facts_ref, rows_ref, top_ref, low_ref, bias_ref, out_ref):
    weight = near_rows(top_ref[0], low_ref[:, 0])
    out_ref[...] = (product(rows_ref[...], weight, 1, 0) + bias_ref[...]).astype(jnp.bfloat16)


def project(facts, rows, top, low, bias, wide):
    count, width = rows.shape
    steps = 3
    return call(
        project_kernel,
        "project",
        (2 * steps,),
        [
            whole(rows),
            block((1,) + top.shape[1:3] + (wide,), lambda i, *_: i // steps, 0, 0, lambda i, *_: i % steps),
            block((low.shape[0], 1, low.shape[2], wide), 0, lambda i, *_: i // steps, 0, lambda i, *_: i % steps),
            block((1, wide), 0, first),
        ],
        block((count, wide), 0, first),
        like((count, 2 * steps * wide), jnp.bfloat16),
        facts,
        rows,
        top,
        low,
        bias[None],
    )


def valid_rows(facts_ref, count, slots):
    place = lax.broadcasted_iota(jnp.int32, (count, 1), 0) + pl.program_id(0) * count + facts_ref[2]
    place = jnp.where(place >= slots, place - slots, place)
    return (place < facts_ref[0]).astype(jnp.float32)


def add_rows(sums_ref, rows):
    total = jnp.concatenate([jnp.sum(part, axis=0, keepdims=True) for part in rows], axis=0)
    total = jnp.concatenate([total, jnp.zeros((8 - len(rows), total.shape[1]), jnp.float32)], axis=0)

    @pl.when(pl.program_id(0) == 0)
    def _():
        sums_ref[...] = total

    @pl.when(pl.program_id(0) > 0)
    def _():
        sums_ref[...] += total


def mean_of(values):
    return jnp.mean(values, axis=-1, keepdims=True)


def out_rows(weight, half, column):
    rows = weight.shape[3] // 2
    part = weight[:, half, :, column * rows : (column + 1) * rows, :]
    return part.reshape(-1, weight.shape[4])


def attend_out_kernel(
    slots, facts_ref, own_ref, other_ref, own_weight_ref, other_weight_ref, tokens_ref, vectors_ref,
    hat_ref, rstd_ref, low_ref, sums_ref,
):
    own, other = own_ref[...], other_ref[...]
    own_weight, other_weight = own_weight_ref[...], other_weight_ref[...]
    parts = []
    for half in range(2):
        for column in range(2):
            parts.append(
                product(own, out_rows(own_weight, half, column), 1, 0)
                + product(other, out_rows(other_weight, half, column), 1, 0)
            )
    branch = jnp.concatenate(parts, axis=1) + vectors_ref[0:1]
    tokens = tokens_ref[...].astype(jnp.float32)
    total = tokens + branch
    centered = total - mean_of(total)
    rstd = lax.rsqrt(mean_of(centered * centered) + 1e-05)
    hat = centered * rstd
    hat_ref[...] = hat
    rstd_ref[...] = rstd
    low_ref[...] = (hat * vectors_ref[1:2] + vectors_ref[2:3]).astype(jnp.bfloat16)
    valid = valid_rows(facts_ref, tokens.shape[0], slots)
    add_rows(sums_ref, [valid * tokens * tokens, valid * branch * branch])


def attend_out(facts, own, other, own_weight, other_weight, tokens, vectors):
    slots, width = tokens.shape
    step = slots // 2
    rows = lambda array: block((step, array.shape[1]), first, 0)
    return call(
        partial(attend_out_kernel, slots),
        "attend_out",
        (2,),
        [rows(own), rows(other), whole(own_weight), whole(other_weight), rows(tokens), whole(vectors)],
        [block((step, width), first, 0), block((step, 1), first, 0), block((step, width), first, 0), block((8, width), 0, 0)],
        [
            like((slots, width), jnp.float32),
            like((slots, 1), jnp.float32),
            like((slots, width), jnp.bfloat16),
            like((8, width), jnp.float32),
        ],
        facts,
        own,
        other,
        own_weight,
        other_weight,
        tokens,
        vectors,
    )


def up_kernel(facts_ref, rows_ref, weight_ref, bias_ref, act_ref, slope_ref):
    weight = weight_ref[...].reshape(rows_ref.shape[1], weight_ref.shape[3])
    pre_act = product(rows_ref[...], weight, 1, 0) + bias_ref[...]
    below = 0.5 + 0.5 * lax.erf(pre_act * 0.7071067811865476)
    act_ref[...] = (pre_act * below).astype(jnp.bfloat16)
    slope = below + pre_act * (0.3989422804014327 * jnp.exp(-0.5 * pre_act * pre_act))
    slope_ref[...] = slope.astype(jnp.bfloat16)


def feed_up(facts, rows, weights, bias):
    count, width = rows.shape
    chips, wide = weights.shape[0], weights.shape[3] // 2
    shape = like((count, 4 * wide), jnp.bfloat16)
    out = block((count, wide), 0, first)
    return call(
        up_kernel,
        "feed_up",
        (4,),
        [
            whole(rows),
            block((chips, 1, width // chips, wide), 0, lambda i, *_: i // 2, 0, lambda i, *_: i % 2),
            block((1, wide), 0, first),
        ],
        [out, out],
        [shape, shape],
        facts,
        rows,
        weights,
        bias[None],
    )


def down_kernel(facts_ref, rows_ref, weight_ref, out_ref):
    weight = weight_ref[...].reshape(rows_ref.shape[1], weight_ref.shape[3])
    out_ref[...] = product(rows_ref[...], weight, 1, 0).astype(out_ref.dtype)


def feed_down(facts, rows, part, weights, dtype):
    count, units = rows.shape
    wide = weights.shape[3]
    return call(
        down_kernel,
        "feed_down",
        (2,),
        [
            block((count // 2, units), part, 0),
            block((1,) + weights.shape[1:], first, 0, 0, 0),
        ],
        block((count // 2, wide), 0, first),
        like((count // 2, 2 * wide), dtype),
        facts,
        rows,
        weights,
    )


def second_norm_kernel(
    slots, facts_ref, part_ref, other_ref, hat_ref, cotangent_ref, vectors_ref,
    mixed_ref, grad_ref, low_ref, sums_ref,
):
    branch = part_ref[...] + other_ref[...].astype(jnp.float32) + vectors_ref[0:1]
    hidden = hat_ref[...] * vectors_ref[1:2] + vectors_ref[2:3]
    gain = vectors_ref[3:4]
    total = hidden + branch
    centered = total - mean_of(total)
    rstd = lax.rsqrt(mean_of(centered * centered) + 1e-05)
    hat = centered * rstd
    mixed_ref[...] = (hat * gain + vectors_ref[4:5]).astype(jnp.bfloat16)
    valid = valid_rows(facts_ref, branch.shape[0], slots)
    grad = cotangent_ref[...].astype(jnp.float32) * valid
    scaled = grad * gain
    result = rstd * (scaled - mean_of(scaled) - hat * mean_of(scaled * hat))
    low = result.astype(jnp.bfloat16)
    grad_ref[...] = result
    low_ref[...] = low
    add_rows(sums_ref, [low.astype(jnp.float32), grad * hat, grad, valid * branch * branch])


def second_norm(facts, part, other, hat, cotangent, vectors):
    slots, width = part.shape
    step = slots // 2
    rows = block((step, width), first, 0)
    return call(
        partial(second_norm_kernel, slots),
        "second_norm",
        (2,),
        [rows, rows, rows, rows, whole(vectors)],
        [rows, rows, rows, block((8, width), 0, 0)],
        [
            like((slots, width), jnp.bfloat16),
            like((slots, width), jnp.float32),
            like((slots, width), jnp.bfloat16),
            like((8, width), jnp.float32),
        ],
        facts,
        part,
        other,
        hat,
        cotangent,
        vectors,
    )


def first_norm_kernel(
    facts_ref, part_ref, other_ref, second_ref, hat_ref, rstd_ref, vectors_ref,
    grad_ref, low_ref, sums_ref,
):
    grad = part_ref[...] + other_ref[...].astype(jnp.float32) + second_ref[...]
    hat = hat_ref[...]
    scaled = grad * vectors_ref[1:2]
    result = rstd_ref[...] * (scaled - mean_of(scaled) - hat * mean_of(scaled * hat))
    low = result.astype(jnp.bfloat16)
    grad_ref[...] = result
    low_ref[...] = low
    add_rows(sums_ref, [low.astype(jnp.float32), grad * hat, grad])


def first_norm(facts, part, other, second, hat, rstd, vectors):
    slots, width = part.shape
    step = slots // 2
    rows = block((step, width), first, 0)
    return call(
        first_norm_kernel,
        "first_norm",
        (2,),
        [rows, rows, rows, rows, block((step, 1), first, 0), whole(vectors)],
        [rows, rows, block((8, width), 0, 0)],
        [
            like((slots, width), jnp.float32),
            like((slots, width), jnp.bfloat16),
            like((8, width), jnp.float32),
        ],
        facts,
        part,
        other,
        second,
        hat,
        rstd,
        vectors,
    )


def act_grad_kernel(facts_ref, rows_ref, weight_ref, slope_ref, out_ref, sums_ref):
    wide = weight_ref.shape[3]
    total = 0.0
    for half in range(2):
        weight = weight_ref[half].reshape(-1, wide)
        total = total + product(rows_ref[:, half * wide : (half + 1) * wide], weight, 1, 1)
    grad = total.astype(jnp.bfloat16).astype(jnp.float32) * slope_ref[...].astype(jnp.float32)
    low = grad.astype(jnp.bfloat16)
    out_ref[...] = low
    sums_ref[...] = jnp.sum(low.astype(jnp.float32), axis=0, keepdims=True)


def act_grad(facts, rows, weights, slope):
    count, units = slope.shape
    chips, wide = weights.shape[1], weights.shape[3]
    step = units // 4
    out = block((count, step), 0, first)
    return call(
        act_grad_kernel,
        "act_grad",
        (4,),
        [whole(rows), block((2, chips // 4, units // chips, wide), 0, first, 0, 0), out],
        [out, block((1, step), 0, first)],
        [like((count, units), jnp.bfloat16), like((1, units), jnp.float32)],
        facts,
        rows,
        weights,
        slope,
    )


def hidden_grad_kernel(facts_ref, rows_ref, weight_ref, out_ref):
    wide = weight_ref.shape[3]
    total = 0.0
    for half in range(2):
        weight = weight_ref[:, half].reshape(-1, wide)
        total = total + product(rows_ref[:, half * wide : (half + 1) * wide], weight, 1, 1)
    out_ref[...] = total.astype(out_ref.dtype)


def hidden_grad_part(facts, rows, part, weights, width, dtype):
    count, units = rows.shape
    chips = weights.shape[0]
    return call(
        hidden_grad_kernel,
        "hidden_grad",
        (2,),
        [
            block((count // 2, units), part, 0),
            block((chips // 2,) + weights.shape[1:], first, 0, 0, 0),
        ],
        block((count // 2, width // 2), 0, first),
        like((count // 2, width), dtype),
        facts,
        rows,
        weights,
    )


def heads_grad_kernel(facts_ref, rows_ref, own_ref, other_ref, out_own_ref, out_other_ref):
    for weight_ref, out_ref in ((own_ref, out_own_ref), (other_ref, out_other_ref)):
        weight = weight_ref[...]
        wide = weight.shape[4]
        total = 0.0
        for half in range(2):
            for column in range(2):
                start = (2 * half + column) * wide
                total = total + product(
                    rows_ref[:, start : start + wide], out_rows(weight, half, column), 1, 1
                )
        out_ref[...] = total.astype(jnp.bfloat16)


def heads_grads(facts, rows, own, other):
    count, width = rows.shape
    step = count // 2
    out = block((step, width // 2), first, 0)
    shape = like((count, width // 2), jnp.bfloat16)
    return call(
        heads_grad_kernel,
        "heads_grad",
        (2,),
        [block((step, width), first, 0), whole(own), whole(other)],
        [out, out],
        [shape, shape],
        facts,
        rows,
        own,
        other,
    )


def tokens_grad_kernel(wide, facts_ref, rows_ref, top_ref, low_ref, out_ref):
    total = 0.0
    for half in range(2):
        weight = near_rows(top_ref[half], low_ref[:, half])
        start = half * 3 * wide
        total = total + product(
            rows_ref[:, start : start + 3 * wide], weight[:, : 3 * wide], 1, 1
        )
    out_ref[...] = total.astype(out_ref.dtype)


def tokens_grad_part(facts, rows, part, top, low, wide, dtype):
    count, columns = rows.shape
    chips = low.shape[0]
    width = chips * 2 * low.shape[2]
    return call(
        partial(tokens_grad_kernel, wide),
        "tokens_grad",
        (2,),
        [
            block((count // 2, columns), part, 0),
            block((2, chips // 2) + top.shape[2:], 0, first, 0, 0),
            block((chips // 2,) + low.shape[1:], first, 0, 0, 0),
        ],
        block((count // 2, width // 2), 0, first),
        like((count // 2, width), dtype),
        facts,
        rows,
        top,
        low,
    )


def split_body(
    tokens,
    lengths,
    cotangent,
    query_weight,
    key_weight,
    value_weight,
    out_weight,
    up_weight,
    down_weight,
    query_bias,
    value_bias,
    out_bias,
    attn_gain,
    attn_shift,
    up_bias,
    down_bias,
    feed_gain,
    feed_shift,
):
    core = lax.axis_index("c")
    half = lax.axis_index("s")
    row_count, width = tokens.shape[1:]
    slots = 2 * row_count
    unit_block = down_weight.shape[0]
    units = up_bias.shape[0] // 2
    cols = width // 2
    wide = cols // 2

    small = [
        split_columns(weight, HD, core) for weight in (query_weight, key_weight, value_weight)
    ]
    large = split_columns(up_weight, unit_block, core)
    up_pair = in_order(large[0], swap(large[1], "c"), core)
    up_cols = up_pair.shape[2]
    up_mine = up_pair.reshape(-1, up_cols)
    rows = up_mine.shape[0]
    near_kept = jnp.concatenate([part[0] for part in small], axis=1)
    near_sent = jnp.concatenate([part[1] for part in small], axis=1)
    near_pair = in_order(near_kept, swap(near_sent, "c"), core)
    out_pair = out_weight.reshape(2, -1, 2, wide).transpose(0, 2, 1, 3)
    out_pair = out_pair.reshape(2, out_weight.shape[0], wide)
    near_pair = jnp.concatenate([near_pair, out_pair], axis=2)
    near_top = gather_top(near_pair[0])
    near_low = gather_low(near_pair[1])
    up_all = gather_low(up_mine)
    down_all = gather_top(down_weight)
    out_own = jnp.stack(
        [near_top[..., 3 * wide :].transpose(1, 0, 2, 3), near_low[..., 3 * wide :]], axis=2
    )
    out_other = swap(out_own, "c")

    def to_sequence(values):
        return jnp.concatenate([pick(values, half, 0), swap(pick(values, 1 - half, 0), "s")], axis=0)

    def from_sequence(values):
        return in_order(values[:row_count], swap(values[row_count:], "s"), half)

    tokens_own = to_sequence(tokens)
    tokens_both = both(tokens_own, "c")
    length_own = lax.dynamic_slice_in_dim(lengths, half, 1, 0)
    facts = jnp.concatenate(
        [
            both(length_own, "c"),
            jnp.stack([half * row_count, half, lax.axis_index("x")]).astype(jnp.int32),
        ]
    )

    def halves_of(vector, size):
        return pick(vector.reshape(-1, 2, size), core, 1).reshape(-1)

    query_part = halves_of(query_bias, HD).reshape(2, wide)
    value_part = halves_of(value_bias, HD).reshape(2, wide)
    in_bias = jnp.stack([query_part, jnp.zeros_like(query_part), value_part], axis=1).reshape(-1)
    projected = project(facts, tokens_both, near_top, near_low, in_bias, wide)
    projected, cotangent_own = lax.optimization_barrier((projected, to_sequence(cotangent)))
    heads_out, totals = attend(facts, projected, slots)
    heads_other = swap(heads_out[slots:], "c")
    vectors = jnp.stack(
        [out_bias, attn_gain, attn_shift, down_bias, feed_gain, feed_shift, out_bias, out_bias]
    )
    first_hat, first_rstd, hidden_low, first_sums = attend_out(
        facts, heads_out, heads_other, out_own, out_other, tokens_own, vectors
    )
    hidden_both = both(hidden_low, "c")
    activation, slope = feed_up(facts, hidden_both, up_all, halves_of(up_bias, unit_block))
    feed_other = swap(feed_down(facts, activation, 1, down_all, jnp.bfloat16), "c")
    feed_part = feed_down(facts, activation, 0, down_all, jnp.float32)
    feed_vectors = jnp.stack(
        [down_bias, attn_gain, attn_shift, feed_gain, feed_shift, out_bias, out_bias, out_bias]
    )
    mixed, second_grad, feed_low, second_sums = second_norm(
        facts, feed_part, feed_other, first_hat, cotangent_own, feed_vectors
    )
    mixed = from_sequence(mixed)

    feed_both = both(feed_low, "c")
    column = lax.axis_index("x")
    down_sum = scatter_top(
        grad_top(activation, feed_both, unit_block, 1 - half),
        grad_top(activation, feed_both, unit_block, half),
    )
    pre_grad, up_bias_grad = act_grad(facts, feed_both, down_all, slope)
    hidden_other = swap(hidden_grad_part(facts, pre_grad, 1, up_all, width, jnp.bfloat16), "c")
    hidden_part = hidden_grad_part(facts, pre_grad, 0, up_all, width, jnp.float32)
    up_sum = scatter_low(
        grad_low(rows_of(hidden_both, rows, 1 - column), pre_grad, rows),
        grad_low(rows_of(hidden_both, rows, column), pre_grad, rows),
    )
    first_grad, attn_low, third_sums = first_norm(
        facts, hidden_part, hidden_other, second_grad, first_hat, first_rstd, vectors
    )
    grad_own, grad_sent = heads_grads(facts, attn_low, out_own, out_other)
    heads_grad = jnp.concatenate([grad_own, swap(grad_sent, "c")], axis=0)
    out_part = product(heads_out[:slots], attn_low, 0, 0)
    out_sent = product(heads_other, attn_low, 0, 0).astype(jnp.bfloat16)
    out_grad = (out_part + swap(out_sent, "c").astype(jnp.float32)).astype(jnp.bfloat16)
    in_low, in_sums = attend_back(facts, projected, heads_grad, totals, slots)
    out_sent = lax.dynamic_slice_in_dim(out_grad, (1 - half) * cols, cols, 1)
    out_kept = lax.dynamic_slice_in_dim(out_grad, half * cols, cols, 1)
    out_sum = scatter_top(
        out_sent.reshape((8,) + out_weight.shape), out_kept.reshape((8,) + out_weight.shape)
    )
    cut = 3 * wide // 2
    in_cuts = [in_low[:, i * cut : (i + 1) * cut] for i in range(4)]
    in_top = jnp.concatenate([in_cuts[0], in_cuts[2]], axis=1)
    in_below = jnp.concatenate([in_cuts[1], in_cuts[3]], axis=1)
    in_sum = jnp.concatenate(
        [
            scatter_top(
                grad_top(tokens_both, in_top, rows, 1 - half), grad_top(tokens_both, in_top, rows, half)
            ),
            scatter_low(
                grad_low(rows_of(tokens_both, rows, 1 - column), in_below, rows),
                grad_low(rows_of(tokens_both, rows, column), in_below, rows),
            ),
        ],
        axis=1,
    )
    tokens_other = swap(
        tokens_grad_part(facts, in_low, 1, near_top, near_low, wide, jnp.bfloat16), "c"
    )
    tokens_part = tokens_grad_part(facts, in_low, 0, near_top, near_low, wide, jnp.float32)
    tokens_grad = tokens_part + tokens_other.astype(jnp.float32) + first_grad
    tokens_grad = from_sequence(tokens_grad.astype(jnp.bfloat16))

    in_bias_grad = jnp.sum(in_sums, axis=(0, 1))
    valid_count = length_own[0].astype(jnp.float32) * width
    stats = jnp.stack(
        [jnp.sum(first_sums[0]), jnp.sum(first_sums[1]), jnp.sum(second_sums[3]), valid_count]
    )
    shared = jnp.concatenate(
        [second_sums[:3].reshape(-1), third_sums[:3].reshape(-1), jnp.pad(stats, (0, 124))]
    )
    own_sums = total_over(
        jnp.concatenate(
            [
                shared,
                up_bias_grad[0],
                in_bias_grad[:wide],
                in_bias_grad[3 * wide : 4 * wide],
                in_bias_grad[2 * wide : 3 * wide],
                in_bias_grad[5 * wide :],
            ]
        )
    )
    other_sums = swap(own_sums, "c")
    count = shared.shape[0]
    shared = own_sums[:count] + other_sums[:count]
    down_bias_grad, feed_gain_grad, feed_shift_grad, out_bias_grad, attn_gain_grad, attn_shift_grad = [
        shared[i * width : (i + 1) * width] for i in range(6)
    ]
    stats = shared[6 * width : 6 * width + 4]

    def interleave(start, size, block):
        own = own_sums[start : start + size].reshape(-1, block)
        other = other_sums[start : start + size].reshape(-1, block)
        first = jnp.where(core == 0, own, other)
        second = jnp.where(core == 0, other, own)
        return jnp.stack([first, second], axis=1).reshape(-1)

    up_bias_grad = interleave(count, units, unit_block)
    query_bias_grad = interleave(count + units, cols, HD)
    value_bias_gradient = interleave(count + units + cols, cols, HD)
    stream_rms = jnp.sqrt(stats[:3] / stats[3])

    joined = jnp.concatenate([in_sum, up_sum], axis=1)
    joined = joined.reshape((2, rows // 2) + joined.shape[1:])
    own = pick(joined, core, 0)
    other = swap(pick(joined, 1 - core, 0), "c")
    down_weight_grad = down_sum.astype(jnp.float32)
    out_weight_grad = out_sum.astype(jnp.float32)

    def merge(start, size, block):
        one = own[:, start : start + size].reshape(rows // 2, -1, block)
        two = other[:, start : start + size].reshape(rows // 2, -1, block)
        first = jnp.where(core == 0, one, two)
        second = jnp.where(core == 0, two, one)
        return jnp.stack([first, second], axis=2).reshape(rows // 2, -1).astype(jnp.float32)

    query_weight_grad = merge(0, wide, HD)
    key_weight_grad = merge(wide, wide, HD)
    value_weight_grad = merge(2 * wide, wide, HD)
    up_weight_grad = merge(3 * wide, up_cols, unit_block)
    return (
        mixed,
        tokens_grad,
        query_weight_grad,
        key_weight_grad,
        value_weight_grad,
        out_weight_grad,
        up_weight_grad,
        down_weight_grad,
        query_bias_grad,
        value_bias_gradient,
        out_bias_grad,
        attn_gain_grad,
        attn_shift_grad,
        up_bias_grad,
        down_bias_grad,
        feed_gain_grad,
        feed_shift_grad,
        stream_rms,
    )


def solution(mesh):
    devices = mesh.devices
    dp_count, seq_count = devices.shape
    split = seq_count == 2 and dp_count == 16
    if split:
        inner = jax.sharding.Mesh(devices.reshape(4, 2, 2, seq_count), ("z", "x", "c", "s"))
        dp, seq, body = ("z", "x", "c"), "s", split_body
    else:
        inner, dp, seq, body = mesh, "dp", "seq", general_body
    weights = (P(dp, seq),) * 6
    vectors = (P(),) * 9
    rows = P(dp, seq, None)
    in_specs = (rows, P(dp), rows) + weights + vectors
    out_specs = (rows, rows) + weights + vectors + (P(),)
    return jax.shard_map(body, mesh=inner, in_specs=in_specs, out_specs=out_specs, check_vma=False)
```

```python
from functools import partial
import math

import jax
import jax.numpy as jnp
from jax import lax
from jax.experimental import pallas as pl
from jax.experimental.pallas import tpu as pltpu
from jax.sharding import PartitionSpec as P

HD = 64


def layer_norm(values_in, gain_vector, shift_vector):
    mean_value = jnp.mean(values_in, axis=-1, keepdims=True)
    centered = values_in - mean_value
    variance = jnp.mean(centered * centered, axis=-1, keepdims=True)
    return centered * lax.rsqrt(variance + 1e-05) * gain_vector + shift_vector


def gather_weights(first, second, third, fourth, fifth, sixth):
    part = (
        lax.all_gather(first, "dp", axis=0, tiled=True),
        lax.all_gather(second, "dp", axis=0, tiled=True),
        lax.all_gather(third, "dp", axis=0, tiled=True),
        lax.all_gather(fourth, "dp", axis=0, tiled=True),
        lax.all_gather(fifth, "dp", axis=0, tiled=True),
        lax.all_gather(sixth, "dp", axis=0, tiled=True),
    )
    return (
        lax.all_gather(part[0], "seq", axis=1, tiled=True),
        lax.all_gather(part[1], "seq", axis=1, tiled=True),
        lax.all_gather(part[2], "seq", axis=1, tiled=True),
        lax.all_gather(part[3], "seq", axis=1, tiled=True),
        lax.all_gather(part[4], "seq", axis=1, tiled=True),
        lax.all_gather(part[5], "seq", axis=1, tiled=True),
    )


def reduce_grads(first, second, third, fourth, fifth, sixth):
    part = (
        lax.psum_scatter(first.astype(jnp.bfloat16), "seq", scatter_dimension=1, tiled=True).astype(
            jnp.float32
        ),
        lax.psum_scatter(
            second.astype(jnp.bfloat16), "seq", scatter_dimension=1, tiled=True
        ).astype(jnp.float32),
        lax.psum_scatter(third.astype(jnp.bfloat16), "seq", scatter_dimension=1, tiled=True).astype(
            jnp.float32
        ),
        lax.psum_scatter(
            fourth.astype(jnp.bfloat16), "seq", scatter_dimension=1, tiled=True
        ).astype(jnp.float32),
        lax.psum_scatter(fifth.astype(jnp.bfloat16), "seq", scatter_dimension=1, tiled=True).astype(
            jnp.float32
        ),
        lax.psum_scatter(sixth.astype(jnp.bfloat16), "seq", scatter_dimension=1, tiled=True).astype(
            jnp.float32
        ),
    )
    return (
        lax.psum_scatter(
            part[0].astype(jnp.bfloat16), "dp", scatter_dimension=0, tiled=True
        ).astype(jnp.float32),
        lax.psum_scatter(
            part[1].astype(jnp.bfloat16), "dp", scatter_dimension=0, tiled=True
        ).astype(jnp.float32),
        lax.psum_scatter(
            part[2].astype(jnp.bfloat16), "dp", scatter_dimension=0, tiled=True
        ).astype(jnp.float32),
        lax.psum_scatter(
            part[3].astype(jnp.bfloat16), "dp", scatter_dimension=0, tiled=True
        ).astype(jnp.float32),
        lax.psum_scatter(
            part[4].astype(jnp.bfloat16), "dp", scatter_dimension=0, tiled=True
        ).astype(jnp.float32),
        lax.psum_scatter(
            part[5].astype(jnp.bfloat16), "dp", scatter_dimension=0, tiled=True
        ).astype(jnp.float32),
    )


def block_layout(seq_count, row_count, head_count):
    block_seqs = math.gcd(seq_count, max(1, 512 // row_count))
    group_heads = math.gcd(head_count, 4)
    return (block_seqs, seq_count // block_seqs, group_heads, head_count // group_heads)


def head_slice(block_part, offset, group_width, group_heads):
    sliced = lax.dynamic_slice_in_dim(block_part, offset, group_width, 2)
    return sliced.reshape(sliced.shape[0], sliced.shape[1], group_heads, HD)


def attention_forward(queries, key_all, value_all, key_mask):
    seq_count, row_count, feature_total = queries.shape
    slot_count = key_all.shape[1]
    block_seqs, block_count, group_heads, group_count = block_layout(
        seq_count, row_count, feature_total // HD
    )
    group_width = group_heads * HD

    def seq_block(inputs):
        query_part, key_part, value_part, mask_part = inputs

        def head_block(group_index):
            offset = group_index * group_width
            query_heads = head_slice(query_part, offset, group_width, group_heads)
            key_heads = head_slice(key_part, offset, group_width, group_heads)
            value_heads = head_slice(value_part, offset, group_width, group_heads)
            scores = (
                jnp.einsum(
                    "brhd,bkhd->bhrk", query_heads, key_heads, preferred_element_type=jnp.float32
                )
                * 0.125
            )
            scores = jnp.where(mask_part[:, None, None, :], scores, -1e30)
            row_max = jnp.max(scores, axis=-1, keepdims=True)
            exponent = jnp.exp(scores - row_max)
            row_total = jnp.sum(exponent, axis=-1, keepdims=True)
            soft_probs = (exponent / row_total).astype(jnp.bfloat16)
            heads_out = jnp.einsum(
                "bhrk,bkhd->brhd", soft_probs, value_heads, preferred_element_type=jnp.float32
            )
            log_total = (row_max + jnp.log(row_total))[..., 0]
            return (heads_out.reshape(block_seqs, row_count, group_width), log_total)

        return lax.map(head_block, jnp.arange(group_count))

    outputs, log_totals = lax.map(
        seq_block,
        (
            queries.reshape(block_count, block_seqs, row_count, feature_total),
            key_all.reshape(block_count, block_seqs, slot_count, feature_total),
            value_all.reshape(block_count, block_seqs, slot_count, feature_total),
            key_mask.reshape(block_count, block_seqs, slot_count),
        ),
    )
    mixed_heads = outputs.transpose(0, 2, 3, 1, 4).reshape(seq_count, row_count, feature_total)
    return (mixed_heads, log_totals)


def attention_backward(queries, key_all, value_all, key_mask, heads_grad, log_totals):
    seq_count, row_count, feature_total = queries.shape
    slot_count = key_all.shape[1]
    block_seqs, block_count, group_heads, group_count = block_layout(
        seq_count, row_count, feature_total // HD
    )
    group_width = group_heads * HD

    def seq_block(inputs):
        query_part, key_part, value_part, mask_part, grad_part, total_part = inputs

        def head_block(group_index):
            offset = group_index * group_width
            query_heads = head_slice(query_part, offset, group_width, group_heads)
            key_heads = head_slice(key_part, offset, group_width, group_heads)
            value_heads = head_slice(value_part, offset, group_width, group_heads)
            grad_heads = head_slice(grad_part, offset, group_width, group_heads)
            log_total = lax.dynamic_index_in_dim(total_part, group_index, 0, keepdims=False)
            scores = (
                jnp.einsum(
                    "brhd,bkhd->bhrk", query_heads, key_heads, preferred_element_type=jnp.float32
                )
                * 0.125
            )
            scores = jnp.where(mask_part[:, None, None, :], scores, -1e30)
            soft_probs = jnp.exp(scores - log_total[..., None])
            value_grad = jnp.einsum(
                "bhrk,brhd->bkhd",
                soft_probs.astype(jnp.bfloat16),
                grad_heads,
                preferred_element_type=jnp.float32,
            )
            prob_grad = jnp.einsum(
                "brhd,bkhd->bhrk", grad_heads, value_heads, preferred_element_type=jnp.float32
            )
            inner = jnp.sum(soft_probs * prob_grad, axis=-1, keepdims=True)
            score_grad = (soft_probs * (prob_grad - inner)).astype(jnp.bfloat16)
            query_grad = (
                jnp.einsum(
                    "bhrk,bkhd->brhd", score_grad, key_heads, preferred_element_type=jnp.float32
                )
                * 0.125
            )
            key_grad = (
                jnp.einsum(
                    "bhrk,brhd->bkhd", score_grad, query_heads, preferred_element_type=jnp.float32
                )
                * 0.125
            )
            return (
                query_grad.reshape(block_seqs, row_count, group_width),
                key_grad.reshape(block_seqs, slot_count, group_width),
                value_grad.reshape(block_seqs, slot_count, group_width),
            )

        return lax.map(head_block, jnp.arange(group_count))

    query_blocks, key_blocks, value_block_list = lax.map(
        seq_block,
        (
            queries.reshape(block_count, block_seqs, row_count, feature_total),
            key_all.reshape(block_count, block_seqs, slot_count, feature_total),
            value_all.reshape(block_count, block_seqs, slot_count, feature_total),
            key_mask.reshape(block_count, block_seqs, slot_count),
            heads_grad.reshape(block_count, block_seqs, row_count, feature_total),
            log_totals,
        ),
    )
    query_grad = query_blocks.transpose(0, 2, 3, 1, 4).reshape(seq_count, row_count, feature_total)
    key_grad = key_blocks.transpose(0, 2, 3, 1, 4).reshape(seq_count, slot_count, feature_total)
    value_grad = value_block_list.transpose(0, 2, 3, 1, 4).reshape(
        seq_count, slot_count, feature_total
    )
    return (query_grad, key_grad, value_grad)


def general_body(
    tokens,
    lengths,
    cotangent,
    query_weight,
    key_weight,
    value_weight,
    out_weight,
    up_weight,
    down_weight,
    query_bias,
    value_bias,
    out_bias,
    attn_gain,
    attn_shift,
    up_bias,
    down_bias,
    feed_gain,
    feed_shift,
):
    seq_count, row_count, feature_total = tokens.shape
    slot_count = row_count * lax.axis_size("seq")
    token_count = seq_count * row_count
    whole = gather_weights(
        query_weight, key_weight, value_weight, out_weight, up_weight, down_weight
    )
    full_query, full_key, full_value, full_out, full_up, full_down = whole
    flat_tokens = tokens.reshape(token_count, feature_total)
    queries = (
        jnp.dot(flat_tokens, full_query, preferred_element_type=jnp.float32) + query_bias
    ).astype(jnp.bfloat16)
    key_rows = jnp.dot(flat_tokens, full_key, preferred_element_type=jnp.float32).astype(
        jnp.bfloat16
    )
    value_rows = (
        jnp.dot(flat_tokens, full_value, preferred_element_type=jnp.float32) + value_bias
    ).astype(jnp.bfloat16)
    first_slot = lax.axis_index("seq") * row_count
    key_mask = jnp.arange(slot_count)[None, :] < lengths[:, None]
    row_valid = ((first_slot + jnp.arange(row_count))[None, :] < lengths[:, None]).astype(
        jnp.float32
    )
    row_valid = row_valid.reshape(token_count, 1)
    query_blocks = queries.reshape(seq_count, row_count, feature_total)
    key_blocks = key_rows.reshape(seq_count, row_count, feature_total)
    value_block_list = value_rows.reshape(seq_count, row_count, feature_total)
    key_all, value_all = (
        lax.all_gather(key_blocks, "seq", axis=1, tiled=True),
        lax.all_gather(value_block_list, "seq", axis=1, tiled=True),
    )
    mixed_heads, log_totals = attention_forward(query_blocks, key_all, value_all, key_mask)
    heads_low = mixed_heads.reshape(token_count, feature_total).astype(jnp.bfloat16)
    attention_out = jnp.dot(heads_low, full_out, preferred_element_type=jnp.float32) + out_bias
    tokens_f32 = flat_tokens.astype(jnp.float32)
    first_sum = tokens_f32 + attention_out
    hidden, first_pull = jax.vjp(layer_norm, first_sum, attn_gain, attn_shift)
    hidden_low = hidden.astype(jnp.bfloat16)
    pre_act = jnp.dot(hidden_low, full_up, preferred_element_type=jnp.float32) + up_bias
    gelu_out, gelu_pull = jax.vjp(partial(jax.nn.gelu, approximate=False), pre_act)
    activation = gelu_out.astype(jnp.bfloat16)
    feed_out = jnp.dot(activation, full_down, preferred_element_type=jnp.float32) + down_bias
    result, second_pull = jax.vjp(layer_norm, hidden + feed_out, feed_gain, feed_shift)
    mixed = result.astype(jnp.bfloat16).reshape(seq_count, row_count, feature_total)
    partial_stats = jnp.stack(
        [
            jnp.sum(row_valid * tokens_f32 * tokens_f32),
            jnp.sum(row_valid * attention_out * attention_out),
            jnp.sum(row_valid * feed_out * feed_out),
            jnp.sum(row_valid) * feature_total,
        ]
    )
    back_weights = gather_weights(
        query_weight, key_weight, value_weight, out_weight, up_weight, down_weight
    )
    back_query, back_key, back_value, back_out, back_up, back_down = back_weights
    out_grad = cotangent.reshape(token_count, feature_total).astype(jnp.float32) * row_valid
    second_grad, feed_gain_grad, feed_shift_grad = second_pull(out_grad)
    feed_low = second_grad.astype(jnp.bfloat16)
    down_weight_grad = jnp.einsum(
        "nf,nd->fd", activation, feed_low, preferred_element_type=jnp.float32
    )
    down_bias_grad = jnp.sum(feed_low, axis=0, dtype=jnp.float32)
    act_grad = jnp.einsum(
        "nd,fd->nf", feed_low, back_down, preferred_element_type=jnp.float32
    ).astype(jnp.bfloat16)
    pre_grad = gelu_pull(act_grad.astype(jnp.float32))[0].astype(jnp.bfloat16)
    up_weight_grad = jnp.einsum(
        "nd,nf->df", hidden_low, pre_grad, preferred_element_type=jnp.float32
    )
    up_bias_grad = jnp.sum(pre_grad, axis=0, dtype=jnp.float32)
    hidden_grad = (
        jnp.einsum("nf,df->nd", pre_grad, back_up, preferred_element_type=jnp.float32) + second_grad
    )
    first_grad, attn_gain_grad, attn_shift_grad = first_pull(hidden_grad)
    attn_low = first_grad.astype(jnp.bfloat16)
    out_weight_grad = jnp.einsum(
        "nd,ne->de", heads_low, attn_low, preferred_element_type=jnp.float32
    )
    out_bias_grad = jnp.sum(attn_low, axis=0, dtype=jnp.float32)
    heads_grad = jnp.einsum(
        "ne,de->nd", attn_low, back_out, preferred_element_type=jnp.float32
    ).astype(jnp.bfloat16)
    heads_grad = heads_grad.reshape(seq_count, row_count, feature_total)
    query_grad, key_part_grad, value_part_grad = attention_backward(
        query_blocks, key_all, value_all, key_mask, heads_grad, log_totals
    )
    key_sum, value_sum = (
        lax.psum_scatter(
            key_part_grad.astype(jnp.bfloat16), "seq", scatter_dimension=1, tiled=True
        ).astype(jnp.float32),
        lax.psum_scatter(
            value_part_grad.astype(jnp.bfloat16), "seq", scatter_dimension=1, tiled=True
        ).astype(jnp.float32),
    )
    query_low = query_grad.reshape(token_count, feature_total).astype(jnp.bfloat16)
    key_low = key_sum.reshape(token_count, feature_total).astype(jnp.bfloat16)
    value_low = value_sum.reshape(token_count, feature_total).astype(jnp.bfloat16)
    query_weight_grad = jnp.einsum(
        "nd,ne->de", flat_tokens, query_low, preferred_element_type=jnp.float32
    )
    key_weight_grad = jnp.einsum(
        "nd,ne->de", flat_tokens, key_low, preferred_element_type=jnp.float32
    )
    value_weight_grad = jnp.einsum(
        "nd,ne->de", flat_tokens, value_low, preferred_element_type=jnp.float32
    )
    query_bias_grad = jnp.sum(query_low, axis=0, dtype=jnp.float32)
    value_bias_gradient = jnp.sum(value_low, axis=0, dtype=jnp.float32)
    tokens_grad = (
        jnp.einsum("ne,de->nd", query_low, back_query, preferred_element_type=jnp.float32)
        + jnp.einsum("ne,de->nd", key_low, back_key, preferred_element_type=jnp.float32)
        + jnp.einsum("ne,de->nd", value_low, back_value, preferred_element_type=jnp.float32)
        + first_grad
    )
    tokens_grad = tokens_grad.astype(jnp.bfloat16).reshape(seq_count, row_count, feature_total)
    matrix_grads = reduce_grads(
        query_weight_grad,
        key_weight_grad,
        value_weight_grad,
        out_weight_grad,
        up_weight_grad,
        down_weight_grad,
    )
    totals = lax.psum(
        (
            partial_stats,
            query_bias_grad,
            value_bias_gradient,
            out_bias_grad,
            attn_gain_grad,
            attn_shift_grad,
            up_bias_grad,
            down_bias_grad,
            feed_gain_grad,
            feed_shift_grad,
        ),
        ("dp", "seq"),
    )
    stream_rms = jnp.sqrt(totals[0][:3] / totals[0][3])
    return (
        mixed,
        tokens_grad,
        matrix_grads[0],
        matrix_grads[1],
        matrix_grads[2],
        matrix_grads[3],
        matrix_grads[4],
        matrix_grads[5],
        totals[1],
        totals[2],
        totals[3],
        totals[4],
        totals[5],
        totals[6],
        totals[7],
        totals[8],
        totals[9],
        stream_rms,
    )


def swap(value, axis):
    return lax.ppermute(value, axis, [(0, 1), (1, 0)])


def both(value, axis):
    return jnp.concatenate([value, swap(value, axis)], axis=0)


def in_order(own, other, index, axis=0):
    return jnp.where(
        index == 0, jnp.stack([own, other], axis=axis), jnp.stack([other, own], axis=axis)
    )


def split_columns(weight, width, core):
    rows = weight.shape[0]
    blocks = weight.reshape(rows, -1, 2, width)
    return pick(blocks, core, 2).reshape(rows, -1), pick(blocks, 1 - core, 2).reshape(rows, -1)


def pick(values, index, axis):
    return lax.dynamic_index_in_dim(values, index, axis, keepdims=False)


def add(left, right):
    return (left.astype(jnp.float32) + right.astype(jnp.float32)).astype(jnp.bfloat16)


def total_over(vector):
    vector = vector + swap(vector, "s")
    vector = vector + swap(vector, "x")
    vector = vector + lax.ppermute(vector, "z", [(0, 1), (1, 0), (2, 3), (3, 2)])
    return vector + lax.ppermute(vector, "z", [(0, 2), (2, 0), (1, 3), (3, 1)])


def fold(values, axis, dim):
    index = lax.axis_index(axis)
    return add(pick(values, index, dim), swap(pick(values, 1 - index, dim), axis))


NEXT = [(0, 1), (1, 0), (2, 3), (3, 2)]
CROSS = [(0, 2), (2, 0), (1, 3), (3, 1)]


def fold_line(values):
    place = lax.axis_index("z")
    odd, upper = place % 2, place // 2
    pairs = values.reshape((2, 2) + values.shape[1:])
    pairs = add(pick(pairs, odd, 1), lax.ppermute(pick(pairs, 1 - odd, 1), "z", NEXT))
    return add(pick(pairs, upper, 0), lax.ppermute(pick(pairs, 1 - upper, 0), "z", CROSS))


def after(value, *others):
    return lax.optimization_barrier((value,) + others)[0]


def line_cross(value):
    place = lax.axis_index("z")
    return in_order(value, lax.ppermute(value, "z", CROSS), place // 2)


def line_next(pair):
    place = lax.axis_index("z")
    whole = in_order(pair, lax.ppermute(pair, "z", NEXT), place % 2, 1)
    return whole.reshape((4,) + pair.shape[1:])


def gather_x(value):
    whole = in_order(value, swap(value, "x"), lax.axis_index("x"), 1)
    return whole.reshape((8,) + value.shape[1:])


def gather_y(value):
    other = swap(value, "s")
    return jnp.where(
        lax.axis_index("s") == 0,
        jnp.concatenate([value, other], axis=-1),
        jnp.concatenate([other, value], axis=-1),
    )


def scatter_top(send, keep):
    total = add(keep, swap(send, "s"))
    total = total.reshape((4, 2) + total.shape[1:])
    return fold_line(fold(total, "x", 1))


def scatter_low(send, keep):
    total = add(keep, swap(send, "x"))
    return fold_line(fold_columns(total))


def fold_columns(total):
    columns = total.shape[-1] // 2
    half = lax.axis_index("s")
    kept = lax.dynamic_slice_in_dim(total, half * columns, columns, total.ndim - 1)
    sent = lax.dynamic_slice_in_dim(total, (1 - half) * columns, columns, total.ndim - 1)
    return add(kept, swap(sent, "s"))


def grad_top(left_t, right, rows, half):
    columns = right.shape[1] // 2
    right = lax.dynamic_slice_in_dim(right, half * columns, columns, 1)
    return product(left_t, right, 1, 0).astype(jnp.bfloat16).reshape(-1, rows, columns)


def rows_of(left_t, rows, index):
    return pick(left_t.reshape(4, 2, rows, -1), index, 1).reshape(4 * rows, -1)


def grad_low(left_t, right, rows):
    return product(left_t, right, 1, 0).astype(jnp.bfloat16).reshape(4, rows, right.shape[1])


PAIR = 2 * HD
LIMIT = 56 * 1024 * 1024


def kernel_params(steps):
    return pltpu.CompilerParams(
        dimension_semantics=("arbitrary",) * steps, vmem_limit_bytes=LIMIT
    )


def product(left, right, left_dim, right_dim):
    return lax.dot_general(
        left, right, (((left_dim,), (right_dim,)), ((), ())), preferred_element_type=jnp.float32
    )


def key_bias(facts_ref, slots):
    place = lax.broadcasted_iota(jnp.int32, (slots, 1), 0) + facts_ref[2]
    place = jnp.where(place >= slots, place - slots, place)
    return jnp.where(place < facts_ref[pl.program_id(0)], 0.0, -1e30)


def head_lanes(value, head):
    lane = lax.broadcasted_iota(jnp.int32, value.shape, 1)
    return jnp.where((lane >= HD) == (head == 1), value, jnp.zeros_like(value))


def turned(value):
    return value.astype(jnp.float32).T


def attend_kernel(facts_ref, query_ref, key_ref, value_ref, out_ref, total_ref):
    slots = key_ref.shape[0]
    bias = key_bias(facts_ref, slots)
    query = query_ref[...] * jnp.bfloat16(0.125)
    key = key_ref[...]
    value_t = turned(value_ref[...]).astype(jnp.bfloat16)
    outs = []
    for head in range(2):
        scores = product(key, head_lanes(query, head), 1, 1) + bias
        peak = jnp.max(scores, axis=0, keepdims=True)
        weight = jnp.exp(scores - peak)
        total = jnp.sum(weight, axis=0, keepdims=True)
        part = product(value_t[head * HD : (head + 1) * HD], weight.astype(jnp.bfloat16), 1, 0)
        outs.append(part * (1.0 / total))
        total_ref[0, 0, head : head + 1, :] = peak + jnp.log(total)
    out_ref[...] = jnp.concatenate(outs, axis=0).T.astype(jnp.bfloat16)


def attend_back_kernel(
    facts_ref, query_ref, key_ref, value_ref, grad_ref, total_ref, low_ref, sums_ref
):
    slots = key_ref.shape[0]
    bias = key_bias(facts_ref, slots)
    query = query_ref[...] * jnp.bfloat16(0.125)
    key = key_ref[...]
    value = value_ref[...]
    grad = grad_ref[...]
    key_t = turned(key).astype(jnp.bfloat16)
    lane = lax.broadcasted_iota(jnp.int32, (slots, PAIR), 1)
    query_parts, key_parts, value_parts = [], [], []
    for head in range(2):
        scores = product(key, head_lanes(query, head), 1, 1) + bias
        soft = jnp.exp(scores - total_ref[0, 0, head : head + 1, :])
        value_parts.append(product(soft.astype(jnp.bfloat16), grad, 1, 0))
        change = product(value, head_lanes(grad, head), 1, 1)
        inner = jnp.sum(soft * change, axis=0, keepdims=True)
        change = (soft * (change - inner)).astype(jnp.bfloat16)
        key_parts.append(product(change, query, 1, 0))
        query_parts.append(product(key_t[head * HD : (head + 1) * HD], change, 1, 0))
    pair = pl.program_id(2)
    groups = low_ref.shape[1] // 3
    query_low = (jnp.concatenate(query_parts, axis=0) * 0.125).T
    key_low = jnp.where(lane < HD, key_parts[0], key_parts[1])
    value_low = jnp.where(lane < HD, value_parts[0], value_parts[1])
    for place, part in enumerate((query_low, key_low, value_low)):
        start = pl.multiple_of(place * groups + pair * PAIR, PAIR)
        low = part.astype(jnp.bfloat16)
        low_ref[:, pl.ds(start, PAIR)] = low
        sums_ref[0, :, pl.ds(start, PAIR)] = jnp.sum(
            low.astype(jnp.float32), axis=0, keepdims=True
        )


def attention_specs(slots, pairs):
    def at(part):
        return pl.BlockSpec(
            (slots, PAIR), lambda b, g, p, *_: (b, g * 3 * pairs + part * pairs + p)
        )

    heads = pl.BlockSpec((slots, PAIR), lambda b, g, p, *_: (b, g * pairs + p))
    totals = pl.BlockSpec((1, 1, 2, slots), lambda b, g, p, *_: (b, g * pairs + p, 0, 0))
    return [at(0), at(1), at(2)], heads, totals


def attend(facts, projected, slots):
    pairs = projected.shape[1] // (6 * PAIR)
    inputs, heads, totals = attention_specs(slots, pairs)
    rows = projected.shape[0]
    return pl.pallas_call(
        attend_kernel,
        grid_spec=pltpu.PrefetchScalarGridSpec(
            num_scalar_prefetch=1,
            grid=(2, 2, pairs),
            in_specs=inputs,
            out_specs=[heads, totals],
        ),
        out_shape=[
            jax.ShapeDtypeStruct((rows, 2 * pairs * PAIR), jnp.bfloat16),
            jax.ShapeDtypeStruct((2, 2 * pairs, 2, slots), jnp.float32),
        ],
        compiler_params=kernel_params(3),
        name="attend",
    )(facts, projected, projected, projected)


def attend_back(facts, projected, heads_grad, totals_in, slots):
    pairs = projected.shape[1] // (6 * PAIR)
    inputs, heads, totals = attention_specs(slots, pairs)
    return pl.pallas_call(
        attend_back_kernel,
        grid_spec=pltpu.PrefetchScalarGridSpec(
            num_scalar_prefetch=1,
            grid=(2, 2, pairs),
            in_specs=inputs + [heads, totals],
            out_specs=[
                pl.BlockSpec((slots, 3 * pairs * PAIR), lambda b, g, p, *_: (b, g)),
                pl.BlockSpec((1, 1, 3 * pairs * PAIR), lambda b, g, p, *_: (b, 0, g)),
            ],
        ),
        out_shape=[
            jax.ShapeDtypeStruct(projected.shape, jnp.bfloat16),
            jax.ShapeDtypeStruct((2, 1, projected.shape[1]), jnp.float32),
        ],
        compiler_params=kernel_params(3),
        name="attend_back",
    )(facts, projected, projected, projected, heads_grad, totals_in)


def call(kernel, name, grid, inputs, outputs, shapes, facts, *args):
    return pl.pallas_call(
        kernel,
        grid_spec=pltpu.PrefetchScalarGridSpec(
            num_scalar_prefetch=1, grid=grid, in_specs=inputs, out_specs=outputs
        ),
        out_shape=shapes,
        compiler_params=kernel_params(len(grid)),
        name=name,
    )(facts, *args)


def block(shape, *index):
    def at(*grid_and_facts):
        return tuple(entry(*grid_and_facts) if callable(entry) else entry for entry in index)

    return pl.BlockSpec(shape, at)


def whole(array):
    zeros = (0,) * array.ndim
    return pl.BlockSpec(array.shape, lambda *_: zeros)


def first(i, *_):
    return i


def like(shape, dtype):
    return jax.ShapeDtypeStruct(shape, dtype)


def near_rows(top, low):
    pieces = []
    for chip in range(top.shape[0]):
        pieces += [top[chip], low[chip]]
    return jnp.concatenate(pieces, axis=0)


def project_kernel(facts_ref, rows_ref, top_ref, low_ref, bias_ref, out_ref):
    weight = near_rows(top_ref[...], low_ref[...])
    out_ref[...] = (product(rows_ref[...], weight, 1, 0) + bias_ref[...]).astype(jnp.bfloat16)


def project(facts, rows, top, low, bias, wide):
    count, width = rows.shape
    steps = 3
    part = block(top.shape[:2] + (wide,), 0, 0, lambda i, *_: i + i // steps)
    return call(
        project_kernel,
        "project",
        (2 * steps,),
        [whole(rows), part, part, block((1, wide), 0, first)],
        block((count, wide), 0, first),
        like((count, 2 * steps * wide), jnp.bfloat16),
        facts,
        rows,
        top,
        low,
        bias[None],
    )


def valid_rows(facts_ref, count, slots):
    place = lax.broadcasted_iota(jnp.int32, (count, 1), 0) + pl.program_id(0) * count + facts_ref[2]
    place = jnp.where(place >= slots, place - slots, place)
    return (place < facts_ref[0]).astype(jnp.float32)


def add_rows(sums_ref, rows):
    total = jnp.concatenate([jnp.sum(part, axis=0, keepdims=True) for part in rows], axis=0)
    total = jnp.concatenate([total, jnp.zeros((8 - len(rows), total.shape[1]), jnp.float32)], axis=0)

    @pl.when(pl.program_id(0) == 0)
    def _():
        sums_ref[...] = total

    @pl.when(pl.program_id(0) > 0)
    def _():
        sums_ref[...] += total


def mean_of(values):
    return jnp.mean(values, axis=-1, keepdims=True)


def out_rows(weight, half, column):
    rows = weight.shape[3] // 2
    part = weight[:, half, :, column * rows : (column + 1) * rows, :]
    return part.reshape(-1, weight.shape[4])


def attend_out_kernel(
    slots, facts_ref, own_ref, other_ref, own_weight_ref, other_weight_ref, tokens_ref, vectors_ref,
    hat_ref, rstd_ref, low_ref, sums_ref,
):
    own, other = own_ref[...], other_ref[...]
    own_weight, other_weight = own_weight_ref[...], other_weight_ref[...]
    parts = []
    for half in range(2):
        for column in range(2):
            parts.append(
                product(own, out_rows(own_weight, half, column), 1, 0)
                + product(other, out_rows(other_weight, half, column), 1, 0)
            )
    branch = jnp.concatenate(parts, axis=1) + vectors_ref[0:1]
    tokens = tokens_ref[...].astype(jnp.float32)
    total = tokens + branch
    centered = total - mean_of(total)
    rstd = lax.rsqrt(mean_of(centered * centered) + 1e-05)
    hat = centered * rstd
    hat_ref[...] = hat
    rstd_ref[...] = rstd
    low_ref[...] = (hat * vectors_ref[1:2] + vectors_ref[2:3]).astype(jnp.bfloat16)
    valid = valid_rows(facts_ref, tokens.shape[0], slots)
    add_rows(sums_ref, [valid * tokens * tokens, valid * branch * branch])


def attend_out(facts, own, other, own_weight, other_weight, tokens, vectors):
    slots, width = tokens.shape
    step = slots // 4
    rows = lambda array: block((step, array.shape[1]), first, 0)
    return call(
        partial(attend_out_kernel, slots),
        "attend_out",
        (4,),
        [rows(own), rows(other), whole(own_weight), whole(other_weight), rows(tokens), whole(vectors)],
        [block((step, width), first, 0), block((step, 1), first, 0), block((step, width), first, 0), block((8, width), 0, 0)],
        [
            like((slots, width), jnp.float32),
            like((slots, 1), jnp.float32),
            like((slots, width), jnp.bfloat16),
            like((8, width), jnp.float32),
        ],
        facts,
        own,
        other,
        own_weight,
        other_weight,
        tokens,
        vectors,
    )


def up_kernel(facts_ref, rows_ref, weight_ref, bias_ref, act_ref, act_t_ref, slope_ref):
    pre_act = product(rows_ref[...], weight_ref[...], 1, 0) + bias_ref[...]
    below = 0.5 + 0.5 * lax.erf(pre_act * 0.7071067811865476)
    act = (pre_act * below).astype(jnp.bfloat16)
    act_ref[...] = act
    act_t_ref[...] = act.T
    slope = below + pre_act * (0.3989422804014327 * jnp.exp(-0.5 * pre_act * pre_act))
    slope_ref[...] = slope.astype(jnp.bfloat16)


def feed_up(facts, rows, weight, bias):
    count, width = rows.shape
    units = weight.shape[1]
    wide = units // 8
    shape = like((count, units), jnp.bfloat16)
    out = block((count, wide), 0, first)
    return call(
        up_kernel,
        "feed_up",
        (8,),
        [whole(rows), block((width, wide), 0, first), block((1, wide), 0, first)],
        [out, block((wide, count), first, 0), out],
        [shape, like((units, count), jnp.bfloat16), shape],
        facts,
        rows,
        weight,
        bias[None],
    )


def second_norm_kernel(
    slots, facts_ref, part_ref, other_ref, hat_ref, cotangent_ref, vectors_ref,
    mixed_ref, grad_ref, low_ref, sums_ref,
):
    branch = part_ref[...] + other_ref[...].astype(jnp.float32) + vectors_ref[0:1]
    hidden = hat_ref[...] * vectors_ref[1:2] + vectors_ref[2:3]
    gain = vectors_ref[3:4]
    total = hidden + branch
    centered = total - mean_of(total)
    rstd = lax.rsqrt(mean_of(centered * centered) + 1e-05)
    hat = centered * rstd
    mixed_ref[...] = (hat * gain + vectors_ref[4:5]).astype(jnp.bfloat16)
    valid = valid_rows(facts_ref, branch.shape[0], slots)
    grad = cotangent_ref[...].astype(jnp.float32) * valid
    scaled = grad * gain
    result = rstd * (scaled - mean_of(scaled) - hat * mean_of(scaled * hat))
    low = result.astype(jnp.bfloat16)
    grad_ref[...] = result
    low_ref[...] = low
    add_rows(sums_ref, [low.astype(jnp.float32), grad * hat, grad, valid * branch * branch])


def second_norm(facts, part, other, hat, cotangent, vectors):
    slots, width = part.shape
    step = slots // 4
    rows = block((step, width), first, 0)
    return call(
        partial(second_norm_kernel, slots),
        "second_norm",
        (4,),
        [rows, rows, rows, rows, whole(vectors)],
        [rows, rows, rows, block((8, width), 0, 0)],
        [
            like((slots, width), jnp.bfloat16),
            like((slots, width), jnp.float32),
            like((slots, width), jnp.bfloat16),
            like((8, width), jnp.float32),
        ],
        facts,
        part,
        other,
        hat,
        cotangent,
        vectors,
    )


def first_norm_kernel(
    facts_ref, part_ref, other_ref, second_ref, hat_ref, rstd_ref, vectors_ref,
    grad_ref, low_ref, sums_ref,
):
    grad = part_ref[...] + other_ref[...].astype(jnp.float32) + second_ref[...]
    hat = hat_ref[...]
    scaled = grad * vectors_ref[1:2]
    result = rstd_ref[...] * (scaled - mean_of(scaled) - hat * mean_of(scaled * hat))
    low = result.astype(jnp.bfloat16)
    grad_ref[...] = result
    low_ref[...] = low
    add_rows(sums_ref, [low.astype(jnp.float32), grad * hat, grad])


def first_norm(facts, part, other, second, hat, rstd, vectors):
    slots, width = part.shape
    step = slots // 4
    rows = block((step, width), first, 0)
    return call(
        first_norm_kernel,
        "first_norm",
        (4,),
        [rows, rows, rows, rows, block((step, 1), first, 0), whole(vectors)],
        [rows, rows, block((8, width), 0, 0)],
        [
            like((slots, width), jnp.float32),
            like((slots, width), jnp.bfloat16),
            like((8, width), jnp.float32),
        ],
        facts,
        part,
        other,
        second,
        hat,
        rstd,
        vectors,
    )


def act_grad_kernel(facts_ref, rows_ref, weight_ref, slope_ref, out_ref, sums_ref):
    total = product(rows_ref[...], weight_ref[...], 1, 1)
    grad = total.astype(jnp.bfloat16).astype(jnp.float32) * slope_ref[...].astype(jnp.float32)
    low = grad.astype(jnp.bfloat16)
    out_ref[...] = low
    sums_ref[...] = jnp.sum(low.astype(jnp.float32), axis=0, keepdims=True)


def act_grad(facts, rows, weight, slope):
    count, units = slope.shape
    step = units // 8
    out = block((count, step), 0, first)
    return call(
        act_grad_kernel,
        "act_grad",
        (8,),
        [whole(rows), block((step, rows.shape[1]), first, 0), out],
        [out, block((1, step), 0, first)],
        [like((count, units), jnp.bfloat16), like((1, units), jnp.float32)],
        facts,
        rows,
        weight,
        slope,
    )


def heads_grad_kernel(facts_ref, rows_ref, own_ref, other_ref, out_own_ref, out_other_ref):
    for weight_ref, out_ref in ((own_ref, out_own_ref), (other_ref, out_other_ref)):
        weight = weight_ref[...]
        wide = weight.shape[4]
        total = 0.0
        for half in range(2):
            for column in range(2):
                start = (2 * half + column) * wide
                total = total + product(
                    rows_ref[:, start : start + wide], out_rows(weight, half, column), 1, 1
                )
        out_ref[...] = total.astype(jnp.bfloat16)


def heads_grads(facts, rows, own, other):
    count, width = rows.shape
    step = count // 2
    out = block((step, width // 2), first, 0)
    shape = like((count, width // 2), jnp.bfloat16)
    return call(
        heads_grad_kernel,
        "heads_grad",
        (2,),
        [block((step, width), first, 0), whole(own), whole(other)],
        [out, out],
        [shape, shape],
        facts,
        rows,
        own,
        other,
    )


def split_body(
    tokens,
    lengths,
    cotangent,
    query_weight,
    key_weight,
    value_weight,
    out_weight,
    up_weight,
    down_weight,
    query_bias,
    value_bias,
    out_bias,
    attn_gain,
    attn_shift,
    up_bias,
    down_bias,
    feed_gain,
    feed_shift,
):
    core = lax.axis_index("c")
    half = lax.axis_index("s")
    row_count, width = tokens.shape[1:]
    slots = 2 * row_count
    unit_block = down_weight.shape[0]
    units = up_bias.shape[0] // 2
    cols = width // 2
    wide = cols // 2

    def to_sequence(values):
        return jnp.concatenate([pick(values, half, 0), swap(pick(values, 1 - half, 0), "s")], axis=0)

    def from_sequence(values):
        return in_order(values[:row_count], swap(values[row_count:], "s"), half)

    small = [
        split_columns(weight, HD, core) for weight in (query_weight, key_weight, value_weight)
    ]
    large = split_columns(up_weight, unit_block, core)
    up_pair = in_order(large[0], swap(large[1], "c"), core)
    up_cols = up_pair.shape[2]
    up_mine = up_pair.reshape(-1, up_cols)
    rows = up_mine.shape[0]
    near_kept = jnp.concatenate([part[0] for part in small], axis=1)
    near_sent = jnp.concatenate([part[1] for part in small], axis=1)
    near_pair = in_order(near_kept, swap(near_sent, "c"), core)
    out_pair = out_weight.reshape(2, -1, 2, wide).transpose(0, 2, 1, 3)
    out_pair = out_pair.reshape(2, out_weight.shape[0], wide)
    near_pair = jnp.concatenate([near_pair, out_pair], axis=2)
    tops = line_cross(near_pair[0])
    lows = line_cross(near_pair[1])
    up_part = line_cross(after(up_mine, tops, lows))
    down_part = line_cross(after(down_weight, tops, lows))
    tops = gather_x(line_next(tops))
    lows = gather_y(line_next(lows))
    up_part = line_next(after(up_part, tops, lows))
    down_part = line_next(after(down_part, tops, lows))
    near_top = gather_y(tops)
    near_low = gather_x(lows)
    tokens_own = to_sequence(tokens)
    tokens_both = both(tokens_own, "c")
    near_top, near_low, tokens_both, up_part, down_part = lax.optimization_barrier(
        (near_top, near_low, tokens_both, up_part, down_part)
    )
    up_part = gather_y(up_part)
    down_part = gather_x(down_part)
    packed = near_top.shape[2] // 2
    out_own = jnp.stack(
        [
            part.reshape(part.shape[:2] + (2, packed))[..., 3 * wide :].transpose(0, 2, 1, 3)
            for part in (near_top, near_low)
        ],
        axis=2,
    )
    out_other = swap(out_own, "c")

    length_own = lax.dynamic_slice_in_dim(lengths, half, 1, 0)
    facts = jnp.concatenate(
        [
            both(length_own, "c"),
            jnp.stack([half * row_count, half, lax.axis_index("x")]).astype(jnp.int32),
        ]
    )

    def halves_of(vector, size):
        return pick(vector.reshape(-1, 2, size), core, 1).reshape(-1)

    query_part = halves_of(query_bias, HD).reshape(2, wide)
    value_part = halves_of(value_bias, HD).reshape(2, wide)
    in_bias = jnp.stack([query_part, jnp.zeros_like(query_part), value_part], axis=1).reshape(-1)
    projected = project(facts, tokens_both, near_top, near_low, in_bias, wide)
    tokens_t, _ = lax.optimization_barrier((tokens_both.T, projected))
    heads_out, totals = attend(facts, projected, slots)
    heads_out, up_part, down_part, tokens_t = lax.optimization_barrier(
        (heads_out, up_part, down_part, tokens_t)
    )
    up_all = gather_x(up_part).reshape(width, units)
    down_all = gather_y(down_part).reshape(units, width)
    heads_other = swap(heads_out[slots:], "c")
    vectors = jnp.stack(
        [out_bias, attn_gain, attn_shift, down_bias, feed_gain, feed_shift, out_bias, out_bias]
    )
    first_hat, first_rstd, hidden_low, first_sums = attend_out(
        facts, heads_out, heads_other, out_own, out_other, tokens_own, vectors
    )
    hidden_both = both(hidden_low, "c")
    hidden_t = hidden_both.T
    near_both = jnp.stack([near_top, near_low], axis=1).reshape(width, 2, packed)
    in_weight = near_both[:, :, : 3 * wide].reshape(width, 6 * wide)
    hidden_both, hidden_t, in_weight = lax.optimization_barrier((hidden_both, hidden_t, in_weight))
    activation, act_t, slope = feed_up(facts, hidden_both, up_all, halves_of(up_bias, unit_block))
    feed_other = swap(
        product(activation[slots:], down_all, 1, 0).astype(jnp.bfloat16), "c"
    )
    cotangent_own = to_sequence(after(cotangent, heads_out))
    feed_part = product(after(activation, feed_other)[:slots], down_all, 1, 0)
    feed_vectors = jnp.stack(
        [down_bias, attn_gain, attn_shift, feed_gain, feed_shift, out_bias, out_bias, out_bias]
    )
    mixed, second_grad, feed_low, second_sums = second_norm(
        facts, feed_part, feed_other, first_hat, cotangent_own, feed_vectors
    )
    mixed = from_sequence(mixed)

    feed_both = both(feed_low, "c")
    column = lax.axis_index("x")
    down_sent = grad_top(act_t, feed_both, unit_block, 1 - half)
    pre_grad, up_bias_grad = act_grad(facts, after(feed_both, down_sent), down_all, slope)
    hidden_other = swap(product(pre_grad[slots:], up_all, 1, 1).astype(jnp.bfloat16), "c")
    up_sent = grad_low(rows_of(hidden_t, rows, 1 - column), pre_grad, rows)
    hidden_part = product(after(pre_grad, up_sent)[:slots], up_all, 1, 1)
    first_grad, attn_low, third_sums = first_norm(
        facts, hidden_part, hidden_other, second_grad, first_hat, first_rstd, vectors
    )
    grad_own, grad_sent = heads_grads(facts, attn_low, out_own, out_other)
    grad_other = swap(grad_sent, "c")
    out_sent = product(heads_other, attn_low, 0, 0).astype(jnp.bfloat16)
    out_grad = add(product(heads_out[:slots], attn_low, 0, 0), swap(out_sent, "c"))
    down_kept = grad_top(after(act_t, out_sent), feed_both, unit_block, half)
    up_kept = grad_low(rows_of(hidden_t, rows, column), after(pre_grad, out_sent), rows)
    out_grad = out_grad.reshape(4, 2, out_weight.shape[0], width)
    out_kept = pick(out_grad, column, 1)
    out_sent = pick(out_grad, 1 - column, 1)
    down_step = add(down_kept, swap(down_sent, "s"))
    up_step = add(up_kept, swap(up_sent, "x"))
    heads_grad = jnp.concatenate([grad_own, grad_other], axis=0)
    heads_grad, out_kept, out_sent, up_kept, down_step = lax.optimization_barrier(
        (heads_grad, out_kept, out_sent, up_kept, down_step)
    )
    in_low, in_sums = attend_back(facts, projected, heads_grad, totals, slots)
    cut = 3 * wide // 2
    in_cuts = [in_low[:, i * cut : (i + 1) * cut] for i in range(4)]
    in_top = jnp.concatenate([in_cuts[0], in_cuts[2]], axis=1)
    in_below = jnp.concatenate([in_cuts[1], in_cuts[3]], axis=1)
    in_top_sent = grad_top(tokens_t, in_top, rows, 1 - half)
    in_low_sent = grad_low(rows_of(tokens_t, rows, 1 - column), in_below, rows)
    in_top, in_below, _, _ = lax.optimization_barrier((in_top, in_below, in_top_sent, in_low_sent))
    in_top_kept = grad_top(tokens_t, in_top, rows, half)
    in_low_kept = grad_low(rows_of(tokens_t, rows, column), in_below, rows)
    tokens_other = swap(product(in_low[slots:], in_weight, 1, 1).astype(jnp.bfloat16), "c")
    tokens_part = product(in_low[:slots], in_weight, 1, 1)
    tokens_grad = tokens_part + tokens_other.astype(jnp.float32) + first_grad
    tokens_grad = from_sequence(tokens_grad.astype(jnp.bfloat16))
    down_step = down_step.reshape((4, 2) + down_step.shape[1:])
    down_sum = fold_line(fold(down_step, "x", 1))
    up_sum = fold_line(fold_columns(up_step))
    out_sum = scatter_low(out_sent, out_kept)
    in_sum = jnp.concatenate(
        [scatter_top(in_top_sent, in_top_kept), scatter_low(in_low_sent, in_low_kept)], axis=1
    )

    in_bias_grad = jnp.sum(in_sums, axis=(0, 1))
    valid_count = length_own[0].astype(jnp.float32) * width
    stats = jnp.stack(
        [jnp.sum(first_sums[0]), jnp.sum(first_sums[1]), jnp.sum(second_sums[3]), valid_count]
    )
    shared = jnp.concatenate(
        [second_sums[:3].reshape(-1), third_sums[:3].reshape(-1), jnp.pad(stats, (0, 124))]
    )
    own_sums = total_over(
        jnp.concatenate(
            [
                shared,
                up_bias_grad[0],
                in_bias_grad[:wide],
                in_bias_grad[3 * wide : 4 * wide],
                in_bias_grad[2 * wide : 3 * wide],
                in_bias_grad[5 * wide :],
            ]
        )
    )
    other_sums = swap(own_sums, "c")
    count = shared.shape[0]
    shared = own_sums[:count] + other_sums[:count]
    down_bias_grad, feed_gain_grad, feed_shift_grad, out_bias_grad, attn_gain_grad, attn_shift_grad = [
        shared[i * width : (i + 1) * width] for i in range(6)
    ]
    stats = shared[6 * width : 6 * width + 4]

    def interleave(start, size, block):
        own = own_sums[start : start + size].reshape(-1, block)
        other = other_sums[start : start + size].reshape(-1, block)
        first = jnp.where(core == 0, own, other)
        second = jnp.where(core == 0, other, own)
        return jnp.stack([first, second], axis=1).reshape(-1)

    up_bias_grad = interleave(count, units, unit_block)
    query_bias_grad = interleave(count + units, cols, HD)
    value_bias_gradient = interleave(count + units + cols, cols, HD)
    stream_rms = jnp.sqrt(stats[:3] / stats[3])

    joined = jnp.concatenate([in_sum, up_sum], axis=1)
    joined = joined.reshape((2, rows // 2) + joined.shape[1:])
    own = pick(joined, core, 0)
    other = swap(pick(joined, 1 - core, 0), "c")
    down_weight_grad = down_sum.astype(jnp.float32)
    out_weight_grad = out_sum.astype(jnp.float32)

    def merge(start, size, block):
        one = own[:, start : start + size].reshape(rows // 2, -1, block)
        two = other[:, start : start + size].reshape(rows // 2, -1, block)
        first = jnp.where(core == 0, one, two)
        second = jnp.where(core == 0, two, one)
        return jnp.stack([first, second], axis=2).reshape(rows // 2, -1).astype(jnp.float32)

    query_weight_grad = merge(0, wide, HD)
    key_weight_grad = merge(wide, wide, HD)
    value_weight_grad = merge(2 * wide, wide, HD)
    up_weight_grad = merge(3 * wide, up_cols, unit_block)
    return (
        mixed,
        tokens_grad,
        query_weight_grad,
        key_weight_grad,
        value_weight_grad,
        out_weight_grad,
        up_weight_grad,
        down_weight_grad,
        query_bias_grad,
        value_bias_gradient,
        out_bias_grad,
        attn_gain_grad,
        attn_shift_grad,
        up_bias_grad,
        down_bias_grad,
        feed_gain_grad,
        feed_shift_grad,
        stream_rms,
    )


def solution(mesh):
    devices = mesh.devices
    dp_count, seq_count = devices.shape
    split = seq_count == 2 and dp_count == 16
    if split:
        inner = jax.sharding.Mesh(devices.reshape(4, 2, 2, seq_count), ("z", "x", "c", "s"))
        dp, seq, body = ("z", "x", "c"), "s", split_body
    else:
        inner, dp, seq, body = mesh, "dp", "seq", general_body
    weights = (P(dp, seq),) * 6
    vectors = (P(),) * 9
    rows = P(dp, seq, None)
    in_specs = (rows, P(dp), rows) + weights + vectors
    out_specs = (rows, rows) + weights + vectors + (P(),)
    return jax.shard_map(body, mesh=inner, in_specs=in_specs, out_specs=out_specs, check_vma=False)
```

```python
from functools import partial
import math

import jax
import jax.numpy as jnp
from jax import lax
from jax.experimental import pallas as pl
from jax.experimental.pallas import tpu as pltpu
from jax.sharding import PartitionSpec as P

HD = 64


def layer_norm(values_in, gain_vector, shift_vector):
    mean_value = jnp.mean(values_in, axis=-1, keepdims=True)
    centered = values_in - mean_value
    variance = jnp.mean(centered * centered, axis=-1, keepdims=True)
    return centered * lax.rsqrt(variance + 1e-05) * gain_vector + shift_vector


def gather_weights(first, second, third, fourth, fifth, sixth):
    part = (
        lax.all_gather(first, "dp", axis=0, tiled=True),
        lax.all_gather(second, "dp", axis=0, tiled=True),
        lax.all_gather(third, "dp", axis=0, tiled=True),
        lax.all_gather(fourth, "dp", axis=0, tiled=True),
        lax.all_gather(fifth, "dp", axis=0, tiled=True),
        lax.all_gather(sixth, "dp", axis=0, tiled=True),
    )
    return (
        lax.all_gather(part[0], "seq", axis=1, tiled=True),
        lax.all_gather(part[1], "seq", axis=1, tiled=True),
        lax.all_gather(part[2], "seq", axis=1, tiled=True),
        lax.all_gather(part[3], "seq", axis=1, tiled=True),
        lax.all_gather(part[4], "seq", axis=1, tiled=True),
        lax.all_gather(part[5], "seq", axis=1, tiled=True),
    )


def reduce_grads(first, second, third, fourth, fifth, sixth):
    part = (
        lax.psum_scatter(first.astype(jnp.bfloat16), "seq", scatter_dimension=1, tiled=True).astype(
            jnp.float32
        ),
        lax.psum_scatter(
            second.astype(jnp.bfloat16), "seq", scatter_dimension=1, tiled=True
        ).astype(jnp.float32),
        lax.psum_scatter(third.astype(jnp.bfloat16), "seq", scatter_dimension=1, tiled=True).astype(
            jnp.float32
        ),
        lax.psum_scatter(
            fourth.astype(jnp.bfloat16), "seq", scatter_dimension=1, tiled=True
        ).astype(jnp.float32),
        lax.psum_scatter(fifth.astype(jnp.bfloat16), "seq", scatter_dimension=1, tiled=True).astype(
            jnp.float32
        ),
        lax.psum_scatter(sixth.astype(jnp.bfloat16), "seq", scatter_dimension=1, tiled=True).astype(
            jnp.float32
        ),
    )
    return (
        lax.psum_scatter(
            part[0].astype(jnp.bfloat16), "dp", scatter_dimension=0, tiled=True
        ).astype(jnp.float32),
        lax.psum_scatter(
            part[1].astype(jnp.bfloat16), "dp", scatter_dimension=0, tiled=True
        ).astype(jnp.float32),
        lax.psum_scatter(
            part[2].astype(jnp.bfloat16), "dp", scatter_dimension=0, tiled=True
        ).astype(jnp.float32),
        lax.psum_scatter(
            part[3].astype(jnp.bfloat16), "dp", scatter_dimension=0, tiled=True
        ).astype(jnp.float32),
        lax.psum_scatter(
            part[4].astype(jnp.bfloat16), "dp", scatter_dimension=0, tiled=True
        ).astype(jnp.float32),
        lax.psum_scatter(
            part[5].astype(jnp.bfloat16), "dp", scatter_dimension=0, tiled=True
        ).astype(jnp.float32),
    )


def block_layout(seq_count, row_count, head_count):
    block_seqs = math.gcd(seq_count, max(1, 512 // row_count))
    group_heads = math.gcd(head_count, 4)
    return (block_seqs, seq_count // block_seqs, group_heads, head_count // group_heads)


def head_slice(block_part, offset, group_width, group_heads):
    sliced = lax.dynamic_slice_in_dim(block_part, offset, group_width, 2)
    return sliced.reshape(sliced.shape[0], sliced.shape[1], group_heads, HD)


def attention_forward(queries, key_all, value_all, key_mask):
    seq_count, row_count, feature_total = queries.shape
    slot_count = key_all.shape[1]
    block_seqs, block_count, group_heads, group_count = block_layout(
        seq_count, row_count, feature_total // HD
    )
    group_width = group_heads * HD

    def seq_block(inputs):
        query_part, key_part, value_part, mask_part = inputs

        def head_block(group_index):
            offset = group_index * group_width
            query_heads = head_slice(query_part, offset, group_width, group_heads)
            key_heads = head_slice(key_part, offset, group_width, group_heads)
            value_heads = head_slice(value_part, offset, group_width, group_heads)
            scores = (
                jnp.einsum(
                    "brhd,bkhd->bhrk", query_heads, key_heads, preferred_element_type=jnp.float32
                )
                * 0.125
            )
            scores = jnp.where(mask_part[:, None, None, :], scores, -1e30)
            row_max = jnp.max(scores, axis=-1, keepdims=True)
            exponent = jnp.exp(scores - row_max)
            row_total = jnp.sum(exponent, axis=-1, keepdims=True)
            soft_probs = (exponent / row_total).astype(jnp.bfloat16)
            heads_out = jnp.einsum(
                "bhrk,bkhd->brhd", soft_probs, value_heads, preferred_element_type=jnp.float32
            )
            log_total = (row_max + jnp.log(row_total))[..., 0]
            return (heads_out.reshape(block_seqs, row_count, group_width), log_total)

        return lax.map(head_block, jnp.arange(group_count))

    outputs, log_totals = lax.map(
        seq_block,
        (
            queries.reshape(block_count, block_seqs, row_count, feature_total),
            key_all.reshape(block_count, block_seqs, slot_count, feature_total),
            value_all.reshape(block_count, block_seqs, slot_count, feature_total),
            key_mask.reshape(block_count, block_seqs, slot_count),
        ),
    )
    mixed_heads = outputs.transpose(0, 2, 3, 1, 4).reshape(seq_count, row_count, feature_total)
    return (mixed_heads, log_totals)


def attention_backward(queries, key_all, value_all, key_mask, heads_grad, log_totals):
    seq_count, row_count, feature_total = queries.shape
    slot_count = key_all.shape[1]
    block_seqs, block_count, group_heads, group_count = block_layout(
        seq_count, row_count, feature_total // HD
    )
    group_width = group_heads * HD

    def seq_block(inputs):
        query_part, key_part, value_part, mask_part, grad_part, total_part = inputs

        def head_block(group_index):
            offset = group_index * group_width
            query_heads = head_slice(query_part, offset, group_width, group_heads)
            key_heads = head_slice(key_part, offset, group_width, group_heads)
            value_heads = head_slice(value_part, offset, group_width, group_heads)
            grad_heads = head_slice(grad_part, offset, group_width, group_heads)
            log_total = lax.dynamic_index_in_dim(total_part, group_index, 0, keepdims=False)
            scores = (
                jnp.einsum(
                    "brhd,bkhd->bhrk", query_heads, key_heads, preferred_element_type=jnp.float32
                )
                * 0.125
            )
            scores = jnp.where(mask_part[:, None, None, :], scores, -1e30)
            soft_probs = jnp.exp(scores - log_total[..., None])
            value_grad = jnp.einsum(
                "bhrk,brhd->bkhd",
                soft_probs.astype(jnp.bfloat16),
                grad_heads,
                preferred_element_type=jnp.float32,
            )
            prob_grad = jnp.einsum(
                "brhd,bkhd->bhrk", grad_heads, value_heads, preferred_element_type=jnp.float32
            )
            inner = jnp.sum(soft_probs * prob_grad, axis=-1, keepdims=True)
            score_grad = (soft_probs * (prob_grad - inner)).astype(jnp.bfloat16)
            query_grad = (
                jnp.einsum(
                    "bhrk,bkhd->brhd", score_grad, key_heads, preferred_element_type=jnp.float32
                )
                * 0.125
            )
            key_grad = (
                jnp.einsum(
                    "bhrk,brhd->bkhd", score_grad, query_heads, preferred_element_type=jnp.float32
                )
                * 0.125
            )
            return (
                query_grad.reshape(block_seqs, row_count, group_width),
                key_grad.reshape(block_seqs, slot_count, group_width),
                value_grad.reshape(block_seqs, slot_count, group_width),
            )

        return lax.map(head_block, jnp.arange(group_count))

    query_blocks, key_blocks, value_block_list = lax.map(
        seq_block,
        (
            queries.reshape(block_count, block_seqs, row_count, feature_total),
            key_all.reshape(block_count, block_seqs, slot_count, feature_total),
            value_all.reshape(block_count, block_seqs, slot_count, feature_total),
            key_mask.reshape(block_count, block_seqs, slot_count),
            heads_grad.reshape(block_count, block_seqs, row_count, feature_total),
            log_totals,
        ),
    )
    query_grad = query_blocks.transpose(0, 2, 3, 1, 4).reshape(seq_count, row_count, feature_total)
    key_grad = key_blocks.transpose(0, 2, 3, 1, 4).reshape(seq_count, slot_count, feature_total)
    value_grad = value_block_list.transpose(0, 2, 3, 1, 4).reshape(
        seq_count, slot_count, feature_total
    )
    return (query_grad, key_grad, value_grad)


def general_body(
    tokens,
    lengths,
    cotangent,
    query_weight,
    key_weight,
    value_weight,
    out_weight,
    up_weight,
    down_weight,
    query_bias,
    value_bias,
    out_bias,
    attn_gain,
    attn_shift,
    up_bias,
    down_bias,
    feed_gain,
    feed_shift,
):
    seq_count, row_count, feature_total = tokens.shape
    slot_count = row_count * lax.axis_size("seq")
    token_count = seq_count * row_count
    whole = gather_weights(
        query_weight, key_weight, value_weight, out_weight, up_weight, down_weight
    )
    full_query, full_key, full_value, full_out, full_up, full_down = whole
    flat_tokens = tokens.reshape(token_count, feature_total)
    queries = (
        jnp.dot(flat_tokens, full_query, preferred_element_type=jnp.float32) + query_bias
    ).astype(jnp.bfloat16)
    key_rows = jnp.dot(flat_tokens, full_key, preferred_element_type=jnp.float32).astype(
        jnp.bfloat16
    )
    value_rows = (
        jnp.dot(flat_tokens, full_value, preferred_element_type=jnp.float32) + value_bias
    ).astype(jnp.bfloat16)
    first_slot = lax.axis_index("seq") * row_count
    key_mask = jnp.arange(slot_count)[None, :] < lengths[:, None]
    row_valid = ((first_slot + jnp.arange(row_count))[None, :] < lengths[:, None]).astype(
        jnp.float32
    )
    row_valid = row_valid.reshape(token_count, 1)
    query_blocks = queries.reshape(seq_count, row_count, feature_total)
    key_blocks = key_rows.reshape(seq_count, row_count, feature_total)
    value_block_list = value_rows.reshape(seq_count, row_count, feature_total)
    key_all, value_all = (
        lax.all_gather(key_blocks, "seq", axis=1, tiled=True),
        lax.all_gather(value_block_list, "seq", axis=1, tiled=True),
    )
    mixed_heads, log_totals = attention_forward(query_blocks, key_all, value_all, key_mask)
    heads_low = mixed_heads.reshape(token_count, feature_total).astype(jnp.bfloat16)
    attention_out = jnp.dot(heads_low, full_out, preferred_element_type=jnp.float32) + out_bias
    tokens_f32 = flat_tokens.astype(jnp.float32)
    first_sum = tokens_f32 + attention_out
    hidden, first_pull = jax.vjp(layer_norm, first_sum, attn_gain, attn_shift)
    hidden_low = hidden.astype(jnp.bfloat16)
    pre_act = jnp.dot(hidden_low, full_up, preferred_element_type=jnp.float32) + up_bias
    gelu_out, gelu_pull = jax.vjp(partial(jax.nn.gelu, approximate=False), pre_act)
    activation = gelu_out.astype(jnp.bfloat16)
    feed_out = jnp.dot(activation, full_down, preferred_element_type=jnp.float32) + down_bias
    result, second_pull = jax.vjp(layer_norm, hidden + feed_out, feed_gain, feed_shift)
    mixed = result.astype(jnp.bfloat16).reshape(seq_count, row_count, feature_total)
    partial_stats = jnp.stack(
        [
            jnp.sum(row_valid * tokens_f32 * tokens_f32),
            jnp.sum(row_valid * attention_out * attention_out),
            jnp.sum(row_valid * feed_out * feed_out),
            jnp.sum(row_valid) * feature_total,
        ]
    )
    back_weights = gather_weights(
        query_weight, key_weight, value_weight, out_weight, up_weight, down_weight
    )
    back_query, back_key, back_value, back_out, back_up, back_down = back_weights
    out_grad = cotangent.reshape(token_count, feature_total).astype(jnp.float32) * row_valid
    second_grad, feed_gain_grad, feed_shift_grad = second_pull(out_grad)
    feed_low = second_grad.astype(jnp.bfloat16)
    down_weight_grad = jnp.einsum(
        "nf,nd->fd", activation, feed_low, preferred_element_type=jnp.float32
    )
    down_bias_grad = jnp.sum(feed_low, axis=0, dtype=jnp.float32)
    act_grad = jnp.einsum(
        "nd,fd->nf", feed_low, back_down, preferred_element_type=jnp.float32
    ).astype(jnp.bfloat16)
    pre_grad = gelu_pull(act_grad.astype(jnp.float32))[0].astype(jnp.bfloat16)
    up_weight_grad = jnp.einsum(
        "nd,nf->df", hidden_low, pre_grad, preferred_element_type=jnp.float32
    )
    up_bias_grad = jnp.sum(pre_grad, axis=0, dtype=jnp.float32)
    hidden_grad = (
        jnp.einsum("nf,df->nd", pre_grad, back_up, preferred_element_type=jnp.float32) + second_grad
    )
    first_grad, attn_gain_grad, attn_shift_grad = first_pull(hidden_grad)
    attn_low = first_grad.astype(jnp.bfloat16)
    out_weight_grad = jnp.einsum(
        "nd,ne->de", heads_low, attn_low, preferred_element_type=jnp.float32
    )
    out_bias_grad = jnp.sum(attn_low, axis=0, dtype=jnp.float32)
    heads_grad = jnp.einsum(
        "ne,de->nd", attn_low, back_out, preferred_element_type=jnp.float32
    ).astype(jnp.bfloat16)
    heads_grad = heads_grad.reshape(seq_count, row_count, feature_total)
    query_grad, key_part_grad, value_part_grad = attention_backward(
        query_blocks, key_all, value_all, key_mask, heads_grad, log_totals
    )
    key_sum, value_sum = (
        lax.psum_scatter(
            key_part_grad.astype(jnp.bfloat16), "seq", scatter_dimension=1, tiled=True
        ).astype(jnp.float32),
        lax.psum_scatter(
            value_part_grad.astype(jnp.bfloat16), "seq", scatter_dimension=1, tiled=True
        ).astype(jnp.float32),
    )
    query_low = query_grad.reshape(token_count, feature_total).astype(jnp.bfloat16)
    key_low = key_sum.reshape(token_count, feature_total).astype(jnp.bfloat16)
    value_low = value_sum.reshape(token_count, feature_total).astype(jnp.bfloat16)
    query_weight_grad = jnp.einsum(
        "nd,ne->de", flat_tokens, query_low, preferred_element_type=jnp.float32
    )
    key_weight_grad = jnp.einsum(
        "nd,ne->de", flat_tokens, key_low, preferred_element_type=jnp.float32
    )
    value_weight_grad = jnp.einsum(
        "nd,ne->de", flat_tokens, value_low, preferred_element_type=jnp.float32
    )
    query_bias_grad = jnp.sum(query_low, axis=0, dtype=jnp.float32)
    value_bias_gradient = jnp.sum(value_low, axis=0, dtype=jnp.float32)
    tokens_grad = (
        jnp.einsum("ne,de->nd", query_low, back_query, preferred_element_type=jnp.float32)
        + jnp.einsum("ne,de->nd", key_low, back_key, preferred_element_type=jnp.float32)
        + jnp.einsum("ne,de->nd", value_low, back_value, preferred_element_type=jnp.float32)
        + first_grad
    )
    tokens_grad = tokens_grad.astype(jnp.bfloat16).reshape(seq_count, row_count, feature_total)
    matrix_grads = reduce_grads(
        query_weight_grad,
        key_weight_grad,
        value_weight_grad,
        out_weight_grad,
        up_weight_grad,
        down_weight_grad,
    )
    totals = lax.psum(
        (
            partial_stats,
            query_bias_grad,
            value_bias_gradient,
            out_bias_grad,
            attn_gain_grad,
            attn_shift_grad,
            up_bias_grad,
            down_bias_grad,
            feed_gain_grad,
            feed_shift_grad,
        ),
        ("dp", "seq"),
    )
    stream_rms = jnp.sqrt(totals[0][:3] / totals[0][3])
    return (
        mixed,
        tokens_grad,
        matrix_grads[0],
        matrix_grads[1],
        matrix_grads[2],
        matrix_grads[3],
        matrix_grads[4],
        matrix_grads[5],
        totals[1],
        totals[2],
        totals[3],
        totals[4],
        totals[5],
        totals[6],
        totals[7],
        totals[8],
        totals[9],
        stream_rms,
    )


def swap(value, axis):
    return lax.ppermute(value, axis, [(0, 1), (1, 0)])


def both(value, axis):
    return jnp.concatenate([value, swap(value, axis)], axis=0)


def in_order(own, other, index, axis=0):
    return jnp.where(
        index == 0, jnp.stack([own, other], axis=axis), jnp.stack([other, own], axis=axis)
    )


def split_columns(weight, width, core):
    rows = weight.shape[0]
    blocks = weight.reshape(rows, -1, 2, width)
    return pick(blocks, core, 2).reshape(rows, -1), pick(blocks, 1 - core, 2).reshape(rows, -1)


def pick(values, index, axis):
    return lax.dynamic_index_in_dim(values, index, axis, keepdims=False)


def add(left, right):
    return (left.astype(jnp.float32) + right.astype(jnp.float32)).astype(jnp.bfloat16)


def fold(values, axis, dim):
    index = lax.axis_index(axis)
    return add(pick(values, index, dim), swap(pick(values, 1 - index, dim), axis))


NEXT = [(0, 1), (1, 0), (2, 3), (3, 2)]
CROSS = [(0, 2), (2, 0), (1, 3), (3, 1)]


def fold_line(values):
    place = lax.axis_index("z")
    odd, upper = place % 2, place // 2
    pairs = values.reshape((2, 2) + values.shape[1:])
    pairs = add(pick(pairs, odd, 1), lax.ppermute(pick(pairs, 1 - odd, 1), "z", NEXT))
    return add(pick(pairs, upper, 0), lax.ppermute(pick(pairs, 1 - upper, 0), "z", CROSS))


def after(value, *others):
    return lax.optimization_barrier((value,) + others)[0]


def line_cross(value):
    place = lax.axis_index("z")
    return in_order(value, lax.ppermute(value, "z", CROSS), place // 2)


def line_next(pair):
    place = lax.axis_index("z")
    whole = in_order(pair, lax.ppermute(pair, "z", NEXT), place % 2, 1)
    return whole.reshape((4,) + pair.shape[1:])


def gather_across(beside, below):
    return swap(below[:2], "x"), swap(beside[2:], "s")


def scatter_across(across):
    return swap(across[:2], "x"), swap(across[2:], "s")


def scatter_beside(beside, below, parts):
    beside = jnp.concatenate([beside[:2], add(beside[2:], parts[1])], axis=0)
    below = jnp.concatenate([add(below[:2], parts[0]), below[2:]], axis=0)
    return swap(beside, "x"), swap(below, "s")


def scatter_own(own, parts):
    total = own.astype(jnp.float32) + parts[0].astype(jnp.float32) + parts[1].astype(jnp.float32)
    return fold_line(total.astype(jnp.bfloat16))


def scatter_top(send, keep):
    total = add(keep, swap(send, "s"))
    total = total.reshape((4, 2) + total.shape[1:])
    return fold_line(fold(total, "x", 1))


def grad_block(left_t, right, rows):
    return product(left_t, right, 1, 0).astype(jnp.bfloat16).reshape(4, rows, -1)


def columns_of(right, index):
    columns = right.shape[1] // 2
    return lax.dynamic_slice_in_dim(right, index * columns, columns, 1)


PAIR = 2 * HD
LIMIT = 56 * 1024 * 1024


def kernel_params(steps):
    return pltpu.CompilerParams(
        dimension_semantics=("arbitrary",) * steps, vmem_limit_bytes=LIMIT
    )


def product(left, right, left_dim, right_dim):
    return lax.dot_general(
        left, right, (((left_dim,), (right_dim,)), ((), ())), preferred_element_type=jnp.float32
    )


def key_bias(facts_ref, slots):
    place = lax.broadcasted_iota(jnp.int32, (slots, 1), 0) + facts_ref[2]
    place = jnp.where(place >= slots, place - slots, place)
    return jnp.where(place < facts_ref[pl.program_id(0)], 0.0, -1e30)


def head_lanes(value, head):
    lane = lax.broadcasted_iota(jnp.int32, value.shape, 1)
    return jnp.where((lane >= HD) == (head == 1), value, jnp.zeros_like(value))


def turned(value):
    return value.astype(jnp.float32).T


def attend_kernel(facts_ref, query_ref, key_ref, value_ref, out_ref, total_ref):
    slots = key_ref.shape[0]
    bias = key_bias(facts_ref, slots)
    query = query_ref[...] * jnp.bfloat16(0.125)
    key = key_ref[...]
    value_t = turned(value_ref[...]).astype(jnp.bfloat16)
    outs = []
    for head in range(2):
        scores = product(key, head_lanes(query, head), 1, 1) + bias
        peak = jnp.max(scores, axis=0, keepdims=True)
        weight = jnp.exp(scores - peak)
        total = jnp.sum(weight, axis=0, keepdims=True)
        part = product(value_t[head * HD : (head + 1) * HD], weight.astype(jnp.bfloat16), 1, 0)
        outs.append(part * (1.0 / total))
        total_ref[0, 0, head : head + 1, :] = peak + jnp.log(total)
    out_ref[...] = jnp.concatenate(outs, axis=0).T.astype(jnp.bfloat16)


def attend_back_kernel(
    facts_ref, query_ref, key_ref, value_ref, grad_ref, total_ref, low_ref, sums_ref
):
    slots = key_ref.shape[0]
    bias = key_bias(facts_ref, slots)
    query = query_ref[...] * jnp.bfloat16(0.125)
    key = key_ref[...]
    value = value_ref[...]
    grad = grad_ref[...]
    key_t = turned(key).astype(jnp.bfloat16)
    lane = lax.broadcasted_iota(jnp.int32, (slots, PAIR), 1)
    query_parts, key_parts, value_parts = [], [], []
    for head in range(2):
        scores = product(key, head_lanes(query, head), 1, 1) + bias
        soft = jnp.exp(scores - total_ref[0, 0, head : head + 1, :])
        value_parts.append(product(soft.astype(jnp.bfloat16), grad, 1, 0))
        change = product(value, head_lanes(grad, head), 1, 1)
        inner = jnp.sum(soft * change, axis=0, keepdims=True)
        change = (soft * (change - inner)).astype(jnp.bfloat16)
        key_parts.append(product(change, query, 1, 0))
        query_parts.append(product(key_t[head * HD : (head + 1) * HD], change, 1, 0))
    pair = pl.program_id(1)
    groups = low_ref.shape[1] // 3
    query_low = (jnp.concatenate(query_parts, axis=0) * 0.125).T
    key_low = jnp.where(lane < HD, key_parts[0], key_parts[1])
    value_low = jnp.where(lane < HD, value_parts[0], value_parts[1])
    for place, part in enumerate((query_low, key_low, value_low)):
        start = pl.multiple_of(place * groups + pair * PAIR, PAIR)
        low = part.astype(jnp.bfloat16)
        low_ref[:, pl.ds(start, PAIR)] = low
        sums_ref[0, :, pl.ds(start, PAIR)] = jnp.sum(
            low.astype(jnp.float32), axis=0, keepdims=True
        )


def attention_specs(slots, pairs):
    def at(part):
        return pl.BlockSpec(
            (slots, PAIR), lambda b, g, p, *_: (b, g * 3 * pairs + part * pairs + p)
        )

    heads = pl.BlockSpec((slots, PAIR), lambda b, g, p, *_: (b, g * pairs + p))
    totals = pl.BlockSpec((1, 1, 2, slots), lambda b, g, p, *_: (b, g * pairs + p, 0, 0))
    return [at(0), at(1), at(2)], heads, totals


def attend(facts, projected, slots):
    pairs = projected.shape[1] // (6 * PAIR)
    inputs, heads, totals = attention_specs(slots, pairs)
    rows = projected.shape[0]
    return pl.pallas_call(
        attend_kernel,
        grid_spec=pltpu.PrefetchScalarGridSpec(
            num_scalar_prefetch=1,
            grid=(2, 2, pairs),
            in_specs=inputs,
            out_specs=[heads, totals],
        ),
        out_shape=[
            jax.ShapeDtypeStruct((rows, 2 * pairs * PAIR), jnp.bfloat16),
            jax.ShapeDtypeStruct((2, 2 * pairs, 2, slots), jnp.float32),
        ],
        compiler_params=kernel_params(3),
        name="attend",
    )(facts, projected, projected, projected)


def attend_back(facts, projected, heads_grad, totals_in, slots, own):
    pairs = projected.shape[1] // (6 * PAIR)

    def group(facts_ref):
        return facts_ref[3] if own else 1 - facts_ref[3]

    def at(part):
        return pl.BlockSpec(
            (slots, PAIR), lambda b, p, f: (b, group(f) * 3 * pairs + part * pairs + p)
        )

    heads = pl.BlockSpec((slots, PAIR), lambda b, p, f: (b, group(f) * pairs + p))
    totals = pl.BlockSpec((1, 1, 2, slots), lambda b, p, f: (b, group(f) * pairs + p, 0, 0))
    width = 3 * pairs * PAIR
    return pl.pallas_call(
        attend_back_kernel,
        grid_spec=pltpu.PrefetchScalarGridSpec(
            num_scalar_prefetch=1,
            grid=(2, pairs),
            in_specs=[at(0), at(1), at(2), heads, totals],
            out_specs=[
                pl.BlockSpec((slots, width), lambda b, p, f: (b, 0)),
                pl.BlockSpec((1, 1, width), lambda b, p, f: (b, 0, 0)),
            ],
        ),
        out_shape=[
            jax.ShapeDtypeStruct((2 * slots, width), jnp.bfloat16),
            jax.ShapeDtypeStruct((2, 1, width), jnp.float32),
        ],
        compiler_params=kernel_params(2),
        name="attend_back",
    )(facts, projected, projected, projected, heads_grad, totals_in)


def call(kernel, name, grid, inputs, outputs, shapes, facts, *args):
    return pl.pallas_call(
        kernel,
        grid_spec=pltpu.PrefetchScalarGridSpec(
            num_scalar_prefetch=1, grid=grid, in_specs=inputs, out_specs=outputs
        ),
        out_shape=shapes,
        compiler_params=kernel_params(len(grid)),
        name=name,
    )(facts, *args)


def block(shape, *index):
    def at(*grid_and_facts):
        return tuple(entry(*grid_and_facts) if callable(entry) else entry for entry in index)

    return pl.BlockSpec(shape, at)


def whole(array):
    zeros = (0,) * array.ndim
    return pl.BlockSpec(array.shape, lambda *_: zeros)


def first(i, *_):
    return i


def like(shape, dtype):
    return jax.ShapeDtypeStruct(shape, dtype)


def square_pieces(facts_ref, refs):
    own, beside, below, first_part, second_part = [ref[0] for ref in refs]
    across = jnp.where(pl.program_id(0) < 2, first_part, second_part)
    half, column = facts_ref[3], facts_ref[4]
    near = (own, beside)
    far = (below, across)
    rows = []
    for x in range(2):
        mine = jnp.where(column == x, near[0], near[1])
        other = jnp.where(column == x, far[0], far[1])
        rows.append((jnp.where(half == 0, mine, other), jnp.where(half == 0, other, mine)))
    return rows


def square_specs(parts):
    shape = (1,) + parts[0].shape[1:]
    plain = block(shape, first, 0, 0)
    early = block(shape, lambda i, *_: jnp.minimum(i, 1), 0, 0)
    late = block(shape, lambda i, *_: jnp.maximum(i - 2, 0), 0, 0)
    return [plain, plain, plain, early, late]


def join_kernel(facts_ref, *refs):
    out_ref = refs[-1]
    rows = square_pieces(facts_ref, refs[:-1])
    for x in range(2):
        out_ref[x] = jnp.concatenate(rows[x], axis=1)


def join(facts, parts):
    _, rows, columns = parts[0].shape
    return call(
        join_kernel,
        "join",
        (4,),
        square_specs(parts),
        block((2, rows, 2 * columns), first, 0, 0),
        like((8, rows, 2 * columns), jnp.bfloat16),
        facts,
        *parts,
    )


def join_near_kernel(facts_ref, *refs):
    in_ref, out_ref = refs[-2:]
    rows = square_pieces(facts_ref, refs[:-2])
    count, width = out_ref.shape[1:]
    wide = width // 4
    for x in range(2):
        in_ref[x] = jnp.concatenate([part[:, : 3 * wide] for part in rows[x]], axis=1)
        out_ref[x] = jnp.concatenate(
            [part[i * count : (i + 1) * count, 3 * wide :] for part in rows[x] for i in range(2)],
            axis=1,
        )


def join_near(facts, parts):
    _, rows, columns = parts[0].shape
    shapes = [(8, rows, columns * 3 // 2), (8, rows // 2, columns)]
    return call(
        join_near_kernel,
        "join_near",
        (4,),
        square_specs(parts),
        [block((2,) + shape[1:], first, 0, 0) for shape in shapes],
        [like(shape, jnp.bfloat16) for shape in shapes],
        facts,
        *parts,
    )


def turn_kernel(facts_ref, own_ref, other_ref, own_t_ref, other_t_ref):
    own_t_ref[...] = own_ref[...].T
    other_t_ref[...] = other_ref[...].T


def turn(facts, values, rows):
    count, width = values.shape
    half = width // 2
    out = block((rows, count), first, 0)
    shape = like((half, count), values.dtype)
    return call(
        turn_kernel,
        "turn",
        (half // rows,),
        [
            block((count, rows), 0, lambda i, f: 2 * i + f[4]),
            block((count, rows), 0, lambda i, f: 2 * i + 1 - f[4]),
        ],
        [out, out],
        [shape, shape],
        facts,
        values,
        values,
    )


def project_kernel(facts_ref, rows_ref, weight_ref, bias_ref, out_ref):
    out_ref[...] = (product(rows_ref[...], weight_ref[...], 1, 0) + bias_ref[...]).astype(jnp.bfloat16)


def project(facts, rows, weight, bias):
    count, width = rows.shape
    columns = weight.shape[1]
    wide = columns // 6
    return call(
        project_kernel,
        "project",
        (6,),
        [whole(rows), block((width, wide), 0, first), block((1, wide), 0, first)],
        block((count, wide), 0, first),
        like((count, columns), jnp.bfloat16),
        facts,
        rows,
        weight,
        bias[None],
    )


def valid_rows(facts_ref, count, slots):
    place = lax.broadcasted_iota(jnp.int32, (count, 1), 0) + pl.program_id(0) * count + facts_ref[2]
    place = jnp.where(place >= slots, place - slots, place)
    return (place < facts_ref[0]).astype(jnp.float32)


def add_rows(sums_ref, rows):
    total = jnp.concatenate([jnp.sum(part, axis=0, keepdims=True) for part in rows], axis=0)
    total = jnp.concatenate([total, jnp.zeros((8 - len(rows), total.shape[1]), jnp.float32)], axis=0)

    @pl.when(pl.program_id(0) == 0)
    def _():
        sums_ref[...] = total

    @pl.when(pl.program_id(0) > 0)
    def _():
        sums_ref[...] += total


def mean_of(values):
    return jnp.mean(values, axis=-1, keepdims=True)


def attend_out_kernel(
    slots, facts_ref, own_ref, other_ref, own_weight_ref, other_weight_ref, tokens_ref, vectors_ref,
    hat_ref, rstd_ref, low_ref, sums_ref,
):
    branch = (
        product(own_ref[...], own_weight_ref[...], 1, 0)
        + product(other_ref[...], other_weight_ref[...], 1, 0)
        + vectors_ref[0:1]
    )
    tokens = tokens_ref[...].astype(jnp.float32)
    total = tokens + branch
    centered = total - mean_of(total)
    rstd = lax.rsqrt(mean_of(centered * centered) + 1e-05)
    hat = centered * rstd
    hat_ref[...] = hat
    rstd_ref[...] = rstd
    low_ref[...] = (hat * vectors_ref[1:2] + vectors_ref[2:3]).astype(jnp.bfloat16)
    valid = valid_rows(facts_ref, tokens.shape[0], slots)
    add_rows(sums_ref, [valid * tokens * tokens, valid * branch * branch])


def attend_out(facts, own, other, own_weight, other_weight, tokens, vectors):
    slots, width = tokens.shape
    step = slots // 4
    rows = lambda array: block((step, array.shape[1]), first, 0)
    return call(
        partial(attend_out_kernel, slots),
        "attend_out",
        (4,),
        [rows(own), rows(other), whole(own_weight), whole(other_weight), rows(tokens), whole(vectors)],
        [block((step, width), first, 0), block((step, 1), first, 0), block((step, width), first, 0), block((8, width), 0, 0)],
        [
            like((slots, width), jnp.float32),
            like((slots, 1), jnp.float32),
            like((slots, width), jnp.bfloat16),
            like((8, width), jnp.float32),
        ],
        facts,
        own,
        other,
        own_weight,
        other_weight,
        tokens,
        vectors,
    )


def up_kernel(
    facts_ref, rows_ref, weight_ref, bias_ref, act_ref, slope_ref, own_t_ref, other_t_ref
):
    pre_act = product(rows_ref[...], weight_ref[...], 1, 0) + bias_ref[...]
    below = 0.5 + 0.5 * lax.erf(pre_act * 0.7071067811865476)
    act = (pre_act * below).astype(jnp.bfloat16)
    act_ref[...] = act
    slope = below + pre_act * (0.3989422804014327 * jnp.exp(-0.5 * pre_act * pre_act))
    slope_ref[...] = slope.astype(jnp.bfloat16)
    act_t = act.T

    @pl.when(pl.program_id(0) < 4)
    def _():
        own_t_ref[...] = act_t

    @pl.when(pl.program_id(0) >= 4)
    def _():
        other_t_ref[...] = act_t


def feed_up(facts, rows, weight, bias):
    count, width = rows.shape
    units = weight.shape[1]
    wide = units // 8

    def chip(i, f):
        return jnp.where(i < 4, 2 * i + f[4], 2 * i - 7 - f[4])

    shape = like((count, units), jnp.bfloat16)
    turned_shape = like((units // 2, count), jnp.bfloat16)
    out = block((count, wide), 0, chip)
    return call(
        up_kernel,
        "feed_up",
        (8,),
        [whole(rows), block((width, wide), 0, chip), block((1, wide), 0, chip)],
        [
            out,
            out,
            block((wide, count), lambda i, *_: jnp.minimum(i, 3), 0),
            block((wide, count), lambda i, *_: jnp.maximum(i - 4, 0), 0),
        ],
        [shape, shape, turned_shape, turned_shape],
        facts,
        rows,
        weight,
        bias[None],
    )


def second_norm_kernel(
    slots, facts_ref, part_ref, other_ref, hat_ref, cotangent_ref, vectors_ref,
    mixed_ref, grad_ref, low_ref, sums_ref,
):
    branch = part_ref[...] + other_ref[...].astype(jnp.float32) + vectors_ref[0:1]
    hidden = hat_ref[...] * vectors_ref[1:2] + vectors_ref[2:3]
    gain = vectors_ref[3:4]
    total = hidden + branch
    centered = total - mean_of(total)
    rstd = lax.rsqrt(mean_of(centered * centered) + 1e-05)
    hat = centered * rstd
    mixed_ref[...] = (hat * gain + vectors_ref[4:5]).astype(jnp.bfloat16)
    valid = valid_rows(facts_ref, branch.shape[0], slots)
    grad = cotangent_ref[...].astype(jnp.float32) * valid
    scaled = grad * gain
    result = rstd * (scaled - mean_of(scaled) - hat * mean_of(scaled * hat))
    low = result.astype(jnp.bfloat16)
    grad_ref[...] = result
    low_ref[...] = low
    add_rows(sums_ref, [low.astype(jnp.float32), grad * hat, grad, valid * branch * branch])


def second_norm(facts, part, other, hat, cotangent, vectors):
    slots, width = part.shape
    step = slots // 4
    rows = block((step, width), first, 0)
    return call(
        partial(second_norm_kernel, slots),
        "second_norm",
        (4,),
        [rows, rows, rows, rows, whole(vectors)],
        [rows, rows, rows, block((8, width), 0, 0)],
        [
            like((slots, width), jnp.bfloat16),
            like((slots, width), jnp.float32),
            like((slots, width), jnp.bfloat16),
            like((8, width), jnp.float32),
        ],
        facts,
        part,
        other,
        hat,
        cotangent,
        vectors,
    )


def first_norm_kernel(
    facts_ref, part_ref, other_ref, second_ref, hat_ref, rstd_ref, vectors_ref,
    grad_ref, low_ref, sums_ref,
):
    grad = part_ref[...] + other_ref[...].astype(jnp.float32) + second_ref[...]
    hat = hat_ref[...]
    scaled = grad * vectors_ref[1:2]
    result = rstd_ref[...] * (scaled - mean_of(scaled) - hat * mean_of(scaled * hat))
    low = result.astype(jnp.bfloat16)
    grad_ref[...] = result
    low_ref[...] = low
    add_rows(sums_ref, [low.astype(jnp.float32), grad * hat, grad])


def first_norm(facts, part, other, second, hat, rstd, vectors):
    slots, width = part.shape
    step = slots // 4
    rows = block((step, width), first, 0)
    return call(
        first_norm_kernel,
        "first_norm",
        (4,),
        [rows, rows, rows, rows, block((step, 1), first, 0), whole(vectors)],
        [rows, rows, block((8, width), 0, 0)],
        [
            like((slots, width), jnp.float32),
            like((slots, width), jnp.bfloat16),
            like((8, width), jnp.float32),
        ],
        facts,
        part,
        other,
        second,
        hat,
        rstd,
        vectors,
    )


def act_grad_kernel(facts_ref, rows_ref, weight_ref, slope_ref, out_ref, sums_ref):
    total = product(rows_ref[...], weight_ref[...], 1, 1)
    grad = total.astype(jnp.bfloat16).astype(jnp.float32) * slope_ref[...].astype(jnp.float32)
    low = grad.astype(jnp.bfloat16)
    out_ref[...] = low
    sums_ref[...] = jnp.sum(low.astype(jnp.float32), axis=0, keepdims=True)


def act_grad(facts, rows, weight, slope):
    count, units = slope.shape
    step = units // 8
    out = block((count, step), 0, first)
    return call(
        act_grad_kernel,
        "act_grad",
        (8,),
        [whole(rows), block((step, rows.shape[1]), first, 0), out],
        [out, block((1, step), 0, first)],
        [like((count, units), jnp.bfloat16), like((1, units), jnp.float32)],
        facts,
        rows,
        weight,
        slope,
    )


def tokens_grad_kernel(facts_ref, own_ref, other_ref, weight_ref, out_ref):
    wide = own_ref.shape[1]
    half = facts_ref[3]
    own = weight_ref[:, pl.ds(pl.multiple_of(half * wide, 128), wide)]
    other = weight_ref[:, pl.ds(pl.multiple_of((1 - half) * wide, 128), wide)]
    total = product(own_ref[...], own, 1, 1) + product(other_ref[...], other, 1, 1)
    out_ref[...] = total.astype(out_ref.dtype)


def tokens_grad_part(facts, own, other, part, weight, dtype):
    count, columns = own.shape
    width = weight.shape[0]
    rows = block((count // 2, columns), part, 0)
    step = width // 4
    return call(
        tokens_grad_kernel,
        "tokens_grad",
        (4,),
        [rows, rows, block((step, 2 * columns), first, 0)],
        block((count // 2, step), 0, first),
        like((count // 2, width), dtype),
        facts,
        own,
        other,
        weight,
    )


def split_body(
    tokens,
    lengths,
    cotangent,
    query_weight,
    key_weight,
    value_weight,
    out_weight,
    up_weight,
    down_weight,
    query_bias,
    value_bias,
    out_bias,
    attn_gain,
    attn_shift,
    up_bias,
    down_bias,
    feed_gain,
    feed_shift,
):
    core = lax.axis_index("c")
    half = lax.axis_index("s")
    row_count, width = tokens.shape[1:]
    slots = 2 * row_count
    unit_block = down_weight.shape[0]
    units = up_bias.shape[0] // 2
    cols = width // 2
    wide = cols // 2

    def to_sequence(values):
        return jnp.concatenate([pick(values, half, 0), swap(pick(values, 1 - half, 0), "s")], axis=0)

    def from_sequence(values):
        return in_order(values[:row_count], swap(values[row_count:], "s"), half)

    small = [
        split_columns(weight, HD, core) for weight in (query_weight, key_weight, value_weight)
    ]
    large = split_columns(up_weight, unit_block, core)
    up_pair = in_order(large[0], swap(large[1], "c"), core)
    up_cols = up_pair.shape[2]
    up_mine = up_pair.reshape(-1, up_cols)
    rows = up_mine.shape[0]
    near_kept = jnp.concatenate([part[0] for part in small], axis=1)
    near_sent = jnp.concatenate([part[1] for part in small], axis=1)
    near_pair = in_order(near_kept, swap(near_sent, "c"), core)
    out_pair = jnp.concatenate([out_weight[:, :wide], out_weight[:, wide:]], axis=0)
    near_mine = jnp.concatenate([near_pair.reshape(rows, -1), out_pair], axis=1)
    near = line_cross(near_mine)
    up_part = line_cross(after(up_mine, near))
    near = line_next(near)
    up_part = line_next(up_part)
    down_part = line_cross(after(down_weight, near))
    near_beside, near_below = swap(near, "x"), swap(near, "s")
    near_across = gather_across(near_beside, near_below)
    tokens_own = to_sequence(tokens)
    tokens_both = both(tokens_own, "c")
    up_part, _, _ = lax.optimization_barrier((up_part, near_across[0], near_across[1]))
    up_beside, up_below = swap(up_part, "x"), swap(up_part, "s")
    down_part = line_next(down_part)
    length_own = lax.dynamic_slice_in_dim(lengths, half, 1, 0)
    facts = jnp.concatenate(
        [
            both(length_own, "c"),
            jnp.stack([half * row_count, half, lax.axis_index("x")]).astype(jnp.int32),
        ]
    )
    in_weight, out_own = join_near(facts, (near, near_beside, near_below) + near_across)
    in_weight = in_weight.reshape(width, 6 * wide)
    out_own = out_own.reshape(cols, width)
    out_other = swap(out_own, "c")

    def halves_of(vector, size):
        return pick(vector.reshape(-1, 2, size), core, 1).reshape(-1)

    query_part = halves_of(query_bias, HD).reshape(2, wide)
    value_part = halves_of(value_bias, HD).reshape(2, wide)
    in_bias = jnp.stack([query_part, jnp.zeros_like(query_part), value_part], axis=1).reshape(-1)
    projected = project(facts, tokens_both, in_weight, in_bias)
    heads_out, totals = attend(facts, projected, slots)
    heads_out, up_beside, up_below = lax.optimization_barrier((heads_out, up_beside, up_below))
    heads_other = swap(heads_out[slots:], "c")
    up_across = gather_across(up_beside, up_below)
    down_part = after(down_part, up_beside, up_below)
    down_beside, down_below = swap(down_part, "x"), swap(down_part, "s")
    vectors = jnp.stack(
        [out_bias, attn_gain, attn_shift, down_bias, feed_gain, feed_shift, out_bias, out_bias]
    )
    first_hat, first_rstd, hidden_low, first_sums = attend_out(
        facts, heads_out, heads_other, out_own, out_other, tokens_own, vectors
    )
    hidden_both = both(hidden_low, "c")
    hidden_turned = turn(facts, hidden_both, rows)
    tokens_turned = turn(facts, after(tokens_both, hidden_turned[0]), rows)
    up_all = join(facts, (up_part, up_beside, up_below) + up_across).reshape(width, units)
    hidden_both, up_all, _ = lax.optimization_barrier((hidden_both, up_all, tokens_turned[0]))
    activation, slope, act_own, act_other = feed_up(
        facts, hidden_both, up_all, halves_of(up_bias, unit_block)
    )
    activation, down_beside, down_below = lax.optimization_barrier(
        (activation, down_beside, down_below)
    )
    down_across = gather_across(down_beside, down_below)
    down_all = join(facts, (down_part, down_beside, down_below) + down_across)
    down_all = down_all.reshape(units, width)
    feed_other = swap(
        product(activation[slots:], down_all, 1, 0).astype(jnp.bfloat16), "c"
    )
    cotangent_own = to_sequence(after(cotangent, heads_out))
    feed_part = product(after(activation, feed_other)[:slots], down_all, 1, 0)
    feed_vectors = jnp.stack(
        [down_bias, attn_gain, attn_shift, feed_gain, feed_shift, out_bias, out_bias, out_bias]
    )
    mixed, second_grad, feed_low, second_sums = second_norm(
        facts, feed_part, feed_other, first_hat, cotangent_own, feed_vectors
    )
    mixed = from_sequence(mixed)

    feed_both = both(feed_low, "c")
    feed_mine, feed_theirs = columns_of(feed_both, half), columns_of(feed_both, 1 - half)
    down_first = scatter_across(grad_block(act_other, feed_theirs, unit_block))
    down_mine = [
        grad_block(act_other, feed_mine, unit_block),
        grad_block(act_own, feed_theirs, unit_block),
    ]
    pre_grad, up_bias_grad = act_grad(
        facts, after(feed_both, down_mine[0], down_mine[1]), down_all, slope
    )
    hidden_sent = product(pre_grad[slots:], up_all, 1, 1).astype(jnp.bfloat16)
    hidden_other = swap(hidden_sent, "c")
    pre_mine, pre_theirs = columns_of(pre_grad, half), columns_of(pre_grad, 1 - half)
    hidden_own_t, hidden_other_t = hidden_turned
    up_across_grad = grad_block(hidden_other_t, after(pre_theirs, hidden_sent), rows)
    down_first = lax.optimization_barrier(down_first + (up_across_grad,))[:2]
    down_second = scatter_beside(down_mine[0], down_mine[1], down_first)
    up_first = scatter_across(up_across_grad)
    hidden_part = product(after(pre_grad, up_across_grad, hidden_sent)[:slots], up_all, 1, 1)
    up_mine_grad = [
        grad_block(hidden_other_t, after(pre_mine, hidden_part), rows),
        grad_block(hidden_own_t, after(pre_theirs, hidden_part), rows),
    ]
    first_grad, attn_low, third_sums = first_norm(
        facts, hidden_part, hidden_other, second_grad, first_hat, first_rstd, vectors
    )
    grad_sent = product(attn_low, out_other, 1, 1).astype(jnp.bfloat16)
    grad_other = swap(grad_sent, "c")
    grad_own = product(after(attn_low, grad_sent), out_own, 1, 1).astype(jnp.bfloat16)
    out_sent = product(heads_other, attn_low, 0, 0).astype(jnp.bfloat16)
    out_grad = add(product(heads_out[:slots], attn_low, 0, 0), swap(out_sent, "c"))
    out_parts = out_grad.reshape(4, 2, out_weight.shape[0], 2, cols).transpose(3, 0, 1, 2, 4)
    out_parts = out_parts.reshape(2, 8, out_weight.shape[0], cols)
    out_total = add(pick(out_parts, half, 0), swap(pick(out_parts, 1 - half, 0), "s"))
    down_own = grad_block(act_own, after(feed_mine, out_sent), unit_block)
    heads_grad = jnp.concatenate([grad_own, grad_other], axis=0)
    heads_grad, up_first = lax.optimization_barrier(
        (heads_grad, up_first + (up_mine_grad[0], up_mine_grad[1], down_own))
    )
    up_second = scatter_beside(up_first[2], up_first[3], up_first[:2])
    down_own = up_first[4]
    theirs_low, theirs_sums = attend_back(facts, projected, heads_grad, totals, slots, False)
    tokens_own_t, tokens_other_t = tokens_turned
    in_across = grad_block(tokens_other_t, theirs_low, rows)
    in_first = scatter_across(in_across)
    down_last = lax.optimization_barrier(down_second + (in_across,))[:2]
    down_sum = scatter_own(down_own, down_last)
    in_below = grad_block(tokens_own_t, theirs_low, rows)
    mine_low, mine_sums = attend_back(
        facts, projected, after(heads_grad, in_across, in_below), totals, slots, True
    )
    in_beside = grad_block(tokens_other_t, mine_low, rows)
    in_first = lax.optimization_barrier(in_first + (in_beside,))[:2]
    in_second = scatter_beside(in_beside, in_below, in_first)
    tokens_sent = tokens_grad_part(
        facts, after(mine_low, in_beside), theirs_low, 1, in_weight, jnp.bfloat16
    )
    tokens_other = swap(tokens_sent, "c")
    up_last = lax.optimization_barrier(up_second + (tokens_sent,))[:2]
    up_own = grad_block(hidden_own_t, pre_mine, rows)
    up_sum = scatter_own(up_own, up_last)
    in_own = grad_block(tokens_own_t, mine_low, rows)
    tokens_part = tokens_grad_part(
        facts, after(mine_low, tokens_sent), theirs_low, 0, in_weight, jnp.float32
    )
    tokens_grad = tokens_part + tokens_other.astype(jnp.float32) + first_grad
    tokens_grad = from_sequence(tokens_grad.astype(jnp.bfloat16))
    out_total = out_total.reshape((4, 2) + out_total.shape[1:])
    out_sum = fold_line(fold(out_total, "x", 1))
    in_sum = scatter_own(in_own, in_second)

    mine_sums, theirs_sums = jnp.sum(mine_sums, axis=(0, 1)), jnp.sum(theirs_sums, axis=(0, 1))
    in_bias_grad = in_order(mine_sums, theirs_sums, half).reshape(-1)
    valid_count = length_own[0].astype(jnp.float32) * width
    stats = jnp.stack(
        [jnp.sum(first_sums[0]), jnp.sum(first_sums[1]), jnp.sum(second_sums[3]), valid_count]
    )
    shared = jnp.concatenate(
        [second_sums[:3].reshape(-1), third_sums[:3].reshape(-1), jnp.pad(stats, (0, 124))]
    )
    own_sums = lax.all_gather(
        jnp.concatenate(
            [
                shared,
                up_bias_grad[0],
                in_bias_grad[:wide],
                in_bias_grad[3 * wide : 4 * wide],
                in_bias_grad[2 * wide : 3 * wide],
                in_bias_grad[5 * wide :],
            ]
        ),
        ("z", "x", "s"),
    )
    own_sums = jnp.sum(own_sums, axis=0)
    other_sums = swap(own_sums, "c")
    count = shared.shape[0]
    shared = own_sums[:count] + other_sums[:count]
    down_bias_grad, feed_gain_grad, feed_shift_grad, out_bias_grad, attn_gain_grad, attn_shift_grad = [
        shared[i * width : (i + 1) * width] for i in range(6)
    ]
    stats = shared[6 * width : 6 * width + 4]

    def interleave(start, size, block):
        own = own_sums[start : start + size].reshape(-1, block)
        other = other_sums[start : start + size].reshape(-1, block)
        first = jnp.where(core == 0, own, other)
        second = jnp.where(core == 0, other, own)
        return jnp.stack([first, second], axis=1).reshape(-1)

    up_bias_grad = interleave(count, units, unit_block)
    query_bias_grad = interleave(count + units, cols, HD)
    value_bias_gradient = interleave(count + units + cols, cols, HD)
    stream_rms = jnp.sqrt(stats[:3] / stats[3])

    def give_back(total):
        total = total.reshape((2, rows // 2) + total.shape[1:])
        return pick(total, core, 0), swap(pick(total, 1 - core, 0), "c")

    up_shares = give_back(up_sum)
    in_shares = give_back(in_sum)
    down_weight_grad = down_sum.astype(jnp.float32)
    out_weight_grad = out_sum.astype(jnp.float32)

    def merge(shares, start, size, block):
        one, two = [
            share[:, start : start + size].reshape(rows // 2, -1, block) for share in shares
        ]
        first = jnp.where(core == 0, one, two)
        second = jnp.where(core == 0, two, one)
        return jnp.stack([first, second], axis=2).reshape(rows // 2, -1).astype(jnp.float32)

    query_weight_grad = merge(in_shares, 0, wide, HD)
    key_weight_grad = merge(in_shares, wide, wide, HD)
    value_weight_grad = merge(in_shares, 2 * wide, wide, HD)
    up_weight_grad = merge(up_shares, 0, up_cols, unit_block)
    return (
        mixed,
        tokens_grad,
        query_weight_grad,
        key_weight_grad,
        value_weight_grad,
        out_weight_grad,
        up_weight_grad,
        down_weight_grad,
        query_bias_grad,
        value_bias_gradient,
        out_bias_grad,
        attn_gain_grad,
        attn_shift_grad,
        up_bias_grad,
        down_bias_grad,
        feed_gain_grad,
        feed_shift_grad,
        stream_rms,
    )


def solution(mesh):
    devices = mesh.devices
    dp_count, seq_count = devices.shape
    split = seq_count == 2 and dp_count == 16
    if split:
        inner = jax.sharding.Mesh(devices.reshape(4, 2, 2, seq_count), ("z", "x", "c", "s"))
        dp, seq, body = ("z", "x", "c"), "s", split_body
    else:
        inner, dp, seq, body = mesh, "dp", "seq", general_body
    weights = (P(dp, seq),) * 6
    vectors = (P(),) * 9
    rows = P(dp, seq, None)
    in_specs = (rows, P(dp), rows) + weights + vectors
    out_specs = (rows, rows) + weights + vectors + (P(),)
    return jax.shard_map(body, mesh=inner, in_specs=in_specs, out_specs=out_specs, check_vma=False)
```

```python
from functools import partial
import math

import jax
import jax.numpy as jnp
from jax import lax
from jax.experimental import pallas as pl
from jax.experimental.pallas import tpu as pltpu
from jax.sharding import PartitionSpec as P

HD = 64


def layer_norm(values_in, gain_vector, shift_vector):
    mean_value = jnp.mean(values_in, axis=-1, keepdims=True)
    centered = values_in - mean_value
    variance = jnp.mean(centered * centered, axis=-1, keepdims=True)
    return centered * lax.rsqrt(variance + 1e-05) * gain_vector + shift_vector


def gather_weights(first, second, third, fourth, fifth, sixth):
    part = (
        lax.all_gather(first, "dp", axis=0, tiled=True),
        lax.all_gather(second, "dp", axis=0, tiled=True),
        lax.all_gather(third, "dp", axis=0, tiled=True),
        lax.all_gather(fourth, "dp", axis=0, tiled=True),
        lax.all_gather(fifth, "dp", axis=0, tiled=True),
        lax.all_gather(sixth, "dp", axis=0, tiled=True),
    )
    return (
        lax.all_gather(part[0], "seq", axis=1, tiled=True),
        lax.all_gather(part[1], "seq", axis=1, tiled=True),
        lax.all_gather(part[2], "seq", axis=1, tiled=True),
        lax.all_gather(part[3], "seq", axis=1, tiled=True),
        lax.all_gather(part[4], "seq", axis=1, tiled=True),
        lax.all_gather(part[5], "seq", axis=1, tiled=True),
    )


def reduce_grads(first, second, third, fourth, fifth, sixth):
    part = (
        lax.psum_scatter(first.astype(jnp.bfloat16), "seq", scatter_dimension=1, tiled=True).astype(
            jnp.float32
        ),
        lax.psum_scatter(
            second.astype(jnp.bfloat16), "seq", scatter_dimension=1, tiled=True
        ).astype(jnp.float32),
        lax.psum_scatter(third.astype(jnp.bfloat16), "seq", scatter_dimension=1, tiled=True).astype(
            jnp.float32
        ),
        lax.psum_scatter(
            fourth.astype(jnp.bfloat16), "seq", scatter_dimension=1, tiled=True
        ).astype(jnp.float32),
        lax.psum_scatter(fifth.astype(jnp.bfloat16), "seq", scatter_dimension=1, tiled=True).astype(
            jnp.float32
        ),
        lax.psum_scatter(sixth.astype(jnp.bfloat16), "seq", scatter_dimension=1, tiled=True).astype(
            jnp.float32
        ),
    )
    return (
        lax.psum_scatter(
            part[0].astype(jnp.bfloat16), "dp", scatter_dimension=0, tiled=True
        ).astype(jnp.float32),
        lax.psum_scatter(
            part[1].astype(jnp.bfloat16), "dp", scatter_dimension=0, tiled=True
        ).astype(jnp.float32),
        lax.psum_scatter(
            part[2].astype(jnp.bfloat16), "dp", scatter_dimension=0, tiled=True
        ).astype(jnp.float32),
        lax.psum_scatter(
            part[3].astype(jnp.bfloat16), "dp", scatter_dimension=0, tiled=True
        ).astype(jnp.float32),
        lax.psum_scatter(
            part[4].astype(jnp.bfloat16), "dp", scatter_dimension=0, tiled=True
        ).astype(jnp.float32),
        lax.psum_scatter(
            part[5].astype(jnp.bfloat16), "dp", scatter_dimension=0, tiled=True
        ).astype(jnp.float32),
    )


def block_layout(seq_count, row_count, head_count):
    block_seqs = math.gcd(seq_count, max(1, 512 // row_count))
    group_heads = math.gcd(head_count, 4)
    return (block_seqs, seq_count // block_seqs, group_heads, head_count // group_heads)


def head_slice(block_part, offset, group_width, group_heads):
    sliced = lax.dynamic_slice_in_dim(block_part, offset, group_width, 2)
    return sliced.reshape(sliced.shape[0], sliced.shape[1], group_heads, HD)


def attention_forward(queries, key_all, value_all, key_mask):
    seq_count, row_count, feature_total = queries.shape
    slot_count = key_all.shape[1]
    block_seqs, block_count, group_heads, group_count = block_layout(
        seq_count, row_count, feature_total // HD
    )
    group_width = group_heads * HD

    def seq_block(inputs):
        query_part, key_part, value_part, mask_part = inputs

        def head_block(group_index):
            offset = group_index * group_width
            query_heads = head_slice(query_part, offset, group_width, group_heads)
            key_heads = head_slice(key_part, offset, group_width, group_heads)
            value_heads = head_slice(value_part, offset, group_width, group_heads)
            scores = (
                jnp.einsum(
                    "brhd,bkhd->bhrk", query_heads, key_heads, preferred_element_type=jnp.float32
                )
                * 0.125
            )
            scores = jnp.where(mask_part[:, None, None, :], scores, -1e30)
            row_max = jnp.max(scores, axis=-1, keepdims=True)
            exponent = jnp.exp(scores - row_max)
            row_total = jnp.sum(exponent, axis=-1, keepdims=True)
            soft_probs = (exponent / row_total).astype(jnp.bfloat16)
            heads_out = jnp.einsum(
                "bhrk,bkhd->brhd", soft_probs, value_heads, preferred_element_type=jnp.float32
            )
            log_total = (row_max + jnp.log(row_total))[..., 0]
            return (heads_out.reshape(block_seqs, row_count, group_width), log_total)

        return lax.map(head_block, jnp.arange(group_count))

    outputs, log_totals = lax.map(
        seq_block,
        (
            queries.reshape(block_count, block_seqs, row_count, feature_total),
            key_all.reshape(block_count, block_seqs, slot_count, feature_total),
            value_all.reshape(block_count, block_seqs, slot_count, feature_total),
            key_mask.reshape(block_count, block_seqs, slot_count),
        ),
    )
    mixed_heads = outputs.transpose(0, 2, 3, 1, 4).reshape(seq_count, row_count, feature_total)
    return (mixed_heads, log_totals)


def attention_backward(queries, key_all, value_all, key_mask, heads_grad, log_totals):
    seq_count, row_count, feature_total = queries.shape
    slot_count = key_all.shape[1]
    block_seqs, block_count, group_heads, group_count = block_layout(
        seq_count, row_count, feature_total // HD
    )
    group_width = group_heads * HD

    def seq_block(inputs):
        query_part, key_part, value_part, mask_part, grad_part, total_part = inputs

        def head_block(group_index):
            offset = group_index * group_width
            query_heads = head_slice(query_part, offset, group_width, group_heads)
            key_heads = head_slice(key_part, offset, group_width, group_heads)
            value_heads = head_slice(value_part, offset, group_width, group_heads)
            grad_heads = head_slice(grad_part, offset, group_width, group_heads)
            log_total = lax.dynamic_index_in_dim(total_part, group_index, 0, keepdims=False)
            scores = (
                jnp.einsum(
                    "brhd,bkhd->bhrk", query_heads, key_heads, preferred_element_type=jnp.float32
                )
                * 0.125
            )
            scores = jnp.where(mask_part[:, None, None, :], scores, -1e30)
            soft_probs = jnp.exp(scores - log_total[..., None])
            value_grad = jnp.einsum(
                "bhrk,brhd->bkhd",
                soft_probs.astype(jnp.bfloat16),
                grad_heads,
                preferred_element_type=jnp.float32,
            )
            prob_grad = jnp.einsum(
                "brhd,bkhd->bhrk", grad_heads, value_heads, preferred_element_type=jnp.float32
            )
            inner = jnp.sum(soft_probs * prob_grad, axis=-1, keepdims=True)
            score_grad = (soft_probs * (prob_grad - inner)).astype(jnp.bfloat16)
            query_grad = (
                jnp.einsum(
                    "bhrk,bkhd->brhd", score_grad, key_heads, preferred_element_type=jnp.float32
                )
                * 0.125
            )
            key_grad = (
                jnp.einsum(
                    "bhrk,brhd->bkhd", score_grad, query_heads, preferred_element_type=jnp.float32
                )
                * 0.125
            )
            return (
                query_grad.reshape(block_seqs, row_count, group_width),
                key_grad.reshape(block_seqs, slot_count, group_width),
                value_grad.reshape(block_seqs, slot_count, group_width),
            )

        return lax.map(head_block, jnp.arange(group_count))

    query_blocks, key_blocks, value_block_list = lax.map(
        seq_block,
        (
            queries.reshape(block_count, block_seqs, row_count, feature_total),
            key_all.reshape(block_count, block_seqs, slot_count, feature_total),
            value_all.reshape(block_count, block_seqs, slot_count, feature_total),
            key_mask.reshape(block_count, block_seqs, slot_count),
            heads_grad.reshape(block_count, block_seqs, row_count, feature_total),
            log_totals,
        ),
    )
    query_grad = query_blocks.transpose(0, 2, 3, 1, 4).reshape(seq_count, row_count, feature_total)
    key_grad = key_blocks.transpose(0, 2, 3, 1, 4).reshape(seq_count, slot_count, feature_total)
    value_grad = value_block_list.transpose(0, 2, 3, 1, 4).reshape(
        seq_count, slot_count, feature_total
    )
    return (query_grad, key_grad, value_grad)


def general_body(
    tokens,
    lengths,
    cotangent,
    query_weight,
    key_weight,
    value_weight,
    out_weight,
    up_weight,
    down_weight,
    query_bias,
    value_bias,
    out_bias,
    attn_gain,
    attn_shift,
    up_bias,
    down_bias,
    feed_gain,
    feed_shift,
):
    seq_count, row_count, feature_total = tokens.shape
    slot_count = row_count * lax.axis_size("seq")
    token_count = seq_count * row_count
    whole = gather_weights(
        query_weight, key_weight, value_weight, out_weight, up_weight, down_weight
    )
    full_query, full_key, full_value, full_out, full_up, full_down = whole
    flat_tokens = tokens.reshape(token_count, feature_total)
    queries = (
        jnp.dot(flat_tokens, full_query, preferred_element_type=jnp.float32) + query_bias
    ).astype(jnp.bfloat16)
    key_rows = jnp.dot(flat_tokens, full_key, preferred_element_type=jnp.float32).astype(
        jnp.bfloat16
    )
    value_rows = (
        jnp.dot(flat_tokens, full_value, preferred_element_type=jnp.float32) + value_bias
    ).astype(jnp.bfloat16)
    first_slot = lax.axis_index("seq") * row_count
    key_mask = jnp.arange(slot_count)[None, :] < lengths[:, None]
    row_valid = ((first_slot + jnp.arange(row_count))[None, :] < lengths[:, None]).astype(
        jnp.float32
    )
    row_valid = row_valid.reshape(token_count, 1)
    query_blocks = queries.reshape(seq_count, row_count, feature_total)
    key_blocks = key_rows.reshape(seq_count, row_count, feature_total)
    value_block_list = value_rows.reshape(seq_count, row_count, feature_total)
    key_all, value_all = (
        lax.all_gather(key_blocks, "seq", axis=1, tiled=True),
        lax.all_gather(value_block_list, "seq", axis=1, tiled=True),
    )
    mixed_heads, log_totals = attention_forward(query_blocks, key_all, value_all, key_mask)
    heads_low = mixed_heads.reshape(token_count, feature_total).astype(jnp.bfloat16)
    attention_out = jnp.dot(heads_low, full_out, preferred_element_type=jnp.float32) + out_bias
    tokens_f32 = flat_tokens.astype(jnp.float32)
    first_sum = tokens_f32 + attention_out
    hidden, first_pull = jax.vjp(layer_norm, first_sum, attn_gain, attn_shift)
    hidden_low = hidden.astype(jnp.bfloat16)
    pre_act = jnp.dot(hidden_low, full_up, preferred_element_type=jnp.float32) + up_bias
    gelu_out, gelu_pull = jax.vjp(partial(jax.nn.gelu, approximate=False), pre_act)
    activation = gelu_out.astype(jnp.bfloat16)
    feed_out = jnp.dot(activation, full_down, preferred_element_type=jnp.float32) + down_bias
    result, second_pull = jax.vjp(layer_norm, hidden + feed_out, feed_gain, feed_shift)
    mixed = result.astype(jnp.bfloat16).reshape(seq_count, row_count, feature_total)
    partial_stats = jnp.stack(
        [
            jnp.sum(row_valid * tokens_f32 * tokens_f32),
            jnp.sum(row_valid * attention_out * attention_out),
            jnp.sum(row_valid * feed_out * feed_out),
            jnp.sum(row_valid) * feature_total,
        ]
    )
    back_weights = gather_weights(
        query_weight, key_weight, value_weight, out_weight, up_weight, down_weight
    )
    back_query, back_key, back_value, back_out, back_up, back_down = back_weights
    out_grad = cotangent.reshape(token_count, feature_total).astype(jnp.float32) * row_valid
    second_grad, feed_gain_grad, feed_shift_grad = second_pull(out_grad)
    feed_low = second_grad.astype(jnp.bfloat16)
    down_weight_grad = jnp.einsum(
        "nf,nd->fd", activation, feed_low, preferred_element_type=jnp.float32
    )
    down_bias_grad = jnp.sum(feed_low, axis=0, dtype=jnp.float32)
    act_grad = jnp.einsum(
        "nd,fd->nf", feed_low, back_down, preferred_element_type=jnp.float32
    ).astype(jnp.bfloat16)
    pre_grad = gelu_pull(act_grad.astype(jnp.float32))[0].astype(jnp.bfloat16)
    up_weight_grad = jnp.einsum(
        "nd,nf->df", hidden_low, pre_grad, preferred_element_type=jnp.float32
    )
    up_bias_grad = jnp.sum(pre_grad, axis=0, dtype=jnp.float32)
    hidden_grad = (
        jnp.einsum("nf,df->nd", pre_grad, back_up, preferred_element_type=jnp.float32) + second_grad
    )
    first_grad, attn_gain_grad, attn_shift_grad = first_pull(hidden_grad)
    attn_low = first_grad.astype(jnp.bfloat16)
    out_weight_grad = jnp.einsum(
        "nd,ne->de", heads_low, attn_low, preferred_element_type=jnp.float32
    )
    out_bias_grad = jnp.sum(attn_low, axis=0, dtype=jnp.float32)
    heads_grad = jnp.einsum(
        "ne,de->nd", attn_low, back_out, preferred_element_type=jnp.float32
    ).astype(jnp.bfloat16)
    heads_grad = heads_grad.reshape(seq_count, row_count, feature_total)
    query_grad, key_part_grad, value_part_grad = attention_backward(
        query_blocks, key_all, value_all, key_mask, heads_grad, log_totals
    )
    key_sum, value_sum = (
        lax.psum_scatter(
            key_part_grad.astype(jnp.bfloat16), "seq", scatter_dimension=1, tiled=True
        ).astype(jnp.float32),
        lax.psum_scatter(
            value_part_grad.astype(jnp.bfloat16), "seq", scatter_dimension=1, tiled=True
        ).astype(jnp.float32),
    )
    query_low = query_grad.reshape(token_count, feature_total).astype(jnp.bfloat16)
    key_low = key_sum.reshape(token_count, feature_total).astype(jnp.bfloat16)
    value_low = value_sum.reshape(token_count, feature_total).astype(jnp.bfloat16)
    query_weight_grad = jnp.einsum(
        "nd,ne->de", flat_tokens, query_low, preferred_element_type=jnp.float32
    )
    key_weight_grad = jnp.einsum(
        "nd,ne->de", flat_tokens, key_low, preferred_element_type=jnp.float32
    )
    value_weight_grad = jnp.einsum(
        "nd,ne->de", flat_tokens, value_low, preferred_element_type=jnp.float32
    )
    query_bias_grad = jnp.sum(query_low, axis=0, dtype=jnp.float32)
    value_bias_gradient = jnp.sum(value_low, axis=0, dtype=jnp.float32)
    tokens_grad = (
        jnp.einsum("ne,de->nd", query_low, back_query, preferred_element_type=jnp.float32)
        + jnp.einsum("ne,de->nd", key_low, back_key, preferred_element_type=jnp.float32)
        + jnp.einsum("ne,de->nd", value_low, back_value, preferred_element_type=jnp.float32)
        + first_grad
    )
    tokens_grad = tokens_grad.astype(jnp.bfloat16).reshape(seq_count, row_count, feature_total)
    matrix_grads = reduce_grads(
        query_weight_grad,
        key_weight_grad,
        value_weight_grad,
        out_weight_grad,
        up_weight_grad,
        down_weight_grad,
    )
    totals = lax.psum(
        (
            partial_stats,
            query_bias_grad,
            value_bias_gradient,
            out_bias_grad,
            attn_gain_grad,
            attn_shift_grad,
            up_bias_grad,
            down_bias_grad,
            feed_gain_grad,
            feed_shift_grad,
        ),
        ("dp", "seq"),
    )
    stream_rms = jnp.sqrt(totals[0][:3] / totals[0][3])
    return (
        mixed,
        tokens_grad,
        matrix_grads[0],
        matrix_grads[1],
        matrix_grads[2],
        matrix_grads[3],
        matrix_grads[4],
        matrix_grads[5],
        totals[1],
        totals[2],
        totals[3],
        totals[4],
        totals[5],
        totals[6],
        totals[7],
        totals[8],
        totals[9],
        stream_rms,
    )


def swap(value, axis):
    return lax.ppermute(value, axis, [(0, 1), (1, 0)])


def both(value, axis):
    return jnp.concatenate([value, swap(value, axis)], axis=0)


def in_order(own, other, index, axis=0):
    return jnp.where(
        index == 0, jnp.stack([own, other], axis=axis), jnp.stack([other, own], axis=axis)
    )


def split_columns(weight, width, core):
    rows = weight.shape[0]
    blocks = weight.reshape(rows, -1, 2, width)
    return pick(blocks, core, 2).reshape(rows, -1), pick(blocks, 1 - core, 2).reshape(rows, -1)


def pick(values, index, axis):
    return lax.dynamic_index_in_dim(values, index, axis, keepdims=False)


def add(left, right):
    return (left.astype(jnp.float32) + right.astype(jnp.float32)).astype(jnp.bfloat16)


def fold(values, axis, dim):
    index = lax.axis_index(axis)
    return add(pick(values, index, dim), swap(pick(values, 1 - index, dim), axis))


NEXT = [(0, 1), (1, 0), (2, 3), (3, 2)]
CROSS = [(0, 2), (2, 0), (1, 3), (3, 1)]


def fold_next(values):
    odd = lax.axis_index("z") % 2
    pairs = values.reshape((2, 2) + values.shape[1:])
    sent = pick(pairs, 1 - odd, 1)
    return add(pick(pairs, odd, 1), lax.ppermute(sent, "z", NEXT)), sent


def fold_cross(pairs):
    upper = lax.axis_index("z") // 2
    sent = pick(pairs, 1 - upper, 0)
    return add(pick(pairs, upper, 0), lax.ppermute(sent, "z", CROSS)), sent


def fold_line(values):
    return fold_cross(fold_next(values)[0])[0]


def line_cross(value):
    return lax.ppermute(value, "z", CROSS)


def line_next(pair):
    return lax.ppermute(pair, "z", NEXT)


def part_of(values, start, facts):
    return lax.dynamic_slice_in_dim(values, start + facts[5], 2, 0)


def gather_across(beside, below, facts):
    first_part, second_part = part_of(below, 0, facts), part_of(beside, 2, facts)
    return (swap(first_part, "x"), swap(second_part, "s")), (first_part, second_part)


def scatter_across(across):
    return swap(across[:2], "x"), swap(across[2:], "s")


def scatter_beside(beside, below, parts, facts):
    beside = jnp.concatenate([beside[:2], add(part_of(beside, 2, facts), parts[1])], axis=0)
    below = jnp.concatenate([add(part_of(below, 0, facts), parts[0]), below[2:]], axis=0)
    return (swap(beside, "x"), swap(below, "s")), (beside, below)


def scatter_own(own, parts):
    total = own.astype(jnp.float32) + parts[0].astype(jnp.float32) + parts[1].astype(jnp.float32)
    return total.astype(jnp.bfloat16)


def scatter_top(send, keep):
    total = add(keep, swap(send, "s"))
    total = total.reshape((4, 2) + total.shape[1:])
    return fold_line(fold(total, "x", 1))


def grad_block(left_t, right, rows):
    return product(left_t, right, 1, 0).astype(jnp.bfloat16).reshape(4, rows, -1)


def columns_of(right, index):
    columns = right.shape[1] // 2
    return lax.dynamic_slice_in_dim(right, index * columns, columns, 1)


PAIR = 2 * HD
LIMIT = 56 * 1024 * 1024


def kernel_params(steps):
    return pltpu.CompilerParams(
        dimension_semantics=("arbitrary",) * steps, vmem_limit_bytes=LIMIT
    )


def product(left, right, left_dim, right_dim):
    return lax.dot_general(
        left, right, (((left_dim,), (right_dim,)), ((), ())), preferred_element_type=jnp.float32
    )


def key_bias(facts_ref, slots):
    place = lax.broadcasted_iota(jnp.int32, (slots, 1), 0) + facts_ref[2]
    place = jnp.where(place >= slots, place - slots, place)
    return jnp.where(place < facts_ref[pl.program_id(0)], 0.0, -1e30)


def head_lanes(value, head):
    lane = lax.broadcasted_iota(jnp.int32, value.shape, 1)
    return jnp.where((lane >= HD) == (head == 1), value, jnp.zeros_like(value))


def turned(value):
    return value.astype(jnp.float32).T


def attend_kernel(facts_ref, query_ref, key_ref, value_ref, out_ref, total_ref):
    slots = key_ref.shape[0]
    bias = key_bias(facts_ref, slots)
    query = query_ref[...] * jnp.bfloat16(0.125)
    key = key_ref[...]
    value_t = turned(value_ref[...]).astype(jnp.bfloat16)
    outs = []
    for head in range(2):
        scores = product(key, head_lanes(query, head), 1, 1) + bias
        peak = jnp.max(scores, axis=0, keepdims=True)
        weight = jnp.exp(scores - peak)
        total = jnp.sum(weight, axis=0, keepdims=True)
        part = product(value_t[head * HD : (head + 1) * HD], weight.astype(jnp.bfloat16), 1, 0)
        outs.append(part * (1.0 / total))
        total_ref[0, 0, head : head + 1, :] = peak + jnp.log(total)
    out_ref[...] = jnp.concatenate(outs, axis=0).T.astype(jnp.bfloat16)


def attend_back_kernel(
    facts_ref, query_ref, key_ref, value_ref, grad_ref, total_ref, low_ref, sums_ref
):
    slots = key_ref.shape[0]
    bias = key_bias(facts_ref, slots)
    query = query_ref[...] * jnp.bfloat16(0.125)
    key = key_ref[...]
    value = value_ref[...]
    grad = grad_ref[...]
    key_t = turned(key).astype(jnp.bfloat16)
    lane = lax.broadcasted_iota(jnp.int32, (slots, PAIR), 1)
    query_parts, key_parts, value_parts = [], [], []
    for head in range(2):
        scores = product(key, head_lanes(query, head), 1, 1) + bias
        soft = jnp.exp(scores - total_ref[0, 0, head : head + 1, :])
        value_parts.append(product(soft.astype(jnp.bfloat16), grad, 1, 0))
        change = product(value, head_lanes(grad, head), 1, 1)
        inner = jnp.sum(soft * change, axis=0, keepdims=True)
        change = (soft * (change - inner)).astype(jnp.bfloat16)
        key_parts.append(product(change, query, 1, 0))
        query_parts.append(product(key_t[head * HD : (head + 1) * HD], change, 1, 0))
    pair = pl.program_id(1)
    groups = low_ref.shape[1] // 3
    query_low = (jnp.concatenate(query_parts, axis=0) * 0.125).T
    key_low = jnp.where(lane < HD, key_parts[0], key_parts[1])
    value_low = jnp.where(lane < HD, value_parts[0], value_parts[1])
    for place, part in enumerate((query_low, key_low, value_low)):
        start = pl.multiple_of(place * groups + pair * PAIR, PAIR)
        low = part.astype(jnp.bfloat16)
        low_ref[:, pl.ds(start, PAIR)] = low
        sums_ref[0, :, pl.ds(start, PAIR)] = jnp.sum(
            low.astype(jnp.float32), axis=0, keepdims=True
        )


def attention_specs(slots, pairs):
    def at(part):
        return pl.BlockSpec(
            (slots, PAIR), lambda b, g, p, *_: (b, g * 3 * pairs + part * pairs + p)
        )

    heads = pl.BlockSpec((slots, PAIR), lambda b, g, p, *_: (b, g * pairs + p))
    totals = pl.BlockSpec((1, 1, 2, slots), lambda b, g, p, *_: (b, g * pairs + p, 0, 0))
    return [at(0), at(1), at(2)], heads, totals


def attend(facts, projected, slots, wait=()):
    pairs = projected.shape[1] // (6 * PAIR)
    inputs, heads, totals = attention_specs(slots, pairs)
    rows = projected.shape[0]
    return call(
        attend_kernel,
        "attend",
        (2, 2, pairs),
        inputs,
        [heads, totals],
        [
            like((rows, 2 * pairs * PAIR), jnp.bfloat16),
            like((2, 2 * pairs, 2, slots), jnp.float32),
        ],
        facts,
        projected,
        projected,
        projected,
        wait=wait,
    )


def attend_back(facts, projected, heads_grad, totals_in, slots, own, wait=()):
    pairs = projected.shape[1] // (6 * PAIR)

    def group(facts_ref):
        return facts_ref[3] if own else 1 - facts_ref[3]

    def at(part):
        return pl.BlockSpec(
            (slots, PAIR), lambda b, p, f: (b, group(f) * 3 * pairs + part * pairs + p)
        )

    heads = pl.BlockSpec((slots, PAIR), lambda b, p, f: (b, group(f) * pairs + p))
    totals = pl.BlockSpec((1, 1, 2, slots), lambda b, p, f: (b, group(f) * pairs + p, 0, 0))
    width = 3 * pairs * PAIR
    return call(
        attend_back_kernel,
        "attend_back",
        (2, pairs),
        [at(0), at(1), at(2), heads, totals],
        [
            pl.BlockSpec((slots, width), lambda b, p, f: (b, 0)),
            pl.BlockSpec((1, 1, width), lambda b, p, f: (b, 0, 0)),
        ],
        [
            like((2 * slots, width), jnp.bfloat16),
            like((2, 1, width), jnp.float32),
        ],
        facts,
        projected,
        projected,
        projected,
        heads_grad,
        totals_in,
        wait=wait,
    )


def call(kernel, name, grid, inputs, outputs, shapes, facts, *args, wait=()):
    single = not isinstance(outputs, list)
    outputs, shapes = ([outputs], [shapes]) if single else (outputs, shapes)
    count, held = len(args), len(wait)

    def body(facts_ref, *refs):
        kernel(facts_ref, *refs[:count], *refs[count + held : -1])
        for place in range(facts.shape[0]):
            refs[-1][place] = facts_ref[place]

    results = pl.pallas_call(
        body,
        grid_spec=pltpu.PrefetchScalarGridSpec(
            num_scalar_prefetch=1,
            grid=grid,
            in_specs=list(inputs) + [pl.BlockSpec(memory_space=pl.ANY)] * held,
            out_specs=list(outputs) + [pl.BlockSpec(memory_space=pltpu.SMEM)],
        ),
        out_shape=list(shapes) + [like(facts.shape, jnp.int32)],
        compiler_params=kernel_params(len(grid)),
        name=name,
    )(facts, *args, *wait)
    return (results[0] if single else tuple(results[:-1])), results[-1]


def block(shape, *index):
    def at(*grid_and_facts):
        return tuple(entry(*grid_and_facts) if callable(entry) else entry for entry in index)

    return pl.BlockSpec(shape, at)


def whole(array):
    zeros = (0,) * array.ndim
    return pl.BlockSpec(array.shape, lambda *_: zeros)


def first(i, *_):
    return i


def like(shape, dtype):
    return jax.ShapeDtypeStruct(shape, dtype)


def square_pieces(facts_ref, refs):
    own, beside, below, first_part, second_part = [ref[0] for ref in refs]
    across = jnp.where(pl.program_id(0) < 2, first_part, second_part)
    half, column = facts_ref[3], facts_ref[4]
    near = (own, beside)
    far = (below, across)
    rows = []
    for x in range(2):
        mine = jnp.where(column == x, near[0], near[1])
        other = jnp.where(column == x, far[0], far[1])
        rows.append((jnp.where(half == 0, mine, other), jnp.where(half == 0, other, mine)))
    return rows


def square_specs(parts):
    shape = (1,) + parts[0].shape[1:]
    plain = block(shape, first, 0, 0)
    early = block(shape, lambda i, *_: jnp.minimum(i, 1), 0, 0)
    late = block(shape, lambda i, *_: jnp.maximum(i - 2, 0), 0, 0)
    return [plain, plain, plain, early, late]


def total_kernel(facts_ref, parts_ref, out_ref):
    for core in range(2):
        total = 0.0
        for chip in range(parts_ref.shape[0]):
            for half in range(parts_ref.shape[2]):
                total = total + parts_ref[chip, core, half]
        out_ref[core] = total


def total_of_parts(facts, parts, wait=()):
    shape = (parts.shape[1],) + parts.shape[3:]
    return call(
        total_kernel,
        "total",
        (1,),
        [whole(parts)],
        block(shape, 0, 0, 0),
        like(shape, jnp.float32),
        facts,
        parts,
        wait=wait,
    )[0]


def stack_kernel(own_at, facts_ref, own_ref, other_ref, out_ref):
    own = facts_ref[own_at] == pl.program_id(0)
    value = jnp.where(own, own_ref[...], other_ref[...])
    out_ref[...] = value.reshape(out_ref.shape)


def stack_pair(facts, own, other, wait=()):
    rows, columns = own.shape
    return call(
        partial(stack_kernel, 6),
        "stack",
        (2,),
        [whole(own), whole(other)],
        block((1, rows, columns), first, 0, 0),
        like((2, rows, columns), own.dtype),
        facts,
        own,
        other,
        wait=wait,
    )


def stack_line(facts, own, other, wait=()):
    _, rows, columns = own.shape
    return call(
        partial(stack_kernel, 7),
        "stack",
        (2,),
        [whole(own), whole(other)],
        block((2, 1, rows, columns), 0, first, 0, 0),
        like((2, 2, rows, columns), own.dtype),
        facts,
        own,
        other,
        wait=wait,
    )


def join_kernel(facts_ref, *refs):
    out_ref = refs[-1]
    rows = square_pieces(facts_ref, refs[:-1])
    for x in range(2):
        out_ref[x] = jnp.concatenate(rows[x], axis=1)


def join(facts, parts, wait=()):
    _, rows, columns = parts[0].shape
    return call(
        join_kernel,
        "join",
        (4,),
        square_specs(parts),
        block((2, rows, 2 * columns), first, 0, 0),
        like((8, rows, 2 * columns), jnp.bfloat16),
        facts,
        *parts,
        wait=wait,
    )


def join_near_kernel(facts_ref, *refs):
    in_ref, out_ref = refs[-2:]
    rows = square_pieces(facts_ref, refs[:-2])
    count, width = out_ref.shape[1:]
    wide = width // 4
    for x in range(2):
        in_ref[x] = jnp.concatenate([part[:, : 3 * wide] for part in rows[x]], axis=1)
        out_ref[x] = jnp.concatenate(
            [part[i * count : (i + 1) * count, 3 * wide :] for part in rows[x] for i in range(2)],
            axis=1,
        )


def join_near(facts, parts, wait=()):
    _, rows, columns = parts[0].shape
    shapes = [(8, rows, columns * 3 // 2), (8, rows // 2, columns)]
    return call(
        join_near_kernel,
        "join_near",
        (4,),
        square_specs(parts),
        [block((2,) + shape[1:], first, 0, 0) for shape in shapes],
        [like(shape, jnp.bfloat16) for shape in shapes],
        facts,
        *parts,
        wait=wait,
    )


def turn_kernel(facts_ref, own_ref, other_ref, own_t_ref, other_t_ref):
    own_t_ref[...] = own_ref[...].T
    other_t_ref[...] = other_ref[...].T


def turn(facts, values, rows, wait=()):
    count, width = values.shape
    half = width // 2
    out = block((rows, count), first, 0)
    shape = like((half, count), values.dtype)
    return call(
        turn_kernel,
        "turn",
        (half // rows,),
        [
            block((count, rows), 0, lambda i, f: 2 * i + f[4]),
            block((count, rows), 0, lambda i, f: 2 * i + 1 - f[4]),
        ],
        [out, out],
        [shape, shape],
        facts,
        values,
        values,
        wait=wait,
    )


def project_kernel(facts_ref, rows_ref, weight_ref, bias_ref, out_ref):
    out_ref[...] = (product(rows_ref[...], weight_ref[...], 1, 0) + bias_ref[...]).astype(jnp.bfloat16)


def project(facts, rows, weight, bias, wait=()):
    count, width = rows.shape
    columns = weight.shape[1]
    wide = columns // 6
    return call(
        project_kernel,
        "project",
        (6,),
        [whole(rows), block((width, wide), 0, first), block((1, wide), 0, first)],
        block((count, wide), 0, first),
        like((count, columns), jnp.bfloat16),
        facts,
        rows,
        weight,
        bias[None],
        wait=wait,
    )


def valid_rows(facts_ref, count, slots):
    place = lax.broadcasted_iota(jnp.int32, (count, 1), 0) + pl.program_id(0) * count + facts_ref[2]
    place = jnp.where(place >= slots, place - slots, place)
    return (place < facts_ref[0]).astype(jnp.float32)


def add_rows(sums_ref, rows):
    total = jnp.concatenate([jnp.sum(part, axis=0, keepdims=True) for part in rows], axis=0)
    total = jnp.concatenate([total, jnp.zeros((8 - len(rows), total.shape[1]), jnp.float32)], axis=0)

    @pl.when(pl.program_id(0) == 0)
    def _():
        sums_ref[...] = total

    @pl.when(pl.program_id(0) > 0)
    def _():
        sums_ref[...] += total


def mean_of(values):
    return jnp.mean(values, axis=-1, keepdims=True)


def attend_out_kernel(
    slots, facts_ref, own_ref, other_ref, own_weight_ref, other_weight_ref, tokens_ref, vectors_ref,
    hat_ref, rstd_ref, low_ref, sums_ref,
):
    branch = (
        product(own_ref[...], own_weight_ref[...], 1, 0)
        + product(other_ref[...], other_weight_ref[...], 1, 0)
        + vectors_ref[0:1]
    )
    tokens = tokens_ref[...].astype(jnp.float32)
    total = tokens + branch
    centered = total - mean_of(total)
    rstd = lax.rsqrt(mean_of(centered * centered) + 1e-05)
    hat = centered * rstd
    hat_ref[...] = hat
    rstd_ref[...] = rstd
    low_ref[...] = (hat * vectors_ref[1:2] + vectors_ref[2:3]).astype(jnp.bfloat16)
    valid = valid_rows(facts_ref, tokens.shape[0], slots)
    add_rows(sums_ref, [valid * tokens * tokens, valid * branch * branch])


def attend_out(facts, own, other, own_weight, other_weight, tokens, vectors, wait=()):
    slots, width = tokens.shape
    step = slots // 4
    rows = lambda array: block((step, array.shape[1]), first, 0)
    return call(
        partial(attend_out_kernel, slots),
        "attend_out",
        (4,),
        [rows(own), rows(other), whole(own_weight), whole(other_weight), rows(tokens), whole(vectors)],
        [block((step, width), first, 0), block((step, 1), first, 0), block((step, width), first, 0), block((8, width), 0, 0)],
        [
            like((slots, width), jnp.float32),
            like((slots, 1), jnp.float32),
            like((slots, width), jnp.bfloat16),
            like((8, width), jnp.float32),
        ],
        facts,
        own,
        other,
        own_weight,
        other_weight,
        tokens,
        vectors,
        wait=wait,
    )


def up_kernel(
    facts_ref, rows_ref, weight_ref, bias_ref, act_ref, slope_ref, own_t_ref, other_t_ref
):
    pre_act = product(rows_ref[...], weight_ref[...], 1, 0) + bias_ref[...]
    below = 0.5 + 0.5 * lax.erf(pre_act * 0.7071067811865476)
    act = (pre_act * below).astype(jnp.bfloat16)
    act_ref[...] = act
    slope = below + pre_act * (0.3989422804014327 * jnp.exp(-0.5 * pre_act * pre_act))
    slope_ref[...] = slope.astype(jnp.bfloat16)
    act_t = act.T

    @pl.when(pl.program_id(0) < 4)
    def _():
        own_t_ref[...] = act_t

    @pl.when(pl.program_id(0) >= 4)
    def _():
        other_t_ref[...] = act_t


def feed_up(facts, rows, weight, bias, wait=()):
    count, width = rows.shape
    units = weight.shape[1]
    wide = units // 8

    def chip(i, f):
        return jnp.where(i < 4, 2 * i + f[4], 2 * i - 7 - f[4])

    shape = like((count, units), jnp.bfloat16)
    turned_shape = like((units // 2, count), jnp.bfloat16)
    out = block((count, wide), 0, chip)
    return call(
        up_kernel,
        "feed_up",
        (8,),
        [whole(rows), block((width, wide), 0, chip), block((1, wide), 0, chip)],
        [
            out,
            out,
            block((wide, count), lambda i, *_: jnp.minimum(i, 3), 0),
            block((wide, count), lambda i, *_: jnp.maximum(i - 4, 0), 0),
        ],
        [shape, shape, turned_shape, turned_shape],
        facts,
        rows,
        weight,
        bias[None],
        wait=wait,
    )


def second_norm_kernel(
    slots, facts_ref, part_ref, other_ref, hat_ref, cotangent_ref, vectors_ref,
    mixed_ref, grad_ref, low_ref, sums_ref,
):
    branch = part_ref[...] + other_ref[...].astype(jnp.float32) + vectors_ref[0:1]
    hidden = hat_ref[...] * vectors_ref[1:2] + vectors_ref[2:3]
    gain = vectors_ref[3:4]
    total = hidden + branch
    centered = total - mean_of(total)
    rstd = lax.rsqrt(mean_of(centered * centered) + 1e-05)
    hat = centered * rstd
    mixed_ref[...] = (hat * gain + vectors_ref[4:5]).astype(jnp.bfloat16)
    valid = valid_rows(facts_ref, branch.shape[0], slots)
    grad = cotangent_ref[...].astype(jnp.float32) * valid
    scaled = grad * gain
    result = rstd * (scaled - mean_of(scaled) - hat * mean_of(scaled * hat))
    low = result.astype(jnp.bfloat16)
    grad_ref[...] = result
    low_ref[...] = low
    add_rows(sums_ref, [low.astype(jnp.float32), grad * hat, grad, valid * branch * branch])


def second_norm(facts, part, other, hat, cotangent, vectors, wait=()):
    slots, width = part.shape
    step = slots // 4
    rows = block((step, width), first, 0)
    return call(
        partial(second_norm_kernel, slots),
        "second_norm",
        (4,),
        [rows, rows, rows, rows, whole(vectors)],
        [rows, rows, rows, block((8, width), 0, 0)],
        [
            like((slots, width), jnp.bfloat16),
            like((slots, width), jnp.float32),
            like((slots, width), jnp.bfloat16),
            like((8, width), jnp.float32),
        ],
        facts,
        part,
        other,
        hat,
        cotangent,
        vectors,
        wait=wait,
    )


def first_norm_kernel(
    facts_ref, part_ref, other_ref, second_ref, hat_ref, rstd_ref, vectors_ref,
    grad_ref, low_ref, sums_ref,
):
    grad = part_ref[...] + other_ref[...].astype(jnp.float32) + second_ref[...]
    hat = hat_ref[...]
    scaled = grad * vectors_ref[1:2]
    result = rstd_ref[...] * (scaled - mean_of(scaled) - hat * mean_of(scaled * hat))
    low = result.astype(jnp.bfloat16)
    grad_ref[...] = result
    low_ref[...] = low
    add_rows(sums_ref, [low.astype(jnp.float32), grad * hat, grad])


def first_norm(facts, part, other, second, hat, rstd, vectors, wait=()):
    slots, width = part.shape
    step = slots // 4
    rows = block((step, width), first, 0)
    return call(
        first_norm_kernel,
        "first_norm",
        (4,),
        [rows, rows, rows, rows, block((step, 1), first, 0), whole(vectors)],
        [rows, rows, block((8, width), 0, 0)],
        [
            like((slots, width), jnp.float32),
            like((slots, width), jnp.bfloat16),
            like((8, width), jnp.float32),
        ],
        facts,
        part,
        other,
        second,
        hat,
        rstd,
        vectors,
        wait=wait,
    )


def act_grad_kernel(facts_ref, rows_ref, weight_ref, slope_ref, out_ref, sums_ref):
    total = product(rows_ref[...], weight_ref[...], 1, 1)
    grad = total.astype(jnp.bfloat16).astype(jnp.float32) * slope_ref[...].astype(jnp.float32)
    low = grad.astype(jnp.bfloat16)
    out_ref[...] = low
    sums_ref[...] = jnp.sum(low.astype(jnp.float32), axis=0, keepdims=True)


def act_grad(facts, rows, weight, slope, wait=()):
    count, units = slope.shape
    step = units // 8
    out = block((count, step), 0, first)
    return call(
        act_grad_kernel,
        "act_grad",
        (8,),
        [whole(rows), block((step, rows.shape[1]), first, 0), out],
        [out, block((1, step), 0, first)],
        [like((count, units), jnp.bfloat16), like((1, units), jnp.float32)],
        facts,
        rows,
        weight,
        slope,
        wait=wait,
    )


def tokens_grad_kernel(facts_ref, own_ref, other_ref, weight_ref, out_ref):
    wide = own_ref.shape[1]
    half = facts_ref[3]
    own = weight_ref[:, pl.ds(pl.multiple_of(half * wide, 128), wide)]
    other = weight_ref[:, pl.ds(pl.multiple_of((1 - half) * wide, 128), wide)]
    total = product(own_ref[...], own, 1, 1) + product(other_ref[...], other, 1, 1)
    out_ref[...] = total.astype(out_ref.dtype)


def tokens_grad_part(facts, own, other, part, weight, dtype, wait=()):
    count, columns = own.shape
    width = weight.shape[0]
    rows = block((count // 2, columns), part, 0)
    step = width // 4
    return call(
        tokens_grad_kernel,
        "tokens_grad",
        (4,),
        [rows, rows, block((step, 2 * columns), first, 0)],
        block((count // 2, step), 0, first),
        like((count // 2, width), dtype),
        facts,
        own,
        other,
        weight,
        wait=wait,
    )


def split_body(
    tokens,
    lengths,
    cotangent,
    query_weight,
    key_weight,
    value_weight,
    out_weight,
    up_weight,
    down_weight,
    query_bias,
    value_bias,
    out_bias,
    attn_gain,
    attn_shift,
    up_bias,
    down_bias,
    feed_gain,
    feed_shift,
):
    core = lax.axis_index("c")
    half = lax.axis_index("s")
    row_count, width = tokens.shape[1:]
    slots = 2 * row_count
    unit_block = down_weight.shape[0]
    units = up_bias.shape[0] // 2
    cols = width // 2
    wide = cols // 2

    def to_sequence(values):
        return jnp.concatenate([pick(values, half, 0), swap(pick(values, 1 - half, 0), "s")], axis=0)

    def from_sequence(values):
        return in_order(values[:row_count], swap(values[row_count:], "s"), half)

    small = [
        split_columns(weight, HD, core) for weight in (query_weight, key_weight, value_weight)
    ]
    large = split_columns(up_weight, unit_block, core)
    up_pair = in_order(large[0], swap(large[1], "c"), core)
    up_cols = up_pair.shape[2]
    up_mine = up_pair.reshape(-1, up_cols)
    rows = up_mine.shape[0]
    near_kept = jnp.concatenate([part[0] for part in small], axis=1)
    near_sent = jnp.concatenate([part[1] for part in small], axis=1)
    near_pair = in_order(near_kept, swap(near_sent, "c"), core)
    out_pair = jnp.concatenate([out_weight[:, :wide], out_weight[:, wide:]], axis=0)
    near_mine = jnp.concatenate([near_pair.reshape(rows, -1), out_pair], axis=1)
    line = lax.axis_index("z")
    length_own = lax.dynamic_slice_in_dim(lengths, half, 1, 0)
    facts = jnp.concatenate(
        [
            both(length_own, "c"),
            jnp.stack(
                [
                    half * row_count,
                    half,
                    lax.axis_index("x"),
                    jnp.int32(0),
                    line // 2,
                    line % 2,
                ]
            ).astype(jnp.int32),
        ]
    )
    tokens_own = to_sequence(tokens)
    cotangent_own = to_sequence(cotangent)
    near, facts = stack_pair(
        facts, near_mine, line_cross(near_mine), wait=(tokens_own, cotangent_own)
    )
    up_part, facts = stack_pair(facts, up_mine, line_cross(up_mine), wait=(near,))
    near, facts = stack_line(facts, near, line_next(near), wait=(up_part,))
    near = near.reshape((4,) + near.shape[2:])
    down_part, facts = stack_pair(facts, down_weight, line_cross(down_weight), wait=(near,))
    tokens_both = both(tokens_own, "c")
    near_beside, near_below = swap(near, "x"), swap(near, "s")
    near_across, near_sent = gather_across(near_beside, near_below, facts)
    up_part, facts = stack_line(facts, up_part, line_next(up_part), wait=near_across)
    up_part = up_part.reshape((4,) + up_part.shape[2:])
    up_beside, up_below = swap(up_part, "x"), swap(up_part, "s")
    (in_weight, out_own), facts = join_near(
        facts, (near, near_beside, near_below) + near_across, wait=(up_part,)
    )
    in_weight = in_weight.reshape(width, 6 * wide)
    out_own = out_own.reshape(cols, width)
    out_other = swap(out_own, "c")

    def halves_of(vector, size):
        return pick(vector.reshape(-1, 2, size), core, 1).reshape(-1)

    query_part = halves_of(query_bias, HD).reshape(2, wide)
    value_part = halves_of(value_bias, HD).reshape(2, wide)
    in_bias = jnp.stack([query_part, jnp.zeros_like(query_part), value_part], axis=1).reshape(-1)
    projected, facts = project(facts, tokens_both, in_weight, in_bias)
    (heads_out, totals), facts = attend(facts, projected, slots)
    heads_other = swap(heads_out[slots:], "c")
    up_across, up_sent = gather_across(up_beside, up_below, facts)
    vectors = jnp.stack(
        [out_bias, attn_gain, attn_shift, down_bias, feed_gain, feed_shift, out_bias, out_bias]
    )
    (first_hat, first_rstd, hidden_low, first_sums), facts = attend_out(
        facts,
        heads_out,
        heads_other,
        out_own,
        out_other,
        tokens_own,
        vectors,
        wait=up_sent + (down_part,),
    )
    hidden_both = both(hidden_low, "c")
    down_part, facts = stack_line(facts, down_part, line_next(down_part), wait=up_across)
    down_part = down_part.reshape((4,) + down_part.shape[2:])
    down_beside, down_below = swap(down_part, "x"), swap(down_part, "s")
    hidden_turned, facts = turn(facts, hidden_both, rows, wait=(down_part,))
    up_all, facts = join(
        facts, (up_part, up_beside, up_below) + up_across, wait=(hidden_turned[0],)
    )
    up_all = up_all.reshape(width, units)
    (activation, slope, act_own, act_other), facts = feed_up(
        facts, hidden_both, up_all, halves_of(up_bias, unit_block)
    )
    down_across, down_sent = gather_across(down_beside, down_below, facts)
    tokens_turned, facts = turn(facts, tokens_both, rows, wait=down_sent)
    down_all, facts = join(
        facts, (down_part, down_beside, down_below) + down_across, wait=(tokens_turned[0],)
    )
    down_all = down_all.reshape(units, width)
    feed_other = swap(
        product(activation[slots:], down_all, 1, 0).astype(jnp.bfloat16), "c"
    )
    feed_part = product(activation[:slots], down_all, 1, 0)
    feed_vectors = jnp.stack(
        [down_bias, attn_gain, attn_shift, feed_gain, feed_shift, out_bias, out_bias, out_bias]
    )
    (mixed, second_grad, feed_low, second_sums), facts = second_norm(
        facts, feed_part, feed_other, first_hat, cotangent_own, feed_vectors
    )
    mixed_other = swap(mixed[row_count:], "s")

    feed_both = both(feed_low, "c")
    feed_mine, feed_theirs = columns_of(feed_both, half), columns_of(feed_both, 1 - half)
    down_sent = grad_block(act_other, feed_theirs, unit_block)
    down_first = scatter_across(down_sent)
    down_mine = (
        grad_block(act_other, feed_mine, unit_block),
        grad_block(act_own, feed_theirs, unit_block),
    )
    (pre_grad, up_bias_grad), facts = act_grad(
        facts, feed_both, down_all, slope, wait=(down_sent,) + down_mine
    )
    hidden_sent = product(pre_grad[slots:], up_all, 1, 1).astype(jnp.bfloat16)
    hidden_other = swap(hidden_sent, "c")
    pre_mine, pre_theirs = columns_of(pre_grad, half), columns_of(pre_grad, 1 - half)
    hidden_own_t, hidden_other_t = hidden_turned
    up_sent = grad_block(hidden_other_t, pre_theirs, rows)
    up_first = scatter_across(up_sent)
    down_second, down_sent = scatter_beside(down_mine[0], down_mine[1], down_first, facts)
    hidden_part = product(pre_grad[:slots], up_all, 1, 1)
    (first_grad, attn_low, third_sums), facts = first_norm(
        facts,
        hidden_part,
        hidden_other,
        second_grad,
        first_hat,
        first_rstd,
        vectors,
        wait=down_sent + (up_sent,),
    )
    grad_sent = product(attn_low, out_other, 1, 1).astype(jnp.bfloat16)
    grad_other = swap(grad_sent, "c")
    grad_own = product(attn_low, out_own, 1, 1).astype(jnp.bfloat16)
    out_sent = product(heads_other, attn_low, 0, 0).astype(jnp.bfloat16)
    out_grad = add(product(heads_out[:slots], attn_low, 0, 0), swap(out_sent, "c"))
    later = facts[5]
    up_mine_grad = (
        grad_block(hidden_other_t, columns_of(pre_grad, half + later), rows),
        grad_block(hidden_own_t, columns_of(pre_grad, 1 - half + later), rows),
    )
    down_own = grad_block(act_own, columns_of(feed_both, half + later), unit_block)
    up_second, up_sent = scatter_beside(up_mine_grad[0], up_mine_grad[1], up_first, facts)
    down_pairs, down_sent = fold_next(scatter_own(down_own, down_second))
    heads_grad = jnp.concatenate([grad_own, grad_other], axis=0)
    (theirs_low, theirs_sums), facts = attend_back(
        facts,
        projected,
        heads_grad,
        totals,
        slots,
        False,
        wait=up_sent + (down_sent, out_sent),
    )
    tokens_own_t, tokens_other_t = tokens_turned
    in_sent = grad_block(tokens_other_t, theirs_low, rows)
    in_first = scatter_across(in_sent)
    in_below = grad_block(tokens_own_t, theirs_low, rows)
    down_sum, down_sent = fold_cross(down_pairs)
    out_parts = out_grad.reshape(4, 2, out_weight.shape[0], 2, cols).transpose(3, 0, 1, 2, 4)
    out_parts = out_parts.reshape(2, 8, out_weight.shape[0], cols)
    out_sent = pick(out_parts, 1 - half, 0)
    out_total = add(pick(out_parts, half, 0), swap(out_sent, "s"))
    (mine_low, mine_sums), facts = attend_back(
        facts,
        projected,
        heads_grad,
        totals,
        slots,
        True,
        wait=(in_sent, in_below, down_sent, out_sent),
    )
    in_beside = grad_block(tokens_other_t, mine_low, rows)
    in_second, in_sent = scatter_beside(in_beside, in_below, in_first, facts)
    up_own = grad_block(hidden_own_t, columns_of(pre_grad, half + facts[5]), rows)
    up_pairs, up_sent = fold_next(scatter_own(up_own, up_second))
    tokens_sent, facts = tokens_grad_part(
        facts, mine_low, theirs_low, 1, in_weight, jnp.bfloat16, wait=in_sent + (up_sent,)
    )
    tokens_other = swap(tokens_sent, "c")
    in_own = grad_block(tokens_own_t, mine_low, rows)
    tokens_part, facts = tokens_grad_part(
        facts, mine_low, theirs_low, 0, in_weight, jnp.float32, wait=(in_own,)
    )
    tokens_grad = tokens_part + tokens_other.astype(jnp.float32) + first_grad
    tokens_grad = from_sequence(tokens_grad.astype(jnp.bfloat16))
    mixed = lax.dynamic_slice_in_dim(mixed, facts[5], row_count, 0)
    mixed = in_order(mixed, mixed_other, half)
    out_total = out_total.reshape((4, 2) + out_total.shape[1:])
    out_sum = fold_line(fold(out_total, "x", 1))
    up_sum = fold_cross(up_pairs)[0]
    in_sum = fold_line(scatter_own(in_own, in_second))

    mine_sums, theirs_sums = jnp.sum(mine_sums, axis=(0, 1)), jnp.sum(theirs_sums, axis=(0, 1))
    in_bias_grad = in_order(mine_sums, theirs_sums, half).reshape(-1)
    valid_count = length_own[0].astype(jnp.float32) * width
    stats = jnp.stack(
        [jnp.sum(first_sums[0]), jnp.sum(first_sums[1]), jnp.sum(second_sums[3]), valid_count]
    )
    def total_of(vector):
        vector = jnp.pad(vector, (0, -vector.shape[0] % 1024)).reshape(-1, 128)
        gathered = lax.all_gather(vector, ("z", "x", "c", "s"))
        gathered = gathered.reshape((8, 2, 2) + vector.shape)
        return total_of_parts(facts, gathered, wait=(in_sum, up_sum, out_sum)).reshape(2, -1)

    shared = jnp.concatenate(
        [second_sums[:3].reshape(-1), third_sums[:3].reshape(-1), jnp.pad(stats, (0, 124))]
    )
    early = jnp.concatenate([shared, up_bias_grad[0]])
    late = jnp.concatenate(
        [
            in_bias_grad[:wide],
            in_bias_grad[3 * wide : 4 * wide],
            in_bias_grad[2 * wide : 3 * wide],
            in_bias_grad[5 * wide :],
        ]
    )
    both_sums = jnp.concatenate([total_of(early)[:, : early.shape[0]], total_of(late)], axis=1)
    count = shared.shape[0]
    shared = both_sums[0, :count] + both_sums[1, :count]
    down_bias_grad, feed_gain_grad, feed_shift_grad, out_bias_grad, attn_gain_grad, attn_shift_grad = [
        shared[i * width : (i + 1) * width] for i in range(6)
    ]
    stats = shared[6 * width : 6 * width + 4]

    def interleave(start, size, block_size):
        sums = both_sums[:, start : start + size].reshape(2, -1, block_size)
        return sums.transpose(1, 0, 2).reshape(-1)

    up_bias_grad = interleave(count, units, unit_block)
    query_bias_grad = interleave(count + units, cols, HD)
    value_bias_gradient = interleave(count + units + cols, cols, HD)
    stream_rms = jnp.sqrt(stats[:3] / stats[3])

    def give_back(total):
        total = total.reshape((2, rows // 2) + total.shape[1:])
        return pick(total, core, 0), swap(pick(total, 1 - core, 0), "c")

    up_shares = give_back(up_sum)
    in_shares = give_back(in_sum)
    down_weight_grad = down_sum.astype(jnp.float32)
    out_weight_grad = out_sum.astype(jnp.float32)

    def merge(shares, start, size, block):
        one, two = [
            share[:, start : start + size].reshape(rows // 2, -1, block) for share in shares
        ]
        first = jnp.where(core == 0, one, two)
        second = jnp.where(core == 0, two, one)
        return jnp.stack([first, second], axis=2).reshape(rows // 2, -1).astype(jnp.float32)

    query_weight_grad = merge(in_shares, 0, wide, HD)
    key_weight_grad = merge(in_shares, wide, wide, HD)
    value_weight_grad = merge(in_shares, 2 * wide, wide, HD)
    up_weight_grad = merge(up_shares, 0, up_cols, unit_block)
    return (
        mixed,
        tokens_grad,
        query_weight_grad,
        key_weight_grad,
        value_weight_grad,
        out_weight_grad,
        up_weight_grad,
        down_weight_grad,
        query_bias_grad,
        value_bias_gradient,
        out_bias_grad,
        attn_gain_grad,
        attn_shift_grad,
        up_bias_grad,
        down_bias_grad,
        feed_gain_grad,
        feed_shift_grad,
        stream_rms,
    )


def solution(mesh):
    devices = mesh.devices
    dp_count, seq_count = devices.shape
    split = seq_count == 2 and dp_count == 16
    if split:
        inner = jax.sharding.Mesh(devices.reshape(4, 2, 2, seq_count), ("z", "x", "c", "s"))
        dp, seq, body = ("z", "x", "c"), "s", split_body
    else:
        inner, dp, seq, body = mesh, "dp", "seq", general_body
    weights = (P(dp, seq),) * 6
    vectors = (P(),) * 9
    rows = P(dp, seq, None)
    in_specs = (rows, P(dp), rows) + weights + vectors
    out_specs = (rows, rows) + weights + vectors + (P(),)
    return jax.shard_map(body, mesh=inner, in_specs=in_specs, out_specs=out_specs, check_vma=False)
```

```python
from functools import partial
import math

import jax
import jax.numpy as jnp
from jax import lax
from jax.experimental import pallas as pl
from jax.experimental.pallas import tpu as pltpu
from jax.sharding import PartitionSpec as P

HD = 64


def layer_norm(values_in, gain_vector, shift_vector):
    mean_value = jnp.mean(values_in, axis=-1, keepdims=True)
    centered = values_in - mean_value
    variance = jnp.mean(centered * centered, axis=-1, keepdims=True)
    return centered * lax.rsqrt(variance + 1e-05) * gain_vector + shift_vector


def gather_weights(first, second, third, fourth, fifth, sixth):
    part = (
        lax.all_gather(first, "dp", axis=0, tiled=True),
        lax.all_gather(second, "dp", axis=0, tiled=True),
        lax.all_gather(third, "dp", axis=0, tiled=True),
        lax.all_gather(fourth, "dp", axis=0, tiled=True),
        lax.all_gather(fifth, "dp", axis=0, tiled=True),
        lax.all_gather(sixth, "dp", axis=0, tiled=True),
    )
    return (
        lax.all_gather(part[0], "seq", axis=1, tiled=True),
        lax.all_gather(part[1], "seq", axis=1, tiled=True),
        lax.all_gather(part[2], "seq", axis=1, tiled=True),
        lax.all_gather(part[3], "seq", axis=1, tiled=True),
        lax.all_gather(part[4], "seq", axis=1, tiled=True),
        lax.all_gather(part[5], "seq", axis=1, tiled=True),
    )


def reduce_grads(first, second, third, fourth, fifth, sixth):
    part = (
        lax.psum_scatter(first.astype(jnp.bfloat16), "seq", scatter_dimension=1, tiled=True).astype(
            jnp.float32
        ),
        lax.psum_scatter(
            second.astype(jnp.bfloat16), "seq", scatter_dimension=1, tiled=True
        ).astype(jnp.float32),
        lax.psum_scatter(third.astype(jnp.bfloat16), "seq", scatter_dimension=1, tiled=True).astype(
            jnp.float32
        ),
        lax.psum_scatter(
            fourth.astype(jnp.bfloat16), "seq", scatter_dimension=1, tiled=True
        ).astype(jnp.float32),
        lax.psum_scatter(fifth.astype(jnp.bfloat16), "seq", scatter_dimension=1, tiled=True).astype(
            jnp.float32
        ),
        lax.psum_scatter(sixth.astype(jnp.bfloat16), "seq", scatter_dimension=1, tiled=True).astype(
            jnp.float32
        ),
    )
    return (
        lax.psum_scatter(
            part[0].astype(jnp.bfloat16), "dp", scatter_dimension=0, tiled=True
        ).astype(jnp.float32),
        lax.psum_scatter(
            part[1].astype(jnp.bfloat16), "dp", scatter_dimension=0, tiled=True
        ).astype(jnp.float32),
        lax.psum_scatter(
            part[2].astype(jnp.bfloat16), "dp", scatter_dimension=0, tiled=True
        ).astype(jnp.float32),
        lax.psum_scatter(
            part[3].astype(jnp.bfloat16), "dp", scatter_dimension=0, tiled=True
        ).astype(jnp.float32),
        lax.psum_scatter(
            part[4].astype(jnp.bfloat16), "dp", scatter_dimension=0, tiled=True
        ).astype(jnp.float32),
        lax.psum_scatter(
            part[5].astype(jnp.bfloat16), "dp", scatter_dimension=0, tiled=True
        ).astype(jnp.float32),
    )


def block_layout(seq_count, row_count, head_count):
    block_seqs = math.gcd(seq_count, max(1, 512 // row_count))
    group_heads = math.gcd(head_count, 4)
    return (block_seqs, seq_count // block_seqs, group_heads, head_count // group_heads)


def head_slice(block_part, offset, group_width, group_heads):
    sliced = lax.dynamic_slice_in_dim(block_part, offset, group_width, 2)
    return sliced.reshape(sliced.shape[0], sliced.shape[1], group_heads, HD)


def attention_forward(queries, key_all, value_all, key_mask):
    seq_count, row_count, feature_total = queries.shape
    slot_count = key_all.shape[1]
    block_seqs, block_count, group_heads, group_count = block_layout(
        seq_count, row_count, feature_total // HD
    )
    group_width = group_heads * HD

    def seq_block(inputs):
        query_part, key_part, value_part, mask_part = inputs

        def head_block(group_index):
            offset = group_index * group_width
            query_heads = head_slice(query_part, offset, group_width, group_heads)
            key_heads = head_slice(key_part, offset, group_width, group_heads)
            value_heads = head_slice(value_part, offset, group_width, group_heads)
            scores = (
                jnp.einsum(
                    "brhd,bkhd->bhrk", query_heads, key_heads, preferred_element_type=jnp.float32
                )
                * 0.125
            )
            scores = jnp.where(mask_part[:, None, None, :], scores, -1e30)
            row_max = jnp.max(scores, axis=-1, keepdims=True)
            exponent = jnp.exp(scores - row_max)
            row_total = jnp.sum(exponent, axis=-1, keepdims=True)
            soft_probs = (exponent / row_total).astype(jnp.bfloat16)
            heads_out = jnp.einsum(
                "bhrk,bkhd->brhd", soft_probs, value_heads, preferred_element_type=jnp.float32
            )
            log_total = (row_max + jnp.log(row_total))[..., 0]
            return (heads_out.reshape(block_seqs, row_count, group_width), log_total)

        return lax.map(head_block, jnp.arange(group_count))

    outputs, log_totals = lax.map(
        seq_block,
        (
            queries.reshape(block_count, block_seqs, row_count, feature_total),
            key_all.reshape(block_count, block_seqs, slot_count, feature_total),
            value_all.reshape(block_count, block_seqs, slot_count, feature_total),
            key_mask.reshape(block_count, block_seqs, slot_count),
        ),
    )
    mixed_heads = outputs.transpose(0, 2, 3, 1, 4).reshape(seq_count, row_count, feature_total)
    return (mixed_heads, log_totals)


def attention_backward(queries, key_all, value_all, key_mask, heads_grad, log_totals):
    seq_count, row_count, feature_total = queries.shape
    slot_count = key_all.shape[1]
    block_seqs, block_count, group_heads, group_count = block_layout(
        seq_count, row_count, feature_total // HD
    )
    group_width = group_heads * HD

    def seq_block(inputs):
        query_part, key_part, value_part, mask_part, grad_part, total_part = inputs

        def head_block(group_index):
            offset = group_index * group_width
            query_heads = head_slice(query_part, offset, group_width, group_heads)
            key_heads = head_slice(key_part, offset, group_width, group_heads)
            value_heads = head_slice(value_part, offset, group_width, group_heads)
            grad_heads = head_slice(grad_part, offset, group_width, group_heads)
            log_total = lax.dynamic_index_in_dim(total_part, group_index, 0, keepdims=False)
            scores = (
                jnp.einsum(
                    "brhd,bkhd->bhrk", query_heads, key_heads, preferred_element_type=jnp.float32
                )
                * 0.125
            )
            scores = jnp.where(mask_part[:, None, None, :], scores, -1e30)
            soft_probs = jnp.exp(scores - log_total[..., None])
            value_grad = jnp.einsum(
                "bhrk,brhd->bkhd",
                soft_probs.astype(jnp.bfloat16),
                grad_heads,
                preferred_element_type=jnp.float32,
            )
            prob_grad = jnp.einsum(
                "brhd,bkhd->bhrk", grad_heads, value_heads, preferred_element_type=jnp.float32
            )
            inner = jnp.sum(soft_probs * prob_grad, axis=-1, keepdims=True)
            score_grad = (soft_probs * (prob_grad - inner)).astype(jnp.bfloat16)
            query_grad = (
                jnp.einsum(
                    "bhrk,bkhd->brhd", score_grad, key_heads, preferred_element_type=jnp.float32
                )
                * 0.125
            )
            key_grad = (
                jnp.einsum(
                    "bhrk,brhd->bkhd", score_grad, query_heads, preferred_element_type=jnp.float32
                )
                * 0.125
            )
            return (
                query_grad.reshape(block_seqs, row_count, group_width),
                key_grad.reshape(block_seqs, slot_count, group_width),
                value_grad.reshape(block_seqs, slot_count, group_width),
            )

        return lax.map(head_block, jnp.arange(group_count))

    query_blocks, key_blocks, value_block_list = lax.map(
        seq_block,
        (
            queries.reshape(block_count, block_seqs, row_count, feature_total),
            key_all.reshape(block_count, block_seqs, slot_count, feature_total),
            value_all.reshape(block_count, block_seqs, slot_count, feature_total),
            key_mask.reshape(block_count, block_seqs, slot_count),
            heads_grad.reshape(block_count, block_seqs, row_count, feature_total),
            log_totals,
        ),
    )
    query_grad = query_blocks.transpose(0, 2, 3, 1, 4).reshape(seq_count, row_count, feature_total)
    key_grad = key_blocks.transpose(0, 2, 3, 1, 4).reshape(seq_count, slot_count, feature_total)
    value_grad = value_block_list.transpose(0, 2, 3, 1, 4).reshape(
        seq_count, slot_count, feature_total
    )
    return (query_grad, key_grad, value_grad)


def general_body(
    tokens,
    lengths,
    cotangent,
    query_weight,
    key_weight,
    value_weight,
    out_weight,
    up_weight,
    down_weight,
    query_bias,
    value_bias,
    out_bias,
    attn_gain,
    attn_shift,
    up_bias,
    down_bias,
    feed_gain,
    feed_shift,
):
    seq_count, row_count, feature_total = tokens.shape
    slot_count = row_count * lax.axis_size("seq")
    token_count = seq_count * row_count
    whole = gather_weights(
        query_weight, key_weight, value_weight, out_weight, up_weight, down_weight
    )
    full_query, full_key, full_value, full_out, full_up, full_down = whole
    flat_tokens = tokens.reshape(token_count, feature_total)
    queries = (
        jnp.dot(flat_tokens, full_query, preferred_element_type=jnp.float32) + query_bias
    ).astype(jnp.bfloat16)
    key_rows = jnp.dot(flat_tokens, full_key, preferred_element_type=jnp.float32).astype(
        jnp.bfloat16
    )
    value_rows = (
        jnp.dot(flat_tokens, full_value, preferred_element_type=jnp.float32) + value_bias
    ).astype(jnp.bfloat16)
    first_slot = lax.axis_index("seq") * row_count
    key_mask = jnp.arange(slot_count)[None, :] < lengths[:, None]
    row_valid = ((first_slot + jnp.arange(row_count))[None, :] < lengths[:, None]).astype(
        jnp.float32
    )
    row_valid = row_valid.reshape(token_count, 1)
    query_blocks = queries.reshape(seq_count, row_count, feature_total)
    key_blocks = key_rows.reshape(seq_count, row_count, feature_total)
    value_block_list = value_rows.reshape(seq_count, row_count, feature_total)
    key_all, value_all = (
        lax.all_gather(key_blocks, "seq", axis=1, tiled=True),
        lax.all_gather(value_block_list, "seq", axis=1, tiled=True),
    )
    mixed_heads, log_totals = attention_forward(query_blocks, key_all, value_all, key_mask)
    heads_low = mixed_heads.reshape(token_count, feature_total).astype(jnp.bfloat16)
    attention_out = jnp.dot(heads_low, full_out, preferred_element_type=jnp.float32) + out_bias
    tokens_f32 = flat_tokens.astype(jnp.float32)
    first_sum = tokens_f32 + attention_out
    hidden, first_pull = jax.vjp(layer_norm, first_sum, attn_gain, attn_shift)
    hidden_low = hidden.astype(jnp.bfloat16)
    pre_act = jnp.dot(hidden_low, full_up, preferred_element_type=jnp.float32) + up_bias
    gelu_out, gelu_pull = jax.vjp(partial(jax.nn.gelu, approximate=False), pre_act)
    activation = gelu_out.astype(jnp.bfloat16)
    feed_out = jnp.dot(activation, full_down, preferred_element_type=jnp.float32) + down_bias
    result, second_pull = jax.vjp(layer_norm, hidden + feed_out, feed_gain, feed_shift)
    mixed = result.astype(jnp.bfloat16).reshape(seq_count, row_count, feature_total)
    partial_stats = jnp.stack(
        [
            jnp.sum(row_valid * tokens_f32 * tokens_f32),
            jnp.sum(row_valid * attention_out * attention_out),
            jnp.sum(row_valid * feed_out * feed_out),
            jnp.sum(row_valid) * feature_total,
        ]
    )
    back_weights = gather_weights(
        query_weight, key_weight, value_weight, out_weight, up_weight, down_weight
    )
    back_query, back_key, back_value, back_out, back_up, back_down = back_weights
    out_grad = cotangent.reshape(token_count, feature_total).astype(jnp.float32) * row_valid
    second_grad, feed_gain_grad, feed_shift_grad = second_pull(out_grad)
    feed_low = second_grad.astype(jnp.bfloat16)
    down_weight_grad = jnp.einsum(
        "nf,nd->fd", activation, feed_low, preferred_element_type=jnp.float32
    )
    down_bias_grad = jnp.sum(feed_low, axis=0, dtype=jnp.float32)
    act_grad = jnp.einsum(
        "nd,fd->nf", feed_low, back_down, preferred_element_type=jnp.float32
    ).astype(jnp.bfloat16)
    pre_grad = gelu_pull(act_grad.astype(jnp.float32))[0].astype(jnp.bfloat16)
    up_weight_grad = jnp.einsum(
        "nd,nf->df", hidden_low, pre_grad, preferred_element_type=jnp.float32
    )
    up_bias_grad = jnp.sum(pre_grad, axis=0, dtype=jnp.float32)
    hidden_grad = (
        jnp.einsum("nf,df->nd", pre_grad, back_up, preferred_element_type=jnp.float32) + second_grad
    )
    first_grad, attn_gain_grad, attn_shift_grad = first_pull(hidden_grad)
    attn_low = first_grad.astype(jnp.bfloat16)
    out_weight_grad = jnp.einsum(
        "nd,ne->de", heads_low, attn_low, preferred_element_type=jnp.float32
    )
    out_bias_grad = jnp.sum(attn_low, axis=0, dtype=jnp.float32)
    heads_grad = jnp.einsum(
        "ne,de->nd", attn_low, back_out, preferred_element_type=jnp.float32
    ).astype(jnp.bfloat16)
    heads_grad = heads_grad.reshape(seq_count, row_count, feature_total)
    query_grad, key_part_grad, value_part_grad = attention_backward(
        query_blocks, key_all, value_all, key_mask, heads_grad, log_totals
    )
    key_sum, value_sum = (
        lax.psum_scatter(
            key_part_grad.astype(jnp.bfloat16), "seq", scatter_dimension=1, tiled=True
        ).astype(jnp.float32),
        lax.psum_scatter(
            value_part_grad.astype(jnp.bfloat16), "seq", scatter_dimension=1, tiled=True
        ).astype(jnp.float32),
    )
    query_low = query_grad.reshape(token_count, feature_total).astype(jnp.bfloat16)
    key_low = key_sum.reshape(token_count, feature_total).astype(jnp.bfloat16)
    value_low = value_sum.reshape(token_count, feature_total).astype(jnp.bfloat16)
    query_weight_grad = jnp.einsum(
        "nd,ne->de", flat_tokens, query_low, preferred_element_type=jnp.float32
    )
    key_weight_grad = jnp.einsum(
        "nd,ne->de", flat_tokens, key_low, preferred_element_type=jnp.float32
    )
    value_weight_grad = jnp.einsum(
        "nd,ne->de", flat_tokens, value_low, preferred_element_type=jnp.float32
    )
    query_bias_grad = jnp.sum(query_low, axis=0, dtype=jnp.float32)
    value_bias_gradient = jnp.sum(value_low, axis=0, dtype=jnp.float32)
    tokens_grad = (
        jnp.einsum("ne,de->nd", query_low, back_query, preferred_element_type=jnp.float32)
        + jnp.einsum("ne,de->nd", key_low, back_key, preferred_element_type=jnp.float32)
        + jnp.einsum("ne,de->nd", value_low, back_value, preferred_element_type=jnp.float32)
        + first_grad
    )
    tokens_grad = tokens_grad.astype(jnp.bfloat16).reshape(seq_count, row_count, feature_total)
    matrix_grads = reduce_grads(
        query_weight_grad,
        key_weight_grad,
        value_weight_grad,
        out_weight_grad,
        up_weight_grad,
        down_weight_grad,
    )
    totals = lax.psum(
        (
            partial_stats,
            query_bias_grad,
            value_bias_gradient,
            out_bias_grad,
            attn_gain_grad,
            attn_shift_grad,
            up_bias_grad,
            down_bias_grad,
            feed_gain_grad,
            feed_shift_grad,
        ),
        ("dp", "seq"),
    )
    stream_rms = jnp.sqrt(totals[0][:3] / totals[0][3])
    return (
        mixed,
        tokens_grad,
        matrix_grads[0],
        matrix_grads[1],
        matrix_grads[2],
        matrix_grads[3],
        matrix_grads[4],
        matrix_grads[5],
        totals[1],
        totals[2],
        totals[3],
        totals[4],
        totals[5],
        totals[6],
        totals[7],
        totals[8],
        totals[9],
        stream_rms,
    )


def swap(value, axis):
    return lax.ppermute(value, axis, [(0, 1), (1, 0)])


def both(value, axis):
    return jnp.concatenate([value, swap(value, axis)], axis=0)


def in_order(own, other, index, axis=0):
    return jnp.where(
        index == 0, jnp.stack([own, other], axis=axis), jnp.stack([other, own], axis=axis)
    )


def split_columns(weight, width, core):
    rows = weight.shape[0]
    blocks = weight.reshape(rows, -1, 2, width)
    return pick(blocks, core, 2).reshape(rows, -1), pick(blocks, 1 - core, 2).reshape(rows, -1)


def pick(values, index, axis):
    return lax.dynamic_index_in_dim(values, index, axis, keepdims=False)


def add(left, right):
    return (left.astype(jnp.float32) + right.astype(jnp.float32)).astype(jnp.bfloat16)


def fold(values, axis, dim):
    index = lax.axis_index(axis)
    return add(pick(values, index, dim), swap(pick(values, 1 - index, dim), axis))


NEXT = [(0, 1), (1, 0), (2, 3), (3, 2)]
CROSS = [(0, 2), (2, 0), (1, 3), (3, 1)]


def fold_cross(pairs):
    upper = lax.axis_index("z") // 2
    return add(pick(pairs, upper, 0), lax.ppermute(pick(pairs, 1 - upper, 0), "z", CROSS))


def fold_line(values):
    odd = lax.axis_index("z") % 2
    pairs = values.reshape((2, 2) + values.shape[1:])
    sent = lax.ppermute(pick(pairs, 1 - odd, 1), "z", NEXT)
    return fold_cross(add(pick(pairs, odd, 1), sent))


def line_cross(value):
    return lax.ppermute(value, "z", CROSS)


def line_next(pair):
    return lax.ppermute(pair, "z", NEXT)


def gather_square(own, way):
    beside, below = swap(own, "x"), swap(own, "s")
    across = swap(below, "x") if way == "x" else swap(beside, "s")
    return [own, beside, below, across]


def halve(values, axis, dim):
    index = lax.axis_index(axis) % 2
    return pick(values, index, dim), pick(values, 1 - index, dim)


def line_parts(values):
    return halve(values.reshape((2, 2) + values.shape[1:]), "z", 1)


def scatter_top(send, keep):
    total = add(keep, swap(send, "s"))
    total = total.reshape((4, 2) + total.shape[1:])
    return fold_line(fold(total, "x", 1))


def grad_block(left_t, right, got=None):
    total = product(left_t, right, 1, 0)
    if got is not None:
        total = total + got.astype(jnp.float32)
    return total.astype(jnp.bfloat16)


def columns_of(right, index):
    columns = right.shape[-1] // 2
    return lax.dynamic_slice_in_dim(right, index * columns, columns, right.ndim - 1)


PAIR = 2 * HD
LIMIT = 56 * 1024 * 1024


def kernel_params(steps):
    return pltpu.CompilerParams(
        dimension_semantics=("arbitrary",) * steps, vmem_limit_bytes=LIMIT
    )


def product(left, right, left_dim, right_dim):
    return lax.dot_general(
        left, right, (((left_dim,), (right_dim,)), ((), ())), preferred_element_type=jnp.float32
    )


def key_bias(facts_ref, slots):
    place = lax.broadcasted_iota(jnp.int32, (slots, 1), 0) + facts_ref[2]
    place = jnp.where(place >= slots, place - slots, place)
    return jnp.where(place < facts_ref[pl.program_id(0)], 0.0, -1e30)


def head_lanes(value, head):
    lane = lax.broadcasted_iota(jnp.int32, value.shape, 1)
    return jnp.where((lane >= HD) == (head == 1), value, jnp.zeros_like(value))


def turned(value):
    return value.astype(jnp.float32).T


def attend_kernel(facts_ref, query_ref, key_ref, value_ref, out_ref, total_ref):
    slots = key_ref.shape[0]
    bias = key_bias(facts_ref, slots)
    query = query_ref[...] * jnp.bfloat16(0.125)
    key = key_ref[...]
    value_t = turned(value_ref[...]).astype(jnp.bfloat16)
    outs = []
    for head in range(2):
        scores = product(key, head_lanes(query, head), 1, 1) + bias
        peak = jnp.max(scores, axis=0, keepdims=True)
        weight = jnp.exp(scores - peak)
        total = jnp.sum(weight, axis=0, keepdims=True)
        part = product(value_t[head * HD : (head + 1) * HD], weight.astype(jnp.bfloat16), 1, 0)
        outs.append(part * (1.0 / total))
        total_ref[0, 0, head : head + 1, :] = peak + jnp.log(total)
    out_ref[...] = jnp.concatenate(outs, axis=0).T.astype(jnp.bfloat16)


def attend_back_kernel(
    facts_ref, query_ref, key_ref, value_ref, grad_ref, total_ref, low_ref, sums_ref
):
    slots = key_ref.shape[0]
    bias = key_bias(facts_ref, slots)
    query = query_ref[...] * jnp.bfloat16(0.125)
    key = key_ref[...]
    value = value_ref[...]
    grad = grad_ref[...]
    key_t = turned(key).astype(jnp.bfloat16)
    lane = lax.broadcasted_iota(jnp.int32, (slots, PAIR), 1)
    query_parts, key_parts, value_parts = [], [], []
    for head in range(2):
        scores = product(key, head_lanes(query, head), 1, 1) + bias
        soft = jnp.exp(scores - total_ref[0, 0, head : head + 1, :])
        value_parts.append(product(soft.astype(jnp.bfloat16), grad, 1, 0))
        change = product(value, head_lanes(grad, head), 1, 1)
        inner = jnp.sum(soft * change, axis=0, keepdims=True)
        change = (soft * (change - inner)).astype(jnp.bfloat16)
        key_parts.append(product(change, query, 1, 0))
        query_parts.append(product(key_t[head * HD : (head + 1) * HD], change, 1, 0))
    pair = pl.program_id(1)
    groups = low_ref.shape[1] // 3
    query_low = (jnp.concatenate(query_parts, axis=0) * 0.125).T
    key_low = jnp.where(lane < HD, key_parts[0], key_parts[1])
    value_low = jnp.where(lane < HD, value_parts[0], value_parts[1])
    for place, part in enumerate((query_low, key_low, value_low)):
        start = pl.multiple_of(place * groups + pair * PAIR, PAIR)
        low = part.astype(jnp.bfloat16)
        low_ref[:, pl.ds(start, PAIR)] = low
        sums_ref[0, :, pl.ds(start, PAIR)] = jnp.sum(
            low.astype(jnp.float32), axis=0, keepdims=True
        )


def attention_specs(slots, pairs):
    def at(part):
        return pl.BlockSpec(
            (slots, PAIR), lambda b, g, p, *_: (b, g * 3 * pairs + part * pairs + p)
        )

    heads = pl.BlockSpec((slots, PAIR), lambda b, g, p, *_: (b, g * pairs + p))
    totals = pl.BlockSpec((1, 1, 2, slots), lambda b, g, p, *_: (b, g * pairs + p, 0, 0))
    return [at(0), at(1), at(2)], heads, totals


def attend(facts, projected, slots, wait=()):
    pairs = projected.shape[1] // (6 * PAIR)
    inputs, heads, totals = attention_specs(slots, pairs)
    rows = projected.shape[0]
    return call(
        attend_kernel,
        "attend",
        (2, 2, pairs),
        inputs,
        [heads, totals],
        [
            like((rows, 2 * pairs * PAIR), jnp.bfloat16),
            like((2, 2 * pairs, 2, slots), jnp.float32),
        ],
        facts,
        projected,
        projected,
        projected,
        wait=wait,
    )


def attend_back(facts, projected, heads_grad, totals_in, slots, own, wait=()):
    pairs = projected.shape[1] // (6 * PAIR)

    def group(facts_ref):
        return facts_ref[3] if own else 1 - facts_ref[3]

    def at(part):
        return pl.BlockSpec(
            (slots, PAIR), lambda b, p, f: (b, group(f) * 3 * pairs + part * pairs + p)
        )

    heads = pl.BlockSpec((slots, PAIR), lambda b, p, f: (b, group(f) * pairs + p))
    totals = pl.BlockSpec((1, 1, 2, slots), lambda b, p, f: (b, group(f) * pairs + p, 0, 0))
    width = 3 * pairs * PAIR
    return call(
        attend_back_kernel,
        "attend_back",
        (2, pairs),
        [at(0), at(1), at(2), heads, totals],
        [
            pl.BlockSpec((slots, width), lambda b, p, f: (b, 0)),
            pl.BlockSpec((1, 1, width), lambda b, p, f: (b, 0, 0)),
        ],
        [
            like((2 * slots, width), jnp.bfloat16),
            like((2, 1, width), jnp.float32),
        ],
        facts,
        projected,
        projected,
        projected,
        heads_grad,
        totals_in,
        wait=wait,
    )


def call(kernel, name, grid, inputs, outputs, shapes, facts, *args, wait=(), scratch=(), through=()):
    single = not isinstance(outputs, list)
    outputs, shapes = ([outputs], [shapes]) if single else (outputs, shapes)
    count, held, passed = len(args), len(wait) + len(through), len(through)
    last = count + held + len(outputs)

    def body(facts_ref, *refs):
        kernel(facts_ref, *refs[:count], *refs[count + held : last], *refs[last + passed + 1 :])
        for place in range(facts.shape[0]):
            refs[last + passed][place] = facts_ref[place]

    results = pl.pallas_call(
        body,
        grid_spec=pltpu.PrefetchScalarGridSpec(
            num_scalar_prefetch=1,
            grid=grid,
            in_specs=list(inputs) + [pl.BlockSpec(memory_space=pl.ANY)] * held,
            out_specs=list(outputs)
            + [pl.BlockSpec(memory_space=pl.ANY)] * passed
            + [pl.BlockSpec(memory_space=pltpu.SMEM)],
            scratch_shapes=list(scratch),
        ),
        out_shape=list(shapes)
        + [like(value.shape, value.dtype) for value in through]
        + [like(facts.shape, jnp.int32)],
        input_output_aliases={1 + count + len(wait) + i: len(outputs) + i for i in range(passed)},
        compiler_params=kernel_params(len(grid)),
        name=name,
    )(facts, *args, *wait, *through)
    values = tuple(results[:-1])
    return (values[0] if single and not passed else values), results[-1]


def block(shape, *index):
    def at(*grid_and_facts):
        return tuple(entry(*grid_and_facts) if callable(entry) else entry for entry in index)

    return pl.BlockSpec(shape, at)


def whole(array):
    zeros = (0,) * array.ndim
    return pl.BlockSpec(array.shape, lambda *_: zeros)


def first(i, *_):
    return i


def like(shape, dtype):
    return jax.ShapeDtypeStruct(shape, dtype)


def rows_in_order(facts_ref, own, beside):
    even = facts_ref[4] == 0
    pieces = []
    for z in range(4):
        pieces += [jnp.where(even, own[z], beside[z]), jnp.where(even, beside[z], own[z])]
    return jnp.concatenate(pieces, axis=0)


def near_or_far(facts_ref, refs, near):
    own, beside, below, across = [ref[...] for ref in refs]
    return rows_in_order(
        facts_ref, jnp.where(near, own, below), jnp.where(near, beside, across)
    )


def square_columns(parts, wide, steps):
    shape = parts[0].shape[:2] + (wide,)
    near = block(shape, 0, 0, lambda i, *_: jnp.minimum(i, steps - 1))
    far = block(shape, 0, 0, lambda i, *_: jnp.maximum(i - steps, 0))
    return [near, near, far, far]


def half_at(i, facts, steps):
    return jnp.where(i < steps, facts[3], 1 - facts[3])


def stack_kernel(own_at, facts_ref, own_ref, other_ref, out_ref):
    own = facts_ref[own_at] == pl.program_id(0)
    value = jnp.where(own, own_ref[...], other_ref[...])
    out_ref[...] = value.reshape(out_ref.shape)


def stack_pair(facts, own, other, wait=()):
    rows, columns = own.shape
    return call(
        partial(stack_kernel, 6),
        "stack",
        (2,),
        [whole(own), whole(other)],
        block((1, rows, columns), first, 0, 0),
        like((2, rows, columns), own.dtype),
        facts,
        own,
        other,
        wait=wait,
    )


def stack_line(facts, own, other, wait=()):
    _, rows, columns = own.shape
    line, facts = call(
        partial(stack_kernel, 7),
        "stack_line",
        (2,),
        [whole(own), whole(other)],
        block((2, 1, rows, columns), 0, first, 0, 0),
        like((2, 2, rows, columns), own.dtype),
        facts,
        own,
        other,
        wait=wait,
    )
    return line.reshape(4, rows, columns), facts


def turn_kernel(facts_ref, own_ref, other_ref, own_t_ref, other_t_ref):
    own_t_ref[...] = own_ref[...].T
    other_t_ref[...] = other_ref[...].T


def turn(facts, values, rows, wait=()):
    count, width = values.shape
    half = width // 2
    out = block((rows, count), first, 0)
    shape = like((half, count), values.dtype)
    return call(
        turn_kernel,
        "turn",
        (half // rows,),
        [
            block((count, rows), 0, lambda i, f: 2 * i + f[4]),
            block((count, rows), 0, lambda i, f: 2 * i + 1 - f[4]),
        ],
        [out, out],
        [shape, shape],
        facts,
        values,
        values,
        wait=wait,
    )


def project_kernel(facts_ref, rows_ref, bias_ref, *refs):
    parts, (out_ref, in_ref, rest_ref) = refs[:4], refs[4:]
    step = pl.program_id(0)
    weight = near_or_far(facts_ref, parts, step < 4)

    @pl.when(step % 4 < 3)
    def _():
        in_ref[...] = weight
        value = product(rows_ref[...], weight, 1, 0) + bias_ref[...]
        out_ref[...] = value.astype(jnp.bfloat16)

    @pl.when(step % 4 == 3)
    def _():
        chips, count, wide = rest_ref.shape
        pairs = weight.reshape(chips, 2, count, wide // 2)
        rest_ref[...] = jnp.concatenate([pairs[:, 0], pairs[:, 1]], axis=2)


def project(facts, rows, bias, parts, wait=()):
    count, width = rows.shape
    wide = parts[0].shape[2] // 4

    def column(i, f):
        return half_at(i, f, 4) * 3 + jnp.minimum(i % 4, 2)

    out = block((count, wide), 0, column)
    rest = (8, parts[0].shape[1] // 2, 2 * wide)
    return call(
        project_kernel,
        "project",
        (8,),
        [whole(rows), block((1, wide), 0, column)] + square_columns(parts, wide, 4),
        [out, block((width, wide), 0, column), block(rest, 0, 0, lambda i, f: half_at(i, f, 4))],
        [
            like((count, 6 * wide), jnp.bfloat16),
            like((width, 6 * wide), jnp.bfloat16),
            like(rest[:2] + (4 * wide,), jnp.bfloat16),
        ],
        facts,
        rows,
        bias[None],
        *parts,
        wait=wait,
    )


def valid_rows(facts_ref, count, slots):
    place = lax.broadcasted_iota(jnp.int32, (count, 1), 0) + pl.program_id(0) * count + facts_ref[2]
    place = jnp.where(place >= slots, place - slots, place)
    return (place < facts_ref[0]).astype(jnp.float32)


def add_rows(sums_ref, rows):
    total = jnp.concatenate([jnp.sum(part, axis=0, keepdims=True) for part in rows], axis=0)
    total = jnp.concatenate([total, jnp.zeros((8 - len(rows), total.shape[1]), jnp.float32)], axis=0)

    @pl.when(pl.program_id(0) == 0)
    def _():
        sums_ref[...] = total

    @pl.when(pl.program_id(0) > 0)
    def _():
        sums_ref[...] += total


def mean_of(values):
    return jnp.mean(values, axis=-1, keepdims=True)


def attend_out_kernel(
    slots, facts_ref, own_ref, other_ref, own_weight_ref, other_weight_ref, tokens_ref, vectors_ref,
    hat_ref, rstd_ref, low_ref, sums_ref,
):
    branch = (
        product(own_ref[...], own_weight_ref[...], 1, 0)
        + product(other_ref[...], other_weight_ref[...], 1, 0)
        + vectors_ref[0:1]
    )
    tokens = tokens_ref[...].astype(jnp.float32)
    total = tokens + branch
    centered = total - mean_of(total)
    rstd = lax.rsqrt(mean_of(centered * centered) + 1e-05)
    hat = centered * rstd
    hat_ref[...] = hat
    rstd_ref[...] = rstd
    low_ref[...] = (hat * vectors_ref[1:2] + vectors_ref[2:3]).astype(jnp.bfloat16)
    valid = valid_rows(facts_ref, tokens.shape[0], slots)
    add_rows(sums_ref, [valid * tokens * tokens, valid * branch * branch])


def attend_out(facts, own, other, own_weight, other_weight, tokens, vectors, wait=()):
    slots, width = tokens.shape
    step = slots // 4
    rows = lambda array: block((step, array.shape[1]), first, 0)
    return call(
        partial(attend_out_kernel, slots),
        "attend_out",
        (4,),
        [rows(own), rows(other), whole(own_weight), whole(other_weight), rows(tokens), whole(vectors)],
        [block((step, width), first, 0), block((step, 1), first, 0), block((step, width), first, 0), block((8, width), 0, 0)],
        [
            like((slots, width), jnp.float32),
            like((slots, 1), jnp.float32),
            like((slots, width), jnp.bfloat16),
            like((8, width), jnp.float32),
        ],
        facts,
        own,
        other,
        own_weight,
        other_weight,
        tokens,
        vectors,
        wait=wait,
    )


def up_kernel(facts_ref, rows_ref, bias_ref, *refs):
    parts, (act_ref, slope_ref, turned_ref, weight_ref) = refs[:4], refs[4:]
    weight = near_or_far(facts_ref, parts, pl.program_id(0) < 4)
    weight_ref[...] = weight
    pre_act = product(rows_ref[...], weight, 1, 0) + bias_ref[...]
    below = 0.5 + 0.5 * lax.erf(pre_act * 0.7071067811865476)
    act = (pre_act * below).astype(jnp.bfloat16)
    act_ref[...] = act
    turned_ref[...] = act.T
    slope = below + pre_act * (0.3989422804014327 * jnp.exp(-0.5 * pre_act * pre_act))
    slope_ref[...] = slope.astype(jnp.bfloat16)


def feed_up(facts, rows, bias, parts, wait=()):
    count, width = rows.shape
    units = bias.shape[0]
    wide = units // 8

    def column(i, f):
        return half_at(i, f, 4) * 4 + i % 4

    shape = like((count, units), jnp.bfloat16)
    out = block((count, wide), 0, column)
    return call(
        up_kernel,
        "feed_up",
        (8,),
        [whole(rows), block((1, wide), 0, column)] + square_columns(parts, wide, 4),
        [out, out, block((wide, count), column, 0), block((width, wide), 0, column)],
        [
            shape,
            shape,
            like((units, count), jnp.bfloat16),
            like((width, units), jnp.bfloat16),
        ],
        facts,
        rows,
        bias[None],
        *parts,
        wait=wait,
    )


def down_kernel(facts_ref, rows_ref, *refs):
    parts, (weight_ref, out_ref, total_ref) = refs[:4], refs[4:]
    step = pl.program_id(0)
    own, beside, below, across = [ref[0] for ref in parts]
    even, left = facts_ref[4] == 0, facts_ref[3] == 0
    for x in range(2):
        mine = jnp.where(even, own, beside) if x == 0 else jnp.where(even, beside, own)
        theirs = jnp.where(even, below, across) if x == 0 else jnp.where(even, across, below)
        weight_ref[x] = jnp.concatenate(
            [jnp.where(left, mine, theirs), jnp.where(left, theirs, mine)], axis=1
        )
    weight = weight_ref[...].reshape(rows_ref.shape[1], out_ref.shape[1])
    value = product(rows_ref[...], weight, 1, 0)

    @pl.when(step == 0)
    def _():
        total_ref[...] = value

    @pl.when(step > 0)
    def _():
        total_ref[...] += value

    @pl.when(step == 3)
    def _():
        out_ref[...] = total_ref[...].astype(jnp.bfloat16)


def feed_down(facts, rows, parts, wait=()):
    count, units = rows.shape
    _, block_rows, half_width = parts[0].shape
    width = 2 * half_width
    shape = (1,) + parts[0].shape[1:]
    return call(
        down_kernel,
        "feed_down",
        (4,),
        [block((count // 2, units // 4), 1, first)] + [block(shape, first, 0, 0)] * 4,
        [block((2, block_rows, width), first, 0, 0), block((count // 2, width), 0, 0)],
        [like((8, block_rows, width), jnp.bfloat16), like((count // 2, width), jnp.bfloat16)],
        facts,
        rows,
        *parts,
        scratch=[pltpu.VMEM((count // 2, width), jnp.float32)],
        wait=wait,
    )


def second_norm_kernel(
    slots, facts_ref, part_ref, other_ref, hat_ref, cotangent_ref, vectors_ref,
    mixed_ref, grad_ref, low_ref, sums_ref,
):
    branch = part_ref[...] + other_ref[...].astype(jnp.float32) + vectors_ref[0:1]
    hidden = hat_ref[...] * vectors_ref[1:2] + vectors_ref[2:3]
    gain = vectors_ref[3:4]
    total = hidden + branch
    centered = total - mean_of(total)
    rstd = lax.rsqrt(mean_of(centered * centered) + 1e-05)
    hat = centered * rstd
    mixed_ref[...] = (hat * gain + vectors_ref[4:5]).astype(jnp.bfloat16)
    valid = valid_rows(facts_ref, branch.shape[0], slots)
    grad = cotangent_ref[...].astype(jnp.float32) * valid
    scaled = grad * gain
    result = rstd * (scaled - mean_of(scaled) - hat * mean_of(scaled * hat))
    low = result.astype(jnp.bfloat16)
    grad_ref[...] = result
    low_ref[...] = low
    add_rows(sums_ref, [low.astype(jnp.float32), grad * hat, grad, valid * branch * branch])


def second_norm(facts, part, other, hat, cotangent, vectors, wait=()):
    slots, width = part.shape
    step = slots // 4
    rows = block((step, width), first, 0)
    return call(
        partial(second_norm_kernel, slots),
        "second_norm",
        (4,),
        [rows, rows, rows, rows, whole(vectors)],
        [rows, rows, rows, block((8, width), 0, 0)],
        [
            like((slots, width), jnp.bfloat16),
            like((slots, width), jnp.float32),
            like((slots, width), jnp.bfloat16),
            like((8, width), jnp.float32),
        ],
        facts,
        part,
        other,
        hat,
        cotangent,
        vectors,
        wait=wait,
    )


def first_norm_kernel(
    facts_ref, part_ref, other_ref, second_ref, hat_ref, rstd_ref, vectors_ref,
    grad_ref, low_ref, sums_ref,
):
    grad = part_ref[...] + other_ref[...].astype(jnp.float32) + second_ref[...]
    hat = hat_ref[...]
    scaled = grad * vectors_ref[1:2]
    result = rstd_ref[...] * (scaled - mean_of(scaled) - hat * mean_of(scaled * hat))
    low = result.astype(jnp.bfloat16)
    grad_ref[...] = result
    low_ref[...] = low
    add_rows(sums_ref, [low.astype(jnp.float32), grad * hat, grad])


def first_norm(facts, part, other, second, hat, rstd, vectors, wait=()):
    slots, width = part.shape
    step = slots // 4
    rows = block((step, width), first, 0)
    return call(
        first_norm_kernel,
        "first_norm",
        (4,),
        [rows, rows, rows, rows, block((step, 1), first, 0), whole(vectors)],
        [rows, rows, block((8, width), 0, 0)],
        [
            like((slots, width), jnp.float32),
            like((slots, width), jnp.bfloat16),
            like((8, width), jnp.float32),
        ],
        facts,
        part,
        other,
        second,
        hat,
        rstd,
        vectors,
        wait=wait,
    )


def act_grad_kernel(facts_ref, rows_ref, weight_ref, slope_ref, out_ref, sums_ref):
    total = product(rows_ref[...], weight_ref[...], 1, 1)
    grad = total.astype(jnp.bfloat16).astype(jnp.float32) * slope_ref[...].astype(jnp.float32)
    low = grad.astype(jnp.bfloat16)
    out_ref[...] = low
    sums_ref[...] = jnp.sum(low.astype(jnp.float32), axis=0, keepdims=True)


def act_grad(facts, rows, weight, slope, wait=()):
    count, units = slope.shape
    step = units // 8
    out = block((count, step), 0, first)
    return call(
        act_grad_kernel,
        "act_grad",
        (8,),
        [whole(rows), block((step, rows.shape[1]), first, 0), out],
        [out, block((1, step), 0, first)],
        [like((count, units), jnp.bfloat16), like((1, units), jnp.float32)],
        facts,
        rows,
        weight,
        slope,
        wait=wait,
    )


def tokens_grad_kernel(facts_ref, own_ref, other_ref, weight_ref, out_ref):
    wide = own_ref.shape[1]
    half = facts_ref[3]
    own = weight_ref[:, pl.ds(pl.multiple_of(half * wide, 128), wide)]
    other = weight_ref[:, pl.ds(pl.multiple_of((1 - half) * wide, 128), wide)]
    total = product(own_ref[...], own, 1, 1) + product(other_ref[...], other, 1, 1)
    out_ref[...] = total.astype(out_ref.dtype)


def tokens_grad_part(facts, own, other, part, weight, dtype, wait=(), through=()):
    count, columns = own.shape
    width = weight.shape[0]
    rows = block((count // 2, columns), part, 0)
    step = width // 4
    return call(
        tokens_grad_kernel,
        "tokens_grad",
        (4,),
        [rows, rows, block((step, 2 * columns), first, 0)],
        block((count // 2, step), 0, first),
        like((count // 2, width), dtype),
        facts,
        own,
        other,
        weight,
        wait=wait,
        through=through,
    )


def split_body(
    tokens,
    lengths,
    cotangent,
    query_weight,
    key_weight,
    value_weight,
    out_weight,
    up_weight,
    down_weight,
    query_bias,
    value_bias,
    out_bias,
    attn_gain,
    attn_shift,
    up_bias,
    down_bias,
    feed_gain,
    feed_shift,
):
    core = lax.axis_index("c")
    half = lax.axis_index("s")
    row_count, width = tokens.shape[1:]
    slots = 2 * row_count
    unit_block = down_weight.shape[0]
    units = up_bias.shape[0] // 2
    cols = width // 2
    wide = cols // 2

    def to_sequence(values):
        return jnp.concatenate([pick(values, half, 0), swap(pick(values, 1 - half, 0), "s")], axis=0)

    def from_sequence(values):
        return in_order(values[:row_count], swap(values[row_count:], "s"), half)

    small = [
        split_columns(weight, HD, core) for weight in (query_weight, key_weight, value_weight)
    ]
    large = split_columns(up_weight, unit_block, core)
    up_pair = in_order(large[0], swap(large[1], "c"), core)
    up_cols = up_pair.shape[2]
    up_mine = up_pair.reshape(-1, up_cols)
    rows = up_mine.shape[0]
    near_kept = jnp.concatenate([part[0] for part in small], axis=1)
    near_sent = jnp.concatenate([part[1] for part in small], axis=1)
    near_pair = in_order(near_kept, swap(near_sent, "c"), core)
    out_pair = jnp.concatenate([out_weight[:, :wide], out_weight[:, wide:]], axis=0)
    near_mine = jnp.concatenate([near_pair.reshape(rows, -1), out_pair], axis=1)
    line = lax.axis_index("z")
    length_own = lax.dynamic_slice_in_dim(lengths, half, 1, 0)
    facts = jnp.concatenate(
        [
            both(length_own, "c"),
            jnp.stack(
                [
                    half * row_count,
                    half,
                    lax.axis_index("x"),
                    jnp.int32(0),
                    line // 2,
                    line % 2,
                ]
            ).astype(jnp.int32),
        ]
    )
    tokens_own = to_sequence(tokens)
    cotangent_own = to_sequence(cotangent)
    near, facts = stack_pair(facts, near_mine, line_cross(near_mine), wait=(tokens_own,))
    near, facts = stack_line(facts, near, line_next(near), wait=(cotangent_own,))
    near_parts = gather_square(near, "x")
    up_pairs, facts = stack_pair(facts, up_mine, line_cross(up_mine), wait=(near[0],))
    down_pairs, facts = stack_pair(facts, down_weight, line_cross(down_weight), wait=(up_pairs,))
    tokens_both = both(tokens_own, "c")
    up_part, facts = stack_line(
        facts, up_pairs, line_next(up_pairs), wait=(near_parts[2], down_pairs)
    )
    up_parts = gather_square(up_part, "s")
    down_part, facts = stack_line(
        facts, down_pairs, line_next(down_pairs), wait=(near_parts[3], up_part)
    )
    down_parts = gather_square(down_part, "x")
    def halves_of(vector, size):
        return pick(vector.reshape(-1, 2, size), core, 1).reshape(-1)

    query_part = halves_of(query_bias, HD).reshape(2, wide)
    value_part = halves_of(value_bias, HD).reshape(2, wide)
    in_bias = jnp.stack([query_part, jnp.zeros_like(query_part), value_part], axis=1).reshape(-1)
    (projected, in_weight, out_own), facts = project(
        facts, tokens_both, in_bias, near_parts, wait=(up_part, down_part)
    )
    out_own = out_own.reshape(cols, width)
    out_other = swap(out_own, "c")
    (heads_out, totals), facts = attend(facts, projected, slots, wait=(up_parts[2],))
    heads_other = swap(heads_out[slots:], "c")
    vectors = jnp.stack(
        [out_bias, attn_gain, attn_shift, down_bias, feed_gain, feed_shift, out_bias, out_bias]
    )
    (first_hat, first_rstd, hidden_low, first_sums), facts = attend_out(
        facts,
        heads_out,
        heads_other,
        out_own,
        out_other,
        tokens_own,
        vectors,
        wait=(up_parts[1], down_parts[2]),
    )
    hidden_both = both(hidden_low, "c")
    hidden_turned, facts = turn(facts, hidden_both, rows)
    (activation, slope, act_t, up_all), facts = feed_up(
        facts, hidden_both, halves_of(up_bias, unit_block), up_parts, wait=hidden_turned + (down_parts[1],)
    )
    (down_all, feed_sent), facts = feed_down(facts, activation, down_parts)
    down_all = down_all.reshape(units, width)
    feed_other = swap(feed_sent, "c")
    feed_part = product(activation[:slots], down_all, 1, 0)
    feed_vectors = jnp.stack(
        [down_bias, attn_gain, attn_shift, feed_gain, feed_shift, out_bias, out_bias, out_bias]
    )
    (mixed, second_grad, feed_low, second_sums), facts = second_norm(
        facts, feed_part, feed_other, first_hat, cotangent_own, feed_vectors
    )
    mixed_other = swap(mixed[row_count:], "s")

    feed_both = both(feed_low, "c")
    tokens_turned, facts = turn(facts, tokens_both, rows, wait=(feed_low,))
    feed_mine, feed_theirs = columns_of(feed_both, half), columns_of(feed_both, 1 - half)
    down_sent = grad_block(act_t, feed_theirs)
    down_got = swap(down_sent, "s")
    (pre_grad, up_bias_grad), facts = act_grad(
        facts, feed_both, down_all, slope, wait=(down_sent,)
    )
    hidden_sent = product(pre_grad[slots:], up_all, 1, 1).astype(jnp.bfloat16)
    hidden_other = swap(hidden_sent, "c")
    hidden_own_t, hidden_other_t = hidden_turned
    up_sent = grad_block(hidden_other_t, pre_grad)
    up_got = swap(up_sent, "x")
    hidden_part = product(pre_grad[:slots], up_all, 1, 1)
    (first_grad, attn_low, third_sums), facts = first_norm(
        facts,
        hidden_part,
        hidden_other,
        second_grad,
        first_hat,
        first_rstd,
        vectors,
        wait=(up_sent,),
    )
    grad_sent = product(attn_low, out_other, 1, 1).astype(jnp.bfloat16)
    grad_other = swap(grad_sent, "c")
    grad_own = product(attn_low, out_own, 1, 1).astype(jnp.bfloat16)
    out_sent = product(heads_other, attn_low, 0, 0).astype(jnp.bfloat16)
    out_got = swap(out_sent, "c")
    heads_grad = jnp.concatenate([grad_own, grad_other], axis=0)
    valid_count = length_own[0].astype(jnp.float32) * width
    stats = jnp.stack(
        [jnp.sum(first_sums[0]), jnp.sum(first_sums[1]), jnp.sum(second_sums[3]), valid_count]
    )
    early = jnp.concatenate(
        [
            second_sums[:3].reshape(-1),
            third_sums[:3].reshape(-1),
            jnp.pad(stats, (0, 124)),
            up_bias_grad[0],
        ]
    )
    early = early + lax.ppermute(early, "z", NEXT)
    (theirs_low, theirs_sums), facts = attend_back(
        facts, projected, heads_grad, totals, slots, False, wait=(out_sent, early)
    )
    tokens_own_t, tokens_other_t = tokens_turned
    across_sent = grad_block(tokens_other_t, theirs_low)
    across_got = swap(across_sent, "x")
    out_grad = grad_block(heads_out[:slots].T, attn_low, out_got)
    early = early + lax.ppermute(early, "z", CROSS)
    (mine_low, mine_sums), facts = attend_back(
        facts, projected, heads_grad, totals, slots, True, wait=(across_sent, out_grad, early)
    )
    down_total = grad_block(act_t, feed_mine, down_got)
    down_kept, down_sent = halve(down_total.reshape(4, 2, unit_block, cols), "x", 1)
    down_got = swap(down_sent, "x")
    up_total = grad_block(hidden_own_t, pre_grad, up_got).reshape(4, rows, 2 * up_cols)
    up_kept, up_sent = columns_of(up_total, half), columns_of(up_total, 1 - half)
    up_got = swap(up_sent, "s")
    beside_sent = grad_block(tokens_other_t, mine_low)
    beside_got = swap(beside_sent, "x")
    below_sent = grad_block(tokens_own_t, theirs_low, across_got)
    below_got = swap(below_sent, "s")
    (tokens_sent, out_grad, mine_sums), facts = tokens_grad_part(
        facts,
        mine_low,
        theirs_low,
        1,
        in_weight,
        jnp.bfloat16,
        wait=(beside_sent, below_sent, down_sent, up_sent),
        through=(out_grad, mine_sums),
    )
    tokens_other = swap(tokens_sent, "c")
    out_kept, out_sent = halve(out_grad.reshape(4, 2, out_weight.shape[0], width), "x", 1)
    out_got = swap(out_sent, "x")
    tokens_part, facts = tokens_grad_part(
        facts, mine_low, theirs_low, 0, in_weight, jnp.float32, wait=(out_sent,)
    )
    tokens_grad = tokens_part + tokens_other.astype(jnp.float32) + first_grad
    tokens_grad = from_sequence(tokens_grad.astype(jnp.bfloat16))
    mixed = in_order(mixed[:row_count], mixed_other, half)
    down_sum = fold_line(add(down_kept, down_got))
    up_sum = fold_line(add(up_kept, up_got))
    out_total = add(out_kept, out_got)
    out_kept, out_sent = columns_of(out_total, half), columns_of(out_total, 1 - half)
    out_sum = fold_line(add(out_kept, swap(out_sent, "s")))
    in_total = product(tokens_own_t, mine_low, 1, 0) + beside_got.astype(jnp.float32)
    in_total = (in_total + below_got.astype(jnp.float32)).astype(jnp.bfloat16)
    in_sum = fold_line(in_total.reshape(4, rows, 3 * wide))

    mine_sums, theirs_sums = jnp.sum(mine_sums, axis=(0, 1)), jnp.sum(theirs_sums, axis=(0, 1))
    late = in_order(mine_sums, theirs_sums, half)
    late = jnp.concatenate([late[:, :wide].reshape(-1), late[:, 2 * wide :].reshape(-1)])
    late = late + lax.ppermute(late, "z", NEXT)
    late = late + lax.ppermute(late, "z", CROSS)
    sums = jnp.concatenate([early, late])
    sums = sums + swap(sums, "s")
    sums = sums + swap(sums, "x")
    both_sums = in_order(sums, swap(sums, "c"), core)
    count = early.shape[0] - units
    shared = both_sums[0, :count] + both_sums[1, :count]
    down_bias_grad, feed_gain_grad, feed_shift_grad, out_bias_grad, attn_gain_grad, attn_shift_grad = [
        shared[i * width : (i + 1) * width] for i in range(6)
    ]
    stats = shared[6 * width : 6 * width + 4]

    def interleave(start, size, block_size):
        sums = both_sums[:, start : start + size].reshape(2, -1, block_size)
        return sums.transpose(1, 0, 2).reshape(-1)

    up_bias_grad = interleave(count, units, unit_block)
    query_bias_grad = interleave(count + units, cols, HD)
    value_bias_gradient = interleave(count + units + cols, cols, HD)
    stream_rms = jnp.sqrt(stats[:3] / stats[3])

    def give_back(total):
        total = total.reshape((2, rows // 2) + total.shape[1:])
        return pick(total, core, 0), swap(pick(total, 1 - core, 0), "c")

    up_shares = give_back(up_sum)
    in_shares = give_back(in_sum)
    down_weight_grad = down_sum.astype(jnp.float32)
    out_weight_grad = out_sum.astype(jnp.float32)

    def merge(shares, start, size, block):
        one, two = [
            share[:, start : start + size].reshape(rows // 2, -1, block) for share in shares
        ]
        first = jnp.where(core == 0, one, two)
        second = jnp.where(core == 0, two, one)
        return jnp.stack([first, second], axis=2).reshape(rows // 2, -1).astype(jnp.float32)

    query_weight_grad = merge(in_shares, 0, wide, HD)
    key_weight_grad = merge(in_shares, wide, wide, HD)
    value_weight_grad = merge(in_shares, 2 * wide, wide, HD)
    up_weight_grad = merge(up_shares, 0, up_cols, unit_block)
    return (
        mixed,
        tokens_grad,
        query_weight_grad,
        key_weight_grad,
        value_weight_grad,
        out_weight_grad,
        up_weight_grad,
        down_weight_grad,
        query_bias_grad,
        value_bias_gradient,
        out_bias_grad,
        attn_gain_grad,
        attn_shift_grad,
        up_bias_grad,
        down_bias_grad,
        feed_gain_grad,
        feed_shift_grad,
        stream_rms,
    )


def solution(mesh):
    devices = mesh.devices
    dp_count, seq_count = devices.shape
    split = seq_count == 2 and dp_count == 16
    if split:
        inner = jax.sharding.Mesh(devices.reshape(4, 2, 2, seq_count), ("z", "x", "c", "s"))
        dp, seq, body = ("z", "x", "c"), "s", split_body
    else:
        inner, dp, seq, body = mesh, "dp", "seq", general_body
    weights = (P(dp, seq),) * 6
    vectors = (P(),) * 9
    rows = P(dp, seq, None)
    in_specs = (rows, P(dp), rows) + weights + vectors
    out_specs = (rows, rows) + weights + vectors + (P(),)
    return jax.shard_map(body, mesh=inner, in_specs=in_specs, out_specs=out_specs, check_vma=False)
```

```python
from functools import partial
import math

import jax
import jax.numpy as jnp
from jax import lax
from jax.experimental import pallas as pl
from jax.experimental.pallas import tpu as pltpu
from jax.sharding import PartitionSpec as P

HD = 64


def layer_norm(values_in, gain_vector, shift_vector):
    mean_value = jnp.mean(values_in, axis=-1, keepdims=True)
    centered = values_in - mean_value
    variance = jnp.mean(centered * centered, axis=-1, keepdims=True)
    return centered * lax.rsqrt(variance + 1e-05) * gain_vector + shift_vector


def gather_weights(first, second, third, fourth, fifth, sixth):
    part = (
        lax.all_gather(first, "dp", axis=0, tiled=True),
        lax.all_gather(second, "dp", axis=0, tiled=True),
        lax.all_gather(third, "dp", axis=0, tiled=True),
        lax.all_gather(fourth, "dp", axis=0, tiled=True),
        lax.all_gather(fifth, "dp", axis=0, tiled=True),
        lax.all_gather(sixth, "dp", axis=0, tiled=True),
    )
    return (
        lax.all_gather(part[0], "seq", axis=1, tiled=True),
        lax.all_gather(part[1], "seq", axis=1, tiled=True),
        lax.all_gather(part[2], "seq", axis=1, tiled=True),
        lax.all_gather(part[3], "seq", axis=1, tiled=True),
        lax.all_gather(part[4], "seq", axis=1, tiled=True),
        lax.all_gather(part[5], "seq", axis=1, tiled=True),
    )


def reduce_grads(first, second, third, fourth, fifth, sixth):
    part = (
        lax.psum_scatter(first.astype(jnp.bfloat16), "seq", scatter_dimension=1, tiled=True).astype(
            jnp.float32
        ),
        lax.psum_scatter(
            second.astype(jnp.bfloat16), "seq", scatter_dimension=1, tiled=True
        ).astype(jnp.float32),
        lax.psum_scatter(third.astype(jnp.bfloat16), "seq", scatter_dimension=1, tiled=True).astype(
            jnp.float32
        ),
        lax.psum_scatter(
            fourth.astype(jnp.bfloat16), "seq", scatter_dimension=1, tiled=True
        ).astype(jnp.float32),
        lax.psum_scatter(fifth.astype(jnp.bfloat16), "seq", scatter_dimension=1, tiled=True).astype(
            jnp.float32
        ),
        lax.psum_scatter(sixth.astype(jnp.bfloat16), "seq", scatter_dimension=1, tiled=True).astype(
            jnp.float32
        ),
    )
    return (
        lax.psum_scatter(
            part[0].astype(jnp.bfloat16), "dp", scatter_dimension=0, tiled=True
        ).astype(jnp.float32),
        lax.psum_scatter(
            part[1].astype(jnp.bfloat16), "dp", scatter_dimension=0, tiled=True
        ).astype(jnp.float32),
        lax.psum_scatter(
            part[2].astype(jnp.bfloat16), "dp", scatter_dimension=0, tiled=True
        ).astype(jnp.float32),
        lax.psum_scatter(
            part[3].astype(jnp.bfloat16), "dp", scatter_dimension=0, tiled=True
        ).astype(jnp.float32),
        lax.psum_scatter(
            part[4].astype(jnp.bfloat16), "dp", scatter_dimension=0, tiled=True
        ).astype(jnp.float32),
        lax.psum_scatter(
            part[5].astype(jnp.bfloat16), "dp", scatter_dimension=0, tiled=True
        ).astype(jnp.float32),
    )


def block_layout(seq_count, row_count, head_count):
    block_seqs = math.gcd(seq_count, max(1, 512 // row_count))
    group_heads = math.gcd(head_count, 4)
    return (block_seqs, seq_count // block_seqs, group_heads, head_count // group_heads)


def head_slice(block_part, offset, group_width, group_heads):
    sliced = lax.dynamic_slice_in_dim(block_part, offset, group_width, 2)
    return sliced.reshape(sliced.shape[0], sliced.shape[1], group_heads, HD)


def attention_forward(queries, key_all, value_all, key_mask):
    seq_count, row_count, feature_total = queries.shape
    slot_count = key_all.shape[1]
    block_seqs, block_count, group_heads, group_count = block_layout(
        seq_count, row_count, feature_total // HD
    )
    group_width = group_heads * HD

    def seq_block(inputs):
        query_part, key_part, value_part, mask_part = inputs

        def head_block(group_index):
            offset = group_index * group_width
            query_heads = head_slice(query_part, offset, group_width, group_heads)
            key_heads = head_slice(key_part, offset, group_width, group_heads)
            value_heads = head_slice(value_part, offset, group_width, group_heads)
            scores = (
                jnp.einsum(
                    "brhd,bkhd->bhrk", query_heads, key_heads, preferred_element_type=jnp.float32
                )
                * 0.125
            )
            scores = jnp.where(mask_part[:, None, None, :], scores, -1e30)
            row_max = jnp.max(scores, axis=-1, keepdims=True)
            exponent = jnp.exp(scores - row_max)
            row_total = jnp.sum(exponent, axis=-1, keepdims=True)
            soft_probs = (exponent / row_total).astype(jnp.bfloat16)
            heads_out = jnp.einsum(
                "bhrk,bkhd->brhd", soft_probs, value_heads, preferred_element_type=jnp.float32
            )
            log_total = (row_max + jnp.log(row_total))[..., 0]
            return (heads_out.reshape(block_seqs, row_count, group_width), log_total)

        return lax.map(head_block, jnp.arange(group_count))

    outputs, log_totals = lax.map(
        seq_block,
        (
            queries.reshape(block_count, block_seqs, row_count, feature_total),
            key_all.reshape(block_count, block_seqs, slot_count, feature_total),
            value_all.reshape(block_count, block_seqs, slot_count, feature_total),
            key_mask.reshape(block_count, block_seqs, slot_count),
        ),
    )
    mixed_heads = outputs.transpose(0, 2, 3, 1, 4).reshape(seq_count, row_count, feature_total)
    return (mixed_heads, log_totals)


def attention_backward(queries, key_all, value_all, key_mask, heads_grad, log_totals):
    seq_count, row_count, feature_total = queries.shape
    slot_count = key_all.shape[1]
    block_seqs, block_count, group_heads, group_count = block_layout(
        seq_count, row_count, feature_total // HD
    )
    group_width = group_heads * HD

    def seq_block(inputs):
        query_part, key_part, value_part, mask_part, grad_part, total_part = inputs

        def head_block(group_index):
            offset = group_index * group_width
            query_heads = head_slice(query_part, offset, group_width, group_heads)
            key_heads = head_slice(key_part, offset, group_width, group_heads)
            value_heads = head_slice(value_part, offset, group_width, group_heads)
            grad_heads = head_slice(grad_part, offset, group_width, group_heads)
            log_total = lax.dynamic_index_in_dim(total_part, group_index, 0, keepdims=False)
            scores = (
                jnp.einsum(
                    "brhd,bkhd->bhrk", query_heads, key_heads, preferred_element_type=jnp.float32
                )
                * 0.125
            )
            scores = jnp.where(mask_part[:, None, None, :], scores, -1e30)
            soft_probs = jnp.exp(scores - log_total[..., None])
            value_grad = jnp.einsum(
                "bhrk,brhd->bkhd",
                soft_probs.astype(jnp.bfloat16),
                grad_heads,
                preferred_element_type=jnp.float32,
            )
            prob_grad = jnp.einsum(
                "brhd,bkhd->bhrk", grad_heads, value_heads, preferred_element_type=jnp.float32
            )
            inner = jnp.sum(soft_probs * prob_grad, axis=-1, keepdims=True)
            score_grad = (soft_probs * (prob_grad - inner)).astype(jnp.bfloat16)
            query_grad = (
                jnp.einsum(
                    "bhrk,bkhd->brhd", score_grad, key_heads, preferred_element_type=jnp.float32
                )
                * 0.125
            )
            key_grad = (
                jnp.einsum(
                    "bhrk,brhd->bkhd", score_grad, query_heads, preferred_element_type=jnp.float32
                )
                * 0.125
            )
            return (
                query_grad.reshape(block_seqs, row_count, group_width),
                key_grad.reshape(block_seqs, slot_count, group_width),
                value_grad.reshape(block_seqs, slot_count, group_width),
            )

        return lax.map(head_block, jnp.arange(group_count))

    query_blocks, key_blocks, value_block_list = lax.map(
        seq_block,
        (
            queries.reshape(block_count, block_seqs, row_count, feature_total),
            key_all.reshape(block_count, block_seqs, slot_count, feature_total),
            value_all.reshape(block_count, block_seqs, slot_count, feature_total),
            key_mask.reshape(block_count, block_seqs, slot_count),
            heads_grad.reshape(block_count, block_seqs, row_count, feature_total),
            log_totals,
        ),
    )
    query_grad = query_blocks.transpose(0, 2, 3, 1, 4).reshape(seq_count, row_count, feature_total)
    key_grad = key_blocks.transpose(0, 2, 3, 1, 4).reshape(seq_count, slot_count, feature_total)
    value_grad = value_block_list.transpose(0, 2, 3, 1, 4).reshape(
        seq_count, slot_count, feature_total
    )
    return (query_grad, key_grad, value_grad)


def general_body(
    tokens,
    lengths,
    cotangent,
    query_weight,
    key_weight,
    value_weight,
    out_weight,
    up_weight,
    down_weight,
    query_bias,
    value_bias,
    out_bias,
    attn_gain,
    attn_shift,
    up_bias,
    down_bias,
    feed_gain,
    feed_shift,
):
    seq_count, row_count, feature_total = tokens.shape
    slot_count = row_count * lax.axis_size("seq")
    token_count = seq_count * row_count
    whole = gather_weights(
        query_weight, key_weight, value_weight, out_weight, up_weight, down_weight
    )
    full_query, full_key, full_value, full_out, full_up, full_down = whole
    flat_tokens = tokens.reshape(token_count, feature_total)
    queries = (
        jnp.dot(flat_tokens, full_query, preferred_element_type=jnp.float32) + query_bias
    ).astype(jnp.bfloat16)
    key_rows = jnp.dot(flat_tokens, full_key, preferred_element_type=jnp.float32).astype(
        jnp.bfloat16
    )
    value_rows = (
        jnp.dot(flat_tokens, full_value, preferred_element_type=jnp.float32) + value_bias
    ).astype(jnp.bfloat16)
    first_slot = lax.axis_index("seq") * row_count
    key_mask = jnp.arange(slot_count)[None, :] < lengths[:, None]
    row_valid = ((first_slot + jnp.arange(row_count))[None, :] < lengths[:, None]).astype(
        jnp.float32
    )
    row_valid = row_valid.reshape(token_count, 1)
    query_blocks = queries.reshape(seq_count, row_count, feature_total)
    key_blocks = key_rows.reshape(seq_count, row_count, feature_total)
    value_block_list = value_rows.reshape(seq_count, row_count, feature_total)
    key_all, value_all = (
        lax.all_gather(key_blocks, "seq", axis=1, tiled=True),
        lax.all_gather(value_block_list, "seq", axis=1, tiled=True),
    )
    mixed_heads, log_totals = attention_forward(query_blocks, key_all, value_all, key_mask)
    heads_low = mixed_heads.reshape(token_count, feature_total).astype(jnp.bfloat16)
    attention_out = jnp.dot(heads_low, full_out, preferred_element_type=jnp.float32) + out_bias
    tokens_f32 = flat_tokens.astype(jnp.float32)
    first_sum = tokens_f32 + attention_out
    hidden, first_pull = jax.vjp(layer_norm, first_sum, attn_gain, attn_shift)
    hidden_low = hidden.astype(jnp.bfloat16)
    pre_act = jnp.dot(hidden_low, full_up, preferred_element_type=jnp.float32) + up_bias
    gelu_out, gelu_pull = jax.vjp(partial(jax.nn.gelu, approximate=False), pre_act)
    activation = gelu_out.astype(jnp.bfloat16)
    feed_out = jnp.dot(activation, full_down, preferred_element_type=jnp.float32) + down_bias
    result, second_pull = jax.vjp(layer_norm, hidden + feed_out, feed_gain, feed_shift)
    mixed = result.astype(jnp.bfloat16).reshape(seq_count, row_count, feature_total)
    partial_stats = jnp.stack(
        [
            jnp.sum(row_valid * tokens_f32 * tokens_f32),
            jnp.sum(row_valid * attention_out * attention_out),
            jnp.sum(row_valid * feed_out * feed_out),
            jnp.sum(row_valid) * feature_total,
        ]
    )
    back_weights = gather_weights(
        query_weight, key_weight, value_weight, out_weight, up_weight, down_weight
    )
    back_query, back_key, back_value, back_out, back_up, back_down = back_weights
    out_grad = cotangent.reshape(token_count, feature_total).astype(jnp.float32) * row_valid
    second_grad, feed_gain_grad, feed_shift_grad = second_pull(out_grad)
    feed_low = second_grad.astype(jnp.bfloat16)
    down_weight_grad = jnp.einsum(
        "nf,nd->fd", activation, feed_low, preferred_element_type=jnp.float32
    )
    down_bias_grad = jnp.sum(feed_low, axis=0, dtype=jnp.float32)
    act_grad = jnp.einsum(
        "nd,fd->nf", feed_low, back_down, preferred_element_type=jnp.float32
    ).astype(jnp.bfloat16)
    pre_grad = gelu_pull(act_grad.astype(jnp.float32))[0].astype(jnp.bfloat16)
    up_weight_grad = jnp.einsum(
        "nd,nf->df", hidden_low, pre_grad, preferred_element_type=jnp.float32
    )
    up_bias_grad = jnp.sum(pre_grad, axis=0, dtype=jnp.float32)
    hidden_grad = (
        jnp.einsum("nf,df->nd", pre_grad, back_up, preferred_element_type=jnp.float32) + second_grad
    )
    first_grad, attn_gain_grad, attn_shift_grad = first_pull(hidden_grad)
    attn_low = first_grad.astype(jnp.bfloat16)
    out_weight_grad = jnp.einsum(
        "nd,ne->de", heads_low, attn_low, preferred_element_type=jnp.float32
    )
    out_bias_grad = jnp.sum(attn_low, axis=0, dtype=jnp.float32)
    heads_grad = jnp.einsum(
        "ne,de->nd", attn_low, back_out, preferred_element_type=jnp.float32
    ).astype(jnp.bfloat16)
    heads_grad = heads_grad.reshape(seq_count, row_count, feature_total)
    query_grad, key_part_grad, value_part_grad = attention_backward(
        query_blocks, key_all, value_all, key_mask, heads_grad, log_totals
    )
    key_sum, value_sum = (
        lax.psum_scatter(
            key_part_grad.astype(jnp.bfloat16), "seq", scatter_dimension=1, tiled=True
        ).astype(jnp.float32),
        lax.psum_scatter(
            value_part_grad.astype(jnp.bfloat16), "seq", scatter_dimension=1, tiled=True
        ).astype(jnp.float32),
    )
    query_low = query_grad.reshape(token_count, feature_total).astype(jnp.bfloat16)
    key_low = key_sum.reshape(token_count, feature_total).astype(jnp.bfloat16)
    value_low = value_sum.reshape(token_count, feature_total).astype(jnp.bfloat16)
    query_weight_grad = jnp.einsum(
        "nd,ne->de", flat_tokens, query_low, preferred_element_type=jnp.float32
    )
    key_weight_grad = jnp.einsum(
        "nd,ne->de", flat_tokens, key_low, preferred_element_type=jnp.float32
    )
    value_weight_grad = jnp.einsum(
        "nd,ne->de", flat_tokens, value_low, preferred_element_type=jnp.float32
    )
    query_bias_grad = jnp.sum(query_low, axis=0, dtype=jnp.float32)
    value_bias_gradient = jnp.sum(value_low, axis=0, dtype=jnp.float32)
    tokens_grad = (
        jnp.einsum("ne,de->nd", query_low, back_query, preferred_element_type=jnp.float32)
        + jnp.einsum("ne,de->nd", key_low, back_key, preferred_element_type=jnp.float32)
        + jnp.einsum("ne,de->nd", value_low, back_value, preferred_element_type=jnp.float32)
        + first_grad
    )
    tokens_grad = tokens_grad.astype(jnp.bfloat16).reshape(seq_count, row_count, feature_total)
    matrix_grads = reduce_grads(
        query_weight_grad,
        key_weight_grad,
        value_weight_grad,
        out_weight_grad,
        up_weight_grad,
        down_weight_grad,
    )
    totals = lax.psum(
        (
            partial_stats,
            query_bias_grad,
            value_bias_gradient,
            out_bias_grad,
            attn_gain_grad,
            attn_shift_grad,
            up_bias_grad,
            down_bias_grad,
            feed_gain_grad,
            feed_shift_grad,
        ),
        ("dp", "seq"),
    )
    stream_rms = jnp.sqrt(totals[0][:3] / totals[0][3])
    return (
        mixed,
        tokens_grad,
        matrix_grads[0],
        matrix_grads[1],
        matrix_grads[2],
        matrix_grads[3],
        matrix_grads[4],
        matrix_grads[5],
        totals[1],
        totals[2],
        totals[3],
        totals[4],
        totals[5],
        totals[6],
        totals[7],
        totals[8],
        totals[9],
        stream_rms,
    )


def swap(value, axis):
    return lax.ppermute(value, axis, [(0, 1), (1, 0)])


def both(value, axis):
    return jnp.concatenate([value, swap(value, axis)], axis=0)


def in_order(own, other, index, axis=0):
    return jnp.where(
        index == 0, jnp.stack([own, other], axis=axis), jnp.stack([other, own], axis=axis)
    )


def split_columns(weight, width, core):
    rows = weight.shape[0]
    blocks = weight.reshape(rows, -1, 2, width)
    return pick(blocks, core, 2).reshape(rows, -1), pick(blocks, 1 - core, 2).reshape(rows, -1)


def pick(values, index, axis):
    return lax.dynamic_index_in_dim(values, index, axis, keepdims=False)


def add(left, right):
    return (left.astype(jnp.float32) + right.astype(jnp.float32)).astype(jnp.bfloat16)


def fold(values, axis, dim):
    index = lax.axis_index(axis)
    return add(pick(values, index, dim), swap(pick(values, 1 - index, dim), axis))


NEXT = [(0, 1), (1, 0), (2, 3), (3, 2)]
CROSS = [(0, 2), (2, 0), (1, 3), (3, 1)]


def fold_cross(pairs):
    upper = lax.axis_index("z") // 2
    return add(pick(pairs, upper, 0), lax.ppermute(pick(pairs, 1 - upper, 0), "z", CROSS))


def fold_line(values):
    odd = lax.axis_index("z") % 2
    pairs = values.reshape((2, 2) + values.shape[1:])
    sent = lax.ppermute(pick(pairs, 1 - odd, 1), "z", NEXT)
    return fold_cross(add(pick(pairs, odd, 1), sent))


def line_cross(value):
    return lax.ppermute(value, "z", CROSS)


def line_next(pair):
    return lax.ppermute(pair, "z", NEXT)


def gather_square(own, way):
    beside, below = swap(own, "x"), swap(own, "s")
    across = swap(below, "x") if way == "x" else swap(beside, "s")
    return [own, beside, below, across]


def fold_columns(total):
    half = lax.axis_index("s")
    return add(columns_of(total, half), swap(columns_of(total, 1 - half), "s"))


def halve(values, axis, dim):
    index = lax.axis_index(axis) % 2
    return pick(values, index, dim), pick(values, 1 - index, dim)


def line_parts(values):
    return halve(values.reshape((2, 2) + values.shape[1:]), "z", 1)


def scatter_top(send, keep):
    total = add(keep, swap(send, "s"))
    total = total.reshape((4, 2) + total.shape[1:])
    return fold_line(fold(total, "x", 1))


def grad_block(left_t, right, got=None):
    total = product(left_t, right, 1, 0)
    if got is not None:
        total = total + got.astype(jnp.float32)
    return total.astype(jnp.bfloat16)


def columns_of(right, index):
    columns = right.shape[-1] // 2
    return lax.dynamic_slice_in_dim(right, index * columns, columns, right.ndim - 1)


PAIR = 2 * HD
LIMIT = 56 * 1024 * 1024


def kernel_params(steps):
    return pltpu.CompilerParams(
        dimension_semantics=("arbitrary",) * steps, vmem_limit_bytes=LIMIT
    )


def product(left, right, left_dim, right_dim):
    return lax.dot_general(
        left, right, (((left_dim,), (right_dim,)), ((), ())), preferred_element_type=jnp.float32
    )


def key_bias(facts_ref, slots):
    place = lax.broadcasted_iota(jnp.int32, (slots, 1), 0) + facts_ref[2]
    place = jnp.where(place >= slots, place - slots, place)
    return jnp.where(place < facts_ref[pl.program_id(0)], 0.0, -1e30)


def head_lanes(value, head):
    lane = lax.broadcasted_iota(jnp.int32, value.shape, 1)
    return jnp.where((lane >= HD) == (head == 1), value, jnp.zeros_like(value))


def turned(value):
    return value.astype(jnp.float32).T


def attend_kernel(facts_ref, query_ref, key_ref, value_ref, out_ref, total_ref):
    slots = key_ref.shape[0]
    bias = key_bias(facts_ref, slots)
    query = query_ref[...] * jnp.bfloat16(0.125)
    key = key_ref[...]
    value_t = turned(value_ref[...]).astype(jnp.bfloat16)
    outs = []
    for head in range(2):
        scores = product(key, head_lanes(query, head), 1, 1) + bias
        peak = jnp.max(scores, axis=0, keepdims=True)
        weight = jnp.exp(scores - peak)
        total = jnp.sum(weight, axis=0, keepdims=True)
        part = product(value_t[head * HD : (head + 1) * HD], weight.astype(jnp.bfloat16), 1, 0)
        outs.append(part * (1.0 / total))
        total_ref[0, 0, head : head + 1, :] = peak + jnp.log(total)
    out_ref[...] = jnp.concatenate(outs, axis=0).T.astype(jnp.bfloat16)


def attend_back_kernel(
    facts_ref, query_ref, key_ref, value_ref, grad_ref, total_ref, low_ref, sums_ref
):
    slots = key_ref.shape[0]
    bias = key_bias(facts_ref, slots)
    query = query_ref[...] * jnp.bfloat16(0.125)
    key = key_ref[...]
    value = value_ref[...]
    grad = grad_ref[...]
    key_t = turned(key).astype(jnp.bfloat16)
    lane = lax.broadcasted_iota(jnp.int32, (slots, PAIR), 1)
    query_parts, key_parts, value_parts = [], [], []
    for head in range(2):
        scores = product(key, head_lanes(query, head), 1, 1) + bias
        soft = jnp.exp(scores - total_ref[0, 0, head : head + 1, :])
        value_parts.append(product(soft.astype(jnp.bfloat16), grad, 1, 0))
        change = product(value, head_lanes(grad, head), 1, 1)
        inner = jnp.sum(soft * change, axis=0, keepdims=True)
        change = (soft * (change - inner)).astype(jnp.bfloat16)
        key_parts.append(product(change, query, 1, 0))
        query_parts.append(product(key_t[head * HD : (head + 1) * HD], change, 1, 0))
    pair = pl.program_id(1)
    groups = low_ref.shape[1] // 3
    query_low = (jnp.concatenate(query_parts, axis=0) * 0.125).T
    key_low = jnp.where(lane < HD, key_parts[0], key_parts[1])
    value_low = jnp.where(lane < HD, value_parts[0], value_parts[1])
    for place, part in enumerate((query_low, key_low, value_low)):
        start = pl.multiple_of(place * groups + pair * PAIR, PAIR)
        low = part.astype(jnp.bfloat16)
        low_ref[:, pl.ds(start, PAIR)] = low
        sums_ref[0, :, pl.ds(start, PAIR)] = jnp.sum(
            low.astype(jnp.float32), axis=0, keepdims=True
        )


def attention_specs(slots, pairs):
    def at(part):
        return pl.BlockSpec(
            (slots, PAIR), lambda b, g, p, *_: (b, g * 3 * pairs + part * pairs + p)
        )

    heads = pl.BlockSpec((slots, PAIR), lambda b, g, p, *_: (b, g * pairs + p))
    totals = pl.BlockSpec((1, 1, 2, slots), lambda b, g, p, *_: (b, g * pairs + p, 0, 0))
    return [at(0), at(1), at(2)], heads, totals


def attend(facts, projected, slots, wait=()):
    pairs = projected.shape[1] // (6 * PAIR)
    inputs, heads, totals = attention_specs(slots, pairs)
    rows = projected.shape[0]
    return call(
        attend_kernel,
        "attend",
        (2, 2, pairs),
        inputs,
        [heads, totals],
        [
            like((rows, 2 * pairs * PAIR), jnp.bfloat16),
            like((2, 2 * pairs, 2, slots), jnp.float32),
        ],
        facts,
        projected,
        projected,
        projected,
        wait=wait,
    )


def attend_back(facts, projected, heads_grad, totals_in, slots, own, wait=()):
    pairs = projected.shape[1] // (6 * PAIR)

    def group(facts_ref):
        return facts_ref[3] if own else 1 - facts_ref[3]

    def at(part):
        return pl.BlockSpec(
            (slots, PAIR), lambda b, p, f: (b, group(f) * 3 * pairs + part * pairs + p)
        )

    heads = pl.BlockSpec((slots, PAIR), lambda b, p, f: (b, group(f) * pairs + p))
    totals = pl.BlockSpec((1, 1, 2, slots), lambda b, p, f: (b, group(f) * pairs + p, 0, 0))
    width = 3 * pairs * PAIR
    return call(
        attend_back_kernel,
        "attend_back",
        (2, pairs),
        [at(0), at(1), at(2), heads, totals],
        [
            pl.BlockSpec((slots, width), lambda b, p, f: (b, 0)),
            pl.BlockSpec((1, 1, width), lambda b, p, f: (b, 0, 0)),
        ],
        [
            like((2 * slots, width), jnp.bfloat16),
            like((2, 1, width), jnp.float32),
        ],
        facts,
        projected,
        projected,
        projected,
        heads_grad,
        totals_in,
        wait=wait,
    )


def call(kernel, name, grid, inputs, outputs, shapes, facts, *args, wait=(), scratch=(), through=()):
    single = not isinstance(outputs, list)
    outputs, shapes = ([outputs], [shapes]) if single else (outputs, shapes)
    count, held, passed = len(args), len(wait) + len(through), len(through)
    last = count + held + len(outputs)

    def body(facts_ref, *refs):
        kernel(facts_ref, *refs[:count], *refs[count + held : last], *refs[last + passed + 1 :])
        for place in range(facts.shape[0]):
            refs[last + passed][place] = facts_ref[place]

    results = pl.pallas_call(
        body,
        grid_spec=pltpu.PrefetchScalarGridSpec(
            num_scalar_prefetch=1,
            grid=grid,
            in_specs=list(inputs) + [pl.BlockSpec(memory_space=pl.ANY)] * held,
            out_specs=list(outputs)
            + [pl.BlockSpec(memory_space=pl.ANY)] * passed
            + [pl.BlockSpec(memory_space=pltpu.SMEM)],
            scratch_shapes=list(scratch),
        ),
        out_shape=list(shapes)
        + [like(value.shape, value.dtype) for value in through]
        + [like(facts.shape, jnp.int32)],
        input_output_aliases={1 + count + len(wait) + i: len(outputs) + i for i in range(passed)},
        compiler_params=kernel_params(len(grid)),
        name=name,
    )(facts, *args, *wait, *through)
    values = tuple(results[:-1])
    return (values[0] if single and not passed else values), results[-1]


def block(shape, *index):
    def at(*grid_and_facts):
        return tuple(entry(*grid_and_facts) if callable(entry) else entry for entry in index)

    return pl.BlockSpec(shape, at)


def whole(array):
    zeros = (0,) * array.ndim
    return pl.BlockSpec(array.shape, lambda *_: zeros)


def first(i, *_):
    return i


def like(shape, dtype):
    return jax.ShapeDtypeStruct(shape, dtype)


def rows_in_order(facts_ref, own, beside):
    even = facts_ref[4] == 0
    pieces = []
    for z in range(4):
        pieces += [jnp.where(even, own[z], beside[z]), jnp.where(even, beside[z], own[z])]
    return jnp.concatenate(pieces, axis=0)


def near_or_far(facts_ref, refs, near):
    own, beside, below, across = [ref[...] for ref in refs]
    return rows_in_order(
        facts_ref, jnp.where(near, own, below), jnp.where(near, beside, across)
    )


def square_columns(parts, wide, steps):
    shape = parts[0].shape[:2] + (wide,)
    near = block(shape, 0, 0, lambda i, *_: jnp.minimum(i, steps - 1))
    far = block(shape, 0, 0, lambda i, *_: jnp.maximum(i - steps, 0))
    return [near, near, far, far]


def half_at(i, facts, steps):
    return jnp.where(i < steps, facts[3], 1 - facts[3])


def stack_kernel(own_at, facts_ref, own_ref, other_ref, out_ref):
    own = facts_ref[own_at] == pl.program_id(0)
    value = jnp.where(own, own_ref[...], other_ref[...])
    out_ref[...] = value.reshape(out_ref.shape)


def stack_pair(facts, own, other, wait=()):
    rows, columns = own.shape
    return call(
        partial(stack_kernel, 6),
        "stack",
        (2,),
        [whole(own), whole(other)],
        block((1, rows, columns), first, 0, 0),
        like((2, rows, columns), own.dtype),
        facts,
        own,
        other,
        wait=wait,
    )


def stack_line(facts, own, other, wait=()):
    _, rows, columns = own.shape
    line, facts = call(
        partial(stack_kernel, 7),
        "stack_line",
        (2,),
        [whole(own), whole(other)],
        block((2, 1, rows, columns), 0, first, 0, 0),
        like((2, 2, rows, columns), own.dtype),
        facts,
        own,
        other,
        wait=wait,
    )
    return line.reshape(4, rows, columns), facts


def turn_kernel(facts_ref, own_ref, other_ref, own_t_ref, other_t_ref):
    own_t_ref[...] = own_ref[...].T
    other_t_ref[...] = other_ref[...].T


def turn(facts, values, rows, wait=()):
    count, width = values.shape
    half = width // 2
    out = block((rows, count), first, 0)
    shape = like((half, count), values.dtype)
    return call(
        turn_kernel,
        "turn",
        (half // rows,),
        [
            block((count, rows), 0, lambda i, f: 2 * i + f[4]),
            block((count, rows), 0, lambda i, f: 2 * i + 1 - f[4]),
        ],
        [out, out],
        [shape, shape],
        facts,
        values,
        values,
        wait=wait,
    )


def project_kernel(facts_ref, rows_ref, bias_ref, *refs):
    parts, (out_ref, in_ref, rest_ref) = refs[:4], refs[4:]
    step = pl.program_id(0)
    weight = near_or_far(facts_ref, parts, step < 4)

    @pl.when(step % 4 < 3)
    def _():
        in_ref[...] = weight
        value = product(rows_ref[...], weight, 1, 0) + bias_ref[...]
        out_ref[...] = value.astype(jnp.bfloat16)

    @pl.when(step % 4 == 3)
    def _():
        chips, count, wide = rest_ref.shape
        pairs = weight.reshape(chips, 2, count, wide // 2)
        rest_ref[...] = jnp.concatenate([pairs[:, 0], pairs[:, 1]], axis=2)


def project(facts, rows, bias, parts, wait=()):
    count, width = rows.shape
    wide = parts[0].shape[2] // 4

    def column(i, f):
        return half_at(i, f, 4) * 3 + jnp.minimum(i % 4, 2)

    out = block((count, wide), 0, column)
    rest = (8, parts[0].shape[1] // 2, 2 * wide)
    return call(
        project_kernel,
        "project",
        (8,),
        [whole(rows), block((1, wide), 0, column)] + square_columns(parts, wide, 4),
        [out, block((width, wide), 0, column), block(rest, 0, 0, lambda i, f: half_at(i, f, 4))],
        [
            like((count, 6 * wide), jnp.bfloat16),
            like((width, 6 * wide), jnp.bfloat16),
            like(rest[:2] + (4 * wide,), jnp.bfloat16),
        ],
        facts,
        rows,
        bias[None],
        *parts,
        wait=wait,
    )


def valid_rows(facts_ref, count, slots):
    place = lax.broadcasted_iota(jnp.int32, (count, 1), 0) + pl.program_id(0) * count + facts_ref[2]
    place = jnp.where(place >= slots, place - slots, place)
    return (place < facts_ref[0]).astype(jnp.float32)


def add_rows(sums_ref, rows):
    total = jnp.concatenate([jnp.sum(part, axis=0, keepdims=True) for part in rows], axis=0)
    total = jnp.concatenate([total, jnp.zeros((8 - len(rows), total.shape[1]), jnp.float32)], axis=0)

    @pl.when(pl.program_id(0) == 0)
    def _():
        sums_ref[...] = total

    @pl.when(pl.program_id(0) > 0)
    def _():
        sums_ref[...] += total


def mean_of(values):
    return jnp.mean(values, axis=-1, keepdims=True)


def attend_out_kernel(
    slots, facts_ref, own_ref, other_ref, own_weight_ref, other_weight_ref, tokens_ref, vectors_ref,
    hat_ref, rstd_ref, low_ref, sums_ref,
):
    branch = (
        product(own_ref[...], own_weight_ref[...], 1, 0)
        + product(other_ref[...], other_weight_ref[...], 1, 0)
        + vectors_ref[0:1]
    )
    tokens = tokens_ref[...].astype(jnp.float32)
    total = tokens + branch
    centered = total - mean_of(total)
    rstd = lax.rsqrt(mean_of(centered * centered) + 1e-05)
    hat = centered * rstd
    hat_ref[...] = hat
    rstd_ref[...] = rstd
    low_ref[...] = (hat * vectors_ref[1:2] + vectors_ref[2:3]).astype(jnp.bfloat16)
    valid = valid_rows(facts_ref, tokens.shape[0], slots)
    add_rows(sums_ref, [valid * tokens * tokens, valid * branch * branch])


def attend_out(facts, own, other, own_weight, other_weight, tokens, vectors, wait=()):
    slots, width = tokens.shape
    step = slots // 4
    rows = lambda array: block((step, array.shape[1]), first, 0)
    return call(
        partial(attend_out_kernel, slots),
        "attend_out",
        (4,),
        [rows(own), rows(other), whole(own_weight), whole(other_weight), rows(tokens), whole(vectors)],
        [block((step, width), first, 0), block((step, 1), first, 0), block((step, width), first, 0), block((8, width), 0, 0)],
        [
            like((slots, width), jnp.float32),
            like((slots, 1), jnp.float32),
            like((slots, width), jnp.bfloat16),
            like((8, width), jnp.float32),
        ],
        facts,
        own,
        other,
        own_weight,
        other_weight,
        tokens,
        vectors,
        wait=wait,
    )


def up_kernel(facts_ref, rows_ref, bias_ref, *refs):
    parts, (act_ref, slope_ref, turned_ref, weight_ref) = refs[:4], refs[4:]
    weight = near_or_far(facts_ref, parts, pl.program_id(0) < 4)
    weight_ref[...] = weight
    pre_act = product(rows_ref[...], weight, 1, 0) + bias_ref[...]
    below = 0.5 + 0.5 * lax.erf(pre_act * 0.7071067811865476)
    act = (pre_act * below).astype(jnp.bfloat16)
    act_ref[...] = act
    turned_ref[...] = act.T
    slope = below + pre_act * (0.3989422804014327 * jnp.exp(-0.5 * pre_act * pre_act))
    slope_ref[...] = slope.astype(jnp.bfloat16)


def feed_up(facts, rows, bias, parts, wait=()):
    count, width = rows.shape
    units = bias.shape[0]
    wide = units // 8

    def column(i, f):
        return half_at(i, f, 4) * 4 + i % 4

    shape = like((count, units), jnp.bfloat16)
    out = block((count, wide), 0, column)
    return call(
        up_kernel,
        "feed_up",
        (8,),
        [whole(rows), block((1, wide), 0, column)] + square_columns(parts, wide, 4),
        [out, out, block((wide, count), column, 0), block((width, wide), 0, column)],
        [
            shape,
            shape,
            like((units, count), jnp.bfloat16),
            like((width, units), jnp.bfloat16),
        ],
        facts,
        rows,
        bias[None],
        *parts,
        wait=wait,
    )


def down_kernel(facts_ref, rows_ref, *refs):
    parts, (weight_ref, out_ref, total_ref) = refs[:4], refs[4:]
    step = pl.program_id(0)
    own, beside, below, across = [ref[0] for ref in parts]
    even, left = facts_ref[4] == 0, facts_ref[3] == 0
    for x in range(2):
        mine = jnp.where(even, own, beside) if x == 0 else jnp.where(even, beside, own)
        theirs = jnp.where(even, below, across) if x == 0 else jnp.where(even, across, below)
        weight_ref[x] = jnp.concatenate(
            [jnp.where(left, mine, theirs), jnp.where(left, theirs, mine)], axis=1
        )
    weight = weight_ref[...].reshape(rows_ref.shape[1], out_ref.shape[1])
    value = product(rows_ref[...], weight, 1, 0)

    @pl.when(step == 0)
    def _():
        total_ref[...] = value

    @pl.when(step > 0)
    def _():
        total_ref[...] += value

    @pl.when(step == 3)
    def _():
        out_ref[...] = total_ref[...].astype(jnp.bfloat16)


def feed_down(facts, rows, parts, wait=()):
    count, units = rows.shape
    _, block_rows, half_width = parts[0].shape
    width = 2 * half_width
    shape = (1,) + parts[0].shape[1:]
    return call(
        down_kernel,
        "feed_down",
        (4,),
        [block((count // 2, units // 4), 1, first)] + [block(shape, first, 0, 0)] * 4,
        [block((2, block_rows, width), first, 0, 0), block((count // 2, width), 0, 0)],
        [like((8, block_rows, width), jnp.bfloat16), like((count // 2, width), jnp.bfloat16)],
        facts,
        rows,
        *parts,
        scratch=[pltpu.VMEM((count // 2, width), jnp.float32)],
        wait=wait,
    )


def second_norm_kernel(
    slots, facts_ref, part_ref, other_ref, hat_ref, cotangent_ref, vectors_ref,
    mixed_ref, grad_ref, low_ref, sums_ref,
):
    branch = part_ref[...] + other_ref[...].astype(jnp.float32) + vectors_ref[0:1]
    hidden = hat_ref[...] * vectors_ref[1:2] + vectors_ref[2:3]
    gain = vectors_ref[3:4]
    total = hidden + branch
    centered = total - mean_of(total)
    rstd = lax.rsqrt(mean_of(centered * centered) + 1e-05)
    hat = centered * rstd
    mixed_ref[...] = (hat * gain + vectors_ref[4:5]).astype(jnp.bfloat16)
    valid = valid_rows(facts_ref, branch.shape[0], slots)
    grad = cotangent_ref[...].astype(jnp.float32) * valid
    scaled = grad * gain
    result = rstd * (scaled - mean_of(scaled) - hat * mean_of(scaled * hat))
    low = result.astype(jnp.bfloat16)
    grad_ref[...] = result
    low_ref[...] = low
    add_rows(sums_ref, [low.astype(jnp.float32), grad * hat, grad, valid * branch * branch])


def second_norm(facts, part, other, hat, cotangent, vectors, wait=()):
    slots, width = part.shape
    step = slots // 4
    rows = block((step, width), first, 0)
    return call(
        partial(second_norm_kernel, slots),
        "second_norm",
        (4,),
        [rows, rows, rows, rows, whole(vectors)],
        [rows, rows, rows, block((8, width), 0, 0)],
        [
            like((slots, width), jnp.bfloat16),
            like((slots, width), jnp.float32),
            like((slots, width), jnp.bfloat16),
            like((8, width), jnp.float32),
        ],
        facts,
        part,
        other,
        hat,
        cotangent,
        vectors,
        wait=wait,
    )


def first_norm_kernel(
    facts_ref, part_ref, other_ref, second_ref, hat_ref, rstd_ref, vectors_ref,
    grad_ref, low_ref, sums_ref,
):
    grad = part_ref[...] + other_ref[...].astype(jnp.float32) + second_ref[...]
    hat = hat_ref[...]
    scaled = grad * vectors_ref[1:2]
    result = rstd_ref[...] * (scaled - mean_of(scaled) - hat * mean_of(scaled * hat))
    low = result.astype(jnp.bfloat16)
    grad_ref[...] = result
    low_ref[...] = low
    add_rows(sums_ref, [low.astype(jnp.float32), grad * hat, grad])


def first_norm(facts, part, other, second, hat, rstd, vectors, wait=()):
    slots, width = part.shape
    step = slots // 4
    rows = block((step, width), first, 0)
    return call(
        first_norm_kernel,
        "first_norm",
        (4,),
        [rows, rows, rows, rows, block((step, 1), first, 0), whole(vectors)],
        [rows, rows, block((8, width), 0, 0)],
        [
            like((slots, width), jnp.float32),
            like((slots, width), jnp.bfloat16),
            like((8, width), jnp.float32),
        ],
        facts,
        part,
        other,
        second,
        hat,
        rstd,
        vectors,
        wait=wait,
    )


def act_grad_kernel(facts_ref, rows_ref, weight_ref, slope_ref, out_ref, sums_ref):
    total = product(rows_ref[...], weight_ref[...], 1, 1)
    grad = total.astype(jnp.bfloat16).astype(jnp.float32) * slope_ref[...].astype(jnp.float32)
    low = grad.astype(jnp.bfloat16)
    out_ref[...] = low
    sums_ref[...] = jnp.sum(low.astype(jnp.float32), axis=0, keepdims=True)


def act_grad(facts, rows, weight, slope, wait=()):
    count, units = slope.shape
    step = units // 8
    out = block((count, step), 0, first)
    return call(
        act_grad_kernel,
        "act_grad",
        (8,),
        [whole(rows), block((step, rows.shape[1]), first, 0), out],
        [out, block((1, step), 0, first)],
        [like((count, units), jnp.bfloat16), like((1, units), jnp.float32)],
        facts,
        rows,
        weight,
        slope,
        wait=wait,
    )


def tokens_grad_kernel(facts_ref, mine_ref, theirs_ref, weight_ref, out_ref, sent_ref):
    wide = mine_ref.shape[1]
    slots = out_ref.shape[0]
    half = facts_ref[3]
    mine = weight_ref[:, pl.ds(pl.multiple_of(half * wide, 128), wide)]
    theirs = weight_ref[:, pl.ds(pl.multiple_of((1 - half) * wide, 128), wide)]
    total = product(mine_ref[...], mine, 1, 1) + product(theirs_ref[...], theirs, 1, 1)
    out_ref[...] = total[:slots]
    sent_ref[...] = total[slots:].astype(sent_ref.dtype)


def tokens_grad(facts, mine, theirs, weight, wait=(), through=()):
    count, columns = mine.shape
    width = weight.shape[0]
    step = width // 4
    out = block((count // 2, step), 0, first)
    return call(
        tokens_grad_kernel,
        "tokens_grad",
        (4,),
        [whole(mine), whole(theirs), block((step, 2 * columns), first, 0)],
        [out, out],
        [
            like((count // 2, width), jnp.float32),
            like((count // 2, width), jnp.bfloat16),
        ],
        facts,
        mine,
        theirs,
        weight,
        wait=wait,
        through=through,
    )


def last_sum_kernel(facts_ref, left_ref, right_ref, one_ref, two_ref, out_ref):
    total = product(left_ref[...], right_ref[...], 1, 0)
    total = total + one_ref[...].astype(jnp.float32) + two_ref[...].astype(jnp.float32)
    out_ref[...] = total.astype(jnp.bfloat16)


def last_sum(facts, left_t, right, one, two, wait=(), through=()):
    rows, count = left_t.shape
    columns = right.shape[1]
    part = block((rows // 2, columns), first, 0)
    return call(
        last_sum_kernel,
        "last_sum",
        (2,),
        [block((rows // 2, count), first, 0), whole(right), part, part],
        part,
        like((rows, columns), jnp.bfloat16),
        facts,
        left_t,
        right,
        one,
        two,
        wait=wait,
        through=through,
    )


def split_body(
    tokens,
    lengths,
    cotangent,
    query_weight,
    key_weight,
    value_weight,
    out_weight,
    up_weight,
    down_weight,
    query_bias,
    value_bias,
    out_bias,
    attn_gain,
    attn_shift,
    up_bias,
    down_bias,
    feed_gain,
    feed_shift,
):
    core = lax.axis_index("c")
    half = lax.axis_index("s")
    row_count, width = tokens.shape[1:]
    slots = 2 * row_count
    unit_block = down_weight.shape[0]
    units = up_bias.shape[0] // 2
    cols = width // 2
    wide = cols // 2

    def to_sequence(values):
        return jnp.concatenate([pick(values, half, 0), swap(pick(values, 1 - half, 0), "s")], axis=0)

    def from_sequence(values):
        return in_order(values[:row_count], swap(values[row_count:], "s"), half)

    small = [
        split_columns(weight, HD, core) for weight in (query_weight, key_weight, value_weight)
    ]
    large = split_columns(up_weight, unit_block, core)
    up_pair = in_order(large[0], swap(large[1], "c"), core)
    up_cols = up_pair.shape[2]
    up_mine = up_pair.reshape(-1, up_cols)
    rows = up_mine.shape[0]
    near_kept = jnp.concatenate([part[0] for part in small], axis=1)
    near_sent = jnp.concatenate([part[1] for part in small], axis=1)
    near_pair = in_order(near_kept, swap(near_sent, "c"), core)
    out_pair = jnp.concatenate([out_weight[:, :wide], out_weight[:, wide:]], axis=0)
    near_mine = jnp.concatenate([near_pair.reshape(rows, -1), out_pair], axis=1)
    line = lax.axis_index("z")
    length_own = lax.dynamic_slice_in_dim(lengths, half, 1, 0)
    facts = jnp.concatenate(
        [
            both(length_own, "c"),
            jnp.stack(
                [
                    half * row_count,
                    half,
                    lax.axis_index("x"),
                    jnp.int32(0),
                    line // 2,
                    line % 2,
                ]
            ).astype(jnp.int32),
        ]
    )
    tokens_own = to_sequence(tokens)
    cotangent_own = to_sequence(cotangent)
    near, facts = stack_pair(facts, near_mine, line_cross(near_mine), wait=(tokens_own,))
    near, facts = stack_line(facts, near, line_next(near), wait=(cotangent_own,))
    near_parts = gather_square(near, "x")
    up_pairs, facts = stack_pair(facts, up_mine, line_cross(up_mine), wait=(near[0],))
    down_pairs, facts = stack_pair(facts, down_weight, line_cross(down_weight), wait=(up_pairs,))
    tokens_both = both(tokens_own, "c")
    up_part, facts = stack_line(
        facts, up_pairs, line_next(up_pairs), wait=(near_parts[1], near_parts[2], down_pairs)
    )
    up_parts = gather_square(up_part, "s")
    down_part, facts = stack_line(
        facts, down_pairs, line_next(down_pairs), wait=(near_parts[3], up_part)
    )
    down_parts = gather_square(down_part, "x")
    def halves_of(vector, size):
        return pick(vector.reshape(-1, 2, size), core, 1).reshape(-1)

    query_part = halves_of(query_bias, HD).reshape(2, wide)
    value_part = halves_of(value_bias, HD).reshape(2, wide)
    in_bias = jnp.stack([query_part, jnp.zeros_like(query_part), value_part], axis=1).reshape(-1)
    (projected, in_weight, out_own), facts = project(
        facts, tokens_both, in_bias, near_parts, wait=(up_part, down_part)
    )
    out_own = out_own.reshape(cols, width)
    out_other = swap(out_own, "c")
    (heads_out, totals), facts = attend(facts, projected, slots, wait=(up_parts[2],))
    heads_other = swap(heads_out[slots:], "c")
    vectors = jnp.stack(
        [out_bias, attn_gain, attn_shift, down_bias, feed_gain, feed_shift, out_bias, out_bias]
    )
    (first_hat, first_rstd, hidden_low, first_sums), facts = attend_out(
        facts,
        heads_out,
        heads_other,
        out_own,
        out_other,
        tokens_own,
        vectors,
        wait=(up_parts[1], down_parts[2]),
    )
    hidden_both = both(hidden_low, "c")
    (activation, slope, act_t, up_all), facts = feed_up(
        facts, hidden_both, halves_of(up_bias, unit_block), up_parts, wait=(down_parts[1],)
    )
    hidden_turned, facts = turn(facts, hidden_both, rows, wait=(act_t,))
    (down_all, feed_sent), facts = feed_down(facts, activation, down_parts)
    down_all = down_all.reshape(units, width)
    feed_other = swap(feed_sent, "c")
    feed_part = product(activation[:slots], down_all, 1, 0)
    feed_vectors = jnp.stack(
        [down_bias, attn_gain, attn_shift, feed_gain, feed_shift, out_bias, out_bias, out_bias]
    )
    (mixed, second_grad, feed_low, second_sums), facts = second_norm(
        facts, feed_part, feed_other, first_hat, cotangent_own, feed_vectors
    )
    mixed_other = swap(mixed[row_count:], "s")

    feed_both = both(feed_low, "c")
    tokens_turned, facts = turn(facts, tokens_both, rows, wait=(feed_low,))
    feed_mine, feed_theirs = columns_of(feed_both, half), columns_of(feed_both, 1 - half)
    down_sent = grad_block(act_t, feed_theirs)
    down_got = swap(down_sent, "s")
    (pre_grad, up_bias_grad), facts = act_grad(
        facts, feed_both, down_all, slope, wait=(down_sent,)
    )
    hidden_sent = product(pre_grad[slots:], up_all, 1, 1).astype(jnp.bfloat16)
    hidden_other = swap(hidden_sent, "c")
    hidden_own_t, hidden_other_t = hidden_turned
    up_sent = grad_block(hidden_other_t, pre_grad)
    up_got = swap(up_sent, "x")
    hidden_part = product(pre_grad[:slots], up_all, 1, 1)
    (first_grad, attn_low, third_sums), facts = first_norm(
        facts,
        hidden_part,
        hidden_other,
        second_grad,
        first_hat,
        first_rstd,
        vectors,
        wait=(up_sent,),
    )
    grad_sent = product(attn_low, out_other, 1, 1).astype(jnp.bfloat16)
    grad_other = swap(grad_sent, "c")
    grad_own = product(attn_low, out_own, 1, 1).astype(jnp.bfloat16)
    out_sent = product(heads_other, attn_low, 0, 0).astype(jnp.bfloat16)
    out_got = swap(out_sent, "c")
    heads_grad = jnp.concatenate([grad_own, grad_other], axis=0)
    (theirs_low, theirs_sums), facts = attend_back(
        facts, projected, heads_grad, totals, slots, False, wait=(out_sent,)
    )
    tokens_own_t, tokens_other_t = tokens_turned
    across_sent = grad_block(tokens_other_t, theirs_low)
    across_got = swap(across_sent, "x")
    out_grad = grad_block(heads_out[:slots].T, attn_low, out_got)
    out_line = out_grad.reshape((4, 2 * out_weight.shape[0], width))
    out_kept, out_sent = line_parts(out_line)
    out_got = lax.ppermute(out_sent, "z", NEXT)
    (mine_low, mine_sums), facts = attend_back(
        facts, projected, heads_grad, totals, slots, True, wait=(across_sent, out_sent)
    )
    down_total = grad_block(act_t, feed_mine, down_got)
    down_kept, down_sent = halve(down_total.reshape(4, 2, unit_block, cols), "x", 1)
    down_got = swap(down_sent, "x")
    up_total = grad_block(hidden_own_t, pre_grad, up_got).reshape(4, rows, 2 * up_cols)
    up_kept, up_sent = columns_of(up_total, half), columns_of(up_total, 1 - half)
    up_got = swap(up_sent, "s")
    beside_sent = grad_block(tokens_other_t, mine_low)
    beside_got = swap(beside_sent, "x")
    below_sent = grad_block(tokens_own_t, theirs_low, across_got)
    below_got = swap(below_sent, "s")
    out_total = add(out_kept, out_got)
    upper = lax.axis_index("z") // 2
    out_kept, out_sent = pick(out_total, upper, 0), pick(out_total, 1 - upper, 0)
    out_got = lax.ppermute(out_sent, "z", CROSS)
    valid_count = length_own[0].astype(jnp.float32) * width
    stats = jnp.stack(
        [jnp.sum(first_sums[0]), jnp.sum(first_sums[1]), jnp.sum(second_sums[3]), valid_count]
    )
    mine_sums, theirs_sums = jnp.sum(mine_sums, axis=(0, 1)), jnp.sum(theirs_sums, axis=(0, 1))
    late = in_order(mine_sums, theirs_sums, half)
    sums = jnp.concatenate(
        [
            second_sums[:3].reshape(-1),
            third_sums[:3].reshape(-1),
            jnp.pad(stats, (0, 124)),
            up_bias_grad[0],
            late[:, :wide].reshape(-1),
            late[:, 2 * wide :].reshape(-1),
        ]
    )
    sums_got = lax.ppermute(sums, "z", NEXT)
    (tokens_part, tokens_sent), facts = tokens_grad(
        facts,
        mine_low,
        theirs_low,
        in_weight,
        wait=(beside_sent, below_sent, down_sent, up_sent, out_sent, sums),
    )
    tokens_other = swap(tokens_sent, "c")
    (in_total, sums, out_kept), facts = last_sum(
        facts,
        tokens_own_t,
        mine_low,
        beside_got,
        below_got,
        wait=(up_got, down_got, tokens_part),
        through=(sums + sums_got, add(out_kept, out_got)),
    )
    in_sum = fold_line(in_total.reshape(4, rows, 3 * wide))
    tokens_grad_sum = tokens_part + tokens_other.astype(jnp.float32) + first_grad
    tokens_grad_sum = from_sequence(tokens_grad_sum.astype(jnp.bfloat16))
    mixed = in_order(mixed[:row_count], mixed_other, half)
    down_sum = fold_line(add(down_kept, down_got))
    up_sum = fold_line(add(up_kept, up_got))
    out_sum = fold_columns(fold(out_kept.reshape(2, out_weight.shape[0], width), "x", 0))

    sums = sums + lax.ppermute(sums, "z", CROSS)
    sums = sums + swap(sums, "s")
    sums = sums + swap(sums, "x")
    both_sums = in_order(sums, swap(sums, "c"), core)
    count = 6 * width + 128
    shared = both_sums[0, :count] + both_sums[1, :count]
    down_bias_grad, feed_gain_grad, feed_shift_grad, out_bias_grad, attn_gain_grad, attn_shift_grad = [
        shared[i * width : (i + 1) * width] for i in range(6)
    ]
    stats = shared[6 * width : 6 * width + 4]

    def interleave(start, size, block_size):
        sums = both_sums[:, start : start + size].reshape(2, -1, block_size)
        return sums.transpose(1, 0, 2).reshape(-1)

    up_bias_grad = interleave(count, units, unit_block)
    query_bias_grad = interleave(count + units, cols, HD)
    value_bias_gradient = interleave(count + units + cols, cols, HD)
    stream_rms = jnp.sqrt(stats[:3] / stats[3])

    def give_back(total):
        total = total.reshape((2, rows // 2) + total.shape[1:])
        return pick(total, core, 0), swap(pick(total, 1 - core, 0), "c")

    up_shares = give_back(up_sum)
    in_shares = give_back(in_sum)
    down_weight_grad = down_sum.astype(jnp.float32)
    out_weight_grad = out_sum.astype(jnp.float32)

    def merge(shares, start, size, block):
        one, two = [
            share[:, start : start + size].reshape(rows // 2, -1, block) for share in shares
        ]
        first = jnp.where(core == 0, one, two)
        second = jnp.where(core == 0, two, one)
        return jnp.stack([first, second], axis=2).reshape(rows // 2, -1).astype(jnp.float32)

    query_weight_grad = merge(in_shares, 0, wide, HD)
    key_weight_grad = merge(in_shares, wide, wide, HD)
    value_weight_grad = merge(in_shares, 2 * wide, wide, HD)
    up_weight_grad = merge(up_shares, 0, up_cols, unit_block)
    return (
        mixed,
        tokens_grad_sum,
        query_weight_grad,
        key_weight_grad,
        value_weight_grad,
        out_weight_grad,
        up_weight_grad,
        down_weight_grad,
        query_bias_grad,
        value_bias_gradient,
        out_bias_grad,
        attn_gain_grad,
        attn_shift_grad,
        up_bias_grad,
        down_bias_grad,
        feed_gain_grad,
        feed_shift_grad,
        stream_rms,
    )


def solution(mesh):
    devices = mesh.devices
    dp_count, seq_count = devices.shape
    split = seq_count == 2 and dp_count == 16
    if split:
        inner = jax.sharding.Mesh(devices.reshape(4, 2, 2, seq_count), ("z", "x", "c", "s"))
        dp, seq, body = ("z", "x", "c"), "s", split_body
    else:
        inner, dp, seq, body = mesh, "dp", "seq", general_body
    weights = (P(dp, seq),) * 6
    vectors = (P(),) * 9
    rows = P(dp, seq, None)
    in_specs = (rows, P(dp), rows) + weights + vectors
    out_specs = (rows, rows) + weights + vectors + (P(),)
    return jax.shard_map(body, mesh=inner, in_specs=in_specs, out_specs=out_specs, check_vma=False)
```

```python
from functools import partial
import math

import jax
import jax.numpy as jnp
from jax import lax
from jax.experimental import pallas as pl
from jax.experimental.pallas import tpu as pltpu
from jax.sharding import PartitionSpec as P

HD = 64


def layer_norm(values_in, gain_vector, shift_vector):
    mean_value = jnp.mean(values_in, axis=-1, keepdims=True)
    centered = values_in - mean_value
    variance = jnp.mean(centered * centered, axis=-1, keepdims=True)
    return centered * lax.rsqrt(variance + 1e-05) * gain_vector + shift_vector


def gather_weights(first, second, third, fourth, fifth, sixth):
    part = (
        lax.all_gather(first, "dp", axis=0, tiled=True),
        lax.all_gather(second, "dp", axis=0, tiled=True),
        lax.all_gather(third, "dp", axis=0, tiled=True),
        lax.all_gather(fourth, "dp", axis=0, tiled=True),
        lax.all_gather(fifth, "dp", axis=0, tiled=True),
        lax.all_gather(sixth, "dp", axis=0, tiled=True),
    )
    return (
        lax.all_gather(part[0], "seq", axis=1, tiled=True),
        lax.all_gather(part[1], "seq", axis=1, tiled=True),
        lax.all_gather(part[2], "seq", axis=1, tiled=True),
        lax.all_gather(part[3], "seq", axis=1, tiled=True),
        lax.all_gather(part[4], "seq", axis=1, tiled=True),
        lax.all_gather(part[5], "seq", axis=1, tiled=True),
    )


def reduce_grads(first, second, third, fourth, fifth, sixth):
    part = (
        lax.psum_scatter(first.astype(jnp.bfloat16), "seq", scatter_dimension=1, tiled=True).astype(
            jnp.float32
        ),
        lax.psum_scatter(
            second.astype(jnp.bfloat16), "seq", scatter_dimension=1, tiled=True
        ).astype(jnp.float32),
        lax.psum_scatter(third.astype(jnp.bfloat16), "seq", scatter_dimension=1, tiled=True).astype(
            jnp.float32
        ),
        lax.psum_scatter(
            fourth.astype(jnp.bfloat16), "seq", scatter_dimension=1, tiled=True
        ).astype(jnp.float32),
        lax.psum_scatter(fifth.astype(jnp.bfloat16), "seq", scatter_dimension=1, tiled=True).astype(
            jnp.float32
        ),
        lax.psum_scatter(sixth.astype(jnp.bfloat16), "seq", scatter_dimension=1, tiled=True).astype(
            jnp.float32
        ),
    )
    return (
        lax.psum_scatter(
            part[0].astype(jnp.bfloat16), "dp", scatter_dimension=0, tiled=True
        ).astype(jnp.float32),
        lax.psum_scatter(
            part[1].astype(jnp.bfloat16), "dp", scatter_dimension=0, tiled=True
        ).astype(jnp.float32),
        lax.psum_scatter(
            part[2].astype(jnp.bfloat16), "dp", scatter_dimension=0, tiled=True
        ).astype(jnp.float32),
        lax.psum_scatter(
            part[3].astype(jnp.bfloat16), "dp", scatter_dimension=0, tiled=True
        ).astype(jnp.float32),
        lax.psum_scatter(
            part[4].astype(jnp.bfloat16), "dp", scatter_dimension=0, tiled=True
        ).astype(jnp.float32),
        lax.psum_scatter(
            part[5].astype(jnp.bfloat16), "dp", scatter_dimension=0, tiled=True
        ).astype(jnp.float32),
    )


def block_layout(seq_count, row_count, head_count):
    block_seqs = math.gcd(seq_count, max(1, 512 // row_count))
    group_heads = math.gcd(head_count, 4)
    return (block_seqs, seq_count // block_seqs, group_heads, head_count // group_heads)


def head_slice(block_part, offset, group_width, group_heads):
    sliced = lax.dynamic_slice_in_dim(block_part, offset, group_width, 2)
    return sliced.reshape(sliced.shape[0], sliced.shape[1], group_heads, HD)


def attention_forward(queries, key_all, value_all, key_mask):
    seq_count, row_count, feature_total = queries.shape
    slot_count = key_all.shape[1]
    block_seqs, block_count, group_heads, group_count = block_layout(
        seq_count, row_count, feature_total // HD
    )
    group_width = group_heads * HD

    def seq_block(inputs):
        query_part, key_part, value_part, mask_part = inputs

        def head_block(group_index):
            offset = group_index * group_width
            query_heads = head_slice(query_part, offset, group_width, group_heads)
            key_heads = head_slice(key_part, offset, group_width, group_heads)
            value_heads = head_slice(value_part, offset, group_width, group_heads)
            scores = (
                jnp.einsum(
                    "brhd,bkhd->bhrk", query_heads, key_heads, preferred_element_type=jnp.float32
                )
                * 0.125
            )
            scores = jnp.where(mask_part[:, None, None, :], scores, -1e30)
            row_max = jnp.max(scores, axis=-1, keepdims=True)
            exponent = jnp.exp(scores - row_max)
            row_total = jnp.sum(exponent, axis=-1, keepdims=True)
            soft_probs = (exponent / row_total).astype(jnp.bfloat16)
            heads_out = jnp.einsum(
                "bhrk,bkhd->brhd", soft_probs, value_heads, preferred_element_type=jnp.float32
            )
            log_total = (row_max + jnp.log(row_total))[..., 0]
            return (heads_out.reshape(block_seqs, row_count, group_width), log_total)

        return lax.map(head_block, jnp.arange(group_count))

    outputs, log_totals = lax.map(
        seq_block,
        (
            queries.reshape(block_count, block_seqs, row_count, feature_total),
            key_all.reshape(block_count, block_seqs, slot_count, feature_total),
            value_all.reshape(block_count, block_seqs, slot_count, feature_total),
            key_mask.reshape(block_count, block_seqs, slot_count),
        ),
    )
    mixed_heads = outputs.transpose(0, 2, 3, 1, 4).reshape(seq_count, row_count, feature_total)
    return (mixed_heads, log_totals)


def attention_backward(queries, key_all, value_all, key_mask, heads_grad, log_totals):
    seq_count, row_count, feature_total = queries.shape
    slot_count = key_all.shape[1]
    block_seqs, block_count, group_heads, group_count = block_layout(
        seq_count, row_count, feature_total // HD
    )
    group_width = group_heads * HD

    def seq_block(inputs):
        query_part, key_part, value_part, mask_part, grad_part, total_part = inputs

        def head_block(group_index):
            offset = group_index * group_width
            query_heads = head_slice(query_part, offset, group_width, group_heads)
            key_heads = head_slice(key_part, offset, group_width, group_heads)
            value_heads = head_slice(value_part, offset, group_width, group_heads)
            grad_heads = head_slice(grad_part, offset, group_width, group_heads)
            log_total = lax.dynamic_index_in_dim(total_part, group_index, 0, keepdims=False)
            scores = (
                jnp.einsum(
                    "brhd,bkhd->bhrk", query_heads, key_heads, preferred_element_type=jnp.float32
                )
                * 0.125
            )
            scores = jnp.where(mask_part[:, None, None, :], scores, -1e30)
            soft_probs = jnp.exp(scores - log_total[..., None])
            value_grad = jnp.einsum(
                "bhrk,brhd->bkhd",
                soft_probs.astype(jnp.bfloat16),
                grad_heads,
                preferred_element_type=jnp.float32,
            )
            prob_grad = jnp.einsum(
                "brhd,bkhd->bhrk", grad_heads, value_heads, preferred_element_type=jnp.float32
            )
            inner = jnp.sum(soft_probs * prob_grad, axis=-1, keepdims=True)
            score_grad = (soft_probs * (prob_grad - inner)).astype(jnp.bfloat16)
            query_grad = (
                jnp.einsum(
                    "bhrk,bkhd->brhd", score_grad, key_heads, preferred_element_type=jnp.float32
                )
                * 0.125
            )
            key_grad = (
                jnp.einsum(
                    "bhrk,brhd->bkhd", score_grad, query_heads, preferred_element_type=jnp.float32
                )
                * 0.125
            )
            return (
                query_grad.reshape(block_seqs, row_count, group_width),
                key_grad.reshape(block_seqs, slot_count, group_width),
                value_grad.reshape(block_seqs, slot_count, group_width),
            )

        return lax.map(head_block, jnp.arange(group_count))

    query_blocks, key_blocks, value_block_list = lax.map(
        seq_block,
        (
            queries.reshape(block_count, block_seqs, row_count, feature_total),
            key_all.reshape(block_count, block_seqs, slot_count, feature_total),
            value_all.reshape(block_count, block_seqs, slot_count, feature_total),
            key_mask.reshape(block_count, block_seqs, slot_count),
            heads_grad.reshape(block_count, block_seqs, row_count, feature_total),
            log_totals,
        ),
    )
    query_grad = query_blocks.transpose(0, 2, 3, 1, 4).reshape(seq_count, row_count, feature_total)
    key_grad = key_blocks.transpose(0, 2, 3, 1, 4).reshape(seq_count, slot_count, feature_total)
    value_grad = value_block_list.transpose(0, 2, 3, 1, 4).reshape(
        seq_count, slot_count, feature_total
    )
    return (query_grad, key_grad, value_grad)


def general_body(
    tokens,
    lengths,
    cotangent,
    query_weight,
    key_weight,
    value_weight,
    out_weight,
    up_weight,
    down_weight,
    query_bias,
    value_bias,
    out_bias,
    attn_gain,
    attn_shift,
    up_bias,
    down_bias,
    feed_gain,
    feed_shift,
):
    seq_count, row_count, feature_total = tokens.shape
    slot_count = row_count * lax.axis_size("seq")
    token_count = seq_count * row_count
    whole = gather_weights(
        query_weight, key_weight, value_weight, out_weight, up_weight, down_weight
    )
    full_query, full_key, full_value, full_out, full_up, full_down = whole
    flat_tokens = tokens.reshape(token_count, feature_total)
    queries = (
        jnp.dot(flat_tokens, full_query, preferred_element_type=jnp.float32) + query_bias
    ).astype(jnp.bfloat16)
    key_rows = jnp.dot(flat_tokens, full_key, preferred_element_type=jnp.float32).astype(
        jnp.bfloat16
    )
    value_rows = (
        jnp.dot(flat_tokens, full_value, preferred_element_type=jnp.float32) + value_bias
    ).astype(jnp.bfloat16)
    first_slot = lax.axis_index("seq") * row_count
    key_mask = jnp.arange(slot_count)[None, :] < lengths[:, None]
    row_valid = ((first_slot + jnp.arange(row_count))[None, :] < lengths[:, None]).astype(
        jnp.float32
    )
    row_valid = row_valid.reshape(token_count, 1)
    query_blocks = queries.reshape(seq_count, row_count, feature_total)
    key_blocks = key_rows.reshape(seq_count, row_count, feature_total)
    value_block_list = value_rows.reshape(seq_count, row_count, feature_total)
    key_all, value_all = (
        lax.all_gather(key_blocks, "seq", axis=1, tiled=True),
        lax.all_gather(value_block_list, "seq", axis=1, tiled=True),
    )
    mixed_heads, log_totals = attention_forward(query_blocks, key_all, value_all, key_mask)
    heads_low = mixed_heads.reshape(token_count, feature_total).astype(jnp.bfloat16)
    attention_out = jnp.dot(heads_low, full_out, preferred_element_type=jnp.float32) + out_bias
    tokens_f32 = flat_tokens.astype(jnp.float32)
    first_sum = tokens_f32 + attention_out
    hidden, first_pull = jax.vjp(layer_norm, first_sum, attn_gain, attn_shift)
    hidden_low = hidden.astype(jnp.bfloat16)
    pre_act = jnp.dot(hidden_low, full_up, preferred_element_type=jnp.float32) + up_bias
    gelu_out, gelu_pull = jax.vjp(partial(jax.nn.gelu, approximate=False), pre_act)
    activation = gelu_out.astype(jnp.bfloat16)
    feed_out = jnp.dot(activation, full_down, preferred_element_type=jnp.float32) + down_bias
    result, second_pull = jax.vjp(layer_norm, hidden + feed_out, feed_gain, feed_shift)
    mixed = result.astype(jnp.bfloat16).reshape(seq_count, row_count, feature_total)
    partial_stats = jnp.stack(
        [
            jnp.sum(row_valid * tokens_f32 * tokens_f32),
            jnp.sum(row_valid * attention_out * attention_out),
            jnp.sum(row_valid * feed_out * feed_out),
            jnp.sum(row_valid) * feature_total,
        ]
    )
    back_weights = gather_weights(
        query_weight, key_weight, value_weight, out_weight, up_weight, down_weight
    )
    back_query, back_key, back_value, back_out, back_up, back_down = back_weights
    out_grad = cotangent.reshape(token_count, feature_total).astype(jnp.float32) * row_valid
    second_grad, feed_gain_grad, feed_shift_grad = second_pull(out_grad)
    feed_low = second_grad.astype(jnp.bfloat16)
    down_weight_grad = jnp.einsum(
        "nf,nd->fd", activation, feed_low, preferred_element_type=jnp.float32
    )
    down_bias_grad = jnp.sum(feed_low, axis=0, dtype=jnp.float32)
    act_grad = jnp.einsum(
        "nd,fd->nf", feed_low, back_down, preferred_element_type=jnp.float32
    ).astype(jnp.bfloat16)
    pre_grad = gelu_pull(act_grad.astype(jnp.float32))[0].astype(jnp.bfloat16)
    up_weight_grad = jnp.einsum(
        "nd,nf->df", hidden_low, pre_grad, preferred_element_type=jnp.float32
    )
    up_bias_grad = jnp.sum(pre_grad, axis=0, dtype=jnp.float32)
    hidden_grad = (
        jnp.einsum("nf,df->nd", pre_grad, back_up, preferred_element_type=jnp.float32) + second_grad
    )
    first_grad, attn_gain_grad, attn_shift_grad = first_pull(hidden_grad)
    attn_low = first_grad.astype(jnp.bfloat16)
    out_weight_grad = jnp.einsum(
        "nd,ne->de", heads_low, attn_low, preferred_element_type=jnp.float32
    )
    out_bias_grad = jnp.sum(attn_low, axis=0, dtype=jnp.float32)
    heads_grad = jnp.einsum(
        "ne,de->nd", attn_low, back_out, preferred_element_type=jnp.float32
    ).astype(jnp.bfloat16)
    heads_grad = heads_grad.reshape(seq_count, row_count, feature_total)
    query_grad, key_part_grad, value_part_grad = attention_backward(
        query_blocks, key_all, value_all, key_mask, heads_grad, log_totals
    )
    key_sum, value_sum = (
        lax.psum_scatter(
            key_part_grad.astype(jnp.bfloat16), "seq", scatter_dimension=1, tiled=True
        ).astype(jnp.float32),
        lax.psum_scatter(
            value_part_grad.astype(jnp.bfloat16), "seq", scatter_dimension=1, tiled=True
        ).astype(jnp.float32),
    )
    query_low = query_grad.reshape(token_count, feature_total).astype(jnp.bfloat16)
    key_low = key_sum.reshape(token_count, feature_total).astype(jnp.bfloat16)
    value_low = value_sum.reshape(token_count, feature_total).astype(jnp.bfloat16)
    query_weight_grad = jnp.einsum(
        "nd,ne->de", flat_tokens, query_low, preferred_element_type=jnp.float32
    )
    key_weight_grad = jnp.einsum(
        "nd,ne->de", flat_tokens, key_low, preferred_element_type=jnp.float32
    )
    value_weight_grad = jnp.einsum(
        "nd,ne->de", flat_tokens, value_low, preferred_element_type=jnp.float32
    )
    query_bias_grad = jnp.sum(query_low, axis=0, dtype=jnp.float32)
    value_bias_gradient = jnp.sum(value_low, axis=0, dtype=jnp.float32)
    tokens_grad = (
        jnp.einsum("ne,de->nd", query_low, back_query, preferred_element_type=jnp.float32)
        + jnp.einsum("ne,de->nd", key_low, back_key, preferred_element_type=jnp.float32)
        + jnp.einsum("ne,de->nd", value_low, back_value, preferred_element_type=jnp.float32)
        + first_grad
    )
    tokens_grad = tokens_grad.astype(jnp.bfloat16).reshape(seq_count, row_count, feature_total)
    matrix_grads = reduce_grads(
        query_weight_grad,
        key_weight_grad,
        value_weight_grad,
        out_weight_grad,
        up_weight_grad,
        down_weight_grad,
    )
    totals = lax.psum(
        (
            partial_stats,
            query_bias_grad,
            value_bias_gradient,
            out_bias_grad,
            attn_gain_grad,
            attn_shift_grad,
            up_bias_grad,
            down_bias_grad,
            feed_gain_grad,
            feed_shift_grad,
        ),
        ("dp", "seq"),
    )
    stream_rms = jnp.sqrt(totals[0][:3] / totals[0][3])
    return (
        mixed,
        tokens_grad,
        matrix_grads[0],
        matrix_grads[1],
        matrix_grads[2],
        matrix_grads[3],
        matrix_grads[4],
        matrix_grads[5],
        totals[1],
        totals[2],
        totals[3],
        totals[4],
        totals[5],
        totals[6],
        totals[7],
        totals[8],
        totals[9],
        stream_rms,
    )


def swap(value, axis):
    return lax.ppermute(value, axis, [(0, 1), (1, 0)])


def both(value, axis):
    return jnp.concatenate([value, swap(value, axis)], axis=0)


def in_order(own, other, index, axis=0):
    return jnp.where(
        index == 0, jnp.stack([own, other], axis=axis), jnp.stack([other, own], axis=axis)
    )


def split_columns(weight, width, core):
    rows = weight.shape[0]
    blocks = weight.reshape(rows, -1, 2, width)
    return pick(blocks, core, 2).reshape(rows, -1), pick(blocks, 1 - core, 2).reshape(rows, -1)


def pick(values, index, axis):
    return lax.dynamic_index_in_dim(values, index, axis, keepdims=False)


def add(left, right):
    return (left.astype(jnp.float32) + right.astype(jnp.float32)).astype(jnp.bfloat16)


def fold(values, axis, dim):
    index = lax.axis_index(axis)
    return add(pick(values, index, dim), swap(pick(values, 1 - index, dim), axis))


NEXT = [(0, 1), (1, 0), (2, 3), (3, 2)]
CROSS = [(0, 2), (2, 0), (1, 3), (3, 1)]


def fold_cross(pairs):
    upper = lax.axis_index("z") // 2
    return add(pick(pairs, upper, 0), lax.ppermute(pick(pairs, 1 - upper, 0), "z", CROSS))


def fold_line(values):
    odd = lax.axis_index("z") % 2
    pairs = values.reshape((2, 2) + values.shape[1:])
    sent = lax.ppermute(pick(pairs, 1 - odd, 1), "z", NEXT)
    return fold_cross(add(pick(pairs, odd, 1), sent))


def line_cross(value):
    return lax.ppermute(value, "z", CROSS)


def line_next(pair):
    return lax.ppermute(pair, "z", NEXT)


def gather_square(own, way):
    beside, below = swap(own, "x"), swap(own, "s")
    across = swap(below, "x") if way == "x" else swap(beside, "s")
    return [own, beside, below, across]


def fold_columns(total):
    half = lax.axis_index("s")
    return add(columns_of(total, half), swap(columns_of(total, 1 - half), "s"))


def halve(values, axis, dim):
    index = lax.axis_index(axis) % 2
    return pick(values, index, dim), pick(values, 1 - index, dim)


def line_parts(values):
    return halve(values.reshape((2, 2) + values.shape[1:]), "z", 1)


def scatter_top(send, keep):
    total = add(keep, swap(send, "s"))
    total = total.reshape((4, 2) + total.shape[1:])
    return fold_line(fold(total, "x", 1))


def grad_block(left_t, right, got=None):
    total = product(left_t, right, 1, 0)
    if got is not None:
        total = total + got.astype(jnp.float32)
    return total.astype(jnp.bfloat16)


def columns_of(right, index):
    columns = right.shape[-1] // 2
    return lax.dynamic_slice_in_dim(right, index * columns, columns, right.ndim - 1)


PAIR = 2 * HD
LIMIT = 56 * 1024 * 1024


def kernel_params(steps):
    return pltpu.CompilerParams(
        dimension_semantics=("arbitrary",) * steps, vmem_limit_bytes=LIMIT
    )


def product(left, right, left_dim, right_dim):
    return lax.dot_general(
        left, right, (((left_dim,), (right_dim,)), ((), ())), preferred_element_type=jnp.float32
    )


def key_bias(facts_ref, slots):
    place = lax.broadcasted_iota(jnp.int32, (slots, 1), 0) + facts_ref[2]
    place = jnp.where(place >= slots, place - slots, place)
    return jnp.where(place < facts_ref[pl.program_id(0)], 0.0, -1e30)


def head_lanes(value, head):
    lane = lax.broadcasted_iota(jnp.int32, value.shape, 1)
    return jnp.where((lane >= HD) == (head == 1), value, jnp.zeros_like(value))


def turned(value):
    return value.astype(jnp.float32).T


def attend_kernel(facts_ref, query_ref, key_ref, value_ref, out_ref, total_ref):
    slots = key_ref.shape[0]
    bias = key_bias(facts_ref, slots)
    query = query_ref[...] * jnp.bfloat16(0.125)
    key = key_ref[...]
    value_t = turned(value_ref[...]).astype(jnp.bfloat16)
    outs = []
    for head in range(2):
        scores = product(key, head_lanes(query, head), 1, 1) + bias
        peak = jnp.max(scores, axis=0, keepdims=True)
        weight = jnp.exp(scores - peak)
        total = jnp.sum(weight, axis=0, keepdims=True)
        part = product(value_t[head * HD : (head + 1) * HD], weight.astype(jnp.bfloat16), 1, 0)
        outs.append(part * (1.0 / total))
        total_ref[0, 0, head : head + 1, :] = peak + jnp.log(total)
    out_ref[...] = jnp.concatenate(outs, axis=0).T.astype(jnp.bfloat16)


def attend_back_kernel(
    facts_ref, query_ref, key_ref, value_ref, grad_ref, total_ref, low_ref, sums_ref
):
    slots = key_ref.shape[0]
    bias = key_bias(facts_ref, slots)
    query = query_ref[...] * jnp.bfloat16(0.125)
    key = key_ref[...]
    value = value_ref[...]
    grad = grad_ref[...]
    key_t = turned(key).astype(jnp.bfloat16)
    lane = lax.broadcasted_iota(jnp.int32, (slots, PAIR), 1)
    query_parts, key_parts, value_parts = [], [], []
    for head in range(2):
        scores = product(key, head_lanes(query, head), 1, 1) + bias
        soft = jnp.exp(scores - total_ref[0, 0, head : head + 1, :])
        value_parts.append(product(soft.astype(jnp.bfloat16), grad, 1, 0))
        change = product(value, head_lanes(grad, head), 1, 1)
        inner = jnp.sum(soft * change, axis=0, keepdims=True)
        change = (soft * (change - inner)).astype(jnp.bfloat16)
        key_parts.append(product(change, query, 1, 0))
        query_parts.append(product(key_t[head * HD : (head + 1) * HD], change, 1, 0))
    pair = pl.program_id(1)
    groups = low_ref.shape[1] // 3
    query_low = (jnp.concatenate(query_parts, axis=0) * 0.125).T
    key_low = jnp.where(lane < HD, key_parts[0], key_parts[1])
    value_low = jnp.where(lane < HD, value_parts[0], value_parts[1])
    for place, part in enumerate((query_low, key_low, value_low)):
        start = pl.multiple_of(place * groups + pair * PAIR, PAIR)
        low = part.astype(jnp.bfloat16)
        low_ref[:, pl.ds(start, PAIR)] = low
        sums_ref[0, :, pl.ds(start, PAIR)] = jnp.sum(
            low.astype(jnp.float32), axis=0, keepdims=True
        )


def attention_specs(slots, pairs):
    def at(part):
        return pl.BlockSpec(
            (slots, PAIR), lambda b, g, p, *_: (b, g * 3 * pairs + part * pairs + p)
        )

    heads = pl.BlockSpec((slots, PAIR), lambda b, g, p, *_: (b, g * pairs + p))
    totals = pl.BlockSpec((1, 1, 2, slots), lambda b, g, p, *_: (b, g * pairs + p, 0, 0))
    return [at(0), at(1), at(2)], heads, totals


def attend(facts, projected, slots, wait=()):
    pairs = projected.shape[1] // (6 * PAIR)
    inputs, heads, totals = attention_specs(slots, pairs)
    rows = projected.shape[0]
    return call(
        attend_kernel,
        "attend",
        (2, 2, pairs),
        inputs,
        [heads, totals],
        [
            like((rows, 2 * pairs * PAIR), jnp.bfloat16),
            like((2, 2 * pairs, 2, slots), jnp.float32),
        ],
        facts,
        projected,
        projected,
        projected,
        wait=wait,
    )


def attend_back(facts, projected, heads_grad, totals_in, slots, own, wait=(), through=()):
    pairs = projected.shape[1] // (6 * PAIR)

    def group(facts_ref):
        return facts_ref[3] if own else 1 - facts_ref[3]

    def at(part):
        return pl.BlockSpec(
            (slots, PAIR), lambda b, p, f: (b, group(f) * 3 * pairs + part * pairs + p)
        )

    heads = pl.BlockSpec((slots, PAIR), lambda b, p, f: (b, group(f) * pairs + p))
    totals = pl.BlockSpec((1, 1, 2, slots), lambda b, p, f: (b, group(f) * pairs + p, 0, 0))
    width = 3 * pairs * PAIR
    return call(
        attend_back_kernel,
        "attend_back",
        (2, pairs),
        [at(0), at(1), at(2), heads, totals],
        [
            pl.BlockSpec((slots, width), lambda b, p, f: (b, 0)),
            pl.BlockSpec((1, 1, width), lambda b, p, f: (b, 0, 0)),
        ],
        [
            like((2 * slots, width), jnp.bfloat16),
            like((2, 1, width), jnp.float32),
        ],
        facts,
        projected,
        projected,
        projected,
        heads_grad,
        totals_in,
        wait=wait,
        through=through,
    )


def call(kernel, name, grid, inputs, outputs, shapes, facts, *args, wait=(), scratch=(), through=()):
    single = not isinstance(outputs, list)
    outputs, shapes = ([outputs], [shapes]) if single else (outputs, shapes)
    count, held, passed = len(args), len(wait) + len(through), len(through)
    last = count + held + len(outputs)

    def body(facts_ref, *refs):
        kernel(facts_ref, *refs[:count], *refs[count + held : last], *refs[last + passed + 1 :])
        for place in range(facts.shape[0]):
            refs[last + passed][place] = facts_ref[place]

    results = pl.pallas_call(
        body,
        grid_spec=pltpu.PrefetchScalarGridSpec(
            num_scalar_prefetch=1,
            grid=grid,
            in_specs=list(inputs) + [pl.BlockSpec(memory_space=pl.ANY)] * held,
            out_specs=list(outputs)
            + [pl.BlockSpec(memory_space=pl.ANY)] * passed
            + [pl.BlockSpec(memory_space=pltpu.SMEM)],
            scratch_shapes=list(scratch),
        ),
        out_shape=list(shapes)
        + [like(value.shape, value.dtype) for value in through]
        + [like(facts.shape, jnp.int32)],
        input_output_aliases={1 + count + len(wait) + i: len(outputs) + i for i in range(passed)},
        compiler_params=kernel_params(len(grid)),
        name=name,
    )(facts, *args, *wait, *through)
    values = tuple(results[:-1])
    return (values[0] if single and not passed else values), results[-1]


def block(shape, *index):
    def at(*grid_and_facts):
        return tuple(entry(*grid_and_facts) if callable(entry) else entry for entry in index)

    return pl.BlockSpec(shape, at)


def whole(array):
    zeros = (0,) * array.ndim
    return pl.BlockSpec(array.shape, lambda *_: zeros)


def first(i, *_):
    return i


def like(shape, dtype):
    return jax.ShapeDtypeStruct(shape, dtype)


def rows_in_order(facts_ref, own, beside):
    even = facts_ref[4] == 0
    pieces = []
    for z in range(4):
        pieces += [jnp.where(even, own[z], beside[z]), jnp.where(even, beside[z], own[z])]
    return jnp.concatenate(pieces, axis=0)


def near_or_far(facts_ref, refs, near):
    own, beside, below, across = [ref[...] for ref in refs]
    return rows_in_order(
        facts_ref, jnp.where(near, own, below), jnp.where(near, beside, across)
    )


def square_columns(parts, wide, steps):
    shape = parts[0].shape[:2] + (wide,)
    near = block(shape, 0, 0, lambda i, *_: jnp.minimum(i, steps - 1))
    far = block(shape, 0, 0, lambda i, *_: jnp.maximum(i - steps, 0))
    return [near, near, far, far]


def half_at(i, facts, steps):
    return jnp.where(i < steps, facts[3], 1 - facts[3])


def stack_kernel(own_at, facts_ref, own_ref, other_ref, out_ref):
    own = facts_ref[own_at] == pl.program_id(0)
    value = jnp.where(own, own_ref[...], other_ref[...])
    out_ref[...] = value.reshape(out_ref.shape)


def stack_pair(facts, own, other, wait=(), through=()):
    rows, columns = own.shape
    return call(
        partial(stack_kernel, 6),
        "stack",
        (2,),
        [whole(own), whole(other)],
        block((1, rows, columns), first, 0, 0),
        like((2, rows, columns), own.dtype),
        facts,
        own,
        other,
        wait=wait,
        through=through,
    )


def stack_line(facts, own, other, wait=()):
    _, rows, columns = own.shape
    line, facts = call(
        partial(stack_kernel, 7),
        "stack_line",
        (2,),
        [whole(own), whole(other)],
        block((2, 1, rows, columns), 0, first, 0, 0),
        like((2, 2, rows, columns), own.dtype),
        facts,
        own,
        other,
        wait=wait,
    )
    return line.reshape(4, rows, columns), facts


def turn_kernel(facts_ref, own_ref, other_ref, own_t_ref, other_t_ref):
    own_t_ref[...] = own_ref[...].T
    other_t_ref[...] = other_ref[...].T


def turn_all_kernel(facts_ref, rows_ref, out_ref):
    out_ref[...] = rows_ref[...].T


def turn_all(facts, values, wait=()):
    count, width = values.shape
    step = width // 4
    return call(
        turn_all_kernel,
        "turn_all",
        (4,),
        [block((count, step), 0, first)],
        block((step, count), first, 0),
        like((width, count), values.dtype),
        facts,
        values,
        wait=wait,
    )


def turn(facts, values, rows, wait=()):
    count, width = values.shape
    half = width // 2
    out = block((rows, count), first, 0)
    shape = like((half, count), values.dtype)
    return call(
        turn_kernel,
        "turn",
        (half // rows,),
        [
            block((count, rows), 0, lambda i, f: 2 * i + f[4]),
            block((count, rows), 0, lambda i, f: 2 * i + 1 - f[4]),
        ],
        [out, out],
        [shape, shape],
        facts,
        values,
        values,
        wait=wait,
    )


def project_kernel(facts_ref, rows_ref, bias_ref, *refs):
    parts, (out_ref, in_ref, rest_ref) = refs[:4], refs[4:]
    step = pl.program_id(0)
    weight = near_or_far(facts_ref, parts, step < 4)

    @pl.when(step % 4 < 3)
    def _():
        in_ref[...] = weight
        value = product(rows_ref[...], weight, 1, 0) + bias_ref[...]
        out_ref[...] = value.astype(jnp.bfloat16)

    @pl.when(step % 4 == 3)
    def _():
        chips, count, wide = rest_ref.shape
        pairs = weight.reshape(chips, 2, count, wide // 2)
        rest_ref[...] = jnp.concatenate([pairs[:, 0], pairs[:, 1]], axis=2)


def project(facts, rows, bias, parts, wait=()):
    count, width = rows.shape
    wide = parts[0].shape[2] // 4

    def column(i, f):
        return half_at(i, f, 4) * 3 + jnp.minimum(i % 4, 2)

    out = block((count, wide), 0, column)
    rest = (8, parts[0].shape[1] // 2, 2 * wide)
    return call(
        project_kernel,
        "project",
        (8,),
        [whole(rows), block((1, wide), 0, column)] + square_columns(parts, wide, 4),
        [out, block((width, wide), 0, column), block(rest, 0, 0, lambda i, f: half_at(i, f, 4))],
        [
            like((count, 6 * wide), jnp.bfloat16),
            like((width, 6 * wide), jnp.bfloat16),
            like(rest[:2] + (4 * wide,), jnp.bfloat16),
        ],
        facts,
        rows,
        bias[None],
        *parts,
        wait=wait,
    )


def valid_rows(facts_ref, count, slots):
    place = lax.broadcasted_iota(jnp.int32, (count, 1), 0) + pl.program_id(0) * count + facts_ref[2]
    place = jnp.where(place >= slots, place - slots, place)
    return (place < facts_ref[0]).astype(jnp.float32)


def add_rows(sums_ref, rows):
    total = jnp.concatenate([jnp.sum(part, axis=0, keepdims=True) for part in rows], axis=0)
    total = jnp.concatenate([total, jnp.zeros((8 - len(rows), total.shape[1]), jnp.float32)], axis=0)

    @pl.when(pl.program_id(0) == 0)
    def _():
        sums_ref[...] = total

    @pl.when(pl.program_id(0) > 0)
    def _():
        sums_ref[...] += total


def mean_of(values):
    return jnp.mean(values, axis=-1, keepdims=True)


def attend_out_kernel(
    slots, facts_ref, own_ref, other_ref, own_weight_ref, other_weight_ref, tokens_ref, vectors_ref,
    hat_ref, rstd_ref, low_ref, sums_ref,
):
    branch = (
        product(own_ref[...], own_weight_ref[...], 1, 0)
        + product(other_ref[...], other_weight_ref[...], 1, 0)
        + vectors_ref[0:1]
    )
    tokens = tokens_ref[...].astype(jnp.float32)
    total = tokens + branch
    centered = total - mean_of(total)
    rstd = lax.rsqrt(mean_of(centered * centered) + 1e-05)
    hat = centered * rstd
    hat_ref[...] = hat
    rstd_ref[...] = rstd
    low_ref[...] = (hat * vectors_ref[1:2] + vectors_ref[2:3]).astype(jnp.bfloat16)
    valid = valid_rows(facts_ref, tokens.shape[0], slots)
    add_rows(sums_ref, [valid * tokens * tokens, valid * branch * branch])


def attend_out(facts, own, other, own_weight, other_weight, tokens, vectors, wait=()):
    slots, width = tokens.shape
    step = slots // 4
    rows = lambda array: block((step, array.shape[1]), first, 0)
    return call(
        partial(attend_out_kernel, slots),
        "attend_out",
        (4,),
        [rows(own), rows(other), whole(own_weight), whole(other_weight), rows(tokens), whole(vectors)],
        [block((step, width), first, 0), block((step, 1), first, 0), block((step, width), first, 0), block((8, width), 0, 0)],
        [
            like((slots, width), jnp.float32),
            like((slots, 1), jnp.float32),
            like((slots, width), jnp.bfloat16),
            like((8, width), jnp.float32),
        ],
        facts,
        own,
        other,
        own_weight,
        other_weight,
        tokens,
        vectors,
        wait=wait,
    )


def up_kernel(facts_ref, rows_ref, bias_ref, *refs):
    parts, (act_ref, slope_ref, turned_ref, weight_ref) = refs[:4], refs[4:]
    weight = near_or_far(facts_ref, parts, pl.program_id(0) < 4)
    weight_ref[...] = weight
    pre_act = product(rows_ref[...], weight, 1, 0) + bias_ref[...]
    below = 0.5 + 0.5 * lax.erf(pre_act * 0.7071067811865476)
    act = (pre_act * below).astype(jnp.bfloat16)
    act_ref[...] = act
    turned_ref[...] = act.T
    slope = below + pre_act * (0.3989422804014327 * jnp.exp(-0.5 * pre_act * pre_act))
    slope_ref[...] = slope.astype(jnp.bfloat16)


def feed_up(facts, rows, bias, parts, wait=()):
    count, width = rows.shape
    units = bias.shape[0]
    wide = units // 8

    def column(i, f):
        return half_at(i, f, 4) * 4 + i % 4

    shape = like((count, units), jnp.bfloat16)
    out = block((count, wide), 0, column)
    return call(
        up_kernel,
        "feed_up",
        (8,),
        [whole(rows), block((1, wide), 0, column)] + square_columns(parts, wide, 4),
        [out, out, block((wide, count), column, 0), block((width, wide), 0, column)],
        [
            shape,
            shape,
            like((units, count), jnp.bfloat16),
            like((width, units), jnp.bfloat16),
        ],
        facts,
        rows,
        bias[None],
        *parts,
        wait=wait,
    )


def down_kernel(facts_ref, rows_ref, *refs):
    parts, (weight_ref, out_ref, total_ref) = refs[:4], refs[4:]
    step = pl.program_id(0)
    own, beside, below, across = [ref[0] for ref in parts]
    even, left = facts_ref[4] == 0, facts_ref[3] == 0
    for x in range(2):
        mine = jnp.where(even, own, beside) if x == 0 else jnp.where(even, beside, own)
        theirs = jnp.where(even, below, across) if x == 0 else jnp.where(even, across, below)
        weight_ref[x] = jnp.concatenate(
            [jnp.where(left, mine, theirs), jnp.where(left, theirs, mine)], axis=1
        )
    weight = weight_ref[...].reshape(rows_ref.shape[1], out_ref.shape[1])
    value = product(rows_ref[...], weight, 1, 0)

    @pl.when(step == 0)
    def _():
        total_ref[...] = value

    @pl.when(step > 0)
    def _():
        total_ref[...] += value

    @pl.when(step == 3)
    def _():
        out_ref[...] = total_ref[...].astype(jnp.bfloat16)


def feed_down(facts, rows, parts, wait=()):
    count, units = rows.shape
    _, block_rows, half_width = parts[0].shape
    width = 2 * half_width
    shape = (1,) + parts[0].shape[1:]
    return call(
        down_kernel,
        "feed_down",
        (4,),
        [block((count // 2, units // 4), 1, first)] + [block(shape, first, 0, 0)] * 4,
        [block((2, block_rows, width), first, 0, 0), block((count // 2, width), 0, 0)],
        [like((8, block_rows, width), jnp.bfloat16), like((count // 2, width), jnp.bfloat16)],
        facts,
        rows,
        *parts,
        scratch=[pltpu.VMEM((count // 2, width), jnp.float32)],
        wait=wait,
    )


def second_norm_kernel(
    slots, facts_ref, part_ref, other_ref, hat_ref, cotangent_ref, vectors_ref,
    mixed_ref, grad_ref, low_ref, sums_ref,
):
    branch = part_ref[...] + other_ref[...].astype(jnp.float32) + vectors_ref[0:1]
    hidden = hat_ref[...] * vectors_ref[1:2] + vectors_ref[2:3]
    gain = vectors_ref[3:4]
    total = hidden + branch
    centered = total - mean_of(total)
    rstd = lax.rsqrt(mean_of(centered * centered) + 1e-05)
    hat = centered * rstd
    mixed_ref[...] = (hat * gain + vectors_ref[4:5]).astype(jnp.bfloat16)
    valid = valid_rows(facts_ref, branch.shape[0], slots)
    grad = cotangent_ref[...].astype(jnp.float32) * valid
    scaled = grad * gain
    result = rstd * (scaled - mean_of(scaled) - hat * mean_of(scaled * hat))
    low = result.astype(jnp.bfloat16)
    grad_ref[...] = result
    low_ref[...] = low
    add_rows(sums_ref, [low.astype(jnp.float32), grad * hat, grad, valid * branch * branch])


def second_norm(facts, part, other, hat, cotangent, vectors, wait=()):
    slots, width = part.shape
    step = slots // 4
    rows = block((step, width), first, 0)
    return call(
        partial(second_norm_kernel, slots),
        "second_norm",
        (4,),
        [rows, rows, rows, rows, whole(vectors)],
        [rows, rows, rows, block((8, width), 0, 0)],
        [
            like((slots, width), jnp.bfloat16),
            like((slots, width), jnp.float32),
            like((slots, width), jnp.bfloat16),
            like((8, width), jnp.float32),
        ],
        facts,
        part,
        other,
        hat,
        cotangent,
        vectors,
        wait=wait,
    )


def first_norm_kernel(
    facts_ref, part_ref, other_ref, second_ref, hat_ref, rstd_ref, vectors_ref,
    grad_ref, low_ref, sums_ref,
):
    grad = part_ref[...] + other_ref[...].astype(jnp.float32) + second_ref[...]
    hat = hat_ref[...]
    scaled = grad * vectors_ref[1:2]
    result = rstd_ref[...] * (scaled - mean_of(scaled) - hat * mean_of(scaled * hat))
    low = result.astype(jnp.bfloat16)
    grad_ref[...] = result
    low_ref[...] = low
    add_rows(sums_ref, [low.astype(jnp.float32), grad * hat, grad])


def first_norm(facts, part, other, second, hat, rstd, vectors, wait=()):
    slots, width = part.shape
    step = slots // 4
    rows = block((step, width), first, 0)
    return call(
        first_norm_kernel,
        "first_norm",
        (4,),
        [rows, rows, rows, rows, block((step, 1), first, 0), whole(vectors)],
        [rows, rows, block((8, width), 0, 0)],
        [
            like((slots, width), jnp.float32),
            like((slots, width), jnp.bfloat16),
            like((8, width), jnp.float32),
        ],
        facts,
        part,
        other,
        second,
        hat,
        rstd,
        vectors,
        wait=wait,
    )


def act_grad_kernel(facts_ref, rows_ref, weight_ref, slope_ref, out_ref, sums_ref):
    total = product(rows_ref[...], weight_ref[...], 1, 1)
    grad = total.astype(jnp.bfloat16).astype(jnp.float32) * slope_ref[...].astype(jnp.float32)
    low = grad.astype(jnp.bfloat16)
    out_ref[...] = low
    sums_ref[...] = jnp.sum(low.astype(jnp.float32), axis=0, keepdims=True)


def act_grad(facts, rows, weight, slope, wait=()):
    count, units = slope.shape
    step = units // 8
    out = block((count, step), 0, first)
    return call(
        act_grad_kernel,
        "act_grad",
        (8,),
        [whole(rows), block((step, rows.shape[1]), first, 0), out],
        [out, block((1, step), 0, first)],
        [like((count, units), jnp.bfloat16), like((1, units), jnp.float32)],
        facts,
        rows,
        weight,
        slope,
        wait=wait,
    )


def tokens_grad_kernel(facts_ref, mine_ref, theirs_ref, weight_ref, out_ref, sent_ref):
    wide = mine_ref.shape[1]
    slots = out_ref.shape[0]
    half = facts_ref[3]
    mine = weight_ref[:, pl.ds(pl.multiple_of(half * wide, 128), wide)]
    theirs = weight_ref[:, pl.ds(pl.multiple_of((1 - half) * wide, 128), wide)]
    total = product(mine_ref[...], mine, 1, 1) + product(theirs_ref[...], theirs, 1, 1)
    out_ref[...] = total[:slots]
    sent_ref[...] = total[slots:].astype(sent_ref.dtype)


def tokens_grad(facts, mine, theirs, weight, wait=(), through=()):
    count, columns = mine.shape
    width = weight.shape[0]
    step = width // 4
    out = block((count // 2, step), 0, first)
    return call(
        tokens_grad_kernel,
        "tokens_grad",
        (4,),
        [whole(mine), whole(theirs), block((step, 2 * columns), first, 0)],
        [out, out],
        [
            like((count // 2, width), jnp.float32),
            like((count // 2, width), jnp.bfloat16),
        ],
        facts,
        mine,
        theirs,
        weight,
        wait=wait,
        through=through,
    )


def add_parts_kernel(facts_ref, own_ref, got_ref, kept_ref, sent_ref):
    step = pl.program_id(0)
    total = own_ref[...].astype(jnp.float32) + got_ref[...].astype(jnp.float32)
    total = total.astype(jnp.bfloat16)

    @pl.when(step < 2)
    def _():
        sent_ref[...] = total

    @pl.when(step >= 2)
    def _():
        kept_ref[...] = total


def add_parts(facts, own, got, wait=(), through=()):
    _, rows, columns = own.shape
    shape = (1, rows, columns)
    part = block(shape, lambda i, f: 2 * (i % 2) + jnp.where(i < 2, 1 - f[7], f[7]), 0, 0)
    half = like((2, rows, columns), jnp.bfloat16)
    return call(
        add_parts_kernel,
        "add_parts",
        (4,),
        [part, part],
        [
            block(shape, lambda i, *_: jnp.maximum(i - 2, 0), 0, 0),
            block(shape, lambda i, *_: jnp.minimum(i, 1), 0, 0),
        ],
        [half, half],
        facts,
        own,
        got,
        wait=wait,
        through=through,
    )


def split_body(
    tokens,
    lengths,
    cotangent,
    query_weight,
    key_weight,
    value_weight,
    out_weight,
    up_weight,
    down_weight,
    query_bias,
    value_bias,
    out_bias,
    attn_gain,
    attn_shift,
    up_bias,
    down_bias,
    feed_gain,
    feed_shift,
):
    core = lax.axis_index("c")
    half = lax.axis_index("s")
    row_count, width = tokens.shape[1:]
    slots = 2 * row_count
    unit_block = down_weight.shape[0]
    units = up_bias.shape[0] // 2
    cols = width // 2
    wide = cols // 2

    def to_sequence(values):
        return jnp.concatenate([pick(values, half, 0), swap(pick(values, 1 - half, 0), "s")], axis=0)

    def from_sequence(values):
        return in_order(values[:row_count], swap(values[row_count:], "s"), half)

    small = [
        split_columns(weight, HD, core) for weight in (query_weight, key_weight, value_weight)
    ]
    large = split_columns(up_weight, unit_block, core)
    up_pair = in_order(large[0], swap(large[1], "c"), core)
    up_cols = up_pair.shape[2]
    up_mine = up_pair.reshape(-1, up_cols)
    rows = up_mine.shape[0]
    near_kept = jnp.concatenate([part[0] for part in small], axis=1)
    near_sent = jnp.concatenate([part[1] for part in small], axis=1)
    near_pair = in_order(near_kept, swap(near_sent, "c"), core)
    out_pair = jnp.concatenate([out_weight[:, :wide], out_weight[:, wide:]], axis=0)
    near_mine = jnp.concatenate([near_pair.reshape(rows, -1), out_pair], axis=1)
    line = lax.axis_index("z")
    length_own = lax.dynamic_slice_in_dim(lengths, half, 1, 0)
    facts = jnp.concatenate(
        [
            both(length_own, "c"),
            jnp.stack(
                [
                    half * row_count,
                    half,
                    lax.axis_index("x"),
                    jnp.int32(0),
                    line // 2,
                    line % 2,
                ]
            ).astype(jnp.int32),
        ]
    )
    tokens_own = to_sequence(tokens)
    cotangent_own = to_sequence(cotangent)
    (near, up_mine, down_mine), facts = stack_pair(
        facts,
        near_mine,
        line_cross(near_mine),
        wait=(tokens_own,),
        through=(up_mine, down_weight),
    )
    up_got = line_cross(up_mine)
    near, facts = stack_line(facts, near, line_next(near), wait=(cotangent_own, up_got))
    near_parts = gather_square(near, "x")
    up_pairs, facts = stack_pair(facts, up_mine, up_got)
    down_pairs, facts = stack_pair(facts, down_mine, line_cross(down_mine), wait=(up_pairs,))
    tokens_both = both(tokens_own, "c")
    up_part, facts = stack_line(
        facts, up_pairs, line_next(up_pairs), wait=(near_parts[1], near_parts[2], down_pairs)
    )
    up_parts = gather_square(up_part, "s")
    down_part, facts = stack_line(
        facts, down_pairs, line_next(down_pairs), wait=(near_parts[3], up_part)
    )
    down_parts = gather_square(down_part, "x")
    def halves_of(vector, size):
        return pick(vector.reshape(-1, 2, size), core, 1).reshape(-1)

    query_part = halves_of(query_bias, HD).reshape(2, wide)
    value_part = halves_of(value_bias, HD).reshape(2, wide)
    in_bias = jnp.stack([query_part, jnp.zeros_like(query_part), value_part], axis=1).reshape(-1)
    (projected, in_weight, out_own), facts = project(
        facts, tokens_both, in_bias, near_parts, wait=(up_part, down_part)
    )
    out_own = out_own.reshape(cols, width)
    out_other = swap(out_own, "c")
    (heads_out, totals), facts = attend(facts, projected, slots, wait=(up_parts[2],))
    heads_other = swap(heads_out[slots:], "c")
    vectors = jnp.stack(
        [out_bias, attn_gain, attn_shift, down_bias, feed_gain, feed_shift, out_bias, out_bias]
    )
    (first_hat, first_rstd, hidden_low, first_sums), facts = attend_out(
        facts,
        heads_out,
        heads_other,
        out_own,
        out_other,
        tokens_own,
        vectors,
        wait=(up_parts[1], down_parts[2]),
    )
    hidden_both = both(hidden_low, "c")
    (activation, slope, act_t, up_all), facts = feed_up(
        facts, hidden_both, halves_of(up_bias, unit_block), up_parts, wait=(down_parts[1],)
    )
    hidden_turned, facts = turn(facts, hidden_both, rows, wait=(act_t,))
    (down_all, feed_sent), facts = feed_down(facts, activation, down_parts)
    down_all = down_all.reshape(units, width)
    feed_other = swap(feed_sent, "c")
    feed_part = product(activation[:slots], down_all, 1, 0)
    feed_vectors = jnp.stack(
        [down_bias, attn_gain, attn_shift, feed_gain, feed_shift, out_bias, out_bias, out_bias]
    )
    (mixed, second_grad, feed_low, second_sums), facts = second_norm(
        facts, feed_part, feed_other, first_hat, cotangent_own, feed_vectors
    )

    feed_both = both(feed_low, "c")
    tokens_t, facts = turn_all(facts, tokens_both, wait=(feed_low,))
    feed_mine, feed_theirs = columns_of(feed_both, half), columns_of(feed_both, 1 - half)
    down_sent = grad_block(act_t, feed_theirs)
    down_got = swap(down_sent, "s")
    (pre_grad, up_bias_grad), facts = act_grad(
        facts, feed_both, down_all, slope, wait=(down_sent,)
    )
    hidden_sent = product(pre_grad[slots:], up_all, 1, 1).astype(jnp.bfloat16)
    hidden_other = swap(hidden_sent, "c")
    hidden_own_t, hidden_other_t = hidden_turned
    up_sent = grad_block(hidden_other_t, pre_grad)
    up_got = swap(up_sent, "x")
    hidden_part = product(pre_grad[:slots], up_all, 1, 1)
    (first_grad, attn_low, third_sums), facts = first_norm(
        facts,
        hidden_part,
        hidden_other,
        second_grad,
        first_hat,
        first_rstd,
        vectors,
        wait=(up_sent,),
    )
    grad_sent = product(attn_low, out_other, 1, 1).astype(jnp.bfloat16)
    grad_other = swap(grad_sent, "c")
    grad_own = product(attn_low, out_own, 1, 1).astype(jnp.bfloat16)
    out_sent = product(heads_other, attn_low, 0, 0).astype(jnp.bfloat16)
    out_got = swap(out_sent, "c")
    heads_grad = jnp.concatenate([grad_own, grad_other], axis=0)
    (theirs_low, theirs_sums, mixed), facts = attend_back(
        facts, projected, heads_grad, totals, slots, False, wait=(out_sent,), through=(mixed,)
    )
    mixed_other = swap(mixed[row_count:], "s")
    in_sent = grad_block(tokens_t, theirs_low)
    in_got = swap(in_sent, "s")
    down_total = grad_block(act_t, feed_mine, down_got)
    down_kept, down_sent = halve(down_total.reshape(4, 2, unit_block, cols), "x", 1)
    down_got = swap(down_sent, "x")
    out_grad = grad_block(heads_out[:slots].T, attn_low, out_got)
    out_line = out_grad.reshape((4, 2 * out_weight.shape[0], width))
    out_kept, out_sent = line_parts(out_line)
    out_got = lax.ppermute(out_sent, "z", NEXT)
    (mine_low, mine_sums), facts = attend_back(
        facts, projected, heads_grad, totals, slots, True, wait=(in_sent, out_sent, down_sent)
    )
    up_total = grad_block(hidden_own_t, pre_grad, up_got).reshape(4, rows, 2 * up_cols)
    up_kept, up_sent = columns_of(up_total, half), columns_of(up_total, 1 - half)
    up_got = swap(up_sent, "s")
    out_total = add(out_kept, out_got)
    upper = lax.axis_index("z") // 2
    out_kept, out_sent = pick(out_total, upper, 0), pick(out_total, 1 - upper, 0)
    out_got = lax.ppermute(out_sent, "z", CROSS)
    valid_count = length_own[0].astype(jnp.float32) * width
    stats = jnp.stack(
        [jnp.sum(first_sums[0]), jnp.sum(first_sums[1]), jnp.sum(second_sums[3]), valid_count]
    )
    mine_sums, theirs_sums = jnp.sum(mine_sums, axis=(0, 1)), jnp.sum(theirs_sums, axis=(0, 1))
    late = in_order(mine_sums, theirs_sums, half)
    sums = jnp.concatenate(
        [
            second_sums[:3].reshape(-1),
            third_sums[:3].reshape(-1),
            jnp.pad(stats, (0, 124)),
            up_bias_grad[0],
            late[:, :wide].reshape(-1),
            late[:, 2 * wide :].reshape(-1),
        ]
    )
    sums_got = lax.ppermute(sums, "z", NEXT)
    (tokens_part, tokens_sent), facts = tokens_grad(
        facts,
        mine_low,
        theirs_low,
        in_weight,
        wait=(up_sent, out_sent, sums),
    )
    tokens_other = swap(tokens_sent, "c")
    in_total = grad_block(tokens_t, mine_low, in_got)
    in_kept, in_sent = halve(in_total.reshape(4, 2, rows, 3 * wide), "x", 1)
    in_got = swap(in_sent, "x")
    (down_pairs, down_next, sums, out_kept), facts = add_parts(
        facts,
        down_kept,
        down_got,
        wait=(in_sent, tokens_part),
        through=(sums + sums_got, add(out_kept, out_got)),
    )
    in_sum = fold_line(add(in_kept, in_got))
    tokens_grad_sum = tokens_part + tokens_other.astype(jnp.float32) + first_grad
    tokens_grad_sum = from_sequence(tokens_grad_sum.astype(jnp.bfloat16))
    mixed = in_order(mixed[:row_count], mixed_other, half)
    down_sum = fold_cross(add(down_pairs, lax.ppermute(down_next, "z", NEXT)))
    up_sum = fold_line(add(up_kept, up_got))
    out_sum = fold_columns(fold(out_kept.reshape(2, out_weight.shape[0], width), "x", 0))

    sums = sums + lax.ppermute(sums, "z", CROSS)
    sums = sums + swap(sums, "s")
    sums = sums + swap(sums, "x")
    both_sums = in_order(sums, swap(sums, "c"), core)
    count = 6 * width + 128
    shared = both_sums[0, :count] + both_sums[1, :count]
    down_bias_grad, feed_gain_grad, feed_shift_grad, out_bias_grad, attn_gain_grad, attn_shift_grad = [
        shared[i * width : (i + 1) * width] for i in range(6)
    ]
    stats = shared[6 * width : 6 * width + 4]

    def interleave(start, size, block_size):
        sums = both_sums[:, start : start + size].reshape(2, -1, block_size)
        return sums.transpose(1, 0, 2).reshape(-1)

    up_bias_grad = interleave(count, units, unit_block)
    query_bias_grad = interleave(count + units, cols, HD)
    value_bias_gradient = interleave(count + units + cols, cols, HD)
    stream_rms = jnp.sqrt(stats[:3] / stats[3])

    def give_back(total):
        total = total.reshape((2, rows // 2) + total.shape[1:])
        return pick(total, core, 0), swap(pick(total, 1 - core, 0), "c")

    up_shares = give_back(up_sum)
    in_shares = give_back(in_sum)
    down_weight_grad = down_sum.astype(jnp.float32)
    out_weight_grad = out_sum.astype(jnp.float32)

    def merge(shares, start, size, block):
        one, two = [
            share[:, start : start + size].reshape(rows // 2, -1, block) for share in shares
        ]
        first = jnp.where(core == 0, one, two)
        second = jnp.where(core == 0, two, one)
        return jnp.stack([first, second], axis=2).reshape(rows // 2, -1).astype(jnp.float32)

    query_weight_grad = merge(in_shares, 0, wide, HD)
    key_weight_grad = merge(in_shares, wide, wide, HD)
    value_weight_grad = merge(in_shares, 2 * wide, wide, HD)
    up_weight_grad = merge(up_shares, 0, up_cols, unit_block)
    return (
        mixed,
        tokens_grad_sum,
        query_weight_grad,
        key_weight_grad,
        value_weight_grad,
        out_weight_grad,
        up_weight_grad,
        down_weight_grad,
        query_bias_grad,
        value_bias_gradient,
        out_bias_grad,
        attn_gain_grad,
        attn_shift_grad,
        up_bias_grad,
        down_bias_grad,
        feed_gain_grad,
        feed_shift_grad,
        stream_rms,
    )


def solution(mesh):
    devices = mesh.devices
    dp_count, seq_count = devices.shape
    split = seq_count == 2 and dp_count == 16
    if split:
        inner = jax.sharding.Mesh(devices.reshape(4, 2, 2, seq_count), ("z", "x", "c", "s"))
        dp, seq, body = ("z", "x", "c"), "s", split_body
    else:
        inner, dp, seq, body = mesh, "dp", "seq", general_body
    weights = (P(dp, seq),) * 6
    vectors = (P(),) * 9
    rows = P(dp, seq, None)
    in_specs = (rows, P(dp), rows) + weights + vectors
    out_specs = (rows, rows) + weights + vectors + (P(),)
    return jax.shard_map(body, mesh=inner, in_specs=in_specs, out_specs=out_specs, check_vma=False)
```

```python
from functools import partial
import math

import jax
import jax.numpy as jnp
from jax import lax
from jax.experimental import pallas as pl
from jax.experimental.pallas import tpu as pltpu
from jax.sharding import PartitionSpec as P

HD = 64


def layer_norm(values_in, gain_vector, shift_vector):
    mean_value = jnp.mean(values_in, axis=-1, keepdims=True)
    centered = values_in - mean_value
    variance = jnp.mean(centered * centered, axis=-1, keepdims=True)
    return centered * lax.rsqrt(variance + 1e-05) * gain_vector + shift_vector


def gather_weights(first, second, third, fourth, fifth, sixth):
    part = (
        lax.all_gather(first, "dp", axis=0, tiled=True),
        lax.all_gather(second, "dp", axis=0, tiled=True),
        lax.all_gather(third, "dp", axis=0, tiled=True),
        lax.all_gather(fourth, "dp", axis=0, tiled=True),
        lax.all_gather(fifth, "dp", axis=0, tiled=True),
        lax.all_gather(sixth, "dp", axis=0, tiled=True),
    )
    return (
        lax.all_gather(part[0], "seq", axis=1, tiled=True),
        lax.all_gather(part[1], "seq", axis=1, tiled=True),
        lax.all_gather(part[2], "seq", axis=1, tiled=True),
        lax.all_gather(part[3], "seq", axis=1, tiled=True),
        lax.all_gather(part[4], "seq", axis=1, tiled=True),
        lax.all_gather(part[5], "seq", axis=1, tiled=True),
    )


def reduce_grads(first, second, third, fourth, fifth, sixth):
    part = (
        lax.psum_scatter(first.astype(jnp.bfloat16), "seq", scatter_dimension=1, tiled=True).astype(
            jnp.float32
        ),
        lax.psum_scatter(
            second.astype(jnp.bfloat16), "seq", scatter_dimension=1, tiled=True
        ).astype(jnp.float32),
        lax.psum_scatter(third.astype(jnp.bfloat16), "seq", scatter_dimension=1, tiled=True).astype(
            jnp.float32
        ),
        lax.psum_scatter(
            fourth.astype(jnp.bfloat16), "seq", scatter_dimension=1, tiled=True
        ).astype(jnp.float32),
        lax.psum_scatter(fifth.astype(jnp.bfloat16), "seq", scatter_dimension=1, tiled=True).astype(
            jnp.float32
        ),
        lax.psum_scatter(sixth.astype(jnp.bfloat16), "seq", scatter_dimension=1, tiled=True).astype(
            jnp.float32
        ),
    )
    return (
        lax.psum_scatter(
            part[0].astype(jnp.bfloat16), "dp", scatter_dimension=0, tiled=True
        ).astype(jnp.float32),
        lax.psum_scatter(
            part[1].astype(jnp.bfloat16), "dp", scatter_dimension=0, tiled=True
        ).astype(jnp.float32),
        lax.psum_scatter(
            part[2].astype(jnp.bfloat16), "dp", scatter_dimension=0, tiled=True
        ).astype(jnp.float32),
        lax.psum_scatter(
            part[3].astype(jnp.bfloat16), "dp", scatter_dimension=0, tiled=True
        ).astype(jnp.float32),
        lax.psum_scatter(
            part[4].astype(jnp.bfloat16), "dp", scatter_dimension=0, tiled=True
        ).astype(jnp.float32),
        lax.psum_scatter(
            part[5].astype(jnp.bfloat16), "dp", scatter_dimension=0, tiled=True
        ).astype(jnp.float32),
    )


def block_layout(seq_count, row_count, head_count):
    block_seqs = math.gcd(seq_count, max(1, 512 // row_count))
    group_heads = math.gcd(head_count, 4)
    return (block_seqs, seq_count // block_seqs, group_heads, head_count // group_heads)


def head_slice(block_part, offset, group_width, group_heads):
    sliced = lax.dynamic_slice_in_dim(block_part, offset, group_width, 2)
    return sliced.reshape(sliced.shape[0], sliced.shape[1], group_heads, HD)


def attention_forward(queries, key_all, value_all, key_mask):
    seq_count, row_count, feature_total = queries.shape
    slot_count = key_all.shape[1]
    block_seqs, block_count, group_heads, group_count = block_layout(
        seq_count, row_count, feature_total // HD
    )
    group_width = group_heads * HD

    def seq_block(inputs):
        query_part, key_part, value_part, mask_part = inputs

        def head_block(group_index):
            offset = group_index * group_width
            query_heads = head_slice(query_part, offset, group_width, group_heads)
            key_heads = head_slice(key_part, offset, group_width, group_heads)
            value_heads = head_slice(value_part, offset, group_width, group_heads)
            scores = (
                jnp.einsum(
                    "brhd,bkhd->bhrk", query_heads, key_heads, preferred_element_type=jnp.float32
                )
                * 0.125
            )
            scores = jnp.where(mask_part[:, None, None, :], scores, -1e30)
            row_max = jnp.max(scores, axis=-1, keepdims=True)
            exponent = jnp.exp(scores - row_max)
            row_total = jnp.sum(exponent, axis=-1, keepdims=True)
            soft_probs = (exponent / row_total).astype(jnp.bfloat16)
            heads_out = jnp.einsum(
                "bhrk,bkhd->brhd", soft_probs, value_heads, preferred_element_type=jnp.float32
            )
            log_total = (row_max + jnp.log(row_total))[..., 0]
            return (heads_out.reshape(block_seqs, row_count, group_width), log_total)

        return lax.map(head_block, jnp.arange(group_count))

    outputs, log_totals = lax.map(
        seq_block,
        (
            queries.reshape(block_count, block_seqs, row_count, feature_total),
            key_all.reshape(block_count, block_seqs, slot_count, feature_total),
            value_all.reshape(block_count, block_seqs, slot_count, feature_total),
            key_mask.reshape(block_count, block_seqs, slot_count),
        ),
    )
    mixed_heads = outputs.transpose(0, 2, 3, 1, 4).reshape(seq_count, row_count, feature_total)
    return (mixed_heads, log_totals)


def attention_backward(queries, key_all, value_all, key_mask, heads_grad, log_totals):
    seq_count, row_count, feature_total = queries.shape
    slot_count = key_all.shape[1]
    block_seqs, block_count, group_heads, group_count = block_layout(
        seq_count, row_count, feature_total // HD
    )
    group_width = group_heads * HD

    def seq_block(inputs):
        query_part, key_part, value_part, mask_part, grad_part, total_part = inputs

        def head_block(group_index):
            offset = group_index * group_width
            query_heads = head_slice(query_part, offset, group_width, group_heads)
            key_heads = head_slice(key_part, offset, group_width, group_heads)
            value_heads = head_slice(value_part, offset, group_width, group_heads)
            grad_heads = head_slice(grad_part, offset, group_width, group_heads)
            log_total = lax.dynamic_index_in_dim(total_part, group_index, 0, keepdims=False)
            scores = (
                jnp.einsum(
                    "brhd,bkhd->bhrk", query_heads, key_heads, preferred_element_type=jnp.float32
                )
                * 0.125
            )
            scores = jnp.where(mask_part[:, None, None, :], scores, -1e30)
            soft_probs = jnp.exp(scores - log_total[..., None])
            value_grad = jnp.einsum(
                "bhrk,brhd->bkhd",
                soft_probs.astype(jnp.bfloat16),
                grad_heads,
                preferred_element_type=jnp.float32,
            )
            prob_grad = jnp.einsum(
                "brhd,bkhd->bhrk", grad_heads, value_heads, preferred_element_type=jnp.float32
            )
            inner = jnp.sum(soft_probs * prob_grad, axis=-1, keepdims=True)
            score_grad = (soft_probs * (prob_grad - inner)).astype(jnp.bfloat16)
            query_grad = (
                jnp.einsum(
                    "bhrk,bkhd->brhd", score_grad, key_heads, preferred_element_type=jnp.float32
                )
                * 0.125
            )
            key_grad = (
                jnp.einsum(
                    "bhrk,brhd->bkhd", score_grad, query_heads, preferred_element_type=jnp.float32
                )
                * 0.125
            )
            return (
                query_grad.reshape(block_seqs, row_count, group_width),
                key_grad.reshape(block_seqs, slot_count, group_width),
                value_grad.reshape(block_seqs, slot_count, group_width),
            )

        return lax.map(head_block, jnp.arange(group_count))

    query_blocks, key_blocks, value_block_list = lax.map(
        seq_block,
        (
            queries.reshape(block_count, block_seqs, row_count, feature_total),
            key_all.reshape(block_count, block_seqs, slot_count, feature_total),
            value_all.reshape(block_count, block_seqs, slot_count, feature_total),
            key_mask.reshape(block_count, block_seqs, slot_count),
            heads_grad.reshape(block_count, block_seqs, row_count, feature_total),
            log_totals,
        ),
    )
    query_grad = query_blocks.transpose(0, 2, 3, 1, 4).reshape(seq_count, row_count, feature_total)
    key_grad = key_blocks.transpose(0, 2, 3, 1, 4).reshape(seq_count, slot_count, feature_total)
    value_grad = value_block_list.transpose(0, 2, 3, 1, 4).reshape(
        seq_count, slot_count, feature_total
    )
    return (query_grad, key_grad, value_grad)


def general_body(
    tokens,
    lengths,
    cotangent,
    query_weight,
    key_weight,
    value_weight,
    out_weight,
    up_weight,
    down_weight,
    query_bias,
    value_bias,
    out_bias,
    attn_gain,
    attn_shift,
    up_bias,
    down_bias,
    feed_gain,
    feed_shift,
):
    seq_count, row_count, feature_total = tokens.shape
    slot_count = row_count * lax.axis_size("seq")
    token_count = seq_count * row_count
    whole = gather_weights(
        query_weight, key_weight, value_weight, out_weight, up_weight, down_weight
    )
    full_query, full_key, full_value, full_out, full_up, full_down = whole
    flat_tokens = tokens.reshape(token_count, feature_total)
    queries = (
        jnp.dot(flat_tokens, full_query, preferred_element_type=jnp.float32) + query_bias
    ).astype(jnp.bfloat16)
    key_rows = jnp.dot(flat_tokens, full_key, preferred_element_type=jnp.float32).astype(
        jnp.bfloat16
    )
    value_rows = (
        jnp.dot(flat_tokens, full_value, preferred_element_type=jnp.float32) + value_bias
    ).astype(jnp.bfloat16)
    first_slot = lax.axis_index("seq") * row_count
    key_mask = jnp.arange(slot_count)[None, :] < lengths[:, None]
    row_valid = ((first_slot + jnp.arange(row_count))[None, :] < lengths[:, None]).astype(
        jnp.float32
    )
    row_valid = row_valid.reshape(token_count, 1)
    query_blocks = queries.reshape(seq_count, row_count, feature_total)
    key_blocks = key_rows.reshape(seq_count, row_count, feature_total)
    value_block_list = value_rows.reshape(seq_count, row_count, feature_total)
    key_all, value_all = (
        lax.all_gather(key_blocks, "seq", axis=1, tiled=True),
        lax.all_gather(value_block_list, "seq", axis=1, tiled=True),
    )
    mixed_heads, log_totals = attention_forward(query_blocks, key_all, value_all, key_mask)
    heads_low = mixed_heads.reshape(token_count, feature_total).astype(jnp.bfloat16)
    attention_out = jnp.dot(heads_low, full_out, preferred_element_type=jnp.float32) + out_bias
    tokens_f32 = flat_tokens.astype(jnp.float32)
    first_sum = tokens_f32 + attention_out
    hidden, first_pull = jax.vjp(layer_norm, first_sum, attn_gain, attn_shift)
    hidden_low = hidden.astype(jnp.bfloat16)
    pre_act = jnp.dot(hidden_low, full_up, preferred_element_type=jnp.float32) + up_bias
    gelu_out, gelu_pull = jax.vjp(partial(jax.nn.gelu, approximate=False), pre_act)
    activation = gelu_out.astype(jnp.bfloat16)
    feed_out = jnp.dot(activation, full_down, preferred_element_type=jnp.float32) + down_bias
    result, second_pull = jax.vjp(layer_norm, hidden + feed_out, feed_gain, feed_shift)
    mixed = result.astype(jnp.bfloat16).reshape(seq_count, row_count, feature_total)
    partial_stats = jnp.stack(
        [
            jnp.sum(row_valid * tokens_f32 * tokens_f32),
            jnp.sum(row_valid * attention_out * attention_out),
            jnp.sum(row_valid * feed_out * feed_out),
            jnp.sum(row_valid) * feature_total,
        ]
    )
    back_weights = gather_weights(
        query_weight, key_weight, value_weight, out_weight, up_weight, down_weight
    )
    back_query, back_key, back_value, back_out, back_up, back_down = back_weights
    out_grad = cotangent.reshape(token_count, feature_total).astype(jnp.float32) * row_valid
    second_grad, feed_gain_grad, feed_shift_grad = second_pull(out_grad)
    feed_low = second_grad.astype(jnp.bfloat16)
    down_weight_grad = jnp.einsum(
        "nf,nd->fd", activation, feed_low, preferred_element_type=jnp.float32
    )
    down_bias_grad = jnp.sum(feed_low, axis=0, dtype=jnp.float32)
    act_grad = jnp.einsum(
        "nd,fd->nf", feed_low, back_down, preferred_element_type=jnp.float32
    ).astype(jnp.bfloat16)
    pre_grad = gelu_pull(act_grad.astype(jnp.float32))[0].astype(jnp.bfloat16)
    up_weight_grad = jnp.einsum(
        "nd,nf->df", hidden_low, pre_grad, preferred_element_type=jnp.float32
    )
    up_bias_grad = jnp.sum(pre_grad, axis=0, dtype=jnp.float32)
    hidden_grad = (
        jnp.einsum("nf,df->nd", pre_grad, back_up, preferred_element_type=jnp.float32) + second_grad
    )
    first_grad, attn_gain_grad, attn_shift_grad = first_pull(hidden_grad)
    attn_low = first_grad.astype(jnp.bfloat16)
    out_weight_grad = jnp.einsum(
        "nd,ne->de", heads_low, attn_low, preferred_element_type=jnp.float32
    )
    out_bias_grad = jnp.sum(attn_low, axis=0, dtype=jnp.float32)
    heads_grad = jnp.einsum(
        "ne,de->nd", attn_low, back_out, preferred_element_type=jnp.float32
    ).astype(jnp.bfloat16)
    heads_grad = heads_grad.reshape(seq_count, row_count, feature_total)
    query_grad, key_part_grad, value_part_grad = attention_backward(
        query_blocks, key_all, value_all, key_mask, heads_grad, log_totals
    )
    key_sum, value_sum = (
        lax.psum_scatter(
            key_part_grad.astype(jnp.bfloat16), "seq", scatter_dimension=1, tiled=True
        ).astype(jnp.float32),
        lax.psum_scatter(
            value_part_grad.astype(jnp.bfloat16), "seq", scatter_dimension=1, tiled=True
        ).astype(jnp.float32),
    )
    query_low = query_grad.reshape(token_count, feature_total).astype(jnp.bfloat16)
    key_low = key_sum.reshape(token_count, feature_total).astype(jnp.bfloat16)
    value_low = value_sum.reshape(token_count, feature_total).astype(jnp.bfloat16)
    query_weight_grad = jnp.einsum(
        "nd,ne->de", flat_tokens, query_low, preferred_element_type=jnp.float32
    )
    key_weight_grad = jnp.einsum(
        "nd,ne->de", flat_tokens, key_low, preferred_element_type=jnp.float32
    )
    value_weight_grad = jnp.einsum(
        "nd,ne->de", flat_tokens, value_low, preferred_element_type=jnp.float32
    )
    query_bias_grad = jnp.sum(query_low, axis=0, dtype=jnp.float32)
    value_bias_gradient = jnp.sum(value_low, axis=0, dtype=jnp.float32)
    tokens_grad = (
        jnp.einsum("ne,de->nd", query_low, back_query, preferred_element_type=jnp.float32)
        + jnp.einsum("ne,de->nd", key_low, back_key, preferred_element_type=jnp.float32)
        + jnp.einsum("ne,de->nd", value_low, back_value, preferred_element_type=jnp.float32)
        + first_grad
    )
    tokens_grad = tokens_grad.astype(jnp.bfloat16).reshape(seq_count, row_count, feature_total)
    matrix_grads = reduce_grads(
        query_weight_grad,
        key_weight_grad,
        value_weight_grad,
        out_weight_grad,
        up_weight_grad,
        down_weight_grad,
    )
    totals = lax.psum(
        (
            partial_stats,
            query_bias_grad,
            value_bias_gradient,
            out_bias_grad,
            attn_gain_grad,
            attn_shift_grad,
            up_bias_grad,
            down_bias_grad,
            feed_gain_grad,
            feed_shift_grad,
        ),
        ("dp", "seq"),
    )
    stream_rms = jnp.sqrt(totals[0][:3] / totals[0][3])
    return (
        mixed,
        tokens_grad,
        matrix_grads[0],
        matrix_grads[1],
        matrix_grads[2],
        matrix_grads[3],
        matrix_grads[4],
        matrix_grads[5],
        totals[1],
        totals[2],
        totals[3],
        totals[4],
        totals[5],
        totals[6],
        totals[7],
        totals[8],
        totals[9],
        stream_rms,
    )


def swap(value, axis):
    return lax.ppermute(value, axis, [(0, 1), (1, 0)])


def both(value, axis):
    return jnp.concatenate([value, swap(value, axis)], axis=0)


def in_order(own, other, index, axis=0):
    return jnp.where(
        index == 0, jnp.stack([own, other], axis=axis), jnp.stack([other, own], axis=axis)
    )


def split_columns(weight, width, core):
    rows = weight.shape[0]
    blocks = weight.reshape(rows, -1, 2, width)
    return pick(blocks, core, 2).reshape(rows, -1), pick(blocks, 1 - core, 2).reshape(rows, -1)


def pick(values, index, axis):
    return lax.dynamic_index_in_dim(values, index, axis, keepdims=False)


def add(left, right):
    return (left.astype(jnp.float32) + right.astype(jnp.float32)).astype(jnp.bfloat16)


def fold(values, axis, dim):
    index = lax.axis_index(axis)
    return add(pick(values, index, dim), swap(pick(values, 1 - index, dim), axis))


NEXT = [(0, 1), (1, 0), (2, 3), (3, 2)]
CROSS = [(0, 2), (2, 0), (1, 3), (3, 1)]


def fold_cross(pairs):
    upper = lax.axis_index("z") // 2
    return add(pick(pairs, upper, 0), lax.ppermute(pick(pairs, 1 - upper, 0), "z", CROSS))


def fold_line(values):
    odd = lax.axis_index("z") % 2
    pairs = values.reshape((2, 2) + values.shape[1:])
    sent = lax.ppermute(pick(pairs, 1 - odd, 1), "z", NEXT)
    return fold_cross(add(pick(pairs, odd, 1), sent))


def line_cross(value):
    return lax.ppermute(value, "z", CROSS)


def line_next(pair):
    return lax.ppermute(pair, "z", NEXT)


def gather_square(own, way):
    beside, below = swap(own, "x"), swap(own, "s")
    across = swap(below, "x") if way == "x" else swap(beside, "s")
    return [own, beside, below, across]


def fold_columns(total):
    half = lax.axis_index("s")
    return add(columns_of(total, half), swap(columns_of(total, 1 - half), "s"))


def halve(values, axis, dim):
    index = lax.axis_index(axis) % 2
    return pick(values, index, dim), pick(values, 1 - index, dim)


def line_parts(values):
    return halve(values.reshape((2, 2) + values.shape[1:]), "z", 1)


def scatter_top(send, keep):
    total = add(keep, swap(send, "s"))
    total = total.reshape((4, 2) + total.shape[1:])
    return fold_line(fold(total, "x", 1))


def grad_block(left_t, right, got=None):
    total = product(left_t, right, 1, 0)
    if got is not None:
        total = total + got.astype(jnp.float32)
    return total.astype(jnp.bfloat16)


def columns_of(right, index):
    columns = right.shape[-1] // 2
    return lax.dynamic_slice_in_dim(right, index * columns, columns, right.ndim - 1)


PAIR = 2 * HD
LIMIT = 56 * 1024 * 1024


def kernel_params(steps):
    return pltpu.CompilerParams(
        dimension_semantics=("arbitrary",) * steps, vmem_limit_bytes=LIMIT
    )


def product(left, right, left_dim, right_dim):
    return lax.dot_general(
        left, right, (((left_dim,), (right_dim,)), ((), ())), preferred_element_type=jnp.float32
    )


def key_bias(facts_ref, slots):
    place = lax.broadcasted_iota(jnp.int32, (slots, 1), 0) + facts_ref[2]
    place = jnp.where(place >= slots, place - slots, place)
    return jnp.where(place < facts_ref[pl.program_id(0)], 0.0, -1e30)


def head_lanes(value, head):
    lane = lax.broadcasted_iota(jnp.int32, value.shape, 1)
    return jnp.where((lane >= HD) == (head == 1), value, jnp.zeros_like(value))


def turned(value):
    return value.astype(jnp.float32).T


def attend_kernel(facts_ref, query_ref, key_ref, value_ref, out_ref, total_ref):
    slots = key_ref.shape[0]
    bias = key_bias(facts_ref, slots)
    query = query_ref[...] * jnp.bfloat16(0.125)
    key = key_ref[...]
    value_t = turned(value_ref[...]).astype(jnp.bfloat16)
    outs = []
    for head in range(2):
        scores = product(key, head_lanes(query, head), 1, 1) + bias
        peak = jnp.max(scores, axis=0, keepdims=True)
        weight = jnp.exp(scores - peak)
        total = jnp.sum(weight, axis=0, keepdims=True)
        part = product(value_t[head * HD : (head + 1) * HD], weight.astype(jnp.bfloat16), 1, 0)
        outs.append(part * (1.0 / total))
        total_ref[0, 0, head : head + 1, :] = peak + jnp.log(total)
    out_ref[...] = jnp.concatenate(outs, axis=0).T.astype(jnp.bfloat16)


def attend_back_kernel(
    facts_ref, query_ref, key_ref, value_ref, grad_ref, total_ref, low_ref, sums_ref
):
    slots = key_ref.shape[0]
    bias = key_bias(facts_ref, slots)
    query = query_ref[...] * jnp.bfloat16(0.125)
    key = key_ref[...]
    value = value_ref[...]
    grad = grad_ref[...]
    key_t = turned(key).astype(jnp.bfloat16)
    lane = lax.broadcasted_iota(jnp.int32, (slots, PAIR), 1)
    query_parts, key_parts, value_parts = [], [], []
    for head in range(2):
        scores = product(key, head_lanes(query, head), 1, 1) + bias
        soft = jnp.exp(scores - total_ref[0, 0, head : head + 1, :])
        value_parts.append(product(soft.astype(jnp.bfloat16), grad, 1, 0))
        change = product(value, head_lanes(grad, head), 1, 1)
        inner = jnp.sum(soft * change, axis=0, keepdims=True)
        change = (soft * (change - inner)).astype(jnp.bfloat16)
        key_parts.append(product(change, query, 1, 0))
        query_parts.append(product(key_t[head * HD : (head + 1) * HD], change, 1, 0))
    pair = pl.program_id(1)
    groups = low_ref.shape[1] // 3
    query_low = (jnp.concatenate(query_parts, axis=0) * 0.125).T
    key_low = jnp.where(lane < HD, key_parts[0], key_parts[1])
    value_low = jnp.where(lane < HD, value_parts[0], value_parts[1])
    for place, part in enumerate((query_low, key_low, value_low)):
        start = pl.multiple_of(place * groups + pair * PAIR, PAIR)
        low = part.astype(jnp.bfloat16)
        low_ref[:, pl.ds(start, PAIR)] = low
        sums_ref[0, :, pl.ds(start, PAIR)] = jnp.sum(
            low.astype(jnp.float32), axis=0, keepdims=True
        )


def attention_specs(slots, pairs):
    def at(part):
        return pl.BlockSpec(
            (slots, PAIR), lambda b, g, p, *_: (b, g * 3 * pairs + part * pairs + p)
        )

    heads = pl.BlockSpec((slots, PAIR), lambda b, g, p, *_: (b, g * pairs + p))
    totals = pl.BlockSpec((1, 1, 2, slots), lambda b, g, p, *_: (b, g * pairs + p, 0, 0))
    return [at(0), at(1), at(2)], heads, totals


def attend(facts, projected, slots, wait=()):
    pairs = projected.shape[1] // (6 * PAIR)
    inputs, heads, totals = attention_specs(slots, pairs)
    rows = projected.shape[0]
    return call(
        attend_kernel,
        "attend",
        (2, 2, pairs),
        inputs,
        [heads, totals],
        [
            like((rows, 2 * pairs * PAIR), jnp.bfloat16),
            like((2, 2 * pairs, 2, slots), jnp.float32),
        ],
        facts,
        projected,
        projected,
        projected,
        wait=wait,
    )


def attend_back(facts, projected, heads_grad, totals_in, slots, own, wait=(), through=()):
    pairs = projected.shape[1] // (6 * PAIR)

    def group(facts_ref):
        return facts_ref[3] if own else 1 - facts_ref[3]

    def at(part):
        return pl.BlockSpec(
            (slots, PAIR), lambda b, p, f: (b, group(f) * 3 * pairs + part * pairs + p)
        )

    heads = pl.BlockSpec((slots, PAIR), lambda b, p, f: (b, group(f) * pairs + p))
    totals = pl.BlockSpec((1, 1, 2, slots), lambda b, p, f: (b, group(f) * pairs + p, 0, 0))
    width = 3 * pairs * PAIR
    return call(
        attend_back_kernel,
        "attend_back",
        (2, pairs),
        [at(0), at(1), at(2), heads, totals],
        [
            pl.BlockSpec((slots, width), lambda b, p, f: (b, 0)),
            pl.BlockSpec((1, 1, width), lambda b, p, f: (b, 0, 0)),
        ],
        [
            like((2 * slots, width), jnp.bfloat16),
            like((2, 1, width), jnp.float32),
        ],
        facts,
        projected,
        projected,
        projected,
        heads_grad,
        totals_in,
        wait=wait,
        through=through,
    )


def call(kernel, name, grid, inputs, outputs, shapes, facts, *args, wait=(), scratch=(), through=(), into=()):
    single = not isinstance(outputs, list)
    outputs, shapes = ([outputs], [shapes]) if single else (outputs, shapes)
    wait = tuple(into) + tuple(wait)
    count, held, passed = len(args), len(wait) + len(through), len(through)
    last = count + held + len(outputs)

    def body(facts_ref, *refs):
        kernel(facts_ref, *refs[:count], *refs[count + held : last], *refs[last + passed + 1 :])
        for place in range(facts.shape[0]):
            refs[last + passed][place] = facts_ref[place]

    results = pl.pallas_call(
        body,
        grid_spec=pltpu.PrefetchScalarGridSpec(
            num_scalar_prefetch=1,
            grid=grid,
            in_specs=list(inputs) + [pl.BlockSpec(memory_space=pl.ANY)] * held,
            out_specs=list(outputs)
            + [pl.BlockSpec(memory_space=pl.ANY)] * passed
            + [pl.BlockSpec(memory_space=pltpu.SMEM)],
            scratch_shapes=list(scratch),
        ),
        out_shape=list(shapes)
        + [like(value.shape, value.dtype) for value in through]
        + [like(facts.shape, jnp.int32)],
        input_output_aliases={
            **{1 + count + i: i for i in range(len(into))},
            **{1 + count + len(wait) + i: len(outputs) + i for i in range(passed)},
        },
        compiler_params=kernel_params(len(grid)),
        name=name,
    )(facts, *args, *wait, *through)
    values = tuple(results[:-1])
    return (values[0] if single and not passed else values), results[-1]


def block(shape, *index):
    def at(*grid_and_facts):
        return tuple(entry(*grid_and_facts) if callable(entry) else entry for entry in index)

    return pl.BlockSpec(shape, at)


def whole(array):
    zeros = (0,) * array.ndim
    return pl.BlockSpec(array.shape, lambda *_: zeros)


def first(i, *_):
    return i


def like(shape, dtype):
    return jax.ShapeDtypeStruct(shape, dtype)


def rows_in_order(facts_ref, own, beside):
    even = facts_ref[4] == 0
    pieces = []
    for z in range(4):
        pieces += [jnp.where(even, own[z], beside[z]), jnp.where(even, beside[z], own[z])]
    return jnp.concatenate(pieces, axis=0)


def near_or_far(facts_ref, refs, near):
    own, beside, below, across = [ref[...] for ref in refs]
    return rows_in_order(
        facts_ref, jnp.where(near, own, below), jnp.where(near, beside, across)
    )


def square_columns(parts, wide, steps):
    shape = parts[0].shape[:2] + (wide,)
    near = block(shape, 0, 0, lambda i, *_: jnp.minimum(i, steps - 1))
    far = block(shape, 0, 0, lambda i, *_: jnp.maximum(i - steps, 0))
    return [near, near, far, far]


def half_at(i, facts, steps):
    return jnp.where(i < steps, facts[3], 1 - facts[3])


def stack_kernel(own_at, facts_ref, own_ref, other_ref, out_ref):
    own = facts_ref[own_at] == pl.program_id(0)
    value = jnp.where(own, own_ref[...], other_ref[...])
    out_ref[...] = value.reshape(out_ref.shape)


def stack_pair(facts, own, other, wait=(), through=()):
    rows, columns = own.shape
    return call(
        partial(stack_kernel, 6),
        "stack",
        (2,),
        [whole(own), whole(other)],
        block((1, rows, columns), first, 0, 0),
        like((2, rows, columns), own.dtype),
        facts,
        own,
        other,
        wait=wait,
        through=through,
    )


def stack_line(facts, own, other, wait=()):
    _, rows, columns = own.shape
    line, facts = call(
        partial(stack_kernel, 7),
        "stack_line",
        (2,),
        [whole(own), whole(other)],
        block((2, 1, rows, columns), 0, first, 0, 0),
        like((2, 2, rows, columns), own.dtype),
        facts,
        own,
        other,
        wait=wait,
    )
    return line.reshape(4, rows, columns), facts


def turn_kernel(facts_ref, *refs):
    for i in range(2):
        refs[4 + i][...] = jnp.concatenate([refs[2 * i][...].T, refs[2 * i + 1][...].T], axis=1)


def turn_all_kernel(facts_ref, rows_ref, out_ref):
    out_ref[...] = rows_ref[...].T


def turn_all(facts, values, wait=()):
    count, width = values.shape
    step = width // 4
    return call(
        turn_all_kernel,
        "turn_all",
        (4,),
        [block((count, step), 0, first)],
        block((step, count), first, 0),
        like((width, count), values.dtype),
        facts,
        values,
        wait=wait,
    )


def turn(facts, values, others, rows, wait=()):
    count, width = values.shape
    half = width // 2
    out = block((rows, 2 * count), first, 0)
    shape = like((half, 2 * count), values.dtype)
    own = block((count, rows), 0, lambda i, f: 2 * i + f[4])
    other = block((count, rows), 0, lambda i, f: 2 * i + 1 - f[4])
    return call(
        turn_kernel,
        "turn",
        (half // rows,),
        [own, own, other, other],
        [out, out],
        [shape, shape],
        facts,
        values,
        others,
        values,
        others,
        wait=wait,
    )


def project_kernel(facts_ref, rows_ref, bias_ref, *refs):
    parts, (out_ref, in_ref, rest_ref) = refs[:4], refs[4:]
    step = pl.program_id(0)
    weight = near_or_far(facts_ref, parts, step < 4)

    @pl.when(step % 4 < 3)
    def _():
        in_ref[...] = weight
        value = product(rows_ref[...], weight, 1, 0) + bias_ref[...]
        out_ref[...] = value.astype(jnp.bfloat16)

    @pl.when(step % 4 == 3)
    def _():
        chips, count, wide = rest_ref.shape
        pairs = weight.reshape(chips, 2, count, wide // 2)
        rest_ref[...] = jnp.concatenate([pairs[:, 0], pairs[:, 1]], axis=2)


def project(facts, rows, bias, parts, wait=()):
    count, width = rows.shape
    wide = parts[0].shape[2] // 4

    def column(i, f):
        return half_at(i, f, 4) * 3 + jnp.minimum(i % 4, 2)

    out = block((count, wide), 0, column)
    rest = (8, parts[0].shape[1] // 2, 2 * wide)
    return call(
        project_kernel,
        "project",
        (8,),
        [whole(rows), block((1, wide), 0, column)] + square_columns(parts, wide, 4),
        [out, block((width, wide), 0, column), block(rest, 0, 0, lambda i, f: half_at(i, f, 4))],
        [
            like((count, 6 * wide), jnp.bfloat16),
            like((width, 6 * wide), jnp.bfloat16),
            like(rest[:2] + (4 * wide,), jnp.bfloat16),
        ],
        facts,
        rows,
        bias[None],
        *parts,
        wait=wait,
    )


def valid_rows(facts_ref, count, slots):
    place = lax.broadcasted_iota(jnp.int32, (count, 1), 0) + pl.program_id(0) * count + facts_ref[2]
    place = jnp.where(place >= slots, place - slots, place)
    return (place < facts_ref[0]).astype(jnp.float32)


def add_rows(sums_ref, rows):
    total = jnp.concatenate([jnp.sum(part, axis=0, keepdims=True) for part in rows], axis=0)
    total = jnp.concatenate([total, jnp.zeros((8 - len(rows), total.shape[1]), jnp.float32)], axis=0)

    @pl.when(pl.program_id(0) == 0)
    def _():
        sums_ref[...] = total

    @pl.when(pl.program_id(0) > 0)
    def _():
        sums_ref[...] += total


def mean_of(values):
    return jnp.mean(values, axis=-1, keepdims=True)


def attend_out_kernel(
    slots, facts_ref, own_ref, other_ref, own_weight_ref, other_weight_ref, tokens_ref, vectors_ref,
    hat_ref, rstd_ref, low_ref, sums_ref,
):
    branch = (
        product(own_ref[...], own_weight_ref[...], 1, 0)
        + product(other_ref[...], other_weight_ref[...], 1, 0)
        + vectors_ref[0:1]
    )
    tokens = tokens_ref[...].astype(jnp.float32)
    total = tokens + branch
    centered = total - mean_of(total)
    rstd = lax.rsqrt(mean_of(centered * centered) + 1e-05)
    hat = centered * rstd
    hat_ref[...] = hat
    rstd_ref[...] = rstd
    low_ref[...] = (hat * vectors_ref[1:2] + vectors_ref[2:3]).astype(jnp.bfloat16)
    valid = valid_rows(facts_ref, tokens.shape[0], slots)
    add_rows(sums_ref, [valid * tokens * tokens, valid * branch * branch])


def attend_out(facts, own, other, own_weight, other_weight, tokens, vectors, wait=()):
    slots, width = tokens.shape
    step = slots // 4
    rows = lambda array: block((step, array.shape[1]), first, 0)
    return call(
        partial(attend_out_kernel, slots),
        "attend_out",
        (4,),
        [rows(own), rows(other), whole(own_weight), whole(other_weight), rows(tokens), whole(vectors)],
        [block((step, width), first, 0), block((step, 1), first, 0), block((step, width), first, 0), block((8, width), 0, 0)],
        [
            like((slots, width), jnp.float32),
            like((slots, 1), jnp.float32),
            like((slots, width), jnp.bfloat16),
            like((8, width), jnp.float32),
        ],
        facts,
        own,
        other,
        own_weight,
        other_weight,
        tokens,
        vectors,
        wait=wait,
    )


def up_values(rows_ref, weight, bias_ref, act_ref, slope_ref, turned_ref):
    pre_act = product(rows_ref[...], weight, 1, 0) + bias_ref[...]
    below = 0.5 + 0.5 * lax.erf(pre_act * 0.7071067811865476)
    act = (pre_act * below).astype(jnp.bfloat16)
    act_ref[...] = act
    turned_ref[...] = act.T
    slope = below + pre_act * (0.3989422804014327 * jnp.exp(-0.5 * pre_act * pre_act))
    slope_ref[...] = slope.astype(jnp.bfloat16)


def up_own_kernel(facts_ref, rows_ref, bias_ref, *refs):
    parts, (act_ref, slope_ref, turned_ref, weight_ref) = refs[:4], refs[4:]
    weight = near_or_far(facts_ref, parts, pl.program_id(0) < 4)
    weight_ref[...] = weight
    up_values(rows_ref, weight, bias_ref, act_ref, slope_ref, turned_ref)


def up_other_kernel(facts_ref, rows_ref, bias_ref, weight_ref, act_ref, slope_ref, turned_ref):
    up_values(rows_ref, weight_ref[...], bias_ref, act_ref, slope_ref, turned_ref)


def up_shapes(count, units):
    shape = like((2 * count, units), jnp.bfloat16)
    return [shape, shape, like((units, 2 * count), jnp.bfloat16)]


def feed_up_own(facts, rows, bias, parts, wait=()):
    count, width = rows.shape
    units = bias.shape[0]
    wide = units // 8

    def column(i, f):
        return half_at(i, f, 4) * 4 + i % 4

    out = block((count, wide), 0, column)
    return call(
        up_own_kernel,
        "feed_up",
        (8,),
        [whole(rows), block((1, wide), 0, column)] + square_columns(parts, wide, 4),
        [out, out, block((wide, count), column, 0), block((width, wide), 0, column)],
        up_shapes(count, units) + [like((width, units), jnp.bfloat16)],
        facts,
        rows,
        bias[None],
        *parts,
        wait=wait,
    )


def feed_up_other(facts, rows, bias, weight, into, wait=()):
    count, width = rows.shape
    units = bias.shape[0]
    wide = units // 8
    out = block((count, wide), 1, first)
    return call(
        up_other_kernel,
        "feed_up_other",
        (8,),
        [whole(rows), block((1, wide), 0, first), block((width, wide), 0, first)],
        [out, out, block((wide, count), first, 1)],
        up_shapes(count, units),
        facts,
        rows,
        bias[None],
        weight,
        into=into,
        wait=wait,
    )


def down_kernel(facts_ref, rows_ref, *refs):
    parts, (weight_ref, out_ref, total_ref) = refs[:4], refs[4:]
    step = pl.program_id(0)
    own, beside, below, across = [ref[0] for ref in parts]
    even, left = facts_ref[4] == 0, facts_ref[3] == 0
    for x in range(2):
        mine = jnp.where(even, own, beside) if x == 0 else jnp.where(even, beside, own)
        theirs = jnp.where(even, below, across) if x == 0 else jnp.where(even, across, below)
        weight_ref[x] = jnp.concatenate(
            [jnp.where(left, mine, theirs), jnp.where(left, theirs, mine)], axis=1
        )
    weight = weight_ref[...].reshape(rows_ref.shape[1], out_ref.shape[1])
    value = product(rows_ref[...], weight, 1, 0)

    @pl.when(step == 0)
    def _():
        total_ref[...] = value

    @pl.when(step > 0)
    def _():
        total_ref[...] += value

    @pl.when(step == 3)
    def _():
        out_ref[...] = total_ref[...].astype(jnp.bfloat16)


def feed_down(facts, rows, parts, wait=()):
    count, units = rows.shape
    _, block_rows, half_width = parts[0].shape
    width = 2 * half_width
    shape = (1,) + parts[0].shape[1:]
    return call(
        down_kernel,
        "feed_down",
        (4,),
        [block((count // 2, units // 4), 1, first)] + [block(shape, first, 0, 0)] * 4,
        [block((2, block_rows, width), first, 0, 0), block((count // 2, width), 0, 0)],
        [like((8, block_rows, width), jnp.bfloat16), like((count // 2, width), jnp.bfloat16)],
        facts,
        rows,
        *parts,
        scratch=[pltpu.VMEM((count // 2, width), jnp.float32)],
        wait=wait,
    )


def second_norm_kernel(
    slots, facts_ref, part_ref, other_ref, hat_ref, cotangent_ref, vectors_ref,
    mixed_ref, grad_ref, low_ref, sums_ref,
):
    branch = part_ref[...] + other_ref[...].astype(jnp.float32) + vectors_ref[0:1]
    hidden = hat_ref[...] * vectors_ref[1:2] + vectors_ref[2:3]
    gain = vectors_ref[3:4]
    total = hidden + branch
    centered = total - mean_of(total)
    rstd = lax.rsqrt(mean_of(centered * centered) + 1e-05)
    hat = centered * rstd
    mixed_ref[...] = (hat * gain + vectors_ref[4:5]).astype(jnp.bfloat16)
    valid = valid_rows(facts_ref, branch.shape[0], slots)
    grad = cotangent_ref[...].astype(jnp.float32) * valid
    scaled = grad * gain
    result = rstd * (scaled - mean_of(scaled) - hat * mean_of(scaled * hat))
    low = result.astype(jnp.bfloat16)
    grad_ref[...] = result
    low_ref[...] = low
    add_rows(sums_ref, [low.astype(jnp.float32), grad * hat, grad, valid * branch * branch])


def second_norm(facts, part, other, hat, cotangent, vectors, wait=()):
    slots, width = part.shape
    step = slots // 4
    rows = block((step, width), first, 0)
    return call(
        partial(second_norm_kernel, slots),
        "second_norm",
        (4,),
        [rows, rows, rows, rows, whole(vectors)],
        [rows, rows, rows, block((8, width), 0, 0)],
        [
            like((slots, width), jnp.bfloat16),
            like((slots, width), jnp.float32),
            like((slots, width), jnp.bfloat16),
            like((8, width), jnp.float32),
        ],
        facts,
        part,
        other,
        hat,
        cotangent,
        vectors,
        wait=wait,
    )


def first_norm_kernel(
    facts_ref, part_ref, other_ref, second_ref, hat_ref, rstd_ref, vectors_ref,
    grad_ref, low_ref, sums_ref,
):
    grad = part_ref[...] + other_ref[...].astype(jnp.float32) + second_ref[...]
    hat = hat_ref[...]
    scaled = grad * vectors_ref[1:2]
    result = rstd_ref[...] * (scaled - mean_of(scaled) - hat * mean_of(scaled * hat))
    low = result.astype(jnp.bfloat16)
    grad_ref[...] = result
    low_ref[...] = low
    add_rows(sums_ref, [low.astype(jnp.float32), grad * hat, grad])


def first_norm(facts, part, other, second, hat, rstd, vectors, wait=()):
    slots, width = part.shape
    step = slots // 4
    rows = block((step, width), first, 0)
    return call(
        first_norm_kernel,
        "first_norm",
        (4,),
        [rows, rows, rows, rows, block((step, 1), first, 0), whole(vectors)],
        [rows, rows, block((8, width), 0, 0)],
        [
            like((slots, width), jnp.float32),
            like((slots, width), jnp.bfloat16),
            like((8, width), jnp.float32),
        ],
        facts,
        part,
        other,
        second,
        hat,
        rstd,
        vectors,
        wait=wait,
    )


def act_grad_kernel(facts_ref, rows_ref, weight_ref, slope_ref, out_ref, sums_ref):
    total = product(rows_ref[...], weight_ref[...], 1, 1)
    grad = total.astype(jnp.bfloat16).astype(jnp.float32) * slope_ref[...].astype(jnp.float32)
    low = grad.astype(jnp.bfloat16)
    out_ref[...] = low
    sums_ref[...] = jnp.sum(low.astype(jnp.float32), axis=0, keepdims=True)


def act_grad(facts, rows, part, weight, slope, into=(), wait=()):
    count, units = slope.shape
    step = units // 8
    out = block((count // 2, step), part, first)
    return call(
        act_grad_kernel,
        "act_grad",
        (8,),
        [whole(rows), block((step, rows.shape[1]), first, 0), out],
        [out, block((1, step), 0, first)],
        [like((count, units), jnp.bfloat16), like((1, units), jnp.float32)],
        facts,
        rows,
        weight,
        slope,
        into=into,
        wait=wait,
    )


def tokens_grad_kernel(facts_ref, mine_ref, theirs_ref, weight_ref, out_ref, sent_ref):
    wide = mine_ref.shape[1]
    slots = out_ref.shape[0]
    half = facts_ref[3]
    mine = weight_ref[:, pl.ds(pl.multiple_of(half * wide, 128), wide)]
    theirs = weight_ref[:, pl.ds(pl.multiple_of((1 - half) * wide, 128), wide)]
    total = product(mine_ref[...], mine, 1, 1) + product(theirs_ref[...], theirs, 1, 1)
    out_ref[...] = total[:slots]
    sent_ref[...] = total[slots:].astype(sent_ref.dtype)


def tokens_grad(facts, mine, theirs, weight, wait=(), through=()):
    count, columns = mine.shape
    width = weight.shape[0]
    step = width // 4
    out = block((count // 2, step), 0, first)
    return call(
        tokens_grad_kernel,
        "tokens_grad",
        (4,),
        [whole(mine), whole(theirs), block((step, 2 * columns), first, 0)],
        [out, out],
        [
            like((count // 2, width), jnp.float32),
            like((count // 2, width), jnp.bfloat16),
        ],
        facts,
        mine,
        theirs,
        weight,
        wait=wait,
        through=through,
    )


def add_parts_kernel(facts_ref, own_ref, got_ref, kept_ref, sent_ref):
    step = pl.program_id(0)
    total = own_ref[...].astype(jnp.float32) + got_ref[...].astype(jnp.float32)
    total = total.astype(jnp.bfloat16)

    @pl.when(step < 2)
    def _():
        sent_ref[...] = total

    @pl.when(step >= 2)
    def _():
        kept_ref[...] = total


def add_parts(facts, own, got, wait=(), through=()):
    _, rows, columns = own.shape
    shape = (1, rows, columns)
    part = block(shape, lambda i, f: 2 * (i % 2) + jnp.where(i < 2, 1 - f[7], f[7]), 0, 0)
    half = like((2, rows, columns), jnp.bfloat16)
    return call(
        add_parts_kernel,
        "add_parts",
        (4,),
        [part, part],
        [
            block(shape, lambda i, *_: jnp.maximum(i - 2, 0), 0, 0),
            block(shape, lambda i, *_: jnp.minimum(i, 1), 0, 0),
        ],
        [half, half],
        facts,
        own,
        got,
        wait=wait,
        through=through,
    )


def split_body(
    tokens,
    lengths,
    cotangent,
    query_weight,
    key_weight,
    value_weight,
    out_weight,
    up_weight,
    down_weight,
    query_bias,
    value_bias,
    out_bias,
    attn_gain,
    attn_shift,
    up_bias,
    down_bias,
    feed_gain,
    feed_shift,
):
    core = lax.axis_index("c")
    half = lax.axis_index("s")
    row_count, width = tokens.shape[1:]
    slots = 2 * row_count
    unit_block = down_weight.shape[0]
    units = up_bias.shape[0] // 2
    cols = width // 2
    wide = cols // 2

    def to_sequence(values):
        return jnp.concatenate([pick(values, half, 0), swap(pick(values, 1 - half, 0), "s")], axis=0)

    def from_sequence(values):
        return in_order(values[:row_count], swap(values[row_count:], "s"), half)

    small = [
        split_columns(weight, HD, core) for weight in (query_weight, key_weight, value_weight)
    ]
    large = split_columns(up_weight, unit_block, core)
    up_pair = in_order(large[0], swap(large[1], "c"), core)
    up_cols = up_pair.shape[2]
    up_mine = up_pair.reshape(-1, up_cols)
    rows = up_mine.shape[0]
    near_kept = jnp.concatenate([part[0] for part in small], axis=1)
    near_sent = jnp.concatenate([part[1] for part in small], axis=1)
    near_pair = in_order(near_kept, swap(near_sent, "c"), core)
    out_pair = jnp.concatenate([out_weight[:, :wide], out_weight[:, wide:]], axis=0)
    near_mine = jnp.concatenate([near_pair.reshape(rows, -1), out_pair], axis=1)
    line = lax.axis_index("z")
    length_own = lax.dynamic_slice_in_dim(lengths, half, 1, 0)
    facts = jnp.concatenate(
        [
            both(length_own, "c"),
            jnp.stack(
                [
                    half * row_count,
                    half,
                    lax.axis_index("x"),
                    jnp.int32(0),
                    line // 2,
                    line % 2,
                ]
            ).astype(jnp.int32),
        ]
    )
    tokens_own = to_sequence(tokens)
    cotangent_own = to_sequence(cotangent)
    (near, up_mine, down_mine), facts = stack_pair(
        facts,
        near_mine,
        line_cross(near_mine),
        wait=(tokens_own,),
        through=(up_mine, down_weight),
    )
    near, facts = stack_line(facts, near, line_next(near), wait=(cotangent_own,))
    near_parts = gather_square(near, "x")
    up_pairs, facts = stack_pair(facts, up_mine, line_cross(up_mine), wait=(near,))
    tokens_both = both(tokens_own, "c")
    up_part, facts = stack_line(
        facts, up_pairs, line_next(up_pairs), wait=(near_parts[1], near_parts[2])
    )
    up_parts = gather_square(up_part, "s")
    down_pairs, facts = stack_pair(facts, down_mine, line_cross(down_mine), wait=(up_part,))
    def halves_of(vector, size):
        return pick(vector.reshape(-1, 2, size), core, 1).reshape(-1)

    query_part = halves_of(query_bias, HD).reshape(2, wide)
    value_part = halves_of(value_bias, HD).reshape(2, wide)
    in_bias = jnp.stack([query_part, jnp.zeros_like(query_part), value_part], axis=1).reshape(-1)
    (projected, in_weight, out_own), facts = project(
        facts, tokens_both, in_bias, near_parts, wait=(down_pairs,)
    )
    out_own = out_own.reshape(cols, width)
    out_other = swap(out_own, "c")
    down_part, facts = stack_line(facts, down_pairs, line_next(down_pairs), wait=(projected,))
    down_parts = gather_square(down_part, "x")
    (heads_out, totals), facts = attend(facts, projected, slots, wait=(up_parts[2],))
    heads_other = swap(heads_out[slots:], "c")
    vectors = jnp.stack(
        [out_bias, attn_gain, attn_shift, down_bias, feed_gain, feed_shift, out_bias, out_bias]
    )
    (first_hat, first_rstd, hidden_low, first_sums), facts = attend_out(
        facts,
        heads_out,
        heads_other,
        out_own,
        out_other,
        tokens_own,
        vectors,
        wait=(up_parts[1], down_parts[2]),
    )
    hidden_from = swap(hidden_low, "c")
    (activation, slope, act_t, up_all), facts = feed_up_own(
        facts, hidden_low, halves_of(up_bias, unit_block), up_parts, wait=(down_parts[1],)
    )
    (activation, slope, act_t), facts = feed_up_other(
        facts,
        hidden_from,
        halves_of(up_bias, unit_block),
        up_all,
        into=(activation, slope, act_t),
    )
    hidden_turned, facts = turn(facts, hidden_low, hidden_from, rows, wait=(act_t,))
    (down_all, feed_sent), facts = feed_down(facts, activation, down_parts)
    down_all = down_all.reshape(units, width)
    feed_other = swap(feed_sent, "c")
    feed_part = product(activation[:slots], down_all, 1, 0)
    feed_vectors = jnp.stack(
        [down_bias, attn_gain, attn_shift, feed_gain, feed_shift, out_bias, out_bias, out_bias]
    )
    (mixed, second_grad, feed_low, second_sums), facts = second_norm(
        facts, feed_part, feed_other, first_hat, cotangent_own, feed_vectors
    )

    feed_both = both(feed_low, "c")
    (pre_grad, up_bias_own), facts = act_grad(facts, feed_low, 0, down_all, slope)
    tokens_t, facts = turn_all(facts, tokens_both, wait=(pre_grad,))
    feed_mine, feed_theirs = columns_of(feed_both, half), columns_of(feed_both, 1 - half)
    down_sent = grad_block(act_t, feed_theirs)
    down_got = swap(down_sent, "s")
    (pre_grad, up_bias_other), facts = act_grad(
        facts, feed_both[slots:], 1, down_all, slope, into=(pre_grad,), wait=(down_sent,)
    )
    up_bias_grad = up_bias_own + up_bias_other
    hidden_sent = product(pre_grad[slots:], up_all, 1, 1).astype(jnp.bfloat16)
    hidden_other = swap(hidden_sent, "c")
    hidden_own_t, hidden_other_t = hidden_turned
    up_sent = grad_block(hidden_other_t, pre_grad)
    up_got = swap(up_sent, "x")
    hidden_part = product(pre_grad[:slots], up_all, 1, 1)
    (first_grad, attn_low, third_sums), facts = first_norm(
        facts,
        hidden_part,
        hidden_other,
        second_grad,
        first_hat,
        first_rstd,
        vectors,
        wait=(up_sent,),
    )
    grad_sent = product(attn_low, out_other, 1, 1).astype(jnp.bfloat16)
    grad_other = swap(grad_sent, "c")
    grad_own = product(attn_low, out_own, 1, 1).astype(jnp.bfloat16)
    out_sent = product(heads_other, attn_low, 0, 0).astype(jnp.bfloat16)
    out_got = swap(out_sent, "c")
    heads_grad = jnp.concatenate([grad_own, grad_other], axis=0)
    (theirs_low, theirs_sums, mixed), facts = attend_back(
        facts, projected, heads_grad, totals, slots, False, wait=(out_sent,), through=(mixed,)
    )
    mixed_other = swap(mixed[row_count:], "s")
    in_sent = grad_block(tokens_t, theirs_low)
    in_got = swap(in_sent, "s")
    down_total = grad_block(act_t, feed_mine, down_got)
    down_kept, down_sent = halve(down_total.reshape(4, 2, unit_block, cols), "x", 1)
    down_got = swap(down_sent, "x")
    out_grad = grad_block(heads_out[:slots].T, attn_low, out_got)
    out_line = out_grad.reshape((4, 2 * out_weight.shape[0], width))
    out_kept, out_sent = line_parts(out_line)
    out_got = lax.ppermute(out_sent, "z", NEXT)
    (mine_low, mine_sums), facts = attend_back(
        facts, projected, heads_grad, totals, slots, True, wait=(in_sent, out_sent, down_sent)
    )
    up_total = grad_block(hidden_own_t, pre_grad, up_got).reshape(4, rows, 2 * up_cols)
    up_kept, up_sent = columns_of(up_total, half), columns_of(up_total, 1 - half)
    up_got = swap(up_sent, "s")
    out_total = add(out_kept, out_got)
    upper = lax.axis_index("z") // 2
    out_kept, out_sent = pick(out_total, upper, 0), pick(out_total, 1 - upper, 0)
    out_got = lax.ppermute(out_sent, "z", CROSS)
    valid_count = length_own[0].astype(jnp.float32) * width
    stats = jnp.stack(
        [jnp.sum(first_sums[0]), jnp.sum(first_sums[1]), jnp.sum(second_sums[3]), valid_count]
    )
    mine_sums, theirs_sums = jnp.sum(mine_sums, axis=(0, 1)), jnp.sum(theirs_sums, axis=(0, 1))
    late = in_order(mine_sums, theirs_sums, half)
    sums = jnp.concatenate(
        [
            second_sums[:3].reshape(-1),
            third_sums[:3].reshape(-1),
            jnp.pad(stats, (0, 124)),
            up_bias_grad[0],
            late[:, :wide].reshape(-1),
            late[:, 2 * wide :].reshape(-1),
        ]
    )
    sums_got = lax.ppermute(sums, "z", NEXT)
    (tokens_part, tokens_sent), facts = tokens_grad(
        facts,
        mine_low,
        theirs_low,
        in_weight,
        wait=(up_sent, out_sent, sums),
    )
    tokens_other = swap(tokens_sent, "c")
    in_total = grad_block(tokens_t, mine_low, in_got)
    in_kept, in_sent = halve(in_total.reshape(4, 2, rows, 3 * wide), "x", 1)
    in_got = swap(in_sent, "x")
    (down_pairs, down_next), facts = add_parts(
        facts, down_kept, down_got, wait=(in_sent, tokens_part)
    )
    down_got = lax.ppermute(down_next, "z", NEXT)
    (up_pairs, up_next), facts = add_parts(facts, up_kept, up_got, wait=(down_next,))
    up_got = lax.ppermute(up_next, "z", NEXT)
    (in_pairs, in_next, sums, out_kept), facts = add_parts(
        facts,
        in_kept,
        in_got,
        wait=(up_next,),
        through=(sums + sums_got, add(out_kept, out_got)),
    )
    in_sum = fold_cross(add(in_pairs, lax.ppermute(in_next, "z", NEXT)))
    tokens_grad_sum = tokens_part + tokens_other.astype(jnp.float32) + first_grad
    tokens_grad_sum = from_sequence(tokens_grad_sum.astype(jnp.bfloat16))
    mixed = in_order(mixed[:row_count], mixed_other, half)
    down_sum = fold_cross(add(down_pairs, down_got))
    up_sum = fold_cross(add(up_pairs, up_got))
    out_sum = fold_columns(fold(out_kept.reshape(2, out_weight.shape[0], width), "x", 0))

    sums = sums + lax.ppermute(sums, "z", CROSS)
    sums = sums + swap(sums, "s")
    sums = sums + swap(sums, "x")
    both_sums = in_order(sums, swap(sums, "c"), core)
    count = 6 * width + 128
    shared = both_sums[0, :count] + both_sums[1, :count]
    down_bias_grad, feed_gain_grad, feed_shift_grad, out_bias_grad, attn_gain_grad, attn_shift_grad = [
        shared[i * width : (i + 1) * width] for i in range(6)
    ]
    stats = shared[6 * width : 6 * width + 4]

    def interleave(start, size, block_size):
        sums = both_sums[:, start : start + size].reshape(2, -1, block_size)
        return sums.transpose(1, 0, 2).reshape(-1)

    up_bias_grad = interleave(count, units, unit_block)
    query_bias_grad = interleave(count + units, cols, HD)
    value_bias_gradient = interleave(count + units + cols, cols, HD)
    stream_rms = jnp.sqrt(stats[:3] / stats[3])

    def give_back(total):
        total = total.reshape((2, rows // 2) + total.shape[1:])
        return pick(total, core, 0), swap(pick(total, 1 - core, 0), "c")

    up_shares = give_back(up_sum)
    in_shares = give_back(in_sum)
    down_weight_grad = down_sum.astype(jnp.float32)
    out_weight_grad = out_sum.astype(jnp.float32)

    def merge(shares, start, size, block):
        one, two = [
            share[:, start : start + size].reshape(rows // 2, -1, block) for share in shares
        ]
        first = jnp.where(core == 0, one, two)
        second = jnp.where(core == 0, two, one)
        return jnp.stack([first, second], axis=2).reshape(rows // 2, -1).astype(jnp.float32)

    query_weight_grad = merge(in_shares, 0, wide, HD)
    key_weight_grad = merge(in_shares, wide, wide, HD)
    value_weight_grad = merge(in_shares, 2 * wide, wide, HD)
    up_weight_grad = merge(up_shares, 0, up_cols, unit_block)
    return (
        mixed,
        tokens_grad_sum,
        query_weight_grad,
        key_weight_grad,
        value_weight_grad,
        out_weight_grad,
        up_weight_grad,
        down_weight_grad,
        query_bias_grad,
        value_bias_gradient,
        out_bias_grad,
        attn_gain_grad,
        attn_shift_grad,
        up_bias_grad,
        down_bias_grad,
        feed_gain_grad,
        feed_shift_grad,
        stream_rms,
    )


def solution(mesh):
    devices = mesh.devices
    dp_count, seq_count = devices.shape
    split = seq_count == 2 and dp_count == 16
    if split:
        inner = jax.sharding.Mesh(devices.reshape(4, 2, 2, seq_count), ("z", "x", "c", "s"))
        dp, seq, body = ("z", "x", "c"), "s", split_body
    else:
        inner, dp, seq, body = mesh, "dp", "seq", general_body
    weights = (P(dp, seq),) * 6
    vectors = (P(),) * 9
    rows = P(dp, seq, None)
    in_specs = (rows, P(dp), rows) + weights + vectors
    out_specs = (rows, rows) + weights + vectors + (P(),)
    return jax.shard_map(body, mesh=inner, in_specs=in_specs, out_specs=out_specs, check_vma=False)
```

```python
from functools import partial
import math

import jax
import jax.numpy as jnp
from jax import lax
from jax.experimental import pallas as pl
from jax.experimental.pallas import tpu as pltpu
from jax.sharding import PartitionSpec as P

HD = 64


def layer_norm(values_in, gain_vector, shift_vector):
    mean_value = jnp.mean(values_in, axis=-1, keepdims=True)
    centered = values_in - mean_value
    variance = jnp.mean(centered * centered, axis=-1, keepdims=True)
    return centered * lax.rsqrt(variance + 1e-05) * gain_vector + shift_vector


def gather_weights(first, second, third, fourth, fifth, sixth):
    part = (
        lax.all_gather(first, "dp", axis=0, tiled=True),
        lax.all_gather(second, "dp", axis=0, tiled=True),
        lax.all_gather(third, "dp", axis=0, tiled=True),
        lax.all_gather(fourth, "dp", axis=0, tiled=True),
        lax.all_gather(fifth, "dp", axis=0, tiled=True),
        lax.all_gather(sixth, "dp", axis=0, tiled=True),
    )
    return (
        lax.all_gather(part[0], "seq", axis=1, tiled=True),
        lax.all_gather(part[1], "seq", axis=1, tiled=True),
        lax.all_gather(part[2], "seq", axis=1, tiled=True),
        lax.all_gather(part[3], "seq", axis=1, tiled=True),
        lax.all_gather(part[4], "seq", axis=1, tiled=True),
        lax.all_gather(part[5], "seq", axis=1, tiled=True),
    )


def reduce_grads(first, second, third, fourth, fifth, sixth):
    part = (
        lax.psum_scatter(first.astype(jnp.bfloat16), "seq", scatter_dimension=1, tiled=True).astype(
            jnp.float32
        ),
        lax.psum_scatter(
            second.astype(jnp.bfloat16), "seq", scatter_dimension=1, tiled=True
        ).astype(jnp.float32),
        lax.psum_scatter(third.astype(jnp.bfloat16), "seq", scatter_dimension=1, tiled=True).astype(
            jnp.float32
        ),
        lax.psum_scatter(
            fourth.astype(jnp.bfloat16), "seq", scatter_dimension=1, tiled=True
        ).astype(jnp.float32),
        lax.psum_scatter(fifth.astype(jnp.bfloat16), "seq", scatter_dimension=1, tiled=True).astype(
            jnp.float32
        ),
        lax.psum_scatter(sixth.astype(jnp.bfloat16), "seq", scatter_dimension=1, tiled=True).astype(
            jnp.float32
        ),
    )
    return (
        lax.psum_scatter(
            part[0].astype(jnp.bfloat16), "dp", scatter_dimension=0, tiled=True
        ).astype(jnp.float32),
        lax.psum_scatter(
            part[1].astype(jnp.bfloat16), "dp", scatter_dimension=0, tiled=True
        ).astype(jnp.float32),
        lax.psum_scatter(
            part[2].astype(jnp.bfloat16), "dp", scatter_dimension=0, tiled=True
        ).astype(jnp.float32),
        lax.psum_scatter(
            part[3].astype(jnp.bfloat16), "dp", scatter_dimension=0, tiled=True
        ).astype(jnp.float32),
        lax.psum_scatter(
            part[4].astype(jnp.bfloat16), "dp", scatter_dimension=0, tiled=True
        ).astype(jnp.float32),
        lax.psum_scatter(
            part[5].astype(jnp.bfloat16), "dp", scatter_dimension=0, tiled=True
        ).astype(jnp.float32),
    )


def block_layout(seq_count, row_count, head_count):
    block_seqs = math.gcd(seq_count, max(1, 512 // row_count))
    group_heads = math.gcd(head_count, 4)
    return (block_seqs, seq_count // block_seqs, group_heads, head_count // group_heads)


def head_slice(block_part, offset, group_width, group_heads):
    sliced = lax.dynamic_slice_in_dim(block_part, offset, group_width, 2)
    return sliced.reshape(sliced.shape[0], sliced.shape[1], group_heads, HD)


def attention_forward(queries, key_all, value_all, key_mask):
    seq_count, row_count, feature_total = queries.shape
    slot_count = key_all.shape[1]
    block_seqs, block_count, group_heads, group_count = block_layout(
        seq_count, row_count, feature_total // HD
    )
    group_width = group_heads * HD

    def seq_block(inputs):
        query_part, key_part, value_part, mask_part = inputs

        def head_block(group_index):
            offset = group_index * group_width
            query_heads = head_slice(query_part, offset, group_width, group_heads)
            key_heads = head_slice(key_part, offset, group_width, group_heads)
            value_heads = head_slice(value_part, offset, group_width, group_heads)
            scores = (
                jnp.einsum(
                    "brhd,bkhd->bhrk", query_heads, key_heads, preferred_element_type=jnp.float32
                )
                * 0.125
            )
            scores = jnp.where(mask_part[:, None, None, :], scores, -1e30)
            row_max = jnp.max(scores, axis=-1, keepdims=True)
            exponent = jnp.exp(scores - row_max)
            row_total = jnp.sum(exponent, axis=-1, keepdims=True)
            soft_probs = (exponent / row_total).astype(jnp.bfloat16)
            heads_out = jnp.einsum(
                "bhrk,bkhd->brhd", soft_probs, value_heads, preferred_element_type=jnp.float32
            )
            log_total = (row_max + jnp.log(row_total))[..., 0]
            return (heads_out.reshape(block_seqs, row_count, group_width), log_total)

        return lax.map(head_block, jnp.arange(group_count))

    outputs, log_totals = lax.map(
        seq_block,
        (
            queries.reshape(block_count, block_seqs, row_count, feature_total),
            key_all.reshape(block_count, block_seqs, slot_count, feature_total),
            value_all.reshape(block_count, block_seqs, slot_count, feature_total),
            key_mask.reshape(block_count, block_seqs, slot_count),
        ),
    )
    mixed_heads = outputs.transpose(0, 2, 3, 1, 4).reshape(seq_count, row_count, feature_total)
    return (mixed_heads, log_totals)


def attention_backward(queries, key_all, value_all, key_mask, heads_grad, log_totals):
    seq_count, row_count, feature_total = queries.shape
    slot_count = key_all.shape[1]
    block_seqs, block_count, group_heads, group_count = block_layout(
        seq_count, row_count, feature_total // HD
    )
    group_width = group_heads * HD

    def seq_block(inputs):
        query_part, key_part, value_part, mask_part, grad_part, total_part = inputs

        def head_block(group_index):
            offset = group_index * group_width
            query_heads = head_slice(query_part, offset, group_width, group_heads)
            key_heads = head_slice(key_part, offset, group_width, group_heads)
            value_heads = head_slice(value_part, offset, group_width, group_heads)
            grad_heads = head_slice(grad_part, offset, group_width, group_heads)
            log_total = lax.dynamic_index_in_dim(total_part, group_index, 0, keepdims=False)
            scores = (
                jnp.einsum(
                    "brhd,bkhd->bhrk", query_heads, key_heads, preferred_element_type=jnp.float32
                )
                * 0.125
            )
            scores = jnp.where(mask_part[:, None, None, :], scores, -1e30)
            soft_probs = jnp.exp(scores - log_total[..., None])
            value_grad = jnp.einsum(
                "bhrk,brhd->bkhd",
                soft_probs.astype(jnp.bfloat16),
                grad_heads,
                preferred_element_type=jnp.float32,
            )
            prob_grad = jnp.einsum(
                "brhd,bkhd->bhrk", grad_heads, value_heads, preferred_element_type=jnp.float32
            )
            inner = jnp.sum(soft_probs * prob_grad, axis=-1, keepdims=True)
            score_grad = (soft_probs * (prob_grad - inner)).astype(jnp.bfloat16)
            query_grad = (
                jnp.einsum(
                    "bhrk,bkhd->brhd", score_grad, key_heads, preferred_element_type=jnp.float32
                )
                * 0.125
            )
            key_grad = (
                jnp.einsum(
                    "bhrk,brhd->bkhd", score_grad, query_heads, preferred_element_type=jnp.float32
                )
                * 0.125
            )
            return (
                query_grad.reshape(block_seqs, row_count, group_width),
                key_grad.reshape(block_seqs, slot_count, group_width),
                value_grad.reshape(block_seqs, slot_count, group_width),
            )

        return lax.map(head_block, jnp.arange(group_count))

    query_blocks, key_blocks, value_block_list = lax.map(
        seq_block,
        (
            queries.reshape(block_count, block_seqs, row_count, feature_total),
            key_all.reshape(block_count, block_seqs, slot_count, feature_total),
            value_all.reshape(block_count, block_seqs, slot_count, feature_total),
            key_mask.reshape(block_count, block_seqs, slot_count),
            heads_grad.reshape(block_count, block_seqs, row_count, feature_total),
            log_totals,
        ),
    )
    query_grad = query_blocks.transpose(0, 2, 3, 1, 4).reshape(seq_count, row_count, feature_total)
    key_grad = key_blocks.transpose(0, 2, 3, 1, 4).reshape(seq_count, slot_count, feature_total)
    value_grad = value_block_list.transpose(0, 2, 3, 1, 4).reshape(
        seq_count, slot_count, feature_total
    )
    return (query_grad, key_grad, value_grad)


def general_body(
    tokens,
    lengths,
    cotangent,
    query_weight,
    key_weight,
    value_weight,
    out_weight,
    up_weight,
    down_weight,
    query_bias,
    value_bias,
    out_bias,
    attn_gain,
    attn_shift,
    up_bias,
    down_bias,
    feed_gain,
    feed_shift,
):
    seq_count, row_count, feature_total = tokens.shape
    slot_count = row_count * lax.axis_size("seq")
    token_count = seq_count * row_count
    whole = gather_weights(
        query_weight, key_weight, value_weight, out_weight, up_weight, down_weight
    )
    full_query, full_key, full_value, full_out, full_up, full_down = whole
    flat_tokens = tokens.reshape(token_count, feature_total)
    queries = (
        jnp.dot(flat_tokens, full_query, preferred_element_type=jnp.float32) + query_bias
    ).astype(jnp.bfloat16)
    key_rows = jnp.dot(flat_tokens, full_key, preferred_element_type=jnp.float32).astype(
        jnp.bfloat16
    )
    value_rows = (
        jnp.dot(flat_tokens, full_value, preferred_element_type=jnp.float32) + value_bias
    ).astype(jnp.bfloat16)
    first_slot = lax.axis_index("seq") * row_count
    key_mask = jnp.arange(slot_count)[None, :] < lengths[:, None]
    row_valid = ((first_slot + jnp.arange(row_count))[None, :] < lengths[:, None]).astype(
        jnp.float32
    )
    row_valid = row_valid.reshape(token_count, 1)
    query_blocks = queries.reshape(seq_count, row_count, feature_total)
    key_blocks = key_rows.reshape(seq_count, row_count, feature_total)
    value_block_list = value_rows.reshape(seq_count, row_count, feature_total)
    key_all, value_all = (
        lax.all_gather(key_blocks, "seq", axis=1, tiled=True),
        lax.all_gather(value_block_list, "seq", axis=1, tiled=True),
    )
    mixed_heads, log_totals = attention_forward(query_blocks, key_all, value_all, key_mask)
    heads_low = mixed_heads.reshape(token_count, feature_total).astype(jnp.bfloat16)
    attention_out = jnp.dot(heads_low, full_out, preferred_element_type=jnp.float32) + out_bias
    tokens_f32 = flat_tokens.astype(jnp.float32)
    first_sum = tokens_f32 + attention_out
    hidden, first_pull = jax.vjp(layer_norm, first_sum, attn_gain, attn_shift)
    hidden_low = hidden.astype(jnp.bfloat16)
    pre_act = jnp.dot(hidden_low, full_up, preferred_element_type=jnp.float32) + up_bias
    gelu_out, gelu_pull = jax.vjp(partial(jax.nn.gelu, approximate=False), pre_act)
    activation = gelu_out.astype(jnp.bfloat16)
    feed_out = jnp.dot(activation, full_down, preferred_element_type=jnp.float32) + down_bias
    result, second_pull = jax.vjp(layer_norm, hidden + feed_out, feed_gain, feed_shift)
    mixed = result.astype(jnp.bfloat16).reshape(seq_count, row_count, feature_total)
    partial_stats = jnp.stack(
        [
            jnp.sum(row_valid * tokens_f32 * tokens_f32),
            jnp.sum(row_valid * attention_out * attention_out),
            jnp.sum(row_valid * feed_out * feed_out),
            jnp.sum(row_valid) * feature_total,
        ]
    )
    back_weights = gather_weights(
        query_weight, key_weight, value_weight, out_weight, up_weight, down_weight
    )
    back_query, back_key, back_value, back_out, back_up, back_down = back_weights
    out_grad = cotangent.reshape(token_count, feature_total).astype(jnp.float32) * row_valid
    second_grad, feed_gain_grad, feed_shift_grad = second_pull(out_grad)
    feed_low = second_grad.astype(jnp.bfloat16)
    down_weight_grad = jnp.einsum(
        "nf,nd->fd", activation, feed_low, preferred_element_type=jnp.float32
    )
    down_bias_grad = jnp.sum(feed_low, axis=0, dtype=jnp.float32)
    act_grad = jnp.einsum(
        "nd,fd->nf", feed_low, back_down, preferred_element_type=jnp.float32
    ).astype(jnp.bfloat16)
    pre_grad = gelu_pull(act_grad.astype(jnp.float32))[0].astype(jnp.bfloat16)
    up_weight_grad = jnp.einsum(
        "nd,nf->df", hidden_low, pre_grad, preferred_element_type=jnp.float32
    )
    up_bias_grad = jnp.sum(pre_grad, axis=0, dtype=jnp.float32)
    hidden_grad = (
        jnp.einsum("nf,df->nd", pre_grad, back_up, preferred_element_type=jnp.float32) + second_grad
    )
    first_grad, attn_gain_grad, attn_shift_grad = first_pull(hidden_grad)
    attn_low = first_grad.astype(jnp.bfloat16)
    out_weight_grad = jnp.einsum(
        "nd,ne->de", heads_low, attn_low, preferred_element_type=jnp.float32
    )
    out_bias_grad = jnp.sum(attn_low, axis=0, dtype=jnp.float32)
    heads_grad = jnp.einsum(
        "ne,de->nd", attn_low, back_out, preferred_element_type=jnp.float32
    ).astype(jnp.bfloat16)
    heads_grad = heads_grad.reshape(seq_count, row_count, feature_total)
    query_grad, key_part_grad, value_part_grad = attention_backward(
        query_blocks, key_all, value_all, key_mask, heads_grad, log_totals
    )
    key_sum, value_sum = (
        lax.psum_scatter(
            key_part_grad.astype(jnp.bfloat16), "seq", scatter_dimension=1, tiled=True
        ).astype(jnp.float32),
        lax.psum_scatter(
            value_part_grad.astype(jnp.bfloat16), "seq", scatter_dimension=1, tiled=True
        ).astype(jnp.float32),
    )
    query_low = query_grad.reshape(token_count, feature_total).astype(jnp.bfloat16)
    key_low = key_sum.reshape(token_count, feature_total).astype(jnp.bfloat16)
    value_low = value_sum.reshape(token_count, feature_total).astype(jnp.bfloat16)
    query_weight_grad = jnp.einsum(
        "nd,ne->de", flat_tokens, query_low, preferred_element_type=jnp.float32
    )
    key_weight_grad = jnp.einsum(
        "nd,ne->de", flat_tokens, key_low, preferred_element_type=jnp.float32
    )
    value_weight_grad = jnp.einsum(
        "nd,ne->de", flat_tokens, value_low, preferred_element_type=jnp.float32
    )
    query_bias_grad = jnp.sum(query_low, axis=0, dtype=jnp.float32)
    value_bias_gradient = jnp.sum(value_low, axis=0, dtype=jnp.float32)
    tokens_grad = (
        jnp.einsum("ne,de->nd", query_low, back_query, preferred_element_type=jnp.float32)
        + jnp.einsum("ne,de->nd", key_low, back_key, preferred_element_type=jnp.float32)
        + jnp.einsum("ne,de->nd", value_low, back_value, preferred_element_type=jnp.float32)
        + first_grad
    )
    tokens_grad = tokens_grad.astype(jnp.bfloat16).reshape(seq_count, row_count, feature_total)
    matrix_grads = reduce_grads(
        query_weight_grad,
        key_weight_grad,
        value_weight_grad,
        out_weight_grad,
        up_weight_grad,
        down_weight_grad,
    )
    totals = lax.psum(
        (
            partial_stats,
            query_bias_grad,
            value_bias_gradient,
            out_bias_grad,
            attn_gain_grad,
            attn_shift_grad,
            up_bias_grad,
            down_bias_grad,
            feed_gain_grad,
            feed_shift_grad,
        ),
        ("dp", "seq"),
    )
    stream_rms = jnp.sqrt(totals[0][:3] / totals[0][3])
    return (
        mixed,
        tokens_grad,
        matrix_grads[0],
        matrix_grads[1],
        matrix_grads[2],
        matrix_grads[3],
        matrix_grads[4],
        matrix_grads[5],
        totals[1],
        totals[2],
        totals[3],
        totals[4],
        totals[5],
        totals[6],
        totals[7],
        totals[8],
        totals[9],
        stream_rms,
    )


def swap(value, axis):
    return lax.ppermute(value, axis, [(0, 1), (1, 0)])


def both(value, axis):
    return jnp.concatenate([value, swap(value, axis)], axis=0)


def in_order(own, other, index, axis=0):
    return jnp.where(
        index == 0, jnp.stack([own, other], axis=axis), jnp.stack([other, own], axis=axis)
    )


def split_columns(weight, width, core):
    rows = weight.shape[0]
    blocks = weight.reshape(rows, -1, 2, width)
    return pick(blocks, core, 2).reshape(rows, -1), pick(blocks, 1 - core, 2).reshape(rows, -1)


def pick(values, index, axis):
    return lax.dynamic_index_in_dim(values, index, axis, keepdims=False)


def add(left, right):
    return (left.astype(jnp.float32) + right.astype(jnp.float32)).astype(jnp.bfloat16)


def fold(values, axis, dim):
    index = lax.axis_index(axis)
    return add(pick(values, index, dim), swap(pick(values, 1 - index, dim), axis))


NEXT = [(0, 1), (1, 0), (2, 3), (3, 2)]
CROSS = [(0, 2), (2, 0), (1, 3), (3, 1)]


def fold_cross(pairs):
    upper = lax.axis_index("z") // 2
    return add(pick(pairs, upper, 0), lax.ppermute(pick(pairs, 1 - upper, 0), "z", CROSS))


def fold_line(values):
    odd = lax.axis_index("z") % 2
    pairs = values.reshape((2, 2) + values.shape[1:])
    sent = lax.ppermute(pick(pairs, 1 - odd, 1), "z", NEXT)
    return fold_cross(add(pick(pairs, odd, 1), sent))


def line_cross(value):
    return lax.ppermute(value, "z", CROSS)


def line_next(pair):
    return lax.ppermute(pair, "z", NEXT)


def gather_square(own, way):
    beside, below = swap(own, "x"), swap(own, "s")
    across = swap(below, "x") if way == "x" else swap(beside, "s")
    return [own, beside, below, across]


def fold_columns(total):
    half = lax.axis_index("s")
    return add(columns_of(total, half), swap(columns_of(total, 1 - half), "s"))


def halve(values, axis, dim):
    index = lax.axis_index(axis) % 2
    return pick(values, index, dim), pick(values, 1 - index, dim)


def line_parts(values):
    return halve(values.reshape((2, 2) + values.shape[1:]), "z", 1)


def scatter_top(send, keep):
    total = add(keep, swap(send, "s"))
    total = total.reshape((4, 2) + total.shape[1:])
    return fold_line(fold(total, "x", 1))


def grad_block(left_t, right, got=None):
    total = product(left_t, right, 1, 0)
    if got is not None:
        total = total + got.astype(jnp.float32)
    return total.astype(jnp.bfloat16)


def columns_of(right, index):
    columns = right.shape[-1] // 2
    return lax.dynamic_slice_in_dim(right, index * columns, columns, right.ndim - 1)


PAIR = 2 * HD
LIMIT = 16 * 1024 * 1024


def kernel_params(steps):
    return pltpu.CompilerParams(
        dimension_semantics=("arbitrary",) * steps, vmem_limit_bytes=LIMIT
    )


def product(left, right, left_dim, right_dim):
    return lax.dot_general(
        left, right, (((left_dim,), (right_dim,)), ((), ())), preferred_element_type=jnp.float32
    )


def key_bias(facts_ref, slots):
    place = lax.broadcasted_iota(jnp.int32, (slots, 1), 0) + facts_ref[2]
    place = jnp.where(place >= slots, place - slots, place)
    return jnp.where(place < facts_ref[pl.program_id(0)], 0.0, -1e30)


def head_lanes(value, head):
    lane = lax.broadcasted_iota(jnp.int32, value.shape, 1)
    return jnp.where((lane >= HD) == (head == 1), value, jnp.zeros_like(value))


def turned(value):
    return value.astype(jnp.float32).T


def attend_kernel(facts_ref, query_ref, key_ref, value_ref, out_ref, total_ref):
    slots = key_ref.shape[0]
    bias = key_bias(facts_ref, slots)
    query = query_ref[...] * jnp.bfloat16(0.125)
    key = key_ref[...]
    value_t = turned(value_ref[...]).astype(jnp.bfloat16)
    outs = []
    for head in range(2):
        scores = product(key, head_lanes(query, head), 1, 1) + bias
        peak = jnp.max(scores, axis=0, keepdims=True)
        weight = jnp.exp(scores - peak)
        total = jnp.sum(weight, axis=0, keepdims=True)
        part = product(value_t[head * HD : (head + 1) * HD], weight.astype(jnp.bfloat16), 1, 0)
        outs.append(part * (1.0 / total))
        total_ref[0, 0, head : head + 1, :] = peak + jnp.log(total)
    out_ref[...] = jnp.concatenate(outs, axis=0).T.astype(jnp.bfloat16)


def attend_back_kernel(
    facts_ref, query_ref, key_ref, value_ref, grad_ref, total_ref, low_ref, sums_ref
):
    slots = key_ref.shape[0]
    bias = key_bias(facts_ref, slots)
    query = query_ref[...] * jnp.bfloat16(0.125)
    key = key_ref[...]
    value = value_ref[...]
    grad = grad_ref[...]
    key_t = turned(key).astype(jnp.bfloat16)
    lane = lax.broadcasted_iota(jnp.int32, (slots, PAIR), 1)
    query_parts, key_parts, value_parts = [], [], []
    for head in range(2):
        scores = product(key, head_lanes(query, head), 1, 1) + bias
        soft = jnp.exp(scores - total_ref[0, 0, head : head + 1, :])
        value_parts.append(product(soft.astype(jnp.bfloat16), grad, 1, 0))
        change = product(value, head_lanes(grad, head), 1, 1)
        inner = jnp.sum(soft * change, axis=0, keepdims=True)
        change = (soft * (change - inner)).astype(jnp.bfloat16)
        key_parts.append(product(change, query, 1, 0))
        query_parts.append(product(key_t[head * HD : (head + 1) * HD], change, 1, 0))
    pair = pl.program_id(1)
    groups = low_ref.shape[1] // 3
    query_low = (jnp.concatenate(query_parts, axis=0) * 0.125).T
    key_low = jnp.where(lane < HD, key_parts[0], key_parts[1])
    value_low = jnp.where(lane < HD, value_parts[0], value_parts[1])
    for place, part in enumerate((query_low, key_low, value_low)):
        start = pl.multiple_of(place * groups + pair * PAIR, PAIR)
        low = part.astype(jnp.bfloat16)
        low_ref[:, pl.ds(start, PAIR)] = low
        sums_ref[0, :, pl.ds(start, PAIR)] = jnp.sum(
            low.astype(jnp.float32), axis=0, keepdims=True
        )


def attention_specs(slots, pairs):
    def at(part):
        return pl.BlockSpec(
            (slots, PAIR), lambda b, g, p, *_: (b, g * 3 * pairs + part * pairs + p)
        )

    heads = pl.BlockSpec((slots, PAIR), lambda b, g, p, *_: (b, g * pairs + p))
    totals = pl.BlockSpec((1, 1, 2, slots), lambda b, g, p, *_: (b, g * pairs + p, 0, 0))
    return [at(0), at(1), at(2)], heads, totals


def attend(facts, projected, slots, wait=()):
    pairs = projected.shape[1] // (6 * PAIR)
    inputs, heads, totals = attention_specs(slots, pairs)
    rows = projected.shape[0]
    return call(
        attend_kernel,
        "attend",
        (2, 2, pairs),
        inputs,
        [heads, totals],
        [
            like((rows, 2 * pairs * PAIR), jnp.bfloat16),
            like((2, 2 * pairs, 2, slots), jnp.float32),
        ],
        facts,
        projected,
        projected,
        projected,
        wait=wait,
    )


def attend_back(facts, projected, heads_grad, totals_in, slots, own, wait=(), through=()):
    pairs = projected.shape[1] // (6 * PAIR)

    def group(facts_ref):
        return facts_ref[3] if own else 1 - facts_ref[3]

    def at(part):
        return pl.BlockSpec(
            (slots, PAIR), lambda b, p, f: (b, group(f) * 3 * pairs + part * pairs + p)
        )

    heads = pl.BlockSpec((slots, PAIR), lambda b, p, f: (b, group(f) * pairs + p))
    totals = pl.BlockSpec((1, 1, 2, slots), lambda b, p, f: (b, group(f) * pairs + p, 0, 0))
    width = 3 * pairs * PAIR
    return call(
        attend_back_kernel,
        "attend_back",
        (2, pairs),
        [at(0), at(1), at(2), heads, totals],
        [
            pl.BlockSpec((slots, width), lambda b, p, f: (b, 0)),
            pl.BlockSpec((1, 1, width), lambda b, p, f: (b, 0, 0)),
        ],
        [
            like((2 * slots, width), jnp.bfloat16),
            like((2, 1, width), jnp.float32),
        ],
        facts,
        projected,
        projected,
        projected,
        heads_grad,
        totals_in,
        wait=wait,
        through=through,
    )


def call(kernel, name, grid, inputs, outputs, shapes, facts, *args, wait=(), scratch=(), through=(), into=()):
    single = not isinstance(outputs, list)
    outputs, shapes = ([outputs], [shapes]) if single else (outputs, shapes)
    wait = tuple(into) + tuple(wait)
    count, held, passed = len(args), len(wait) + len(through), len(through)
    last = count + held + len(outputs)

    def body(facts_ref, *refs):
        kernel(facts_ref, *refs[:count], *refs[count + held : last], *refs[last + passed + 1 :])
        for place in range(facts.shape[0]):
            refs[last + passed][place] = facts_ref[place]

    results = pl.pallas_call(
        body,
        grid_spec=pltpu.PrefetchScalarGridSpec(
            num_scalar_prefetch=1,
            grid=grid,
            in_specs=list(inputs) + [pl.BlockSpec(memory_space=pl.ANY)] * held,
            out_specs=list(outputs)
            + [pl.BlockSpec(memory_space=pl.ANY)] * passed
            + [pl.BlockSpec(memory_space=pltpu.SMEM)],
            scratch_shapes=list(scratch),
        ),
        out_shape=list(shapes)
        + [like(value.shape, value.dtype) for value in through]
        + [like(facts.shape, jnp.int32)],
        input_output_aliases={
            **{1 + count + i: i for i in range(len(into))},
            **{1 + count + len(wait) + i: len(outputs) + i for i in range(passed)},
        },
        compiler_params=kernel_params(len(grid)),
        name=name,
    )(facts, *args, *wait, *through)
    values = tuple(results[:-1])
    return (values[0] if single and not passed else values), results[-1]


def block(shape, *index):
    def at(*grid_and_facts):
        return tuple(entry(*grid_and_facts) if callable(entry) else entry for entry in index)

    return pl.BlockSpec(shape, at)


def whole(array):
    zeros = (0,) * array.ndim
    return pl.BlockSpec(array.shape, lambda *_: zeros)


def first(i, *_):
    return i


def like(shape, dtype):
    return jax.ShapeDtypeStruct(shape, dtype)


def rows_in_order(facts_ref, own, beside):
    even = facts_ref[4] == 0
    pieces = []
    for z in range(4):
        pieces += [jnp.where(even, own[z], beside[z]), jnp.where(even, beside[z], own[z])]
    return jnp.concatenate(pieces, axis=0)


def near_or_far(facts_ref, refs, near):
    own, beside, below, across = [ref[...] for ref in refs]
    return rows_in_order(
        facts_ref, jnp.where(near, own, below), jnp.where(near, beside, across)
    )


def square_columns(parts, wide, steps):
    shape = parts[0].shape[:2] + (wide,)
    near = block(shape, 0, 0, lambda i, *_: jnp.minimum(i, steps - 1))
    far = block(shape, 0, 0, lambda i, *_: jnp.maximum(i - steps, 0))
    return [near, near, far, far]


def half_at(i, facts, steps):
    return jnp.where(i < steps, facts[3], 1 - facts[3])


def stack_kernel(own_at, facts_ref, own_ref, other_ref, out_ref):
    own = facts_ref[own_at] == pl.program_id(0)
    value = jnp.where(own, own_ref[...], other_ref[...])
    out_ref[...] = value.reshape(out_ref.shape)


def stack_pair(facts, own, other, wait=(), through=()):
    rows, columns = own.shape
    return call(
        partial(stack_kernel, 6),
        "stack",
        (2,),
        [whole(own), whole(other)],
        block((1, rows, columns), first, 0, 0),
        like((2, rows, columns), own.dtype),
        facts,
        own,
        other,
        wait=wait,
        through=through,
    )


def stack_line(facts, own, other, wait=()):
    _, rows, columns = own.shape
    line, facts = call(
        partial(stack_kernel, 7),
        "stack_line",
        (2,),
        [whole(own), whole(other)],
        block((2, 1, rows, columns), 0, first, 0, 0),
        like((2, 2, rows, columns), own.dtype),
        facts,
        own,
        other,
        wait=wait,
    )
    return line.reshape(4, rows, columns), facts


def turn_kernel(facts_ref, *refs):
    for i in range(2):
        refs[4 + i][...] = jnp.concatenate([refs[2 * i][...].T, refs[2 * i + 1][...].T], axis=1)


def turn_all_kernel(facts_ref, rows_ref, out_ref):
    out_ref[...] = rows_ref[...].T


def turn_all(facts, values, wait=()):
    count, width = values.shape
    step = width // 4
    return call(
        turn_all_kernel,
        "turn_all",
        (4,),
        [block((count, step), 0, first)],
        block((step, count), first, 0),
        like((width, count), values.dtype),
        facts,
        values,
        wait=wait,
    )


def turn(facts, values, others, rows, wait=()):
    count, width = values.shape
    half = width // 2
    out = block((rows, 2 * count), first, 0)
    shape = like((half, 2 * count), values.dtype)
    own = block((count, rows), 0, lambda i, f: 2 * i + f[4])
    other = block((count, rows), 0, lambda i, f: 2 * i + 1 - f[4])
    return call(
        turn_kernel,
        "turn",
        (half // rows,),
        [own, own, other, other],
        [out, out],
        [shape, shape],
        facts,
        values,
        others,
        values,
        others,
        wait=wait,
    )


def project_kernel(facts_ref, rows_ref, bias_ref, *refs):
    parts, (out_ref, in_ref, rest_ref) = refs[:4], refs[4:]
    step = pl.program_id(0)
    weight = near_or_far(facts_ref, parts, step < 4)

    @pl.when(step % 4 < 3)
    def _():
        in_ref[...] = weight
        value = product(rows_ref[...], weight, 1, 0) + bias_ref[...]
        out_ref[...] = value.astype(jnp.bfloat16)

    @pl.when(step % 4 == 3)
    def _():
        chips, count, wide = rest_ref.shape
        pairs = weight.reshape(chips, 2, count, wide // 2)
        rest_ref[...] = jnp.concatenate([pairs[:, 0], pairs[:, 1]], axis=2)


def project(facts, rows, bias, parts, wait=()):
    count, width = rows.shape
    wide = parts[0].shape[2] // 4

    def column(i, f):
        return half_at(i, f, 4) * 3 + jnp.minimum(i % 4, 2)

    out = block((count, wide), 0, column)
    rest = (8, parts[0].shape[1] // 2, 2 * wide)
    return call(
        project_kernel,
        "project",
        (8,),
        [whole(rows), block((1, wide), 0, column)] + square_columns(parts, wide, 4),
        [out, block((width, wide), 0, column), block(rest, 0, 0, lambda i, f: half_at(i, f, 4))],
        [
            like((count, 6 * wide), jnp.bfloat16),
            like((width, 6 * wide), jnp.bfloat16),
            like(rest[:2] + (4 * wide,), jnp.bfloat16),
        ],
        facts,
        rows,
        bias[None],
        *parts,
        wait=wait,
    )


def valid_rows(facts_ref, count, slots):
    place = lax.broadcasted_iota(jnp.int32, (count, 1), 0) + pl.program_id(0) * count + facts_ref[2]
    place = jnp.where(place >= slots, place - slots, place)
    return (place < facts_ref[0]).astype(jnp.float32)


def add_rows(sums_ref, rows):
    total = jnp.concatenate([jnp.sum(part, axis=0, keepdims=True) for part in rows], axis=0)
    total = jnp.concatenate([total, jnp.zeros((8 - len(rows), total.shape[1]), jnp.float32)], axis=0)

    @pl.when(pl.program_id(0) == 0)
    def _():
        sums_ref[...] = total

    @pl.when(pl.program_id(0) > 0)
    def _():
        sums_ref[...] += total


def mean_of(values):
    return jnp.mean(values, axis=-1, keepdims=True)


def attend_out_kernel(
    slots, facts_ref, own_ref, other_ref, own_weight_ref, other_weight_ref, tokens_ref, vectors_ref,
    hat_ref, rstd_ref, low_ref, sums_ref,
):
    branch = (
        product(own_ref[...], own_weight_ref[...], 1, 0)
        + product(other_ref[...], other_weight_ref[...], 1, 0)
        + vectors_ref[0:1]
    )
    tokens = tokens_ref[...].astype(jnp.float32)
    total = tokens + branch
    centered = total - mean_of(total)
    rstd = lax.rsqrt(mean_of(centered * centered) + 1e-05)
    hat = centered * rstd
    hat_ref[...] = hat
    rstd_ref[...] = rstd
    low_ref[...] = (hat * vectors_ref[1:2] + vectors_ref[2:3]).astype(jnp.bfloat16)
    valid = valid_rows(facts_ref, tokens.shape[0], slots)
    add_rows(sums_ref, [valid * tokens * tokens, valid * branch * branch])


def attend_out(facts, own, other, own_weight, other_weight, tokens, vectors, wait=()):
    slots, width = tokens.shape
    step = slots // 4
    rows = lambda array: block((step, array.shape[1]), first, 0)
    return call(
        partial(attend_out_kernel, slots),
        "attend_out",
        (4,),
        [rows(own), rows(other), whole(own_weight), whole(other_weight), rows(tokens), whole(vectors)],
        [block((step, width), first, 0), block((step, 1), first, 0), block((step, width), first, 0), block((8, width), 0, 0)],
        [
            like((slots, width), jnp.float32),
            like((slots, 1), jnp.float32),
            like((slots, width), jnp.bfloat16),
            like((8, width), jnp.float32),
        ],
        facts,
        own,
        other,
        own_weight,
        other_weight,
        tokens,
        vectors,
        wait=wait,
    )


def up_values(rows_ref, weight, bias_ref, act_ref, slope_ref, turned_ref):
    pre_act = product(rows_ref[...], weight, 1, 0) + bias_ref[...]
    below = 0.5 + 0.5 * lax.erf(pre_act * 0.7071067811865476)
    act = (pre_act * below).astype(jnp.bfloat16)
    act_ref[...] = act
    turned_ref[...] = act.T
    slope = below + pre_act * (0.3989422804014327 * jnp.exp(-0.5 * pre_act * pre_act))
    slope_ref[...] = slope.astype(jnp.bfloat16)


def up_own_kernel(facts_ref, rows_ref, bias_ref, *refs):
    parts, (act_ref, slope_ref, turned_ref, weight_ref) = refs[:4], refs[4:]
    weight = near_or_far(facts_ref, parts, pl.program_id(0) < 4)
    weight_ref[...] = weight
    up_values(rows_ref, weight, bias_ref, act_ref, slope_ref, turned_ref)


def up_other_kernel(facts_ref, rows_ref, bias_ref, weight_ref, act_ref, slope_ref, turned_ref):
    up_values(rows_ref, weight_ref[...], bias_ref, act_ref, slope_ref, turned_ref)


def up_shapes(count, units):
    shape = like((2 * count, units), jnp.bfloat16)
    return [shape, shape, like((units, 2 * count), jnp.bfloat16)]


def feed_up_own(facts, rows, bias, parts, wait=()):
    count, width = rows.shape
    units = bias.shape[0]
    wide = units // 8

    def column(i, f):
        return half_at(i, f, 4) * 4 + i % 4

    out = block((count, wide), 0, column)
    return call(
        up_own_kernel,
        "feed_up",
        (8,),
        [whole(rows), block((1, wide), 0, column)] + square_columns(parts, wide, 4),
        [out, out, block((wide, count), column, 0), block((width, wide), 0, column)],
        up_shapes(count, units) + [like((width, units), jnp.bfloat16)],
        facts,
        rows,
        bias[None],
        *parts,
        wait=wait,
    )


def feed_up_other(facts, rows, bias, weight, into, wait=()):
    count, width = rows.shape
    units = bias.shape[0]
    wide = units // 8
    out = block((count, wide), 1, first)
    return call(
        up_other_kernel,
        "feed_up_other",
        (8,),
        [whole(rows), block((1, wide), 0, first), block((width, wide), 0, first)],
        [out, out, block((wide, count), first, 1)],
        up_shapes(count, units),
        facts,
        rows,
        bias[None],
        weight,
        into=into,
        wait=wait,
    )


def down_kernel(facts_ref, rows_ref, *refs):
    parts, (weight_ref, out_ref, total_ref) = refs[:4], refs[4:]
    step = pl.program_id(0)
    own, beside, below, across = [ref[0] for ref in parts]
    even, left = facts_ref[4] == 0, facts_ref[3] == 0
    for x in range(2):
        mine = jnp.where(even, own, beside) if x == 0 else jnp.where(even, beside, own)
        theirs = jnp.where(even, below, across) if x == 0 else jnp.where(even, across, below)
        weight_ref[x] = jnp.concatenate(
            [jnp.where(left, mine, theirs), jnp.where(left, theirs, mine)], axis=1
        )
    weight = weight_ref[...].reshape(rows_ref.shape[1], out_ref.shape[1])
    value = product(rows_ref[...], weight, 1, 0)

    @pl.when(step == 0)
    def _():
        total_ref[...] = value

    @pl.when(step > 0)
    def _():
        total_ref[...] += value

    @pl.when(step == 3)
    def _():
        out_ref[...] = total_ref[...].astype(jnp.bfloat16)


def feed_down(facts, rows, parts, wait=()):
    count, units = rows.shape
    _, block_rows, half_width = parts[0].shape
    width = 2 * half_width
    shape = (1,) + parts[0].shape[1:]
    return call(
        down_kernel,
        "feed_down",
        (4,),
        [block((count // 2, units // 4), 1, first)] + [block(shape, first, 0, 0)] * 4,
        [block((2, block_rows, width), first, 0, 0), block((count // 2, width), 0, 0)],
        [like((8, block_rows, width), jnp.bfloat16), like((count // 2, width), jnp.bfloat16)],
        facts,
        rows,
        *parts,
        scratch=[pltpu.VMEM((count // 2, width), jnp.float32)],
        wait=wait,
    )


def second_norm_kernel(
    slots, facts_ref, part_ref, other_ref, hat_ref, cotangent_ref, vectors_ref,
    mixed_ref, grad_ref, low_ref, sums_ref,
):
    branch = part_ref[...] + other_ref[...].astype(jnp.float32) + vectors_ref[0:1]
    hidden = hat_ref[...] * vectors_ref[1:2] + vectors_ref[2:3]
    gain = vectors_ref[3:4]
    total = hidden + branch
    centered = total - mean_of(total)
    rstd = lax.rsqrt(mean_of(centered * centered) + 1e-05)
    hat = centered * rstd
    mixed_ref[...] = (hat * gain + vectors_ref[4:5]).astype(jnp.bfloat16)
    valid = valid_rows(facts_ref, branch.shape[0], slots)
    grad = cotangent_ref[...].astype(jnp.float32) * valid
    scaled = grad * gain
    result = rstd * (scaled - mean_of(scaled) - hat * mean_of(scaled * hat))
    low = result.astype(jnp.bfloat16)
    grad_ref[...] = result
    low_ref[...] = low
    add_rows(sums_ref, [low.astype(jnp.float32), grad * hat, grad, valid * branch * branch])


def second_norm(facts, part, other, hat, cotangent, vectors, wait=()):
    slots, width = part.shape
    step = slots // 4
    rows = block((step, width), first, 0)
    return call(
        partial(second_norm_kernel, slots),
        "second_norm",
        (4,),
        [rows, rows, rows, rows, whole(vectors)],
        [rows, rows, rows, block((8, width), 0, 0)],
        [
            like((slots, width), jnp.bfloat16),
            like((slots, width), jnp.float32),
            like((slots, width), jnp.bfloat16),
            like((8, width), jnp.float32),
        ],
        facts,
        part,
        other,
        hat,
        cotangent,
        vectors,
        wait=wait,
    )


def first_norm_kernel(
    facts_ref, part_ref, other_ref, second_ref, hat_ref, rstd_ref, vectors_ref,
    grad_ref, low_ref, sums_ref,
):
    grad = part_ref[...] + other_ref[...].astype(jnp.float32) + second_ref[...]
    hat = hat_ref[...]
    scaled = grad * vectors_ref[1:2]
    result = rstd_ref[...] * (scaled - mean_of(scaled) - hat * mean_of(scaled * hat))
    low = result.astype(jnp.bfloat16)
    grad_ref[...] = result
    low_ref[...] = low
    add_rows(sums_ref, [low.astype(jnp.float32), grad * hat, grad])


def first_norm(facts, part, other, second, hat, rstd, vectors, wait=()):
    slots, width = part.shape
    step = slots // 4
    rows = block((step, width), first, 0)
    return call(
        first_norm_kernel,
        "first_norm",
        (4,),
        [rows, rows, rows, rows, block((step, 1), first, 0), whole(vectors)],
        [rows, rows, block((8, width), 0, 0)],
        [
            like((slots, width), jnp.float32),
            like((slots, width), jnp.bfloat16),
            like((8, width), jnp.float32),
        ],
        facts,
        part,
        other,
        second,
        hat,
        rstd,
        vectors,
        wait=wait,
    )


def act_grad_kernel(facts_ref, rows_ref, weight_ref, slope_ref, out_ref, sums_ref):
    total = product(rows_ref[...], weight_ref[...], 1, 1)
    grad = total.astype(jnp.bfloat16).astype(jnp.float32) * slope_ref[...].astype(jnp.float32)
    low = grad.astype(jnp.bfloat16)
    out_ref[...] = low
    sums_ref[...] = jnp.sum(low.astype(jnp.float32), axis=0, keepdims=True)


def act_grad(facts, rows, part, weight, slope, into=(), wait=()):
    count, units = slope.shape
    step = units // 8
    out = block((count // 2, step), part, first)
    return call(
        act_grad_kernel,
        "act_grad",
        (8,),
        [whole(rows), block((step, rows.shape[1]), first, 0), out],
        [out, block((1, step), 0, first)],
        [like((count, units), jnp.bfloat16), like((1, units), jnp.float32)],
        facts,
        rows,
        weight,
        slope,
        into=into,
        wait=wait,
    )


def tokens_grad_kernel(facts_ref, mine_ref, theirs_ref, weight_ref, out_ref, sent_ref):
    wide = mine_ref.shape[1]
    slots = out_ref.shape[0]
    half = facts_ref[3]
    mine = weight_ref[:, pl.ds(pl.multiple_of(half * wide, 128), wide)]
    theirs = weight_ref[:, pl.ds(pl.multiple_of((1 - half) * wide, 128), wide)]
    total = product(mine_ref[...], mine, 1, 1) + product(theirs_ref[...], theirs, 1, 1)
    out_ref[...] = total[:slots]
    sent_ref[...] = total[slots:].astype(sent_ref.dtype)


def tokens_grad(facts, mine, theirs, weight, wait=(), through=()):
    count, columns = mine.shape
    width = weight.shape[0]
    step = width // 4
    out = block((count // 2, step), 0, first)
    return call(
        tokens_grad_kernel,
        "tokens_grad",
        (4,),
        [whole(mine), whole(theirs), block((step, 2 * columns), first, 0)],
        [out, out],
        [
            like((count // 2, width), jnp.float32),
            like((count // 2, width), jnp.bfloat16),
        ],
        facts,
        mine,
        theirs,
        weight,
        wait=wait,
        through=through,
    )


def add_parts_kernel(facts_ref, own_ref, got_ref, kept_ref, sent_ref):
    step = pl.program_id(0)
    total = own_ref[...].astype(jnp.float32) + got_ref[...].astype(jnp.float32)
    total = total.astype(jnp.bfloat16)

    @pl.when(step < 2)
    def _():
        sent_ref[...] = total

    @pl.when(step >= 2)
    def _():
        kept_ref[...] = total


def add_parts(facts, own, got, wait=(), through=()):
    _, rows, columns = own.shape
    shape = (1, rows, columns)
    part = block(shape, lambda i, f: 2 * (i % 2) + jnp.where(i < 2, 1 - f[7], f[7]), 0, 0)
    half = like((2, rows, columns), jnp.bfloat16)
    return call(
        add_parts_kernel,
        "add_parts",
        (4,),
        [part, part],
        [
            block(shape, lambda i, *_: jnp.maximum(i - 2, 0), 0, 0),
            block(shape, lambda i, *_: jnp.minimum(i, 1), 0, 0),
        ],
        [half, half],
        facts,
        own,
        got,
        wait=wait,
        through=through,
    )


def split_body(
    tokens,
    lengths,
    cotangent,
    query_weight,
    key_weight,
    value_weight,
    out_weight,
    up_weight,
    down_weight,
    query_bias,
    value_bias,
    out_bias,
    attn_gain,
    attn_shift,
    up_bias,
    down_bias,
    feed_gain,
    feed_shift,
):
    core = lax.axis_index("c")
    half = lax.axis_index("s")
    row_count, width = tokens.shape[1:]
    slots = 2 * row_count
    unit_block = down_weight.shape[0]
    units = up_bias.shape[0] // 2
    cols = width // 2
    wide = cols // 2

    def to_sequence(values):
        return jnp.concatenate([pick(values, half, 0), swap(pick(values, 1 - half, 0), "s")], axis=0)

    def from_sequence(values):
        return in_order(values[:row_count], swap(values[row_count:], "s"), half)

    small = [
        split_columns(weight, HD, core) for weight in (query_weight, key_weight, value_weight)
    ]
    large = split_columns(up_weight, unit_block, core)
    up_pair = in_order(large[0], swap(large[1], "c"), core)
    up_cols = up_pair.shape[2]
    up_mine = up_pair.reshape(-1, up_cols)
    rows = up_mine.shape[0]
    near_kept = jnp.concatenate([part[0] for part in small], axis=1)
    near_sent = jnp.concatenate([part[1] for part in small], axis=1)
    near_pair = in_order(near_kept, swap(near_sent, "c"), core)
    out_pair = jnp.concatenate([out_weight[:, :wide], out_weight[:, wide:]], axis=0)
    near_mine = jnp.concatenate([near_pair.reshape(rows, -1), out_pair], axis=1)
    line = lax.axis_index("z")
    length_own = lax.dynamic_slice_in_dim(lengths, half, 1, 0)
    facts = jnp.concatenate(
        [
            both(length_own, "c"),
            jnp.stack(
                [
                    half * row_count,
                    half,
                    lax.axis_index("x"),
                    jnp.int32(0),
                    line // 2,
                    line % 2,
                ]
            ).astype(jnp.int32),
        ]
    )
    tokens_own = to_sequence(tokens)
    cotangent_own = to_sequence(cotangent)
    (near, up_mine, down_mine), facts = stack_pair(
        facts,
        near_mine,
        line_cross(near_mine),
        wait=(tokens_own,),
        through=(up_mine, down_weight),
    )
    near, facts = stack_line(facts, near, line_next(near), wait=(cotangent_own,))
    near_parts = gather_square(near, "x")
    up_pairs, facts = stack_pair(facts, up_mine, line_cross(up_mine), wait=(near,))
    tokens_both = both(tokens_own, "c")
    up_part, facts = stack_line(
        facts, up_pairs, line_next(up_pairs), wait=(near_parts[1], near_parts[2])
    )
    up_parts = gather_square(up_part, "s")
    down_pairs, facts = stack_pair(facts, down_mine, line_cross(down_mine), wait=(up_part,))
    def halves_of(vector, size):
        return pick(vector.reshape(-1, 2, size), core, 1).reshape(-1)

    query_part = halves_of(query_bias, HD).reshape(2, wide)
    value_part = halves_of(value_bias, HD).reshape(2, wide)
    in_bias = jnp.stack([query_part, jnp.zeros_like(query_part), value_part], axis=1).reshape(-1)
    (projected, in_weight, out_own), facts = project(
        facts, tokens_both, in_bias, near_parts, wait=(down_pairs,)
    )
    out_own = out_own.reshape(cols, width)
    out_other = swap(out_own, "c")
    down_part, facts = stack_line(facts, down_pairs, line_next(down_pairs), wait=(projected,))
    down_parts = gather_square(down_part, "x")
    (heads_out, totals), facts = attend(facts, projected, slots, wait=(up_parts[2],))
    heads_other = swap(heads_out[slots:], "c")
    vectors = jnp.stack(
        [out_bias, attn_gain, attn_shift, down_bias, feed_gain, feed_shift, out_bias, out_bias]
    )
    (first_hat, first_rstd, hidden_low, first_sums), facts = attend_out(
        facts,
        heads_out,
        heads_other,
        out_own,
        out_other,
        tokens_own,
        vectors,
        wait=(up_parts[1], down_parts[2]),
    )
    hidden_from = swap(hidden_low, "c")
    (activation, slope, act_t, up_all), facts = feed_up_own(
        facts, hidden_low, halves_of(up_bias, unit_block), up_parts, wait=(down_parts[1],)
    )
    (activation, slope, act_t), facts = feed_up_other(
        facts,
        hidden_from,
        halves_of(up_bias, unit_block),
        up_all,
        into=(activation, slope, act_t),
    )
    hidden_turned, facts = turn(facts, hidden_low, hidden_from, rows, wait=(act_t,))
    (down_all, feed_sent), facts = feed_down(facts, activation, down_parts)
    down_all = down_all.reshape(units, width)
    feed_other = swap(feed_sent, "c")
    feed_part = product(activation[:slots], down_all, 1, 0)
    feed_vectors = jnp.stack(
        [down_bias, attn_gain, attn_shift, feed_gain, feed_shift, out_bias, out_bias, out_bias]
    )
    (mixed, second_grad, feed_low, second_sums), facts = second_norm(
        facts, feed_part, feed_other, first_hat, cotangent_own, feed_vectors
    )

    feed_both = both(feed_low, "c")
    (pre_grad, up_bias_own), facts = act_grad(facts, feed_low, 0, down_all, slope)
    tokens_t, facts = turn_all(facts, tokens_both, wait=(pre_grad,))
    feed_mine, feed_theirs = columns_of(feed_both, half), columns_of(feed_both, 1 - half)
    down_sent = grad_block(act_t, feed_theirs)
    down_got = swap(down_sent, "s")
    (pre_grad, up_bias_other), facts = act_grad(
        facts, feed_both[slots:], 1, down_all, slope, into=(pre_grad,), wait=(down_sent,)
    )
    up_bias_grad = up_bias_own + up_bias_other
    hidden_sent = product(pre_grad[slots:], up_all, 1, 1).astype(jnp.bfloat16)
    hidden_other = swap(hidden_sent, "c")
    hidden_own_t, hidden_other_t = hidden_turned
    up_sent = grad_block(hidden_other_t, pre_grad)
    up_got = swap(up_sent, "x")
    hidden_part = product(pre_grad[:slots], up_all, 1, 1)
    (first_grad, attn_low, third_sums), facts = first_norm(
        facts,
        hidden_part,
        hidden_other,
        second_grad,
        first_hat,
        first_rstd,
        vectors,
        wait=(up_sent,),
    )
    grad_sent = product(attn_low, out_other, 1, 1).astype(jnp.bfloat16)
    grad_other = swap(grad_sent, "c")
    grad_own = product(attn_low, out_own, 1, 1).astype(jnp.bfloat16)
    out_sent = product(heads_other, attn_low, 0, 0).astype(jnp.bfloat16)
    out_got = swap(out_sent, "c")
    heads_grad = jnp.concatenate([grad_own, grad_other], axis=0)
    (theirs_low, theirs_sums, mixed), facts = attend_back(
        facts, projected, heads_grad, totals, slots, False, wait=(out_sent,), through=(mixed,)
    )
    mixed_other = swap(mixed[row_count:], "s")
    in_sent = grad_block(tokens_t, theirs_low)
    in_got = swap(in_sent, "s")
    down_total = grad_block(act_t, feed_mine, down_got)
    down_kept, down_sent = halve(down_total.reshape(4, 2, unit_block, cols), "x", 1)
    down_got = swap(down_sent, "x")
    out_grad = grad_block(heads_out[:slots].T, attn_low, out_got)
    out_line = out_grad.reshape((4, 2 * out_weight.shape[0], width))
    out_kept, out_sent = line_parts(out_line)
    out_got = lax.ppermute(out_sent, "z", NEXT)
    (mine_low, mine_sums), facts = attend_back(
        facts, projected, heads_grad, totals, slots, True, wait=(in_sent, out_sent, down_sent)
    )
    up_total = grad_block(hidden_own_t, pre_grad, up_got).reshape(4, rows, 2 * up_cols)
    up_kept, up_sent = columns_of(up_total, half), columns_of(up_total, 1 - half)
    up_got = swap(up_sent, "s")
    out_total = add(out_kept, out_got)
    upper = lax.axis_index("z") // 2
    out_kept, out_sent = pick(out_total, upper, 0), pick(out_total, 1 - upper, 0)
    out_got = lax.ppermute(out_sent, "z", CROSS)
    valid_count = length_own[0].astype(jnp.float32) * width
    stats = jnp.stack(
        [jnp.sum(first_sums[0]), jnp.sum(first_sums[1]), jnp.sum(second_sums[3]), valid_count]
    )
    mine_sums, theirs_sums = jnp.sum(mine_sums, axis=(0, 1)), jnp.sum(theirs_sums, axis=(0, 1))
    late = in_order(mine_sums, theirs_sums, half)
    sums = jnp.concatenate(
        [
            second_sums[:3].reshape(-1),
            third_sums[:3].reshape(-1),
            jnp.pad(stats, (0, 124)),
            up_bias_grad[0],
            late[:, :wide].reshape(-1),
            late[:, 2 * wide :].reshape(-1),
        ]
    )
    sums_got = lax.ppermute(sums, "z", NEXT)
    (tokens_part, tokens_sent), facts = tokens_grad(
        facts,
        mine_low,
        theirs_low,
        in_weight,
        wait=(up_sent, out_sent, sums),
    )
    tokens_other = swap(tokens_sent, "c")
    in_total = grad_block(tokens_t, mine_low, in_got)
    in_kept, in_sent = halve(in_total.reshape(4, 2, rows, 3 * wide), "x", 1)
    in_got = swap(in_sent, "x")
    (down_pairs, down_next), facts = add_parts(
        facts, down_kept, down_got, wait=(in_sent, tokens_part)
    )
    down_got = lax.ppermute(down_next, "z", NEXT)
    (up_pairs, up_next), facts = add_parts(facts, up_kept, up_got, wait=(down_next,))
    up_got = lax.ppermute(up_next, "z", NEXT)
    (in_pairs, in_next, sums, out_kept), facts = add_parts(
        facts,
        in_kept,
        in_got,
        wait=(up_next,),
        through=(sums + sums_got, add(out_kept, out_got)),
    )
    in_sum = fold_cross(add(in_pairs, lax.ppermute(in_next, "z", NEXT)))
    tokens_grad_sum = tokens_part + tokens_other.astype(jnp.float32) + first_grad
    tokens_grad_sum = from_sequence(tokens_grad_sum.astype(jnp.bfloat16))
    mixed = in_order(mixed[:row_count], mixed_other, half)
    down_sum = fold_cross(add(down_pairs, down_got))
    up_sum = fold_cross(add(up_pairs, up_got))
    out_sum = fold_columns(fold(out_kept.reshape(2, out_weight.shape[0], width), "x", 0))

    sums = sums + lax.ppermute(sums, "z", CROSS)
    sums = sums + swap(sums, "s")
    sums = sums + swap(sums, "x")
    both_sums = in_order(sums, swap(sums, "c"), core)
    count = 6 * width + 128
    shared = both_sums[0, :count] + both_sums[1, :count]
    down_bias_grad, feed_gain_grad, feed_shift_grad, out_bias_grad, attn_gain_grad, attn_shift_grad = [
        shared[i * width : (i + 1) * width] for i in range(6)
    ]
    stats = shared[6 * width : 6 * width + 4]

    def interleave(start, size, block_size):
        sums = both_sums[:, start : start + size].reshape(2, -1, block_size)
        return sums.transpose(1, 0, 2).reshape(-1)

    up_bias_grad = interleave(count, units, unit_block)
    query_bias_grad = interleave(count + units, cols, HD)
    value_bias_gradient = interleave(count + units + cols, cols, HD)
    stream_rms = jnp.sqrt(stats[:3] / stats[3])

    def give_back(total):
        total = total.reshape((2, rows // 2) + total.shape[1:])
        return pick(total, core, 0), swap(pick(total, 1 - core, 0), "c")

    up_shares = give_back(up_sum)
    in_shares = give_back(in_sum)
    down_weight_grad = down_sum.astype(jnp.float32)
    out_weight_grad = out_sum.astype(jnp.float32)

    def merge(shares, start, size, block):
        one, two = [
            share[:, start : start + size].reshape(rows // 2, -1, block) for share in shares
        ]
        first = jnp.where(core == 0, one, two)
        second = jnp.where(core == 0, two, one)
        return jnp.stack([first, second], axis=2).reshape(rows // 2, -1).astype(jnp.float32)

    query_weight_grad = merge(in_shares, 0, wide, HD)
    key_weight_grad = merge(in_shares, wide, wide, HD)
    value_weight_grad = merge(in_shares, 2 * wide, wide, HD)
    up_weight_grad = merge(up_shares, 0, up_cols, unit_block)
    return (
        mixed,
        tokens_grad_sum,
        query_weight_grad,
        key_weight_grad,
        value_weight_grad,
        out_weight_grad,
        up_weight_grad,
        down_weight_grad,
        query_bias_grad,
        value_bias_gradient,
        out_bias_grad,
        attn_gain_grad,
        attn_shift_grad,
        up_bias_grad,
        down_bias_grad,
        feed_gain_grad,
        feed_shift_grad,
        stream_rms,
    )


def solution(mesh):
    devices = mesh.devices
    dp_count, seq_count = devices.shape
    split = seq_count == 2 and dp_count == 16
    if split:
        inner = jax.sharding.Mesh(devices.reshape(4, 2, 2, seq_count), ("z", "x", "c", "s"))
        dp, seq, body = ("z", "x", "c"), "s", split_body
    else:
        inner, dp, seq, body = mesh, "dp", "seq", general_body
    weights = (P(dp, seq),) * 6
    vectors = (P(),) * 9
    rows = P(dp, seq, None)
    in_specs = (rows, P(dp), rows) + weights + vectors
    out_specs = (rows, rows) + weights + vectors + (P(),)
    return jax.shard_map(body, mesh=inner, in_specs=in_specs, out_specs=out_specs, check_vma=False)
```

```python
from functools import partial
import math

import jax
import jax.numpy as jnp
from jax import lax
from jax.experimental import pallas as pl
from jax.experimental.pallas import tpu as pltpu
from jax.sharding import PartitionSpec as P

HD = 64


def layer_norm(values_in, gain_vector, shift_vector):
    mean_value = jnp.mean(values_in, axis=-1, keepdims=True)
    centered = values_in - mean_value
    variance = jnp.mean(centered * centered, axis=-1, keepdims=True)
    return centered * lax.rsqrt(variance + 1e-05) * gain_vector + shift_vector


def gather_weights(first, second, third, fourth, fifth, sixth):
    part = (
        lax.all_gather(first, "dp", axis=0, tiled=True),
        lax.all_gather(second, "dp", axis=0, tiled=True),
        lax.all_gather(third, "dp", axis=0, tiled=True),
        lax.all_gather(fourth, "dp", axis=0, tiled=True),
        lax.all_gather(fifth, "dp", axis=0, tiled=True),
        lax.all_gather(sixth, "dp", axis=0, tiled=True),
    )
    return (
        lax.all_gather(part[0], "seq", axis=1, tiled=True),
        lax.all_gather(part[1], "seq", axis=1, tiled=True),
        lax.all_gather(part[2], "seq", axis=1, tiled=True),
        lax.all_gather(part[3], "seq", axis=1, tiled=True),
        lax.all_gather(part[4], "seq", axis=1, tiled=True),
        lax.all_gather(part[5], "seq", axis=1, tiled=True),
    )


def reduce_grads(first, second, third, fourth, fifth, sixth):
    part = (
        lax.psum_scatter(first.astype(jnp.bfloat16), "seq", scatter_dimension=1, tiled=True).astype(
            jnp.float32
        ),
        lax.psum_scatter(
            second.astype(jnp.bfloat16), "seq", scatter_dimension=1, tiled=True
        ).astype(jnp.float32),
        lax.psum_scatter(third.astype(jnp.bfloat16), "seq", scatter_dimension=1, tiled=True).astype(
            jnp.float32
        ),
        lax.psum_scatter(
            fourth.astype(jnp.bfloat16), "seq", scatter_dimension=1, tiled=True
        ).astype(jnp.float32),
        lax.psum_scatter(fifth.astype(jnp.bfloat16), "seq", scatter_dimension=1, tiled=True).astype(
            jnp.float32
        ),
        lax.psum_scatter(sixth.astype(jnp.bfloat16), "seq", scatter_dimension=1, tiled=True).astype(
            jnp.float32
        ),
    )
    return (
        lax.psum_scatter(
            part[0].astype(jnp.bfloat16), "dp", scatter_dimension=0, tiled=True
        ).astype(jnp.float32),
        lax.psum_scatter(
            part[1].astype(jnp.bfloat16), "dp", scatter_dimension=0, tiled=True
        ).astype(jnp.float32),
        lax.psum_scatter(
            part[2].astype(jnp.bfloat16), "dp", scatter_dimension=0, tiled=True
        ).astype(jnp.float32),
        lax.psum_scatter(
            part[3].astype(jnp.bfloat16), "dp", scatter_dimension=0, tiled=True
        ).astype(jnp.float32),
        lax.psum_scatter(
            part[4].astype(jnp.bfloat16), "dp", scatter_dimension=0, tiled=True
        ).astype(jnp.float32),
        lax.psum_scatter(
            part[5].astype(jnp.bfloat16), "dp", scatter_dimension=0, tiled=True
        ).astype(jnp.float32),
    )


def block_layout(seq_count, row_count, head_count):
    block_seqs = math.gcd(seq_count, max(1, 512 // row_count))
    group_heads = math.gcd(head_count, 4)
    return (block_seqs, seq_count // block_seqs, group_heads, head_count // group_heads)


def head_slice(block_part, offset, group_width, group_heads):
    sliced = lax.dynamic_slice_in_dim(block_part, offset, group_width, 2)
    return sliced.reshape(sliced.shape[0], sliced.shape[1], group_heads, HD)


def attention_forward(queries, key_all, value_all, key_mask):
    seq_count, row_count, feature_total = queries.shape
    slot_count = key_all.shape[1]
    block_seqs, block_count, group_heads, group_count = block_layout(
        seq_count, row_count, feature_total // HD
    )
    group_width = group_heads * HD

    def seq_block(inputs):
        query_part, key_part, value_part, mask_part = inputs

        def head_block(group_index):
            offset = group_index * group_width
            query_heads = head_slice(query_part, offset, group_width, group_heads)
            key_heads = head_slice(key_part, offset, group_width, group_heads)
            value_heads = head_slice(value_part, offset, group_width, group_heads)
            scores = (
                jnp.einsum(
                    "brhd,bkhd->bhrk", query_heads, key_heads, preferred_element_type=jnp.float32
                )
                * 0.125
            )
            scores = jnp.where(mask_part[:, None, None, :], scores, -1e30)
            row_max = jnp.max(scores, axis=-1, keepdims=True)
            exponent = jnp.exp(scores - row_max)
            row_total = jnp.sum(exponent, axis=-1, keepdims=True)
            soft_probs = (exponent / row_total).astype(jnp.bfloat16)
            heads_out = jnp.einsum(
                "bhrk,bkhd->brhd", soft_probs, value_heads, preferred_element_type=jnp.float32
            )
            log_total = (row_max + jnp.log(row_total))[..., 0]
            return (heads_out.reshape(block_seqs, row_count, group_width), log_total)

        return lax.map(head_block, jnp.arange(group_count))

    outputs, log_totals = lax.map(
        seq_block,
        (
            queries.reshape(block_count, block_seqs, row_count, feature_total),
            key_all.reshape(block_count, block_seqs, slot_count, feature_total),
            value_all.reshape(block_count, block_seqs, slot_count, feature_total),
            key_mask.reshape(block_count, block_seqs, slot_count),
        ),
    )
    mixed_heads = outputs.transpose(0, 2, 3, 1, 4).reshape(seq_count, row_count, feature_total)
    return (mixed_heads, log_totals)


def attention_backward(queries, key_all, value_all, key_mask, heads_grad, log_totals):
    seq_count, row_count, feature_total = queries.shape
    slot_count = key_all.shape[1]
    block_seqs, block_count, group_heads, group_count = block_layout(
        seq_count, row_count, feature_total // HD
    )
    group_width = group_heads * HD

    def seq_block(inputs):
        query_part, key_part, value_part, mask_part, grad_part, total_part = inputs

        def head_block(group_index):
            offset = group_index * group_width
            query_heads = head_slice(query_part, offset, group_width, group_heads)
            key_heads = head_slice(key_part, offset, group_width, group_heads)
            value_heads = head_slice(value_part, offset, group_width, group_heads)
            grad_heads = head_slice(grad_part, offset, group_width, group_heads)
            log_total = lax.dynamic_index_in_dim(total_part, group_index, 0, keepdims=False)
            scores = (
                jnp.einsum(
                    "brhd,bkhd->bhrk", query_heads, key_heads, preferred_element_type=jnp.float32
                )
                * 0.125
            )
            scores = jnp.where(mask_part[:, None, None, :], scores, -1e30)
            soft_probs = jnp.exp(scores - log_total[..., None])
            value_grad = jnp.einsum(
                "bhrk,brhd->bkhd",
                soft_probs.astype(jnp.bfloat16),
                grad_heads,
                preferred_element_type=jnp.float32,
            )
            prob_grad = jnp.einsum(
                "brhd,bkhd->bhrk", grad_heads, value_heads, preferred_element_type=jnp.float32
            )
            inner = jnp.sum(soft_probs * prob_grad, axis=-1, keepdims=True)
            score_grad = (soft_probs * (prob_grad - inner)).astype(jnp.bfloat16)
            query_grad = (
                jnp.einsum(
                    "bhrk,bkhd->brhd", score_grad, key_heads, preferred_element_type=jnp.float32
                )
                * 0.125
            )
            key_grad = (
                jnp.einsum(
                    "bhrk,brhd->bkhd", score_grad, query_heads, preferred_element_type=jnp.float32
                )
                * 0.125
            )
            return (
                query_grad.reshape(block_seqs, row_count, group_width),
                key_grad.reshape(block_seqs, slot_count, group_width),
                value_grad.reshape(block_seqs, slot_count, group_width),
            )

        return lax.map(head_block, jnp.arange(group_count))

    query_blocks, key_blocks, value_block_list = lax.map(
        seq_block,
        (
            queries.reshape(block_count, block_seqs, row_count, feature_total),
            key_all.reshape(block_count, block_seqs, slot_count, feature_total),
            value_all.reshape(block_count, block_seqs, slot_count, feature_total),
            key_mask.reshape(block_count, block_seqs, slot_count),
            heads_grad.reshape(block_count, block_seqs, row_count, feature_total),
            log_totals,
        ),
    )
    query_grad = query_blocks.transpose(0, 2, 3, 1, 4).reshape(seq_count, row_count, feature_total)
    key_grad = key_blocks.transpose(0, 2, 3, 1, 4).reshape(seq_count, slot_count, feature_total)
    value_grad = value_block_list.transpose(0, 2, 3, 1, 4).reshape(
        seq_count, slot_count, feature_total
    )
    return (query_grad, key_grad, value_grad)


def general_body(
    tokens,
    lengths,
    cotangent,
    query_weight,
    key_weight,
    value_weight,
    out_weight,
    up_weight,
    down_weight,
    query_bias,
    value_bias,
    out_bias,
    attn_gain,
    attn_shift,
    up_bias,
    down_bias,
    feed_gain,
    feed_shift,
):
    seq_count, row_count, feature_total = tokens.shape
    slot_count = row_count * lax.axis_size("seq")
    token_count = seq_count * row_count
    whole = gather_weights(
        query_weight, key_weight, value_weight, out_weight, up_weight, down_weight
    )
    full_query, full_key, full_value, full_out, full_up, full_down = whole
    flat_tokens = tokens.reshape(token_count, feature_total)
    queries = (
        jnp.dot(flat_tokens, full_query, preferred_element_type=jnp.float32) + query_bias
    ).astype(jnp.bfloat16)
    key_rows = jnp.dot(flat_tokens, full_key, preferred_element_type=jnp.float32).astype(
        jnp.bfloat16
    )
    value_rows = (
        jnp.dot(flat_tokens, full_value, preferred_element_type=jnp.float32) + value_bias
    ).astype(jnp.bfloat16)
    first_slot = lax.axis_index("seq") * row_count
    key_mask = jnp.arange(slot_count)[None, :] < lengths[:, None]
    row_valid = ((first_slot + jnp.arange(row_count))[None, :] < lengths[:, None]).astype(
        jnp.float32
    )
    row_valid = row_valid.reshape(token_count, 1)
    query_blocks = queries.reshape(seq_count, row_count, feature_total)
    key_blocks = key_rows.reshape(seq_count, row_count, feature_total)
    value_block_list = value_rows.reshape(seq_count, row_count, feature_total)
    key_all, value_all = (
        lax.all_gather(key_blocks, "seq", axis=1, tiled=True),
        lax.all_gather(value_block_list, "seq", axis=1, tiled=True),
    )
    mixed_heads, log_totals = attention_forward(query_blocks, key_all, value_all, key_mask)
    heads_low = mixed_heads.reshape(token_count, feature_total).astype(jnp.bfloat16)
    attention_out = jnp.dot(heads_low, full_out, preferred_element_type=jnp.float32) + out_bias
    tokens_f32 = flat_tokens.astype(jnp.float32)
    first_sum = tokens_f32 + attention_out
    hidden, first_pull = jax.vjp(layer_norm, first_sum, attn_gain, attn_shift)
    hidden_low = hidden.astype(jnp.bfloat16)
    pre_act = jnp.dot(hidden_low, full_up, preferred_element_type=jnp.float32) + up_bias
    gelu_out, gelu_pull = jax.vjp(partial(jax.nn.gelu, approximate=False), pre_act)
    activation = gelu_out.astype(jnp.bfloat16)
    feed_out = jnp.dot(activation, full_down, preferred_element_type=jnp.float32) + down_bias
    result, second_pull = jax.vjp(layer_norm, hidden + feed_out, feed_gain, feed_shift)
    mixed = result.astype(jnp.bfloat16).reshape(seq_count, row_count, feature_total)
    partial_stats = jnp.stack(
        [
            jnp.sum(row_valid * tokens_f32 * tokens_f32),
            jnp.sum(row_valid * attention_out * attention_out),
            jnp.sum(row_valid * feed_out * feed_out),
            jnp.sum(row_valid) * feature_total,
        ]
    )
    back_weights = gather_weights(
        query_weight, key_weight, value_weight, out_weight, up_weight, down_weight
    )
    back_query, back_key, back_value, back_out, back_up, back_down = back_weights
    out_grad = cotangent.reshape(token_count, feature_total).astype(jnp.float32) * row_valid
    second_grad, feed_gain_grad, feed_shift_grad = second_pull(out_grad)
    feed_low = second_grad.astype(jnp.bfloat16)
    down_weight_grad = jnp.einsum(
        "nf,nd->fd", activation, feed_low, preferred_element_type=jnp.float32
    )
    down_bias_grad = jnp.sum(feed_low, axis=0, dtype=jnp.float32)
    act_grad = jnp.einsum(
        "nd,fd->nf", feed_low, back_down, preferred_element_type=jnp.float32
    ).astype(jnp.bfloat16)
    pre_grad = gelu_pull(act_grad.astype(jnp.float32))[0].astype(jnp.bfloat16)
    up_weight_grad = jnp.einsum(
        "nd,nf->df", hidden_low, pre_grad, preferred_element_type=jnp.float32
    )
    up_bias_grad = jnp.sum(pre_grad, axis=0, dtype=jnp.float32)
    hidden_grad = (
        jnp.einsum("nf,df->nd", pre_grad, back_up, preferred_element_type=jnp.float32) + second_grad
    )
    first_grad, attn_gain_grad, attn_shift_grad = first_pull(hidden_grad)
    attn_low = first_grad.astype(jnp.bfloat16)
    out_weight_grad = jnp.einsum(
        "nd,ne->de", heads_low, attn_low, preferred_element_type=jnp.float32
    )
    out_bias_grad = jnp.sum(attn_low, axis=0, dtype=jnp.float32)
    heads_grad = jnp.einsum(
        "ne,de->nd", attn_low, back_out, preferred_element_type=jnp.float32
    ).astype(jnp.bfloat16)
    heads_grad = heads_grad.reshape(seq_count, row_count, feature_total)
    query_grad, key_part_grad, value_part_grad = attention_backward(
        query_blocks, key_all, value_all, key_mask, heads_grad, log_totals
    )
    key_sum, value_sum = (
        lax.psum_scatter(
            key_part_grad.astype(jnp.bfloat16), "seq", scatter_dimension=1, tiled=True
        ).astype(jnp.float32),
        lax.psum_scatter(
            value_part_grad.astype(jnp.bfloat16), "seq", scatter_dimension=1, tiled=True
        ).astype(jnp.float32),
    )
    query_low = query_grad.reshape(token_count, feature_total).astype(jnp.bfloat16)
    key_low = key_sum.reshape(token_count, feature_total).astype(jnp.bfloat16)
    value_low = value_sum.reshape(token_count, feature_total).astype(jnp.bfloat16)
    query_weight_grad = jnp.einsum(
        "nd,ne->de", flat_tokens, query_low, preferred_element_type=jnp.float32
    )
    key_weight_grad = jnp.einsum(
        "nd,ne->de", flat_tokens, key_low, preferred_element_type=jnp.float32
    )
    value_weight_grad = jnp.einsum(
        "nd,ne->de", flat_tokens, value_low, preferred_element_type=jnp.float32
    )
    query_bias_grad = jnp.sum(query_low, axis=0, dtype=jnp.float32)
    value_bias_gradient = jnp.sum(value_low, axis=0, dtype=jnp.float32)
    tokens_grad = (
        jnp.einsum("ne,de->nd", query_low, back_query, preferred_element_type=jnp.float32)
        + jnp.einsum("ne,de->nd", key_low, back_key, preferred_element_type=jnp.float32)
        + jnp.einsum("ne,de->nd", value_low, back_value, preferred_element_type=jnp.float32)
        + first_grad
    )
    tokens_grad = tokens_grad.astype(jnp.bfloat16).reshape(seq_count, row_count, feature_total)
    matrix_grads = reduce_grads(
        query_weight_grad,
        key_weight_grad,
        value_weight_grad,
        out_weight_grad,
        up_weight_grad,
        down_weight_grad,
    )
    totals = lax.psum(
        (
            partial_stats,
            query_bias_grad,
            value_bias_gradient,
            out_bias_grad,
            attn_gain_grad,
            attn_shift_grad,
            up_bias_grad,
            down_bias_grad,
            feed_gain_grad,
            feed_shift_grad,
        ),
        ("dp", "seq"),
    )
    stream_rms = jnp.sqrt(totals[0][:3] / totals[0][3])
    return (
        mixed,
        tokens_grad,
        matrix_grads[0],
        matrix_grads[1],
        matrix_grads[2],
        matrix_grads[3],
        matrix_grads[4],
        matrix_grads[5],
        totals[1],
        totals[2],
        totals[3],
        totals[4],
        totals[5],
        totals[6],
        totals[7],
        totals[8],
        totals[9],
        stream_rms,
    )


def swap(value, axis):
    return lax.ppermute(value, axis, [(0, 1), (1, 0)])


def both(value, axis):
    return jnp.concatenate([value, swap(value, axis)], axis=0)


def in_order(own, other, index, axis=0):
    return jnp.where(
        index == 0, jnp.stack([own, other], axis=axis), jnp.stack([other, own], axis=axis)
    )


def pick(values, index, axis):
    return lax.dynamic_index_in_dim(values, index, axis, keepdims=False)


def add(left, right):
    return (left.astype(jnp.float32) + right.astype(jnp.float32)).astype(jnp.bfloat16)


def fold(values, axis, dim):
    index = lax.axis_index(axis)
    return add(pick(values, index, dim), swap(pick(values, 1 - index, dim), axis))


NEXT = [(0, 1), (1, 0), (2, 3), (3, 2)]
CROSS = [(0, 2), (2, 0), (1, 3), (3, 1)]


def fold_cross(pairs):
    upper = lax.axis_index("z") // 2
    return add(pick(pairs, upper, 0), lax.ppermute(pick(pairs, 1 - upper, 0), "z", CROSS))


def fold_line(values):
    odd = lax.axis_index("z") % 2
    pairs = values.reshape((2, 2) + values.shape[1:])
    sent = lax.ppermute(pick(pairs, 1 - odd, 1), "z", NEXT)
    return fold_cross(add(pick(pairs, odd, 1), sent))


def line_cross(value):
    return lax.ppermute(value, "z", CROSS)


def line_next(pair):
    return lax.ppermute(pair, "z", NEXT)


def gather_square(own, way):
    beside, below = swap(own, "x"), swap(own, "s")
    across = swap(below, "x") if way == "x" else swap(beside, "s")
    return [own, beside, below, across]


def fold_columns(total):
    half = lax.axis_index("s")
    return add(columns_of(total, half), swap(columns_of(total, 1 - half), "s"))


def halve(values, axis, dim):
    index = lax.axis_index(axis) % 2
    return pick(values, index, dim), pick(values, 1 - index, dim)


def line_parts(values):
    return halve(values.reshape((2, 2) + values.shape[1:]), "z", 1)


def scatter_top(send, keep):
    total = add(keep, swap(send, "s"))
    total = total.reshape((4, 2) + total.shape[1:])
    return fold_line(fold(total, "x", 1))


def grad_block(left_t, right, got=None):
    total = product(left_t, right, 1, 0)
    if got is not None:
        total = total + got.astype(jnp.float32)
    return total.astype(jnp.bfloat16)


def columns_of(right, index):
    columns = right.shape[-1] // 2
    return lax.dynamic_slice_in_dim(right, index * columns, columns, right.ndim - 1)


PAIR = 2 * HD
LIMIT = 16 * 1024 * 1024


def kernel_params(steps):
    return pltpu.CompilerParams(
        dimension_semantics=("arbitrary",) * steps, vmem_limit_bytes=LIMIT
    )


def product(left, right, left_dim, right_dim):
    return lax.dot_general(
        left, right, (((left_dim,), (right_dim,)), ((), ())), preferred_element_type=jnp.float32
    )


def key_bias(facts_ref, slots):
    place = lax.broadcasted_iota(jnp.int32, (slots, 1), 0) + facts_ref[2]
    place = jnp.where(place >= slots, place - slots, place)
    return jnp.where(place < facts_ref[pl.program_id(0)], 0.0, -1e30)


def head_lanes(value, head):
    lane = lax.broadcasted_iota(jnp.int32, value.shape, 1)
    return jnp.where((lane >= HD) == (head == 1), value, jnp.zeros_like(value))


def turned(value):
    return value.astype(jnp.float32).T


def attend_kernel(facts_ref, query_ref, key_ref, value_ref, out_ref, total_ref):
    slots = key_ref.shape[0]
    bias = key_bias(facts_ref, slots)
    query = query_ref[...] * jnp.bfloat16(0.125)
    key = key_ref[...]
    value_t = turned(value_ref[...]).astype(jnp.bfloat16)
    outs = []
    for head in range(2):
        scores = product(key, head_lanes(query, head), 1, 1) + bias
        peak = jnp.max(scores, axis=0, keepdims=True)
        weight = jnp.exp(scores - peak)
        total = jnp.sum(weight, axis=0, keepdims=True)
        part = product(value_t[head * HD : (head + 1) * HD], weight.astype(jnp.bfloat16), 1, 0)
        outs.append(part * (1.0 / total))
        total_ref[0, 0, head : head + 1, :] = peak + jnp.log(total)
    out_ref[...] = jnp.concatenate(outs, axis=0).T.astype(jnp.bfloat16)


def attend_back_kernel(
    facts_ref, query_ref, key_ref, value_ref, grad_ref, total_ref, low_ref, sums_ref
):
    slots = key_ref.shape[0]
    bias = key_bias(facts_ref, slots)
    query = query_ref[...] * jnp.bfloat16(0.125)
    key = key_ref[...]
    value = value_ref[...]
    grad = grad_ref[...]
    key_t = turned(key).astype(jnp.bfloat16)
    lane = lax.broadcasted_iota(jnp.int32, (slots, PAIR), 1)
    query_parts, key_parts, value_parts = [], [], []
    for head in range(2):
        scores = product(key, head_lanes(query, head), 1, 1) + bias
        soft = jnp.exp(scores - total_ref[0, 0, head : head + 1, :])
        value_parts.append(product(soft.astype(jnp.bfloat16), grad, 1, 0))
        change = product(value, head_lanes(grad, head), 1, 1)
        inner = jnp.sum(soft * change, axis=0, keepdims=True)
        change = (soft * (change - inner)).astype(jnp.bfloat16)
        key_parts.append(product(change, query, 1, 0))
        query_parts.append(product(key_t[head * HD : (head + 1) * HD], change, 1, 0))
    pair = pl.program_id(1)
    groups = low_ref.shape[1] // 3
    query_low = (jnp.concatenate(query_parts, axis=0) * 0.125).T
    key_low = jnp.where(lane < HD, key_parts[0], key_parts[1])
    value_low = jnp.where(lane < HD, value_parts[0], value_parts[1])
    for place, part in enumerate((query_low, key_low, value_low)):
        start = pl.multiple_of(place * groups + pair * PAIR, PAIR)
        low = part.astype(jnp.bfloat16)
        low_ref[:, pl.ds(start, PAIR)] = low
        sums_ref[0, :, pl.ds(start, PAIR)] = jnp.sum(
            low.astype(jnp.float32), axis=0, keepdims=True
        )


def attention_specs(slots, pairs):
    def at(part):
        return pl.BlockSpec(
            (slots, PAIR), lambda b, g, p, *_: (b, g * 3 * pairs + part * pairs + p)
        )

    heads = pl.BlockSpec((slots, PAIR), lambda b, g, p, *_: (b, g * pairs + p))
    totals = pl.BlockSpec((1, 1, 2, slots), lambda b, g, p, *_: (b, g * pairs + p, 0, 0))
    return [at(0), at(1), at(2)], heads, totals


def attend(facts, projected, slots, wait=()):
    pairs = projected.shape[1] // (6 * PAIR)
    inputs, heads, totals = attention_specs(slots, pairs)
    rows = projected.shape[0]
    return call(
        attend_kernel,
        "attend",
        (2, 2, pairs),
        inputs,
        [heads, totals],
        [
            like((rows, 2 * pairs * PAIR), jnp.bfloat16),
            like((2, 2 * pairs, 2, slots), jnp.float32),
        ],
        facts,
        projected,
        projected,
        projected,
        wait=wait,
    )


def attend_back(facts, projected, heads_grad, totals_in, slots, own, wait=(), through=()):
    pairs = projected.shape[1] // (6 * PAIR)

    def group(facts_ref):
        return facts_ref[3] if own else 1 - facts_ref[3]

    def at(part):
        return pl.BlockSpec(
            (slots, PAIR), lambda b, p, f: (b, group(f) * 3 * pairs + part * pairs + p)
        )

    heads = pl.BlockSpec((slots, PAIR), lambda b, p, f: (b, group(f) * pairs + p))
    totals = pl.BlockSpec((1, 1, 2, slots), lambda b, p, f: (b, group(f) * pairs + p, 0, 0))
    width = 3 * pairs * PAIR
    return call(
        attend_back_kernel,
        "attend_back",
        (2, pairs),
        [at(0), at(1), at(2), heads, totals],
        [
            pl.BlockSpec((slots, width), lambda b, p, f: (b, 0)),
            pl.BlockSpec((1, 1, width), lambda b, p, f: (b, 0, 0)),
        ],
        [
            like((2 * slots, width), jnp.bfloat16),
            like((2, 1, width), jnp.float32),
        ],
        facts,
        projected,
        projected,
        projected,
        heads_grad,
        totals_in,
        wait=wait,
        through=through,
    )


def call(kernel, name, grid, inputs, outputs, shapes, facts, *args, wait=(), scratch=(), through=(), into=()):
    single = not isinstance(outputs, list)
    outputs, shapes = ([outputs], [shapes]) if single else (outputs, shapes)
    wait = tuple(into) + tuple(wait)
    count, held, passed = len(args), len(wait) + len(through), len(through)
    last = count + held + len(outputs)

    def body(facts_ref, *refs):
        kernel(facts_ref, *refs[:count], *refs[count + held : last], *refs[last + passed + 1 :])
        for place in range(facts.shape[0]):
            refs[last + passed][place] = facts_ref[place]

    results = pl.pallas_call(
        body,
        grid_spec=pltpu.PrefetchScalarGridSpec(
            num_scalar_prefetch=1,
            grid=grid,
            in_specs=list(inputs) + [pl.BlockSpec(memory_space=pl.ANY)] * held,
            out_specs=list(outputs)
            + [pl.BlockSpec(memory_space=pl.ANY)] * passed
            + [pl.BlockSpec(memory_space=pltpu.SMEM)],
            scratch_shapes=list(scratch),
        ),
        out_shape=list(shapes)
        + [like(value.shape, value.dtype) for value in through]
        + [like(facts.shape, jnp.int32)],
        input_output_aliases={
            **{1 + count + i: i for i in range(len(into))},
            **{1 + count + len(wait) + i: len(outputs) + i for i in range(passed)},
        },
        compiler_params=kernel_params(len(grid)),
        name=name,
    )(facts, *args, *wait, *through)
    values = tuple(results[:-1])
    return (values[0] if single and not passed else values), results[-1]


def block(shape, *index):
    def at(*grid_and_facts):
        return tuple(entry(*grid_and_facts) if callable(entry) else entry for entry in index)

    return pl.BlockSpec(shape, at)


def whole(array):
    zeros = (0,) * array.ndim
    return pl.BlockSpec(array.shape, lambda *_: zeros)


def first(i, *_):
    return i


def like(shape, dtype):
    return jax.ShapeDtypeStruct(shape, dtype)


def rows_in_order(facts_ref, own, beside):
    even = facts_ref[4] == 0
    pieces = []
    for z in range(4):
        pieces += [jnp.where(even, own[z], beside[z]), jnp.where(even, beside[z], own[z])]
    return jnp.concatenate(pieces, axis=0)


def near_or_far(facts_ref, refs, near):
    own, beside, below, across = [ref[...] for ref in refs]
    return rows_in_order(
        facts_ref, jnp.where(near, own, below), jnp.where(near, beside, across)
    )


def square_columns(parts, wide, steps):
    shape = parts[0].shape[:2] + (wide,)
    near = block(shape, 0, 0, lambda i, *_: jnp.minimum(i, steps - 1))
    far = block(shape, 0, 0, lambda i, *_: jnp.maximum(i - steps, 0))
    return [near, near, far, far]


def half_at(i, facts, steps):
    return jnp.where(i < steps, facts[3], 1 - facts[3])


def stack_kernel(own_at, facts_ref, own_ref, other_ref, out_ref):
    own = facts_ref[own_at] == pl.program_id(0)
    value = jnp.where(own, own_ref[...], other_ref[...])
    out_ref[...] = value.reshape(out_ref.shape)


def stack_pair(facts, own, other, wait=(), through=()):
    rows, columns = own.shape
    return call(
        partial(stack_kernel, 6),
        "stack",
        (2,),
        [whole(own), whole(other)],
        block((1, rows, columns), first, 0, 0),
        like((2, rows, columns), own.dtype),
        facts,
        own,
        other,
        wait=wait,
        through=through,
    )


def stack_line(facts, own, other, wait=()):
    _, rows, columns = own.shape
    line, facts = call(
        partial(stack_kernel, 7),
        "stack_line",
        (2,),
        [whole(own), whole(other)],
        block((2, 1, rows, columns), 0, first, 0, 0),
        like((2, 2, rows, columns), own.dtype),
        facts,
        own,
        other,
        wait=wait,
    )
    return line.reshape(4, rows, columns), facts


def turn_kernel(facts_ref, *refs):
    for i in range(2):
        refs[4 + i][...] = jnp.concatenate([refs[2 * i][...].T, refs[2 * i + 1][...].T], axis=1)


def turn_all_kernel(facts_ref, rows_ref, out_ref):
    out_ref[...] = rows_ref[...].T


def turn_all(facts, values, wait=()):
    count, width = values.shape
    step = width // 4
    return call(
        turn_all_kernel,
        "turn_all",
        (4,),
        [block((count, step), 0, first)],
        block((step, count), first, 0),
        like((width, count), values.dtype),
        facts,
        values,
        wait=wait,
    )


def turn(facts, values, others, rows, wait=()):
    count, width = values.shape
    half = width // 2
    out = block((rows, 2 * count), first, 0)
    shape = like((half, 2 * count), values.dtype)
    own = block((count, rows), 0, lambda i, f: 2 * i + f[4])
    other = block((count, rows), 0, lambda i, f: 2 * i + 1 - f[4])
    return call(
        turn_kernel,
        "turn",
        (half // rows,),
        [own, own, other, other],
        [out, out],
        [shape, shape],
        facts,
        values,
        others,
        values,
        others,
        wait=wait,
    )


def project_kernel(facts_ref, rows_ref, bias_ref, *refs):
    parts, (out_ref, in_ref, rest_ref) = refs[:4], refs[4:]
    step = pl.program_id(0)
    weight = near_or_far(facts_ref, parts, step < 4)

    @pl.when(step % 4 < 3)
    def _():
        in_ref[...] = weight
        value = product(rows_ref[...], weight, 1, 0) + bias_ref[...]
        out_ref[...] = value.astype(jnp.bfloat16)

    @pl.when(step % 4 == 3)
    def _():
        chips, count, wide = rest_ref.shape
        pairs = weight.reshape(chips, 2, count, wide // 2)
        rest_ref[...] = jnp.concatenate([pairs[:, 0], pairs[:, 1]], axis=2)


def project(facts, rows, bias, parts, wait=()):
    count, width = rows.shape
    wide = parts[0].shape[2] // 4

    def column(i, f):
        return half_at(i, f, 4) * 3 + jnp.minimum(i % 4, 2)

    out = block((count, wide), 0, column)
    rest = (8, parts[0].shape[1] // 2, 2 * wide)
    return call(
        project_kernel,
        "project",
        (8,),
        [whole(rows), block((1, wide), 0, column)] + square_columns(parts, wide, 4),
        [out, block((width, wide), 0, column), block(rest, 0, 0, lambda i, f: half_at(i, f, 4))],
        [
            like((count, 6 * wide), jnp.bfloat16),
            like((width, 6 * wide), jnp.bfloat16),
            like(rest[:2] + (4 * wide,), jnp.bfloat16),
        ],
        facts,
        rows,
        bias[None],
        *parts,
        wait=wait,
    )


def valid_rows(facts_ref, count, slots):
    place = lax.broadcasted_iota(jnp.int32, (count, 1), 0) + pl.program_id(0) * count + facts_ref[2]
    place = jnp.where(place >= slots, place - slots, place)
    return (place < facts_ref[0]).astype(jnp.float32)


def add_rows(sums_ref, rows):
    total = jnp.concatenate([jnp.sum(part, axis=0, keepdims=True) for part in rows], axis=0)
    total = jnp.concatenate([total, jnp.zeros((8 - len(rows), total.shape[1]), jnp.float32)], axis=0)

    @pl.when(pl.program_id(0) == 0)
    def _():
        sums_ref[...] = total

    @pl.when(pl.program_id(0) > 0)
    def _():
        sums_ref[...] += total


def mean_of(values):
    return jnp.mean(values, axis=-1, keepdims=True)


def attend_out_kernel(
    slots, facts_ref, own_ref, other_ref, own_weight_ref, other_weight_ref, tokens_ref, vectors_ref,
    hat_ref, rstd_ref, low_ref, sums_ref,
):
    branch = (
        product(own_ref[...], own_weight_ref[...], 1, 0)
        + product(other_ref[...], other_weight_ref[...], 1, 0)
        + vectors_ref[0:1]
    )
    tokens = tokens_ref[...].astype(jnp.float32)
    total = tokens + branch
    centered = total - mean_of(total)
    rstd = lax.rsqrt(mean_of(centered * centered) + 1e-05)
    hat = centered * rstd
    hat_ref[...] = hat
    rstd_ref[...] = rstd
    low_ref[...] = (hat * vectors_ref[1:2] + vectors_ref[2:3]).astype(jnp.bfloat16)
    valid = valid_rows(facts_ref, tokens.shape[0], slots)
    add_rows(sums_ref, [valid * tokens * tokens, valid * branch * branch])


def attend_out(facts, own, other, own_weight, other_weight, tokens, vectors, wait=()):
    slots, width = tokens.shape
    step = slots // 4
    rows = lambda array: block((step, array.shape[1]), first, 0)
    return call(
        partial(attend_out_kernel, slots),
        "attend_out",
        (4,),
        [rows(own), rows(other), whole(own_weight), whole(other_weight), rows(tokens), whole(vectors)],
        [block((step, width), first, 0), block((step, 1), first, 0), block((step, width), first, 0), block((8, width), 0, 0)],
        [
            like((slots, width), jnp.float32),
            like((slots, 1), jnp.float32),
            like((slots, width), jnp.bfloat16),
            like((8, width), jnp.float32),
        ],
        facts,
        own,
        other,
        own_weight,
        other_weight,
        tokens,
        vectors,
        wait=wait,
    )


def up_kernel(facts_ref, rows_ref, bias_ref, *refs):
    parts, (act_ref, slope_ref, turned_ref, weight_ref) = refs[:4], refs[4:]
    weight = near_or_far(facts_ref, parts, pl.program_id(0) < 4)
    weight_ref[...] = weight
    pre_act = product(rows_ref[...], weight, 1, 0) + bias_ref[...]
    below = 0.5 + 0.5 * lax.erf(pre_act * 0.7071067811865476)
    act = (pre_act * below).astype(jnp.bfloat16)
    act_ref[...] = act
    turned_ref[...] = act.T
    slope = below + pre_act * (0.3989422804014327 * jnp.exp(-0.5 * pre_act * pre_act))
    slope_ref[...] = slope.astype(jnp.bfloat16)


def feed_up(facts, rows, bias, parts, wait=()):
    count, width = rows.shape
    units = bias.shape[0]
    wide = units // 8

    def column(i, f):
        return half_at(i, f, 4) * 4 + i % 4

    shape = like((count, units), jnp.bfloat16)
    out = block((count, wide), 0, column)
    return call(
        up_kernel,
        "feed_up",
        (8,),
        [whole(rows), block((1, wide), 0, column)] + square_columns(parts, wide, 4),
        [out, out, block((wide, count), column, 0), block((width, wide), 0, column)],
        [
            shape,
            shape,
            like((units, count), jnp.bfloat16),
            like((width, units), jnp.bfloat16),
        ],
        facts,
        rows,
        bias[None],
        *parts,
        wait=wait,
    )


def down_kernel(facts_ref, rows_ref, *refs):
    parts, (weight_ref, out_ref, total_ref) = refs[:4], refs[4:]
    step = pl.program_id(0)
    own, beside, below, across = [ref[0] for ref in parts]
    even, left = facts_ref[4] == 0, facts_ref[3] == 0
    for x in range(2):
        mine = jnp.where(even, own, beside) if x == 0 else jnp.where(even, beside, own)
        theirs = jnp.where(even, below, across) if x == 0 else jnp.where(even, across, below)
        weight_ref[x] = jnp.concatenate(
            [jnp.where(left, mine, theirs), jnp.where(left, theirs, mine)], axis=1
        )
    weight = weight_ref[...].reshape(rows_ref.shape[1], out_ref.shape[1])
    value = product(rows_ref[...], weight, 1, 0)

    @pl.when(step == 0)
    def _():
        total_ref[...] = value

    @pl.when(step > 0)
    def _():
        total_ref[...] += value

    @pl.when(step == 3)
    def _():
        out_ref[...] = total_ref[...].astype(jnp.bfloat16)


def feed_down(facts, rows, parts, wait=()):
    count, units = rows.shape
    _, block_rows, half_width = parts[0].shape
    width = 2 * half_width
    shape = (1,) + parts[0].shape[1:]
    return call(
        down_kernel,
        "feed_down",
        (4,),
        [block((count // 2, units // 4), 1, first)] + [block(shape, first, 0, 0)] * 4,
        [block((2, block_rows, width), first, 0, 0), block((count // 2, width), 0, 0)],
        [like((8, block_rows, width), jnp.bfloat16), like((count // 2, width), jnp.bfloat16)],
        facts,
        rows,
        *parts,
        scratch=[pltpu.VMEM((count // 2, width), jnp.float32)],
        wait=wait,
    )


def second_norm_kernel(
    slots, facts_ref, part_ref, other_ref, hat_ref, cotangent_ref, vectors_ref,
    mixed_ref, grad_ref, low_ref, sums_ref,
):
    branch = part_ref[...] + other_ref[...].astype(jnp.float32) + vectors_ref[0:1]
    hidden = hat_ref[...] * vectors_ref[1:2] + vectors_ref[2:3]
    gain = vectors_ref[3:4]
    total = hidden + branch
    centered = total - mean_of(total)
    rstd = lax.rsqrt(mean_of(centered * centered) + 1e-05)
    hat = centered * rstd
    mixed_ref[...] = (hat * gain + vectors_ref[4:5]).astype(jnp.bfloat16)
    valid = valid_rows(facts_ref, branch.shape[0], slots)
    grad = cotangent_ref[...].astype(jnp.float32) * valid
    scaled = grad * gain
    result = rstd * (scaled - mean_of(scaled) - hat * mean_of(scaled * hat))
    low = result.astype(jnp.bfloat16)
    grad_ref[...] = result
    low_ref[...] = low
    add_rows(sums_ref, [low.astype(jnp.float32), grad * hat, grad, valid * branch * branch])


def second_norm(facts, part, other, hat, cotangent, vectors, wait=()):
    slots, width = part.shape
    step = slots // 4
    rows = block((step, width), first, 0)
    return call(
        partial(second_norm_kernel, slots),
        "second_norm",
        (4,),
        [rows, rows, rows, rows, whole(vectors)],
        [rows, rows, rows, block((8, width), 0, 0)],
        [
            like((slots, width), jnp.bfloat16),
            like((slots, width), jnp.float32),
            like((slots, width), jnp.bfloat16),
            like((8, width), jnp.float32),
        ],
        facts,
        part,
        other,
        hat,
        cotangent,
        vectors,
        wait=wait,
    )


def first_norm_kernel(
    facts_ref, part_ref, other_ref, second_ref, hat_ref, rstd_ref, vectors_ref,
    grad_ref, low_ref, sums_ref,
):
    grad = part_ref[...] + other_ref[...].astype(jnp.float32) + second_ref[...]
    hat = hat_ref[...]
    scaled = grad * vectors_ref[1:2]
    result = rstd_ref[...] * (scaled - mean_of(scaled) - hat * mean_of(scaled * hat))
    low = result.astype(jnp.bfloat16)
    grad_ref[...] = result
    low_ref[...] = low
    add_rows(sums_ref, [low.astype(jnp.float32), grad * hat, grad])


def first_norm(facts, part, other, second, hat, rstd, vectors, wait=()):
    slots, width = part.shape
    step = slots // 4
    rows = block((step, width), first, 0)
    return call(
        first_norm_kernel,
        "first_norm",
        (4,),
        [rows, rows, rows, rows, block((step, 1), first, 0), whole(vectors)],
        [rows, rows, block((8, width), 0, 0)],
        [
            like((slots, width), jnp.float32),
            like((slots, width), jnp.bfloat16),
            like((8, width), jnp.float32),
        ],
        facts,
        part,
        other,
        second,
        hat,
        rstd,
        vectors,
        wait=wait,
    )


def act_grad_kernel(facts_ref, rows_ref, weight_ref, slope_ref, out_ref, sums_ref):
    total = product(rows_ref[...], weight_ref[...], 1, 1)
    grad = total.astype(jnp.bfloat16).astype(jnp.float32) * slope_ref[...].astype(jnp.float32)
    low = grad.astype(jnp.bfloat16)
    out_ref[...] = low
    sums_ref[...] = jnp.sum(low.astype(jnp.float32), axis=0, keepdims=True)


def act_grad(facts, rows, weight, slope, wait=()):
    count, units = slope.shape
    step = units // 8
    out = block((count, step), 0, first)
    return call(
        act_grad_kernel,
        "act_grad",
        (8,),
        [whole(rows), block((step, rows.shape[1]), first, 0), out],
        [out, block((1, step), 0, first)],
        [like((count, units), jnp.bfloat16), like((1, units), jnp.float32)],
        facts,
        rows,
        weight,
        slope,
        wait=wait,
    )


def tokens_grad_kernel(facts_ref, mine_ref, theirs_ref, weight_ref, out_ref, sent_ref):
    wide = mine_ref.shape[1]
    slots = out_ref.shape[0]
    half = facts_ref[3]
    mine = weight_ref[:, pl.ds(pl.multiple_of(half * wide, 128), wide)]
    theirs = weight_ref[:, pl.ds(pl.multiple_of((1 - half) * wide, 128), wide)]
    total = product(mine_ref[...], mine, 1, 1) + product(theirs_ref[...], theirs, 1, 1)
    out_ref[...] = total[:slots]
    sent_ref[...] = total[slots:].astype(sent_ref.dtype)


def tokens_grad(facts, mine, theirs, weight, wait=(), through=()):
    count, columns = mine.shape
    width = weight.shape[0]
    step = width // 4
    out = block((count // 2, step), 0, first)
    return call(
        tokens_grad_kernel,
        "tokens_grad",
        (4,),
        [whole(mine), whole(theirs), block((step, 2 * columns), first, 0)],
        [out, out],
        [
            like((count // 2, width), jnp.float32),
            like((count // 2, width), jnp.bfloat16),
        ],
        facts,
        mine,
        theirs,
        weight,
        wait=wait,
        through=through,
    )


def add_parts_kernel(facts_ref, own_ref, got_ref, kept_ref, sent_ref):
    step = pl.program_id(0)
    total = own_ref[...].astype(jnp.float32) + got_ref[...].astype(jnp.float32)
    total = total.astype(jnp.bfloat16)

    @pl.when(step < 2)
    def _():
        sent_ref[...] = total

    @pl.when(step >= 2)
    def _():
        kept_ref[...] = total


def add_last_kernel(facts_ref, own_ref, got_ref, kept_ref, sent_ref):
    total = own_ref[0].astype(jnp.float32) + got_ref[0].astype(jnp.float32)
    total = total.astype(jnp.bfloat16)

    @pl.when(pl.program_id(0) == 0)
    def _():
        sent_ref[...] = total

    @pl.when(pl.program_id(0) == 1)
    def _():
        kept_ref[...] = total


def add_last(facts, own, got, wait=(), through=()):
    _, rows, columns = own.shape
    part = block((1, rows, columns), lambda i, f: jnp.where(i == 0, 1 - f[6], f[6]), 0, 0)
    shape = like((rows, columns), jnp.bfloat16)
    out = block((rows, columns), 0, 0)
    return call(
        add_last_kernel,
        "add_last",
        (2,),
        [part, part],
        [out, out],
        [shape, shape],
        facts,
        own,
        got,
        wait=wait,
        through=through,
    )


def add_parts(facts, own, got, wait=(), through=()):
    _, rows, columns = own.shape
    shape = (1, rows, columns)
    part = block(shape, lambda i, f: 2 * (i % 2) + jnp.where(i < 2, 1 - f[7], f[7]), 0, 0)
    half = like((2, rows, columns), jnp.bfloat16)
    return call(
        add_parts_kernel,
        "add_parts",
        (4,),
        [part, part],
        [
            block(shape, lambda i, *_: jnp.maximum(i - 2, 0), 0, 0),
            block(shape, lambda i, *_: jnp.minimum(i, 1), 0, 0),
        ],
        [half, half],
        facts,
        own,
        got,
        wait=wait,
        through=through,
    )


def alternate(value, width, offset):
    starts = range(offset * width, value.shape[1], 2 * width)
    return jnp.concatenate([value[:, start : start + width] for start in starts], axis=1)


def deal_kernel(unit_block, core_ref, query_ref, key_ref, value_ref, up_ref, *refs):
    first_core = core_ref[0] == 0
    near = [ref[...] for ref in (query_ref, key_ref, value_ref)]
    even = jnp.concatenate([alternate(value, HD, 0) for value in near], axis=1)
    odd = jnp.concatenate([alternate(value, HD, 1) for value in near], axis=1)
    up = up_ref[...]
    up_even, up_odd = alternate(up, unit_block, 0), alternate(up, unit_block, 1)
    refs[0][...] = jnp.where(first_core, even, odd)
    refs[1][...] = jnp.where(first_core, odd, even)
    refs[2][...] = jnp.where(first_core, up_even, up_odd)
    refs[3][...] = jnp.where(first_core, up_odd, up_even)


def deal(core, query, key, value, up, unit_block):
    near = like((query.shape[0], 3 * query.shape[1] // 2), jnp.bfloat16)
    half = like((up.shape[0], up.shape[1] // 2), jnp.bfloat16)
    shapes = [near, near, half, half]
    return call(
        partial(deal_kernel, unit_block),
        "deal",
        (1,),
        [whole(value) for value in (query, key, value, up)],
        [whole(shape) for shape in shapes],
        shapes,
        core,
        query,
        key,
        value,
        up,
    )


def lay_out_kernel(core_ref, near_ref, near_got_ref, out_ref, up_ref, up_got_ref, *refs):
    first_core = core_ref[0] == 0
    near, near_got, up, up_got = [
        ref[...] for ref in (near_ref, near_got_ref, up_ref, up_got_ref)
    ]
    out = out_ref[...]
    wide = out.shape[1] // 2
    near_rows = jnp.concatenate(
        [jnp.where(first_core, near, near_got), jnp.where(first_core, near_got, near)], axis=0
    )
    out_rows = jnp.concatenate([out[:, :wide], out[:, wide:]], axis=0)
    refs[0][...] = jnp.concatenate([near_rows, out_rows], axis=1)
    refs[1][...] = jnp.concatenate(
        [jnp.where(first_core, up, up_got), jnp.where(first_core, up_got, up)], axis=0
    )


def lay_out(core, near, near_got, out, up, up_got):
    rows = 2 * near.shape[0]
    shapes = [
        like((rows, near.shape[1] + out.shape[1] // 2), jnp.bfloat16),
        like((rows, up.shape[1]), jnp.bfloat16),
    ]
    arrays = (near, near_got, out, up, up_got)
    return call(
        lay_out_kernel,
        "lay_out",
        (1,),
        [whole(value) for value in arrays],
        [whole(shape) for shape in shapes],
        shapes,
        core,
        *arrays,
    )[0]


def split_body(
    tokens,
    lengths,
    cotangent,
    query_weight,
    key_weight,
    value_weight,
    out_weight,
    up_weight,
    down_weight,
    query_bias,
    value_bias,
    out_bias,
    attn_gain,
    attn_shift,
    up_bias,
    down_bias,
    feed_gain,
    feed_shift,
):
    core = lax.axis_index("c")
    half = lax.axis_index("s")
    row_count, width = tokens.shape[1:]
    slots = 2 * row_count
    unit_block = down_weight.shape[0]
    units = up_bias.shape[0] // 2
    cols = width // 2
    wide = cols // 2

    def to_sequence(values):
        return jnp.concatenate([pick(values, half, 0), swap(pick(values, 1 - half, 0), "s")], axis=0)

    def from_sequence(values):
        return in_order(values[:row_count], swap(values[row_count:], "s"), half)

    place = jnp.stack([core]).astype(jnp.int32)
    (near_kept, near_sent, up_kept, up_sent), place = deal(
        place, query_weight, key_weight, value_weight, up_weight, unit_block
    )
    near_mine, up_mine = lay_out(
        place, near_kept, swap(near_sent, "c"), out_weight, up_kept, swap(up_sent, "c")
    )
    rows, up_cols = up_mine.shape
    line = lax.axis_index("z")
    length_own = lax.dynamic_slice_in_dim(lengths, half, 1, 0)
    facts = jnp.concatenate(
        [
            both(length_own, "c"),
            jnp.stack(
                [
                    half * row_count,
                    half,
                    lax.axis_index("x"),
                    jnp.int32(0),
                    line // 2,
                    line % 2,
                ]
            ).astype(jnp.int32),
        ]
    )
    tokens_own = to_sequence(tokens)
    cotangent_own = to_sequence(cotangent)
    (near, up_mine, down_mine), facts = stack_pair(
        facts,
        near_mine,
        line_cross(near_mine),
        wait=(tokens_own,),
        through=(up_mine, down_weight),
    )
    near, facts = stack_line(facts, near, line_next(near), wait=(cotangent_own,))
    near_parts = gather_square(near, "x")
    up_pairs, facts = stack_pair(facts, up_mine, line_cross(up_mine), wait=(near,))
    tokens_both = both(tokens_own, "c")
    up_part, facts = stack_line(
        facts, up_pairs, line_next(up_pairs), wait=(near_parts[1], near_parts[2])
    )
    up_parts = gather_square(up_part, "s")
    down_pairs, facts = stack_pair(facts, down_mine, line_cross(down_mine), wait=(up_part,))
    def halves_of(vector, size):
        return pick(vector.reshape(-1, 2, size), core, 1).reshape(-1)

    query_part = halves_of(query_bias, HD).reshape(2, wide)
    value_part = halves_of(value_bias, HD).reshape(2, wide)
    in_bias = jnp.stack([query_part, jnp.zeros_like(query_part), value_part], axis=1).reshape(-1)
    (projected, in_weight, out_own), facts = project(
        facts, tokens_both, in_bias, near_parts, wait=(down_pairs,)
    )
    out_own = out_own.reshape(cols, width)
    out_other = swap(out_own, "c")
    down_part, facts = stack_line(facts, down_pairs, line_next(down_pairs), wait=(projected,))
    down_parts = gather_square(down_part, "x")
    (heads_out, totals), facts = attend(facts, projected, slots, wait=(up_parts[2],))
    heads_other = swap(heads_out[slots:], "c")
    vectors = jnp.stack(
        [out_bias, attn_gain, attn_shift, down_bias, feed_gain, feed_shift, out_bias, out_bias]
    )
    (first_hat, first_rstd, hidden_low, first_sums), facts = attend_out(
        facts,
        heads_out,
        heads_other,
        out_own,
        out_other,
        tokens_own,
        vectors,
        wait=(up_parts[1], down_parts[2]),
    )
    hidden_from = swap(hidden_low, "c")
    hidden_both = jnp.concatenate([hidden_low, hidden_from], axis=0)
    (activation, slope, act_t, up_all), facts = feed_up(
        facts, hidden_both, halves_of(up_bias, unit_block), up_parts, wait=(down_parts[1],)
    )
    hidden_turned, facts = turn(facts, hidden_low, hidden_from, rows, wait=(act_t,))
    (down_all, feed_sent), facts = feed_down(facts, activation, down_parts)
    down_all = down_all.reshape(units, width)
    feed_other = swap(feed_sent, "c")
    feed_part = product(activation[:slots], down_all, 1, 0)
    feed_vectors = jnp.stack(
        [down_bias, attn_gain, attn_shift, feed_gain, feed_shift, out_bias, out_bias, out_bias]
    )
    (mixed, second_grad, feed_low, second_sums), facts = second_norm(
        facts, feed_part, feed_other, first_hat, cotangent_own, feed_vectors
    )

    mixed_got = swap(mixed[row_count:], "s")

    feed_both = both(feed_low, "c")
    tokens_t, facts = turn_all(facts, tokens_both, wait=(feed_low,))
    feed_mine, feed_theirs = columns_of(feed_both, half), columns_of(feed_both, 1 - half)
    down_sent = grad_block(act_t, feed_theirs)
    down_got = swap(down_sent, "s")
    (pre_grad, up_bias_grad), facts = act_grad(
        facts, feed_both, down_all, slope, wait=(down_sent,)
    )
    hidden_sent = product(pre_grad[slots:], up_all, 1, 1).astype(jnp.bfloat16)
    hidden_other = swap(hidden_sent, "c")
    hidden_own_t, hidden_other_t = hidden_turned
    up_sent = grad_block(hidden_other_t, pre_grad)
    up_got = swap(up_sent, "x")
    hidden_part = product(pre_grad[:slots], up_all, 1, 1)
    (first_grad, attn_low, third_sums), facts = first_norm(
        facts,
        hidden_part,
        hidden_other,
        second_grad,
        first_hat,
        first_rstd,
        vectors,
        wait=(up_sent,),
    )
    grad_sent = product(attn_low, out_other, 1, 1).astype(jnp.bfloat16)
    grad_other = swap(grad_sent, "c")
    grad_own = product(attn_low, out_own, 1, 1).astype(jnp.bfloat16)
    out_sent = product(heads_other, attn_low, 0, 0).astype(jnp.bfloat16)
    out_got = swap(out_sent, "c")
    heads_grad = jnp.concatenate([grad_own, grad_other], axis=0)
    (theirs_low, theirs_sums), facts = attend_back(
        facts, projected, heads_grad, totals, slots, False, wait=(out_sent, mixed_got)
    )
    in_sent = grad_block(tokens_t, theirs_low)
    in_got = swap(in_sent, "s")
    down_total = grad_block(act_t, feed_mine, down_got)
    down_kept, down_sent = halve(down_total.reshape(4, 2, unit_block, cols), "x", 1)
    down_got = swap(down_sent, "x")
    out_grad = grad_block(heads_out[:slots].T, attn_low, out_got)
    out_line = out_grad.reshape((4, 2 * out_weight.shape[0], width))
    out_kept, out_sent = line_parts(out_line)
    out_got = lax.ppermute(out_sent, "z", NEXT)
    (mine_low, mine_sums), facts = attend_back(
        facts, projected, heads_grad, totals, slots, True, wait=(in_sent, out_sent, down_sent)
    )
    up_total = grad_block(hidden_own_t, pre_grad, up_got).reshape(4, rows, 2 * up_cols)
    up_kept, up_sent = columns_of(up_total, half), columns_of(up_total, 1 - half)
    up_got = swap(up_sent, "s")
    out_total = add(out_kept, out_got)
    upper = lax.axis_index("z") // 2
    out_kept, out_sent = pick(out_total, upper, 0), pick(out_total, 1 - upper, 0)
    out_got = lax.ppermute(out_sent, "z", CROSS)
    valid_count = length_own[0].astype(jnp.float32) * width
    stats = jnp.stack(
        [jnp.sum(first_sums[0]), jnp.sum(first_sums[1]), jnp.sum(second_sums[3]), valid_count]
    )
    mine_sums, theirs_sums = jnp.sum(mine_sums, axis=(0, 1)), jnp.sum(theirs_sums, axis=(0, 1))
    late = in_order(mine_sums, theirs_sums, half)
    sums = jnp.concatenate(
        [
            second_sums[:3].reshape(-1),
            third_sums[:3].reshape(-1),
            jnp.pad(stats, (0, 124)),
            up_bias_grad[0],
            late[:, :wide].reshape(-1),
            late[:, 2 * wide :].reshape(-1),
        ]
    )
    sums_got = lax.ppermute(sums, "z", NEXT)
    (tokens_part, tokens_sent), facts = tokens_grad(
        facts,
        mine_low,
        theirs_low,
        in_weight,
        wait=(up_sent, out_sent, sums),
    )
    tokens_other = swap(tokens_sent, "c")
    in_total = grad_block(tokens_t, mine_low, in_got)
    in_kept, in_sent = halve(in_total.reshape(4, 2, rows, 3 * wide), "x", 1)
    in_got = swap(in_sent, "x")
    (down_pairs, down_next), facts = add_parts(
        facts, down_kept, down_got, wait=(in_sent, tokens_part)
    )
    down_got = lax.ppermute(down_next, "z", NEXT)
    (up_pairs, up_next), facts = add_parts(facts, up_kept, up_got, wait=(down_next,))
    up_got = lax.ppermute(up_next, "z", NEXT)
    (in_pairs, in_next, up_pairs, down_pairs), facts = add_parts(
        facts, in_kept, in_got, wait=(up_next,), through=(up_pairs, down_pairs)
    )
    in_got = lax.ppermute(in_next, "z", NEXT)
    (in_kept, in_sent, sums, out_kept), facts = add_last(
        facts, in_pairs, in_got, through=(sums + sums_got, add(out_kept, out_got))
    )
    in_sum = add(in_kept, lax.ppermute(in_sent, "z", CROSS))
    tokens_grad_sum = tokens_part + tokens_other.astype(jnp.float32) + first_grad
    tokens_grad_sum = from_sequence(tokens_grad_sum.astype(jnp.bfloat16))
    mixed = in_order(mixed[:row_count], mixed_got, half)
    down_sum = fold_cross(add(down_pairs, down_got))
    up_sum = fold_cross(add(up_pairs, up_got))
    out_sum = fold_columns(fold(out_kept.reshape(2, out_weight.shape[0], width), "x", 0))

    sums = sums + lax.ppermute(sums, "z", CROSS)
    sums = sums + swap(sums, "s")
    sums = sums + swap(sums, "x")
    both_sums = in_order(sums, swap(sums, "c"), core)
    count = 6 * width + 128
    shared = both_sums[0, :count] + both_sums[1, :count]
    down_bias_grad, feed_gain_grad, feed_shift_grad, out_bias_grad, attn_gain_grad, attn_shift_grad = [
        shared[i * width : (i + 1) * width] for i in range(6)
    ]
    stats = shared[6 * width : 6 * width + 4]

    def interleave(start, size, block_size):
        sums = both_sums[:, start : start + size].reshape(2, -1, block_size)
        return sums.transpose(1, 0, 2).reshape(-1)

    up_bias_grad = interleave(count, units, unit_block)
    query_bias_grad = interleave(count + units, cols, HD)
    value_bias_gradient = interleave(count + units + cols, cols, HD)
    stream_rms = jnp.sqrt(stats[:3] / stats[3])

    def give_back(total):
        total = total.reshape((2, rows // 2) + total.shape[1:])
        return pick(total, core, 0), swap(pick(total, 1 - core, 0), "c")

    up_shares = give_back(up_sum)
    in_shares = give_back(in_sum)
    down_weight_grad = down_sum.astype(jnp.float32)
    out_weight_grad = out_sum.astype(jnp.float32)

    def merge(shares, start, size, block):
        one, two = [
            share[:, start : start + size].reshape(rows // 2, -1, block) for share in shares
        ]
        first = jnp.where(core == 0, one, two)
        second = jnp.where(core == 0, two, one)
        return jnp.stack([first, second], axis=2).reshape(rows // 2, -1).astype(jnp.float32)

    query_weight_grad = merge(in_shares, 0, wide, HD)
    key_weight_grad = merge(in_shares, wide, wide, HD)
    value_weight_grad = merge(in_shares, 2 * wide, wide, HD)
    up_weight_grad = merge(up_shares, 0, up_cols, unit_block)
    return (
        mixed,
        tokens_grad_sum,
        query_weight_grad,
        key_weight_grad,
        value_weight_grad,
        out_weight_grad,
        up_weight_grad,
        down_weight_grad,
        query_bias_grad,
        value_bias_gradient,
        out_bias_grad,
        attn_gain_grad,
        attn_shift_grad,
        up_bias_grad,
        down_bias_grad,
        feed_gain_grad,
        feed_shift_grad,
        stream_rms,
    )


def solution(mesh):
    devices = mesh.devices
    dp_count, seq_count = devices.shape
    split = seq_count == 2 and dp_count == 16
    if split:
        inner = jax.sharding.Mesh(devices.reshape(4, 2, 2, seq_count), ("z", "x", "c", "s"))
        dp, seq, body = ("z", "x", "c"), "s", split_body
    else:
        inner, dp, seq, body = mesh, "dp", "seq", general_body
    weights = (P(dp, seq),) * 6
    vectors = (P(),) * 9
    rows = P(dp, seq, None)
    in_specs = (rows, P(dp), rows) + weights + vectors
    out_specs = (rows, rows) + weights + vectors + (P(),)
    return jax.shard_map(body, mesh=inner, in_specs=in_specs, out_specs=out_specs, check_vma=False)
```

```python
from functools import partial
import math

import jax
import jax.numpy as jnp
from jax import lax
from jax.experimental import pallas as pl
from jax.experimental.pallas import tpu as pltpu
from jax.sharding import PartitionSpec as P

HD = 64


def layer_norm(values_in, gain_vector, shift_vector):
    mean_value = jnp.mean(values_in, axis=-1, keepdims=True)
    centered = values_in - mean_value
    variance = jnp.mean(centered * centered, axis=-1, keepdims=True)
    return centered * lax.rsqrt(variance + 1e-05) * gain_vector + shift_vector


def gather_weights(first, second, third, fourth, fifth, sixth):
    part = (
        lax.all_gather(first, "dp", axis=0, tiled=True),
        lax.all_gather(second, "dp", axis=0, tiled=True),
        lax.all_gather(third, "dp", axis=0, tiled=True),
        lax.all_gather(fourth, "dp", axis=0, tiled=True),
        lax.all_gather(fifth, "dp", axis=0, tiled=True),
        lax.all_gather(sixth, "dp", axis=0, tiled=True),
    )
    return (
        lax.all_gather(part[0], "seq", axis=1, tiled=True),
        lax.all_gather(part[1], "seq", axis=1, tiled=True),
        lax.all_gather(part[2], "seq", axis=1, tiled=True),
        lax.all_gather(part[3], "seq", axis=1, tiled=True),
        lax.all_gather(part[4], "seq", axis=1, tiled=True),
        lax.all_gather(part[5], "seq", axis=1, tiled=True),
    )


def reduce_grads(first, second, third, fourth, fifth, sixth):
    part = (
        lax.psum_scatter(first.astype(jnp.bfloat16), "seq", scatter_dimension=1, tiled=True).astype(
            jnp.float32
        ),
        lax.psum_scatter(
            second.astype(jnp.bfloat16), "seq", scatter_dimension=1, tiled=True
        ).astype(jnp.float32),
        lax.psum_scatter(third.astype(jnp.bfloat16), "seq", scatter_dimension=1, tiled=True).astype(
            jnp.float32
        ),
        lax.psum_scatter(
            fourth.astype(jnp.bfloat16), "seq", scatter_dimension=1, tiled=True
        ).astype(jnp.float32),
        lax.psum_scatter(fifth.astype(jnp.bfloat16), "seq", scatter_dimension=1, tiled=True).astype(
            jnp.float32
        ),
        lax.psum_scatter(sixth.astype(jnp.bfloat16), "seq", scatter_dimension=1, tiled=True).astype(
            jnp.float32
        ),
    )
    return (
        lax.psum_scatter(
            part[0].astype(jnp.bfloat16), "dp", scatter_dimension=0, tiled=True
        ).astype(jnp.float32),
        lax.psum_scatter(
            part[1].astype(jnp.bfloat16), "dp", scatter_dimension=0, tiled=True
        ).astype(jnp.float32),
        lax.psum_scatter(
            part[2].astype(jnp.bfloat16), "dp", scatter_dimension=0, tiled=True
        ).astype(jnp.float32),
        lax.psum_scatter(
            part[3].astype(jnp.bfloat16), "dp", scatter_dimension=0, tiled=True
        ).astype(jnp.float32),
        lax.psum_scatter(
            part[4].astype(jnp.bfloat16), "dp", scatter_dimension=0, tiled=True
        ).astype(jnp.float32),
        lax.psum_scatter(
            part[5].astype(jnp.bfloat16), "dp", scatter_dimension=0, tiled=True
        ).astype(jnp.float32),
    )


def block_layout(seq_count, row_count, head_count):
    block_seqs = math.gcd(seq_count, max(1, 512 // row_count))
    group_heads = math.gcd(head_count, 4)
    return (block_seqs, seq_count // block_seqs, group_heads, head_count // group_heads)


def head_slice(block_part, offset, group_width, group_heads):
    sliced = lax.dynamic_slice_in_dim(block_part, offset, group_width, 2)
    return sliced.reshape(sliced.shape[0], sliced.shape[1], group_heads, HD)


def attention_forward(queries, key_all, value_all, key_mask):
    seq_count, row_count, feature_total = queries.shape
    slot_count = key_all.shape[1]
    block_seqs, block_count, group_heads, group_count = block_layout(
        seq_count, row_count, feature_total // HD
    )
    group_width = group_heads * HD

    def seq_block(inputs):
        query_part, key_part, value_part, mask_part = inputs

        def head_block(group_index):
            offset = group_index * group_width
            query_heads = head_slice(query_part, offset, group_width, group_heads)
            key_heads = head_slice(key_part, offset, group_width, group_heads)
            value_heads = head_slice(value_part, offset, group_width, group_heads)
            scores = (
                jnp.einsum(
                    "brhd,bkhd->bhrk", query_heads, key_heads, preferred_element_type=jnp.float32
                )
                * 0.125
            )
            scores = jnp.where(mask_part[:, None, None, :], scores, -1e30)
            row_max = jnp.max(scores, axis=-1, keepdims=True)
            exponent = jnp.exp(scores - row_max)
            row_total = jnp.sum(exponent, axis=-1, keepdims=True)
            soft_probs = (exponent / row_total).astype(jnp.bfloat16)
            heads_out = jnp.einsum(
                "bhrk,bkhd->brhd", soft_probs, value_heads, preferred_element_type=jnp.float32
            )
            log_total = (row_max + jnp.log(row_total))[..., 0]
            return (heads_out.reshape(block_seqs, row_count, group_width), log_total)

        return lax.map(head_block, jnp.arange(group_count))

    outputs, log_totals = lax.map(
        seq_block,
        (
            queries.reshape(block_count, block_seqs, row_count, feature_total),
            key_all.reshape(block_count, block_seqs, slot_count, feature_total),
            value_all.reshape(block_count, block_seqs, slot_count, feature_total),
            key_mask.reshape(block_count, block_seqs, slot_count),
        ),
    )
    mixed_heads = outputs.transpose(0, 2, 3, 1, 4).reshape(seq_count, row_count, feature_total)
    return (mixed_heads, log_totals)


def attention_backward(queries, key_all, value_all, key_mask, heads_grad, log_totals):
    seq_count, row_count, feature_total = queries.shape
    slot_count = key_all.shape[1]
    block_seqs, block_count, group_heads, group_count = block_layout(
        seq_count, row_count, feature_total // HD
    )
    group_width = group_heads * HD

    def seq_block(inputs):
        query_part, key_part, value_part, mask_part, grad_part, total_part = inputs

        def head_block(group_index):
            offset = group_index * group_width
            query_heads = head_slice(query_part, offset, group_width, group_heads)
            key_heads = head_slice(key_part, offset, group_width, group_heads)
            value_heads = head_slice(value_part, offset, group_width, group_heads)
            grad_heads = head_slice(grad_part, offset, group_width, group_heads)
            log_total = lax.dynamic_index_in_dim(total_part, group_index, 0, keepdims=False)
            scores = (
                jnp.einsum(
                    "brhd,bkhd->bhrk", query_heads, key_heads, preferred_element_type=jnp.float32
                )
                * 0.125
            )
            scores = jnp.where(mask_part[:, None, None, :], scores, -1e30)
            soft_probs = jnp.exp(scores - log_total[..., None])
            value_grad = jnp.einsum(
                "bhrk,brhd->bkhd",
                soft_probs.astype(jnp.bfloat16),
                grad_heads,
                preferred_element_type=jnp.float32,
            )
            prob_grad = jnp.einsum(
                "brhd,bkhd->bhrk", grad_heads, value_heads, preferred_element_type=jnp.float32
            )
            inner = jnp.sum(soft_probs * prob_grad, axis=-1, keepdims=True)
            score_grad = (soft_probs * (prob_grad - inner)).astype(jnp.bfloat16)
            query_grad = (
                jnp.einsum(
                    "bhrk,bkhd->brhd", score_grad, key_heads, preferred_element_type=jnp.float32
                )
                * 0.125
            )
            key_grad = (
                jnp.einsum(
                    "bhrk,brhd->bkhd", score_grad, query_heads, preferred_element_type=jnp.float32
                )
                * 0.125
            )
            return (
                query_grad.reshape(block_seqs, row_count, group_width),
                key_grad.reshape(block_seqs, slot_count, group_width),
                value_grad.reshape(block_seqs, slot_count, group_width),
            )

        return lax.map(head_block, jnp.arange(group_count))

    query_blocks, key_blocks, value_block_list = lax.map(
        seq_block,
        (
            queries.reshape(block_count, block_seqs, row_count, feature_total),
            key_all.reshape(block_count, block_seqs, slot_count, feature_total),
            value_all.reshape(block_count, block_seqs, slot_count, feature_total),
            key_mask.reshape(block_count, block_seqs, slot_count),
            heads_grad.reshape(block_count, block_seqs, row_count, feature_total),
            log_totals,
        ),
    )
    query_grad = query_blocks.transpose(0, 2, 3, 1, 4).reshape(seq_count, row_count, feature_total)
    key_grad = key_blocks.transpose(0, 2, 3, 1, 4).reshape(seq_count, slot_count, feature_total)
    value_grad = value_block_list.transpose(0, 2, 3, 1, 4).reshape(
        seq_count, slot_count, feature_total
    )
    return (query_grad, key_grad, value_grad)


def general_body(
    tokens,
    lengths,
    cotangent,
    query_weight,
    key_weight,
    value_weight,
    out_weight,
    up_weight,
    down_weight,
    query_bias,
    value_bias,
    out_bias,
    attn_gain,
    attn_shift,
    up_bias,
    down_bias,
    feed_gain,
    feed_shift,
):
    seq_count, row_count, feature_total = tokens.shape
    slot_count = row_count * lax.axis_size("seq")
    token_count = seq_count * row_count
    whole = gather_weights(
        query_weight, key_weight, value_weight, out_weight, up_weight, down_weight
    )
    full_query, full_key, full_value, full_out, full_up, full_down = whole
    flat_tokens = tokens.reshape(token_count, feature_total)
    queries = (
        jnp.dot(flat_tokens, full_query, preferred_element_type=jnp.float32) + query_bias
    ).astype(jnp.bfloat16)
    key_rows = jnp.dot(flat_tokens, full_key, preferred_element_type=jnp.float32).astype(
        jnp.bfloat16
    )
    value_rows = (
        jnp.dot(flat_tokens, full_value, preferred_element_type=jnp.float32) + value_bias
    ).astype(jnp.bfloat16)
    first_slot = lax.axis_index("seq") * row_count
    key_mask = jnp.arange(slot_count)[None, :] < lengths[:, None]
    row_valid = ((first_slot + jnp.arange(row_count))[None, :] < lengths[:, None]).astype(
        jnp.float32
    )
    row_valid = row_valid.reshape(token_count, 1)
    query_blocks = queries.reshape(seq_count, row_count, feature_total)
    key_blocks = key_rows.reshape(seq_count, row_count, feature_total)
    value_block_list = value_rows.reshape(seq_count, row_count, feature_total)
    key_all, value_all = (
        lax.all_gather(key_blocks, "seq", axis=1, tiled=True),
        lax.all_gather(value_block_list, "seq", axis=1, tiled=True),
    )
    mixed_heads, log_totals = attention_forward(query_blocks, key_all, value_all, key_mask)
    heads_low = mixed_heads.reshape(token_count, feature_total).astype(jnp.bfloat16)
    attention_out = jnp.dot(heads_low, full_out, preferred_element_type=jnp.float32) + out_bias
    tokens_f32 = flat_tokens.astype(jnp.float32)
    first_sum = tokens_f32 + attention_out
    hidden, first_pull = jax.vjp(layer_norm, first_sum, attn_gain, attn_shift)
    hidden_low = hidden.astype(jnp.bfloat16)
    pre_act = jnp.dot(hidden_low, full_up, preferred_element_type=jnp.float32) + up_bias
    gelu_out, gelu_pull = jax.vjp(partial(jax.nn.gelu, approximate=False), pre_act)
    activation = gelu_out.astype(jnp.bfloat16)
    feed_out = jnp.dot(activation, full_down, preferred_element_type=jnp.float32) + down_bias
    result, second_pull = jax.vjp(layer_norm, hidden + feed_out, feed_gain, feed_shift)
    mixed = result.astype(jnp.bfloat16).reshape(seq_count, row_count, feature_total)
    partial_stats = jnp.stack(
        [
            jnp.sum(row_valid * tokens_f32 * tokens_f32),
            jnp.sum(row_valid * attention_out * attention_out),
            jnp.sum(row_valid * feed_out * feed_out),
            jnp.sum(row_valid) * feature_total,
        ]
    )
    back_weights = gather_weights(
        query_weight, key_weight, value_weight, out_weight, up_weight, down_weight
    )
    back_query, back_key, back_value, back_out, back_up, back_down = back_weights
    out_grad = cotangent.reshape(token_count, feature_total).astype(jnp.float32) * row_valid
    second_grad, feed_gain_grad, feed_shift_grad = second_pull(out_grad)
    feed_low = second_grad.astype(jnp.bfloat16)
    down_weight_grad = jnp.einsum(
        "nf,nd->fd", activation, feed_low, preferred_element_type=jnp.float32
    )
    down_bias_grad = jnp.sum(feed_low, axis=0, dtype=jnp.float32)
    act_grad = jnp.einsum(
        "nd,fd->nf", feed_low, back_down, preferred_element_type=jnp.float32
    ).astype(jnp.bfloat16)
    pre_grad = gelu_pull(act_grad.astype(jnp.float32))[0].astype(jnp.bfloat16)
    up_weight_grad = jnp.einsum(
        "nd,nf->df", hidden_low, pre_grad, preferred_element_type=jnp.float32
    )
    up_bias_grad = jnp.sum(pre_grad, axis=0, dtype=jnp.float32)
    hidden_grad = (
        jnp.einsum("nf,df->nd", pre_grad, back_up, preferred_element_type=jnp.float32) + second_grad
    )
    first_grad, attn_gain_grad, attn_shift_grad = first_pull(hidden_grad)
    attn_low = first_grad.astype(jnp.bfloat16)
    out_weight_grad = jnp.einsum(
        "nd,ne->de", heads_low, attn_low, preferred_element_type=jnp.float32
    )
    out_bias_grad = jnp.sum(attn_low, axis=0, dtype=jnp.float32)
    heads_grad = jnp.einsum(
        "ne,de->nd", attn_low, back_out, preferred_element_type=jnp.float32
    ).astype(jnp.bfloat16)
    heads_grad = heads_grad.reshape(seq_count, row_count, feature_total)
    query_grad, key_part_grad, value_part_grad = attention_backward(
        query_blocks, key_all, value_all, key_mask, heads_grad, log_totals
    )
    key_sum, value_sum = (
        lax.psum_scatter(
            key_part_grad.astype(jnp.bfloat16), "seq", scatter_dimension=1, tiled=True
        ).astype(jnp.float32),
        lax.psum_scatter(
            value_part_grad.astype(jnp.bfloat16), "seq", scatter_dimension=1, tiled=True
        ).astype(jnp.float32),
    )
    query_low = query_grad.reshape(token_count, feature_total).astype(jnp.bfloat16)
    key_low = key_sum.reshape(token_count, feature_total).astype(jnp.bfloat16)
    value_low = value_sum.reshape(token_count, feature_total).astype(jnp.bfloat16)
    query_weight_grad = jnp.einsum(
        "nd,ne->de", flat_tokens, query_low, preferred_element_type=jnp.float32
    )
    key_weight_grad = jnp.einsum(
        "nd,ne->de", flat_tokens, key_low, preferred_element_type=jnp.float32
    )
    value_weight_grad = jnp.einsum(
        "nd,ne->de", flat_tokens, value_low, preferred_element_type=jnp.float32
    )
    query_bias_grad = jnp.sum(query_low, axis=0, dtype=jnp.float32)
    value_bias_gradient = jnp.sum(value_low, axis=0, dtype=jnp.float32)
    tokens_grad = (
        jnp.einsum("ne,de->nd", query_low, back_query, preferred_element_type=jnp.float32)
        + jnp.einsum("ne,de->nd", key_low, back_key, preferred_element_type=jnp.float32)
        + jnp.einsum("ne,de->nd", value_low, back_value, preferred_element_type=jnp.float32)
        + first_grad
    )
    tokens_grad = tokens_grad.astype(jnp.bfloat16).reshape(seq_count, row_count, feature_total)
    matrix_grads = reduce_grads(
        query_weight_grad,
        key_weight_grad,
        value_weight_grad,
        out_weight_grad,
        up_weight_grad,
        down_weight_grad,
    )
    totals = lax.psum(
        (
            partial_stats,
            query_bias_grad,
            value_bias_gradient,
            out_bias_grad,
            attn_gain_grad,
            attn_shift_grad,
            up_bias_grad,
            down_bias_grad,
            feed_gain_grad,
            feed_shift_grad,
        ),
        ("dp", "seq"),
    )
    stream_rms = jnp.sqrt(totals[0][:3] / totals[0][3])
    return (
        mixed,
        tokens_grad,
        matrix_grads[0],
        matrix_grads[1],
        matrix_grads[2],
        matrix_grads[3],
        matrix_grads[4],
        matrix_grads[5],
        totals[1],
        totals[2],
        totals[3],
        totals[4],
        totals[5],
        totals[6],
        totals[7],
        totals[8],
        totals[9],
        stream_rms,
    )


def swap(value, axis):
    return lax.ppermute(value, axis, [(0, 1), (1, 0)])


def both(value, axis):
    return jnp.concatenate([value, swap(value, axis)], axis=0)


def in_order(own, other, index, axis=0):
    return jnp.where(
        index == 0, jnp.stack([own, other], axis=axis), jnp.stack([other, own], axis=axis)
    )


def pick(values, index, axis):
    return lax.dynamic_index_in_dim(values, index, axis, keepdims=False)


def add(left, right):
    return (left.astype(jnp.float32) + right.astype(jnp.float32)).astype(jnp.bfloat16)


def fold(values, axis, dim):
    index = lax.axis_index(axis)
    return add(pick(values, index, dim), swap(pick(values, 1 - index, dim), axis))


NEXT = [(0, 1), (1, 0), (2, 3), (3, 2)]
CROSS = [(0, 2), (2, 0), (1, 3), (3, 1)]


def fold_cross(pairs):
    upper = lax.axis_index("z") // 2
    return add(pick(pairs, upper, 0), lax.ppermute(pick(pairs, 1 - upper, 0), "z", CROSS))


def fold_line(values):
    odd = lax.axis_index("z") % 2
    pairs = values.reshape((2, 2) + values.shape[1:])
    sent = lax.ppermute(pick(pairs, 1 - odd, 1), "z", NEXT)
    return fold_cross(add(pick(pairs, odd, 1), sent))


def line_cross(value):
    return lax.ppermute(value, "z", CROSS)


def line_next(pair):
    return lax.ppermute(pair, "z", NEXT)


def gather_square(own, way):
    beside, below = swap(own, "x"), swap(own, "s")
    across = swap(below, "x") if way == "x" else swap(beside, "s")
    return [own, beside, below, across]


def fold_columns(total):
    half = lax.axis_index("s")
    return add(columns_of(total, half), swap(columns_of(total, 1 - half), "s"))


def halve(values, axis, dim):
    index = lax.axis_index(axis) % 2
    return pick(values, index, dim), pick(values, 1 - index, dim)


def line_parts(values):
    return halve(values.reshape((2, 2) + values.shape[1:]), "z", 1)


def scatter_top(send, keep):
    total = add(keep, swap(send, "s"))
    total = total.reshape((4, 2) + total.shape[1:])
    return fold_line(fold(total, "x", 1))


def grad_block(left_t, right, got=None):
    total = product(left_t, right, 1, 0)
    if got is not None:
        total = total + got.astype(jnp.float32)
    return total.astype(jnp.bfloat16)


def columns_of(right, index):
    columns = right.shape[-1] // 2
    return lax.dynamic_slice_in_dim(right, index * columns, columns, right.ndim - 1)


PAIR = 2 * HD
LIMIT = 16 * 1024 * 1024


def kernel_params(steps):
    return pltpu.CompilerParams(
        dimension_semantics=("arbitrary",) * steps, vmem_limit_bytes=LIMIT
    )


def product(left, right, left_dim, right_dim):
    return lax.dot_general(
        left, right, (((left_dim,), (right_dim,)), ((), ())), preferred_element_type=jnp.float32
    )


def key_bias(facts_ref, slots):
    place = lax.broadcasted_iota(jnp.int32, (slots, 1), 0) + facts_ref[2]
    place = jnp.where(place >= slots, place - slots, place)
    return jnp.where(place < facts_ref[pl.program_id(0)], 0.0, -1e30)


def head_lanes(value, head):
    lane = lax.broadcasted_iota(jnp.int32, value.shape, 1)
    return jnp.where((lane >= HD) == (head == 1), value, jnp.zeros_like(value))


def turned(value):
    return value.astype(jnp.float32).T


def attend_kernel(facts_ref, query_ref, key_ref, value_ref, out_ref, total_ref):
    slots = key_ref.shape[0]
    bias = key_bias(facts_ref, slots)
    query = query_ref[...] * jnp.bfloat16(0.125)
    key = key_ref[...]
    value_t = turned(value_ref[...]).astype(jnp.bfloat16)
    outs = []
    for head in range(2):
        scores = product(key, head_lanes(query, head), 1, 1) + bias
        peak = jnp.max(scores, axis=0, keepdims=True)
        weight = jnp.exp(scores - peak)
        total = jnp.sum(weight, axis=0, keepdims=True)
        part = product(value_t[head * HD : (head + 1) * HD], weight.astype(jnp.bfloat16), 1, 0)
        outs.append(part * (1.0 / total))
        total_ref[0, 0, head : head + 1, :] = peak + jnp.log(total)
    out_ref[...] = jnp.concatenate(outs, axis=0).T.astype(jnp.bfloat16)


def attend_back_kernel(
    facts_ref, query_ref, key_ref, value_ref, grad_ref, total_ref, low_ref, sums_ref
):
    slots = key_ref.shape[0]
    bias = key_bias(facts_ref, slots)
    query = query_ref[...] * jnp.bfloat16(0.125)
    key = key_ref[...]
    value = value_ref[...]
    grad = grad_ref[...]
    key_t = turned(key).astype(jnp.bfloat16)
    lane = lax.broadcasted_iota(jnp.int32, (slots, PAIR), 1)
    query_parts, key_parts, value_parts = [], [], []
    for head in range(2):
        scores = product(key, head_lanes(query, head), 1, 1) + bias
        soft = jnp.exp(scores - total_ref[0, 0, head : head + 1, :])
        value_parts.append(product(soft.astype(jnp.bfloat16), grad, 1, 0))
        change = product(value, head_lanes(grad, head), 1, 1)
        inner = jnp.sum(soft * change, axis=0, keepdims=True)
        change = (soft * (change - inner)).astype(jnp.bfloat16)
        key_parts.append(product(change, query, 1, 0))
        query_parts.append(product(key_t[head * HD : (head + 1) * HD], change, 1, 0))
    pair = pl.program_id(1)
    groups = low_ref.shape[1] // 3
    query_low = (jnp.concatenate(query_parts, axis=0) * 0.125).T
    key_low = jnp.where(lane < HD, key_parts[0], key_parts[1])
    value_low = jnp.where(lane < HD, value_parts[0], value_parts[1])
    for place, part in enumerate((query_low, key_low, value_low)):
        start = pl.multiple_of(place * groups + pair * PAIR, PAIR)
        low = part.astype(jnp.bfloat16)
        low_ref[:, pl.ds(start, PAIR)] = low
        sums_ref[0, :, pl.ds(start, PAIR)] = jnp.sum(
            low.astype(jnp.float32), axis=0, keepdims=True
        )


def attention_specs(slots, pairs):
    def at(part):
        return pl.BlockSpec(
            (slots, PAIR), lambda b, g, p, *_: (b, g * 3 * pairs + part * pairs + p)
        )

    heads = pl.BlockSpec((slots, PAIR), lambda b, g, p, *_: (b, g * pairs + p))
    totals = pl.BlockSpec((1, 1, 2, slots), lambda b, g, p, *_: (b, g * pairs + p, 0, 0))
    return [at(0), at(1), at(2)], heads, totals


def attend(facts, projected, slots, wait=()):
    pairs = projected.shape[1] // (6 * PAIR)
    inputs, heads, totals = attention_specs(slots, pairs)
    rows = projected.shape[0]
    return call(
        attend_kernel,
        "attend",
        (2, 2, pairs),
        inputs,
        [heads, totals],
        [
            like((rows, 2 * pairs * PAIR), jnp.bfloat16),
            like((2, 2 * pairs, 2, slots), jnp.float32),
        ],
        facts,
        projected,
        projected,
        projected,
        wait=wait,
    )


def attend_back(facts, projected, heads_grad, totals_in, slots, own, wait=(), through=()):
    pairs = projected.shape[1] // (6 * PAIR)

    def group(facts_ref):
        return facts_ref[3] if own else 1 - facts_ref[3]

    def at(part):
        return pl.BlockSpec(
            (slots, PAIR), lambda b, p, f: (b, group(f) * 3 * pairs + part * pairs + p)
        )

    heads = pl.BlockSpec((slots, PAIR), lambda b, p, f: (b, group(f) * pairs + p))
    totals = pl.BlockSpec((1, 1, 2, slots), lambda b, p, f: (b, group(f) * pairs + p, 0, 0))
    width = 3 * pairs * PAIR
    return call(
        attend_back_kernel,
        "attend_back",
        (2, pairs),
        [at(0), at(1), at(2), heads, totals],
        [
            pl.BlockSpec((slots, width), lambda b, p, f: (b, 0)),
            pl.BlockSpec((1, 1, width), lambda b, p, f: (b, 0, 0)),
        ],
        [
            like((2 * slots, width), jnp.bfloat16),
            like((2, 1, width), jnp.float32),
        ],
        facts,
        projected,
        projected,
        projected,
        heads_grad,
        totals_in,
        wait=wait,
        through=through,
    )


def call(kernel, name, grid, inputs, outputs, shapes, facts, *args, wait=(), scratch=(), through=(), into=()):
    single = not isinstance(outputs, list)
    outputs, shapes = ([outputs], [shapes]) if single else (outputs, shapes)
    wait = tuple(into) + tuple(wait)
    count, held, passed = len(args), len(wait) + len(through), len(through)
    last = count + held + len(outputs)

    def body(facts_ref, *refs):
        kernel(facts_ref, *refs[:count], *refs[count + held : last], *refs[last + passed + 1 :])
        for place in range(facts.shape[0]):
            refs[last + passed][place] = facts_ref[place]

    results = pl.pallas_call(
        body,
        grid_spec=pltpu.PrefetchScalarGridSpec(
            num_scalar_prefetch=1,
            grid=grid,
            in_specs=list(inputs) + [pl.BlockSpec(memory_space=pl.ANY)] * held,
            out_specs=list(outputs)
            + [pl.BlockSpec(memory_space=pl.ANY)] * passed
            + [pl.BlockSpec(memory_space=pltpu.SMEM)],
            scratch_shapes=list(scratch),
        ),
        out_shape=list(shapes)
        + [like(value.shape, value.dtype) for value in through]
        + [like(facts.shape, jnp.int32)],
        input_output_aliases={
            **{1 + count + i: i for i in range(len(into))},
            **{1 + count + len(wait) + i: len(outputs) + i for i in range(passed)},
        },
        compiler_params=kernel_params(len(grid)),
        name=name,
    )(facts, *args, *wait, *through)
    values = tuple(results[:-1])
    return (values[0] if single and not passed else values), results[-1]


def block(shape, *index):
    def at(*grid_and_facts):
        return tuple(entry(*grid_and_facts) if callable(entry) else entry for entry in index)

    return pl.BlockSpec(shape, at)


def whole(array):
    zeros = (0,) * array.ndim
    return pl.BlockSpec(array.shape, lambda *_: zeros)


def first(i, *_):
    return i


def like(shape, dtype):
    return jax.ShapeDtypeStruct(shape, dtype)


def rows_in_order(facts_ref, own, beside):
    even = facts_ref[4] == 0
    pieces = []
    for z in range(4):
        pieces += [jnp.where(even, own[z], beside[z]), jnp.where(even, beside[z], own[z])]
    return jnp.concatenate(pieces, axis=0)


def near_or_far(facts_ref, refs, near):
    own, beside, below, across = [ref[...] for ref in refs]
    return rows_in_order(
        facts_ref, jnp.where(near, own, below), jnp.where(near, beside, across)
    )


def square_columns(parts, wide, steps):
    shape = parts[0].shape[:2] + (wide,)
    near = block(shape, 0, 0, lambda i, *_: jnp.minimum(i, steps - 1))
    far = block(shape, 0, 0, lambda i, *_: jnp.maximum(i - steps, 0))
    return [near, near, far, far]


def half_at(i, facts, steps):
    return jnp.where(i < steps, facts[3], 1 - facts[3])


def gate_kernel(facts_ref):
    del facts_ref


def gate(facts, through, wait):
    return call(gate_kernel, "gate", (1,), [], [], [], facts, wait=wait, through=through)


def stack_kernel(own_at, facts_ref, own_ref, other_ref, out_ref):
    own = facts_ref[own_at] == pl.program_id(0)
    value = jnp.where(own, own_ref[...], other_ref[...])
    out_ref[...] = value.reshape(out_ref.shape)


def stack_pair(facts, own, other, wait=(), through=()):
    rows, columns = own.shape
    return call(
        partial(stack_kernel, 6),
        "stack",
        (2,),
        [whole(own), whole(other)],
        block((1, rows, columns), first, 0, 0),
        like((2, rows, columns), own.dtype),
        facts,
        own,
        other,
        wait=wait,
        through=through,
    )


def stack_line(facts, own, other, wait=()):
    _, rows, columns = own.shape
    line, facts = call(
        partial(stack_kernel, 7),
        "stack_line",
        (2,),
        [whole(own), whole(other)],
        block((2, 1, rows, columns), 0, first, 0, 0),
        like((2, 2, rows, columns), own.dtype),
        facts,
        own,
        other,
        wait=wait,
    )
    return line.reshape(4, rows, columns), facts


def turn_kernel(facts_ref, *refs):
    for i in range(2):
        refs[4 + i][...] = jnp.concatenate([refs[2 * i][...].T, refs[2 * i + 1][...].T], axis=1)


def turn_all_kernel(facts_ref, rows_ref, out_ref):
    out_ref[...] = rows_ref[...].T


def turn_all(facts, values, wait=()):
    count, width = values.shape
    step = width // 4
    return call(
        turn_all_kernel,
        "turn_all",
        (4,),
        [block((count, step), 0, first)],
        block((step, count), first, 0),
        like((width, count), values.dtype),
        facts,
        values,
        wait=wait,
    )


def turn(facts, values, others, rows, wait=()):
    count, width = values.shape
    half = width // 2
    out = block((rows, 2 * count), first, 0)
    shape = like((half, 2 * count), values.dtype)
    own = block((count, rows), 0, lambda i, f: 2 * i + f[4])
    other = block((count, rows), 0, lambda i, f: 2 * i + 1 - f[4])
    return call(
        turn_kernel,
        "turn",
        (half // rows,),
        [own, own, other, other],
        [out, out],
        [shape, shape],
        facts,
        values,
        others,
        values,
        others,
        wait=wait,
    )


def project_kernel(facts_ref, rows_ref, bias_ref, *refs):
    parts, (out_ref, in_ref, rest_ref) = refs[:4], refs[4:]
    step = pl.program_id(0)
    weight = near_or_far(facts_ref, parts, step < 4)

    @pl.when(step % 4 < 3)
    def _():
        in_ref[...] = weight
        value = product(rows_ref[...], weight, 1, 0) + bias_ref[...]
        out_ref[...] = value.astype(jnp.bfloat16)

    @pl.when(step % 4 == 3)
    def _():
        chips, count, wide = rest_ref.shape
        pairs = weight.reshape(chips, 2, count, wide // 2)
        rest_ref[...] = jnp.concatenate([pairs[:, 0], pairs[:, 1]], axis=2)


def project(facts, rows, bias, parts, wait=()):
    count, width = rows.shape
    wide = parts[0].shape[2] // 4

    def column(i, f):
        return half_at(i, f, 4) * 3 + jnp.minimum(i % 4, 2)

    out = block((count, wide), 0, column)
    rest = (8, parts[0].shape[1] // 2, 2 * wide)
    return call(
        project_kernel,
        "project",
        (8,),
        [whole(rows), block((1, wide), 0, column)] + square_columns(parts, wide, 4),
        [out, block((width, wide), 0, column), block(rest, 0, 0, lambda i, f: half_at(i, f, 4))],
        [
            like((count, 6 * wide), jnp.bfloat16),
            like((width, 6 * wide), jnp.bfloat16),
            like(rest[:2] + (4 * wide,), jnp.bfloat16),
        ],
        facts,
        rows,
        bias[None],
        *parts,
        wait=wait,
    )


def valid_rows(facts_ref, count, slots):
    place = lax.broadcasted_iota(jnp.int32, (count, 1), 0) + pl.program_id(0) * count + facts_ref[2]
    place = jnp.where(place >= slots, place - slots, place)
    return (place < facts_ref[0]).astype(jnp.float32)


def add_rows(sums_ref, rows):
    total = jnp.concatenate([jnp.sum(part, axis=0, keepdims=True) for part in rows], axis=0)
    total = jnp.concatenate([total, jnp.zeros((8 - len(rows), total.shape[1]), jnp.float32)], axis=0)

    @pl.when(pl.program_id(0) == 0)
    def _():
        sums_ref[...] = total

    @pl.when(pl.program_id(0) > 0)
    def _():
        sums_ref[...] += total


def mean_of(values):
    return jnp.mean(values, axis=-1, keepdims=True)


def attend_out_kernel(
    slots, facts_ref, own_ref, other_ref, own_weight_ref, other_weight_ref, tokens_ref, vectors_ref,
    hat_ref, rstd_ref, low_ref, sums_ref,
):
    branch = (
        product(own_ref[...], own_weight_ref[...], 1, 0)
        + product(other_ref[...], other_weight_ref[...], 1, 0)
        + vectors_ref[0:1]
    )
    tokens = tokens_ref[...].astype(jnp.float32)
    total = tokens + branch
    centered = total - mean_of(total)
    rstd = lax.rsqrt(mean_of(centered * centered) + 1e-05)
    hat = centered * rstd
    hat_ref[...] = hat
    rstd_ref[...] = rstd
    low_ref[...] = (hat * vectors_ref[1:2] + vectors_ref[2:3]).astype(jnp.bfloat16)
    valid = valid_rows(facts_ref, tokens.shape[0], slots)
    add_rows(sums_ref, [valid * tokens * tokens, valid * branch * branch])


def attend_out(facts, own, other, own_weight, other_weight, tokens, vectors, wait=()):
    slots, width = tokens.shape
    step = slots // 4
    rows = lambda array: block((step, array.shape[1]), first, 0)
    return call(
        partial(attend_out_kernel, slots),
        "attend_out",
        (4,),
        [rows(own), rows(other), whole(own_weight), whole(other_weight), rows(tokens), whole(vectors)],
        [block((step, width), first, 0), block((step, 1), first, 0), block((step, width), first, 0), block((8, width), 0, 0)],
        [
            like((slots, width), jnp.float32),
            like((slots, 1), jnp.float32),
            like((slots, width), jnp.bfloat16),
            like((8, width), jnp.float32),
        ],
        facts,
        own,
        other,
        own_weight,
        other_weight,
        tokens,
        vectors,
        wait=wait,
    )


def up_kernel(facts_ref, rows_ref, others_ref, bias_ref, *refs):
    parts, (act_ref, slope_ref, turned_ref, weight_ref) = refs[:4], refs[4:]
    weight = near_or_far(facts_ref, parts, pl.program_id(0) < 4)
    weight_ref[...] = weight
    pre_act = [product(ref[...], weight, 1, 0) for ref in (rows_ref, others_ref)]
    pre_act = jnp.concatenate(pre_act, axis=0) + bias_ref[...]
    below = 0.5 + 0.5 * lax.erf(pre_act * 0.7071067811865476)
    act = (pre_act * below).astype(jnp.bfloat16)
    act_ref[...] = act
    turned_ref[...] = act.T
    slope = below + pre_act * (0.3989422804014327 * jnp.exp(-0.5 * pre_act * pre_act))
    slope_ref[...] = slope.astype(jnp.bfloat16)


def feed_up(facts, rows, others, bias, parts, wait=()):
    count, width = 2 * rows.shape[0], rows.shape[1]
    units = bias.shape[0]
    wide = units // 8

    def column(i, f):
        return half_at(i, f, 4) * 4 + i % 4

    shape = like((count, units), jnp.bfloat16)
    out = block((count, wide), 0, column)
    return call(
        up_kernel,
        "feed_up",
        (8,),
        [whole(rows), whole(others), block((1, wide), 0, column)] + square_columns(parts, wide, 4),
        [out, out, block((wide, count), column, 0), block((width, wide), 0, column)],
        [
            shape,
            shape,
            like((units, count), jnp.bfloat16),
            like((width, units), jnp.bfloat16),
        ],
        facts,
        rows,
        others,
        bias[None],
        *parts,
        wait=wait,
    )


def down_kernel(facts_ref, rows_ref, *refs):
    parts, (weight_ref, out_ref, total_ref) = refs[:4], refs[4:]
    step = pl.program_id(0)
    own, beside, below, across = [ref[0] for ref in parts]
    even, left = facts_ref[4] == 0, facts_ref[3] == 0
    for x in range(2):
        mine = jnp.where(even, own, beside) if x == 0 else jnp.where(even, beside, own)
        theirs = jnp.where(even, below, across) if x == 0 else jnp.where(even, across, below)
        weight_ref[x] = jnp.concatenate(
            [jnp.where(left, mine, theirs), jnp.where(left, theirs, mine)], axis=1
        )
    weight = weight_ref[...].reshape(rows_ref.shape[1], out_ref.shape[1])
    value = product(rows_ref[...], weight, 1, 0)

    @pl.when(step == 0)
    def _():
        total_ref[...] = value

    @pl.when(step > 0)
    def _():
        total_ref[...] += value

    @pl.when(step == 3)
    def _():
        out_ref[...] = total_ref[...].astype(jnp.bfloat16)


def feed_down(facts, rows, parts, wait=()):
    count, units = rows.shape
    _, block_rows, half_width = parts[0].shape
    width = 2 * half_width
    shape = (1,) + parts[0].shape[1:]
    return call(
        down_kernel,
        "feed_down",
        (4,),
        [block((count // 2, units // 4), 1, first)] + [block(shape, first, 0, 0)] * 4,
        [block((2, block_rows, width), first, 0, 0), block((count // 2, width), 0, 0)],
        [like((8, block_rows, width), jnp.bfloat16), like((count // 2, width), jnp.bfloat16)],
        facts,
        rows,
        *parts,
        scratch=[pltpu.VMEM((count // 2, width), jnp.float32)],
        wait=wait,
    )


def second_norm_kernel(
    slots, facts_ref, part_ref, other_ref, hat_ref, cotangent_ref, vectors_ref,
    mixed_ref, grad_ref, low_ref, sums_ref,
):
    branch = part_ref[...] + other_ref[...].astype(jnp.float32) + vectors_ref[0:1]
    hidden = hat_ref[...] * vectors_ref[1:2] + vectors_ref[2:3]
    gain = vectors_ref[3:4]
    total = hidden + branch
    centered = total - mean_of(total)
    rstd = lax.rsqrt(mean_of(centered * centered) + 1e-05)
    hat = centered * rstd
    mixed_ref[...] = (hat * gain + vectors_ref[4:5]).astype(jnp.bfloat16)
    valid = valid_rows(facts_ref, branch.shape[0], slots)
    grad = cotangent_ref[...].astype(jnp.float32) * valid
    scaled = grad * gain
    result = rstd * (scaled - mean_of(scaled) - hat * mean_of(scaled * hat))
    low = result.astype(jnp.bfloat16)
    grad_ref[...] = result
    low_ref[...] = low
    add_rows(sums_ref, [low.astype(jnp.float32), grad * hat, grad, valid * branch * branch])


def second_norm(facts, part, other, hat, cotangent, vectors, wait=()):
    slots, width = part.shape
    step = slots // 4
    rows = block((step, width), first, 0)
    return call(
        partial(second_norm_kernel, slots),
        "second_norm",
        (4,),
        [rows, rows, rows, rows, whole(vectors)],
        [rows, rows, rows, block((8, width), 0, 0)],
        [
            like((slots, width), jnp.bfloat16),
            like((slots, width), jnp.float32),
            like((slots, width), jnp.bfloat16),
            like((8, width), jnp.float32),
        ],
        facts,
        part,
        other,
        hat,
        cotangent,
        vectors,
        wait=wait,
    )


def first_norm_kernel(
    facts_ref, part_ref, other_ref, second_ref, hat_ref, rstd_ref, vectors_ref,
    grad_ref, low_ref, sums_ref,
):
    grad = part_ref[...] + other_ref[...].astype(jnp.float32) + second_ref[...]
    hat = hat_ref[...]
    scaled = grad * vectors_ref[1:2]
    result = rstd_ref[...] * (scaled - mean_of(scaled) - hat * mean_of(scaled * hat))
    low = result.astype(jnp.bfloat16)
    grad_ref[...] = result
    low_ref[...] = low
    add_rows(sums_ref, [low.astype(jnp.float32), grad * hat, grad])


def first_norm(facts, part, other, second, hat, rstd, vectors, wait=()):
    slots, width = part.shape
    step = slots // 4
    rows = block((step, width), first, 0)
    return call(
        first_norm_kernel,
        "first_norm",
        (4,),
        [rows, rows, rows, rows, block((step, 1), first, 0), whole(vectors)],
        [rows, rows, block((8, width), 0, 0)],
        [
            like((slots, width), jnp.float32),
            like((slots, width), jnp.bfloat16),
            like((8, width), jnp.float32),
        ],
        facts,
        part,
        other,
        second,
        hat,
        rstd,
        vectors,
        wait=wait,
    )


def act_grad_kernel(facts_ref, rows_ref, weight_ref, slope_ref, out_ref, sums_ref):
    total = product(rows_ref[...], weight_ref[...], 1, 1)
    grad = total.astype(jnp.bfloat16).astype(jnp.float32) * slope_ref[...].astype(jnp.float32)
    low = grad.astype(jnp.bfloat16)
    out_ref[...] = low
    sums_ref[...] = jnp.sum(low.astype(jnp.float32), axis=0, keepdims=True)


def act_grad(facts, rows, weight, slope, wait=()):
    count, units = slope.shape
    step = units // 8
    out = block((count, step), 0, first)
    return call(
        act_grad_kernel,
        "act_grad",
        (8,),
        [whole(rows), block((step, rows.shape[1]), first, 0), out],
        [out, block((1, step), 0, first)],
        [like((count, units), jnp.bfloat16), like((1, units), jnp.float32)],
        facts,
        rows,
        weight,
        slope,
        wait=wait,
    )


def tokens_grad_kernel(facts_ref, mine_ref, theirs_ref, weight_ref, out_ref, sent_ref):
    wide = mine_ref.shape[1]
    slots = out_ref.shape[0]
    half = facts_ref[3]
    mine = weight_ref[:, pl.ds(pl.multiple_of(half * wide, 128), wide)]
    theirs = weight_ref[:, pl.ds(pl.multiple_of((1 - half) * wide, 128), wide)]
    total = product(mine_ref[...], mine, 1, 1) + product(theirs_ref[...], theirs, 1, 1)
    out_ref[...] = total[:slots]
    sent_ref[...] = total[slots:].astype(sent_ref.dtype)


def tokens_grad(facts, mine, theirs, weight, wait=(), through=()):
    count, columns = mine.shape
    width = weight.shape[0]
    step = width // 4
    out = block((count // 2, step), 0, first)
    return call(
        tokens_grad_kernel,
        "tokens_grad",
        (4,),
        [whole(mine), whole(theirs), block((step, 2 * columns), first, 0)],
        [out, out],
        [
            like((count // 2, width), jnp.float32),
            like((count // 2, width), jnp.bfloat16),
        ],
        facts,
        mine,
        theirs,
        weight,
        wait=wait,
        through=through,
    )


def add_parts_kernel(facts_ref, own_ref, got_ref, kept_ref, sent_ref):
    step = pl.program_id(0)
    total = own_ref[...].astype(jnp.float32) + got_ref[...].astype(jnp.float32)
    total = total.astype(jnp.bfloat16)

    @pl.when(step < 2)
    def _():
        sent_ref[...] = total

    @pl.when(step >= 2)
    def _():
        kept_ref[...] = total


def add_last_kernel(facts_ref, own_ref, got_ref, kept_ref, sent_ref):
    total = own_ref[0].astype(jnp.float32) + got_ref[0].astype(jnp.float32)
    total = total.astype(jnp.bfloat16)

    @pl.when(pl.program_id(0) == 0)
    def _():
        sent_ref[...] = total

    @pl.when(pl.program_id(0) == 1)
    def _():
        kept_ref[...] = total


def add_last(facts, own, got, wait=(), through=()):
    _, rows, columns = own.shape
    part = block((1, rows, columns), lambda i, f: jnp.where(i == 0, 1 - f[6], f[6]), 0, 0)
    shape = like((rows, columns), jnp.bfloat16)
    out = block((rows, columns), 0, 0)
    return call(
        add_last_kernel,
        "add_last",
        (2,),
        [part, part],
        [out, out],
        [shape, shape],
        facts,
        own,
        got,
        wait=wait,
        through=through,
    )


def add_parts(facts, own, got, wait=(), through=()):
    _, rows, columns = own.shape
    shape = (1, rows, columns)
    part = block(shape, lambda i, f: 2 * (i % 2) + jnp.where(i < 2, 1 - f[7], f[7]), 0, 0)
    half = like((2, rows, columns), jnp.bfloat16)
    return call(
        add_parts_kernel,
        "add_parts",
        (4,),
        [part, part],
        [
            block(shape, lambda i, *_: jnp.maximum(i - 2, 0), 0, 0),
            block(shape, lambda i, *_: jnp.minimum(i, 1), 0, 0),
        ],
        [half, half],
        facts,
        own,
        got,
        wait=wait,
        through=through,
    )


def alternate(value, width, offset):
    starts = range(offset * width, value.shape[1], 2 * width)
    return jnp.concatenate([value[:, start : start + width] for start in starts], axis=1)


def deal_kernel(unit_block, core_ref, query_ref, key_ref, value_ref, up_ref, *refs):
    first_core = core_ref[0] == 0
    near = [ref[...] for ref in (query_ref, key_ref, value_ref)]
    even = jnp.concatenate([alternate(value, HD, 0) for value in near], axis=1)
    odd = jnp.concatenate([alternate(value, HD, 1) for value in near], axis=1)
    up = up_ref[...]
    up_even, up_odd = alternate(up, unit_block, 0), alternate(up, unit_block, 1)
    refs[0][...] = jnp.where(first_core, even, odd)
    refs[1][...] = jnp.where(first_core, odd, even)
    refs[2][...] = jnp.where(first_core, up_even, up_odd)
    refs[3][...] = jnp.where(first_core, up_odd, up_even)


def deal(core, query, key, value, up, unit_block):
    near = like((query.shape[0], 3 * query.shape[1] // 2), jnp.bfloat16)
    half = like((up.shape[0], up.shape[1] // 2), jnp.bfloat16)
    shapes = [near, near, half, half]
    return call(
        partial(deal_kernel, unit_block),
        "deal",
        (1,),
        [whole(value) for value in (query, key, value, up)],
        [whole(shape) for shape in shapes],
        shapes,
        core,
        query,
        key,
        value,
        up,
    )


def lay_out_kernel(core_ref, near_ref, near_got_ref, out_ref, up_ref, up_got_ref, *refs):
    first_core = core_ref[0] == 0
    near, near_got, up, up_got = [
        ref[...] for ref in (near_ref, near_got_ref, up_ref, up_got_ref)
    ]
    out = out_ref[...]
    wide = out.shape[1] // 2
    near_rows = jnp.concatenate(
        [jnp.where(first_core, near, near_got), jnp.where(first_core, near_got, near)], axis=0
    )
    out_rows = jnp.concatenate([out[:, :wide], out[:, wide:]], axis=0)
    refs[0][...] = jnp.concatenate([near_rows, out_rows], axis=1)
    refs[1][...] = jnp.concatenate(
        [jnp.where(first_core, up, up_got), jnp.where(first_core, up_got, up)], axis=0
    )


def lay_out(core, near, near_got, out, up, up_got):
    rows = 2 * near.shape[0]
    shapes = [
        like((rows, near.shape[1] + out.shape[1] // 2), jnp.bfloat16),
        like((rows, up.shape[1]), jnp.bfloat16),
    ]
    arrays = (near, near_got, out, up, up_got)
    return call(
        lay_out_kernel,
        "lay_out",
        (1,),
        [whole(value) for value in arrays],
        [whole(shape) for shape in shapes],
        shapes,
        core,
        *arrays,
    )[0]


def split_body(
    tokens,
    lengths,
    cotangent,
    query_weight,
    key_weight,
    value_weight,
    out_weight,
    up_weight,
    down_weight,
    query_bias,
    value_bias,
    out_bias,
    attn_gain,
    attn_shift,
    up_bias,
    down_bias,
    feed_gain,
    feed_shift,
):
    core = lax.axis_index("c")
    half = lax.axis_index("s")
    row_count, width = tokens.shape[1:]
    slots = 2 * row_count
    unit_block = down_weight.shape[0]
    units = up_bias.shape[0] // 2
    cols = width // 2
    wide = cols // 2

    def to_sequence(values):
        return jnp.concatenate([pick(values, half, 0), swap(pick(values, 1 - half, 0), "s")], axis=0)

    def from_sequence(values):
        return in_order(values[:row_count], swap(values[row_count:], "s"), half)

    place = jnp.stack([core]).astype(jnp.int32)
    (near_kept, near_sent, up_kept, up_sent), place = deal(
        place, query_weight, key_weight, value_weight, up_weight, unit_block
    )
    near_mine, up_mine = lay_out(
        place, near_kept, swap(near_sent, "c"), out_weight, up_kept, swap(up_sent, "c")
    )
    rows, up_cols = up_mine.shape
    line = lax.axis_index("z")
    length_own = lax.dynamic_slice_in_dim(lengths, half, 1, 0)
    facts = jnp.concatenate(
        [
            both(length_own, "c"),
            jnp.stack(
                [
                    half * row_count,
                    half,
                    lax.axis_index("x"),
                    jnp.int32(0),
                    line // 2,
                    line % 2,
                ]
            ).astype(jnp.int32),
        ]
    )
    tokens_own = to_sequence(tokens)
    cotangent_own = to_sequence(cotangent)
    (near, up_mine, down_mine), facts = stack_pair(
        facts,
        near_mine,
        line_cross(near_mine),
        wait=(tokens_own,),
        through=(up_mine, down_weight),
    )
    near, facts = stack_line(facts, near, line_next(near), wait=(cotangent_own,))
    near_parts = gather_square(near, "x")
    up_pairs, facts = stack_pair(facts, up_mine, line_cross(up_mine), wait=(near,))
    tokens_both = both(tokens_own, "c")
    up_part, facts = stack_line(
        facts, up_pairs, line_next(up_pairs), wait=(near_parts[1], near_parts[2])
    )
    up_parts = gather_square(up_part, "s")
    down_pairs, facts = stack_pair(facts, down_mine, line_cross(down_mine), wait=(up_part,))
    def halves_of(vector, size):
        return pick(vector.reshape(-1, 2, size), core, 1).reshape(-1)

    query_part = halves_of(query_bias, HD).reshape(2, wide)
    value_part = halves_of(value_bias, HD).reshape(2, wide)
    in_bias = jnp.stack([query_part, jnp.zeros_like(query_part), value_part], axis=1).reshape(-1)
    (projected, in_weight, out_own), facts = project(
        facts, tokens_both, in_bias, near_parts, wait=(down_pairs,)
    )
    out_own = out_own.reshape(cols, width)
    out_other = swap(out_own, "c")
    down_part, facts = stack_line(facts, down_pairs, line_next(down_pairs), wait=(projected,))
    down_parts = gather_square(down_part, "x")
    (heads_out, totals), facts = attend(facts, projected, slots, wait=(up_parts[2],))
    heads_other = swap(heads_out[slots:], "c")
    vectors = jnp.stack(
        [out_bias, attn_gain, attn_shift, down_bias, feed_gain, feed_shift, out_bias, out_bias]
    )
    (first_hat, first_rstd, hidden_low, first_sums), facts = attend_out(
        facts,
        heads_out,
        heads_other,
        out_own,
        out_other,
        tokens_own,
        vectors,
        wait=(up_parts[1], down_parts[2]),
    )
    (hidden_low,), facts = gate(facts, (hidden_low,), (up_parts[3], down_parts[1]))
    hidden_from = swap(hidden_low, "c")
    (activation, slope, act_t, up_all), facts = feed_up(
        facts, hidden_low, hidden_from, halves_of(up_bias, unit_block), up_parts
    )
    hidden_turned, facts = turn(facts, hidden_low, hidden_from, rows, wait=(act_t,))
    (down_all, feed_sent), facts = feed_down(facts, activation, down_parts)
    down_all = down_all.reshape(units, width)
    feed_other = swap(feed_sent, "c")
    feed_part = product(activation[:slots], down_all, 1, 0)
    feed_vectors = jnp.stack(
        [down_bias, attn_gain, attn_shift, feed_gain, feed_shift, out_bias, out_bias, out_bias]
    )
    (mixed, second_grad, feed_low, second_sums), facts = second_norm(
        facts, feed_part, feed_other, first_hat, cotangent_own, feed_vectors
    )

    mixed_got = swap(mixed[row_count:], "s")

    feed_both = both(feed_low, "c")
    tokens_t, facts = turn_all(facts, tokens_both, wait=(feed_low,))
    feed_mine, feed_theirs = columns_of(feed_both, half), columns_of(feed_both, 1 - half)
    down_sent = grad_block(act_t, feed_theirs)
    down_got = swap(down_sent, "s")
    (pre_grad, up_bias_grad), facts = act_grad(
        facts, feed_both, down_all, slope, wait=(down_sent,)
    )
    hidden_sent = product(pre_grad[slots:], up_all, 1, 1).astype(jnp.bfloat16)
    hidden_other = swap(hidden_sent, "c")
    hidden_own_t, hidden_other_t = hidden_turned
    up_sent = grad_block(hidden_other_t, pre_grad)
    up_got = swap(up_sent, "x")
    hidden_part = product(pre_grad[:slots], up_all, 1, 1)
    (first_grad, attn_low, third_sums), facts = first_norm(
        facts,
        hidden_part,
        hidden_other,
        second_grad,
        first_hat,
        first_rstd,
        vectors,
        wait=(up_sent,),
    )
    grad_sent = product(attn_low, out_other, 1, 1).astype(jnp.bfloat16)
    grad_other = swap(grad_sent, "c")
    grad_own = product(attn_low, out_own, 1, 1).astype(jnp.bfloat16)
    out_sent = product(heads_other, attn_low, 0, 0).astype(jnp.bfloat16)
    out_got = swap(out_sent, "c")
    out_grad = grad_block(heads_out[:slots].T, attn_low, out_got)
    out_line = out_grad.reshape((4, 2 * out_weight.shape[0], width))
    out_kept, out_sent = line_parts(out_line)
    out_got = lax.ppermute(out_sent, "z", NEXT)
    heads_grad = jnp.concatenate([grad_own, grad_other], axis=0)
    (theirs_low, theirs_sums), facts = attend_back(
        facts, projected, heads_grad, totals, slots, False, wait=(out_sent, mixed_got)
    )
    in_sent = grad_block(tokens_t, theirs_low)
    in_got = swap(in_sent, "s")
    down_total = grad_block(act_t, feed_mine, down_got)
    down_kept, down_sent = halve(down_total.reshape(4, 2, unit_block, cols), "x", 1)
    down_got = swap(down_sent, "x")
    out_total = add(out_kept, out_got)
    upper = lax.axis_index("z") // 2
    out_kept, out_sent = pick(out_total, upper, 0), pick(out_total, 1 - upper, 0)
    out_got = lax.ppermute(out_sent, "z", CROSS)
    (mine_low, mine_sums), facts = attend_back(
        facts, projected, heads_grad, totals, slots, True, wait=(in_sent, out_sent, down_sent)
    )
    up_total = grad_block(hidden_own_t, pre_grad, up_got).reshape(4, rows, 2 * up_cols)
    up_kept, up_sent = line_parts(up_total)
    up_got = lax.ppermute(up_sent, "z", NEXT)
    out_kept = add(out_kept, out_got)
    valid_count = length_own[0].astype(jnp.float32) * width
    stats = jnp.stack(
        [jnp.sum(first_sums[0]), jnp.sum(first_sums[1]), jnp.sum(second_sums[3]), valid_count]
    )
    mine_sums, theirs_sums = jnp.sum(mine_sums, axis=(0, 1)), jnp.sum(theirs_sums, axis=(0, 1))
    late = in_order(mine_sums, theirs_sums, half)
    sums = jnp.concatenate(
        [
            second_sums[:3].reshape(-1),
            third_sums[:3].reshape(-1),
            jnp.pad(stats, (0, 124)),
            up_bias_grad[0],
            late[:, :wide].reshape(-1),
            late[:, 2 * wide :].reshape(-1),
        ]
    )
    sums_got = lax.ppermute(sums, "z", NEXT)
    (tokens_part, tokens_sent), facts = tokens_grad(
        facts,
        mine_low,
        theirs_low,
        in_weight,
        wait=(up_sent, out_kept, sums),
    )
    tokens_other = swap(tokens_sent, "c")
    in_total = grad_block(tokens_t, mine_low, in_got)
    in_kept, in_sent = halve(in_total.reshape(4, 2, rows, 3 * wide), "x", 1)
    in_got = swap(in_sent, "x")
    (down_pairs, down_next), facts = add_parts(
        facts, down_kept, down_got, wait=(in_sent, tokens_part)
    )
    down_got = lax.ppermute(down_next, "z", NEXT)
    (up_kept, up_next), facts = add_last(facts, up_kept, up_got, wait=(down_next,))
    up_got = lax.ppermute(up_next, "z", CROSS)
    (in_pairs, in_next, down_pairs, sums), facts = add_parts(
        facts, in_kept, in_got, wait=(up_next,), through=(down_pairs, sums + sums_got)
    )
    in_got = lax.ppermute(in_next, "z", NEXT)
    sums = sums + swap(sums, "x")
    sums = sums + swap(sums, "s")
    (in_kept, in_sent, out_kept, up_kept), facts = add_last(
        facts, in_pairs, in_got, wait=(sums,), through=(out_kept, up_kept)
    )
    in_sum = add(in_kept, lax.ppermute(in_sent, "z", CROSS))
    tokens_grad_sum = tokens_part + tokens_other.astype(jnp.float32) + first_grad
    tokens_grad_sum = from_sequence(tokens_grad_sum.astype(jnp.bfloat16))
    mixed = in_order(mixed[:row_count], mixed_got, half)
    down_sum = fold_cross(add(down_pairs, down_got))
    up_sum = fold_columns(add(up_kept, up_got))
    out_sum = fold_columns(fold(out_kept.reshape(2, out_weight.shape[0], width), "x", 0))

    sums = sums + lax.ppermute(sums, "z", CROSS)
    both_sums = in_order(sums, swap(sums, "c"), core)
    count = 6 * width + 128
    shared = both_sums[0, :count] + both_sums[1, :count]
    down_bias_grad, feed_gain_grad, feed_shift_grad, out_bias_grad, attn_gain_grad, attn_shift_grad = [
        shared[i * width : (i + 1) * width] for i in range(6)
    ]
    stats = shared[6 * width : 6 * width + 4]

    def interleave(start, size, block_size):
        sums = both_sums[:, start : start + size].reshape(2, -1, block_size)
        return sums.transpose(1, 0, 2).reshape(-1)

    up_bias_grad = interleave(count, units, unit_block)
    query_bias_grad = interleave(count + units, cols, HD)
    value_bias_gradient = interleave(count + units + cols, cols, HD)
    stream_rms = jnp.sqrt(stats[:3] / stats[3])

    def give_back(total):
        total = total.reshape((2, rows // 2) + total.shape[1:])
        return pick(total, core, 0), swap(pick(total, 1 - core, 0), "c")

    up_shares = give_back(up_sum)
    in_shares = give_back(in_sum)
    down_weight_grad = down_sum.astype(jnp.float32)
    out_weight_grad = out_sum.astype(jnp.float32)

    def merge(shares, start, size, block):
        one, two = [
            share[:, start : start + size].reshape(rows // 2, -1, block) for share in shares
        ]
        first = jnp.where(core == 0, one, two)
        second = jnp.where(core == 0, two, one)
        return jnp.stack([first, second], axis=2).reshape(rows // 2, -1).astype(jnp.float32)

    query_weight_grad = merge(in_shares, 0, wide, HD)
    key_weight_grad = merge(in_shares, wide, wide, HD)
    value_weight_grad = merge(in_shares, 2 * wide, wide, HD)
    up_weight_grad = merge(up_shares, 0, up_cols, unit_block)
    return (
        mixed,
        tokens_grad_sum,
        query_weight_grad,
        key_weight_grad,
        value_weight_grad,
        out_weight_grad,
        up_weight_grad,
        down_weight_grad,
        query_bias_grad,
        value_bias_gradient,
        out_bias_grad,
        attn_gain_grad,
        attn_shift_grad,
        up_bias_grad,
        down_bias_grad,
        feed_gain_grad,
        feed_shift_grad,
        stream_rms,
    )


def solution(mesh):
    devices = mesh.devices
    dp_count, seq_count = devices.shape
    split = seq_count == 2 and dp_count == 16
    if split:
        inner = jax.sharding.Mesh(devices.reshape(4, 2, 2, seq_count), ("z", "x", "c", "s"))
        dp, seq, body = ("z", "x", "c"), "s", split_body
    else:
        inner, dp, seq, body = mesh, "dp", "seq", general_body
    weights = (P(dp, seq),) * 6
    vectors = (P(),) * 9
    rows = P(dp, seq, None)
    in_specs = (rows, P(dp), rows) + weights + vectors
    out_specs = (rows, rows) + weights + vectors + (P(),)
    return jax.shard_map(body, mesh=inner, in_specs=in_specs, out_specs=out_specs, check_vma=False)
```

```python
from functools import partial
import math

import jax
import jax.numpy as jnp
from jax import lax
from jax.experimental import pallas as pl
from jax.experimental.pallas import tpu as pltpu
from jax.sharding import PartitionSpec as P

HD = 64


def layer_norm(values_in, gain_vector, shift_vector):
    mean_value = jnp.mean(values_in, axis=-1, keepdims=True)
    centered = values_in - mean_value
    variance = jnp.mean(centered * centered, axis=-1, keepdims=True)
    return centered * lax.rsqrt(variance + 1e-05) * gain_vector + shift_vector


def gather_weights(first, second, third, fourth, fifth, sixth):
    part = (
        lax.all_gather(first, "dp", axis=0, tiled=True),
        lax.all_gather(second, "dp", axis=0, tiled=True),
        lax.all_gather(third, "dp", axis=0, tiled=True),
        lax.all_gather(fourth, "dp", axis=0, tiled=True),
        lax.all_gather(fifth, "dp", axis=0, tiled=True),
        lax.all_gather(sixth, "dp", axis=0, tiled=True),
    )
    return (
        lax.all_gather(part[0], "seq", axis=1, tiled=True),
        lax.all_gather(part[1], "seq", axis=1, tiled=True),
        lax.all_gather(part[2], "seq", axis=1, tiled=True),
        lax.all_gather(part[3], "seq", axis=1, tiled=True),
        lax.all_gather(part[4], "seq", axis=1, tiled=True),
        lax.all_gather(part[5], "seq", axis=1, tiled=True),
    )


def reduce_grads(first, second, third, fourth, fifth, sixth):
    part = (
        lax.psum_scatter(first.astype(jnp.bfloat16), "seq", scatter_dimension=1, tiled=True).astype(
            jnp.float32
        ),
        lax.psum_scatter(
            second.astype(jnp.bfloat16), "seq", scatter_dimension=1, tiled=True
        ).astype(jnp.float32),
        lax.psum_scatter(third.astype(jnp.bfloat16), "seq", scatter_dimension=1, tiled=True).astype(
            jnp.float32
        ),
        lax.psum_scatter(
            fourth.astype(jnp.bfloat16), "seq", scatter_dimension=1, tiled=True
        ).astype(jnp.float32),
        lax.psum_scatter(fifth.astype(jnp.bfloat16), "seq", scatter_dimension=1, tiled=True).astype(
            jnp.float32
        ),
        lax.psum_scatter(sixth.astype(jnp.bfloat16), "seq", scatter_dimension=1, tiled=True).astype(
            jnp.float32
        ),
    )
    return (
        lax.psum_scatter(
            part[0].astype(jnp.bfloat16), "dp", scatter_dimension=0, tiled=True
        ).astype(jnp.float32),
        lax.psum_scatter(
            part[1].astype(jnp.bfloat16), "dp", scatter_dimension=0, tiled=True
        ).astype(jnp.float32),
        lax.psum_scatter(
            part[2].astype(jnp.bfloat16), "dp", scatter_dimension=0, tiled=True
        ).astype(jnp.float32),
        lax.psum_scatter(
            part[3].astype(jnp.bfloat16), "dp", scatter_dimension=0, tiled=True
        ).astype(jnp.float32),
        lax.psum_scatter(
            part[4].astype(jnp.bfloat16), "dp", scatter_dimension=0, tiled=True
        ).astype(jnp.float32),
        lax.psum_scatter(
            part[5].astype(jnp.bfloat16), "dp", scatter_dimension=0, tiled=True
        ).astype(jnp.float32),
    )


def block_layout(seq_count, row_count, head_count):
    block_seqs = math.gcd(seq_count, max(1, 512 // row_count))
    group_heads = math.gcd(head_count, 4)
    return (block_seqs, seq_count // block_seqs, group_heads, head_count // group_heads)


def head_slice(block_part, offset, group_width, group_heads):
    sliced = lax.dynamic_slice_in_dim(block_part, offset, group_width, 2)
    return sliced.reshape(sliced.shape[0], sliced.shape[1], group_heads, HD)


def attention_forward(queries, key_all, value_all, key_mask):
    seq_count, row_count, feature_total = queries.shape
    slot_count = key_all.shape[1]
    block_seqs, block_count, group_heads, group_count = block_layout(
        seq_count, row_count, feature_total // HD
    )
    group_width = group_heads * HD

    def seq_block(inputs):
        query_part, key_part, value_part, mask_part = inputs

        def head_block(group_index):
            offset = group_index * group_width
            query_heads = head_slice(query_part, offset, group_width, group_heads)
            key_heads = head_slice(key_part, offset, group_width, group_heads)
            value_heads = head_slice(value_part, offset, group_width, group_heads)
            scores = (
                jnp.einsum(
                    "brhd,bkhd->bhrk", query_heads, key_heads, preferred_element_type=jnp.float32
                )
                * 0.125
            )
            scores = jnp.where(mask_part[:, None, None, :], scores, -1e30)
            row_max = jnp.max(scores, axis=-1, keepdims=True)
            exponent = jnp.exp(scores - row_max)
            row_total = jnp.sum(exponent, axis=-1, keepdims=True)
            soft_probs = (exponent / row_total).astype(jnp.bfloat16)
            heads_out = jnp.einsum(
                "bhrk,bkhd->brhd", soft_probs, value_heads, preferred_element_type=jnp.float32
            )
            log_total = (row_max + jnp.log(row_total))[..., 0]
            return (heads_out.reshape(block_seqs, row_count, group_width), log_total)

        return lax.map(head_block, jnp.arange(group_count))

    outputs, log_totals = lax.map(
        seq_block,
        (
            queries.reshape(block_count, block_seqs, row_count, feature_total),
            key_all.reshape(block_count, block_seqs, slot_count, feature_total),
            value_all.reshape(block_count, block_seqs, slot_count, feature_total),
            key_mask.reshape(block_count, block_seqs, slot_count),
        ),
    )
    mixed_heads = outputs.transpose(0, 2, 3, 1, 4).reshape(seq_count, row_count, feature_total)
    return (mixed_heads, log_totals)


def attention_backward(queries, key_all, value_all, key_mask, heads_grad, log_totals):
    seq_count, row_count, feature_total = queries.shape
    slot_count = key_all.shape[1]
    block_seqs, block_count, group_heads, group_count = block_layout(
        seq_count, row_count, feature_total // HD
    )
    group_width = group_heads * HD

    def seq_block(inputs):
        query_part, key_part, value_part, mask_part, grad_part, total_part = inputs

        def head_block(group_index):
            offset = group_index * group_width
            query_heads = head_slice(query_part, offset, group_width, group_heads)
            key_heads = head_slice(key_part, offset, group_width, group_heads)
            value_heads = head_slice(value_part, offset, group_width, group_heads)
            grad_heads = head_slice(grad_part, offset, group_width, group_heads)
            log_total = lax.dynamic_index_in_dim(total_part, group_index, 0, keepdims=False)
            scores = (
                jnp.einsum(
                    "brhd,bkhd->bhrk", query_heads, key_heads, preferred_element_type=jnp.float32
                )
                * 0.125
            )
            scores = jnp.where(mask_part[:, None, None, :], scores, -1e30)
            soft_probs = jnp.exp(scores - log_total[..., None])
            value_grad = jnp.einsum(
                "bhrk,brhd->bkhd",
                soft_probs.astype(jnp.bfloat16),
                grad_heads,
                preferred_element_type=jnp.float32,
            )
            prob_grad = jnp.einsum(
                "brhd,bkhd->bhrk", grad_heads, value_heads, preferred_element_type=jnp.float32
            )
            inner = jnp.sum(soft_probs * prob_grad, axis=-1, keepdims=True)
            score_grad = (soft_probs * (prob_grad - inner)).astype(jnp.bfloat16)
            query_grad = (
                jnp.einsum(
                    "bhrk,bkhd->brhd", score_grad, key_heads, preferred_element_type=jnp.float32
                )
                * 0.125
            )
            key_grad = (
                jnp.einsum(
                    "bhrk,brhd->bkhd", score_grad, query_heads, preferred_element_type=jnp.float32
                )
                * 0.125
            )
            return (
                query_grad.reshape(block_seqs, row_count, group_width),
                key_grad.reshape(block_seqs, slot_count, group_width),
                value_grad.reshape(block_seqs, slot_count, group_width),
            )

        return lax.map(head_block, jnp.arange(group_count))

    query_blocks, key_blocks, value_block_list = lax.map(
        seq_block,
        (
            queries.reshape(block_count, block_seqs, row_count, feature_total),
            key_all.reshape(block_count, block_seqs, slot_count, feature_total),
            value_all.reshape(block_count, block_seqs, slot_count, feature_total),
            key_mask.reshape(block_count, block_seqs, slot_count),
            heads_grad.reshape(block_count, block_seqs, row_count, feature_total),
            log_totals,
        ),
    )
    query_grad = query_blocks.transpose(0, 2, 3, 1, 4).reshape(seq_count, row_count, feature_total)
    key_grad = key_blocks.transpose(0, 2, 3, 1, 4).reshape(seq_count, slot_count, feature_total)
    value_grad = value_block_list.transpose(0, 2, 3, 1, 4).reshape(
        seq_count, slot_count, feature_total
    )
    return (query_grad, key_grad, value_grad)


def general_body(
    tokens,
    lengths,
    cotangent,
    query_weight,
    key_weight,
    value_weight,
    out_weight,
    up_weight,
    down_weight,
    query_bias,
    value_bias,
    out_bias,
    attn_gain,
    attn_shift,
    up_bias,
    down_bias,
    feed_gain,
    feed_shift,
):
    seq_count, row_count, feature_total = tokens.shape
    slot_count = row_count * lax.axis_size("seq")
    token_count = seq_count * row_count
    whole = gather_weights(
        query_weight, key_weight, value_weight, out_weight, up_weight, down_weight
    )
    full_query, full_key, full_value, full_out, full_up, full_down = whole
    flat_tokens = tokens.reshape(token_count, feature_total)
    queries = (
        jnp.dot(flat_tokens, full_query, preferred_element_type=jnp.float32) + query_bias
    ).astype(jnp.bfloat16)
    key_rows = jnp.dot(flat_tokens, full_key, preferred_element_type=jnp.float32).astype(
        jnp.bfloat16
    )
    value_rows = (
        jnp.dot(flat_tokens, full_value, preferred_element_type=jnp.float32) + value_bias
    ).astype(jnp.bfloat16)
    first_slot = lax.axis_index("seq") * row_count
    key_mask = jnp.arange(slot_count)[None, :] < lengths[:, None]
    row_valid = ((first_slot + jnp.arange(row_count))[None, :] < lengths[:, None]).astype(
        jnp.float32
    )
    row_valid = row_valid.reshape(token_count, 1)
    query_blocks = queries.reshape(seq_count, row_count, feature_total)
    key_blocks = key_rows.reshape(seq_count, row_count, feature_total)
    value_block_list = value_rows.reshape(seq_count, row_count, feature_total)
    key_all, value_all = (
        lax.all_gather(key_blocks, "seq", axis=1, tiled=True),
        lax.all_gather(value_block_list, "seq", axis=1, tiled=True),
    )
    mixed_heads, log_totals = attention_forward(query_blocks, key_all, value_all, key_mask)
    heads_low = mixed_heads.reshape(token_count, feature_total).astype(jnp.bfloat16)
    attention_out = jnp.dot(heads_low, full_out, preferred_element_type=jnp.float32) + out_bias
    tokens_f32 = flat_tokens.astype(jnp.float32)
    first_sum = tokens_f32 + attention_out
    hidden, first_pull = jax.vjp(layer_norm, first_sum, attn_gain, attn_shift)
    hidden_low = hidden.astype(jnp.bfloat16)
    pre_act = jnp.dot(hidden_low, full_up, preferred_element_type=jnp.float32) + up_bias
    gelu_out, gelu_pull = jax.vjp(partial(jax.nn.gelu, approximate=False), pre_act)
    activation = gelu_out.astype(jnp.bfloat16)
    feed_out = jnp.dot(activation, full_down, preferred_element_type=jnp.float32) + down_bias
    result, second_pull = jax.vjp(layer_norm, hidden + feed_out, feed_gain, feed_shift)
    mixed = result.astype(jnp.bfloat16).reshape(seq_count, row_count, feature_total)
    partial_stats = jnp.stack(
        [
            jnp.sum(row_valid * tokens_f32 * tokens_f32),
            jnp.sum(row_valid * attention_out * attention_out),
            jnp.sum(row_valid * feed_out * feed_out),
            jnp.sum(row_valid) * feature_total,
        ]
    )
    back_weights = gather_weights(
        query_weight, key_weight, value_weight, out_weight, up_weight, down_weight
    )
    back_query, back_key, back_value, back_out, back_up, back_down = back_weights
    out_grad = cotangent.reshape(token_count, feature_total).astype(jnp.float32) * row_valid
    second_grad, feed_gain_grad, feed_shift_grad = second_pull(out_grad)
    feed_low = second_grad.astype(jnp.bfloat16)
    down_weight_grad = jnp.einsum(
        "nf,nd->fd", activation, feed_low, preferred_element_type=jnp.float32
    )
    down_bias_grad = jnp.sum(feed_low, axis=0, dtype=jnp.float32)
    act_grad = jnp.einsum(
        "nd,fd->nf", feed_low, back_down, preferred_element_type=jnp.float32
    ).astype(jnp.bfloat16)
    pre_grad = gelu_pull(act_grad.astype(jnp.float32))[0].astype(jnp.bfloat16)
    up_weight_grad = jnp.einsum(
        "nd,nf->df", hidden_low, pre_grad, preferred_element_type=jnp.float32
    )
    up_bias_grad = jnp.sum(pre_grad, axis=0, dtype=jnp.float32)
    hidden_grad = (
        jnp.einsum("nf,df->nd", pre_grad, back_up, preferred_element_type=jnp.float32) + second_grad
    )
    first_grad, attn_gain_grad, attn_shift_grad = first_pull(hidden_grad)
    attn_low = first_grad.astype(jnp.bfloat16)
    out_weight_grad = jnp.einsum(
        "nd,ne->de", heads_low, attn_low, preferred_element_type=jnp.float32
    )
    out_bias_grad = jnp.sum(attn_low, axis=0, dtype=jnp.float32)
    heads_grad = jnp.einsum(
        "ne,de->nd", attn_low, back_out, preferred_element_type=jnp.float32
    ).astype(jnp.bfloat16)
    heads_grad = heads_grad.reshape(seq_count, row_count, feature_total)
    query_grad, key_part_grad, value_part_grad = attention_backward(
        query_blocks, key_all, value_all, key_mask, heads_grad, log_totals
    )
    key_sum, value_sum = (
        lax.psum_scatter(
            key_part_grad.astype(jnp.bfloat16), "seq", scatter_dimension=1, tiled=True
        ).astype(jnp.float32),
        lax.psum_scatter(
            value_part_grad.astype(jnp.bfloat16), "seq", scatter_dimension=1, tiled=True
        ).astype(jnp.float32),
    )
    query_low = query_grad.reshape(token_count, feature_total).astype(jnp.bfloat16)
    key_low = key_sum.reshape(token_count, feature_total).astype(jnp.bfloat16)
    value_low = value_sum.reshape(token_count, feature_total).astype(jnp.bfloat16)
    query_weight_grad = jnp.einsum(
        "nd,ne->de", flat_tokens, query_low, preferred_element_type=jnp.float32
    )
    key_weight_grad = jnp.einsum(
        "nd,ne->de", flat_tokens, key_low, preferred_element_type=jnp.float32
    )
    value_weight_grad = jnp.einsum(
        "nd,ne->de", flat_tokens, value_low, preferred_element_type=jnp.float32
    )
    query_bias_grad = jnp.sum(query_low, axis=0, dtype=jnp.float32)
    value_bias_gradient = jnp.sum(value_low, axis=0, dtype=jnp.float32)
    tokens_grad = (
        jnp.einsum("ne,de->nd", query_low, back_query, preferred_element_type=jnp.float32)
        + jnp.einsum("ne,de->nd", key_low, back_key, preferred_element_type=jnp.float32)
        + jnp.einsum("ne,de->nd", value_low, back_value, preferred_element_type=jnp.float32)
        + first_grad
    )
    tokens_grad = tokens_grad.astype(jnp.bfloat16).reshape(seq_count, row_count, feature_total)
    matrix_grads = reduce_grads(
        query_weight_grad,
        key_weight_grad,
        value_weight_grad,
        out_weight_grad,
        up_weight_grad,
        down_weight_grad,
    )
    totals = lax.psum(
        (
            partial_stats,
            query_bias_grad,
            value_bias_gradient,
            out_bias_grad,
            attn_gain_grad,
            attn_shift_grad,
            up_bias_grad,
            down_bias_grad,
            feed_gain_grad,
            feed_shift_grad,
        ),
        ("dp", "seq"),
    )
    stream_rms = jnp.sqrt(totals[0][:3] / totals[0][3])
    return (
        mixed,
        tokens_grad,
        matrix_grads[0],
        matrix_grads[1],
        matrix_grads[2],
        matrix_grads[3],
        matrix_grads[4],
        matrix_grads[5],
        totals[1],
        totals[2],
        totals[3],
        totals[4],
        totals[5],
        totals[6],
        totals[7],
        totals[8],
        totals[9],
        stream_rms,
    )


def swap(value, axis):
    return lax.ppermute(value, axis, [(0, 1), (1, 0)])


def both(value, axis):
    return jnp.concatenate([value, swap(value, axis)], axis=0)


def in_order(own, other, index, axis=0):
    return jnp.where(
        index == 0, jnp.stack([own, other], axis=axis), jnp.stack([other, own], axis=axis)
    )


def pick(values, index, axis):
    return lax.dynamic_index_in_dim(values, index, axis, keepdims=False)


def add(left, right):
    return (left.astype(jnp.float32) + right.astype(jnp.float32)).astype(jnp.bfloat16)


def fold(values, axis, dim):
    index = lax.axis_index(axis)
    return add(pick(values, index, dim), swap(pick(values, 1 - index, dim), axis))


NEXT = [(0, 1), (1, 0), (2, 3), (3, 2)]
CROSS = [(0, 2), (2, 0), (1, 3), (3, 1)]


def fold_cross(pairs):
    upper = lax.axis_index("z") // 2
    return add(pick(pairs, upper, 0), lax.ppermute(pick(pairs, 1 - upper, 0), "z", CROSS))


def fold_line(values):
    odd = lax.axis_index("z") % 2
    pairs = values.reshape((2, 2) + values.shape[1:])
    sent = lax.ppermute(pick(pairs, 1 - odd, 1), "z", NEXT)
    return fold_cross(add(pick(pairs, odd, 1), sent))


def line_cross(value):
    return lax.ppermute(value, "z", CROSS)


def line_next(pair):
    return lax.ppermute(pair, "z", NEXT)


def gather_square(own, way):
    beside, below = swap(own, "x"), swap(own, "s")
    across = swap(below, "x") if way == "x" else swap(beside, "s")
    return [own, beside, below, across]


def fold_columns(total):
    half = lax.axis_index("s")
    return add(columns_of(total, half), swap(columns_of(total, 1 - half), "s"))


def halve(values, axis, dim):
    index = lax.axis_index(axis) % 2
    return pick(values, index, dim), pick(values, 1 - index, dim)


def line_parts(values):
    return halve(values.reshape((2, 2) + values.shape[1:]), "z", 1)


def scatter_top(send, keep):
    total = add(keep, swap(send, "s"))
    total = total.reshape((4, 2) + total.shape[1:])
    return fold_line(fold(total, "x", 1))


def grad_block(left_t, right, got=None):
    total = product(left_t, right, 1, 0)
    if got is not None:
        total = total + got.astype(jnp.float32)
    return total.astype(jnp.bfloat16)


def columns_of(right, index):
    columns = right.shape[-1] // 2
    return lax.dynamic_slice_in_dim(right, index * columns, columns, right.ndim - 1)


PAIR = 2 * HD
LIMIT = 16 * 1024 * 1024


def kernel_params(steps):
    return pltpu.CompilerParams(
        dimension_semantics=("arbitrary",) * steps, vmem_limit_bytes=LIMIT
    )


def product(left, right, left_dim, right_dim):
    return lax.dot_general(
        left, right, (((left_dim,), (right_dim,)), ((), ())), preferred_element_type=jnp.float32
    )


def key_bias(facts_ref, slots):
    place = lax.broadcasted_iota(jnp.int32, (slots, 1), 0) + facts_ref[2]
    place = jnp.where(place >= slots, place - slots, place)
    return jnp.where(place < facts_ref[pl.program_id(0)], 0.0, -1e30)


def head_lanes(value, head):
    lane = lax.broadcasted_iota(jnp.int32, value.shape, 1)
    return jnp.where((lane >= HD) == (head == 1), value, jnp.zeros_like(value))


def turned(value):
    return value.astype(jnp.float32).T


def attend_kernel(facts_ref, query_ref, key_ref, value_ref, out_ref, total_ref):
    slots = key_ref.shape[0]
    bias = key_bias(facts_ref, slots)
    query = query_ref[...] * jnp.bfloat16(0.125)
    key = key_ref[...]
    value_t = turned(value_ref[...]).astype(jnp.bfloat16)
    outs = []
    for head in range(2):
        scores = product(key, head_lanes(query, head), 1, 1) + bias
        peak = jnp.max(scores, axis=0, keepdims=True)
        weight = jnp.exp(scores - peak)
        total = jnp.sum(weight, axis=0, keepdims=True)
        part = product(value_t[head * HD : (head + 1) * HD], weight.astype(jnp.bfloat16), 1, 0)
        outs.append(part * (1.0 / total))
        total_ref[0, 0, head : head + 1, :] = peak + jnp.log(total)
    out_ref[...] = jnp.concatenate(outs, axis=0).T.astype(jnp.bfloat16)


def attend_back_kernel(
    facts_ref, query_ref, key_ref, value_ref, grad_ref, total_ref, low_ref, sums_ref
):
    slots = key_ref.shape[0]
    bias = key_bias(facts_ref, slots)
    query = query_ref[...] * jnp.bfloat16(0.125)
    key = key_ref[...]
    value = value_ref[...]
    grad = grad_ref[...]
    key_t = turned(key).astype(jnp.bfloat16)
    lane = lax.broadcasted_iota(jnp.int32, (slots, PAIR), 1)
    query_parts, key_parts, value_parts = [], [], []
    for head in range(2):
        scores = product(key, head_lanes(query, head), 1, 1) + bias
        soft = jnp.exp(scores - total_ref[0, 0, head : head + 1, :])
        value_parts.append(product(soft.astype(jnp.bfloat16), grad, 1, 0))
        change = product(value, head_lanes(grad, head), 1, 1)
        inner = jnp.sum(soft * change, axis=0, keepdims=True)
        change = (soft * (change - inner)).astype(jnp.bfloat16)
        key_parts.append(product(change, query, 1, 0))
        query_parts.append(product(key_t[head * HD : (head + 1) * HD], change, 1, 0))
    pair = pl.program_id(1)
    groups = low_ref.shape[1] // 3
    query_low = (jnp.concatenate(query_parts, axis=0) * 0.125).T
    key_low = jnp.where(lane < HD, key_parts[0], key_parts[1])
    value_low = jnp.where(lane < HD, value_parts[0], value_parts[1])
    for place, part in enumerate((query_low, key_low, value_low)):
        start = pl.multiple_of(place * groups + pair * PAIR, PAIR)
        low = part.astype(jnp.bfloat16)
        low_ref[:, pl.ds(start, PAIR)] = low
        sums_ref[0, :, pl.ds(start, PAIR)] = jnp.sum(
            low.astype(jnp.float32), axis=0, keepdims=True
        )


def attention_specs(slots, pairs):
    def at(part):
        return pl.BlockSpec(
            (slots, PAIR), lambda b, g, p, *_: (b, g * 3 * pairs + part * pairs + p)
        )

    heads = pl.BlockSpec((slots, PAIR), lambda b, g, p, *_: (b, g * pairs + p))
    totals = pl.BlockSpec((1, 1, 2, slots), lambda b, g, p, *_: (b, g * pairs + p, 0, 0))
    return [at(0), at(1), at(2)], heads, totals


def attend(facts, projected, slots, wait=()):
    pairs = projected.shape[1] // (6 * PAIR)
    inputs, heads, totals = attention_specs(slots, pairs)
    rows = projected.shape[0]
    return call(
        attend_kernel,
        "attend",
        (2, 2, pairs),
        inputs,
        [heads, totals],
        [
            like((rows, 2 * pairs * PAIR), jnp.bfloat16),
            like((2, 2 * pairs, 2, slots), jnp.float32),
        ],
        facts,
        projected,
        projected,
        projected,
        wait=wait,
    )


def attend_back(facts, projected, heads_grad, totals_in, slots, own, wait=(), through=()):
    pairs = projected.shape[1] // (6 * PAIR)

    def group(facts_ref):
        return facts_ref[3] if own else 1 - facts_ref[3]

    def at(part):
        return pl.BlockSpec(
            (slots, PAIR), lambda b, p, f: (b, group(f) * 3 * pairs + part * pairs + p)
        )

    heads = pl.BlockSpec((slots, PAIR), lambda b, p, f: (b, group(f) * pairs + p))
    totals = pl.BlockSpec((1, 1, 2, slots), lambda b, p, f: (b, group(f) * pairs + p, 0, 0))
    width = 3 * pairs * PAIR
    return call(
        attend_back_kernel,
        "attend_back",
        (2, pairs),
        [at(0), at(1), at(2), heads, totals],
        [
            pl.BlockSpec((slots, width), lambda b, p, f: (b, 0)),
            pl.BlockSpec((1, 1, width), lambda b, p, f: (b, 0, 0)),
        ],
        [
            like((2 * slots, width), jnp.bfloat16),
            like((2, 1, width), jnp.float32),
        ],
        facts,
        projected,
        projected,
        projected,
        heads_grad,
        totals_in,
        wait=wait,
        through=through,
    )


def call(kernel, name, grid, inputs, outputs, shapes, facts, *args, wait=(), scratch=(), through=(), into=()):
    single = not isinstance(outputs, list)
    outputs, shapes = ([outputs], [shapes]) if single else (outputs, shapes)
    wait = tuple(into) + tuple(wait)
    count, held, passed = len(args), len(wait) + len(through), len(through)
    last = count + held + len(outputs)

    def body(facts_ref, *refs):
        kernel(facts_ref, *refs[:count], *refs[count + held : last], *refs[last + passed + 1 :])
        for place in range(facts.shape[0]):
            refs[last + passed][place] = facts_ref[place]

    results = pl.pallas_call(
        body,
        grid_spec=pltpu.PrefetchScalarGridSpec(
            num_scalar_prefetch=1,
            grid=grid,
            in_specs=list(inputs) + [pl.BlockSpec(memory_space=pl.ANY)] * held,
            out_specs=list(outputs)
            + [pl.BlockSpec(memory_space=pl.ANY)] * passed
            + [pl.BlockSpec(memory_space=pltpu.SMEM)],
            scratch_shapes=list(scratch),
        ),
        out_shape=list(shapes)
        + [like(value.shape, value.dtype) for value in through]
        + [like(facts.shape, jnp.int32)],
        input_output_aliases={
            **{1 + count + i: i for i in range(len(into))},
            **{1 + count + len(wait) + i: len(outputs) + i for i in range(passed)},
        },
        compiler_params=kernel_params(len(grid)),
        name=name,
    )(facts, *args, *wait, *through)
    values = tuple(results[:-1])
    return (values[0] if single and not passed else values), results[-1]


def block(shape, *index):
    def at(*grid_and_facts):
        return tuple(entry(*grid_and_facts) if callable(entry) else entry for entry in index)

    return pl.BlockSpec(shape, at)


def whole(array):
    zeros = (0,) * array.ndim
    return pl.BlockSpec(array.shape, lambda *_: zeros)


def first(i, *_):
    return i


def like(shape, dtype):
    return jax.ShapeDtypeStruct(shape, dtype)


def rows_in_order(facts_ref, own, beside):
    even = facts_ref[4] == 0
    pieces = []
    for z in range(4):
        pieces += [jnp.where(even, own[z], beside[z]), jnp.where(even, beside[z], own[z])]
    return jnp.concatenate(pieces, axis=0)


def near_or_far(facts_ref, refs, near):
    own, beside, below, across = [ref[...] for ref in refs]
    return rows_in_order(
        facts_ref, jnp.where(near, own, below), jnp.where(near, beside, across)
    )


def square_columns(parts, wide, steps):
    shape = parts[0].shape[:2] + (wide,)
    near = block(shape, 0, 0, lambda i, *_: jnp.minimum(i, steps - 1))
    far = block(shape, 0, 0, lambda i, *_: jnp.maximum(i - steps, 0))
    return [near, near, far, far]


def half_at(i, facts, steps):
    return jnp.where(i < steps, facts[3], 1 - facts[3])


def gate_kernel(facts_ref):
    del facts_ref


def gate(facts, through, wait):
    return call(gate_kernel, "gate", (1,), [], [], [], facts, wait=wait, through=through)


def stack_kernel(own_at, facts_ref, own_ref, other_ref, out_ref):
    own = facts_ref[own_at] == pl.program_id(0)
    value = jnp.where(own, own_ref[...], other_ref[...])
    out_ref[...] = value.reshape(out_ref.shape)


def stack_pair(facts, own, other, wait=(), through=()):
    rows, columns = own.shape
    return call(
        partial(stack_kernel, 6),
        "stack",
        (2,),
        [whole(own), whole(other)],
        block((1, rows, columns), first, 0, 0),
        like((2, rows, columns), own.dtype),
        facts,
        own,
        other,
        wait=wait,
        through=through,
    )


def stack_line(facts, own, other, wait=()):
    _, rows, columns = own.shape
    line, facts = call(
        partial(stack_kernel, 7),
        "stack_line",
        (2,),
        [whole(own), whole(other)],
        block((2, 1, rows, columns), 0, first, 0, 0),
        like((2, 2, rows, columns), own.dtype),
        facts,
        own,
        other,
        wait=wait,
    )
    return line.reshape(4, rows, columns), facts


def turn_kernel(facts_ref, *refs):
    for i in range(2):
        refs[4 + i][...] = jnp.concatenate([refs[2 * i][...].T, refs[2 * i + 1][...].T], axis=1)


def turn_all_kernel(facts_ref, rows_ref, out_ref):
    out_ref[...] = rows_ref[...].T


def turn_all(facts, values, wait=()):
    count, width = values.shape
    step = width // 4
    return call(
        turn_all_kernel,
        "turn_all",
        (4,),
        [block((count, step), 0, first)],
        block((step, count), first, 0),
        like((width, count), values.dtype),
        facts,
        values,
        wait=wait,
    )


def turn(facts, values, others, rows, wait=()):
    count, width = values.shape
    half = width // 2
    out = block((rows, 2 * count), first, 0)
    shape = like((half, 2 * count), values.dtype)
    own = block((count, rows), 0, lambda i, f: 2 * i + f[4])
    other = block((count, rows), 0, lambda i, f: 2 * i + 1 - f[4])
    return call(
        turn_kernel,
        "turn",
        (half // rows,),
        [own, own, other, other],
        [out, out],
        [shape, shape],
        facts,
        values,
        others,
        values,
        others,
        wait=wait,
    )


def project_kernel(facts_ref, rows_ref, bias_ref, *refs):
    parts, (out_ref, in_ref, rest_ref) = refs[:4], refs[4:]
    step = pl.program_id(0)
    weight = near_or_far(facts_ref, parts, step < 4)

    @pl.when(step % 4 < 3)
    def _():
        in_ref[...] = weight
        value = product(rows_ref[...], weight, 1, 0) + bias_ref[...]
        out_ref[...] = value.astype(jnp.bfloat16)

    @pl.when(step % 4 == 3)
    def _():
        chips, count, wide = rest_ref.shape
        pairs = weight.reshape(chips, 2, count, wide // 2)
        rest_ref[...] = jnp.concatenate([pairs[:, 0], pairs[:, 1]], axis=2)


def project(facts, rows, bias, parts, wait=()):
    count, width = rows.shape
    wide = parts[0].shape[2] // 4

    def column(i, f):
        return half_at(i, f, 4) * 3 + jnp.minimum(i % 4, 2)

    out = block((count, wide), 0, column)
    rest = (8, parts[0].shape[1] // 2, 2 * wide)
    return call(
        project_kernel,
        "project",
        (8,),
        [whole(rows), block((1, wide), 0, column)] + square_columns(parts, wide, 4),
        [out, block((width, wide), 0, column), block(rest, 0, 0, lambda i, f: half_at(i, f, 4))],
        [
            like((count, 6 * wide), jnp.bfloat16),
            like((width, 6 * wide), jnp.bfloat16),
            like(rest[:2] + (4 * wide,), jnp.bfloat16),
        ],
        facts,
        rows,
        bias[None],
        *parts,
        wait=wait,
    )


def valid_rows(facts_ref, count, slots):
    place = lax.broadcasted_iota(jnp.int32, (count, 1), 0) + pl.program_id(0) * count + facts_ref[2]
    place = jnp.where(place >= slots, place - slots, place)
    return (place < facts_ref[0]).astype(jnp.float32)


def add_rows(sums_ref, rows):
    total = jnp.concatenate([jnp.sum(part, axis=0, keepdims=True) for part in rows], axis=0)
    total = jnp.concatenate([total, jnp.zeros((8 - len(rows), total.shape[1]), jnp.float32)], axis=0)

    @pl.when(pl.program_id(0) == 0)
    def _():
        sums_ref[...] = total

    @pl.when(pl.program_id(0) > 0)
    def _():
        sums_ref[...] += total


def mean_of(values):
    return jnp.mean(values, axis=-1, keepdims=True)


def attend_out_kernel(
    slots, facts_ref, own_ref, other_ref, own_weight_ref, other_weight_ref, tokens_ref, vectors_ref,
    hat_ref, rstd_ref, low_ref, sums_ref,
):
    branch = (
        product(own_ref[...], own_weight_ref[...], 1, 0)
        + product(other_ref[...], other_weight_ref[...], 1, 0)
        + vectors_ref[0:1]
    )
    tokens = tokens_ref[...].astype(jnp.float32)
    total = tokens + branch
    centered = total - mean_of(total)
    rstd = lax.rsqrt(mean_of(centered * centered) + 1e-05)
    hat = centered * rstd
    hat_ref[...] = hat
    rstd_ref[...] = rstd
    low_ref[...] = (hat * vectors_ref[1:2] + vectors_ref[2:3]).astype(jnp.bfloat16)
    valid = valid_rows(facts_ref, tokens.shape[0], slots)
    add_rows(sums_ref, [valid * tokens * tokens, valid * branch * branch])


def attend_out(facts, own, other, own_weight, other_weight, tokens, vectors, wait=()):
    slots, width = tokens.shape
    step = slots // 4
    rows = lambda array: block((step, array.shape[1]), first, 0)
    return call(
        partial(attend_out_kernel, slots),
        "attend_out",
        (4,),
        [rows(own), rows(other), whole(own_weight), whole(other_weight), rows(tokens), whole(vectors)],
        [block((step, width), first, 0), block((step, 1), first, 0), block((step, width), first, 0), block((8, width), 0, 0)],
        [
            like((slots, width), jnp.float32),
            like((slots, 1), jnp.float32),
            like((slots, width), jnp.bfloat16),
            like((8, width), jnp.float32),
        ],
        facts,
        own,
        other,
        own_weight,
        other_weight,
        tokens,
        vectors,
        wait=wait,
    )


def up_kernel(facts_ref, rows_ref, others_ref, bias_ref, *refs):
    parts, (act_ref, slope_ref, turned_ref, weight_ref) = refs[:4], refs[4:]
    weight = near_or_far(facts_ref, parts, pl.program_id(0) < 4)
    weight_ref[...] = weight
    pre_act = [product(ref[...], weight, 1, 0) for ref in (rows_ref, others_ref)]
    pre_act = jnp.concatenate(pre_act, axis=0) + bias_ref[...]
    below = 0.5 + 0.5 * lax.erf(pre_act * 0.7071067811865476)
    act = (pre_act * below).astype(jnp.bfloat16)
    act_ref[...] = act
    turned_ref[...] = act.T
    slope = below + pre_act * (0.3989422804014327 * jnp.exp(-0.5 * pre_act * pre_act))
    slope_ref[...] = slope.astype(jnp.bfloat16)


def feed_up(facts, rows, others, bias, parts, wait=()):
    count, width = 2 * rows.shape[0], rows.shape[1]
    units = bias.shape[0]
    wide = units // 8

    def column(i, f):
        return half_at(i, f, 4) * 4 + i % 4

    shape = like((count, units), jnp.bfloat16)
    out = block((count, wide), 0, column)
    return call(
        up_kernel,
        "feed_up",
        (8,),
        [whole(rows), whole(others), block((1, wide), 0, column)] + square_columns(parts, wide, 4),
        [out, out, block((wide, count), column, 0), block((width, wide), 0, column)],
        [
            shape,
            shape,
            like((units, count), jnp.bfloat16),
            like((width, units), jnp.bfloat16),
        ],
        facts,
        rows,
        others,
        bias[None],
        *parts,
        wait=wait,
    )


def down_kernel(facts_ref, rows_ref, *refs):
    parts, (weight_ref, out_ref, total_ref) = refs[:4], refs[4:]
    step = pl.program_id(0)
    own, beside, below, across = [ref[0] for ref in parts]
    even, left = facts_ref[4] == 0, facts_ref[3] == 0
    for x in range(2):
        mine = jnp.where(even, own, beside) if x == 0 else jnp.where(even, beside, own)
        theirs = jnp.where(even, below, across) if x == 0 else jnp.where(even, across, below)
        weight_ref[x] = jnp.concatenate(
            [jnp.where(left, mine, theirs), jnp.where(left, theirs, mine)], axis=1
        )
    weight = weight_ref[...].reshape(rows_ref.shape[1], out_ref.shape[1])
    value = product(rows_ref[...], weight, 1, 0)

    @pl.when(step == 0)
    def _():
        total_ref[...] = value

    @pl.when(step > 0)
    def _():
        total_ref[...] += value

    @pl.when(step == 3)
    def _():
        out_ref[...] = total_ref[...].astype(jnp.bfloat16)


def feed_down(facts, rows, parts, wait=()):
    count, units = rows.shape
    _, block_rows, half_width = parts[0].shape
    width = 2 * half_width
    shape = (1,) + parts[0].shape[1:]
    return call(
        down_kernel,
        "feed_down",
        (4,),
        [block((count // 2, units // 4), 1, first)] + [block(shape, first, 0, 0)] * 4,
        [block((2, block_rows, width), first, 0, 0), block((count // 2, width), 0, 0)],
        [like((8, block_rows, width), jnp.bfloat16), like((count // 2, width), jnp.bfloat16)],
        facts,
        rows,
        *parts,
        scratch=[pltpu.VMEM((count // 2, width), jnp.float32)],
        wait=wait,
    )


def second_norm_kernel(
    slots, facts_ref, part_ref, other_ref, hat_ref, cotangent_ref, vectors_ref,
    mixed_ref, grad_ref, low_ref, sums_ref,
):
    branch = part_ref[...] + other_ref[...].astype(jnp.float32) + vectors_ref[0:1]
    hidden = hat_ref[...] * vectors_ref[1:2] + vectors_ref[2:3]
    gain = vectors_ref[3:4]
    total = hidden + branch
    centered = total - mean_of(total)
    rstd = lax.rsqrt(mean_of(centered * centered) + 1e-05)
    hat = centered * rstd
    mixed_ref[...] = (hat * gain + vectors_ref[4:5]).astype(jnp.bfloat16)
    valid = valid_rows(facts_ref, branch.shape[0], slots)
    grad = cotangent_ref[...].astype(jnp.float32) * valid
    scaled = grad * gain
    result = rstd * (scaled - mean_of(scaled) - hat * mean_of(scaled * hat))
    low = result.astype(jnp.bfloat16)
    grad_ref[...] = result
    low_ref[...] = low
    add_rows(sums_ref, [low.astype(jnp.float32), grad * hat, grad, valid * branch * branch])


def second_norm(facts, part, other, hat, cotangent, vectors, wait=()):
    slots, width = part.shape
    step = slots // 4
    rows = block((step, width), first, 0)
    return call(
        partial(second_norm_kernel, slots),
        "second_norm",
        (4,),
        [rows, rows, rows, rows, whole(vectors)],
        [rows, rows, rows, block((8, width), 0, 0)],
        [
            like((slots, width), jnp.bfloat16),
            like((slots, width), jnp.float32),
            like((slots, width), jnp.bfloat16),
            like((8, width), jnp.float32),
        ],
        facts,
        part,
        other,
        hat,
        cotangent,
        vectors,
        wait=wait,
    )


def first_norm_kernel(
    facts_ref, part_ref, other_ref, second_ref, hat_ref, rstd_ref, vectors_ref,
    grad_ref, low_ref, sums_ref,
):
    grad = part_ref[...] + other_ref[...].astype(jnp.float32) + second_ref[...]
    hat = hat_ref[...]
    scaled = grad * vectors_ref[1:2]
    result = rstd_ref[...] * (scaled - mean_of(scaled) - hat * mean_of(scaled * hat))
    low = result.astype(jnp.bfloat16)
    grad_ref[...] = result
    low_ref[...] = low
    add_rows(sums_ref, [low.astype(jnp.float32), grad * hat, grad])


def first_norm(facts, part, other, second, hat, rstd, vectors, wait=()):
    slots, width = part.shape
    step = slots // 4
    rows = block((step, width), first, 0)
    return call(
        first_norm_kernel,
        "first_norm",
        (4,),
        [rows, rows, rows, rows, block((step, 1), first, 0), whole(vectors)],
        [rows, rows, block((8, width), 0, 0)],
        [
            like((slots, width), jnp.float32),
            like((slots, width), jnp.bfloat16),
            like((8, width), jnp.float32),
        ],
        facts,
        part,
        other,
        second,
        hat,
        rstd,
        vectors,
        wait=wait,
    )


def act_grad_kernel(facts_ref, rows_ref, weight_ref, slope_ref, out_ref, sums_ref):
    total = product(rows_ref[...], weight_ref[...], 1, 1)
    grad = total.astype(jnp.bfloat16).astype(jnp.float32) * slope_ref[...].astype(jnp.float32)
    low = grad.astype(jnp.bfloat16)
    out_ref[...] = low
    sums_ref[...] = jnp.sum(low.astype(jnp.float32), axis=0, keepdims=True)


def act_grad(facts, rows, weight, slope, wait=()):
    count, units = slope.shape
    step = units // 8
    out = block((count, step), 0, first)
    return call(
        act_grad_kernel,
        "act_grad",
        (8,),
        [whole(rows), block((step, rows.shape[1]), first, 0), out],
        [out, block((1, step), 0, first)],
        [like((count, units), jnp.bfloat16), like((1, units), jnp.float32)],
        facts,
        rows,
        weight,
        slope,
        wait=wait,
    )


def tokens_grad_kernel(facts_ref, mine_ref, theirs_ref, weight_ref, out_ref, sent_ref):
    wide = mine_ref.shape[1]
    slots = out_ref.shape[0]
    half = facts_ref[3]
    mine = weight_ref[:, pl.ds(pl.multiple_of(half * wide, 128), wide)]
    theirs = weight_ref[:, pl.ds(pl.multiple_of((1 - half) * wide, 128), wide)]
    total = product(mine_ref[...], mine, 1, 1) + product(theirs_ref[...], theirs, 1, 1)
    out_ref[...] = total[:slots]
    sent_ref[...] = total[slots:].astype(sent_ref.dtype)


def tokens_grad(facts, mine, theirs, weight, wait=(), through=()):
    count, columns = mine.shape
    width = weight.shape[0]
    step = width // 4
    out = block((count // 2, step), 0, first)
    return call(
        tokens_grad_kernel,
        "tokens_grad",
        (4,),
        [whole(mine), whole(theirs), block((step, 2 * columns), first, 0)],
        [out, out],
        [
            like((count // 2, width), jnp.float32),
            like((count // 2, width), jnp.bfloat16),
        ],
        facts,
        mine,
        theirs,
        weight,
        wait=wait,
        through=through,
    )


def add_parts_kernel(facts_ref, own_ref, got_ref, kept_ref, sent_ref):
    step = pl.program_id(0)
    total = own_ref[...].astype(jnp.float32) + got_ref[...].astype(jnp.float32)
    total = total.astype(jnp.bfloat16)

    @pl.when(step < 2)
    def _():
        sent_ref[...] = total

    @pl.when(step >= 2)
    def _():
        kept_ref[...] = total


def add_last_kernel(facts_ref, own_ref, got_ref, kept_ref, sent_ref):
    total = own_ref[0].astype(jnp.float32) + got_ref[0].astype(jnp.float32)
    total = total.astype(jnp.bfloat16)

    @pl.when(pl.program_id(0) == 0)
    def _():
        sent_ref[...] = total

    @pl.when(pl.program_id(0) == 1)
    def _():
        kept_ref[...] = total


def add_last(facts, own, got, wait=(), through=()):
    _, rows, columns = own.shape
    part = block((1, rows, columns), lambda i, f: jnp.where(i == 0, 1 - f[6], f[6]), 0, 0)
    shape = like((rows, columns), jnp.bfloat16)
    out = block((rows, columns), 0, 0)
    return call(
        add_last_kernel,
        "add_last",
        (2,),
        [part, part],
        [out, out],
        [shape, shape],
        facts,
        own,
        got,
        wait=wait,
        through=through,
    )


def add_parts(facts, own, got, wait=(), through=()):
    _, rows, columns = own.shape
    shape = (1, rows, columns)
    part = block(shape, lambda i, f: 2 * (i % 2) + jnp.where(i < 2, 1 - f[7], f[7]), 0, 0)
    half = like((2, rows, columns), jnp.bfloat16)
    return call(
        add_parts_kernel,
        "add_parts",
        (4,),
        [part, part],
        [
            block(shape, lambda i, *_: jnp.maximum(i - 2, 0), 0, 0),
            block(shape, lambda i, *_: jnp.minimum(i, 1), 0, 0),
        ],
        [half, half],
        facts,
        own,
        got,
        wait=wait,
        through=through,
    )


def alternate(value, width, offset):
    starts = range(offset * width, value.shape[1], 2 * width)
    return jnp.concatenate([value[:, start : start + width] for start in starts], axis=1)


def deal_kernel(unit_block, core_ref, query_ref, key_ref, value_ref, up_ref, *refs):
    first_core = core_ref[0] == 0
    near = [ref[...] for ref in (query_ref, key_ref, value_ref)]
    even = jnp.concatenate([alternate(value, HD, 0) for value in near], axis=1)
    odd = jnp.concatenate([alternate(value, HD, 1) for value in near], axis=1)
    up = up_ref[...]
    up_even, up_odd = alternate(up, unit_block, 0), alternate(up, unit_block, 1)
    refs[0][...] = jnp.where(first_core, even, odd)
    refs[1][...] = jnp.where(first_core, odd, even)
    refs[2][...] = jnp.where(first_core, up_even, up_odd)
    refs[3][...] = jnp.where(first_core, up_odd, up_even)


def deal(core, query, key, value, up, unit_block):
    near = like((query.shape[0], 3 * query.shape[1] // 2), jnp.bfloat16)
    half = like((up.shape[0], up.shape[1] // 2), jnp.bfloat16)
    shapes = [near, near, half, half]
    return call(
        partial(deal_kernel, unit_block),
        "deal",
        (1,),
        [whole(value) for value in (query, key, value, up)],
        [whole(shape) for shape in shapes],
        shapes,
        core,
        query,
        key,
        value,
        up,
    )


def lay_out_kernel(core_ref, near_ref, near_got_ref, out_ref, up_ref, up_got_ref, *refs):
    first_core = core_ref[0] == 0
    near, near_got, up, up_got = [
        ref[...] for ref in (near_ref, near_got_ref, up_ref, up_got_ref)
    ]
    out = out_ref[...]
    wide = out.shape[1] // 2
    near_rows = jnp.concatenate(
        [jnp.where(first_core, near, near_got), jnp.where(first_core, near_got, near)], axis=0
    )
    out_rows = jnp.concatenate([out[:, :wide], out[:, wide:]], axis=0)
    refs[0][...] = jnp.concatenate([near_rows, out_rows], axis=1)
    refs[1][...] = jnp.concatenate(
        [jnp.where(first_core, up, up_got), jnp.where(first_core, up_got, up)], axis=0
    )


def lay_out(core, near, near_got, out, up, up_got):
    rows = 2 * near.shape[0]
    shapes = [
        like((rows, near.shape[1] + out.shape[1] // 2), jnp.bfloat16),
        like((rows, up.shape[1]), jnp.bfloat16),
    ]
    arrays = (near, near_got, out, up, up_got)
    return call(
        lay_out_kernel,
        "lay_out",
        (1,),
        [whole(value) for value in arrays],
        [whole(shape) for shape in shapes],
        shapes,
        core,
        *arrays,
    )[0]


def split_body(
    tokens,
    lengths,
    cotangent,
    query_weight,
    key_weight,
    value_weight,
    out_weight,
    up_weight,
    down_weight,
    query_bias,
    value_bias,
    out_bias,
    attn_gain,
    attn_shift,
    up_bias,
    down_bias,
    feed_gain,
    feed_shift,
):
    core = lax.axis_index("c")
    half = lax.axis_index("s")
    row_count, width = tokens.shape[1:]
    slots = 2 * row_count
    unit_block = down_weight.shape[0]
    units = up_bias.shape[0] // 2
    cols = width // 2
    wide = cols // 2

    def to_sequence(values):
        return jnp.concatenate([pick(values, half, 0), swap(pick(values, 1 - half, 0), "s")], axis=0)

    def from_sequence(values):
        return in_order(values[:row_count], swap(values[row_count:], "s"), half)

    place = jnp.stack([core]).astype(jnp.int32)
    (near_kept, near_sent, up_kept, up_sent), place = deal(
        place, query_weight, key_weight, value_weight, up_weight, unit_block
    )
    near_mine, up_mine = lay_out(
        place, near_kept, swap(near_sent, "c"), out_weight, up_kept, swap(up_sent, "c")
    )
    rows, up_cols = up_mine.shape
    line = lax.axis_index("z")
    length_own = lax.dynamic_slice_in_dim(lengths, half, 1, 0)
    facts = jnp.concatenate(
        [
            both(length_own, "c"),
            jnp.stack(
                [
                    half * row_count,
                    half,
                    lax.axis_index("x"),
                    jnp.int32(0),
                    line // 2,
                    line % 2,
                ]
            ).astype(jnp.int32),
        ]
    )
    tokens_own = to_sequence(tokens)
    cotangent_own = to_sequence(cotangent)
    (near, up_mine, down_mine), facts = stack_pair(
        facts,
        near_mine,
        line_cross(near_mine),
        wait=(tokens_own,),
        through=(up_mine, down_weight),
    )
    near, facts = stack_line(facts, near, line_next(near), wait=(cotangent_own,))
    near_parts = gather_square(near, "x")
    up_pairs, facts = stack_pair(facts, up_mine, line_cross(up_mine), wait=(near,))
    tokens_both = both(tokens_own, "c")
    up_part, facts = stack_line(
        facts, up_pairs, line_next(up_pairs), wait=(near_parts[1], near_parts[2])
    )
    up_parts = gather_square(up_part, "s")
    down_pairs, facts = stack_pair(facts, down_mine, line_cross(down_mine), wait=(up_part,))
    def halves_of(vector, size):
        return pick(vector.reshape(-1, 2, size), core, 1).reshape(-1)

    query_part = halves_of(query_bias, HD).reshape(2, wide)
    value_part = halves_of(value_bias, HD).reshape(2, wide)
    in_bias = jnp.stack([query_part, jnp.zeros_like(query_part), value_part], axis=1).reshape(-1)
    (projected, in_weight, out_own), facts = project(
        facts, tokens_both, in_bias, near_parts, wait=(down_pairs,)
    )
    out_own = out_own.reshape(cols, width)
    out_other = swap(out_own, "c")
    down_part, facts = stack_line(facts, down_pairs, line_next(down_pairs), wait=(projected,))
    down_parts = gather_square(down_part, "x")
    (heads_out, totals), facts = attend(facts, projected, slots, wait=(up_parts[2],))
    heads_other = swap(heads_out[slots:], "c")
    vectors = jnp.stack(
        [out_bias, attn_gain, attn_shift, down_bias, feed_gain, feed_shift, out_bias, out_bias]
    )
    (first_hat, first_rstd, hidden_low, first_sums), facts = attend_out(
        facts,
        heads_out,
        heads_other,
        out_own,
        out_other,
        tokens_own,
        vectors,
        wait=(up_parts[1], down_parts[2]),
    )
    (hidden_low,), facts = gate(
        facts, (hidden_low,), (up_parts[3], down_parts[1], down_parts[3])
    )
    hidden_from = swap(hidden_low, "c")
    (activation, slope, act_t, up_all), facts = feed_up(
        facts, hidden_low, hidden_from, halves_of(up_bias, unit_block), up_parts
    )
    (down_all, feed_sent), facts = feed_down(facts, activation, down_parts)
    down_all = down_all.reshape(units, width)
    feed_other = swap(feed_sent, "c")
    feed_part = product(activation[:slots], down_all, 1, 0)
    feed_vectors = jnp.stack(
        [down_bias, attn_gain, attn_shift, feed_gain, feed_shift, out_bias, out_bias, out_bias]
    )
    (mixed, second_grad, feed_low, second_sums), facts = second_norm(
        facts, feed_part, feed_other, first_hat, cotangent_own, feed_vectors
    )

    mixed_got = swap(mixed[row_count:], "s")

    feed_both = both(feed_low, "c")
    tokens_t, facts = turn_all(facts, tokens_both, wait=(feed_low,))
    hidden_turned, facts = turn(facts, hidden_low, hidden_from, rows)
    feed_mine, feed_theirs = columns_of(feed_both, half), columns_of(feed_both, 1 - half)
    down_sent = grad_block(act_t, feed_theirs)
    down_got = swap(down_sent, "s")
    (pre_grad, up_bias_grad), facts = act_grad(
        facts, feed_both, down_all, slope, wait=(down_sent,)
    )
    hidden_sent = product(pre_grad[slots:], up_all, 1, 1).astype(jnp.bfloat16)
    hidden_other = swap(hidden_sent, "c")
    hidden_own_t, hidden_other_t = hidden_turned
    up_sent = grad_block(hidden_other_t, pre_grad)
    up_got = swap(up_sent, "x")
    hidden_part = product(pre_grad[:slots], up_all, 1, 1)
    (first_grad, attn_low, third_sums), facts = first_norm(
        facts,
        hidden_part,
        hidden_other,
        second_grad,
        first_hat,
        first_rstd,
        vectors,
        wait=(up_sent,),
    )
    grad_sent = product(attn_low, out_other, 1, 1).astype(jnp.bfloat16)
    grad_other = swap(grad_sent, "c")
    grad_own = product(attn_low, out_own, 1, 1).astype(jnp.bfloat16)
    out_sent = product(heads_other, attn_low, 0, 0).astype(jnp.bfloat16)
    out_got = swap(out_sent, "c")
    out_grad = grad_block(heads_out[:slots].T, attn_low, out_got)
    out_line = out_grad.reshape((4, 2 * out_weight.shape[0], width))
    out_kept, out_sent = line_parts(out_line)
    out_got = lax.ppermute(out_sent, "z", NEXT)
    heads_grad = jnp.concatenate([grad_own, grad_other], axis=0)
    (theirs_low, theirs_sums), facts = attend_back(
        facts, projected, heads_grad, totals, slots, False, wait=(out_sent, mixed_got)
    )
    in_sent = grad_block(tokens_t, theirs_low)
    in_got = swap(in_sent, "s")
    down_total = grad_block(act_t, feed_mine, down_got)
    down_kept, down_sent = halve(down_total.reshape(4, 2, unit_block, cols), "x", 1)
    down_got = swap(down_sent, "x")
    out_total = add(out_kept, out_got)
    upper = lax.axis_index("z") // 2
    out_kept, out_sent = pick(out_total, upper, 0), pick(out_total, 1 - upper, 0)
    out_got = lax.ppermute(out_sent, "z", CROSS)
    (mine_low, mine_sums), facts = attend_back(
        facts, projected, heads_grad, totals, slots, True, wait=(in_sent, out_sent, down_sent)
    )
    up_total = grad_block(hidden_own_t, pre_grad, up_got).reshape(4, rows, 2 * up_cols)
    up_kept, up_sent = columns_of(up_total, half), columns_of(up_total, 1 - half)
    up_got = swap(up_sent, "s")
    out_kept = add(out_kept, out_got)
    valid_count = length_own[0].astype(jnp.float32) * width
    stats = jnp.stack(
        [jnp.sum(first_sums[0]), jnp.sum(first_sums[1]), jnp.sum(second_sums[3]), valid_count]
    )
    mine_sums, theirs_sums = jnp.sum(mine_sums, axis=(0, 1)), jnp.sum(theirs_sums, axis=(0, 1))
    late = in_order(mine_sums, theirs_sums, half)
    sums = jnp.concatenate(
        [
            second_sums[:3].reshape(-1),
            third_sums[:3].reshape(-1),
            jnp.pad(stats, (0, 124)),
            up_bias_grad[0],
            late[:, :wide].reshape(-1),
            late[:, 2 * wide :].reshape(-1),
        ]
    )
    sums = sums + lax.ppermute(sums, "z", NEXT)
    (tokens_part, tokens_sent), facts = tokens_grad(
        facts,
        mine_low,
        theirs_low,
        in_weight,
        wait=(up_sent, out_kept, sums),
    )
    tokens_other = swap(tokens_sent, "c")
    in_total = grad_block(tokens_t, mine_low, in_got)
    in_kept, in_sent = halve(in_total.reshape(4, 2, rows, 3 * wide), "x", 1)
    in_got = swap(in_sent, "x")
    (down_pairs, down_next), facts = add_parts(
        facts, down_kept, down_got, wait=(in_sent, tokens_part)
    )
    down_got = lax.ppermute(down_next, "z", NEXT)
    (in_pairs, in_next, sums, out_kept), facts = add_parts(
        facts, in_kept, in_got, wait=(down_next,), through=(sums, out_kept)
    )
    in_got = lax.ppermute(in_next, "z", NEXT)
    (down_kept, down_sent), facts = add_last(facts, down_pairs, down_got, wait=(in_next,))
    (up_pairs, up_next), facts = add_parts(facts, up_kept, up_got, wait=(down_sent,))
    up_got = lax.ppermute(up_next, "z", NEXT)
    sums = sums + swap(sums, "x")
    sums = sums + swap(sums, "s")
    (in_kept, in_sent, out_kept), facts = add_last(
        facts, in_pairs, in_got, wait=(sums, up_next), through=(out_kept,)
    )
    (up_kept, up_sent, sums), facts = add_last(
        facts, up_pairs, up_got, wait=(in_sent,), through=(sums,)
    )
    in_sum = add(in_kept, lax.ppermute(in_sent, "z", CROSS))
    tokens_grad_sum = tokens_part + tokens_other.astype(jnp.float32) + first_grad
    tokens_grad_sum = from_sequence(tokens_grad_sum.astype(jnp.bfloat16))
    mixed = in_order(mixed[:row_count], mixed_got, half)
    down_sum = add(down_kept, lax.ppermute(down_sent, "z", CROSS))
    up_sum = add(up_kept, lax.ppermute(up_sent, "z", CROSS))
    out_sum = fold_columns(fold(out_kept.reshape(2, out_weight.shape[0], width), "x", 0))

    sums = sums + lax.ppermute(sums, "z", CROSS)
    both_sums = in_order(sums, swap(sums, "c"), core)
    count = 6 * width + 128
    shared = both_sums[0, :count] + both_sums[1, :count]
    down_bias_grad, feed_gain_grad, feed_shift_grad, out_bias_grad, attn_gain_grad, attn_shift_grad = [
        shared[i * width : (i + 1) * width] for i in range(6)
    ]
    stats = shared[6 * width : 6 * width + 4]

    def interleave(start, size, block_size):
        sums = both_sums[:, start : start + size].reshape(2, -1, block_size)
        return sums.transpose(1, 0, 2).reshape(-1)

    up_bias_grad = interleave(count, units, unit_block)
    query_bias_grad = interleave(count + units, cols, HD)
    value_bias_gradient = interleave(count + units + cols, cols, HD)
    stream_rms = jnp.sqrt(stats[:3] / stats[3])

    def give_back(total):
        total = total.reshape((2, rows // 2) + total.shape[1:])
        return pick(total, core, 0), swap(pick(total, 1 - core, 0), "c")

    up_shares = give_back(up_sum)
    in_shares = give_back(in_sum)
    down_weight_grad = down_sum.astype(jnp.float32)
    out_weight_grad = out_sum.astype(jnp.float32)

    def merge(shares, start, size, block):
        one, two = [
            share[:, start : start + size].reshape(rows // 2, -1, block) for share in shares
        ]
        first = jnp.where(core == 0, one, two)
        second = jnp.where(core == 0, two, one)
        return jnp.stack([first, second], axis=2).reshape(rows // 2, -1).astype(jnp.float32)

    query_weight_grad = merge(in_shares, 0, wide, HD)
    key_weight_grad = merge(in_shares, wide, wide, HD)
    value_weight_grad = merge(in_shares, 2 * wide, wide, HD)
    up_weight_grad = merge(up_shares, 0, up_cols, unit_block)
    return (
        mixed,
        tokens_grad_sum,
        query_weight_grad,
        key_weight_grad,
        value_weight_grad,
        out_weight_grad,
        up_weight_grad,
        down_weight_grad,
        query_bias_grad,
        value_bias_gradient,
        out_bias_grad,
        attn_gain_grad,
        attn_shift_grad,
        up_bias_grad,
        down_bias_grad,
        feed_gain_grad,
        feed_shift_grad,
        stream_rms,
    )


def solution(mesh):
    devices = mesh.devices
    dp_count, seq_count = devices.shape
    split = seq_count == 2 and dp_count == 16
    if split:
        inner = jax.sharding.Mesh(devices.reshape(4, 2, 2, seq_count), ("z", "x", "c", "s"))
        dp, seq, body = ("z", "x", "c"), "s", split_body
    else:
        inner, dp, seq, body = mesh, "dp", "seq", general_body
    weights = (P(dp, seq),) * 6
    vectors = (P(),) * 9
    rows = P(dp, seq, None)
    in_specs = (rows, P(dp), rows) + weights + vectors
    out_specs = (rows, rows) + weights + vectors + (P(),)
    return jax.shard_map(body, mesh=inner, in_specs=in_specs, out_specs=out_specs, check_vma=False)
```

```python
from functools import partial
import math

import jax
import jax.numpy as jnp
from jax import lax
from jax.experimental import pallas as pl
from jax.experimental.pallas import tpu as pltpu
from jax.sharding import PartitionSpec as P

HD = 64


def layer_norm(values_in, gain_vector, shift_vector):
    mean_value = jnp.mean(values_in, axis=-1, keepdims=True)
    centered = values_in - mean_value
    variance = jnp.mean(centered * centered, axis=-1, keepdims=True)
    return centered * lax.rsqrt(variance + 1e-05) * gain_vector + shift_vector


def gather_weights(first, second, third, fourth, fifth, sixth):
    part = (
        lax.all_gather(first, "dp", axis=0, tiled=True),
        lax.all_gather(second, "dp", axis=0, tiled=True),
        lax.all_gather(third, "dp", axis=0, tiled=True),
        lax.all_gather(fourth, "dp", axis=0, tiled=True),
        lax.all_gather(fifth, "dp", axis=0, tiled=True),
        lax.all_gather(sixth, "dp", axis=0, tiled=True),
    )
    return (
        lax.all_gather(part[0], "seq", axis=1, tiled=True),
        lax.all_gather(part[1], "seq", axis=1, tiled=True),
        lax.all_gather(part[2], "seq", axis=1, tiled=True),
        lax.all_gather(part[3], "seq", axis=1, tiled=True),
        lax.all_gather(part[4], "seq", axis=1, tiled=True),
        lax.all_gather(part[5], "seq", axis=1, tiled=True),
    )


def reduce_grads(first, second, third, fourth, fifth, sixth):
    part = (
        lax.psum_scatter(first.astype(jnp.bfloat16), "seq", scatter_dimension=1, tiled=True).astype(
            jnp.float32
        ),
        lax.psum_scatter(
            second.astype(jnp.bfloat16), "seq", scatter_dimension=1, tiled=True
        ).astype(jnp.float32),
        lax.psum_scatter(third.astype(jnp.bfloat16), "seq", scatter_dimension=1, tiled=True).astype(
            jnp.float32
        ),
        lax.psum_scatter(
            fourth.astype(jnp.bfloat16), "seq", scatter_dimension=1, tiled=True
        ).astype(jnp.float32),
        lax.psum_scatter(fifth.astype(jnp.bfloat16), "seq", scatter_dimension=1, tiled=True).astype(
            jnp.float32
        ),
        lax.psum_scatter(sixth.astype(jnp.bfloat16), "seq", scatter_dimension=1, tiled=True).astype(
            jnp.float32
        ),
    )
    return (
        lax.psum_scatter(
            part[0].astype(jnp.bfloat16), "dp", scatter_dimension=0, tiled=True
        ).astype(jnp.float32),
        lax.psum_scatter(
            part[1].astype(jnp.bfloat16), "dp", scatter_dimension=0, tiled=True
        ).astype(jnp.float32),
        lax.psum_scatter(
            part[2].astype(jnp.bfloat16), "dp", scatter_dimension=0, tiled=True
        ).astype(jnp.float32),
        lax.psum_scatter(
            part[3].astype(jnp.bfloat16), "dp", scatter_dimension=0, tiled=True
        ).astype(jnp.float32),
        lax.psum_scatter(
            part[4].astype(jnp.bfloat16), "dp", scatter_dimension=0, tiled=True
        ).astype(jnp.float32),
        lax.psum_scatter(
            part[5].astype(jnp.bfloat16), "dp", scatter_dimension=0, tiled=True
        ).astype(jnp.float32),
    )


def block_layout(seq_count, row_count, head_count):
    block_seqs = math.gcd(seq_count, max(1, 512 // row_count))
    group_heads = math.gcd(head_count, 4)
    return (block_seqs, seq_count // block_seqs, group_heads, head_count // group_heads)


def head_slice(block_part, offset, group_width, group_heads):
    sliced = lax.dynamic_slice_in_dim(block_part, offset, group_width, 2)
    return sliced.reshape(sliced.shape[0], sliced.shape[1], group_heads, HD)


def attention_forward(queries, key_all, value_all, key_mask):
    seq_count, row_count, feature_total = queries.shape
    slot_count = key_all.shape[1]
    block_seqs, block_count, group_heads, group_count = block_layout(
        seq_count, row_count, feature_total // HD
    )
    group_width = group_heads * HD

    def seq_block(inputs):
        query_part, key_part, value_part, mask_part = inputs

        def head_block(group_index):
            offset = group_index * group_width
            query_heads = head_slice(query_part, offset, group_width, group_heads)
            key_heads = head_slice(key_part, offset, group_width, group_heads)
            value_heads = head_slice(value_part, offset, group_width, group_heads)
            scores = (
                jnp.einsum(
                    "brhd,bkhd->bhrk", query_heads, key_heads, preferred_element_type=jnp.float32
                )
                * 0.125
            )
            scores = jnp.where(mask_part[:, None, None, :], scores, -1e30)
            row_max = jnp.max(scores, axis=-1, keepdims=True)
            exponent = jnp.exp(scores - row_max)
            row_total = jnp.sum(exponent, axis=-1, keepdims=True)
            soft_probs = (exponent / row_total).astype(jnp.bfloat16)
            heads_out = jnp.einsum(
                "bhrk,bkhd->brhd", soft_probs, value_heads, preferred_element_type=jnp.float32
            )
            log_total = (row_max + jnp.log(row_total))[..., 0]
            return (heads_out.reshape(block_seqs, row_count, group_width), log_total)

        return lax.map(head_block, jnp.arange(group_count))

    outputs, log_totals = lax.map(
        seq_block,
        (
            queries.reshape(block_count, block_seqs, row_count, feature_total),
            key_all.reshape(block_count, block_seqs, slot_count, feature_total),
            value_all.reshape(block_count, block_seqs, slot_count, feature_total),
            key_mask.reshape(block_count, block_seqs, slot_count),
        ),
    )
    mixed_heads = outputs.transpose(0, 2, 3, 1, 4).reshape(seq_count, row_count, feature_total)
    return (mixed_heads, log_totals)


def attention_backward(queries, key_all, value_all, key_mask, heads_grad, log_totals):
    seq_count, row_count, feature_total = queries.shape
    slot_count = key_all.shape[1]
    block_seqs, block_count, group_heads, group_count = block_layout(
        seq_count, row_count, feature_total // HD
    )
    group_width = group_heads * HD

    def seq_block(inputs):
        query_part, key_part, value_part, mask_part, grad_part, total_part = inputs

        def head_block(group_index):
            offset = group_index * group_width
            query_heads = head_slice(query_part, offset, group_width, group_heads)
            key_heads = head_slice(key_part, offset, group_width, group_heads)
            value_heads = head_slice(value_part, offset, group_width, group_heads)
            grad_heads = head_slice(grad_part, offset, group_width, group_heads)
            log_total = lax.dynamic_index_in_dim(total_part, group_index, 0, keepdims=False)
            scores = (
                jnp.einsum(
                    "brhd,bkhd->bhrk", query_heads, key_heads, preferred_element_type=jnp.float32
                )
                * 0.125
            )
            scores = jnp.where(mask_part[:, None, None, :], scores, -1e30)
            soft_probs = jnp.exp(scores - log_total[..., None])
            value_grad = jnp.einsum(
                "bhrk,brhd->bkhd",
                soft_probs.astype(jnp.bfloat16),
                grad_heads,
                preferred_element_type=jnp.float32,
            )
            prob_grad = jnp.einsum(
                "brhd,bkhd->bhrk", grad_heads, value_heads, preferred_element_type=jnp.float32
            )
            inner = jnp.sum(soft_probs * prob_grad, axis=-1, keepdims=True)
            score_grad = (soft_probs * (prob_grad - inner)).astype(jnp.bfloat16)
            query_grad = (
                jnp.einsum(
                    "bhrk,bkhd->brhd", score_grad, key_heads, preferred_element_type=jnp.float32
                )
                * 0.125
            )
            key_grad = (
                jnp.einsum(
                    "bhrk,brhd->bkhd", score_grad, query_heads, preferred_element_type=jnp.float32
                )
                * 0.125
            )
            return (
                query_grad.reshape(block_seqs, row_count, group_width),
                key_grad.reshape(block_seqs, slot_count, group_width),
                value_grad.reshape(block_seqs, slot_count, group_width),
            )

        return lax.map(head_block, jnp.arange(group_count))

    query_blocks, key_blocks, value_block_list = lax.map(
        seq_block,
        (
            queries.reshape(block_count, block_seqs, row_count, feature_total),
            key_all.reshape(block_count, block_seqs, slot_count, feature_total),
            value_all.reshape(block_count, block_seqs, slot_count, feature_total),
            key_mask.reshape(block_count, block_seqs, slot_count),
            heads_grad.reshape(block_count, block_seqs, row_count, feature_total),
            log_totals,
        ),
    )
    query_grad = query_blocks.transpose(0, 2, 3, 1, 4).reshape(seq_count, row_count, feature_total)
    key_grad = key_blocks.transpose(0, 2, 3, 1, 4).reshape(seq_count, slot_count, feature_total)
    value_grad = value_block_list.transpose(0, 2, 3, 1, 4).reshape(
        seq_count, slot_count, feature_total
    )
    return (query_grad, key_grad, value_grad)


def general_body(
    tokens,
    lengths,
    cotangent,
    query_weight,
    key_weight,
    value_weight,
    out_weight,
    up_weight,
    down_weight,
    query_bias,
    value_bias,
    out_bias,
    attn_gain,
    attn_shift,
    up_bias,
    down_bias,
    feed_gain,
    feed_shift,
):
    seq_count, row_count, feature_total = tokens.shape
    slot_count = row_count * lax.axis_size("seq")
    token_count = seq_count * row_count
    whole = gather_weights(
        query_weight, key_weight, value_weight, out_weight, up_weight, down_weight
    )
    full_query, full_key, full_value, full_out, full_up, full_down = whole
    flat_tokens = tokens.reshape(token_count, feature_total)
    queries = (
        jnp.dot(flat_tokens, full_query, preferred_element_type=jnp.float32) + query_bias
    ).astype(jnp.bfloat16)
    key_rows = jnp.dot(flat_tokens, full_key, preferred_element_type=jnp.float32).astype(
        jnp.bfloat16
    )
    value_rows = (
        jnp.dot(flat_tokens, full_value, preferred_element_type=jnp.float32) + value_bias
    ).astype(jnp.bfloat16)
    first_slot = lax.axis_index("seq") * row_count
    key_mask = jnp.arange(slot_count)[None, :] < lengths[:, None]
    row_valid = ((first_slot + jnp.arange(row_count))[None, :] < lengths[:, None]).astype(
        jnp.float32
    )
    row_valid = row_valid.reshape(token_count, 1)
    query_blocks = queries.reshape(seq_count, row_count, feature_total)
    key_blocks = key_rows.reshape(seq_count, row_count, feature_total)
    value_block_list = value_rows.reshape(seq_count, row_count, feature_total)
    key_all, value_all = (
        lax.all_gather(key_blocks, "seq", axis=1, tiled=True),
        lax.all_gather(value_block_list, "seq", axis=1, tiled=True),
    )
    mixed_heads, log_totals = attention_forward(query_blocks, key_all, value_all, key_mask)
    heads_low = mixed_heads.reshape(token_count, feature_total).astype(jnp.bfloat16)
    attention_out = jnp.dot(heads_low, full_out, preferred_element_type=jnp.float32) + out_bias
    tokens_f32 = flat_tokens.astype(jnp.float32)
    first_sum = tokens_f32 + attention_out
    hidden, first_pull = jax.vjp(layer_norm, first_sum, attn_gain, attn_shift)
    hidden_low = hidden.astype(jnp.bfloat16)
    pre_act = jnp.dot(hidden_low, full_up, preferred_element_type=jnp.float32) + up_bias
    gelu_out, gelu_pull = jax.vjp(partial(jax.nn.gelu, approximate=False), pre_act)
    activation = gelu_out.astype(jnp.bfloat16)
    feed_out = jnp.dot(activation, full_down, preferred_element_type=jnp.float32) + down_bias
    result, second_pull = jax.vjp(layer_norm, hidden + feed_out, feed_gain, feed_shift)
    mixed = result.astype(jnp.bfloat16).reshape(seq_count, row_count, feature_total)
    partial_stats = jnp.stack(
        [
            jnp.sum(row_valid * tokens_f32 * tokens_f32),
            jnp.sum(row_valid * attention_out * attention_out),
            jnp.sum(row_valid * feed_out * feed_out),
            jnp.sum(row_valid) * feature_total,
        ]
    )
    back_weights = gather_weights(
        query_weight, key_weight, value_weight, out_weight, up_weight, down_weight
    )
    back_query, back_key, back_value, back_out, back_up, back_down = back_weights
    out_grad = cotangent.reshape(token_count, feature_total).astype(jnp.float32) * row_valid
    second_grad, feed_gain_grad, feed_shift_grad = second_pull(out_grad)
    feed_low = second_grad.astype(jnp.bfloat16)
    down_weight_grad = jnp.einsum(
        "nf,nd->fd", activation, feed_low, preferred_element_type=jnp.float32
    )
    down_bias_grad = jnp.sum(feed_low, axis=0, dtype=jnp.float32)
    act_grad = jnp.einsum(
        "nd,fd->nf", feed_low, back_down, preferred_element_type=jnp.float32
    ).astype(jnp.bfloat16)
    pre_grad = gelu_pull(act_grad.astype(jnp.float32))[0].astype(jnp.bfloat16)
    up_weight_grad = jnp.einsum(
        "nd,nf->df", hidden_low, pre_grad, preferred_element_type=jnp.float32
    )
    up_bias_grad = jnp.sum(pre_grad, axis=0, dtype=jnp.float32)
    hidden_grad = (
        jnp.einsum("nf,df->nd", pre_grad, back_up, preferred_element_type=jnp.float32) + second_grad
    )
    first_grad, attn_gain_grad, attn_shift_grad = first_pull(hidden_grad)
    attn_low = first_grad.astype(jnp.bfloat16)
    out_weight_grad = jnp.einsum(
        "nd,ne->de", heads_low, attn_low, preferred_element_type=jnp.float32
    )
    out_bias_grad = jnp.sum(attn_low, axis=0, dtype=jnp.float32)
    heads_grad = jnp.einsum(
        "ne,de->nd", attn_low, back_out, preferred_element_type=jnp.float32
    ).astype(jnp.bfloat16)
    heads_grad = heads_grad.reshape(seq_count, row_count, feature_total)
    query_grad, key_part_grad, value_part_grad = attention_backward(
        query_blocks, key_all, value_all, key_mask, heads_grad, log_totals
    )
    key_sum, value_sum = (
        lax.psum_scatter(
            key_part_grad.astype(jnp.bfloat16), "seq", scatter_dimension=1, tiled=True
        ).astype(jnp.float32),
        lax.psum_scatter(
            value_part_grad.astype(jnp.bfloat16), "seq", scatter_dimension=1, tiled=True
        ).astype(jnp.float32),
    )
    query_low = query_grad.reshape(token_count, feature_total).astype(jnp.bfloat16)
    key_low = key_sum.reshape(token_count, feature_total).astype(jnp.bfloat16)
    value_low = value_sum.reshape(token_count, feature_total).astype(jnp.bfloat16)
    query_weight_grad = jnp.einsum(
        "nd,ne->de", flat_tokens, query_low, preferred_element_type=jnp.float32
    )
    key_weight_grad = jnp.einsum(
        "nd,ne->de", flat_tokens, key_low, preferred_element_type=jnp.float32
    )
    value_weight_grad = jnp.einsum(
        "nd,ne->de", flat_tokens, value_low, preferred_element_type=jnp.float32
    )
    query_bias_grad = jnp.sum(query_low, axis=0, dtype=jnp.float32)
    value_bias_gradient = jnp.sum(value_low, axis=0, dtype=jnp.float32)
    tokens_grad = (
        jnp.einsum("ne,de->nd", query_low, back_query, preferred_element_type=jnp.float32)
        + jnp.einsum("ne,de->nd", key_low, back_key, preferred_element_type=jnp.float32)
        + jnp.einsum("ne,de->nd", value_low, back_value, preferred_element_type=jnp.float32)
        + first_grad
    )
    tokens_grad = tokens_grad.astype(jnp.bfloat16).reshape(seq_count, row_count, feature_total)
    matrix_grads = reduce_grads(
        query_weight_grad,
        key_weight_grad,
        value_weight_grad,
        out_weight_grad,
        up_weight_grad,
        down_weight_grad,
    )
    totals = lax.psum(
        (
            partial_stats,
            query_bias_grad,
            value_bias_gradient,
            out_bias_grad,
            attn_gain_grad,
            attn_shift_grad,
            up_bias_grad,
            down_bias_grad,
            feed_gain_grad,
            feed_shift_grad,
        ),
        ("dp", "seq"),
    )
    stream_rms = jnp.sqrt(totals[0][:3] / totals[0][3])
    return (
        mixed,
        tokens_grad,
        matrix_grads[0],
        matrix_grads[1],
        matrix_grads[2],
        matrix_grads[3],
        matrix_grads[4],
        matrix_grads[5],
        totals[1],
        totals[2],
        totals[3],
        totals[4],
        totals[5],
        totals[6],
        totals[7],
        totals[8],
        totals[9],
        stream_rms,
    )


def swap(value, axis):
    return lax.ppermute(value, axis, [(0, 1), (1, 0)])


def both(value, axis):
    return jnp.concatenate([value, swap(value, axis)], axis=0)


def in_order(own, other, index, axis=0):
    return jnp.where(
        index == 0, jnp.stack([own, other], axis=axis), jnp.stack([other, own], axis=axis)
    )


def pick(values, index, axis):
    return lax.dynamic_index_in_dim(values, index, axis, keepdims=False)


def add(left, right):
    return (left.astype(jnp.float32) + right.astype(jnp.float32)).astype(jnp.bfloat16)


def fold(values, axis, dim):
    index = lax.axis_index(axis)
    return add(pick(values, index, dim), swap(pick(values, 1 - index, dim), axis))


NEXT = [(0, 1), (1, 0), (2, 3), (3, 2)]
CROSS = [(0, 2), (2, 0), (1, 3), (3, 1)]


def fold_cross(pairs):
    upper = lax.axis_index("z") // 2
    return add(pick(pairs, upper, 0), lax.ppermute(pick(pairs, 1 - upper, 0), "z", CROSS))


def fold_line(values):
    odd = lax.axis_index("z") % 2
    pairs = values.reshape((2, 2) + values.shape[1:])
    sent = lax.ppermute(pick(pairs, 1 - odd, 1), "z", NEXT)
    return fold_cross(add(pick(pairs, odd, 1), sent))


def line_cross(value):
    return lax.ppermute(value, "z", CROSS)


def line_next(pair):
    return lax.ppermute(pair, "z", NEXT)


def gather_square(own, way):
    beside, below = swap(own, "x"), swap(own, "s")
    across = swap(below, "x") if way == "x" else swap(beside, "s")
    return [own, beside, below, across]


def fold_columns(total):
    half = lax.axis_index("s")
    return add(columns_of(total, half), swap(columns_of(total, 1 - half), "s"))


def halve(values, axis, dim):
    index = lax.axis_index(axis) % 2
    return pick(values, index, dim), pick(values, 1 - index, dim)


def line_parts(values):
    return halve(values.reshape((2, 2) + values.shape[1:]), "z", 1)


def scatter_top(send, keep):
    total = add(keep, swap(send, "s"))
    total = total.reshape((4, 2) + total.shape[1:])
    return fold_line(fold(total, "x", 1))


def grad_block(left_t, right, got=None):
    total = product(left_t, right, 1, 0)
    if got is not None:
        total = total + got.astype(jnp.float32)
    return total.astype(jnp.bfloat16)


def columns_of(right, index):
    columns = right.shape[-1] // 2
    return lax.dynamic_slice_in_dim(right, index * columns, columns, right.ndim - 1)


PAIR = 2 * HD
LIMIT = 16 * 1024 * 1024


def kernel_params(steps):
    return pltpu.CompilerParams(
        dimension_semantics=("arbitrary",) * steps, vmem_limit_bytes=LIMIT
    )


def product(left, right, left_dim, right_dim):
    return lax.dot_general(
        left, right, (((left_dim,), (right_dim,)), ((), ())), preferred_element_type=jnp.float32
    )


def key_bias(facts_ref, slots):
    place = lax.broadcasted_iota(jnp.int32, (slots, 1), 0) + facts_ref[2]
    place = jnp.where(place >= slots, place - slots, place)
    return jnp.where(place < facts_ref[pl.program_id(0)], 0.0, -1e30)


def head_lanes(value, head):
    lane = lax.broadcasted_iota(jnp.int32, value.shape, 1)
    return jnp.where((lane >= HD) == (head == 1), value, jnp.zeros_like(value))


def turned(value):
    return value.astype(jnp.float32).T


def attend_kernel(facts_ref, query_ref, key_ref, value_ref, out_ref, total_ref):
    slots = key_ref.shape[0]
    bias = key_bias(facts_ref, slots)
    query = query_ref[...] * jnp.bfloat16(0.125)
    key = key_ref[...]
    value_t = turned(value_ref[...]).astype(jnp.bfloat16)
    outs = []
    for head in range(2):
        scores = product(key, head_lanes(query, head), 1, 1) + bias
        peak = jnp.max(scores, axis=0, keepdims=True)
        weight = jnp.exp(scores - peak)
        total = jnp.sum(weight, axis=0, keepdims=True)
        part = product(value_t[head * HD : (head + 1) * HD], weight.astype(jnp.bfloat16), 1, 0)
        outs.append(part * (1.0 / total))
        total_ref[0, 0, head : head + 1, :] = peak + jnp.log(total)
    out_ref[...] = jnp.concatenate(outs, axis=0).T.astype(jnp.bfloat16)


def attend_back_kernel(
    facts_ref, query_ref, key_ref, value_ref, grad_ref, total_ref, low_ref, sums_ref
):
    slots = key_ref.shape[0]
    bias = key_bias(facts_ref, slots)
    query = query_ref[...] * jnp.bfloat16(0.125)
    key = key_ref[...]
    value = value_ref[...]
    grad = grad_ref[...]
    key_t = turned(key).astype(jnp.bfloat16)
    lane = lax.broadcasted_iota(jnp.int32, (slots, PAIR), 1)
    query_parts, key_parts, value_parts = [], [], []
    for head in range(2):
        scores = product(key, head_lanes(query, head), 1, 1) + bias
        soft = jnp.exp(scores - total_ref[0, 0, head : head + 1, :])
        value_parts.append(product(soft.astype(jnp.bfloat16), grad, 1, 0))
        change = product(value, head_lanes(grad, head), 1, 1)
        inner = jnp.sum(soft * change, axis=0, keepdims=True)
        change = (soft * (change - inner)).astype(jnp.bfloat16)
        key_parts.append(product(change, query, 1, 0))
        query_parts.append(product(key_t[head * HD : (head + 1) * HD], change, 1, 0))
    pair = pl.program_id(1)
    groups = low_ref.shape[1] // 3
    query_low = (jnp.concatenate(query_parts, axis=0) * 0.125).T
    key_low = jnp.where(lane < HD, key_parts[0], key_parts[1])
    value_low = jnp.where(lane < HD, value_parts[0], value_parts[1])
    for place, part in enumerate((query_low, key_low, value_low)):
        start = pl.multiple_of(place * groups + pair * PAIR, PAIR)
        low = part.astype(jnp.bfloat16)
        low_ref[:, pl.ds(start, PAIR)] = low
        sums_ref[0, :, pl.ds(start, PAIR)] = jnp.sum(
            low.astype(jnp.float32), axis=0, keepdims=True
        )


def attention_specs(slots, pairs):
    def at(part):
        return pl.BlockSpec(
            (slots, PAIR), lambda b, g, p, *_: (b, g * 3 * pairs + part * pairs + p)
        )

    heads = pl.BlockSpec((slots, PAIR), lambda b, g, p, *_: (b, g * pairs + p))
    totals = pl.BlockSpec((1, 1, 2, slots), lambda b, g, p, *_: (b, g * pairs + p, 0, 0))
    return [at(0), at(1), at(2)], heads, totals


def attend(facts, projected, slots, wait=()):
    pairs = projected.shape[1] // (6 * PAIR)
    inputs, heads, totals = attention_specs(slots, pairs)
    rows = projected.shape[0]
    return call(
        attend_kernel,
        "attend",
        (2, 2, pairs),
        inputs,
        [heads, totals],
        [
            like((rows, 2 * pairs * PAIR), jnp.bfloat16),
            like((2, 2 * pairs, 2, slots), jnp.float32),
        ],
        facts,
        projected,
        projected,
        projected,
        wait=wait,
    )


def attend_back(facts, projected, heads_grad, totals_in, slots, own, wait=(), through=()):
    pairs = projected.shape[1] // (6 * PAIR)

    def group(facts_ref):
        return facts_ref[3] if own else 1 - facts_ref[3]

    def at(part):
        return pl.BlockSpec(
            (slots, PAIR), lambda b, p, f: (b, group(f) * 3 * pairs + part * pairs + p)
        )

    heads = pl.BlockSpec((slots, PAIR), lambda b, p, f: (b, group(f) * pairs + p))
    totals = pl.BlockSpec((1, 1, 2, slots), lambda b, p, f: (b, group(f) * pairs + p, 0, 0))
    width = 3 * pairs * PAIR
    return call(
        attend_back_kernel,
        "attend_back",
        (2, pairs),
        [at(0), at(1), at(2), heads, totals],
        [
            pl.BlockSpec((slots, width), lambda b, p, f: (b, 0)),
            pl.BlockSpec((1, 1, width), lambda b, p, f: (b, 0, 0)),
        ],
        [
            like((2 * slots, width), jnp.bfloat16),
            like((2, 1, width), jnp.float32),
        ],
        facts,
        projected,
        projected,
        projected,
        heads_grad,
        totals_in,
        wait=wait,
        through=through,
    )


def call(kernel, name, grid, inputs, outputs, shapes, facts, *args, wait=(), scratch=(), through=(), into=()):
    single = not isinstance(outputs, list)
    outputs, shapes = ([outputs], [shapes]) if single else (outputs, shapes)
    wait = tuple(into) + tuple(wait)
    count, held, passed = len(args), len(wait) + len(through), len(through)
    last = count + held + len(outputs)

    def body(facts_ref, *refs):
        kernel(facts_ref, *refs[:count], *refs[count + held : last], *refs[last + passed + 1 :])
        for place in range(facts.shape[0]):
            refs[last + passed][place] = facts_ref[place]

    results = pl.pallas_call(
        body,
        grid_spec=pltpu.PrefetchScalarGridSpec(
            num_scalar_prefetch=1,
            grid=grid,
            in_specs=list(inputs) + [pl.BlockSpec(memory_space=pl.ANY)] * held,
            out_specs=list(outputs)
            + [pl.BlockSpec(memory_space=pl.ANY)] * passed
            + [pl.BlockSpec(memory_space=pltpu.SMEM)],
            scratch_shapes=list(scratch),
        ),
        out_shape=list(shapes)
        + [like(value.shape, value.dtype) for value in through]
        + [like(facts.shape, jnp.int32)],
        input_output_aliases={
            **{1 + count + i: i for i in range(len(into))},
            **{1 + count + len(wait) + i: len(outputs) + i for i in range(passed)},
        },
        compiler_params=kernel_params(len(grid)),
        name=name,
    )(facts, *args, *wait, *through)
    values = tuple(results[:-1])
    return (values[0] if single and not passed else values), results[-1]


def block(shape, *index):
    def at(*grid_and_facts):
        return tuple(entry(*grid_and_facts) if callable(entry) else entry for entry in index)

    return pl.BlockSpec(shape, at)


def whole(array):
    zeros = (0,) * array.ndim
    return pl.BlockSpec(array.shape, lambda *_: zeros)


def first(i, *_):
    return i


def like(shape, dtype):
    return jax.ShapeDtypeStruct(shape, dtype)


def rows_in_order(facts_ref, own, beside):
    even = facts_ref[4] == 0
    pieces = []
    for z in range(4):
        pieces += [jnp.where(even, own[z], beside[z]), jnp.where(even, beside[z], own[z])]
    return jnp.concatenate(pieces, axis=0)


def near_or_far(facts_ref, refs, near):
    own, beside, below, across = [ref[...] for ref in refs]
    return rows_in_order(
        facts_ref, jnp.where(near, own, below), jnp.where(near, beside, across)
    )


def square_columns(parts, wide, steps):
    shape = parts[0].shape[:2] + (wide,)
    near = block(shape, 0, 0, lambda i, *_: jnp.minimum(i, steps - 1))
    far = block(shape, 0, 0, lambda i, *_: jnp.maximum(i - steps, 0))
    return [near, near, far, far]


def half_at(i, facts, steps):
    return jnp.where(i < steps, facts[3], 1 - facts[3])


def gate_kernel(facts_ref):
    del facts_ref


def gate(facts, through, wait):
    return call(gate_kernel, "gate", (1,), [], [], [], facts, wait=wait, through=through)


def stack_kernel(own_at, facts_ref, own_ref, other_ref, out_ref):
    own = facts_ref[own_at] == pl.program_id(0)
    value = jnp.where(own, own_ref[...], other_ref[...])
    out_ref[...] = value.reshape(out_ref.shape)


def stack_pair(facts, own, other, wait=(), through=()):
    rows, columns = own.shape
    return call(
        partial(stack_kernel, 6),
        "stack",
        (2,),
        [whole(own), whole(other)],
        block((1, rows, columns), first, 0, 0),
        like((2, rows, columns), own.dtype),
        facts,
        own,
        other,
        wait=wait,
        through=through,
    )


def stack_line(facts, own, other, wait=()):
    _, rows, columns = own.shape
    line, facts = call(
        partial(stack_kernel, 7),
        "stack_line",
        (2,),
        [whole(own), whole(other)],
        block((2, 1, rows, columns), 0, first, 0, 0),
        like((2, 2, rows, columns), own.dtype),
        facts,
        own,
        other,
        wait=wait,
    )
    return line.reshape(4, rows, columns), facts


def turn_kernel(facts_ref, *refs):
    for i in range(2):
        refs[4 + i][...] = jnp.concatenate([refs[2 * i][...].T, refs[2 * i + 1][...].T], axis=1)


def turn_all_kernel(facts_ref, rows_ref, out_ref):
    out_ref[...] = rows_ref[...].T


def turn_all(facts, values, wait=()):
    count, width = values.shape
    step = width // 4
    return call(
        turn_all_kernel,
        "turn_all",
        (4,),
        [block((count, step), 0, first)],
        block((step, count), first, 0),
        like((width, count), values.dtype),
        facts,
        values,
        wait=wait,
    )


def turn(facts, values, others, rows, wait=()):
    count, width = values.shape
    half = width // 2
    out = block((rows, 2 * count), first, 0)
    shape = like((half, 2 * count), values.dtype)
    own = block((count, rows), 0, lambda i, f: 2 * i + f[4])
    other = block((count, rows), 0, lambda i, f: 2 * i + 1 - f[4])
    return call(
        turn_kernel,
        "turn",
        (half // rows,),
        [own, own, other, other],
        [out, out],
        [shape, shape],
        facts,
        values,
        others,
        values,
        others,
        wait=wait,
    )


def project_kernel(facts_ref, rows_ref, bias_ref, *refs):
    parts, (out_ref, in_ref, rest_ref) = refs[:4], refs[4:]
    step = pl.program_id(0)
    weight = near_or_far(facts_ref, parts, step < 4)

    @pl.when(step % 4 < 3)
    def _():
        in_ref[...] = weight
        value = product(rows_ref[...], weight, 1, 0) + bias_ref[...]
        out_ref[...] = value.astype(jnp.bfloat16)

    @pl.when(step % 4 == 3)
    def _():
        chips, count, wide = rest_ref.shape
        pairs = weight.reshape(chips, 2, count, wide // 2)
        rest_ref[...] = jnp.concatenate([pairs[:, 0], pairs[:, 1]], axis=2)


def project(facts, rows, bias, parts, wait=()):
    count, width = rows.shape
    wide = parts[0].shape[2] // 4

    def column(i, f):
        return half_at(i, f, 4) * 3 + jnp.minimum(i % 4, 2)

    out = block((count, wide), 0, column)
    rest = (8, parts[0].shape[1] // 2, 2 * wide)
    return call(
        project_kernel,
        "project",
        (8,),
        [whole(rows), block((1, wide), 0, column)] + square_columns(parts, wide, 4),
        [out, block((width, wide), 0, column), block(rest, 0, 0, lambda i, f: half_at(i, f, 4))],
        [
            like((count, 6 * wide), jnp.bfloat16),
            like((width, 6 * wide), jnp.bfloat16),
            like(rest[:2] + (4 * wide,), jnp.bfloat16),
        ],
        facts,
        rows,
        bias[None],
        *parts,
        wait=wait,
    )


def valid_rows(facts_ref, count, slots):
    place = lax.broadcasted_iota(jnp.int32, (count, 1), 0) + pl.program_id(0) * count + facts_ref[2]
    place = jnp.where(place >= slots, place - slots, place)
    return (place < facts_ref[0]).astype(jnp.float32)


def add_rows(sums_ref, rows):
    total = jnp.concatenate([jnp.sum(part, axis=0, keepdims=True) for part in rows], axis=0)
    total = jnp.concatenate([total, jnp.zeros((8 - len(rows), total.shape[1]), jnp.float32)], axis=0)

    @pl.when(pl.program_id(0) == 0)
    def _():
        sums_ref[...] = total

    @pl.when(pl.program_id(0) > 0)
    def _():
        sums_ref[...] += total


def mean_of(values):
    return jnp.mean(values, axis=-1, keepdims=True)


def attend_out_kernel(
    slots, facts_ref, own_ref, other_ref, own_weight_ref, other_weight_ref, tokens_ref, vectors_ref,
    hat_ref, rstd_ref, low_ref, sums_ref,
):
    branch = (
        product(own_ref[...], own_weight_ref[...], 1, 0)
        + product(other_ref[...], other_weight_ref[...], 1, 0)
        + vectors_ref[0:1]
    )
    tokens = tokens_ref[...].astype(jnp.float32)
    total = tokens + branch
    centered = total - mean_of(total)
    rstd = lax.rsqrt(mean_of(centered * centered) + 1e-05)
    hat = centered * rstd
    hat_ref[...] = hat
    rstd_ref[...] = rstd
    low_ref[...] = (hat * vectors_ref[1:2] + vectors_ref[2:3]).astype(jnp.bfloat16)
    valid = valid_rows(facts_ref, tokens.shape[0], slots)
    add_rows(sums_ref, [valid * tokens * tokens, valid * branch * branch])


def attend_out(facts, own, other, own_weight, other_weight, tokens, vectors, wait=()):
    slots, width = tokens.shape
    step = slots // 4
    rows = lambda array: block((step, array.shape[1]), first, 0)
    return call(
        partial(attend_out_kernel, slots),
        "attend_out",
        (4,),
        [rows(own), rows(other), whole(own_weight), whole(other_weight), rows(tokens), whole(vectors)],
        [block((step, width), first, 0), block((step, 1), first, 0), block((step, width), first, 0), block((8, width), 0, 0)],
        [
            like((slots, width), jnp.float32),
            like((slots, 1), jnp.float32),
            like((slots, width), jnp.bfloat16),
            like((8, width), jnp.float32),
        ],
        facts,
        own,
        other,
        own_weight,
        other_weight,
        tokens,
        vectors,
        wait=wait,
    )


def up_kernel(facts_ref, rows_ref, others_ref, bias_ref, *refs):
    parts, (act_ref, slope_ref, turned_ref, weight_ref) = refs[:4], refs[4:]
    weight = near_or_far(facts_ref, parts, pl.program_id(0) < 4)
    weight_ref[...] = weight
    pre_act = [product(ref[...], weight, 1, 0) for ref in (rows_ref, others_ref)]
    pre_act = jnp.concatenate(pre_act, axis=0) + bias_ref[...]
    below = 0.5 + 0.5 * lax.erf(pre_act * 0.7071067811865476)
    act = (pre_act * below).astype(jnp.bfloat16)
    act_ref[...] = act
    turned_ref[...] = act.T
    slope = below + pre_act * (0.3989422804014327 * jnp.exp(-0.5 * pre_act * pre_act))
    slope_ref[...] = slope.astype(jnp.bfloat16)


def feed_up(facts, rows, others, bias, parts, wait=()):
    count, width = 2 * rows.shape[0], rows.shape[1]
    units = bias.shape[0]
    wide = units // 8

    def column(i, f):
        return half_at(i, f, 4) * 4 + i % 4

    shape = like((count, units), jnp.bfloat16)
    out = block((count, wide), 0, column)
    return call(
        up_kernel,
        "feed_up",
        (8,),
        [whole(rows), whole(others), block((1, wide), 0, column)] + square_columns(parts, wide, 4),
        [out, out, block((wide, count), column, 0), block((width, wide), 0, column)],
        [
            shape,
            shape,
            like((units, count), jnp.bfloat16),
            like((width, units), jnp.bfloat16),
        ],
        facts,
        rows,
        others,
        bias[None],
        *parts,
        wait=wait,
    )


def down_kernel(facts_ref, rows_ref, *refs):
    parts, (weight_ref, out_ref, total_ref) = refs[:4], refs[4:]
    step = pl.program_id(0)
    own, beside, below, across = [ref[0] for ref in parts]
    even, left = facts_ref[4] == 0, facts_ref[3] == 0
    for x in range(2):
        mine = jnp.where(even, own, beside) if x == 0 else jnp.where(even, beside, own)
        theirs = jnp.where(even, below, across) if x == 0 else jnp.where(even, across, below)
        weight_ref[x] = jnp.concatenate(
            [jnp.where(left, mine, theirs), jnp.where(left, theirs, mine)], axis=1
        )
    weight = weight_ref[...].reshape(rows_ref.shape[1], out_ref.shape[1])
    value = product(rows_ref[...], weight, 1, 0)

    @pl.when(step == 0)
    def _():
        total_ref[...] = value

    @pl.when(step > 0)
    def _():
        total_ref[...] += value

    @pl.when(step == 3)
    def _():
        out_ref[...] = total_ref[...].astype(jnp.bfloat16)


def feed_down(facts, rows, parts, wait=()):
    count, units = rows.shape
    _, block_rows, half_width = parts[0].shape
    width = 2 * half_width
    shape = (1,) + parts[0].shape[1:]
    return call(
        down_kernel,
        "feed_down",
        (4,),
        [block((count // 2, units // 4), 1, first)] + [block(shape, first, 0, 0)] * 4,
        [block((2, block_rows, width), first, 0, 0), block((count // 2, width), 0, 0)],
        [like((8, block_rows, width), jnp.bfloat16), like((count // 2, width), jnp.bfloat16)],
        facts,
        rows,
        *parts,
        scratch=[pltpu.VMEM((count // 2, width), jnp.float32)],
        wait=wait,
    )


def second_norm_kernel(
    slots, facts_ref, part_ref, other_ref, hat_ref, cotangent_ref, vectors_ref,
    mixed_ref, grad_ref, low_ref, sums_ref,
):
    branch = part_ref[...] + other_ref[...].astype(jnp.float32) + vectors_ref[0:1]
    hidden = hat_ref[...] * vectors_ref[1:2] + vectors_ref[2:3]
    gain = vectors_ref[3:4]
    total = hidden + branch
    centered = total - mean_of(total)
    rstd = lax.rsqrt(mean_of(centered * centered) + 1e-05)
    hat = centered * rstd
    mixed_ref[...] = (hat * gain + vectors_ref[4:5]).astype(jnp.bfloat16)
    valid = valid_rows(facts_ref, branch.shape[0], slots)
    grad = cotangent_ref[...].astype(jnp.float32) * valid
    scaled = grad * gain
    result = rstd * (scaled - mean_of(scaled) - hat * mean_of(scaled * hat))
    low = result.astype(jnp.bfloat16)
    grad_ref[...] = result
    low_ref[...] = low
    add_rows(sums_ref, [low.astype(jnp.float32), grad * hat, grad, valid * branch * branch])


def second_norm(facts, part, other, hat, cotangent, vectors, wait=()):
    slots, width = part.shape
    step = slots // 4
    rows = block((step, width), first, 0)
    return call(
        partial(second_norm_kernel, slots),
        "second_norm",
        (4,),
        [rows, rows, rows, rows, whole(vectors)],
        [rows, rows, rows, block((8, width), 0, 0)],
        [
            like((slots, width), jnp.bfloat16),
            like((slots, width), jnp.float32),
            like((slots, width), jnp.bfloat16),
            like((8, width), jnp.float32),
        ],
        facts,
        part,
        other,
        hat,
        cotangent,
        vectors,
        wait=wait,
    )


def first_norm_kernel(
    facts_ref, part_ref, other_ref, second_ref, hat_ref, rstd_ref, vectors_ref,
    grad_ref, low_ref, sums_ref,
):
    grad = part_ref[...] + other_ref[...].astype(jnp.float32) + second_ref[...]
    hat = hat_ref[...]
    scaled = grad * vectors_ref[1:2]
    result = rstd_ref[...] * (scaled - mean_of(scaled) - hat * mean_of(scaled * hat))
    low = result.astype(jnp.bfloat16)
    grad_ref[...] = result
    low_ref[...] = low
    add_rows(sums_ref, [low.astype(jnp.float32), grad * hat, grad])


def first_norm(facts, part, other, second, hat, rstd, vectors, wait=()):
    slots, width = part.shape
    step = slots // 4
    rows = block((step, width), first, 0)
    return call(
        first_norm_kernel,
        "first_norm",
        (4,),
        [rows, rows, rows, rows, block((step, 1), first, 0), whole(vectors)],
        [rows, rows, block((8, width), 0, 0)],
        [
            like((slots, width), jnp.float32),
            like((slots, width), jnp.bfloat16),
            like((8, width), jnp.float32),
        ],
        facts,
        part,
        other,
        second,
        hat,
        rstd,
        vectors,
        wait=wait,
    )


def act_grad_kernel(facts_ref, rows_ref, weight_ref, slope_ref, out_ref, sums_ref):
    total = product(rows_ref[...], weight_ref[...], 1, 1)
    grad = total.astype(jnp.bfloat16).astype(jnp.float32) * slope_ref[...].astype(jnp.float32)
    low = grad.astype(jnp.bfloat16)
    out_ref[...] = low
    sums_ref[...] = jnp.sum(low.astype(jnp.float32), axis=0, keepdims=True)


def act_grad(facts, rows, weight, slope, wait=()):
    count, units = slope.shape
    step = units // 8
    out = block((count, step), 0, first)
    return call(
        act_grad_kernel,
        "act_grad",
        (8,),
        [whole(rows), block((step, rows.shape[1]), first, 0), out],
        [out, block((1, step), 0, first)],
        [like((count, units), jnp.bfloat16), like((1, units), jnp.float32)],
        facts,
        rows,
        weight,
        slope,
        wait=wait,
    )


def tokens_grad_kernel(facts_ref, mine_ref, theirs_ref, weight_ref, out_ref, sent_ref):
    wide = mine_ref.shape[1]
    slots = out_ref.shape[0]
    half = facts_ref[3]
    mine = weight_ref[:, pl.ds(pl.multiple_of(half * wide, 128), wide)]
    theirs = weight_ref[:, pl.ds(pl.multiple_of((1 - half) * wide, 128), wide)]
    total = product(mine_ref[...], mine, 1, 1) + product(theirs_ref[...], theirs, 1, 1)
    out_ref[...] = total[:slots]
    sent_ref[...] = total[slots:].astype(sent_ref.dtype)


def tokens_grad(facts, mine, theirs, weight, wait=(), through=()):
    count, columns = mine.shape
    width = weight.shape[0]
    step = width // 4
    out = block((count // 2, step), 0, first)
    return call(
        tokens_grad_kernel,
        "tokens_grad",
        (4,),
        [whole(mine), whole(theirs), block((step, 2 * columns), first, 0)],
        [out, out],
        [
            like((count // 2, width), jnp.float32),
            like((count // 2, width), jnp.bfloat16),
        ],
        facts,
        mine,
        theirs,
        weight,
        wait=wait,
        through=through,
    )


def add_parts_kernel(facts_ref, own_ref, got_ref, kept_ref, sent_ref):
    step = pl.program_id(0)
    total = own_ref[...].astype(jnp.float32) + got_ref[...].astype(jnp.float32)
    total = total.astype(jnp.bfloat16)

    @pl.when(step < 2)
    def _():
        sent_ref[...] = total

    @pl.when(step >= 2)
    def _():
        kept_ref[...] = total


def add_last_kernel(facts_ref, own_ref, got_ref, kept_ref, sent_ref):
    total = own_ref[0].astype(jnp.float32) + got_ref[0].astype(jnp.float32)
    total = total.astype(jnp.bfloat16)

    @pl.when(pl.program_id(0) == 0)
    def _():
        sent_ref[...] = total

    @pl.when(pl.program_id(0) == 1)
    def _():
        kept_ref[...] = total


def add_last(facts, own, got, wait=(), through=()):
    _, rows, columns = own.shape
    part = block((1, rows, columns), lambda i, f: jnp.where(i == 0, 1 - f[6], f[6]), 0, 0)
    shape = like((rows, columns), jnp.bfloat16)
    out = block((rows, columns), 0, 0)
    return call(
        add_last_kernel,
        "add_last",
        (2,),
        [part, part],
        [out, out],
        [shape, shape],
        facts,
        own,
        got,
        wait=wait,
        through=through,
    )


def add_parts(facts, own, got, wait=(), through=()):
    _, rows, columns = own.shape
    shape = (1, rows, columns)
    part = block(shape, lambda i, f: 2 * (i % 2) + jnp.where(i < 2, 1 - f[7], f[7]), 0, 0)
    half = like((2, rows, columns), jnp.bfloat16)
    return call(
        add_parts_kernel,
        "add_parts",
        (4,),
        [part, part],
        [
            block(shape, lambda i, *_: jnp.maximum(i - 2, 0), 0, 0),
            block(shape, lambda i, *_: jnp.minimum(i, 1), 0, 0),
        ],
        [half, half],
        facts,
        own,
        got,
        wait=wait,
        through=through,
    )


def alternate(value, width, offset):
    starts = range(offset * width, value.shape[1], 2 * width)
    return jnp.concatenate([value[:, start : start + width] for start in starts], axis=1)


def deal_kernel(unit_block, core_ref, query_ref, key_ref, value_ref, up_ref, *refs):
    first_core = core_ref[0] == 0
    near = [ref[...] for ref in (query_ref, key_ref, value_ref)]
    even = jnp.concatenate([alternate(value, HD, 0) for value in near], axis=1)
    odd = jnp.concatenate([alternate(value, HD, 1) for value in near], axis=1)
    up = up_ref[...]
    up_even, up_odd = alternate(up, unit_block, 0), alternate(up, unit_block, 1)
    refs[0][...] = jnp.where(first_core, even, odd)
    refs[1][...] = jnp.where(first_core, odd, even)
    refs[2][...] = jnp.where(first_core, up_even, up_odd)
    refs[3][...] = jnp.where(first_core, up_odd, up_even)


def deal(core, query, key, value, up, unit_block):
    near = like((query.shape[0], 3 * query.shape[1] // 2), jnp.bfloat16)
    half = like((up.shape[0], up.shape[1] // 2), jnp.bfloat16)
    shapes = [near, near, half, half]
    return call(
        partial(deal_kernel, unit_block),
        "deal",
        (1,),
        [whole(value) for value in (query, key, value, up)],
        [whole(shape) for shape in shapes],
        shapes,
        core,
        query,
        key,
        value,
        up,
    )


def lay_out_kernel(core_ref, near_ref, near_got_ref, out_ref, up_ref, up_got_ref, *refs):
    first_core = core_ref[0] == 0
    near, near_got, up, up_got = [
        ref[...] for ref in (near_ref, near_got_ref, up_ref, up_got_ref)
    ]
    out = out_ref[...]
    wide = out.shape[1] // 2
    near_rows = jnp.concatenate(
        [jnp.where(first_core, near, near_got), jnp.where(first_core, near_got, near)], axis=0
    )
    out_rows = jnp.concatenate([out[:, :wide], out[:, wide:]], axis=0)
    refs[0][...] = jnp.concatenate([near_rows, out_rows], axis=1)
    refs[1][...] = jnp.concatenate(
        [jnp.where(first_core, up, up_got), jnp.where(first_core, up_got, up)], axis=0
    )


def lay_out(core, near, near_got, out, up, up_got):
    rows = 2 * near.shape[0]
    shapes = [
        like((rows, near.shape[1] + out.shape[1] // 2), jnp.bfloat16),
        like((rows, up.shape[1]), jnp.bfloat16),
    ]
    arrays = (near, near_got, out, up, up_got)
    return call(
        lay_out_kernel,
        "lay_out",
        (1,),
        [whole(value) for value in arrays],
        [whole(shape) for shape in shapes],
        shapes,
        core,
        *arrays,
    )[0]


def split_body(
    tokens,
    lengths,
    cotangent,
    query_weight,
    key_weight,
    value_weight,
    out_weight,
    up_weight,
    down_weight,
    query_bias,
    value_bias,
    out_bias,
    attn_gain,
    attn_shift,
    up_bias,
    down_bias,
    feed_gain,
    feed_shift,
):
    core = lax.axis_index("c")
    half = lax.axis_index("s")
    row_count, width = tokens.shape[1:]
    slots = 2 * row_count
    unit_block = down_weight.shape[0]
    units = up_bias.shape[0] // 2
    cols = width // 2
    wide = cols // 2

    def to_sequence(values):
        return jnp.concatenate([pick(values, half, 0), swap(pick(values, 1 - half, 0), "s")], axis=0)

    def from_sequence(values):
        return in_order(values[:row_count], swap(values[row_count:], "s"), half)

    place = jnp.stack([core]).astype(jnp.int32)
    (near_kept, near_sent, up_kept, up_sent), place = deal(
        place, query_weight, key_weight, value_weight, up_weight, unit_block
    )
    near_mine, up_mine = lay_out(
        place, near_kept, swap(near_sent, "c"), out_weight, up_kept, swap(up_sent, "c")
    )
    rows, up_cols = up_mine.shape
    line = lax.axis_index("z")
    length_own = lax.dynamic_slice_in_dim(lengths, half, 1, 0)
    facts = jnp.concatenate(
        [
            both(length_own, "c"),
            jnp.stack(
                [
                    half * row_count,
                    half,
                    lax.axis_index("x"),
                    jnp.int32(0),
                    line // 2,
                    line % 2,
                ]
            ).astype(jnp.int32),
        ]
    )
    tokens_own = to_sequence(tokens)
    cotangent_own = to_sequence(cotangent)
    (near, up_mine, down_mine), facts = stack_pair(
        facts,
        near_mine,
        line_cross(near_mine),
        wait=(tokens_own,),
        through=(up_mine, down_weight),
    )
    near, facts = stack_line(facts, near, line_next(near), wait=(cotangent_own,))
    near_parts = gather_square(near, "x")
    up_pairs, facts = stack_pair(facts, up_mine, line_cross(up_mine), wait=(near,))
    tokens_both = both(tokens_own, "c")
    up_part, facts = stack_line(
        facts, up_pairs, line_next(up_pairs), wait=(near_parts[1], near_parts[2])
    )
    up_parts = gather_square(up_part, "s")
    down_pairs, facts = stack_pair(facts, down_mine, line_cross(down_mine), wait=(up_part,))
    def halves_of(vector, size):
        return pick(vector.reshape(-1, 2, size), core, 1).reshape(-1)

    query_part = halves_of(query_bias, HD).reshape(2, wide)
    value_part = halves_of(value_bias, HD).reshape(2, wide)
    in_bias = jnp.stack([query_part, jnp.zeros_like(query_part), value_part], axis=1).reshape(-1)
    (projected, in_weight, out_own), facts = project(
        facts, tokens_both, in_bias, near_parts, wait=(down_pairs,)
    )
    out_own = out_own.reshape(cols, width)
    out_other = swap(out_own, "c")
    down_part, facts = stack_line(facts, down_pairs, line_next(down_pairs), wait=(projected,))
    down_parts = gather_square(down_part, "x")
    (heads_out, totals), facts = attend(facts, projected, slots, wait=(up_parts[2],))
    heads_other = swap(heads_out[slots:], "c")
    vectors = jnp.stack(
        [out_bias, attn_gain, attn_shift, down_bias, feed_gain, feed_shift, out_bias, out_bias]
    )
    (first_hat, first_rstd, hidden_low, first_sums), facts = attend_out(
        facts,
        heads_out,
        heads_other,
        out_own,
        out_other,
        tokens_own,
        vectors,
        wait=(up_parts[1], down_parts[2]),
    )
    (hidden_low,), facts = gate(facts, (hidden_low,), (up_parts[3], down_parts[1]))
    hidden_from = swap(hidden_low, "c")
    (activation, slope, act_t, up_all), facts = feed_up(
        facts, hidden_low, hidden_from, halves_of(up_bias, unit_block), up_parts
    )
    hidden_turned, facts = turn(facts, hidden_low, hidden_from, rows, wait=(act_t,))
    (down_all, feed_sent), facts = feed_down(facts, activation, down_parts)
    down_all = down_all.reshape(units, width)
    feed_other = swap(feed_sent, "c")
    feed_part = product(activation[:slots], down_all, 1, 0)
    feed_vectors = jnp.stack(
        [down_bias, attn_gain, attn_shift, feed_gain, feed_shift, out_bias, out_bias, out_bias]
    )
    (mixed, second_grad, feed_low, second_sums), facts = second_norm(
        facts, feed_part, feed_other, first_hat, cotangent_own, feed_vectors
    )

    mixed_got = swap(mixed[row_count:], "s")

    feed_both = both(feed_low, "c")
    tokens_t, facts = turn_all(facts, tokens_both, wait=(feed_low,))
    feed_mine, feed_theirs = columns_of(feed_both, half), columns_of(feed_both, 1 - half)
    down_sent = grad_block(act_t, feed_theirs)
    down_got = swap(down_sent, "s")
    (pre_grad, up_bias_grad), facts = act_grad(
        facts, feed_both, down_all, slope, wait=(down_sent,)
    )
    hidden_sent = product(pre_grad[slots:], up_all, 1, 1).astype(jnp.bfloat16)
    hidden_other = swap(hidden_sent, "c")
    hidden_own_t, hidden_other_t = hidden_turned
    up_sent = grad_block(hidden_other_t, pre_grad)
    up_got = swap(up_sent, "x")
    hidden_part = product(pre_grad[:slots], up_all, 1, 1)
    (first_grad, attn_low, third_sums), facts = first_norm(
        facts,
        hidden_part,
        hidden_other,
        second_grad,
        first_hat,
        first_rstd,
        vectors,
        wait=(up_sent,),
    )
    grad_sent = product(attn_low, out_other, 1, 1).astype(jnp.bfloat16)
    grad_other = swap(grad_sent, "c")
    grad_own = product(attn_low, out_own, 1, 1).astype(jnp.bfloat16)
    out_sent = product(heads_other, attn_low, 0, 0).astype(jnp.bfloat16)
    out_got = swap(out_sent, "c")
    heads_grad = jnp.concatenate([grad_own, grad_other], axis=0)
    (theirs_low, theirs_sums), facts = attend_back(
        facts, projected, heads_grad, totals, slots, False, wait=(out_sent, mixed_got)
    )
    in_sent = grad_block(tokens_t, theirs_low)
    in_got = swap(in_sent, "s")
    down_total = grad_block(act_t, feed_mine, down_got)
    down_kept, down_sent = halve(down_total.reshape(4, 2, unit_block, cols), "x", 1)
    down_got = swap(down_sent, "x")
    out_grad = grad_block(heads_out[:slots].T, attn_low, out_got)
    out_line = out_grad.reshape((4, 2 * out_weight.shape[0], width))
    out_kept, out_sent = line_parts(out_line)
    out_got = lax.ppermute(out_sent, "z", NEXT)
    (mine_low, mine_sums), facts = attend_back(
        facts, projected, heads_grad, totals, slots, True, wait=(in_sent, out_sent, down_sent)
    )
    up_total = grad_block(hidden_own_t, pre_grad, up_got).reshape(4, rows, 2 * up_cols)
    up_kept, up_sent = columns_of(up_total, half), columns_of(up_total, 1 - half)
    up_got = swap(up_sent, "s")
    out_total = add(out_kept, out_got)
    valid_count = length_own[0].astype(jnp.float32) * width
    stats = jnp.stack(
        [jnp.sum(first_sums[0]), jnp.sum(first_sums[1]), jnp.sum(second_sums[3]), valid_count]
    )
    mine_sums, theirs_sums = jnp.sum(mine_sums, axis=(0, 1)), jnp.sum(theirs_sums, axis=(0, 1))
    late = in_order(mine_sums, theirs_sums, half)
    sums = jnp.concatenate(
        [
            second_sums[:3].reshape(-1),
            third_sums[:3].reshape(-1),
            jnp.pad(stats, (0, 124)),
            up_bias_grad[0],
            late[:, :wide].reshape(-1),
            late[:, 2 * wide :].reshape(-1),
        ]
    )
    sums = sums + lax.ppermute(sums, "z", NEXT)
    (tokens_part, tokens_sent), facts = tokens_grad(
        facts,
        mine_low,
        theirs_low,
        in_weight,
        wait=(up_sent, out_total, sums),
    )
    tokens_other = swap(tokens_sent, "c")
    in_total = grad_block(tokens_t, mine_low, in_got)
    in_kept, in_sent = halve(in_total.reshape(4, 2, rows, 3 * wide), "x", 1)
    in_got = swap(in_sent, "x")
    (down_pairs, down_next), facts = add_parts(
        facts, down_kept, down_got, wait=(in_sent, tokens_part)
    )
    down_got = lax.ppermute(down_next, "z", NEXT)
    (in_pairs, in_next, sums), facts = add_parts(
        facts, in_kept, in_got, wait=(down_next,), through=(sums,)
    )
    in_got = lax.ppermute(in_next, "z", NEXT)
    (down_kept, down_sent), facts = add_last(facts, down_pairs, down_got, wait=(in_next,))
    (up_pairs, up_next), facts = add_parts(facts, up_kept, up_got, wait=(down_sent,))
    up_got = lax.ppermute(up_next, "z", NEXT)
    sums = sums + swap(sums, "x")
    sums = sums + swap(sums, "s")
    (in_kept, in_sent, out_total), facts = add_last(
        facts, in_pairs, in_got, wait=(sums, up_next), through=(out_total,)
    )
    upper = lax.axis_index("z") // 2
    out_kept, out_sent = pick(out_total, upper, 0), pick(out_total, 1 - upper, 0)
    out_kept = add(out_kept, lax.ppermute(out_sent, "z", CROSS))
    (up_kept, up_sent, sums), facts = add_last(
        facts, up_pairs, up_got, wait=(in_sent,), through=(sums,)
    )
    in_sum = add(in_kept, lax.ppermute(in_sent, "z", CROSS))
    tokens_grad_sum = tokens_part + tokens_other.astype(jnp.float32) + first_grad
    tokens_grad_sum = from_sequence(tokens_grad_sum.astype(jnp.bfloat16))
    mixed = in_order(mixed[:row_count], mixed_got, half)
    down_sum = add(down_kept, lax.ppermute(down_sent, "z", CROSS))
    up_sum = add(up_kept, lax.ppermute(up_sent, "z", CROSS))
    out_sum = fold_columns(fold(out_kept.reshape(2, out_weight.shape[0], width), "x", 0))

    sums = sums + lax.ppermute(sums, "z", CROSS)
    both_sums = in_order(sums, swap(sums, "c"), core)
    count = 6 * width + 128
    shared = both_sums[0, :count] + both_sums[1, :count]
    down_bias_grad, feed_gain_grad, feed_shift_grad, out_bias_grad, attn_gain_grad, attn_shift_grad = [
        shared[i * width : (i + 1) * width] for i in range(6)
    ]
    stats = shared[6 * width : 6 * width + 4]

    def interleave(start, size, block_size):
        sums = both_sums[:, start : start + size].reshape(2, -1, block_size)
        return sums.transpose(1, 0, 2).reshape(-1)

    up_bias_grad = interleave(count, units, unit_block)
    query_bias_grad = interleave(count + units, cols, HD)
    value_bias_gradient = interleave(count + units + cols, cols, HD)
    stream_rms = jnp.sqrt(stats[:3] / stats[3])

    def give_back(total):
        total = total.reshape((2, rows // 2) + total.shape[1:])
        return pick(total, core, 0), swap(pick(total, 1 - core, 0), "c")

    up_shares = give_back(up_sum)
    in_shares = give_back(in_sum)
    down_weight_grad = down_sum.astype(jnp.float32)
    out_weight_grad = out_sum.astype(jnp.float32)

    def merge(shares, start, size, block):
        one, two = [
            share[:, start : start + size].reshape(rows // 2, -1, block) for share in shares
        ]
        first = jnp.where(core == 0, one, two)
        second = jnp.where(core == 0, two, one)
        return jnp.stack([first, second], axis=2).reshape(rows // 2, -1).astype(jnp.float32)

    query_weight_grad = merge(in_shares, 0, wide, HD)
    key_weight_grad = merge(in_shares, wide, wide, HD)
    value_weight_grad = merge(in_shares, 2 * wide, wide, HD)
    up_weight_grad = merge(up_shares, 0, up_cols, unit_block)
    return (
        mixed,
        tokens_grad_sum,
        query_weight_grad,
        key_weight_grad,
        value_weight_grad,
        out_weight_grad,
        up_weight_grad,
        down_weight_grad,
        query_bias_grad,
        value_bias_gradient,
        out_bias_grad,
        attn_gain_grad,
        attn_shift_grad,
        up_bias_grad,
        down_bias_grad,
        feed_gain_grad,
        feed_shift_grad,
        stream_rms,
    )


def solution(mesh):
    devices = mesh.devices
    dp_count, seq_count = devices.shape
    split = seq_count == 2 and dp_count == 16
    if split:
        inner = jax.sharding.Mesh(devices.reshape(4, 2, 2, seq_count), ("z", "x", "c", "s"))
        dp, seq, body = ("z", "x", "c"), "s", split_body
    else:
        inner, dp, seq, body = mesh, "dp", "seq", general_body
    weights = (P(dp, seq),) * 6
    vectors = (P(),) * 9
    rows = P(dp, seq, None)
    in_specs = (rows, P(dp), rows) + weights + vectors
    out_specs = (rows, rows) + weights + vectors + (P(),)
    return jax.shard_map(body, mesh=inner, in_specs=in_specs, out_specs=out_specs, check_vma=False)
```

```python
from functools import partial
import math

import jax
import jax.numpy as jnp
from jax import lax
from jax.experimental import pallas as pl
from jax.experimental.pallas import tpu as pltpu
from jax.sharding import PartitionSpec as P

HD = 64


def layer_norm(values_in, gain_vector, shift_vector):
    mean_value = jnp.mean(values_in, axis=-1, keepdims=True)
    centered = values_in - mean_value
    variance = jnp.mean(centered * centered, axis=-1, keepdims=True)
    return centered * lax.rsqrt(variance + 1e-05) * gain_vector + shift_vector


def gather_weights(first, second, third, fourth, fifth, sixth):
    part = (
        lax.all_gather(first, "dp", axis=0, tiled=True),
        lax.all_gather(second, "dp", axis=0, tiled=True),
        lax.all_gather(third, "dp", axis=0, tiled=True),
        lax.all_gather(fourth, "dp", axis=0, tiled=True),
        lax.all_gather(fifth, "dp", axis=0, tiled=True),
        lax.all_gather(sixth, "dp", axis=0, tiled=True),
    )
    return (
        lax.all_gather(part[0], "seq", axis=1, tiled=True),
        lax.all_gather(part[1], "seq", axis=1, tiled=True),
        lax.all_gather(part[2], "seq", axis=1, tiled=True),
        lax.all_gather(part[3], "seq", axis=1, tiled=True),
        lax.all_gather(part[4], "seq", axis=1, tiled=True),
        lax.all_gather(part[5], "seq", axis=1, tiled=True),
    )


def reduce_grads(first, second, third, fourth, fifth, sixth):
    part = (
        lax.psum_scatter(first.astype(jnp.bfloat16), "seq", scatter_dimension=1, tiled=True).astype(
            jnp.float32
        ),
        lax.psum_scatter(
            second.astype(jnp.bfloat16), "seq", scatter_dimension=1, tiled=True
        ).astype(jnp.float32),
        lax.psum_scatter(third.astype(jnp.bfloat16), "seq", scatter_dimension=1, tiled=True).astype(
            jnp.float32
        ),
        lax.psum_scatter(
            fourth.astype(jnp.bfloat16), "seq", scatter_dimension=1, tiled=True
        ).astype(jnp.float32),
        lax.psum_scatter(fifth.astype(jnp.bfloat16), "seq", scatter_dimension=1, tiled=True).astype(
            jnp.float32
        ),
        lax.psum_scatter(sixth.astype(jnp.bfloat16), "seq", scatter_dimension=1, tiled=True).astype(
            jnp.float32
        ),
    )
    return (
        lax.psum_scatter(
            part[0].astype(jnp.bfloat16), "dp", scatter_dimension=0, tiled=True
        ).astype(jnp.float32),
        lax.psum_scatter(
            part[1].astype(jnp.bfloat16), "dp", scatter_dimension=0, tiled=True
        ).astype(jnp.float32),
        lax.psum_scatter(
            part[2].astype(jnp.bfloat16), "dp", scatter_dimension=0, tiled=True
        ).astype(jnp.float32),
        lax.psum_scatter(
            part[3].astype(jnp.bfloat16), "dp", scatter_dimension=0, tiled=True
        ).astype(jnp.float32),
        lax.psum_scatter(
            part[4].astype(jnp.bfloat16), "dp", scatter_dimension=0, tiled=True
        ).astype(jnp.float32),
        lax.psum_scatter(
            part[5].astype(jnp.bfloat16), "dp", scatter_dimension=0, tiled=True
        ).astype(jnp.float32),
    )


def block_layout(seq_count, row_count, head_count):
    block_seqs = math.gcd(seq_count, max(1, 512 // row_count))
    group_heads = math.gcd(head_count, 4)
    return (block_seqs, seq_count // block_seqs, group_heads, head_count // group_heads)


def head_slice(block_part, offset, group_width, group_heads):
    sliced = lax.dynamic_slice_in_dim(block_part, offset, group_width, 2)
    return sliced.reshape(sliced.shape[0], sliced.shape[1], group_heads, HD)


def attention_forward(queries, key_all, value_all, key_mask):
    seq_count, row_count, feature_total = queries.shape
    slot_count = key_all.shape[1]
    block_seqs, block_count, group_heads, group_count = block_layout(
        seq_count, row_count, feature_total // HD
    )
    group_width = group_heads * HD

    def seq_block(inputs):
        query_part, key_part, value_part, mask_part = inputs

        def head_block(group_index):
            offset = group_index * group_width
            query_heads = head_slice(query_part, offset, group_width, group_heads)
            key_heads = head_slice(key_part, offset, group_width, group_heads)
            value_heads = head_slice(value_part, offset, group_width, group_heads)
            scores = (
                jnp.einsum(
                    "brhd,bkhd->bhrk", query_heads, key_heads, preferred_element_type=jnp.float32
                )
                * 0.125
            )
            scores = jnp.where(mask_part[:, None, None, :], scores, -1e30)
            row_max = jnp.max(scores, axis=-1, keepdims=True)
            exponent = jnp.exp(scores - row_max)
            row_total = jnp.sum(exponent, axis=-1, keepdims=True)
            soft_probs = (exponent / row_total).astype(jnp.bfloat16)
            heads_out = jnp.einsum(
                "bhrk,bkhd->brhd", soft_probs, value_heads, preferred_element_type=jnp.float32
            )
            log_total = (row_max + jnp.log(row_total))[..., 0]
            return (heads_out.reshape(block_seqs, row_count, group_width), log_total)

        return lax.map(head_block, jnp.arange(group_count))

    outputs, log_totals = lax.map(
        seq_block,
        (
            queries.reshape(block_count, block_seqs, row_count, feature_total),
            key_all.reshape(block_count, block_seqs, slot_count, feature_total),
            value_all.reshape(block_count, block_seqs, slot_count, feature_total),
            key_mask.reshape(block_count, block_seqs, slot_count),
        ),
    )
    mixed_heads = outputs.transpose(0, 2, 3, 1, 4).reshape(seq_count, row_count, feature_total)
    return (mixed_heads, log_totals)


def attention_backward(queries, key_all, value_all, key_mask, heads_grad, log_totals):
    seq_count, row_count, feature_total = queries.shape
    slot_count = key_all.shape[1]
    block_seqs, block_count, group_heads, group_count = block_layout(
        seq_count, row_count, feature_total // HD
    )
    group_width = group_heads * HD

    def seq_block(inputs):
        query_part, key_part, value_part, mask_part, grad_part, total_part = inputs

        def head_block(group_index):
            offset = group_index * group_width
            query_heads = head_slice(query_part, offset, group_width, group_heads)
            key_heads = head_slice(key_part, offset, group_width, group_heads)
            value_heads = head_slice(value_part, offset, group_width, group_heads)
            grad_heads = head_slice(grad_part, offset, group_width, group_heads)
            log_total = lax.dynamic_index_in_dim(total_part, group_index, 0, keepdims=False)
            scores = (
                jnp.einsum(
                    "brhd,bkhd->bhrk", query_heads, key_heads, preferred_element_type=jnp.float32
                )
                * 0.125
            )
            scores = jnp.where(mask_part[:, None, None, :], scores, -1e30)
            soft_probs = jnp.exp(scores - log_total[..., None])
            value_grad = jnp.einsum(
                "bhrk,brhd->bkhd",
                soft_probs.astype(jnp.bfloat16),
                grad_heads,
                preferred_element_type=jnp.float32,
            )
            prob_grad = jnp.einsum(
                "brhd,bkhd->bhrk", grad_heads, value_heads, preferred_element_type=jnp.float32
            )
            inner = jnp.sum(soft_probs * prob_grad, axis=-1, keepdims=True)
            score_grad = (soft_probs * (prob_grad - inner)).astype(jnp.bfloat16)
            query_grad = (
                jnp.einsum(
                    "bhrk,bkhd->brhd", score_grad, key_heads, preferred_element_type=jnp.float32
                )
                * 0.125
            )
            key_grad = (
                jnp.einsum(
                    "bhrk,brhd->bkhd", score_grad, query_heads, preferred_element_type=jnp.float32
                )
                * 0.125
            )
            return (
                query_grad.reshape(block_seqs, row_count, group_width),
                key_grad.reshape(block_seqs, slot_count, group_width),
                value_grad.reshape(block_seqs, slot_count, group_width),
            )

        return lax.map(head_block, jnp.arange(group_count))

    query_blocks, key_blocks, value_block_list = lax.map(
        seq_block,
        (
            queries.reshape(block_count, block_seqs, row_count, feature_total),
            key_all.reshape(block_count, block_seqs, slot_count, feature_total),
            value_all.reshape(block_count, block_seqs, slot_count, feature_total),
            key_mask.reshape(block_count, block_seqs, slot_count),
            heads_grad.reshape(block_count, block_seqs, row_count, feature_total),
            log_totals,
        ),
    )
    query_grad = query_blocks.transpose(0, 2, 3, 1, 4).reshape(seq_count, row_count, feature_total)
    key_grad = key_blocks.transpose(0, 2, 3, 1, 4).reshape(seq_count, slot_count, feature_total)
    value_grad = value_block_list.transpose(0, 2, 3, 1, 4).reshape(
        seq_count, slot_count, feature_total
    )
    return (query_grad, key_grad, value_grad)


def general_body(
    tokens,
    lengths,
    cotangent,
    query_weight,
    key_weight,
    value_weight,
    out_weight,
    up_weight,
    down_weight,
    query_bias,
    value_bias,
    out_bias,
    attn_gain,
    attn_shift,
    up_bias,
    down_bias,
    feed_gain,
    feed_shift,
):
    seq_count, row_count, feature_total = tokens.shape
    slot_count = row_count * lax.axis_size("seq")
    token_count = seq_count * row_count
    whole = gather_weights(
        query_weight, key_weight, value_weight, out_weight, up_weight, down_weight
    )
    full_query, full_key, full_value, full_out, full_up, full_down = whole
    flat_tokens = tokens.reshape(token_count, feature_total)
    queries = (
        jnp.dot(flat_tokens, full_query, preferred_element_type=jnp.float32) + query_bias
    ).astype(jnp.bfloat16)
    key_rows = jnp.dot(flat_tokens, full_key, preferred_element_type=jnp.float32).astype(
        jnp.bfloat16
    )
    value_rows = (
        jnp.dot(flat_tokens, full_value, preferred_element_type=jnp.float32) + value_bias
    ).astype(jnp.bfloat16)
    first_slot = lax.axis_index("seq") * row_count
    key_mask = jnp.arange(slot_count)[None, :] < lengths[:, None]
    row_valid = ((first_slot + jnp.arange(row_count))[None, :] < lengths[:, None]).astype(
        jnp.float32
    )
    row_valid = row_valid.reshape(token_count, 1)
    query_blocks = queries.reshape(seq_count, row_count, feature_total)
    key_blocks = key_rows.reshape(seq_count, row_count, feature_total)
    value_block_list = value_rows.reshape(seq_count, row_count, feature_total)
    key_all, value_all = (
        lax.all_gather(key_blocks, "seq", axis=1, tiled=True),
        lax.all_gather(value_block_list, "seq", axis=1, tiled=True),
    )
    mixed_heads, log_totals = attention_forward(query_blocks, key_all, value_all, key_mask)
    heads_low = mixed_heads.reshape(token_count, feature_total).astype(jnp.bfloat16)
    attention_out = jnp.dot(heads_low, full_out, preferred_element_type=jnp.float32) + out_bias
    tokens_f32 = flat_tokens.astype(jnp.float32)
    first_sum = tokens_f32 + attention_out
    hidden, first_pull = jax.vjp(layer_norm, first_sum, attn_gain, attn_shift)
    hidden_low = hidden.astype(jnp.bfloat16)
    pre_act = jnp.dot(hidden_low, full_up, preferred_element_type=jnp.float32) + up_bias
    gelu_out, gelu_pull = jax.vjp(partial(jax.nn.gelu, approximate=False), pre_act)
    activation = gelu_out.astype(jnp.bfloat16)
    feed_out = jnp.dot(activation, full_down, preferred_element_type=jnp.float32) + down_bias
    result, second_pull = jax.vjp(layer_norm, hidden + feed_out, feed_gain, feed_shift)
    mixed = result.astype(jnp.bfloat16).reshape(seq_count, row_count, feature_total)
    partial_stats = jnp.stack(
        [
            jnp.sum(row_valid * tokens_f32 * tokens_f32),
            jnp.sum(row_valid * attention_out * attention_out),
            jnp.sum(row_valid * feed_out * feed_out),
            jnp.sum(row_valid) * feature_total,
        ]
    )
    back_weights = gather_weights(
        query_weight, key_weight, value_weight, out_weight, up_weight, down_weight
    )
    back_query, back_key, back_value, back_out, back_up, back_down = back_weights
    out_grad = cotangent.reshape(token_count, feature_total).astype(jnp.float32) * row_valid
    second_grad, feed_gain_grad, feed_shift_grad = second_pull(out_grad)
    feed_low = second_grad.astype(jnp.bfloat16)
    down_weight_grad = jnp.einsum(
        "nf,nd->fd", activation, feed_low, preferred_element_type=jnp.float32
    )
    down_bias_grad = jnp.sum(feed_low, axis=0, dtype=jnp.float32)
    act_grad = jnp.einsum(
        "nd,fd->nf", feed_low, back_down, preferred_element_type=jnp.float32
    ).astype(jnp.bfloat16)
    pre_grad = gelu_pull(act_grad.astype(jnp.float32))[0].astype(jnp.bfloat16)
    up_weight_grad = jnp.einsum(
        "nd,nf->df", hidden_low, pre_grad, preferred_element_type=jnp.float32
    )
    up_bias_grad = jnp.sum(pre_grad, axis=0, dtype=jnp.float32)
    hidden_grad = (
        jnp.einsum("nf,df->nd", pre_grad, back_up, preferred_element_type=jnp.float32) + second_grad
    )
    first_grad, attn_gain_grad, attn_shift_grad = first_pull(hidden_grad)
    attn_low = first_grad.astype(jnp.bfloat16)
    out_weight_grad = jnp.einsum(
        "nd,ne->de", heads_low, attn_low, preferred_element_type=jnp.float32
    )
    out_bias_grad = jnp.sum(attn_low, axis=0, dtype=jnp.float32)
    heads_grad = jnp.einsum(
        "ne,de->nd", attn_low, back_out, preferred_element_type=jnp.float32
    ).astype(jnp.bfloat16)
    heads_grad = heads_grad.reshape(seq_count, row_count, feature_total)
    query_grad, key_part_grad, value_part_grad = attention_backward(
        query_blocks, key_all, value_all, key_mask, heads_grad, log_totals
    )
    key_sum, value_sum = (
        lax.psum_scatter(
            key_part_grad.astype(jnp.bfloat16), "seq", scatter_dimension=1, tiled=True
        ).astype(jnp.float32),
        lax.psum_scatter(
            value_part_grad.astype(jnp.bfloat16), "seq", scatter_dimension=1, tiled=True
        ).astype(jnp.float32),
    )
    query_low = query_grad.reshape(token_count, feature_total).astype(jnp.bfloat16)
    key_low = key_sum.reshape(token_count, feature_total).astype(jnp.bfloat16)
    value_low = value_sum.reshape(token_count, feature_total).astype(jnp.bfloat16)
    query_weight_grad = jnp.einsum(
        "nd,ne->de", flat_tokens, query_low, preferred_element_type=jnp.float32
    )
    key_weight_grad = jnp.einsum(
        "nd,ne->de", flat_tokens, key_low, preferred_element_type=jnp.float32
    )
    value_weight_grad = jnp.einsum(
        "nd,ne->de", flat_tokens, value_low, preferred_element_type=jnp.float32
    )
    query_bias_grad = jnp.sum(query_low, axis=0, dtype=jnp.float32)
    value_bias_gradient = jnp.sum(value_low, axis=0, dtype=jnp.float32)
    tokens_grad = (
        jnp.einsum("ne,de->nd", query_low, back_query, preferred_element_type=jnp.float32)
        + jnp.einsum("ne,de->nd", key_low, back_key, preferred_element_type=jnp.float32)
        + jnp.einsum("ne,de->nd", value_low, back_value, preferred_element_type=jnp.float32)
        + first_grad
    )
    tokens_grad = tokens_grad.astype(jnp.bfloat16).reshape(seq_count, row_count, feature_total)
    matrix_grads = reduce_grads(
        query_weight_grad,
        key_weight_grad,
        value_weight_grad,
        out_weight_grad,
        up_weight_grad,
        down_weight_grad,
    )
    totals = lax.psum(
        (
            partial_stats,
            query_bias_grad,
            value_bias_gradient,
            out_bias_grad,
            attn_gain_grad,
            attn_shift_grad,
            up_bias_grad,
            down_bias_grad,
            feed_gain_grad,
            feed_shift_grad,
        ),
        ("dp", "seq"),
    )
    stream_rms = jnp.sqrt(totals[0][:3] / totals[0][3])
    return (
        mixed,
        tokens_grad,
        matrix_grads[0],
        matrix_grads[1],
        matrix_grads[2],
        matrix_grads[3],
        matrix_grads[4],
        matrix_grads[5],
        totals[1],
        totals[2],
        totals[3],
        totals[4],
        totals[5],
        totals[6],
        totals[7],
        totals[8],
        totals[9],
        stream_rms,
    )


def swap(value, axis):
    return lax.ppermute(value, axis, [(0, 1), (1, 0)])


def both(value, axis):
    return jnp.concatenate([value, swap(value, axis)], axis=0)


def in_order(own, other, index, axis=0):
    return jnp.where(
        index == 0, jnp.stack([own, other], axis=axis), jnp.stack([other, own], axis=axis)
    )


def pick(values, index, axis):
    return lax.dynamic_index_in_dim(values, index, axis, keepdims=False)


def add(left, right):
    return (left.astype(jnp.float32) + right.astype(jnp.float32)).astype(jnp.bfloat16)


def fold(values, axis, dim):
    index = lax.axis_index(axis)
    return add(pick(values, index, dim), swap(pick(values, 1 - index, dim), axis))


NEXT = [(0, 1), (1, 0), (2, 3), (3, 2)]
CROSS = [(0, 2), (2, 0), (1, 3), (3, 1)]


def fold_cross(pairs):
    upper = lax.axis_index("z") // 2
    return add(pick(pairs, upper, 0), lax.ppermute(pick(pairs, 1 - upper, 0), "z", CROSS))


def fold_line(values):
    odd = lax.axis_index("z") % 2
    pairs = values.reshape((2, 2) + values.shape[1:])
    sent = lax.ppermute(pick(pairs, 1 - odd, 1), "z", NEXT)
    return fold_cross(add(pick(pairs, odd, 1), sent))


def line_cross(value):
    return lax.ppermute(value, "z", CROSS)


def line_next(pair):
    return lax.ppermute(pair, "z", NEXT)


def gather_square(own, way):
    beside, below = swap(own, "x"), swap(own, "s")
    across = swap(below, "x") if way == "x" else swap(beside, "s")
    return [own, beside, below, across]


def fold_columns(total):
    half = lax.axis_index("s")
    return add(columns_of(total, half), swap(columns_of(total, 1 - half), "s"))


def halve(values, axis, dim):
    index = lax.axis_index(axis) % 2
    return pick(values, index, dim), pick(values, 1 - index, dim)


def line_parts(values):
    return halve(values.reshape((2, 2) + values.shape[1:]), "z", 1)


def scatter_top(send, keep):
    total = add(keep, swap(send, "s"))
    total = total.reshape((4, 2) + total.shape[1:])
    return fold_line(fold(total, "x", 1))


def grad_block(left_t, right, got=None):
    total = product(left_t, right, 1, 0)
    if got is not None:
        total = total + got.astype(jnp.float32)
    return total.astype(jnp.bfloat16)


def columns_of(right, index):
    columns = right.shape[-1] // 2
    return lax.dynamic_slice_in_dim(right, index * columns, columns, right.ndim - 1)


PAIR = 2 * HD
LIMIT = 10 * 1024 * 1024


def kernel_params(steps):
    return pltpu.CompilerParams(
        dimension_semantics=("arbitrary",) * steps, vmem_limit_bytes=LIMIT
    )


def product(left, right, left_dim, right_dim):
    return lax.dot_general(
        left, right, (((left_dim,), (right_dim,)), ((), ())), preferred_element_type=jnp.float32
    )


def key_bias(facts_ref, slots):
    place = lax.broadcasted_iota(jnp.int32, (slots, 1), 0) + facts_ref[2]
    place = jnp.where(place >= slots, place - slots, place)
    return jnp.where(place < facts_ref[pl.program_id(0)], 0.0, -1e30)


def head_lanes(value, head):
    lane = lax.broadcasted_iota(jnp.int32, value.shape, 1)
    return jnp.where((lane >= HD) == (head == 1), value, jnp.zeros_like(value))


def turned(value):
    return value.astype(jnp.float32).T


def attend_kernel(facts_ref, query_ref, key_ref, value_ref, out_ref, total_ref):
    slots = key_ref.shape[0]
    bias = key_bias(facts_ref, slots)
    query = query_ref[...] * jnp.bfloat16(0.125)
    key = key_ref[...]
    value_t = turned(value_ref[...]).astype(jnp.bfloat16)
    outs = []
    for head in range(2):
        scores = product(key, head_lanes(query, head), 1, 1) + bias
        peak = jnp.max(scores, axis=0, keepdims=True)
        weight = jnp.exp(scores - peak)
        total = jnp.sum(weight, axis=0, keepdims=True)
        part = product(value_t[head * HD : (head + 1) * HD], weight.astype(jnp.bfloat16), 1, 0)
        outs.append(part * (1.0 / total))
        total_ref[0, 0, head : head + 1, :] = peak + jnp.log(total)
    out_ref[...] = jnp.concatenate(outs, axis=0).T.astype(jnp.bfloat16)


def attend_back_kernel(
    facts_ref, query_ref, key_ref, value_ref, grad_ref, total_ref, low_ref, sums_ref
):
    slots = key_ref.shape[0]
    bias = key_bias(facts_ref, slots)
    query = query_ref[...] * jnp.bfloat16(0.125)
    key = key_ref[...]
    value = value_ref[...]
    grad = grad_ref[...]
    key_t = turned(key).astype(jnp.bfloat16)
    lane = lax.broadcasted_iota(jnp.int32, (slots, PAIR), 1)
    query_parts, key_parts, value_parts = [], [], []
    for head in range(2):
        scores = product(key, head_lanes(query, head), 1, 1) + bias
        soft = jnp.exp(scores - total_ref[0, 0, head : head + 1, :])
        value_parts.append(product(soft.astype(jnp.bfloat16), grad, 1, 0))
        change = product(value, head_lanes(grad, head), 1, 1)
        inner = jnp.sum(soft * change, axis=0, keepdims=True)
        change = (soft * (change - inner)).astype(jnp.bfloat16)
        key_parts.append(product(change, query, 1, 0))
        query_parts.append(product(key_t[head * HD : (head + 1) * HD], change, 1, 0))
    pair = pl.program_id(1)
    groups = low_ref.shape[1] // 3
    query_low = (jnp.concatenate(query_parts, axis=0) * 0.125).T
    key_low = jnp.where(lane < HD, key_parts[0], key_parts[1])
    value_low = jnp.where(lane < HD, value_parts[0], value_parts[1])
    for place, part in enumerate((query_low, key_low, value_low)):
        start = pl.multiple_of(place * groups + pair * PAIR, PAIR)
        low = part.astype(jnp.bfloat16)
        low_ref[:, pl.ds(start, PAIR)] = low
        sums_ref[0, :, pl.ds(start, PAIR)] = jnp.sum(
            low.astype(jnp.float32), axis=0, keepdims=True
        )


def attention_specs(slots, pairs):
    def at(part):
        return pl.BlockSpec(
            (slots, PAIR), lambda b, g, p, *_: (b, g * 3 * pairs + part * pairs + p)
        )

    heads = pl.BlockSpec((slots, PAIR), lambda b, g, p, *_: (b, g * pairs + p))
    totals = pl.BlockSpec((1, 1, 2, slots), lambda b, g, p, *_: (b, g * pairs + p, 0, 0))
    return [at(0), at(1), at(2)], heads, totals


def attend(facts, projected, slots, wait=()):
    pairs = projected.shape[1] // (6 * PAIR)
    inputs, heads, totals = attention_specs(slots, pairs)
    rows = projected.shape[0]
    return call(
        attend_kernel,
        "attend",
        (2, 2, pairs),
        inputs,
        [heads, totals],
        [
            like((rows, 2 * pairs * PAIR), jnp.bfloat16),
            like((2, 2 * pairs, 2, slots), jnp.float32),
        ],
        facts,
        projected,
        projected,
        projected,
        wait=wait,
    )


def attend_back(facts, projected, heads_grad, totals_in, slots, own, wait=(), through=()):
    pairs = projected.shape[1] // (6 * PAIR)

    def group(facts_ref):
        return facts_ref[3] if own else 1 - facts_ref[3]

    def at(part):
        return pl.BlockSpec(
            (slots, PAIR), lambda b, p, f: (b, group(f) * 3 * pairs + part * pairs + p)
        )

    heads = pl.BlockSpec((slots, PAIR), lambda b, p, f: (b, group(f) * pairs + p))
    totals = pl.BlockSpec((1, 1, 2, slots), lambda b, p, f: (b, group(f) * pairs + p, 0, 0))
    width = 3 * pairs * PAIR
    return call(
        attend_back_kernel,
        "attend_back",
        (2, pairs),
        [at(0), at(1), at(2), heads, totals],
        [
            pl.BlockSpec((slots, width), lambda b, p, f: (b, 0)),
            pl.BlockSpec((1, 1, width), lambda b, p, f: (b, 0, 0)),
        ],
        [
            like((2 * slots, width), jnp.bfloat16),
            like((2, 1, width), jnp.float32),
        ],
        facts,
        projected,
        projected,
        projected,
        heads_grad,
        totals_in,
        wait=wait,
        through=through,
    )


def call(kernel, name, grid, inputs, outputs, shapes, facts, *args, wait=(), scratch=(), through=(), into=()):
    single = not isinstance(outputs, list)
    outputs, shapes = ([outputs], [shapes]) if single else (outputs, shapes)
    wait = tuple(into) + tuple(wait)
    count, held, passed = len(args), len(wait) + len(through), len(through)
    last = count + held + len(outputs)

    def body(facts_ref, *refs):
        kernel(facts_ref, *refs[:count], *refs[count + held : last], *refs[last + passed + 1 :])
        for place in range(facts.shape[0]):
            refs[last + passed][place] = facts_ref[place]

    results = pl.pallas_call(
        body,
        grid_spec=pltpu.PrefetchScalarGridSpec(
            num_scalar_prefetch=1,
            grid=grid,
            in_specs=list(inputs) + [pl.BlockSpec(memory_space=pl.ANY)] * held,
            out_specs=list(outputs)
            + [pl.BlockSpec(memory_space=pl.ANY)] * passed
            + [pl.BlockSpec(memory_space=pltpu.SMEM)],
            scratch_shapes=list(scratch),
        ),
        out_shape=list(shapes)
        + [like(value.shape, value.dtype) for value in through]
        + [like(facts.shape, jnp.int32)],
        input_output_aliases={
            **{1 + count + i: i for i in range(len(into))},
            **{1 + count + len(wait) + i: len(outputs) + i for i in range(passed)},
        },
        compiler_params=kernel_params(len(grid)),
        name=name,
    )(facts, *args, *wait, *through)
    values = tuple(results[:-1])
    return (values[0] if single and not passed else values), results[-1]


def block(shape, *index):
    def at(*grid_and_facts):
        return tuple(entry(*grid_and_facts) if callable(entry) else entry for entry in index)

    return pl.BlockSpec(shape, at)


def whole(array):
    zeros = (0,) * array.ndim
    return pl.BlockSpec(array.shape, lambda *_: zeros)


def first(i, *_):
    return i


def like(shape, dtype):
    return jax.ShapeDtypeStruct(shape, dtype)


def rows_in_order(facts_ref, own, beside):
    even = facts_ref[4] == 0
    pieces = []
    for z in range(4):
        pieces += [jnp.where(even, own[z], beside[z]), jnp.where(even, beside[z], own[z])]
    return jnp.concatenate(pieces, axis=0)


def near_or_far(facts_ref, refs, near):
    own, beside, below, across = [ref[...] for ref in refs]
    return rows_in_order(
        facts_ref, jnp.where(near, own, below), jnp.where(near, beside, across)
    )


def square_columns(parts, wide, steps):
    shape = parts[0].shape[:2] + (wide,)
    near = block(shape, 0, 0, lambda i, *_: jnp.minimum(i, steps - 1))
    far = block(shape, 0, 0, lambda i, *_: jnp.maximum(i - steps, 0))
    return [near, near, far, far]


def half_at(i, facts, steps):
    return jnp.where(i < steps, facts[3], 1 - facts[3])


def gate_kernel(facts_ref):
    del facts_ref


def gate(facts, through, wait):
    return call(gate_kernel, "gate", (1,), [], [], [], facts, wait=wait, through=through)


def stack_kernel(own_at, facts_ref, own_ref, other_ref, out_ref):
    own = facts_ref[own_at] == pl.program_id(0)
    value = jnp.where(own, own_ref[...], other_ref[...])
    out_ref[...] = value.reshape(out_ref.shape)


def stack_pair(facts, own, other, wait=(), through=()):
    rows, columns = own.shape
    return call(
        partial(stack_kernel, 6),
        "stack",
        (2,),
        [whole(own), whole(other)],
        block((1, rows, columns), first, 0, 0),
        like((2, rows, columns), own.dtype),
        facts,
        own,
        other,
        wait=wait,
        through=through,
    )


def stack_line(facts, own, other, wait=()):
    _, rows, columns = own.shape
    line, facts = call(
        partial(stack_kernel, 7),
        "stack_line",
        (2,),
        [whole(own), whole(other)],
        block((2, 1, rows, columns), 0, first, 0, 0),
        like((2, 2, rows, columns), own.dtype),
        facts,
        own,
        other,
        wait=wait,
    )
    return line.reshape(4, rows, columns), facts


def turn_kernel(facts_ref, *refs):
    for i in range(2):
        refs[4 + i][...] = jnp.concatenate([refs[2 * i][...].T, refs[2 * i + 1][...].T], axis=1)


def turn_all_kernel(facts_ref, rows_ref, out_ref):
    out_ref[...] = rows_ref[...].T


def turn_all(facts, values, wait=()):
    count, width = values.shape
    step = width // 4
    return call(
        turn_all_kernel,
        "turn_all",
        (4,),
        [block((count, step), 0, first)],
        block((step, count), first, 0),
        like((width, count), values.dtype),
        facts,
        values,
        wait=wait,
    )


def turn(facts, values, others, rows, wait=()):
    count, width = values.shape
    half = width // 2
    out = block((rows, 2 * count), first, 0)
    shape = like((half, 2 * count), values.dtype)
    own = block((count, rows), 0, lambda i, f: 2 * i + f[4])
    other = block((count, rows), 0, lambda i, f: 2 * i + 1 - f[4])
    return call(
        turn_kernel,
        "turn",
        (half // rows,),
        [own, own, other, other],
        [out, out],
        [shape, shape],
        facts,
        values,
        others,
        values,
        others,
        wait=wait,
    )


def project_kernel(facts_ref, rows_ref, bias_ref, *refs):
    parts, (out_ref, in_ref, rest_ref) = refs[:4], refs[4:]
    step = pl.program_id(0)
    weight = near_or_far(facts_ref, parts, step < 4)

    @pl.when(step % 4 < 3)
    def _():
        in_ref[...] = weight
        value = product(rows_ref[...], weight, 1, 0) + bias_ref[...]
        out_ref[...] = value.astype(jnp.bfloat16)

    @pl.when(step % 4 == 3)
    def _():
        chips, count, wide = rest_ref.shape
        pairs = weight.reshape(chips, 2, count, wide // 2)
        rest_ref[...] = jnp.concatenate([pairs[:, 0], pairs[:, 1]], axis=2)


def project(facts, rows, bias, parts, wait=()):
    count, width = rows.shape
    wide = parts[0].shape[2] // 4

    def column(i, f):
        return half_at(i, f, 4) * 3 + jnp.minimum(i % 4, 2)

    out = block((count, wide), 0, column)
    rest = (8, parts[0].shape[1] // 2, 2 * wide)
    return call(
        project_kernel,
        "project",
        (8,),
        [whole(rows), block((1, wide), 0, column)] + square_columns(parts, wide, 4),
        [out, block((width, wide), 0, column), block(rest, 0, 0, lambda i, f: half_at(i, f, 4))],
        [
            like((count, 6 * wide), jnp.bfloat16),
            like((width, 6 * wide), jnp.bfloat16),
            like(rest[:2] + (4 * wide,), jnp.bfloat16),
        ],
        facts,
        rows,
        bias[None],
        *parts,
        wait=wait,
    )


def valid_rows(facts_ref, count, slots):
    place = lax.broadcasted_iota(jnp.int32, (count, 1), 0) + pl.program_id(0) * count + facts_ref[2]
    place = jnp.where(place >= slots, place - slots, place)
    return (place < facts_ref[0]).astype(jnp.float32)


def add_rows(sums_ref, rows):
    total = jnp.concatenate([jnp.sum(part, axis=0, keepdims=True) for part in rows], axis=0)
    total = jnp.concatenate([total, jnp.zeros((8 - len(rows), total.shape[1]), jnp.float32)], axis=0)

    @pl.when(pl.program_id(0) == 0)
    def _():
        sums_ref[...] = total

    @pl.when(pl.program_id(0) > 0)
    def _():
        sums_ref[...] += total


def mean_of(values):
    return jnp.mean(values, axis=-1, keepdims=True)


def attend_out_kernel(
    slots, facts_ref, own_ref, other_ref, own_weight_ref, other_weight_ref, tokens_ref, vectors_ref,
    hat_ref, rstd_ref, low_ref, sums_ref,
):
    branch = (
        product(own_ref[...], own_weight_ref[...], 1, 0)
        + product(other_ref[...], other_weight_ref[...], 1, 0)
        + vectors_ref[0:1]
    )
    tokens = tokens_ref[...].astype(jnp.float32)
    total = tokens + branch
    centered = total - mean_of(total)
    rstd = lax.rsqrt(mean_of(centered * centered) + 1e-05)
    hat = centered * rstd
    hat_ref[...] = hat
    rstd_ref[...] = rstd
    low_ref[...] = (hat * vectors_ref[1:2] + vectors_ref[2:3]).astype(jnp.bfloat16)
    valid = valid_rows(facts_ref, tokens.shape[0], slots)
    add_rows(sums_ref, [valid * tokens * tokens, valid * branch * branch])


def attend_out(facts, own, other, own_weight, other_weight, tokens, vectors, wait=()):
    slots, width = tokens.shape
    step = slots // 4
    rows = lambda array: block((step, array.shape[1]), first, 0)
    return call(
        partial(attend_out_kernel, slots),
        "attend_out",
        (4,),
        [rows(own), rows(other), whole(own_weight), whole(other_weight), rows(tokens), whole(vectors)],
        [block((step, width), first, 0), block((step, 1), first, 0), block((step, width), first, 0), block((8, width), 0, 0)],
        [
            like((slots, width), jnp.float32),
            like((slots, 1), jnp.float32),
            like((slots, width), jnp.bfloat16),
            like((8, width), jnp.float32),
        ],
        facts,
        own,
        other,
        own_weight,
        other_weight,
        tokens,
        vectors,
        wait=wait,
    )


def up_kernel(facts_ref, rows_ref, others_ref, bias_ref, *refs):
    parts, (act_ref, slope_ref, turned_ref, weight_ref) = refs[:4], refs[4:]
    weight = near_or_far(facts_ref, parts, pl.program_id(0) < 4)
    weight_ref[...] = weight
    pre_act = [product(ref[...], weight, 1, 0) for ref in (rows_ref, others_ref)]
    pre_act = jnp.concatenate(pre_act, axis=0) + bias_ref[...]
    below = 0.5 + 0.5 * lax.erf(pre_act * 0.7071067811865476)
    act = (pre_act * below).astype(jnp.bfloat16)
    act_ref[...] = act
    turned_ref[...] = act.T
    slope = below + pre_act * (0.3989422804014327 * jnp.exp(-0.5 * pre_act * pre_act))
    slope_ref[...] = slope.astype(jnp.bfloat16)


def feed_up(facts, rows, others, bias, parts, wait=()):
    count, width = 2 * rows.shape[0], rows.shape[1]
    units = bias.shape[0]
    wide = units // 8

    def column(i, f):
        return half_at(i, f, 4) * 4 + i % 4

    shape = like((count, units), jnp.bfloat16)
    out = block((count, wide), 0, column)
    return call(
        up_kernel,
        "feed_up",
        (8,),
        [whole(rows), whole(others), block((1, wide), 0, column)] + square_columns(parts, wide, 4),
        [out, out, block((wide, count), column, 0), block((width, wide), 0, column)],
        [
            shape,
            shape,
            like((units, count), jnp.bfloat16),
            like((width, units), jnp.bfloat16),
        ],
        facts,
        rows,
        others,
        bias[None],
        *parts,
        wait=wait,
    )


def down_kernel(facts_ref, rows_ref, *refs):
    parts, (weight_ref, out_ref, total_ref) = refs[:4], refs[4:]
    step = pl.program_id(0)
    own, beside, below, across = [ref[0] for ref in parts]
    even, left = facts_ref[4] == 0, facts_ref[3] == 0
    for x in range(2):
        mine = jnp.where(even, own, beside) if x == 0 else jnp.where(even, beside, own)
        theirs = jnp.where(even, below, across) if x == 0 else jnp.where(even, across, below)
        weight_ref[x] = jnp.concatenate(
            [jnp.where(left, mine, theirs), jnp.where(left, theirs, mine)], axis=1
        )
    weight = weight_ref[...].reshape(rows_ref.shape[1], out_ref.shape[1])
    value = product(rows_ref[...], weight, 1, 0)

    @pl.when(step == 0)
    def _():
        total_ref[...] = value

    @pl.when(step > 0)
    def _():
        total_ref[...] += value

    @pl.when(step == 3)
    def _():
        out_ref[...] = total_ref[...].astype(jnp.bfloat16)


def feed_down(facts, rows, parts, wait=()):
    count, units = rows.shape
    _, block_rows, half_width = parts[0].shape
    width = 2 * half_width
    shape = (1,) + parts[0].shape[1:]
    return call(
        down_kernel,
        "feed_down",
        (4,),
        [block((count // 2, units // 4), 1, first)] + [block(shape, first, 0, 0)] * 4,
        [block((2, block_rows, width), first, 0, 0), block((count // 2, width), 0, 0)],
        [like((8, block_rows, width), jnp.bfloat16), like((count // 2, width), jnp.bfloat16)],
        facts,
        rows,
        *parts,
        scratch=[pltpu.VMEM((count // 2, width), jnp.float32)],
        wait=wait,
    )


def second_norm_kernel(
    slots, facts_ref, part_ref, other_ref, hat_ref, cotangent_ref, vectors_ref,
    mixed_ref, grad_ref, low_ref, sums_ref,
):
    branch = part_ref[...] + other_ref[...].astype(jnp.float32) + vectors_ref[0:1]
    hidden = hat_ref[...] * vectors_ref[1:2] + vectors_ref[2:3]
    gain = vectors_ref[3:4]
    total = hidden + branch
    centered = total - mean_of(total)
    rstd = lax.rsqrt(mean_of(centered * centered) + 1e-05)
    hat = centered * rstd
    mixed_ref[...] = (hat * gain + vectors_ref[4:5]).astype(jnp.bfloat16)
    valid = valid_rows(facts_ref, branch.shape[0], slots)
    grad = cotangent_ref[...].astype(jnp.float32) * valid
    scaled = grad * gain
    result = rstd * (scaled - mean_of(scaled) - hat * mean_of(scaled * hat))
    low = result.astype(jnp.bfloat16)
    grad_ref[...] = result
    low_ref[...] = low
    add_rows(sums_ref, [low.astype(jnp.float32), grad * hat, grad, valid * branch * branch])


def second_norm(facts, part, other, hat, cotangent, vectors, wait=()):
    slots, width = part.shape
    step = slots // 4
    rows = block((step, width), first, 0)
    return call(
        partial(second_norm_kernel, slots),
        "second_norm",
        (4,),
        [rows, rows, rows, rows, whole(vectors)],
        [rows, rows, rows, block((8, width), 0, 0)],
        [
            like((slots, width), jnp.bfloat16),
            like((slots, width), jnp.float32),
            like((slots, width), jnp.bfloat16),
            like((8, width), jnp.float32),
        ],
        facts,
        part,
        other,
        hat,
        cotangent,
        vectors,
        wait=wait,
    )


def first_norm_kernel(
    facts_ref, part_ref, other_ref, second_ref, hat_ref, rstd_ref, vectors_ref,
    grad_ref, low_ref, sums_ref,
):
    grad = part_ref[...] + other_ref[...].astype(jnp.float32) + second_ref[...]
    hat = hat_ref[...]
    scaled = grad * vectors_ref[1:2]
    result = rstd_ref[...] * (scaled - mean_of(scaled) - hat * mean_of(scaled * hat))
    low = result.astype(jnp.bfloat16)
    grad_ref[...] = result
    low_ref[...] = low
    add_rows(sums_ref, [low.astype(jnp.float32), grad * hat, grad])


def first_norm(facts, part, other, second, hat, rstd, vectors, wait=()):
    slots, width = part.shape
    step = slots // 4
    rows = block((step, width), first, 0)
    return call(
        first_norm_kernel,
        "first_norm",
        (4,),
        [rows, rows, rows, rows, block((step, 1), first, 0), whole(vectors)],
        [rows, rows, block((8, width), 0, 0)],
        [
            like((slots, width), jnp.float32),
            like((slots, width), jnp.bfloat16),
            like((8, width), jnp.float32),
        ],
        facts,
        part,
        other,
        second,
        hat,
        rstd,
        vectors,
        wait=wait,
    )


def act_grad_kernel(facts_ref, rows_ref, weight_ref, slope_ref, out_ref, sums_ref):
    total = product(rows_ref[...], weight_ref[...], 1, 1)
    grad = total.astype(jnp.bfloat16).astype(jnp.float32) * slope_ref[...].astype(jnp.float32)
    low = grad.astype(jnp.bfloat16)
    out_ref[...] = low
    sums_ref[...] = jnp.sum(low.astype(jnp.float32), axis=0, keepdims=True)


def act_grad(facts, rows, weight, slope, wait=()):
    count, units = slope.shape
    step = units // 8
    out = block((count, step), 0, first)
    return call(
        act_grad_kernel,
        "act_grad",
        (8,),
        [whole(rows), block((step, rows.shape[1]), first, 0), out],
        [out, block((1, step), 0, first)],
        [like((count, units), jnp.bfloat16), like((1, units), jnp.float32)],
        facts,
        rows,
        weight,
        slope,
        wait=wait,
    )


def tokens_grad_kernel(facts_ref, mine_ref, theirs_ref, weight_ref, out_ref, sent_ref):
    wide = mine_ref.shape[1]
    slots = out_ref.shape[0]
    half = facts_ref[3]
    mine = weight_ref[:, pl.ds(pl.multiple_of(half * wide, 128), wide)]
    theirs = weight_ref[:, pl.ds(pl.multiple_of((1 - half) * wide, 128), wide)]
    total = product(mine_ref[...], mine, 1, 1) + product(theirs_ref[...], theirs, 1, 1)
    out_ref[...] = total[:slots]
    sent_ref[...] = total[slots:].astype(sent_ref.dtype)


def tokens_grad(facts, mine, theirs, weight, wait=(), through=()):
    count, columns = mine.shape
    width = weight.shape[0]
    step = width // 4
    out = block((count // 2, step), 0, first)
    return call(
        tokens_grad_kernel,
        "tokens_grad",
        (4,),
        [whole(mine), whole(theirs), block((step, 2 * columns), first, 0)],
        [out, out],
        [
            like((count // 2, width), jnp.float32),
            like((count // 2, width), jnp.bfloat16),
        ],
        facts,
        mine,
        theirs,
        weight,
        wait=wait,
        through=through,
    )


def add_parts_kernel(facts_ref, own_ref, got_ref, kept_ref, sent_ref):
    step = pl.program_id(0)
    total = own_ref[...].astype(jnp.float32) + got_ref[...].astype(jnp.float32)
    total = total.astype(jnp.bfloat16)

    @pl.when(step < 2)
    def _():
        sent_ref[...] = total

    @pl.when(step >= 2)
    def _():
        kept_ref[...] = total


def add_last_kernel(facts_ref, own_ref, got_ref, kept_ref, sent_ref):
    total = own_ref[0].astype(jnp.float32) + got_ref[0].astype(jnp.float32)
    total = total.astype(jnp.bfloat16)

    @pl.when(pl.program_id(0) == 0)
    def _():
        sent_ref[...] = total

    @pl.when(pl.program_id(0) == 1)
    def _():
        kept_ref[...] = total


def add_last(facts, own, got, wait=(), through=()):
    _, rows, columns = own.shape
    part = block((1, rows, columns), lambda i, f: jnp.where(i == 0, 1 - f[6], f[6]), 0, 0)
    shape = like((rows, columns), jnp.bfloat16)
    out = block((rows, columns), 0, 0)
    return call(
        add_last_kernel,
        "add_last",
        (2,),
        [part, part],
        [out, out],
        [shape, shape],
        facts,
        own,
        got,
        wait=wait,
        through=through,
    )


def add_parts(facts, own, got, wait=(), through=()):
    _, rows, columns = own.shape
    shape = (1, rows, columns)
    part = block(shape, lambda i, f: 2 * (i % 2) + jnp.where(i < 2, 1 - f[7], f[7]), 0, 0)
    half = like((2, rows, columns), jnp.bfloat16)
    return call(
        add_parts_kernel,
        "add_parts",
        (4,),
        [part, part],
        [
            block(shape, lambda i, *_: jnp.maximum(i - 2, 0), 0, 0),
            block(shape, lambda i, *_: jnp.minimum(i, 1), 0, 0),
        ],
        [half, half],
        facts,
        own,
        got,
        wait=wait,
        through=through,
    )


def alternate(value, width, offset):
    starts = range(offset * width, value.shape[1], 2 * width)
    return jnp.concatenate([value[:, start : start + width] for start in starts], axis=1)


def deal_kernel(unit_block, core_ref, query_ref, key_ref, value_ref, up_ref, *refs):
    first_core = core_ref[0] == 0
    near = [ref[...] for ref in (query_ref, key_ref, value_ref)]
    even = jnp.concatenate([alternate(value, HD, 0) for value in near], axis=1)
    odd = jnp.concatenate([alternate(value, HD, 1) for value in near], axis=1)
    up = up_ref[...]
    up_even, up_odd = alternate(up, unit_block, 0), alternate(up, unit_block, 1)
    refs[0][...] = jnp.where(first_core, even, odd)
    refs[1][...] = jnp.where(first_core, odd, even)
    refs[2][...] = jnp.where(first_core, up_even, up_odd)
    refs[3][...] = jnp.where(first_core, up_odd, up_even)


def deal(core, query, key, value, up, unit_block):
    near = like((query.shape[0], 3 * query.shape[1] // 2), jnp.bfloat16)
    half = like((up.shape[0], up.shape[1] // 2), jnp.bfloat16)
    shapes = [near, near, half, half]
    return call(
        partial(deal_kernel, unit_block),
        "deal",
        (1,),
        [whole(value) for value in (query, key, value, up)],
        [whole(shape) for shape in shapes],
        shapes,
        core,
        query,
        key,
        value,
        up,
    )


def lay_out_kernel(core_ref, near_ref, near_got_ref, out_ref, up_ref, up_got_ref, *refs):
    first_core = core_ref[0] == 0
    near, near_got, up, up_got = [
        ref[...] for ref in (near_ref, near_got_ref, up_ref, up_got_ref)
    ]
    out = out_ref[...]
    wide = out.shape[1] // 2
    near_rows = jnp.concatenate(
        [jnp.where(first_core, near, near_got), jnp.where(first_core, near_got, near)], axis=0
    )
    out_rows = jnp.concatenate([out[:, :wide], out[:, wide:]], axis=0)
    refs[0][...] = jnp.concatenate([near_rows, out_rows], axis=1)
    refs[1][...] = jnp.concatenate(
        [jnp.where(first_core, up, up_got), jnp.where(first_core, up_got, up)], axis=0
    )


def lay_out(core, near, near_got, out, up, up_got):
    rows = 2 * near.shape[0]
    shapes = [
        like((rows, near.shape[1] + out.shape[1] // 2), jnp.bfloat16),
        like((rows, up.shape[1]), jnp.bfloat16),
    ]
    arrays = (near, near_got, out, up, up_got)
    return call(
        lay_out_kernel,
        "lay_out",
        (1,),
        [whole(value) for value in arrays],
        [whole(shape) for shape in shapes],
        shapes,
        core,
        *arrays,
    )[0]


def split_body(
    tokens,
    lengths,
    cotangent,
    query_weight,
    key_weight,
    value_weight,
    out_weight,
    up_weight,
    down_weight,
    query_bias,
    value_bias,
    out_bias,
    attn_gain,
    attn_shift,
    up_bias,
    down_bias,
    feed_gain,
    feed_shift,
):
    core = lax.axis_index("c")
    half = lax.axis_index("s")
    row_count, width = tokens.shape[1:]
    slots = 2 * row_count
    unit_block = down_weight.shape[0]
    units = up_bias.shape[0] // 2
    cols = width // 2
    wide = cols // 2

    def to_sequence(values):
        return jnp.concatenate([pick(values, half, 0), swap(pick(values, 1 - half, 0), "s")], axis=0)

    def from_sequence(values):
        return in_order(values[:row_count], swap(values[row_count:], "s"), half)

    place = jnp.stack([core]).astype(jnp.int32)
    (near_kept, near_sent, up_kept, up_sent), place = deal(
        place, query_weight, key_weight, value_weight, up_weight, unit_block
    )
    near_mine, up_mine = lay_out(
        place, near_kept, swap(near_sent, "c"), out_weight, up_kept, swap(up_sent, "c")
    )
    rows, up_cols = up_mine.shape
    line = lax.axis_index("z")
    length_own = lax.dynamic_slice_in_dim(lengths, half, 1, 0)
    facts = jnp.concatenate(
        [
            both(length_own, "c"),
            jnp.stack(
                [
                    half * row_count,
                    half,
                    lax.axis_index("x"),
                    jnp.int32(0),
                    line // 2,
                    line % 2,
                ]
            ).astype(jnp.int32),
        ]
    )
    tokens_own = to_sequence(tokens)
    cotangent_own = to_sequence(cotangent)
    (near, up_mine, down_mine), facts = stack_pair(
        facts,
        near_mine,
        line_cross(near_mine),
        wait=(tokens_own,),
        through=(up_mine, down_weight),
    )
    near, facts = stack_line(facts, near, line_next(near), wait=(cotangent_own,))
    near_parts = gather_square(near, "x")
    up_pairs, facts = stack_pair(facts, up_mine, line_cross(up_mine), wait=(near,))
    tokens_both = both(tokens_own, "c")
    up_part, facts = stack_line(
        facts, up_pairs, line_next(up_pairs), wait=(near_parts[1], near_parts[2])
    )
    up_parts = gather_square(up_part, "s")
    down_pairs, facts = stack_pair(facts, down_mine, line_cross(down_mine), wait=(up_part,))
    def halves_of(vector, size):
        return pick(vector.reshape(-1, 2, size), core, 1).reshape(-1)

    query_part = halves_of(query_bias, HD).reshape(2, wide)
    value_part = halves_of(value_bias, HD).reshape(2, wide)
    in_bias = jnp.stack([query_part, jnp.zeros_like(query_part), value_part], axis=1).reshape(-1)
    (projected, in_weight, out_own), facts = project(
        facts, tokens_both, in_bias, near_parts, wait=(down_pairs,)
    )
    out_own = out_own.reshape(cols, width)
    out_other = swap(out_own, "c")
    down_part, facts = stack_line(facts, down_pairs, line_next(down_pairs), wait=(projected,))
    down_parts = gather_square(down_part, "x")
    (heads_out, totals), facts = attend(facts, projected, slots, wait=(up_parts[2],))
    heads_other = swap(heads_out[slots:], "c")
    vectors = jnp.stack(
        [out_bias, attn_gain, attn_shift, down_bias, feed_gain, feed_shift, out_bias, out_bias]
    )
    (first_hat, first_rstd, hidden_low, first_sums), facts = attend_out(
        facts,
        heads_out,
        heads_other,
        out_own,
        out_other,
        tokens_own,
        vectors,
        wait=(up_parts[1], down_parts[2]),
    )
    tokens_t, facts = turn_all(facts, tokens_both, wait=(hidden_low,))
    (hidden_low,), facts = gate(facts, (hidden_low,), (up_parts[3], down_parts[1]))
    hidden_from = swap(hidden_low, "c")
    (activation, slope, act_t, up_all), facts = feed_up(
        facts, hidden_low, hidden_from, halves_of(up_bias, unit_block), up_parts
    )
    hidden_turned, facts = turn(facts, hidden_low, hidden_from, rows, wait=(act_t,))
    (down_all, feed_sent), facts = feed_down(facts, activation, down_parts)
    down_all = down_all.reshape(units, width)
    feed_other = swap(feed_sent, "c")
    feed_part = product(activation[:slots], down_all, 1, 0)
    feed_vectors = jnp.stack(
        [down_bias, attn_gain, attn_shift, feed_gain, feed_shift, out_bias, out_bias, out_bias]
    )
    (mixed, second_grad, feed_low, second_sums), facts = second_norm(
        facts, feed_part, feed_other, first_hat, cotangent_own, feed_vectors
    )

    feed_both = both(feed_low, "c")
    feed_mine, feed_theirs = columns_of(feed_both, half), columns_of(feed_both, 1 - half)
    down_sent = grad_block(act_t, feed_theirs)
    down_got = swap(down_sent, "s")
    (pre_grad, up_bias_grad), facts = act_grad(
        facts, feed_both, down_all, slope, wait=(down_sent,)
    )
    hidden_sent = product(pre_grad[slots:], up_all, 1, 1).astype(jnp.bfloat16)
    hidden_other = swap(hidden_sent, "c")
    hidden_own_t, hidden_other_t = hidden_turned
    up_sent = grad_block(hidden_other_t, pre_grad)
    up_got = swap(up_sent, "x")
    hidden_part = product(pre_grad[:slots], up_all, 1, 1)
    (first_grad, attn_low, third_sums), facts = first_norm(
        facts,
        hidden_part,
        hidden_other,
        second_grad,
        first_hat,
        first_rstd,
        vectors,
        wait=(up_sent,),
    )
    grad_sent = product(attn_low, out_other, 1, 1).astype(jnp.bfloat16)
    grad_other = swap(grad_sent, "c")
    grad_own = product(attn_low, out_own, 1, 1).astype(jnp.bfloat16)
    out_sent = product(heads_other, attn_low, 0, 0).astype(jnp.bfloat16)
    out_got = swap(out_sent, "c")
    heads_grad = jnp.concatenate([grad_own, grad_other], axis=0)
    (theirs_low, theirs_sums), facts = attend_back(
        facts, projected, heads_grad, totals, slots, False, wait=(out_sent,)
    )
    in_sent = grad_block(tokens_t, theirs_low)
    in_got = swap(in_sent, "s")
    down_total = grad_block(act_t, feed_mine, down_got)
    down_kept, down_sent = halve(down_total.reshape(4, 2, unit_block, cols), "x", 1)
    down_got = swap(down_sent, "x")
    out_grad = grad_block(heads_out[:slots].T, attn_low, out_got)
    out_line = out_grad.reshape((4, 2 * out_weight.shape[0], width))
    out_kept, out_sent = line_parts(out_line)
    out_got = lax.ppermute(out_sent, "z", NEXT)
    (mine_low, mine_sums), facts = attend_back(
        facts, projected, heads_grad, totals, slots, True, wait=(in_sent, out_sent, down_sent)
    )
    up_total = grad_block(hidden_own_t, pre_grad, up_got).reshape(4, rows, 2 * up_cols)
    up_kept, up_sent = columns_of(up_total, half), columns_of(up_total, 1 - half)
    up_got = swap(up_sent, "s")
    out_total = add(out_kept, out_got)
    valid_count = length_own[0].astype(jnp.float32) * width
    stats = jnp.stack(
        [jnp.sum(first_sums[0]), jnp.sum(first_sums[1]), jnp.sum(second_sums[3]), valid_count]
    )
    mine_sums, theirs_sums = jnp.sum(mine_sums, axis=(0, 1)), jnp.sum(theirs_sums, axis=(0, 1))
    late = in_order(mine_sums, theirs_sums, half)
    sums = jnp.concatenate(
        [
            second_sums[:3].reshape(-1),
            third_sums[:3].reshape(-1),
            jnp.pad(stats, (0, 124)),
            up_bias_grad[0],
            late[:, :wide].reshape(-1),
            late[:, 2 * wide :].reshape(-1),
        ]
    )
    sums = sums + lax.ppermute(sums, "z", NEXT)
    (tokens_part, tokens_sent), facts = tokens_grad(
        facts,
        mine_low,
        theirs_low,
        in_weight,
        wait=(up_sent, out_total, sums),
    )
    in_total = grad_block(tokens_t, mine_low, in_got)
    in_kept, in_sent = halve(in_total.reshape(4, 2, rows, 3 * wide), "x", 1)
    in_got = swap(in_sent, "x")
    tokens_other = swap(tokens_sent, "c")
    (down_pairs, down_next), facts = add_parts(
        facts, down_kept, down_got, wait=(in_sent, tokens_part)
    )
    down_got = lax.ppermute(down_next, "z", NEXT)
    upper = lax.axis_index("z") // 2
    out_kept, out_sent = pick(out_total, upper, 0), pick(out_total, 1 - upper, 0)
    out_kept = add(out_kept, lax.ppermute(out_sent, "z", CROSS))
    (in_pairs, in_next, sums), facts = add_parts(
        facts, in_kept, in_got, wait=(down_next, out_kept), through=(sums,)
    )
    in_got = lax.ppermute(in_next, "z", NEXT)
    (down_kept, down_sent), facts = add_last(facts, down_pairs, down_got, wait=(in_next,))
    (up_pairs, up_next), facts = add_parts(facts, up_kept, up_got, wait=(down_sent,))
    up_got = lax.ppermute(up_next, "z", NEXT)
    sums = sums + swap(sums, "x")
    sums = sums + swap(sums, "s")
    (in_kept, in_sent, out_kept, mixed), facts = add_last(
        facts, in_pairs, in_got, wait=(sums, up_next), through=(out_kept, mixed)
    )
    (up_kept, up_sent, sums), facts = add_last(
        facts, up_pairs, up_got, wait=(in_sent,), through=(sums,)
    )
    in_sum = add(in_kept, lax.ppermute(in_sent, "z", CROSS))
    tokens_grad_sum = tokens_part + tokens_other.astype(jnp.float32) + first_grad
    tokens_grad_sum = from_sequence(tokens_grad_sum.astype(jnp.bfloat16))
    mixed = in_order(mixed[:row_count], swap(mixed[row_count:], "s"), half)
    down_sum = add(down_kept, lax.ppermute(down_sent, "z", CROSS))
    up_sum = add(up_kept, lax.ppermute(up_sent, "z", CROSS))
    out_sum = fold_columns(fold(out_kept.reshape(2, out_weight.shape[0], width), "x", 0))

    sums = sums + lax.ppermute(sums, "z", CROSS)
    both_sums = in_order(sums, swap(sums, "c"), core)
    count = 6 * width + 128
    shared = both_sums[0, :count] + both_sums[1, :count]
    down_bias_grad, feed_gain_grad, feed_shift_grad, out_bias_grad, attn_gain_grad, attn_shift_grad = [
        shared[i * width : (i + 1) * width] for i in range(6)
    ]
    stats = shared[6 * width : 6 * width + 4]

    def interleave(start, size, block_size):
        sums = both_sums[:, start : start + size].reshape(2, -1, block_size)
        return sums.transpose(1, 0, 2).reshape(-1)

    up_bias_grad = interleave(count, units, unit_block)
    query_bias_grad = interleave(count + units, cols, HD)
    value_bias_gradient = interleave(count + units + cols, cols, HD)
    stream_rms = jnp.sqrt(stats[:3] / stats[3])

    def give_back(total):
        total = total.reshape((2, rows // 2) + total.shape[1:])
        return pick(total, core, 0), swap(pick(total, 1 - core, 0), "c")

    up_shares = give_back(up_sum)
    in_shares = give_back(in_sum)
    down_weight_grad = down_sum.astype(jnp.float32)
    out_weight_grad = out_sum.astype(jnp.float32)

    def merge(shares, start, size, block):
        one, two = [
            share[:, start : start + size].reshape(rows // 2, -1, block) for share in shares
        ]
        first = jnp.where(core == 0, one, two)
        second = jnp.where(core == 0, two, one)
        return jnp.stack([first, second], axis=2).reshape(rows // 2, -1).astype(jnp.float32)

    query_weight_grad = merge(in_shares, 0, wide, HD)
    key_weight_grad = merge(in_shares, wide, wide, HD)
    value_weight_grad = merge(in_shares, 2 * wide, wide, HD)
    up_weight_grad = merge(up_shares, 0, up_cols, unit_block)
    return (
        mixed,
        tokens_grad_sum,
        query_weight_grad,
        key_weight_grad,
        value_weight_grad,
        out_weight_grad,
        up_weight_grad,
        down_weight_grad,
        query_bias_grad,
        value_bias_gradient,
        out_bias_grad,
        attn_gain_grad,
        attn_shift_grad,
        up_bias_grad,
        down_bias_grad,
        feed_gain_grad,
        feed_shift_grad,
        stream_rms,
    )


def solution(mesh):
    devices = mesh.devices
    dp_count, seq_count = devices.shape
    split = seq_count == 2 and dp_count == 16
    if split:
        inner = jax.sharding.Mesh(devices.reshape(4, 2, 2, seq_count), ("z", "x", "c", "s"))
        dp, seq, body = ("z", "x", "c"), "s", split_body
    else:
        inner, dp, seq, body = mesh, "dp", "seq", general_body
    weights = (P(dp, seq),) * 6
    vectors = (P(),) * 9
    rows = P(dp, seq, None)
    in_specs = (rows, P(dp), rows) + weights + vectors
    out_specs = (rows, rows) + weights + vectors + (P(),)
    return jax.shard_map(body, mesh=inner, in_specs=in_specs, out_specs=out_specs, check_vma=False)
```

```python
from functools import partial
import math

import jax
import jax.numpy as jnp
from jax import lax
from jax.experimental import pallas as pl
from jax.experimental.pallas import tpu as pltpu
from jax.sharding import PartitionSpec as P

HD = 64


def layer_norm(values_in, gain_vector, shift_vector):
    mean_value = jnp.mean(values_in, axis=-1, keepdims=True)
    centered = values_in - mean_value
    variance = jnp.mean(centered * centered, axis=-1, keepdims=True)
    return centered * lax.rsqrt(variance + 1e-05) * gain_vector + shift_vector


def gather_weights(first, second, third, fourth, fifth, sixth):
    part = (
        lax.all_gather(first, "dp", axis=0, tiled=True),
        lax.all_gather(second, "dp", axis=0, tiled=True),
        lax.all_gather(third, "dp", axis=0, tiled=True),
        lax.all_gather(fourth, "dp", axis=0, tiled=True),
        lax.all_gather(fifth, "dp", axis=0, tiled=True),
        lax.all_gather(sixth, "dp", axis=0, tiled=True),
    )
    return (
        lax.all_gather(part[0], "seq", axis=1, tiled=True),
        lax.all_gather(part[1], "seq", axis=1, tiled=True),
        lax.all_gather(part[2], "seq", axis=1, tiled=True),
        lax.all_gather(part[3], "seq", axis=1, tiled=True),
        lax.all_gather(part[4], "seq", axis=1, tiled=True),
        lax.all_gather(part[5], "seq", axis=1, tiled=True),
    )


def reduce_grads(first, second, third, fourth, fifth, sixth):
    part = (
        lax.psum_scatter(first.astype(jnp.bfloat16), "seq", scatter_dimension=1, tiled=True).astype(
            jnp.float32
        ),
        lax.psum_scatter(
            second.astype(jnp.bfloat16), "seq", scatter_dimension=1, tiled=True
        ).astype(jnp.float32),
        lax.psum_scatter(third.astype(jnp.bfloat16), "seq", scatter_dimension=1, tiled=True).astype(
            jnp.float32
        ),
        lax.psum_scatter(
            fourth.astype(jnp.bfloat16), "seq", scatter_dimension=1, tiled=True
        ).astype(jnp.float32),
        lax.psum_scatter(fifth.astype(jnp.bfloat16), "seq", scatter_dimension=1, tiled=True).astype(
            jnp.float32
        ),
        lax.psum_scatter(sixth.astype(jnp.bfloat16), "seq", scatter_dimension=1, tiled=True).astype(
            jnp.float32
        ),
    )
    return (
        lax.psum_scatter(
            part[0].astype(jnp.bfloat16), "dp", scatter_dimension=0, tiled=True
        ).astype(jnp.float32),
        lax.psum_scatter(
            part[1].astype(jnp.bfloat16), "dp", scatter_dimension=0, tiled=True
        ).astype(jnp.float32),
        lax.psum_scatter(
            part[2].astype(jnp.bfloat16), "dp", scatter_dimension=0, tiled=True
        ).astype(jnp.float32),
        lax.psum_scatter(
            part[3].astype(jnp.bfloat16), "dp", scatter_dimension=0, tiled=True
        ).astype(jnp.float32),
        lax.psum_scatter(
            part[4].astype(jnp.bfloat16), "dp", scatter_dimension=0, tiled=True
        ).astype(jnp.float32),
        lax.psum_scatter(
            part[5].astype(jnp.bfloat16), "dp", scatter_dimension=0, tiled=True
        ).astype(jnp.float32),
    )


def block_layout(seq_count, row_count, head_count):
    block_seqs = math.gcd(seq_count, max(1, 512 // row_count))
    group_heads = math.gcd(head_count, 4)
    return (block_seqs, seq_count // block_seqs, group_heads, head_count // group_heads)


def head_slice(block_part, offset, group_width, group_heads):
    sliced = lax.dynamic_slice_in_dim(block_part, offset, group_width, 2)
    return sliced.reshape(sliced.shape[0], sliced.shape[1], group_heads, HD)


def attention_forward(queries, key_all, value_all, key_mask):
    seq_count, row_count, feature_total = queries.shape
    slot_count = key_all.shape[1]
    block_seqs, block_count, group_heads, group_count = block_layout(
        seq_count, row_count, feature_total // HD
    )
    group_width = group_heads * HD

    def seq_block(inputs):
        query_part, key_part, value_part, mask_part = inputs

        def head_block(group_index):
            offset = group_index * group_width
            query_heads = head_slice(query_part, offset, group_width, group_heads)
            key_heads = head_slice(key_part, offset, group_width, group_heads)
            value_heads = head_slice(value_part, offset, group_width, group_heads)
            scores = (
                jnp.einsum(
                    "brhd,bkhd->bhrk", query_heads, key_heads, preferred_element_type=jnp.float32
                )
                * 0.125
            )
            scores = jnp.where(mask_part[:, None, None, :], scores, -1e30)
            row_max = jnp.max(scores, axis=-1, keepdims=True)
            exponent = jnp.exp(scores - row_max)
            row_total = jnp.sum(exponent, axis=-1, keepdims=True)
            soft_probs = (exponent / row_total).astype(jnp.bfloat16)
            heads_out = jnp.einsum(
                "bhrk,bkhd->brhd", soft_probs, value_heads, preferred_element_type=jnp.float32
            )
            log_total = (row_max + jnp.log(row_total))[..., 0]
            return (heads_out.reshape(block_seqs, row_count, group_width), log_total)

        return lax.map(head_block, jnp.arange(group_count))

    outputs, log_totals = lax.map(
        seq_block,
        (
            queries.reshape(block_count, block_seqs, row_count, feature_total),
            key_all.reshape(block_count, block_seqs, slot_count, feature_total),
            value_all.reshape(block_count, block_seqs, slot_count, feature_total),
            key_mask.reshape(block_count, block_seqs, slot_count),
        ),
    )
    mixed_heads = outputs.transpose(0, 2, 3, 1, 4).reshape(seq_count, row_count, feature_total)
    return (mixed_heads, log_totals)


def attention_backward(queries, key_all, value_all, key_mask, heads_grad, log_totals):
    seq_count, row_count, feature_total = queries.shape
    slot_count = key_all.shape[1]
    block_seqs, block_count, group_heads, group_count = block_layout(
        seq_count, row_count, feature_total // HD
    )
    group_width = group_heads * HD

    def seq_block(inputs):
        query_part, key_part, value_part, mask_part, grad_part, total_part = inputs

        def head_block(group_index):
            offset = group_index * group_width
            query_heads = head_slice(query_part, offset, group_width, group_heads)
            key_heads = head_slice(key_part, offset, group_width, group_heads)
            value_heads = head_slice(value_part, offset, group_width, group_heads)
            grad_heads = head_slice(grad_part, offset, group_width, group_heads)
            log_total = lax.dynamic_index_in_dim(total_part, group_index, 0, keepdims=False)
            scores = (
                jnp.einsum(
                    "brhd,bkhd->bhrk", query_heads, key_heads, preferred_element_type=jnp.float32
                )
                * 0.125
            )
            scores = jnp.where(mask_part[:, None, None, :], scores, -1e30)
            soft_probs = jnp.exp(scores - log_total[..., None])
            value_grad = jnp.einsum(
                "bhrk,brhd->bkhd",
                soft_probs.astype(jnp.bfloat16),
                grad_heads,
                preferred_element_type=jnp.float32,
            )
            prob_grad = jnp.einsum(
                "brhd,bkhd->bhrk", grad_heads, value_heads, preferred_element_type=jnp.float32
            )
            inner = jnp.sum(soft_probs * prob_grad, axis=-1, keepdims=True)
            score_grad = (soft_probs * (prob_grad - inner)).astype(jnp.bfloat16)
            query_grad = (
                jnp.einsum(
                    "bhrk,bkhd->brhd", score_grad, key_heads, preferred_element_type=jnp.float32
                )
                * 0.125
            )
            key_grad = (
                jnp.einsum(
                    "bhrk,brhd->bkhd", score_grad, query_heads, preferred_element_type=jnp.float32
                )
                * 0.125
            )
            return (
                query_grad.reshape(block_seqs, row_count, group_width),
                key_grad.reshape(block_seqs, slot_count, group_width),
                value_grad.reshape(block_seqs, slot_count, group_width),
            )

        return lax.map(head_block, jnp.arange(group_count))

    query_blocks, key_blocks, value_block_list = lax.map(
        seq_block,
        (
            queries.reshape(block_count, block_seqs, row_count, feature_total),
            key_all.reshape(block_count, block_seqs, slot_count, feature_total),
            value_all.reshape(block_count, block_seqs, slot_count, feature_total),
            key_mask.reshape(block_count, block_seqs, slot_count),
            heads_grad.reshape(block_count, block_seqs, row_count, feature_total),
            log_totals,
        ),
    )
    query_grad = query_blocks.transpose(0, 2, 3, 1, 4).reshape(seq_count, row_count, feature_total)
    key_grad = key_blocks.transpose(0, 2, 3, 1, 4).reshape(seq_count, slot_count, feature_total)
    value_grad = value_block_list.transpose(0, 2, 3, 1, 4).reshape(
        seq_count, slot_count, feature_total
    )
    return (query_grad, key_grad, value_grad)


def general_body(
    tokens,
    lengths,
    cotangent,
    query_weight,
    key_weight,
    value_weight,
    out_weight,
    up_weight,
    down_weight,
    query_bias,
    value_bias,
    out_bias,
    attn_gain,
    attn_shift,
    up_bias,
    down_bias,
    feed_gain,
    feed_shift,
):
    seq_count, row_count, feature_total = tokens.shape
    slot_count = row_count * lax.axis_size("seq")
    token_count = seq_count * row_count
    whole = gather_weights(
        query_weight, key_weight, value_weight, out_weight, up_weight, down_weight
    )
    full_query, full_key, full_value, full_out, full_up, full_down = whole
    flat_tokens = tokens.reshape(token_count, feature_total)
    queries = (
        jnp.dot(flat_tokens, full_query, preferred_element_type=jnp.float32) + query_bias
    ).astype(jnp.bfloat16)
    key_rows = jnp.dot(flat_tokens, full_key, preferred_element_type=jnp.float32).astype(
        jnp.bfloat16
    )
    value_rows = (
        jnp.dot(flat_tokens, full_value, preferred_element_type=jnp.float32) + value_bias
    ).astype(jnp.bfloat16)
    first_slot = lax.axis_index("seq") * row_count
    key_mask = jnp.arange(slot_count)[None, :] < lengths[:, None]
    row_valid = ((first_slot + jnp.arange(row_count))[None, :] < lengths[:, None]).astype(
        jnp.float32
    )
    row_valid = row_valid.reshape(token_count, 1)
    query_blocks = queries.reshape(seq_count, row_count, feature_total)
    key_blocks = key_rows.reshape(seq_count, row_count, feature_total)
    value_block_list = value_rows.reshape(seq_count, row_count, feature_total)
    key_all, value_all = (
        lax.all_gather(key_blocks, "seq", axis=1, tiled=True),
        lax.all_gather(value_block_list, "seq", axis=1, tiled=True),
    )
    mixed_heads, log_totals = attention_forward(query_blocks, key_all, value_all, key_mask)
    heads_low = mixed_heads.reshape(token_count, feature_total).astype(jnp.bfloat16)
    attention_out = jnp.dot(heads_low, full_out, preferred_element_type=jnp.float32) + out_bias
    tokens_f32 = flat_tokens.astype(jnp.float32)
    first_sum = tokens_f32 + attention_out
    hidden, first_pull = jax.vjp(layer_norm, first_sum, attn_gain, attn_shift)
    hidden_low = hidden.astype(jnp.bfloat16)
    pre_act = jnp.dot(hidden_low, full_up, preferred_element_type=jnp.float32) + up_bias
    gelu_out, gelu_pull = jax.vjp(partial(jax.nn.gelu, approximate=False), pre_act)
    activation = gelu_out.astype(jnp.bfloat16)
    feed_out = jnp.dot(activation, full_down, preferred_element_type=jnp.float32) + down_bias
    result, second_pull = jax.vjp(layer_norm, hidden + feed_out, feed_gain, feed_shift)
    mixed = result.astype(jnp.bfloat16).reshape(seq_count, row_count, feature_total)
    partial_stats = jnp.stack(
        [
            jnp.sum(row_valid * tokens_f32 * tokens_f32),
            jnp.sum(row_valid * attention_out * attention_out),
            jnp.sum(row_valid * feed_out * feed_out),
            jnp.sum(row_valid) * feature_total,
        ]
    )
    back_weights = gather_weights(
        query_weight, key_weight, value_weight, out_weight, up_weight, down_weight
    )
    back_query, back_key, back_value, back_out, back_up, back_down = back_weights
    out_grad = cotangent.reshape(token_count, feature_total).astype(jnp.float32) * row_valid
    second_grad, feed_gain_grad, feed_shift_grad = second_pull(out_grad)
    feed_low = second_grad.astype(jnp.bfloat16)
    down_weight_grad = jnp.einsum(
        "nf,nd->fd", activation, feed_low, preferred_element_type=jnp.float32
    )
    down_bias_grad = jnp.sum(feed_low, axis=0, dtype=jnp.float32)
    act_grad = jnp.einsum(
        "nd,fd->nf", feed_low, back_down, preferred_element_type=jnp.float32
    ).astype(jnp.bfloat16)
    pre_grad = gelu_pull(act_grad.astype(jnp.float32))[0].astype(jnp.bfloat16)
    up_weight_grad = jnp.einsum(
        "nd,nf->df", hidden_low, pre_grad, preferred_element_type=jnp.float32
    )
    up_bias_grad = jnp.sum(pre_grad, axis=0, dtype=jnp.float32)
    hidden_grad = (
        jnp.einsum("nf,df->nd", pre_grad, back_up, preferred_element_type=jnp.float32) + second_grad
    )
    first_grad, attn_gain_grad, attn_shift_grad = first_pull(hidden_grad)
    attn_low = first_grad.astype(jnp.bfloat16)
    out_weight_grad = jnp.einsum(
        "nd,ne->de", heads_low, attn_low, preferred_element_type=jnp.float32
    )
    out_bias_grad = jnp.sum(attn_low, axis=0, dtype=jnp.float32)
    heads_grad = jnp.einsum(
        "ne,de->nd", attn_low, back_out, preferred_element_type=jnp.float32
    ).astype(jnp.bfloat16)
    heads_grad = heads_grad.reshape(seq_count, row_count, feature_total)
    query_grad, key_part_grad, value_part_grad = attention_backward(
        query_blocks, key_all, value_all, key_mask, heads_grad, log_totals
    )
    key_sum, value_sum = (
        lax.psum_scatter(
            key_part_grad.astype(jnp.bfloat16), "seq", scatter_dimension=1, tiled=True
        ).astype(jnp.float32),
        lax.psum_scatter(
            value_part_grad.astype(jnp.bfloat16), "seq", scatter_dimension=1, tiled=True
        ).astype(jnp.float32),
    )
    query_low = query_grad.reshape(token_count, feature_total).astype(jnp.bfloat16)
    key_low = key_sum.reshape(token_count, feature_total).astype(jnp.bfloat16)
    value_low = value_sum.reshape(token_count, feature_total).astype(jnp.bfloat16)
    query_weight_grad = jnp.einsum(
        "nd,ne->de", flat_tokens, query_low, preferred_element_type=jnp.float32
    )
    key_weight_grad = jnp.einsum(
        "nd,ne->de", flat_tokens, key_low, preferred_element_type=jnp.float32
    )
    value_weight_grad = jnp.einsum(
        "nd,ne->de", flat_tokens, value_low, preferred_element_type=jnp.float32
    )
    query_bias_grad = jnp.sum(query_low, axis=0, dtype=jnp.float32)
    value_bias_gradient = jnp.sum(value_low, axis=0, dtype=jnp.float32)
    tokens_grad = (
        jnp.einsum("ne,de->nd", query_low, back_query, preferred_element_type=jnp.float32)
        + jnp.einsum("ne,de->nd", key_low, back_key, preferred_element_type=jnp.float32)
        + jnp.einsum("ne,de->nd", value_low, back_value, preferred_element_type=jnp.float32)
        + first_grad
    )
    tokens_grad = tokens_grad.astype(jnp.bfloat16).reshape(seq_count, row_count, feature_total)
    matrix_grads = reduce_grads(
        query_weight_grad,
        key_weight_grad,
        value_weight_grad,
        out_weight_grad,
        up_weight_grad,
        down_weight_grad,
    )
    totals = lax.psum(
        (
            partial_stats,
            query_bias_grad,
            value_bias_gradient,
            out_bias_grad,
            attn_gain_grad,
            attn_shift_grad,
            up_bias_grad,
            down_bias_grad,
            feed_gain_grad,
            feed_shift_grad,
        ),
        ("dp", "seq"),
    )
    stream_rms = jnp.sqrt(totals[0][:3] / totals[0][3])
    return (
        mixed,
        tokens_grad,
        matrix_grads[0],
        matrix_grads[1],
        matrix_grads[2],
        matrix_grads[3],
        matrix_grads[4],
        matrix_grads[5],
        totals[1],
        totals[2],
        totals[3],
        totals[4],
        totals[5],
        totals[6],
        totals[7],
        totals[8],
        totals[9],
        stream_rms,
    )


def swap(value, axis):
    return lax.ppermute(value, axis, [(0, 1), (1, 0)])


def both(value, axis):
    return jnp.concatenate([value, swap(value, axis)], axis=0)


def in_order(own, other, index, axis=0):
    return jnp.where(
        index == 0, jnp.stack([own, other], axis=axis), jnp.stack([other, own], axis=axis)
    )


def pick(values, index, axis):
    return lax.dynamic_index_in_dim(values, index, axis, keepdims=False)


def add(left, right):
    return (left.astype(jnp.float32) + right.astype(jnp.float32)).astype(jnp.bfloat16)


def fold(values, axis, dim):
    index = lax.axis_index(axis)
    return add(pick(values, index, dim), swap(pick(values, 1 - index, dim), axis))


NEXT = [(0, 1), (1, 0), (2, 3), (3, 2)]
CROSS = [(0, 2), (2, 0), (1, 3), (3, 1)]


def fold_cross(pairs):
    upper = lax.axis_index("z") // 2
    return add(pick(pairs, upper, 0), lax.ppermute(pick(pairs, 1 - upper, 0), "z", CROSS))


def fold_line(values):
    odd = lax.axis_index("z") % 2
    pairs = values.reshape((2, 2) + values.shape[1:])
    sent = lax.ppermute(pick(pairs, 1 - odd, 1), "z", NEXT)
    return fold_cross(add(pick(pairs, odd, 1), sent))


def line_cross(value):
    return lax.ppermute(value, "z", CROSS)


def line_next(pair):
    return lax.ppermute(pair, "z", NEXT)


def gather_square(own, way):
    beside, below = swap(own, "x"), swap(own, "s")
    across = swap(below, "x") if way == "x" else swap(beside, "s")
    return [own, beside, below, across]


def fold_columns(total):
    half = lax.axis_index("s")
    return add(columns_of(total, half), swap(columns_of(total, 1 - half), "s"))


def halve(values, axis, dim):
    index = lax.axis_index(axis) % 2
    return pick(values, index, dim), pick(values, 1 - index, dim)


def line_parts(values):
    return halve(values.reshape((2, 2) + values.shape[1:]), "z", 1)


def scatter_top(send, keep):
    total = add(keep, swap(send, "s"))
    total = total.reshape((4, 2) + total.shape[1:])
    return fold_line(fold(total, "x", 1))


def grad_block(left_t, right, got=None):
    total = product(left_t, right, 1, 0)
    if got is not None:
        total = total + got.astype(jnp.float32)
    return total.astype(jnp.bfloat16)


def columns_of(right, index):
    columns = right.shape[-1] // 2
    return lax.dynamic_slice_in_dim(right, index * columns, columns, right.ndim - 1)


PAIR = 2 * HD
LIMIT = 10 * 1024 * 1024


def kernel_params(steps):
    return pltpu.CompilerParams(
        dimension_semantics=("arbitrary",) * steps, vmem_limit_bytes=LIMIT
    )


def product(left, right, left_dim, right_dim):
    return lax.dot_general(
        left, right, (((left_dim,), (right_dim,)), ((), ())), preferred_element_type=jnp.float32
    )


def key_bias(facts_ref, slots):
    place = lax.broadcasted_iota(jnp.int32, (slots, 1), 0) + facts_ref[2]
    place = jnp.where(place >= slots, place - slots, place)
    return jnp.where(place < facts_ref[pl.program_id(0)], 0.0, -1e30)


def head_lanes(value, head):
    lane = lax.broadcasted_iota(jnp.int32, value.shape, 1)
    return jnp.where((lane >= HD) == (head == 1), value, jnp.zeros_like(value))


def turned(value):
    return value.astype(jnp.float32).T


def attend_kernel(facts_ref, query_ref, key_ref, value_ref, out_ref, total_ref):
    slots = key_ref.shape[0]
    bias = key_bias(facts_ref, slots)
    query = query_ref[...] * jnp.bfloat16(0.125)
    key = key_ref[...]
    value_t = turned(value_ref[...]).astype(jnp.bfloat16)
    outs = []
    for head in range(2):
        scores = product(key, head_lanes(query, head), 1, 1) + bias
        peak = jnp.max(scores, axis=0, keepdims=True)
        weight = jnp.exp(scores - peak)
        total = jnp.sum(weight, axis=0, keepdims=True)
        part = product(value_t[head * HD : (head + 1) * HD], weight.astype(jnp.bfloat16), 1, 0)
        outs.append(part * (1.0 / total))
        total_ref[0, 0, head : head + 1, :] = peak + jnp.log(total)
    out_ref[...] = jnp.concatenate(outs, axis=0).T.astype(jnp.bfloat16)


def attend_back_kernel(
    facts_ref, query_ref, key_ref, value_ref, grad_ref, total_ref, low_ref, sums_ref
):
    slots = key_ref.shape[0]
    bias = key_bias(facts_ref, slots)
    query = query_ref[...] * jnp.bfloat16(0.125)
    key = key_ref[...]
    value = value_ref[...]
    grad = grad_ref[...]
    key_t = turned(key).astype(jnp.bfloat16)
    lane = lax.broadcasted_iota(jnp.int32, (slots, PAIR), 1)
    query_parts, key_parts, value_parts = [], [], []
    for head in range(2):
        scores = product(key, head_lanes(query, head), 1, 1) + bias
        soft = jnp.exp(scores - total_ref[0, 0, head : head + 1, :])
        value_parts.append(product(soft.astype(jnp.bfloat16), grad, 1, 0))
        change = product(value, head_lanes(grad, head), 1, 1)
        inner = jnp.sum(soft * change, axis=0, keepdims=True)
        change = (soft * (change - inner)).astype(jnp.bfloat16)
        key_parts.append(product(change, query, 1, 0))
        query_parts.append(product(key_t[head * HD : (head + 1) * HD], change, 1, 0))
    pair = pl.program_id(1)
    groups = low_ref.shape[1] // 3
    query_low = (jnp.concatenate(query_parts, axis=0) * 0.125).T
    key_low = jnp.where(lane < HD, key_parts[0], key_parts[1])
    value_low = jnp.where(lane < HD, value_parts[0], value_parts[1])
    for place, part in enumerate((query_low, key_low, value_low)):
        start = pl.multiple_of(place * groups + pair * PAIR, PAIR)
        low = part.astype(jnp.bfloat16)
        low_ref[:, pl.ds(start, PAIR)] = low
        sums_ref[0, :, pl.ds(start, PAIR)] = jnp.sum(
            low.astype(jnp.float32), axis=0, keepdims=True
        )


def attention_specs(slots, pairs):
    def at(part):
        return pl.BlockSpec(
            (slots, PAIR), lambda b, g, p, *_: (b, g * 3 * pairs + part * pairs + p)
        )

    heads = pl.BlockSpec((slots, PAIR), lambda b, g, p, *_: (b, g * pairs + p))
    totals = pl.BlockSpec((1, 1, 2, slots), lambda b, g, p, *_: (b, g * pairs + p, 0, 0))
    return [at(0), at(1), at(2)], heads, totals


def attend(facts, projected, slots, wait=()):
    pairs = projected.shape[1] // (6 * PAIR)
    inputs, heads, totals = attention_specs(slots, pairs)
    rows = projected.shape[0]
    return call(
        attend_kernel,
        "attend",
        (2, 2, pairs),
        inputs,
        [heads, totals],
        [
            like((rows, 2 * pairs * PAIR), jnp.bfloat16),
            like((2, 2 * pairs, 2, slots), jnp.float32),
        ],
        facts,
        projected,
        projected,
        projected,
        wait=wait,
    )


def attend_back(facts, projected, heads_grad, totals_in, slots, own, wait=(), through=()):
    pairs = projected.shape[1] // (6 * PAIR)

    def group(facts_ref):
        return facts_ref[3] if own else 1 - facts_ref[3]

    def at(part):
        return pl.BlockSpec(
            (slots, PAIR), lambda b, p, f: (b, group(f) * 3 * pairs + part * pairs + p)
        )

    heads = pl.BlockSpec((slots, PAIR), lambda b, p, f: (b, group(f) * pairs + p))
    totals = pl.BlockSpec((1, 1, 2, slots), lambda b, p, f: (b, group(f) * pairs + p, 0, 0))
    width = 3 * pairs * PAIR
    return call(
        attend_back_kernel,
        "attend_back",
        (2, pairs),
        [at(0), at(1), at(2), heads, totals],
        [
            pl.BlockSpec((slots, width), lambda b, p, f: (b, 0)),
            pl.BlockSpec((1, 1, width), lambda b, p, f: (b, 0, 0)),
        ],
        [
            like((2 * slots, width), jnp.bfloat16),
            like((2, 1, width), jnp.float32),
        ],
        facts,
        projected,
        projected,
        projected,
        heads_grad,
        totals_in,
        wait=wait,
        through=through,
    )


def call(kernel, name, grid, inputs, outputs, shapes, facts, *args, wait=(), scratch=(), through=(), into=()):
    single = not isinstance(outputs, list)
    outputs, shapes = ([outputs], [shapes]) if single else (outputs, shapes)
    wait = tuple(into) + tuple(wait)
    count, held, passed = len(args), len(wait) + len(through), len(through)
    last = count + held + len(outputs)

    def body(facts_ref, *refs):
        kernel(facts_ref, *refs[:count], *refs[count + held : last], *refs[last + passed + 1 :])
        for place in range(facts.shape[0]):
            refs[last + passed][place] = facts_ref[place]

    results = pl.pallas_call(
        body,
        grid_spec=pltpu.PrefetchScalarGridSpec(
            num_scalar_prefetch=1,
            grid=grid,
            in_specs=list(inputs) + [pl.BlockSpec(memory_space=pl.ANY)] * held,
            out_specs=list(outputs)
            + [pl.BlockSpec(memory_space=pl.ANY)] * passed
            + [pl.BlockSpec(memory_space=pltpu.SMEM)],
            scratch_shapes=list(scratch),
        ),
        out_shape=list(shapes)
        + [like(value.shape, value.dtype) for value in through]
        + [like(facts.shape, jnp.int32)],
        input_output_aliases={
            **{1 + count + i: i for i in range(len(into))},
            **{1 + count + len(wait) + i: len(outputs) + i for i in range(passed)},
        },
        compiler_params=kernel_params(len(grid)),
        name=name,
    )(facts, *args, *wait, *through)
    values = tuple(results[:-1])
    return (values[0] if single and not passed else values), results[-1]


def block(shape, *index):
    def at(*grid_and_facts):
        return tuple(entry(*grid_and_facts) if callable(entry) else entry for entry in index)

    return pl.BlockSpec(shape, at)


def whole(array):
    zeros = (0,) * array.ndim
    return pl.BlockSpec(array.shape, lambda *_: zeros)


def first(i, *_):
    return i


def like(shape, dtype):
    return jax.ShapeDtypeStruct(shape, dtype)


def rows_in_order(facts_ref, own, beside):
    even = facts_ref[4] == 0
    pieces = []
    for z in range(4):
        pieces += [jnp.where(even, own[z], beside[z]), jnp.where(even, beside[z], own[z])]
    return jnp.concatenate(pieces, axis=0)


def near_or_far(facts_ref, refs, near):
    own, beside, below, across = [ref[...] for ref in refs]
    return rows_in_order(
        facts_ref, jnp.where(near, own, below), jnp.where(near, beside, across)
    )


def square_columns(parts, wide, steps):
    shape = parts[0].shape[:2] + (wide,)
    near = block(shape, 0, 0, lambda i, *_: jnp.minimum(i, steps - 1))
    far = block(shape, 0, 0, lambda i, *_: jnp.maximum(i - steps, 0))
    return [near, near, far, far]


def half_at(i, facts, steps):
    return jnp.where(i < steps, facts[3], 1 - facts[3])


def gate_kernel(facts_ref):
    del facts_ref


def gate(facts, through, wait):
    return call(gate_kernel, "gate", (1,), [], [], [], facts, wait=wait, through=through)


def stack_kernel(own_at, facts_ref, own_ref, other_ref, out_ref):
    own = facts_ref[own_at] == pl.program_id(0)
    value = jnp.where(own, own_ref[...], other_ref[...])
    out_ref[...] = value.reshape(out_ref.shape)


def stack_pair(facts, own, other, wait=(), through=()):
    rows, columns = own.shape
    return call(
        partial(stack_kernel, 6),
        "stack",
        (2,),
        [whole(own), whole(other)],
        block((1, rows, columns), first, 0, 0),
        like((2, rows, columns), own.dtype),
        facts,
        own,
        other,
        wait=wait,
        through=through,
    )


def stack_line(facts, own, other, wait=()):
    _, rows, columns = own.shape
    line, facts = call(
        partial(stack_kernel, 7),
        "stack_line",
        (2,),
        [whole(own), whole(other)],
        block((2, 1, rows, columns), 0, first, 0, 0),
        like((2, 2, rows, columns), own.dtype),
        facts,
        own,
        other,
        wait=wait,
    )
    return line.reshape(4, rows, columns), facts


def turn_kernel(facts_ref, *refs):
    for i in range(2):
        refs[4 + i][...] = jnp.concatenate([refs[2 * i][...].T, refs[2 * i + 1][...].T], axis=1)


def turn_all_kernel(facts_ref, rows_ref, out_ref):
    out_ref[...] = rows_ref[...].T


def turn_all(facts, values, wait=()):
    count, width = values.shape
    step = width // 4
    return call(
        turn_all_kernel,
        "turn_all",
        (4,),
        [block((count, step), 0, first)],
        block((step, count), first, 0),
        like((width, count), values.dtype),
        facts,
        values,
        wait=wait,
    )


def turn(facts, values, others, rows, wait=()):
    count, width = values.shape
    half = width // 2
    out = block((rows, 2 * count), first, 0)
    shape = like((half, 2 * count), values.dtype)
    own = block((count, rows), 0, lambda i, f: 2 * i + f[4])
    other = block((count, rows), 0, lambda i, f: 2 * i + 1 - f[4])
    return call(
        turn_kernel,
        "turn",
        (half // rows,),
        [own, own, other, other],
        [out, out],
        [shape, shape],
        facts,
        values,
        others,
        values,
        others,
        wait=wait,
    )


def project_kernel(facts_ref, rows_ref, bias_ref, *refs):
    parts, (out_ref, in_ref, rest_ref) = refs[:4], refs[4:]
    step = pl.program_id(0)
    weight = near_or_far(facts_ref, parts, step < 4)

    @pl.when(step % 4 < 3)
    def _():
        in_ref[...] = weight
        value = product(rows_ref[...], weight, 1, 0) + bias_ref[...]
        out_ref[...] = value.astype(jnp.bfloat16)

    @pl.when(step % 4 == 3)
    def _():
        chips, count, wide = rest_ref.shape
        pairs = weight.reshape(chips, 2, count, wide // 2)
        rest_ref[...] = jnp.concatenate([pairs[:, 0], pairs[:, 1]], axis=2)


def project(facts, rows, bias, parts, wait=()):
    count, width = rows.shape
    wide = parts[0].shape[2] // 4

    def column(i, f):
        return half_at(i, f, 4) * 3 + jnp.minimum(i % 4, 2)

    out = block((count, wide), 0, column)
    rest = (8, parts[0].shape[1] // 2, 2 * wide)
    return call(
        project_kernel,
        "project",
        (8,),
        [whole(rows), block((1, wide), 0, column)] + square_columns(parts, wide, 4),
        [out, block((width, wide), 0, column), block(rest, 0, 0, lambda i, f: half_at(i, f, 4))],
        [
            like((count, 6 * wide), jnp.bfloat16),
            like((width, 6 * wide), jnp.bfloat16),
            like(rest[:2] + (4 * wide,), jnp.bfloat16),
        ],
        facts,
        rows,
        bias[None],
        *parts,
        wait=wait,
    )


def valid_rows(facts_ref, count, slots):
    place = lax.broadcasted_iota(jnp.int32, (count, 1), 0) + pl.program_id(0) * count + facts_ref[2]
    place = jnp.where(place >= slots, place - slots, place)
    return (place < facts_ref[0]).astype(jnp.float32)


def add_rows(sums_ref, rows):
    total = jnp.concatenate([jnp.sum(part, axis=0, keepdims=True) for part in rows], axis=0)
    total = jnp.concatenate([total, jnp.zeros((8 - len(rows), total.shape[1]), jnp.float32)], axis=0)

    @pl.when(pl.program_id(0) == 0)
    def _():
        sums_ref[...] = total

    @pl.when(pl.program_id(0) > 0)
    def _():
        sums_ref[...] += total


def mean_of(values):
    return jnp.mean(values, axis=-1, keepdims=True)


def attend_out_kernel(
    slots, facts_ref, own_ref, other_ref, own_weight_ref, other_weight_ref, tokens_ref, vectors_ref,
    hat_ref, rstd_ref, low_ref, sums_ref,
):
    branch = (
        product(own_ref[...], own_weight_ref[...], 1, 0)
        + product(other_ref[...], other_weight_ref[...], 1, 0)
        + vectors_ref[0:1]
    )
    tokens = tokens_ref[...].astype(jnp.float32)
    total = tokens + branch
    centered = total - mean_of(total)
    rstd = lax.rsqrt(mean_of(centered * centered) + 1e-05)
    hat = centered * rstd
    hat_ref[...] = hat
    rstd_ref[...] = rstd
    low_ref[...] = (hat * vectors_ref[1:2] + vectors_ref[2:3]).astype(jnp.bfloat16)
    valid = valid_rows(facts_ref, tokens.shape[0], slots)
    add_rows(sums_ref, [valid * tokens * tokens, valid * branch * branch])


def attend_out(facts, own, other, own_weight, other_weight, tokens, vectors, wait=()):
    slots, width = tokens.shape
    step = slots // 4
    rows = lambda array: block((step, array.shape[1]), first, 0)
    return call(
        partial(attend_out_kernel, slots),
        "attend_out",
        (4,),
        [rows(own), rows(other), whole(own_weight), whole(other_weight), rows(tokens), whole(vectors)],
        [block((step, width), first, 0), block((step, 1), first, 0), block((step, width), first, 0), block((8, width), 0, 0)],
        [
            like((slots, width), jnp.float32),
            like((slots, 1), jnp.float32),
            like((slots, width), jnp.bfloat16),
            like((8, width), jnp.float32),
        ],
        facts,
        own,
        other,
        own_weight,
        other_weight,
        tokens,
        vectors,
        wait=wait,
    )


def up_kernel(facts_ref, rows_ref, others_ref, bias_ref, *refs):
    parts, (act_ref, slope_ref, turned_ref, weight_ref) = refs[:4], refs[4:]
    weight = near_or_far(facts_ref, parts, pl.program_id(0) < 4)
    weight_ref[...] = weight
    pre_act = [product(ref[...], weight, 1, 0) for ref in (rows_ref, others_ref)]
    pre_act = jnp.concatenate(pre_act, axis=0) + bias_ref[...]
    below = 0.5 + 0.5 * lax.erf(pre_act * 0.7071067811865476)
    act = (pre_act * below).astype(jnp.bfloat16)
    act_ref[...] = act
    turned_ref[...] = act.T
    slope = below + pre_act * (0.3989422804014327 * jnp.exp(-0.5 * pre_act * pre_act))
    slope_ref[...] = slope.astype(jnp.bfloat16)


def feed_up(facts, rows, others, bias, parts, wait=()):
    count, width = 2 * rows.shape[0], rows.shape[1]
    units = bias.shape[0]
    wide = units // 8

    def column(i, f):
        return half_at(i, f, 4) * 4 + i % 4

    shape = like((count, units), jnp.bfloat16)
    out = block((count, wide), 0, column)
    return call(
        up_kernel,
        "feed_up",
        (8,),
        [whole(rows), whole(others), block((1, wide), 0, column)] + square_columns(parts, wide, 4),
        [out, out, block((wide, count), column, 0), block((width, wide), 0, column)],
        [
            shape,
            shape,
            like((units, count), jnp.bfloat16),
            like((width, units), jnp.bfloat16),
        ],
        facts,
        rows,
        others,
        bias[None],
        *parts,
        wait=wait,
    )


def down_kernel(facts_ref, rows_ref, *refs):
    parts, (weight_ref, out_ref, total_ref) = refs[:4], refs[4:]
    step = pl.program_id(0)
    own, beside, below, across = [ref[0] for ref in parts]
    even, left = facts_ref[4] == 0, facts_ref[3] == 0
    for x in range(2):
        mine = jnp.where(even, own, beside) if x == 0 else jnp.where(even, beside, own)
        theirs = jnp.where(even, below, across) if x == 0 else jnp.where(even, across, below)
        weight_ref[x] = jnp.concatenate(
            [jnp.where(left, mine, theirs), jnp.where(left, theirs, mine)], axis=1
        )
    weight = weight_ref[...].reshape(rows_ref.shape[1], out_ref.shape[1])
    value = product(rows_ref[...], weight, 1, 0)

    @pl.when(step == 0)
    def _():
        total_ref[...] = value

    @pl.when(step > 0)
    def _():
        total_ref[...] += value

    @pl.when(step == 3)
    def _():
        out_ref[...] = total_ref[...].astype(jnp.bfloat16)


def feed_down(facts, rows, parts, wait=()):
    count, units = rows.shape
    _, block_rows, half_width = parts[0].shape
    width = 2 * half_width
    shape = (1,) + parts[0].shape[1:]
    return call(
        down_kernel,
        "feed_down",
        (4,),
        [block((count // 2, units // 4), 1, first)] + [block(shape, first, 0, 0)] * 4,
        [block((2, block_rows, width), first, 0, 0), block((count // 2, width), 0, 0)],
        [like((8, block_rows, width), jnp.bfloat16), like((count // 2, width), jnp.bfloat16)],
        facts,
        rows,
        *parts,
        scratch=[pltpu.VMEM((count // 2, width), jnp.float32)],
        wait=wait,
    )


def second_norm_kernel(
    slots, facts_ref, part_ref, other_ref, hat_ref, cotangent_ref, vectors_ref,
    mixed_ref, grad_ref, low_ref, sums_ref,
):
    branch = part_ref[...] + other_ref[...].astype(jnp.float32) + vectors_ref[0:1]
    hidden = hat_ref[...] * vectors_ref[1:2] + vectors_ref[2:3]
    gain = vectors_ref[3:4]
    total = hidden + branch
    centered = total - mean_of(total)
    rstd = lax.rsqrt(mean_of(centered * centered) + 1e-05)
    hat = centered * rstd
    mixed_ref[...] = (hat * gain + vectors_ref[4:5]).astype(jnp.bfloat16)
    valid = valid_rows(facts_ref, branch.shape[0], slots)
    grad = cotangent_ref[...].astype(jnp.float32) * valid
    scaled = grad * gain
    result = rstd * (scaled - mean_of(scaled) - hat * mean_of(scaled * hat))
    low = result.astype(jnp.bfloat16)
    grad_ref[...] = result
    low_ref[...] = low
    add_rows(sums_ref, [low.astype(jnp.float32), grad * hat, grad, valid * branch * branch])


def second_norm(facts, part, other, hat, cotangent, vectors, wait=()):
    slots, width = part.shape
    step = slots // 4
    rows = block((step, width), first, 0)
    return call(
        partial(second_norm_kernel, slots),
        "second_norm",
        (4,),
        [rows, rows, rows, rows, whole(vectors)],
        [rows, rows, rows, block((8, width), 0, 0)],
        [
            like((slots, width), jnp.bfloat16),
            like((slots, width), jnp.float32),
            like((slots, width), jnp.bfloat16),
            like((8, width), jnp.float32),
        ],
        facts,
        part,
        other,
        hat,
        cotangent,
        vectors,
        wait=wait,
    )


def first_norm_kernel(
    facts_ref, part_ref, other_ref, second_ref, hat_ref, rstd_ref, vectors_ref,
    grad_ref, low_ref, sums_ref,
):
    grad = part_ref[...] + other_ref[...].astype(jnp.float32) + second_ref[...]
    hat = hat_ref[...]
    scaled = grad * vectors_ref[1:2]
    result = rstd_ref[...] * (scaled - mean_of(scaled) - hat * mean_of(scaled * hat))
    low = result.astype(jnp.bfloat16)
    grad_ref[...] = result
    low_ref[...] = low
    add_rows(sums_ref, [low.astype(jnp.float32), grad * hat, grad])


def first_norm(facts, part, other, second, hat, rstd, vectors, wait=()):
    slots, width = part.shape
    step = slots // 4
    rows = block((step, width), first, 0)
    return call(
        first_norm_kernel,
        "first_norm",
        (4,),
        [rows, rows, rows, rows, block((step, 1), first, 0), whole(vectors)],
        [rows, rows, block((8, width), 0, 0)],
        [
            like((slots, width), jnp.float32),
            like((slots, width), jnp.bfloat16),
            like((8, width), jnp.float32),
        ],
        facts,
        part,
        other,
        second,
        hat,
        rstd,
        vectors,
        wait=wait,
    )


def act_grad_kernel(facts_ref, rows_ref, weight_ref, slope_ref, out_ref, sums_ref):
    total = product(rows_ref[...], weight_ref[...], 1, 1)
    grad = total.astype(jnp.bfloat16).astype(jnp.float32) * slope_ref[...].astype(jnp.float32)
    low = grad.astype(jnp.bfloat16)
    out_ref[...] = low
    sums_ref[...] = jnp.sum(low.astype(jnp.float32), axis=0, keepdims=True)


def act_grad(facts, rows, weight, slope, wait=()):
    count, units = slope.shape
    step = units // 8
    out = block((count, step), 0, first)
    return call(
        act_grad_kernel,
        "act_grad",
        (8,),
        [whole(rows), block((step, rows.shape[1]), first, 0), out],
        [out, block((1, step), 0, first)],
        [like((count, units), jnp.bfloat16), like((1, units), jnp.float32)],
        facts,
        rows,
        weight,
        slope,
        wait=wait,
    )


def tokens_grad_kernel(facts_ref, mine_ref, theirs_ref, weight_ref, out_ref, sent_ref):
    wide = mine_ref.shape[1]
    slots = out_ref.shape[0]
    half = facts_ref[3]
    mine = weight_ref[:, pl.ds(pl.multiple_of(half * wide, 128), wide)]
    theirs = weight_ref[:, pl.ds(pl.multiple_of((1 - half) * wide, 128), wide)]
    total = product(mine_ref[...], mine, 1, 1) + product(theirs_ref[...], theirs, 1, 1)
    out_ref[...] = total[:slots]
    sent_ref[...] = total[slots:].astype(sent_ref.dtype)


def tokens_grad(facts, mine, theirs, weight, wait=(), through=()):
    count, columns = mine.shape
    width = weight.shape[0]
    step = width // 4
    out = block((count // 2, step), 0, first)
    return call(
        tokens_grad_kernel,
        "tokens_grad",
        (4,),
        [whole(mine), whole(theirs), block((step, 2 * columns), first, 0)],
        [out, out],
        [
            like((count // 2, width), jnp.float32),
            like((count // 2, width), jnp.bfloat16),
        ],
        facts,
        mine,
        theirs,
        weight,
        wait=wait,
        through=through,
    )


def add_parts_kernel(facts_ref, own_ref, got_ref, kept_ref, sent_ref):
    step = pl.program_id(0)
    total = own_ref[...].astype(jnp.float32) + got_ref[...].astype(jnp.float32)
    total = total.astype(jnp.bfloat16)

    @pl.when(step < 2)
    def _():
        sent_ref[...] = total

    @pl.when(step >= 2)
    def _():
        kept_ref[...] = total


def add_last_kernel(facts_ref, own_ref, got_ref, kept_ref, sent_ref):
    total = own_ref[0].astype(jnp.float32) + got_ref[0].astype(jnp.float32)
    total = total.astype(jnp.bfloat16)

    @pl.when(pl.program_id(0) == 0)
    def _():
        sent_ref[...] = total

    @pl.when(pl.program_id(0) == 1)
    def _():
        kept_ref[...] = total


def add_last(facts, own, got, wait=(), through=()):
    _, rows, columns = own.shape
    part = block((1, rows, columns), lambda i, f: jnp.where(i == 0, 1 - f[6], f[6]), 0, 0)
    shape = like((rows, columns), jnp.bfloat16)
    out = block((rows, columns), 0, 0)
    return call(
        add_last_kernel,
        "add_last",
        (2,),
        [part, part],
        [out, out],
        [shape, shape],
        facts,
        own,
        got,
        wait=wait,
        through=through,
    )


def add_parts(facts, own, got, wait=(), through=()):
    _, rows, columns = own.shape
    shape = (1, rows, columns)
    part = block(shape, lambda i, f: 2 * (i % 2) + jnp.where(i < 2, 1 - f[7], f[7]), 0, 0)
    half = like((2, rows, columns), jnp.bfloat16)
    return call(
        add_parts_kernel,
        "add_parts",
        (4,),
        [part, part],
        [
            block(shape, lambda i, *_: jnp.maximum(i - 2, 0), 0, 0),
            block(shape, lambda i, *_: jnp.minimum(i, 1), 0, 0),
        ],
        [half, half],
        facts,
        own,
        got,
        wait=wait,
        through=through,
    )


def alternate(value, width, offset):
    starts = range(offset * width, value.shape[1], 2 * width)
    return jnp.concatenate([value[:, start : start + width] for start in starts], axis=1)


def deal_kernel(unit_block, core_ref, query_ref, key_ref, value_ref, up_ref, *refs):
    first_core = core_ref[0] == 0
    near = [ref[...] for ref in (query_ref, key_ref, value_ref)]
    even = jnp.concatenate([alternate(value, HD, 0) for value in near], axis=1)
    odd = jnp.concatenate([alternate(value, HD, 1) for value in near], axis=1)
    up = up_ref[...]
    up_even, up_odd = alternate(up, unit_block, 0), alternate(up, unit_block, 1)
    refs[0][...] = jnp.where(first_core, even, odd)
    refs[1][...] = jnp.where(first_core, odd, even)
    refs[2][...] = jnp.where(first_core, up_even, up_odd)
    refs[3][...] = jnp.where(first_core, up_odd, up_even)


def deal(core, query, key, value, up, unit_block):
    near = like((query.shape[0], 3 * query.shape[1] // 2), jnp.bfloat16)
    half = like((up.shape[0], up.shape[1] // 2), jnp.bfloat16)
    shapes = [near, near, half, half]
    return call(
        partial(deal_kernel, unit_block),
        "deal",
        (1,),
        [whole(value) for value in (query, key, value, up)],
        [whole(shape) for shape in shapes],
        shapes,
        core,
        query,
        key,
        value,
        up,
    )


def lay_out_kernel(core_ref, near_ref, near_got_ref, out_ref, up_ref, up_got_ref, *refs):
    first_core = core_ref[0] == 0
    near, near_got, up, up_got = [
        ref[...] for ref in (near_ref, near_got_ref, up_ref, up_got_ref)
    ]
    out = out_ref[...]
    wide = out.shape[1] // 2
    near_rows = jnp.concatenate(
        [jnp.where(first_core, near, near_got), jnp.where(first_core, near_got, near)], axis=0
    )
    out_rows = jnp.concatenate([out[:, :wide], out[:, wide:]], axis=0)
    refs[0][...] = jnp.concatenate([near_rows, out_rows], axis=1)
    refs[1][...] = jnp.concatenate(
        [jnp.where(first_core, up, up_got), jnp.where(first_core, up_got, up)], axis=0
    )


def lay_out(core, near, near_got, out, up, up_got):
    rows = 2 * near.shape[0]
    shapes = [
        like((rows, near.shape[1] + out.shape[1] // 2), jnp.bfloat16),
        like((rows, up.shape[1]), jnp.bfloat16),
    ]
    arrays = (near, near_got, out, up, up_got)
    return call(
        lay_out_kernel,
        "lay_out",
        (1,),
        [whole(value) for value in arrays],
        [whole(shape) for shape in shapes],
        shapes,
        core,
        *arrays,
    )[0]


def split_body(
    tokens,
    lengths,
    cotangent,
    query_weight,
    key_weight,
    value_weight,
    out_weight,
    up_weight,
    down_weight,
    query_bias,
    value_bias,
    out_bias,
    attn_gain,
    attn_shift,
    up_bias,
    down_bias,
    feed_gain,
    feed_shift,
):
    core = lax.axis_index("c")
    half = lax.axis_index("s")
    row_count, width = tokens.shape[1:]
    slots = 2 * row_count
    unit_block = down_weight.shape[0]
    units = up_bias.shape[0] // 2
    cols = width // 2
    wide = cols // 2

    def to_sequence(values):
        return jnp.concatenate([pick(values, half, 0), swap(pick(values, 1 - half, 0), "s")], axis=0)

    def from_sequence(values):
        return in_order(values[:row_count], swap(values[row_count:], "s"), half)

    place = jnp.stack([core]).astype(jnp.int32)
    (near_kept, near_sent, up_kept, up_sent), place = deal(
        place, query_weight, key_weight, value_weight, up_weight, unit_block
    )
    near_mine, up_mine = lay_out(
        place, near_kept, swap(near_sent, "c"), out_weight, up_kept, swap(up_sent, "c")
    )
    rows, up_cols = up_mine.shape
    line = lax.axis_index("z")
    length_own = lax.dynamic_slice_in_dim(lengths, half, 1, 0)
    facts = jnp.concatenate(
        [
            both(length_own, "c"),
            jnp.stack(
                [
                    half * row_count,
                    half,
                    lax.axis_index("x"),
                    jnp.int32(0),
                    line // 2,
                    line % 2,
                ]
            ).astype(jnp.int32),
        ]
    )
    tokens_own = to_sequence(tokens)
    cotangent_own = to_sequence(cotangent)
    (near, up_mine, down_mine), facts = stack_pair(
        facts,
        near_mine,
        line_cross(near_mine),
        wait=(tokens_own,),
        through=(up_mine, down_weight),
    )
    near, facts = stack_line(facts, near, line_next(near), wait=(cotangent_own,))
    near_parts = gather_square(near, "x")
    up_pairs, facts = stack_pair(facts, up_mine, line_cross(up_mine), wait=(near,))
    tokens_both = both(tokens_own, "c")
    up_part, facts = stack_line(
        facts, up_pairs, line_next(up_pairs), wait=(near_parts[1], near_parts[2])
    )
    up_parts = gather_square(up_part, "s")
    down_pairs, facts = stack_pair(facts, down_mine, line_cross(down_mine), wait=(up_part,))
    def halves_of(vector, size):
        return pick(vector.reshape(-1, 2, size), core, 1).reshape(-1)

    query_part = halves_of(query_bias, HD).reshape(2, wide)
    value_part = halves_of(value_bias, HD).reshape(2, wide)
    in_bias = jnp.stack([query_part, jnp.zeros_like(query_part), value_part], axis=1).reshape(-1)
    (projected, in_weight, out_own), facts = project(
        facts, tokens_both, in_bias, near_parts, wait=(down_pairs, up_parts[2])
    )
    out_own = out_own.reshape(cols, width)
    out_other = swap(out_own, "c")
    down_part, facts = stack_line(facts, down_pairs, line_next(down_pairs), wait=(projected,))
    down_parts = gather_square(down_part, "x")
    (heads_out, totals), facts = attend(facts, projected, slots)
    heads_other = swap(heads_out[slots:], "c")
    vectors = jnp.stack(
        [out_bias, attn_gain, attn_shift, down_bias, feed_gain, feed_shift, out_bias, out_bias]
    )
    (first_hat, first_rstd, hidden_low, first_sums), facts = attend_out(
        facts,
        heads_out,
        heads_other,
        out_own,
        out_other,
        tokens_own,
        vectors,
        wait=(up_parts[1], down_parts[2]),
    )
    tokens_t, facts = turn_all(facts, tokens_both, wait=(hidden_low,))
    (hidden_low,), facts = gate(facts, (hidden_low,), (up_parts[3], down_parts[1]))
    hidden_from = swap(hidden_low, "c")
    (activation, slope, act_t, up_all), facts = feed_up(
        facts, hidden_low, hidden_from, halves_of(up_bias, unit_block), up_parts
    )
    hidden_turned, facts = turn(facts, hidden_low, hidden_from, rows, wait=(act_t,))
    (down_all, feed_sent), facts = feed_down(facts, activation, down_parts)
    down_all = down_all.reshape(units, width)
    feed_other = swap(feed_sent, "c")
    feed_part = product(activation[:slots], down_all, 1, 0)
    feed_vectors = jnp.stack(
        [down_bias, attn_gain, attn_shift, feed_gain, feed_shift, out_bias, out_bias, out_bias]
    )
    (mixed, second_grad, feed_low, second_sums), facts = second_norm(
        facts, feed_part, feed_other, first_hat, cotangent_own, feed_vectors
    )

    feed_both = both(feed_low, "c")
    feed_mine, feed_theirs = columns_of(feed_both, half), columns_of(feed_both, 1 - half)
    down_sent = grad_block(act_t, feed_theirs)
    down_got = swap(down_sent, "s")
    (pre_grad, up_bias_grad), facts = act_grad(
        facts, feed_both, down_all, slope, wait=(down_sent,)
    )
    hidden_sent = product(pre_grad[slots:], up_all, 1, 1).astype(jnp.bfloat16)
    hidden_other = swap(hidden_sent, "c")
    hidden_own_t, hidden_other_t = hidden_turned
    up_sent = grad_block(hidden_other_t, pre_grad)
    up_got = swap(up_sent, "x")
    hidden_part = product(pre_grad[:slots], up_all, 1, 1)
    (first_grad, attn_low, third_sums), facts = first_norm(
        facts,
        hidden_part,
        hidden_other,
        second_grad,
        first_hat,
        first_rstd,
        vectors,
        wait=(up_sent,),
    )
    grad_sent = product(attn_low, out_other, 1, 1).astype(jnp.bfloat16)
    grad_other = swap(grad_sent, "c")
    grad_own = product(attn_low, out_own, 1, 1).astype(jnp.bfloat16)
    out_sent = product(heads_other, attn_low, 0, 0).astype(jnp.bfloat16)
    out_got = swap(out_sent, "c")
    heads_grad = jnp.concatenate([grad_own, grad_other], axis=0)
    (theirs_low, theirs_sums), facts = attend_back(
        facts, projected, heads_grad, totals, slots, False, wait=(out_sent,)
    )
    in_sent = grad_block(tokens_t, theirs_low)
    in_got = swap(in_sent, "s")
    down_total = grad_block(act_t, feed_mine, down_got)
    down_kept, down_sent = halve(down_total.reshape(4, 2, unit_block, cols), "x", 1)
    down_got = swap(down_sent, "x")
    out_grad = grad_block(heads_out[:slots].T, attn_low, out_got)
    out_line = out_grad.reshape((4, 2 * out_weight.shape[0], width))
    out_kept, out_sent = line_parts(out_line)
    out_got = lax.ppermute(out_sent, "z", NEXT)
    (mine_low, mine_sums), facts = attend_back(
        facts, projected, heads_grad, totals, slots, True, wait=(in_sent, out_sent, down_sent)
    )
    up_total = grad_block(hidden_own_t, pre_grad, up_got).reshape(4, rows, 2 * up_cols)
    up_kept, up_sent = columns_of(up_total, half), columns_of(up_total, 1 - half)
    up_got = swap(up_sent, "s")
    out_total = add(out_kept, out_got)
    valid_count = length_own[0].astype(jnp.float32) * width
    stats = jnp.stack(
        [jnp.sum(first_sums[0]), jnp.sum(first_sums[1]), jnp.sum(second_sums[3]), valid_count]
    )
    mine_sums, theirs_sums = jnp.sum(mine_sums, axis=(0, 1)), jnp.sum(theirs_sums, axis=(0, 1))
    late = in_order(mine_sums, theirs_sums, half)
    sums = jnp.concatenate(
        [
            second_sums[:3].reshape(-1),
            third_sums[:3].reshape(-1),
            jnp.pad(stats, (0, 124)),
            up_bias_grad[0],
            late[:, :wide].reshape(-1),
            late[:, 2 * wide :].reshape(-1),
        ]
    )
    sums = sums + lax.ppermute(sums, "z", NEXT)
    (tokens_part, tokens_sent), facts = tokens_grad(
        facts,
        mine_low,
        theirs_low,
        in_weight,
        wait=(up_sent, out_total, sums),
    )
    in_total = grad_block(tokens_t, mine_low, in_got)
    in_kept, in_sent = halve(in_total.reshape(4, 2, rows, 3 * wide), "x", 1)
    in_got = swap(in_sent, "x")
    tokens_other = swap(tokens_sent, "c")
    (down_pairs, down_next), facts = add_parts(
        facts, down_kept, down_got, wait=(in_sent, tokens_part)
    )
    down_got = lax.ppermute(down_next, "z", NEXT)
    upper = lax.axis_index("z") // 2
    out_kept, out_sent = pick(out_total, upper, 0), pick(out_total, 1 - upper, 0)
    out_kept = add(out_kept, lax.ppermute(out_sent, "z", CROSS))
    (in_pairs, in_next), facts = add_parts(
        facts, in_kept, in_got, wait=(down_next, out_kept)
    )
    in_got = lax.ppermute(in_next, "z", NEXT)
    (down_kept, down_sent), facts = add_last(facts, down_pairs, down_got, wait=(in_next,))
    (up_pairs, up_next), facts = add_parts(facts, up_kept, up_got, wait=(down_sent,))
    up_got = lax.ppermute(up_next, "z", NEXT)
    (in_kept, in_sent, out_kept, mixed), facts = add_last(
        facts, in_pairs, in_got, wait=(up_next,), through=(out_kept, mixed)
    )
    (up_kept, up_sent, sums), facts = add_last(
        facts, up_pairs, up_got, wait=(in_sent,), through=(sums,)
    )
    sums = sums + swap(sums, "x")
    sums = sums + swap(sums, "s")
    in_sum = add(in_kept, lax.ppermute(in_sent, "z", CROSS))
    tokens_grad_sum = tokens_part + tokens_other.astype(jnp.float32) + first_grad
    tokens_grad_sum = from_sequence(tokens_grad_sum.astype(jnp.bfloat16))
    mixed = in_order(mixed[:row_count], swap(mixed[row_count:], "s"), half)
    down_sum = add(down_kept, lax.ppermute(down_sent, "z", CROSS))
    up_sum = add(up_kept, lax.ppermute(up_sent, "z", CROSS))
    out_sum = fold_columns(fold(out_kept.reshape(2, out_weight.shape[0], width), "x", 0))

    sums = sums + lax.ppermute(sums, "z", CROSS)
    both_sums = in_order(sums, swap(sums, "c"), core)
    count = 6 * width + 128
    shared = both_sums[0, :count] + both_sums[1, :count]
    down_bias_grad, feed_gain_grad, feed_shift_grad, out_bias_grad, attn_gain_grad, attn_shift_grad = [
        shared[i * width : (i + 1) * width] for i in range(6)
    ]
    stats = shared[6 * width : 6 * width + 4]

    def interleave(start, size, block_size):
        sums = both_sums[:, start : start + size].reshape(2, -1, block_size)
        return sums.transpose(1, 0, 2).reshape(-1)

    up_bias_grad = interleave(count, units, unit_block)
    query_bias_grad = interleave(count + units, cols, HD)
    value_bias_gradient = interleave(count + units + cols, cols, HD)
    stream_rms = jnp.sqrt(stats[:3] / stats[3])

    def give_back(total):
        total = total.reshape((2, rows // 2) + total.shape[1:])
        return pick(total, core, 0), swap(pick(total, 1 - core, 0), "c")

    up_shares = give_back(up_sum)
    in_shares = give_back(in_sum)
    down_weight_grad = down_sum.astype(jnp.float32)
    out_weight_grad = out_sum.astype(jnp.float32)

    def merge(shares, start, size, block):
        one, two = [
            share[:, start : start + size].reshape(rows // 2, -1, block) for share in shares
        ]
        first = jnp.where(core == 0, one, two)
        second = jnp.where(core == 0, two, one)
        return jnp.stack([first, second], axis=2).reshape(rows // 2, -1).astype(jnp.float32)

    query_weight_grad = merge(in_shares, 0, wide, HD)
    key_weight_grad = merge(in_shares, wide, wide, HD)
    value_weight_grad = merge(in_shares, 2 * wide, wide, HD)
    up_weight_grad = merge(up_shares, 0, up_cols, unit_block)
    return (
        mixed,
        tokens_grad_sum,
        query_weight_grad,
        key_weight_grad,
        value_weight_grad,
        out_weight_grad,
        up_weight_grad,
        down_weight_grad,
        query_bias_grad,
        value_bias_gradient,
        out_bias_grad,
        attn_gain_grad,
        attn_shift_grad,
        up_bias_grad,
        down_bias_grad,
        feed_gain_grad,
        feed_shift_grad,
        stream_rms,
    )


def solution(mesh):
    devices = mesh.devices
    dp_count, seq_count = devices.shape
    split = seq_count == 2 and dp_count == 16
    if split:
        inner = jax.sharding.Mesh(devices.reshape(4, 2, 2, seq_count), ("z", "x", "c", "s"))
        dp, seq, body = ("z", "x", "c"), "s", split_body
    else:
        inner, dp, seq, body = mesh, "dp", "seq", general_body
    weights = (P(dp, seq),) * 6
    vectors = (P(),) * 9
    rows = P(dp, seq, None)
    in_specs = (rows, P(dp), rows) + weights + vectors
    out_specs = (rows, rows) + weights + vectors + (P(),)
    return jax.shard_map(body, mesh=inner, in_specs=in_specs, out_specs=out_specs, check_vma=False)
```

```python
from functools import partial
import math

import jax
import jax.numpy as jnp
from jax import lax
from jax.experimental import pallas as pl
from jax.experimental.pallas import tpu as pltpu
from jax.sharding import PartitionSpec as P

HD = 64


def layer_norm(values_in, gain_vector, shift_vector):
    mean_value = jnp.mean(values_in, axis=-1, keepdims=True)
    centered = values_in - mean_value
    variance = jnp.mean(centered * centered, axis=-1, keepdims=True)
    return centered * lax.rsqrt(variance + 1e-05) * gain_vector + shift_vector


def gather_weights(first, second, third, fourth, fifth, sixth):
    part = (
        lax.all_gather(first, "dp", axis=0, tiled=True),
        lax.all_gather(second, "dp", axis=0, tiled=True),
        lax.all_gather(third, "dp", axis=0, tiled=True),
        lax.all_gather(fourth, "dp", axis=0, tiled=True),
        lax.all_gather(fifth, "dp", axis=0, tiled=True),
        lax.all_gather(sixth, "dp", axis=0, tiled=True),
    )
    return (
        lax.all_gather(part[0], "seq", axis=1, tiled=True),
        lax.all_gather(part[1], "seq", axis=1, tiled=True),
        lax.all_gather(part[2], "seq", axis=1, tiled=True),
        lax.all_gather(part[3], "seq", axis=1, tiled=True),
        lax.all_gather(part[4], "seq", axis=1, tiled=True),
        lax.all_gather(part[5], "seq", axis=1, tiled=True),
    )


def reduce_grads(first, second, third, fourth, fifth, sixth):
    part = (
        lax.psum_scatter(first.astype(jnp.bfloat16), "seq", scatter_dimension=1, tiled=True).astype(
            jnp.float32
        ),
        lax.psum_scatter(
            second.astype(jnp.bfloat16), "seq", scatter_dimension=1, tiled=True
        ).astype(jnp.float32),
        lax.psum_scatter(third.astype(jnp.bfloat16), "seq", scatter_dimension=1, tiled=True).astype(
            jnp.float32
        ),
        lax.psum_scatter(
            fourth.astype(jnp.bfloat16), "seq", scatter_dimension=1, tiled=True
        ).astype(jnp.float32),
        lax.psum_scatter(fifth.astype(jnp.bfloat16), "seq", scatter_dimension=1, tiled=True).astype(
            jnp.float32
        ),
        lax.psum_scatter(sixth.astype(jnp.bfloat16), "seq", scatter_dimension=1, tiled=True).astype(
            jnp.float32
        ),
    )
    return (
        lax.psum_scatter(
            part[0].astype(jnp.bfloat16), "dp", scatter_dimension=0, tiled=True
        ).astype(jnp.float32),
        lax.psum_scatter(
            part[1].astype(jnp.bfloat16), "dp", scatter_dimension=0, tiled=True
        ).astype(jnp.float32),
        lax.psum_scatter(
            part[2].astype(jnp.bfloat16), "dp", scatter_dimension=0, tiled=True
        ).astype(jnp.float32),
        lax.psum_scatter(
            part[3].astype(jnp.bfloat16), "dp", scatter_dimension=0, tiled=True
        ).astype(jnp.float32),
        lax.psum_scatter(
            part[4].astype(jnp.bfloat16), "dp", scatter_dimension=0, tiled=True
        ).astype(jnp.float32),
        lax.psum_scatter(
            part[5].astype(jnp.bfloat16), "dp", scatter_dimension=0, tiled=True
        ).astype(jnp.float32),
    )


def block_layout(seq_count, row_count, head_count):
    block_seqs = math.gcd(seq_count, max(1, 512 // row_count))
    group_heads = math.gcd(head_count, 4)
    return (block_seqs, seq_count // block_seqs, group_heads, head_count // group_heads)


def head_slice(block_part, offset, group_width, group_heads):
    sliced = lax.dynamic_slice_in_dim(block_part, offset, group_width, 2)
    return sliced.reshape(sliced.shape[0], sliced.shape[1], group_heads, HD)


def attention_forward(queries, key_all, value_all, key_mask):
    seq_count, row_count, feature_total = queries.shape
    slot_count = key_all.shape[1]
    block_seqs, block_count, group_heads, group_count = block_layout(
        seq_count, row_count, feature_total // HD
    )
    group_width = group_heads * HD

    def seq_block(inputs):
        query_part, key_part, value_part, mask_part = inputs

        def head_block(group_index):
            offset = group_index * group_width
            query_heads = head_slice(query_part, offset, group_width, group_heads)
            key_heads = head_slice(key_part, offset, group_width, group_heads)
            value_heads = head_slice(value_part, offset, group_width, group_heads)
            scores = (
                jnp.einsum(
                    "brhd,bkhd->bhrk", query_heads, key_heads, preferred_element_type=jnp.float32
                )
                * 0.125
            )
            scores = jnp.where(mask_part[:, None, None, :], scores, -1e30)
            row_max = jnp.max(scores, axis=-1, keepdims=True)
            exponent = jnp.exp(scores - row_max)
            row_total = jnp.sum(exponent, axis=-1, keepdims=True)
            soft_probs = (exponent / row_total).astype(jnp.bfloat16)
            heads_out = jnp.einsum(
                "bhrk,bkhd->brhd", soft_probs, value_heads, preferred_element_type=jnp.float32
            )
            log_total = (row_max + jnp.log(row_total))[..., 0]
            return (heads_out.reshape(block_seqs, row_count, group_width), log_total)

        return lax.map(head_block, jnp.arange(group_count))

    outputs, log_totals = lax.map(
        seq_block,
        (
            queries.reshape(block_count, block_seqs, row_count, feature_total),
            key_all.reshape(block_count, block_seqs, slot_count, feature_total),
            value_all.reshape(block_count, block_seqs, slot_count, feature_total),
            key_mask.reshape(block_count, block_seqs, slot_count),
        ),
    )
    mixed_heads = outputs.transpose(0, 2, 3, 1, 4).reshape(seq_count, row_count, feature_total)
    return (mixed_heads, log_totals)


def attention_backward(queries, key_all, value_all, key_mask, heads_grad, log_totals):
    seq_count, row_count, feature_total = queries.shape
    slot_count = key_all.shape[1]
    block_seqs, block_count, group_heads, group_count = block_layout(
        seq_count, row_count, feature_total // HD
    )
    group_width = group_heads * HD

    def seq_block(inputs):
        query_part, key_part, value_part, mask_part, grad_part, total_part = inputs

        def head_block(group_index):
            offset = group_index * group_width
            query_heads = head_slice(query_part, offset, group_width, group_heads)
            key_heads = head_slice(key_part, offset, group_width, group_heads)
            value_heads = head_slice(value_part, offset, group_width, group_heads)
            grad_heads = head_slice(grad_part, offset, group_width, group_heads)
            log_total = lax.dynamic_index_in_dim(total_part, group_index, 0, keepdims=False)
            scores = (
                jnp.einsum(
                    "brhd,bkhd->bhrk", query_heads, key_heads, preferred_element_type=jnp.float32
                )
                * 0.125
            )
            scores = jnp.where(mask_part[:, None, None, :], scores, -1e30)
            soft_probs = jnp.exp(scores - log_total[..., None])
            value_grad = jnp.einsum(
                "bhrk,brhd->bkhd",
                soft_probs.astype(jnp.bfloat16),
                grad_heads,
                preferred_element_type=jnp.float32,
            )
            prob_grad = jnp.einsum(
                "brhd,bkhd->bhrk", grad_heads, value_heads, preferred_element_type=jnp.float32
            )
            inner = jnp.sum(soft_probs * prob_grad, axis=-1, keepdims=True)
            score_grad = (soft_probs * (prob_grad - inner)).astype(jnp.bfloat16)
            query_grad = (
                jnp.einsum(
                    "bhrk,bkhd->brhd", score_grad, key_heads, preferred_element_type=jnp.float32
                )
                * 0.125
            )
            key_grad = (
                jnp.einsum(
                    "bhrk,brhd->bkhd", score_grad, query_heads, preferred_element_type=jnp.float32
                )
                * 0.125
            )
            return (
                query_grad.reshape(block_seqs, row_count, group_width),
                key_grad.reshape(block_seqs, slot_count, group_width),
                value_grad.reshape(block_seqs, slot_count, group_width),
            )

        return lax.map(head_block, jnp.arange(group_count))

    query_blocks, key_blocks, value_block_list = lax.map(
        seq_block,
        (
            queries.reshape(block_count, block_seqs, row_count, feature_total),
            key_all.reshape(block_count, block_seqs, slot_count, feature_total),
            value_all.reshape(block_count, block_seqs, slot_count, feature_total),
            key_mask.reshape(block_count, block_seqs, slot_count),
            heads_grad.reshape(block_count, block_seqs, row_count, feature_total),
            log_totals,
        ),
    )
    query_grad = query_blocks.transpose(0, 2, 3, 1, 4).reshape(seq_count, row_count, feature_total)
    key_grad = key_blocks.transpose(0, 2, 3, 1, 4).reshape(seq_count, slot_count, feature_total)
    value_grad = value_block_list.transpose(0, 2, 3, 1, 4).reshape(
        seq_count, slot_count, feature_total
    )
    return (query_grad, key_grad, value_grad)


def general_body(
    tokens,
    lengths,
    cotangent,
    query_weight,
    key_weight,
    value_weight,
    out_weight,
    up_weight,
    down_weight,
    query_bias,
    value_bias,
    out_bias,
    attn_gain,
    attn_shift,
    up_bias,
    down_bias,
    feed_gain,
    feed_shift,
):
    seq_count, row_count, feature_total = tokens.shape
    slot_count = row_count * lax.axis_size("seq")
    token_count = seq_count * row_count
    whole = gather_weights(
        query_weight, key_weight, value_weight, out_weight, up_weight, down_weight
    )
    full_query, full_key, full_value, full_out, full_up, full_down = whole
    flat_tokens = tokens.reshape(token_count, feature_total)
    queries = (
        jnp.dot(flat_tokens, full_query, preferred_element_type=jnp.float32) + query_bias
    ).astype(jnp.bfloat16)
    key_rows = jnp.dot(flat_tokens, full_key, preferred_element_type=jnp.float32).astype(
        jnp.bfloat16
    )
    value_rows = (
        jnp.dot(flat_tokens, full_value, preferred_element_type=jnp.float32) + value_bias
    ).astype(jnp.bfloat16)
    first_slot = lax.axis_index("seq") * row_count
    key_mask = jnp.arange(slot_count)[None, :] < lengths[:, None]
    row_valid = ((first_slot + jnp.arange(row_count))[None, :] < lengths[:, None]).astype(
        jnp.float32
    )
    row_valid = row_valid.reshape(token_count, 1)
    query_blocks = queries.reshape(seq_count, row_count, feature_total)
    key_blocks = key_rows.reshape(seq_count, row_count, feature_total)
    value_block_list = value_rows.reshape(seq_count, row_count, feature_total)
    key_all, value_all = (
        lax.all_gather(key_blocks, "seq", axis=1, tiled=True),
        lax.all_gather(value_block_list, "seq", axis=1, tiled=True),
    )
    mixed_heads, log_totals = attention_forward(query_blocks, key_all, value_all, key_mask)
    heads_low = mixed_heads.reshape(token_count, feature_total).astype(jnp.bfloat16)
    attention_out = jnp.dot(heads_low, full_out, preferred_element_type=jnp.float32) + out_bias
    tokens_f32 = flat_tokens.astype(jnp.float32)
    first_sum = tokens_f32 + attention_out
    hidden, first_pull = jax.vjp(layer_norm, first_sum, attn_gain, attn_shift)
    hidden_low = hidden.astype(jnp.bfloat16)
    pre_act = jnp.dot(hidden_low, full_up, preferred_element_type=jnp.float32) + up_bias
    gelu_out, gelu_pull = jax.vjp(partial(jax.nn.gelu, approximate=False), pre_act)
    activation = gelu_out.astype(jnp.bfloat16)
    feed_out = jnp.dot(activation, full_down, preferred_element_type=jnp.float32) + down_bias
    result, second_pull = jax.vjp(layer_norm, hidden + feed_out, feed_gain, feed_shift)
    mixed = result.astype(jnp.bfloat16).reshape(seq_count, row_count, feature_total)
    partial_stats = jnp.stack(
        [
            jnp.sum(row_valid * tokens_f32 * tokens_f32),
            jnp.sum(row_valid * attention_out * attention_out),
            jnp.sum(row_valid * feed_out * feed_out),
            jnp.sum(row_valid) * feature_total,
        ]
    )
    back_weights = gather_weights(
        query_weight, key_weight, value_weight, out_weight, up_weight, down_weight
    )
    back_query, back_key, back_value, back_out, back_up, back_down = back_weights
    out_grad = cotangent.reshape(token_count, feature_total).astype(jnp.float32) * row_valid
    second_grad, feed_gain_grad, feed_shift_grad = second_pull(out_grad)
    feed_low = second_grad.astype(jnp.bfloat16)
    down_weight_grad = jnp.einsum(
        "nf,nd->fd", activation, feed_low, preferred_element_type=jnp.float32
    )
    down_bias_grad = jnp.sum(feed_low, axis=0, dtype=jnp.float32)
    act_grad = jnp.einsum(
        "nd,fd->nf", feed_low, back_down, preferred_element_type=jnp.float32
    ).astype(jnp.bfloat16)
    pre_grad = gelu_pull(act_grad.astype(jnp.float32))[0].astype(jnp.bfloat16)
    up_weight_grad = jnp.einsum(
        "nd,nf->df", hidden_low, pre_grad, preferred_element_type=jnp.float32
    )
    up_bias_grad = jnp.sum(pre_grad, axis=0, dtype=jnp.float32)
    hidden_grad = (
        jnp.einsum("nf,df->nd", pre_grad, back_up, preferred_element_type=jnp.float32) + second_grad
    )
    first_grad, attn_gain_grad, attn_shift_grad = first_pull(hidden_grad)
    attn_low = first_grad.astype(jnp.bfloat16)
    out_weight_grad = jnp.einsum(
        "nd,ne->de", heads_low, attn_low, preferred_element_type=jnp.float32
    )
    out_bias_grad = jnp.sum(attn_low, axis=0, dtype=jnp.float32)
    heads_grad = jnp.einsum(
        "ne,de->nd", attn_low, back_out, preferred_element_type=jnp.float32
    ).astype(jnp.bfloat16)
    heads_grad = heads_grad.reshape(seq_count, row_count, feature_total)
    query_grad, key_part_grad, value_part_grad = attention_backward(
        query_blocks, key_all, value_all, key_mask, heads_grad, log_totals
    )
    key_sum, value_sum = (
        lax.psum_scatter(
            key_part_grad.astype(jnp.bfloat16), "seq", scatter_dimension=1, tiled=True
        ).astype(jnp.float32),
        lax.psum_scatter(
            value_part_grad.astype(jnp.bfloat16), "seq", scatter_dimension=1, tiled=True
        ).astype(jnp.float32),
    )
    query_low = query_grad.reshape(token_count, feature_total).astype(jnp.bfloat16)
    key_low = key_sum.reshape(token_count, feature_total).astype(jnp.bfloat16)
    value_low = value_sum.reshape(token_count, feature_total).astype(jnp.bfloat16)
    query_weight_grad = jnp.einsum(
        "nd,ne->de", flat_tokens, query_low, preferred_element_type=jnp.float32
    )
    key_weight_grad = jnp.einsum(
        "nd,ne->de", flat_tokens, key_low, preferred_element_type=jnp.float32
    )
    value_weight_grad = jnp.einsum(
        "nd,ne->de", flat_tokens, value_low, preferred_element_type=jnp.float32
    )
    query_bias_grad = jnp.sum(query_low, axis=0, dtype=jnp.float32)
    value_bias_gradient = jnp.sum(value_low, axis=0, dtype=jnp.float32)
    tokens_grad = (
        jnp.einsum("ne,de->nd", query_low, back_query, preferred_element_type=jnp.float32)
        + jnp.einsum("ne,de->nd", key_low, back_key, preferred_element_type=jnp.float32)
        + jnp.einsum("ne,de->nd", value_low, back_value, preferred_element_type=jnp.float32)
        + first_grad
    )
    tokens_grad = tokens_grad.astype(jnp.bfloat16).reshape(seq_count, row_count, feature_total)
    matrix_grads = reduce_grads(
        query_weight_grad,
        key_weight_grad,
        value_weight_grad,
        out_weight_grad,
        up_weight_grad,
        down_weight_grad,
    )
    totals = lax.psum(
        (
            partial_stats,
            query_bias_grad,
            value_bias_gradient,
            out_bias_grad,
            attn_gain_grad,
            attn_shift_grad,
            up_bias_grad,
            down_bias_grad,
            feed_gain_grad,
            feed_shift_grad,
        ),
        ("dp", "seq"),
    )
    stream_rms = jnp.sqrt(totals[0][:3] / totals[0][3])
    return (
        mixed,
        tokens_grad,
        matrix_grads[0],
        matrix_grads[1],
        matrix_grads[2],
        matrix_grads[3],
        matrix_grads[4],
        matrix_grads[5],
        totals[1],
        totals[2],
        totals[3],
        totals[4],
        totals[5],
        totals[6],
        totals[7],
        totals[8],
        totals[9],
        stream_rms,
    )


def swap(value, axis):
    return lax.ppermute(value, axis, [(0, 1), (1, 0)])


def both(value, axis):
    return jnp.concatenate([value, swap(value, axis)], axis=0)


def in_order(own, other, index, axis=0):
    return jnp.where(
        index == 0, jnp.stack([own, other], axis=axis), jnp.stack([other, own], axis=axis)
    )


def pick(values, index, axis):
    return lax.dynamic_index_in_dim(values, index, axis, keepdims=False)


def add(left, right):
    return (left.astype(jnp.float32) + right.astype(jnp.float32)).astype(jnp.bfloat16)


def fold(values, axis, dim):
    index = lax.axis_index(axis)
    return add(pick(values, index, dim), swap(pick(values, 1 - index, dim), axis))


NEXT = [(0, 1), (1, 0), (2, 3), (3, 2)]
CROSS = [(0, 2), (2, 0), (1, 3), (3, 1)]


def fold_cross(pairs):
    upper = lax.axis_index("z") // 2
    return add(pick(pairs, upper, 0), lax.ppermute(pick(pairs, 1 - upper, 0), "z", CROSS))


def fold_line(values):
    odd = lax.axis_index("z") % 2
    pairs = values.reshape((2, 2) + values.shape[1:])
    sent = lax.ppermute(pick(pairs, 1 - odd, 1), "z", NEXT)
    return fold_cross(add(pick(pairs, odd, 1), sent))


def line_cross(value):
    return lax.ppermute(value, "z", CROSS)


def line_next(pair):
    return lax.ppermute(pair, "z", NEXT)


def gather_square(own, way):
    beside, below = swap(own, "x"), swap(own, "s")
    across = swap(below, "x") if way == "x" else swap(beside, "s")
    return [own, beside, below, across]


def fold_columns(total):
    half = lax.axis_index("s")
    return add(columns_of(total, half), swap(columns_of(total, 1 - half), "s"))


def halve(values, axis, dim):
    index = lax.axis_index(axis) % 2
    return pick(values, index, dim), pick(values, 1 - index, dim)


def line_parts(values):
    return halve(values.reshape((2, 2) + values.shape[1:]), "z", 1)


def scatter_top(send, keep):
    total = add(keep, swap(send, "s"))
    total = total.reshape((4, 2) + total.shape[1:])
    return fold_line(fold(total, "x", 1))


def grad_block(left_t, right, got=None):
    total = product(left_t, right, 1, 0)
    if got is not None:
        total = total + got.astype(jnp.float32)
    return total.astype(jnp.bfloat16)


def columns_of(right, index):
    columns = right.shape[-1] // 2
    return lax.dynamic_slice_in_dim(right, index * columns, columns, right.ndim - 1)


PAIR = 2 * HD
LIMIT = 10 * 1024 * 1024


def kernel_params(steps):
    return pltpu.CompilerParams(
        dimension_semantics=("arbitrary",) * steps, vmem_limit_bytes=LIMIT
    )


def product(left, right, left_dim, right_dim):
    return lax.dot_general(
        left, right, (((left_dim,), (right_dim,)), ((), ())), preferred_element_type=jnp.float32
    )


def key_bias(facts_ref, slots):
    place = lax.broadcasted_iota(jnp.int32, (slots, 1), 0) + facts_ref[2]
    place = jnp.where(place >= slots, place - slots, place)
    return jnp.where(place < facts_ref[pl.program_id(0)], 0.0, -1e30)


def head_lanes(value, head):
    lane = lax.broadcasted_iota(jnp.int32, value.shape, 1)
    return jnp.where((lane >= HD) == (head == 1), value, jnp.zeros_like(value))


def turned(value):
    return value.astype(jnp.float32).T


def attend_kernel(facts_ref, query_ref, key_ref, value_ref, out_ref, total_ref):
    slots = key_ref.shape[0]
    bias = key_bias(facts_ref, slots)
    query = query_ref[...] * jnp.bfloat16(0.125)
    key = key_ref[...]
    value_t = turned(value_ref[...]).astype(jnp.bfloat16)
    outs = []
    for head in range(2):
        scores = product(key, head_lanes(query, head), 1, 1) + bias
        peak = jnp.max(scores, axis=0, keepdims=True)
        weight = jnp.exp(scores - peak)
        total = jnp.sum(weight, axis=0, keepdims=True)
        part = product(value_t[head * HD : (head + 1) * HD], weight.astype(jnp.bfloat16), 1, 0)
        outs.append(part * (1.0 / total))
        total_ref[0, 0, head : head + 1, :] = peak + jnp.log(total)
    out_ref[...] = jnp.concatenate(outs, axis=0).T.astype(jnp.bfloat16)


def attend_back_kernel(
    facts_ref, query_ref, key_ref, value_ref, grad_ref, total_ref, low_ref, sums_ref
):
    slots = key_ref.shape[0]
    bias = key_bias(facts_ref, slots)
    query = query_ref[...] * jnp.bfloat16(0.125)
    key = key_ref[...]
    value = value_ref[...]
    grad = grad_ref[...]
    key_t = turned(key).astype(jnp.bfloat16)
    lane = lax.broadcasted_iota(jnp.int32, (slots, PAIR), 1)
    query_parts, key_parts, value_parts = [], [], []
    for head in range(2):
        scores = product(key, head_lanes(query, head), 1, 1) + bias
        soft = jnp.exp(scores - total_ref[0, 0, head : head + 1, :])
        value_parts.append(product(soft.astype(jnp.bfloat16), grad, 1, 0))
        change = product(value, head_lanes(grad, head), 1, 1)
        inner = jnp.sum(soft * change, axis=0, keepdims=True)
        change = (soft * (change - inner)).astype(jnp.bfloat16)
        key_parts.append(product(change, query, 1, 0))
        query_parts.append(product(key_t[head * HD : (head + 1) * HD], change, 1, 0))
    pair = pl.program_id(1)
    groups = low_ref.shape[1] // 3
    query_low = (jnp.concatenate(query_parts, axis=0) * 0.125).T
    key_low = jnp.where(lane < HD, key_parts[0], key_parts[1])
    value_low = jnp.where(lane < HD, value_parts[0], value_parts[1])
    for place, part in enumerate((query_low, key_low, value_low)):
        start = pl.multiple_of(place * groups + pair * PAIR, PAIR)
        low = part.astype(jnp.bfloat16)
        low_ref[:, pl.ds(start, PAIR)] = low
        sums_ref[0, :, pl.ds(start, PAIR)] = jnp.sum(
            low.astype(jnp.float32), axis=0, keepdims=True
        )


def attention_specs(slots, pairs):
    def at(part):
        return pl.BlockSpec(
            (slots, PAIR), lambda b, g, p, *_: (b, g * 3 * pairs + part * pairs + p)
        )

    heads = pl.BlockSpec((slots, PAIR), lambda b, g, p, *_: (b, g * pairs + p))
    totals = pl.BlockSpec((1, 1, 2, slots), lambda b, g, p, *_: (b, g * pairs + p, 0, 0))
    return [at(0), at(1), at(2)], heads, totals


def attend(facts, projected, slots, wait=()):
    pairs = projected.shape[1] // (6 * PAIR)
    inputs, heads, totals = attention_specs(slots, pairs)
    rows = projected.shape[0]
    return call(
        attend_kernel,
        "attend",
        (2, 2, pairs),
        inputs,
        [heads, totals],
        [
            like((rows, 2 * pairs * PAIR), jnp.bfloat16),
            like((2, 2 * pairs, 2, slots), jnp.float32),
        ],
        facts,
        projected,
        projected,
        projected,
        wait=wait,
    )


def attend_back(facts, projected, heads_grad, totals_in, slots, own, wait=(), through=()):
    pairs = projected.shape[1] // (6 * PAIR)

    def group(facts_ref):
        return facts_ref[3] if own else 1 - facts_ref[3]

    def at(part):
        return pl.BlockSpec(
            (slots, PAIR), lambda b, p, f: (b, group(f) * 3 * pairs + part * pairs + p)
        )

    heads = pl.BlockSpec((slots, PAIR), lambda b, p, f: (b, group(f) * pairs + p))
    totals = pl.BlockSpec((1, 1, 2, slots), lambda b, p, f: (b, group(f) * pairs + p, 0, 0))
    width = 3 * pairs * PAIR
    return call(
        attend_back_kernel,
        "attend_back",
        (2, pairs),
        [at(0), at(1), at(2), heads, totals],
        [
            pl.BlockSpec((slots, width), lambda b, p, f: (b, 0)),
            pl.BlockSpec((1, 1, width), lambda b, p, f: (b, 0, 0)),
        ],
        [
            like((2 * slots, width), jnp.bfloat16),
            like((2, 1, width), jnp.float32),
        ],
        facts,
        projected,
        projected,
        projected,
        heads_grad,
        totals_in,
        wait=wait,
        through=through,
    )


def call(kernel, name, grid, inputs, outputs, shapes, facts, *args, wait=(), scratch=(), through=(), into=()):
    single = not isinstance(outputs, list)
    outputs, shapes = ([outputs], [shapes]) if single else (outputs, shapes)
    wait = tuple(into) + tuple(wait)
    count, held, passed = len(args), len(wait) + len(through), len(through)
    last = count + held + len(outputs)

    def body(facts_ref, *refs):
        kernel(facts_ref, *refs[:count], *refs[count + held : last], *refs[last + passed + 1 :])
        for place in range(facts.shape[0]):
            refs[last + passed][place] = facts_ref[place]

    results = pl.pallas_call(
        body,
        grid_spec=pltpu.PrefetchScalarGridSpec(
            num_scalar_prefetch=1,
            grid=grid,
            in_specs=list(inputs) + [pl.BlockSpec(memory_space=pl.ANY)] * held,
            out_specs=list(outputs)
            + [pl.BlockSpec(memory_space=pl.ANY)] * passed
            + [pl.BlockSpec(memory_space=pltpu.SMEM)],
            scratch_shapes=list(scratch),
        ),
        out_shape=list(shapes)
        + [like(value.shape, value.dtype) for value in through]
        + [like(facts.shape, jnp.int32)],
        input_output_aliases={
            **{1 + count + i: i for i in range(len(into))},
            **{1 + count + len(wait) + i: len(outputs) + i for i in range(passed)},
        },
        compiler_params=kernel_params(len(grid)),
        name=name,
    )(facts, *args, *wait, *through)
    values = tuple(results[:-1])
    return (values[0] if single and not passed else values), results[-1]


def block(shape, *index):
    def at(*grid_and_facts):
        return tuple(entry(*grid_and_facts) if callable(entry) else entry for entry in index)

    return pl.BlockSpec(shape, at)


def whole(array):
    zeros = (0,) * array.ndim
    return pl.BlockSpec(array.shape, lambda *_: zeros)


def first(i, *_):
    return i


def like(shape, dtype):
    return jax.ShapeDtypeStruct(shape, dtype)


def rows_in_order(facts_ref, own, beside):
    even = facts_ref[4] == 0
    pieces = []
    for z in range(4):
        pieces += [jnp.where(even, own[z], beside[z]), jnp.where(even, beside[z], own[z])]
    return jnp.concatenate(pieces, axis=0)


def near_or_far(facts_ref, refs, near):
    own, beside, below, across = [ref[...] for ref in refs]
    return rows_in_order(
        facts_ref, jnp.where(near, own, below), jnp.where(near, beside, across)
    )


def square_columns(parts, wide, steps):
    shape = parts[0].shape[:2] + (wide,)
    near = block(shape, 0, 0, lambda i, *_: jnp.minimum(i, steps - 1))
    far = block(shape, 0, 0, lambda i, *_: jnp.maximum(i - steps, 0))
    return [near, near, far, far]


def half_at(i, facts, steps):
    return jnp.where(i < steps, facts[3], 1 - facts[3])


def gate_kernel(facts_ref):
    del facts_ref


def gate(facts, through, wait):
    return call(gate_kernel, "gate", (1,), [], [], [], facts, wait=wait, through=through)


def stack_kernel(own_at, facts_ref, own_ref, other_ref, out_ref):
    own = facts_ref[own_at] == pl.program_id(0)
    value = jnp.where(own, own_ref[...], other_ref[...])
    out_ref[...] = value.reshape(out_ref.shape)


def stack_pair(facts, own, other, wait=(), through=()):
    rows, columns = own.shape
    return call(
        partial(stack_kernel, 6),
        "stack",
        (2,),
        [whole(own), whole(other)],
        block((1, rows, columns), first, 0, 0),
        like((2, rows, columns), own.dtype),
        facts,
        own,
        other,
        wait=wait,
        through=through,
    )


def stack_line(facts, own, other, wait=()):
    _, rows, columns = own.shape
    line, facts = call(
        partial(stack_kernel, 7),
        "stack_line",
        (2,),
        [whole(own), whole(other)],
        block((2, 1, rows, columns), 0, first, 0, 0),
        like((2, 2, rows, columns), own.dtype),
        facts,
        own,
        other,
        wait=wait,
    )
    return line.reshape(4, rows, columns), facts


def turn_kernel(facts_ref, *refs):
    for i in range(2):
        refs[4 + i][...] = jnp.concatenate([refs[2 * i][...].T, refs[2 * i + 1][...].T], axis=1)


def turn_all_kernel(facts_ref, rows_ref, out_ref):
    out_ref[...] = rows_ref[...].T


def turn_all(facts, values, wait=()):
    count, width = values.shape
    step = width // 4
    return call(
        turn_all_kernel,
        "turn_all",
        (4,),
        [block((count, step), 0, first)],
        block((step, count), first, 0),
        like((width, count), values.dtype),
        facts,
        values,
        wait=wait,
    )


def turn(facts, values, others, rows, wait=()):
    count, width = values.shape
    half = width // 2
    out = block((rows, 2 * count), first, 0)
    shape = like((half, 2 * count), values.dtype)
    own = block((count, rows), 0, lambda i, f: 2 * i + f[4])
    other = block((count, rows), 0, lambda i, f: 2 * i + 1 - f[4])
    return call(
        turn_kernel,
        "turn",
        (half // rows,),
        [own, own, other, other],
        [out, out],
        [shape, shape],
        facts,
        values,
        others,
        values,
        others,
        wait=wait,
    )


def project_kernel(facts_ref, rows_ref, bias_ref, *refs):
    parts, (out_ref, in_ref, rest_ref) = refs[:4], refs[4:]
    step = pl.program_id(0)
    weight = near_or_far(facts_ref, parts, step < 4)

    @pl.when(step % 4 < 3)
    def _():
        in_ref[...] = weight
        value = product(rows_ref[...], weight, 1, 0) + bias_ref[...]
        out_ref[...] = value.astype(jnp.bfloat16)

    @pl.when(step % 4 == 3)
    def _():
        chips, count, wide = rest_ref.shape
        pairs = weight.reshape(chips, 2, count, wide // 2)
        rest_ref[...] = jnp.concatenate([pairs[:, 0], pairs[:, 1]], axis=2)


def project(facts, rows, bias, parts, wait=()):
    count, width = rows.shape
    wide = parts[0].shape[2] // 4

    def column(i, f):
        return half_at(i, f, 4) * 3 + jnp.minimum(i % 4, 2)

    out = block((count, wide), 0, column)
    rest = (8, parts[0].shape[1] // 2, 2 * wide)
    return call(
        project_kernel,
        "project",
        (8,),
        [whole(rows), block((1, wide), 0, column)] + square_columns(parts, wide, 4),
        [out, block((width, wide), 0, column), block(rest, 0, 0, lambda i, f: half_at(i, f, 4))],
        [
            like((count, 6 * wide), jnp.bfloat16),
            like((width, 6 * wide), jnp.bfloat16),
            like(rest[:2] + (4 * wide,), jnp.bfloat16),
        ],
        facts,
        rows,
        bias[None],
        *parts,
        wait=wait,
    )


def valid_rows(facts_ref, count, slots):
    place = lax.broadcasted_iota(jnp.int32, (count, 1), 0) + pl.program_id(0) * count + facts_ref[2]
    place = jnp.where(place >= slots, place - slots, place)
    return (place < facts_ref[0]).astype(jnp.float32)


def add_rows(sums_ref, rows):
    total = jnp.concatenate([jnp.sum(part, axis=0, keepdims=True) for part in rows], axis=0)
    total = jnp.concatenate([total, jnp.zeros((8 - len(rows), total.shape[1]), jnp.float32)], axis=0)

    @pl.when(pl.program_id(0) == 0)
    def _():
        sums_ref[...] = total

    @pl.when(pl.program_id(0) > 0)
    def _():
        sums_ref[...] += total


def mean_of(values):
    return jnp.mean(values, axis=-1, keepdims=True)


def attend_out_kernel(
    slots, facts_ref, own_ref, other_ref, own_weight_ref, other_weight_ref, tokens_ref, vectors_ref,
    hat_ref, rstd_ref, low_ref, sums_ref,
):
    branch = (
        product(own_ref[...], own_weight_ref[...], 1, 0)
        + product(other_ref[...], other_weight_ref[...], 1, 0)
        + vectors_ref[0:1]
    )
    tokens = tokens_ref[...].astype(jnp.float32)
    total = tokens + branch
    centered = total - mean_of(total)
    rstd = lax.rsqrt(mean_of(centered * centered) + 1e-05)
    hat = centered * rstd
    hat_ref[...] = hat
    rstd_ref[...] = rstd
    low_ref[...] = (hat * vectors_ref[1:2] + vectors_ref[2:3]).astype(jnp.bfloat16)
    valid = valid_rows(facts_ref, tokens.shape[0], slots)
    add_rows(sums_ref, [valid * tokens * tokens, valid * branch * branch])


def attend_out(facts, own, other, own_weight, other_weight, tokens, vectors, wait=()):
    slots, width = tokens.shape
    step = slots // 4
    rows = lambda array: block((step, array.shape[1]), first, 0)
    return call(
        partial(attend_out_kernel, slots),
        "attend_out",
        (4,),
        [rows(own), rows(other), whole(own_weight), whole(other_weight), rows(tokens), whole(vectors)],
        [block((step, width), first, 0), block((step, 1), first, 0), block((step, width), first, 0), block((8, width), 0, 0)],
        [
            like((slots, width), jnp.float32),
            like((slots, 1), jnp.float32),
            like((slots, width), jnp.bfloat16),
            like((8, width), jnp.float32),
        ],
        facts,
        own,
        other,
        own_weight,
        other_weight,
        tokens,
        vectors,
        wait=wait,
    )


def up_kernel(facts_ref, rows_ref, others_ref, bias_ref, *refs):
    parts, (act_ref, slope_ref, turned_ref, weight_ref) = refs[:4], refs[4:]
    weight = near_or_far(facts_ref, parts, pl.program_id(0) < 4)
    weight_ref[...] = weight
    pre_act = [product(ref[...], weight, 1, 0) for ref in (rows_ref, others_ref)]
    pre_act = jnp.concatenate(pre_act, axis=0) + bias_ref[...]
    below = 0.5 + 0.5 * lax.erf(pre_act * 0.7071067811865476)
    act = (pre_act * below).astype(jnp.bfloat16)
    act_ref[...] = act
    turned_ref[...] = act.T
    slope = below + pre_act * (0.3989422804014327 * jnp.exp(-0.5 * pre_act * pre_act))
    slope_ref[...] = slope.astype(jnp.bfloat16)


def feed_up(facts, rows, others, bias, parts, wait=()):
    count, width = 2 * rows.shape[0], rows.shape[1]
    units = bias.shape[0]
    wide = units // 8

    def column(i, f):
        return half_at(i, f, 4) * 4 + i % 4

    shape = like((count, units), jnp.bfloat16)
    out = block((count, wide), 0, column)
    return call(
        up_kernel,
        "feed_up",
        (8,),
        [whole(rows), whole(others), block((1, wide), 0, column)] + square_columns(parts, wide, 4),
        [out, out, block((wide, count), column, 0), block((width, wide), 0, column)],
        [
            shape,
            shape,
            like((units, count), jnp.bfloat16),
            like((width, units), jnp.bfloat16),
        ],
        facts,
        rows,
        others,
        bias[None],
        *parts,
        wait=wait,
    )


def down_kernel(facts_ref, rows_ref, *refs):
    parts, (weight_ref, out_ref, total_ref) = refs[:4], refs[4:]
    step = pl.program_id(0)
    own, beside, below, across = [ref[0] for ref in parts]
    even, left = facts_ref[4] == 0, facts_ref[3] == 0
    for x in range(2):
        mine = jnp.where(even, own, beside) if x == 0 else jnp.where(even, beside, own)
        theirs = jnp.where(even, below, across) if x == 0 else jnp.where(even, across, below)
        weight_ref[x] = jnp.concatenate(
            [jnp.where(left, mine, theirs), jnp.where(left, theirs, mine)], axis=1
        )
    weight = weight_ref[...].reshape(rows_ref.shape[1], out_ref.shape[1])
    value = product(rows_ref[...], weight, 1, 0)

    @pl.when(step == 0)
    def _():
        total_ref[...] = value

    @pl.when(step > 0)
    def _():
        total_ref[...] += value

    @pl.when(step == 3)
    def _():
        out_ref[...] = total_ref[...].astype(jnp.bfloat16)


def feed_down(facts, rows, parts, wait=()):
    count, units = rows.shape
    _, block_rows, half_width = parts[0].shape
    width = 2 * half_width
    shape = (1,) + parts[0].shape[1:]
    return call(
        down_kernel,
        "feed_down",
        (4,),
        [block((count // 2, units // 4), 1, first)] + [block(shape, first, 0, 0)] * 4,
        [block((2, block_rows, width), first, 0, 0), block((count // 2, width), 0, 0)],
        [like((8, block_rows, width), jnp.bfloat16), like((count // 2, width), jnp.bfloat16)],
        facts,
        rows,
        *parts,
        scratch=[pltpu.VMEM((count // 2, width), jnp.float32)],
        wait=wait,
    )


def second_norm_kernel(
    slots, facts_ref, part_ref, other_ref, hat_ref, cotangent_ref, vectors_ref,
    mixed_ref, grad_ref, low_ref, sums_ref,
):
    branch = part_ref[...] + other_ref[...].astype(jnp.float32) + vectors_ref[0:1]
    hidden = hat_ref[...] * vectors_ref[1:2] + vectors_ref[2:3]
    gain = vectors_ref[3:4]
    total = hidden + branch
    centered = total - mean_of(total)
    rstd = lax.rsqrt(mean_of(centered * centered) + 1e-05)
    hat = centered * rstd
    mixed_ref[...] = (hat * gain + vectors_ref[4:5]).astype(jnp.bfloat16)
    valid = valid_rows(facts_ref, branch.shape[0], slots)
    grad = cotangent_ref[...].astype(jnp.float32) * valid
    scaled = grad * gain
    result = rstd * (scaled - mean_of(scaled) - hat * mean_of(scaled * hat))
    low = result.astype(jnp.bfloat16)
    grad_ref[...] = result
    low_ref[...] = low
    add_rows(sums_ref, [low.astype(jnp.float32), grad * hat, grad, valid * branch * branch])


def second_norm(facts, part, other, hat, cotangent, vectors, wait=()):
    slots, width = part.shape
    step = slots // 4
    rows = block((step, width), first, 0)
    return call(
        partial(second_norm_kernel, slots),
        "second_norm",
        (4,),
        [rows, rows, rows, rows, whole(vectors)],
        [rows, rows, rows, block((8, width), 0, 0)],
        [
            like((slots, width), jnp.bfloat16),
            like((slots, width), jnp.float32),
            like((slots, width), jnp.bfloat16),
            like((8, width), jnp.float32),
        ],
        facts,
        part,
        other,
        hat,
        cotangent,
        vectors,
        wait=wait,
    )


def first_norm_kernel(
    facts_ref, part_ref, other_ref, second_ref, hat_ref, rstd_ref, vectors_ref,
    grad_ref, low_ref, sums_ref,
):
    grad = part_ref[...] + other_ref[...].astype(jnp.float32) + second_ref[...]
    hat = hat_ref[...]
    scaled = grad * vectors_ref[1:2]
    result = rstd_ref[...] * (scaled - mean_of(scaled) - hat * mean_of(scaled * hat))
    low = result.astype(jnp.bfloat16)
    grad_ref[...] = result
    low_ref[...] = low
    add_rows(sums_ref, [low.astype(jnp.float32), grad * hat, grad])


def first_norm(facts, part, other, second, hat, rstd, vectors, wait=()):
    slots, width = part.shape
    step = slots // 4
    rows = block((step, width), first, 0)
    return call(
        first_norm_kernel,
        "first_norm",
        (4,),
        [rows, rows, rows, rows, block((step, 1), first, 0), whole(vectors)],
        [rows, rows, block((8, width), 0, 0)],
        [
            like((slots, width), jnp.float32),
            like((slots, width), jnp.bfloat16),
            like((8, width), jnp.float32),
        ],
        facts,
        part,
        other,
        second,
        hat,
        rstd,
        vectors,
        wait=wait,
    )


def act_grad_kernel(facts_ref, rows_ref, weight_ref, slope_ref, out_ref, sums_ref):
    total = product(rows_ref[...], weight_ref[...], 1, 1)
    grad = total.astype(jnp.bfloat16).astype(jnp.float32) * slope_ref[...].astype(jnp.float32)
    low = grad.astype(jnp.bfloat16)
    out_ref[...] = low
    sums_ref[...] = jnp.sum(low.astype(jnp.float32), axis=0, keepdims=True)


def act_grad(facts, rows, weight, slope, wait=()):
    count, units = slope.shape
    step = units // 8
    out = block((count, step), 0, first)
    return call(
        act_grad_kernel,
        "act_grad",
        (8,),
        [whole(rows), block((step, rows.shape[1]), first, 0), out],
        [out, block((1, step), 0, first)],
        [like((count, units), jnp.bfloat16), like((1, units), jnp.float32)],
        facts,
        rows,
        weight,
        slope,
        wait=wait,
    )


def tokens_grad_kernel(facts_ref, mine_ref, theirs_ref, weight_ref, out_ref, sent_ref):
    wide = mine_ref.shape[1]
    slots = out_ref.shape[0]
    half = facts_ref[3]
    mine = weight_ref[:, pl.ds(pl.multiple_of(half * wide, 128), wide)]
    theirs = weight_ref[:, pl.ds(pl.multiple_of((1 - half) * wide, 128), wide)]
    total = product(mine_ref[...], mine, 1, 1) + product(theirs_ref[...], theirs, 1, 1)
    out_ref[...] = total[:slots]
    sent_ref[...] = total[slots:].astype(sent_ref.dtype)


def tokens_grad(facts, mine, theirs, weight, wait=(), through=()):
    count, columns = mine.shape
    width = weight.shape[0]
    step = width // 4
    out = block((count // 2, step), 0, first)
    return call(
        tokens_grad_kernel,
        "tokens_grad",
        (4,),
        [whole(mine), whole(theirs), block((step, 2 * columns), first, 0)],
        [out, out],
        [
            like((count // 2, width), jnp.float32),
            like((count // 2, width), jnp.bfloat16),
        ],
        facts,
        mine,
        theirs,
        weight,
        wait=wait,
        through=through,
    )


def add_parts_kernel(facts_ref, own_ref, got_ref, kept_ref, sent_ref):
    step = pl.program_id(0)
    total = own_ref[...].astype(jnp.float32) + got_ref[...].astype(jnp.float32)
    total = total.astype(jnp.bfloat16)

    @pl.when(step < 2)
    def _():
        sent_ref[...] = total

    @pl.when(step >= 2)
    def _():
        kept_ref[...] = total


def add_last_kernel(facts_ref, own_ref, got_ref, kept_ref, sent_ref):
    total = own_ref[0].astype(jnp.float32) + got_ref[0].astype(jnp.float32)
    total = total.astype(jnp.bfloat16)

    @pl.when(pl.program_id(0) == 0)
    def _():
        sent_ref[...] = total

    @pl.when(pl.program_id(0) == 1)
    def _():
        kept_ref[...] = total


def add_last(facts, own, got, wait=(), through=()):
    _, rows, columns = own.shape
    part = block((1, rows, columns), lambda i, f: jnp.where(i == 0, 1 - f[6], f[6]), 0, 0)
    shape = like((rows, columns), jnp.bfloat16)
    out = block((rows, columns), 0, 0)
    return call(
        add_last_kernel,
        "add_last",
        (2,),
        [part, part],
        [out, out],
        [shape, shape],
        facts,
        own,
        got,
        wait=wait,
        through=through,
    )


def add_parts(facts, own, got, wait=(), through=()):
    _, rows, columns = own.shape
    shape = (1, rows, columns)
    part = block(shape, lambda i, f: 2 * (i % 2) + jnp.where(i < 2, 1 - f[7], f[7]), 0, 0)
    half = like((2, rows, columns), jnp.bfloat16)
    return call(
        add_parts_kernel,
        "add_parts",
        (4,),
        [part, part],
        [
            block(shape, lambda i, *_: jnp.maximum(i - 2, 0), 0, 0),
            block(shape, lambda i, *_: jnp.minimum(i, 1), 0, 0),
        ],
        [half, half],
        facts,
        own,
        got,
        wait=wait,
        through=through,
    )


def alternate(value, width, offset):
    starts = range(offset * width, value.shape[1], 2 * width)
    return jnp.concatenate([value[:, start : start + width] for start in starts], axis=1)


def deal_kernel(unit_block, core_ref, query_ref, key_ref, value_ref, up_ref, *refs):
    first_core = core_ref[0] == 0
    near = [ref[...] for ref in (query_ref, key_ref, value_ref)]
    even = jnp.concatenate([alternate(value, HD, 0) for value in near], axis=1)
    odd = jnp.concatenate([alternate(value, HD, 1) for value in near], axis=1)
    up = up_ref[...]
    up_even, up_odd = alternate(up, unit_block, 0), alternate(up, unit_block, 1)
    refs[0][...] = jnp.where(first_core, even, odd)
    refs[1][...] = jnp.where(first_core, odd, even)
    refs[2][...] = jnp.where(first_core, up_even, up_odd)
    refs[3][...] = jnp.where(first_core, up_odd, up_even)


def deal(core, query, key, value, up, unit_block):
    near = like((query.shape[0], 3 * query.shape[1] // 2), jnp.bfloat16)
    half = like((up.shape[0], up.shape[1] // 2), jnp.bfloat16)
    shapes = [near, near, half, half]
    return call(
        partial(deal_kernel, unit_block),
        "deal",
        (1,),
        [whole(value) for value in (query, key, value, up)],
        [whole(shape) for shape in shapes],
        shapes,
        core,
        query,
        key,
        value,
        up,
    )


def lay_out_kernel(core_ref, near_ref, near_got_ref, out_ref, up_ref, up_got_ref, *refs):
    first_core = core_ref[0] == 0
    near, near_got, up, up_got = [
        ref[...] for ref in (near_ref, near_got_ref, up_ref, up_got_ref)
    ]
    out = out_ref[...]
    wide = out.shape[1] // 2
    near_rows = jnp.concatenate(
        [jnp.where(first_core, near, near_got), jnp.where(first_core, near_got, near)], axis=0
    )
    out_rows = jnp.concatenate([out[:, :wide], out[:, wide:]], axis=0)
    refs[0][...] = jnp.concatenate([near_rows, out_rows], axis=1)
    refs[1][...] = jnp.concatenate(
        [jnp.where(first_core, up, up_got), jnp.where(first_core, up_got, up)], axis=0
    )


def lay_out(core, near, near_got, out, up, up_got):
    rows = 2 * near.shape[0]
    shapes = [
        like((rows, near.shape[1] + out.shape[1] // 2), jnp.bfloat16),
        like((rows, up.shape[1]), jnp.bfloat16),
    ]
    arrays = (near, near_got, out, up, up_got)
    return call(
        lay_out_kernel,
        "lay_out",
        (1,),
        [whole(value) for value in arrays],
        [whole(shape) for shape in shapes],
        shapes,
        core,
        *arrays,
    )[0]


def split_body(
    tokens,
    lengths,
    cotangent,
    query_weight,
    key_weight,
    value_weight,
    out_weight,
    up_weight,
    down_weight,
    query_bias,
    value_bias,
    out_bias,
    attn_gain,
    attn_shift,
    up_bias,
    down_bias,
    feed_gain,
    feed_shift,
):
    core = lax.axis_index("c")
    half = lax.axis_index("s")
    row_count, width = tokens.shape[1:]
    slots = 2 * row_count
    unit_block = down_weight.shape[0]
    units = up_bias.shape[0] // 2
    cols = width // 2
    wide = cols // 2

    def to_sequence(values):
        return jnp.concatenate([pick(values, half, 0), swap(pick(values, 1 - half, 0), "s")], axis=0)

    def from_sequence(values):
        return in_order(values[:row_count], swap(values[row_count:], "s"), half)

    place = jnp.stack([core]).astype(jnp.int32)
    (near_kept, near_sent, up_kept, up_sent), place = deal(
        place, query_weight, key_weight, value_weight, up_weight, unit_block
    )
    near_mine, up_mine = lay_out(
        place, near_kept, swap(near_sent, "c"), out_weight, up_kept, swap(up_sent, "c")
    )
    rows, up_cols = up_mine.shape
    line = lax.axis_index("z")
    length_own = lax.dynamic_slice_in_dim(lengths, half, 1, 0)
    facts = jnp.concatenate(
        [
            both(length_own, "c"),
            jnp.stack(
                [
                    half * row_count,
                    half,
                    lax.axis_index("x"),
                    jnp.int32(0),
                    line // 2,
                    line % 2,
                ]
            ).astype(jnp.int32),
        ]
    )
    tokens_own = to_sequence(tokens)
    cotangent_own = to_sequence(cotangent)
    (near, up_mine, down_mine), facts = stack_pair(
        facts,
        near_mine,
        line_cross(near_mine),
        wait=(tokens_own,),
        through=(up_mine, down_weight),
    )
    near, facts = stack_line(facts, near, line_next(near), wait=(cotangent_own,))
    near_parts = gather_square(near, "x")
    up_pairs, facts = stack_pair(facts, up_mine, line_cross(up_mine), wait=(near,))
    tokens_both = both(tokens_own, "c")
    up_part, facts = stack_line(
        facts, up_pairs, line_next(up_pairs), wait=(near_parts[1], near_parts[2])
    )
    up_parts = gather_square(up_part, "s")
    down_pairs, facts = stack_pair(facts, down_mine, line_cross(down_mine), wait=(up_part,))
    def halves_of(vector, size):
        return pick(vector.reshape(-1, 2, size), core, 1).reshape(-1)

    query_part = halves_of(query_bias, HD).reshape(2, wide)
    value_part = halves_of(value_bias, HD).reshape(2, wide)
    in_bias = jnp.stack([query_part, jnp.zeros_like(query_part), value_part], axis=1).reshape(-1)
    down_part, facts = stack_line(facts, down_pairs, line_next(down_pairs))
    down_parts = gather_square(down_part, "x")
    (projected, in_weight, out_own), facts = project(
        facts, tokens_both, in_bias, near_parts, wait=(down_part, up_parts[2])
    )
    out_own = out_own.reshape(cols, width)
    out_other = swap(out_own, "c")
    (heads_out, totals), facts = attend(facts, projected, slots)
    heads_other = swap(heads_out[slots:], "c")
    vectors = jnp.stack(
        [out_bias, attn_gain, attn_shift, down_bias, feed_gain, feed_shift, out_bias, out_bias]
    )
    (first_hat, first_rstd, hidden_low, first_sums), facts = attend_out(
        facts,
        heads_out,
        heads_other,
        out_own,
        out_other,
        tokens_own,
        vectors,
        wait=(up_parts[1], down_parts[2]),
    )
    tokens_t, facts = turn_all(facts, tokens_both, wait=(hidden_low,))
    (hidden_low,), facts = gate(facts, (hidden_low,), (up_parts[3], down_parts[1]))
    hidden_from = swap(hidden_low, "c")
    (activation, slope, act_t, up_all), facts = feed_up(
        facts, hidden_low, hidden_from, halves_of(up_bias, unit_block), up_parts
    )
    hidden_turned, facts = turn(facts, hidden_low, hidden_from, rows, wait=(act_t,))
    (down_all, feed_sent), facts = feed_down(facts, activation, down_parts)
    down_all = down_all.reshape(units, width)
    feed_other = swap(feed_sent, "c")
    feed_part = product(activation[:slots], down_all, 1, 0)
    feed_vectors = jnp.stack(
        [down_bias, attn_gain, attn_shift, feed_gain, feed_shift, out_bias, out_bias, out_bias]
    )
    (mixed, second_grad, feed_low, second_sums), facts = second_norm(
        facts, feed_part, feed_other, first_hat, cotangent_own, feed_vectors
    )

    feed_both = both(feed_low, "c")
    feed_mine, feed_theirs = columns_of(feed_both, half), columns_of(feed_both, 1 - half)
    down_sent = grad_block(act_t, feed_theirs)
    down_got = swap(down_sent, "s")
    (pre_grad, up_bias_grad), facts = act_grad(
        facts, feed_both, down_all, slope, wait=(down_sent,)
    )
    hidden_sent = product(pre_grad[slots:], up_all, 1, 1).astype(jnp.bfloat16)
    hidden_other = swap(hidden_sent, "c")
    hidden_own_t, hidden_other_t = hidden_turned
    up_sent = grad_block(hidden_other_t, pre_grad)
    up_got = swap(up_sent, "x")
    hidden_part = product(pre_grad[:slots], up_all, 1, 1)
    (first_grad, attn_low, third_sums), facts = first_norm(
        facts,
        hidden_part,
        hidden_other,
        second_grad,
        first_hat,
        first_rstd,
        vectors,
        wait=(up_sent,),
    )
    grad_sent = product(attn_low, out_other, 1, 1).astype(jnp.bfloat16)
    grad_other = swap(grad_sent, "c")
    grad_own = product(attn_low, out_own, 1, 1).astype(jnp.bfloat16)
    out_sent = product(heads_other, attn_low, 0, 0).astype(jnp.bfloat16)
    out_got = swap(out_sent, "c")
    heads_grad = jnp.concatenate([grad_own, grad_other], axis=0)
    (theirs_low, theirs_sums), facts = attend_back(
        facts, projected, heads_grad, totals, slots, False, wait=(out_sent,)
    )
    in_sent = grad_block(tokens_t, theirs_low)
    in_got = swap(in_sent, "s")
    down_total = grad_block(act_t, feed_mine, down_got)
    down_kept, down_sent = halve(down_total.reshape(4, 2, unit_block, cols), "x", 1)
    down_got = swap(down_sent, "x")
    out_grad = grad_block(heads_out[:slots].T, attn_low, out_got)
    out_line = out_grad.reshape((4, 2 * out_weight.shape[0], width))
    out_kept, out_sent = line_parts(out_line)
    out_got = lax.ppermute(out_sent, "z", NEXT)
    (mine_low, mine_sums), facts = attend_back(
        facts, projected, heads_grad, totals, slots, True, wait=(in_sent, out_sent, down_sent)
    )
    up_total = grad_block(hidden_own_t, pre_grad, up_got).reshape(4, rows, 2 * up_cols)
    up_kept, up_sent = columns_of(up_total, half), columns_of(up_total, 1 - half)
    up_got = swap(up_sent, "s")
    out_total = add(out_kept, out_got)
    valid_count = length_own[0].astype(jnp.float32) * width
    stats = jnp.stack(
        [jnp.sum(first_sums[0]), jnp.sum(first_sums[1]), jnp.sum(second_sums[3]), valid_count]
    )
    mine_sums, theirs_sums = jnp.sum(mine_sums, axis=(0, 1)), jnp.sum(theirs_sums, axis=(0, 1))
    late = in_order(mine_sums, theirs_sums, half)
    sums = jnp.concatenate(
        [
            second_sums[:3].reshape(-1),
            third_sums[:3].reshape(-1),
            jnp.pad(stats, (0, 124)),
            up_bias_grad[0],
            late[:, :wide].reshape(-1),
            late[:, 2 * wide :].reshape(-1),
        ]
    )
    sums = sums + lax.ppermute(sums, "z", NEXT)
    (tokens_part, tokens_sent), facts = tokens_grad(
        facts,
        mine_low,
        theirs_low,
        in_weight,
        wait=(up_sent, out_total, sums),
    )
    in_total = grad_block(tokens_t, mine_low, in_got)
    in_kept, in_sent = halve(in_total.reshape(4, 2, rows, 3 * wide), "x", 1)
    in_got = swap(in_sent, "x")
    tokens_other = swap(tokens_sent, "c")
    (down_pairs, down_next), facts = add_parts(
        facts, down_kept, down_got, wait=(in_sent, tokens_part)
    )
    down_got = lax.ppermute(down_next, "z", NEXT)
    upper = lax.axis_index("z") // 2
    out_kept, out_sent = pick(out_total, upper, 0), pick(out_total, 1 - upper, 0)
    out_kept = add(out_kept, lax.ppermute(out_sent, "z", CROSS))
    (in_pairs, in_next, sums), facts = add_parts(
        facts, in_kept, in_got, wait=(down_next, out_kept), through=(sums,)
    )
    in_got = lax.ppermute(in_next, "z", NEXT)
    (down_kept, down_sent), facts = add_last(facts, down_pairs, down_got, wait=(in_next,))
    (up_pairs, up_next), facts = add_parts(facts, up_kept, up_got, wait=(down_sent,))
    up_got = lax.ppermute(up_next, "z", NEXT)
    sums = sums + swap(sums, "x")
    sums = sums + swap(sums, "s")
    (in_kept, in_sent, out_kept, mixed), facts = add_last(
        facts, in_pairs, in_got, wait=(sums, up_next), through=(out_kept, mixed)
    )
    (up_kept, up_sent, sums), facts = add_last(
        facts, up_pairs, up_got, wait=(in_sent,), through=(sums,)
    )
    in_sum = add(in_kept, lax.ppermute(in_sent, "z", CROSS))
    tokens_grad_sum = tokens_part + tokens_other.astype(jnp.float32) + first_grad
    tokens_grad_sum = from_sequence(tokens_grad_sum.astype(jnp.bfloat16))
    mixed = in_order(mixed[:row_count], swap(mixed[row_count:], "s"), half)
    down_sum = add(down_kept, lax.ppermute(down_sent, "z", CROSS))
    up_sum = add(up_kept, lax.ppermute(up_sent, "z", CROSS))
    out_sum = fold_columns(fold(out_kept.reshape(2, out_weight.shape[0], width), "x", 0))

    sums = sums + lax.ppermute(sums, "z", CROSS)
    both_sums = in_order(sums, swap(sums, "c"), core)
    count = 6 * width + 128
    shared = both_sums[0, :count] + both_sums[1, :count]
    down_bias_grad, feed_gain_grad, feed_shift_grad, out_bias_grad, attn_gain_grad, attn_shift_grad = [
        shared[i * width : (i + 1) * width] for i in range(6)
    ]
    stats = shared[6 * width : 6 * width + 4]

    def interleave(start, size, block_size):
        sums = both_sums[:, start : start + size].reshape(2, -1, block_size)
        return sums.transpose(1, 0, 2).reshape(-1)

    up_bias_grad = interleave(count, units, unit_block)
    query_bias_grad = interleave(count + units, cols, HD)
    value_bias_gradient = interleave(count + units + cols, cols, HD)
    stream_rms = jnp.sqrt(stats[:3] / stats[3])

    def give_back(total):
        total = total.reshape((2, rows // 2) + total.shape[1:])
        return pick(total, core, 0), swap(pick(total, 1 - core, 0), "c")

    up_shares = give_back(up_sum)
    in_shares = give_back(in_sum)
    down_weight_grad = down_sum.astype(jnp.float32)
    out_weight_grad = out_sum.astype(jnp.float32)

    def merge(shares, start, size, block):
        one, two = [
            share[:, start : start + size].reshape(rows // 2, -1, block) for share in shares
        ]
        first = jnp.where(core == 0, one, two)
        second = jnp.where(core == 0, two, one)
        return jnp.stack([first, second], axis=2).reshape(rows // 2, -1).astype(jnp.float32)

    query_weight_grad = merge(in_shares, 0, wide, HD)
    key_weight_grad = merge(in_shares, wide, wide, HD)
    value_weight_grad = merge(in_shares, 2 * wide, wide, HD)
    up_weight_grad = merge(up_shares, 0, up_cols, unit_block)
    return (
        mixed,
        tokens_grad_sum,
        query_weight_grad,
        key_weight_grad,
        value_weight_grad,
        out_weight_grad,
        up_weight_grad,
        down_weight_grad,
        query_bias_grad,
        value_bias_gradient,
        out_bias_grad,
        attn_gain_grad,
        attn_shift_grad,
        up_bias_grad,
        down_bias_grad,
        feed_gain_grad,
        feed_shift_grad,
        stream_rms,
    )


def solution(mesh):
    devices = mesh.devices
    dp_count, seq_count = devices.shape
    split = seq_count == 2 and dp_count == 16
    if split:
        inner = jax.sharding.Mesh(devices.reshape(4, 2, 2, seq_count), ("z", "x", "c", "s"))
        dp, seq, body = ("z", "x", "c"), "s", split_body
    else:
        inner, dp, seq, body = mesh, "dp", "seq", general_body
    weights = (P(dp, seq),) * 6
    vectors = (P(),) * 9
    rows = P(dp, seq, None)
    in_specs = (rows, P(dp), rows) + weights + vectors
    out_specs = (rows, rows) + weights + vectors + (P(),)
    return jax.shard_map(body, mesh=inner, in_specs=in_specs, out_specs=out_specs, check_vma=False)
```

```python
from functools import partial
import math

import jax
import jax.numpy as jnp
from jax import lax
from jax.experimental import pallas as pl
from jax.experimental.pallas import tpu as pltpu
from jax.sharding import PartitionSpec as P

HD = 64


def layer_norm(values_in, gain_vector, shift_vector):
    mean_value = jnp.mean(values_in, axis=-1, keepdims=True)
    centered = values_in - mean_value
    variance = jnp.mean(centered * centered, axis=-1, keepdims=True)
    return centered * lax.rsqrt(variance + 1e-05) * gain_vector + shift_vector


def gather_weights(first, second, third, fourth, fifth, sixth):
    part = (
        lax.all_gather(first, "dp", axis=0, tiled=True),
        lax.all_gather(second, "dp", axis=0, tiled=True),
        lax.all_gather(third, "dp", axis=0, tiled=True),
        lax.all_gather(fourth, "dp", axis=0, tiled=True),
        lax.all_gather(fifth, "dp", axis=0, tiled=True),
        lax.all_gather(sixth, "dp", axis=0, tiled=True),
    )
    return (
        lax.all_gather(part[0], "seq", axis=1, tiled=True),
        lax.all_gather(part[1], "seq", axis=1, tiled=True),
        lax.all_gather(part[2], "seq", axis=1, tiled=True),
        lax.all_gather(part[3], "seq", axis=1, tiled=True),
        lax.all_gather(part[4], "seq", axis=1, tiled=True),
        lax.all_gather(part[5], "seq", axis=1, tiled=True),
    )


def reduce_grads(first, second, third, fourth, fifth, sixth):
    part = (
        lax.psum_scatter(first.astype(jnp.bfloat16), "seq", scatter_dimension=1, tiled=True).astype(
            jnp.float32
        ),
        lax.psum_scatter(
            second.astype(jnp.bfloat16), "seq", scatter_dimension=1, tiled=True
        ).astype(jnp.float32),
        lax.psum_scatter(third.astype(jnp.bfloat16), "seq", scatter_dimension=1, tiled=True).astype(
            jnp.float32
        ),
        lax.psum_scatter(
            fourth.astype(jnp.bfloat16), "seq", scatter_dimension=1, tiled=True
        ).astype(jnp.float32),
        lax.psum_scatter(fifth.astype(jnp.bfloat16), "seq", scatter_dimension=1, tiled=True).astype(
            jnp.float32
        ),
        lax.psum_scatter(sixth.astype(jnp.bfloat16), "seq", scatter_dimension=1, tiled=True).astype(
            jnp.float32
        ),
    )
    return (
        lax.psum_scatter(
            part[0].astype(jnp.bfloat16), "dp", scatter_dimension=0, tiled=True
        ).astype(jnp.float32),
        lax.psum_scatter(
            part[1].astype(jnp.bfloat16), "dp", scatter_dimension=0, tiled=True
        ).astype(jnp.float32),
        lax.psum_scatter(
            part[2].astype(jnp.bfloat16), "dp", scatter_dimension=0, tiled=True
        ).astype(jnp.float32),
        lax.psum_scatter(
            part[3].astype(jnp.bfloat16), "dp", scatter_dimension=0, tiled=True
        ).astype(jnp.float32),
        lax.psum_scatter(
            part[4].astype(jnp.bfloat16), "dp", scatter_dimension=0, tiled=True
        ).astype(jnp.float32),
        lax.psum_scatter(
            part[5].astype(jnp.bfloat16), "dp", scatter_dimension=0, tiled=True
        ).astype(jnp.float32),
    )


def block_layout(seq_count, row_count, head_count):
    block_seqs = math.gcd(seq_count, max(1, 512 // row_count))
    group_heads = math.gcd(head_count, 4)
    return (block_seqs, seq_count // block_seqs, group_heads, head_count // group_heads)


def head_slice(block_part, offset, group_width, group_heads):
    sliced = lax.dynamic_slice_in_dim(block_part, offset, group_width, 2)
    return sliced.reshape(sliced.shape[0], sliced.shape[1], group_heads, HD)


def attention_forward(queries, key_all, value_all, key_mask):
    seq_count, row_count, feature_total = queries.shape
    slot_count = key_all.shape[1]
    block_seqs, block_count, group_heads, group_count = block_layout(
        seq_count, row_count, feature_total // HD
    )
    group_width = group_heads * HD

    def seq_block(inputs):
        query_part, key_part, value_part, mask_part = inputs

        def head_block(group_index):
            offset = group_index * group_width
            query_heads = head_slice(query_part, offset, group_width, group_heads)
            key_heads = head_slice(key_part, offset, group_width, group_heads)
            value_heads = head_slice(value_part, offset, group_width, group_heads)
            scores = (
                jnp.einsum(
                    "brhd,bkhd->bhrk", query_heads, key_heads, preferred_element_type=jnp.float32
                )
                * 0.125
            )
            scores = jnp.where(mask_part[:, None, None, :], scores, -1e30)
            row_max = jnp.max(scores, axis=-1, keepdims=True)
            exponent = jnp.exp(scores - row_max)
            row_total = jnp.sum(exponent, axis=-1, keepdims=True)
            soft_probs = (exponent / row_total).astype(jnp.bfloat16)
            heads_out = jnp.einsum(
                "bhrk,bkhd->brhd", soft_probs, value_heads, preferred_element_type=jnp.float32
            )
            log_total = (row_max + jnp.log(row_total))[..., 0]
            return (heads_out.reshape(block_seqs, row_count, group_width), log_total)

        return lax.map(head_block, jnp.arange(group_count))

    outputs, log_totals = lax.map(
        seq_block,
        (
            queries.reshape(block_count, block_seqs, row_count, feature_total),
            key_all.reshape(block_count, block_seqs, slot_count, feature_total),
            value_all.reshape(block_count, block_seqs, slot_count, feature_total),
            key_mask.reshape(block_count, block_seqs, slot_count),
        ),
    )
    mixed_heads = outputs.transpose(0, 2, 3, 1, 4).reshape(seq_count, row_count, feature_total)
    return (mixed_heads, log_totals)


def attention_backward(queries, key_all, value_all, key_mask, heads_grad, log_totals):
    seq_count, row_count, feature_total = queries.shape
    slot_count = key_all.shape[1]
    block_seqs, block_count, group_heads, group_count = block_layout(
        seq_count, row_count, feature_total // HD
    )
    group_width = group_heads * HD

    def seq_block(inputs):
        query_part, key_part, value_part, mask_part, grad_part, total_part = inputs

        def head_block(group_index):
            offset = group_index * group_width
            query_heads = head_slice(query_part, offset, group_width, group_heads)
            key_heads = head_slice(key_part, offset, group_width, group_heads)
            value_heads = head_slice(value_part, offset, group_width, group_heads)
            grad_heads = head_slice(grad_part, offset, group_width, group_heads)
            log_total = lax.dynamic_index_in_dim(total_part, group_index, 0, keepdims=False)
            scores = (
                jnp.einsum(
                    "brhd,bkhd->bhrk", query_heads, key_heads, preferred_element_type=jnp.float32
                )
                * 0.125
            )
            scores = jnp.where(mask_part[:, None, None, :], scores, -1e30)
            soft_probs = jnp.exp(scores - log_total[..., None])
            value_grad = jnp.einsum(
                "bhrk,brhd->bkhd",
                soft_probs.astype(jnp.bfloat16),
                grad_heads,
                preferred_element_type=jnp.float32,
            )
            prob_grad = jnp.einsum(
                "brhd,bkhd->bhrk", grad_heads, value_heads, preferred_element_type=jnp.float32
            )
            inner = jnp.sum(soft_probs * prob_grad, axis=-1, keepdims=True)
            score_grad = (soft_probs * (prob_grad - inner)).astype(jnp.bfloat16)
            query_grad = (
                jnp.einsum(
                    "bhrk,bkhd->brhd", score_grad, key_heads, preferred_element_type=jnp.float32
                )
                * 0.125
            )
            key_grad = (
                jnp.einsum(
                    "bhrk,brhd->bkhd", score_grad, query_heads, preferred_element_type=jnp.float32
                )
                * 0.125
            )
            return (
                query_grad.reshape(block_seqs, row_count, group_width),
                key_grad.reshape(block_seqs, slot_count, group_width),
                value_grad.reshape(block_seqs, slot_count, group_width),
            )

        return lax.map(head_block, jnp.arange(group_count))

    query_blocks, key_blocks, value_block_list = lax.map(
        seq_block,
        (
            queries.reshape(block_count, block_seqs, row_count, feature_total),
            key_all.reshape(block_count, block_seqs, slot_count, feature_total),
            value_all.reshape(block_count, block_seqs, slot_count, feature_total),
            key_mask.reshape(block_count, block_seqs, slot_count),
            heads_grad.reshape(block_count, block_seqs, row_count, feature_total),
            log_totals,
        ),
    )
    query_grad = query_blocks.transpose(0, 2, 3, 1, 4).reshape(seq_count, row_count, feature_total)
    key_grad = key_blocks.transpose(0, 2, 3, 1, 4).reshape(seq_count, slot_count, feature_total)
    value_grad = value_block_list.transpose(0, 2, 3, 1, 4).reshape(
        seq_count, slot_count, feature_total
    )
    return (query_grad, key_grad, value_grad)


def general_body(
    tokens,
    lengths,
    cotangent,
    query_weight,
    key_weight,
    value_weight,
    out_weight,
    up_weight,
    down_weight,
    query_bias,
    value_bias,
    out_bias,
    attn_gain,
    attn_shift,
    up_bias,
    down_bias,
    feed_gain,
    feed_shift,
):
    seq_count, row_count, feature_total = tokens.shape
    slot_count = row_count * lax.axis_size("seq")
    token_count = seq_count * row_count
    whole = gather_weights(
        query_weight, key_weight, value_weight, out_weight, up_weight, down_weight
    )
    full_query, full_key, full_value, full_out, full_up, full_down = whole
    flat_tokens = tokens.reshape(token_count, feature_total)
    queries = (
        jnp.dot(flat_tokens, full_query, preferred_element_type=jnp.float32) + query_bias
    ).astype(jnp.bfloat16)
    key_rows = jnp.dot(flat_tokens, full_key, preferred_element_type=jnp.float32).astype(
        jnp.bfloat16
    )
    value_rows = (
        jnp.dot(flat_tokens, full_value, preferred_element_type=jnp.float32) + value_bias
    ).astype(jnp.bfloat16)
    first_slot = lax.axis_index("seq") * row_count
    key_mask = jnp.arange(slot_count)[None, :] < lengths[:, None]
    row_valid = ((first_slot + jnp.arange(row_count))[None, :] < lengths[:, None]).astype(
        jnp.float32
    )
    row_valid = row_valid.reshape(token_count, 1)
    query_blocks = queries.reshape(seq_count, row_count, feature_total)
    key_blocks = key_rows.reshape(seq_count, row_count, feature_total)
    value_block_list = value_rows.reshape(seq_count, row_count, feature_total)
    key_all, value_all = (
        lax.all_gather(key_blocks, "seq", axis=1, tiled=True),
        lax.all_gather(value_block_list, "seq", axis=1, tiled=True),
    )
    mixed_heads, log_totals = attention_forward(query_blocks, key_all, value_all, key_mask)
    heads_low = mixed_heads.reshape(token_count, feature_total).astype(jnp.bfloat16)
    attention_out = jnp.dot(heads_low, full_out, preferred_element_type=jnp.float32) + out_bias
    tokens_f32 = flat_tokens.astype(jnp.float32)
    first_sum = tokens_f32 + attention_out
    hidden, first_pull = jax.vjp(layer_norm, first_sum, attn_gain, attn_shift)
    hidden_low = hidden.astype(jnp.bfloat16)
    pre_act = jnp.dot(hidden_low, full_up, preferred_element_type=jnp.float32) + up_bias
    gelu_out, gelu_pull = jax.vjp(partial(jax.nn.gelu, approximate=False), pre_act)
    activation = gelu_out.astype(jnp.bfloat16)
    feed_out = jnp.dot(activation, full_down, preferred_element_type=jnp.float32) + down_bias
    result, second_pull = jax.vjp(layer_norm, hidden + feed_out, feed_gain, feed_shift)
    mixed = result.astype(jnp.bfloat16).reshape(seq_count, row_count, feature_total)
    partial_stats = jnp.stack(
        [
            jnp.sum(row_valid * tokens_f32 * tokens_f32),
            jnp.sum(row_valid * attention_out * attention_out),
            jnp.sum(row_valid * feed_out * feed_out),
            jnp.sum(row_valid) * feature_total,
        ]
    )
    back_weights = gather_weights(
        query_weight, key_weight, value_weight, out_weight, up_weight, down_weight
    )
    back_query, back_key, back_value, back_out, back_up, back_down = back_weights
    out_grad = cotangent.reshape(token_count, feature_total).astype(jnp.float32) * row_valid
    second_grad, feed_gain_grad, feed_shift_grad = second_pull(out_grad)
    feed_low = second_grad.astype(jnp.bfloat16)
    down_weight_grad = jnp.einsum(
        "nf,nd->fd", activation, feed_low, preferred_element_type=jnp.float32
    )
    down_bias_grad = jnp.sum(feed_low, axis=0, dtype=jnp.float32)
    act_grad = jnp.einsum(
        "nd,fd->nf", feed_low, back_down, preferred_element_type=jnp.float32
    ).astype(jnp.bfloat16)
    pre_grad = gelu_pull(act_grad.astype(jnp.float32))[0].astype(jnp.bfloat16)
    up_weight_grad = jnp.einsum(
        "nd,nf->df", hidden_low, pre_grad, preferred_element_type=jnp.float32
    )
    up_bias_grad = jnp.sum(pre_grad, axis=0, dtype=jnp.float32)
    hidden_grad = (
        jnp.einsum("nf,df->nd", pre_grad, back_up, preferred_element_type=jnp.float32) + second_grad
    )
    first_grad, attn_gain_grad, attn_shift_grad = first_pull(hidden_grad)
    attn_low = first_grad.astype(jnp.bfloat16)
    out_weight_grad = jnp.einsum(
        "nd,ne->de", heads_low, attn_low, preferred_element_type=jnp.float32
    )
    out_bias_grad = jnp.sum(attn_low, axis=0, dtype=jnp.float32)
    heads_grad = jnp.einsum(
        "ne,de->nd", attn_low, back_out, preferred_element_type=jnp.float32
    ).astype(jnp.bfloat16)
    heads_grad = heads_grad.reshape(seq_count, row_count, feature_total)
    query_grad, key_part_grad, value_part_grad = attention_backward(
        query_blocks, key_all, value_all, key_mask, heads_grad, log_totals
    )
    key_sum, value_sum = (
        lax.psum_scatter(
            key_part_grad.astype(jnp.bfloat16), "seq", scatter_dimension=1, tiled=True
        ).astype(jnp.float32),
        lax.psum_scatter(
            value_part_grad.astype(jnp.bfloat16), "seq", scatter_dimension=1, tiled=True
        ).astype(jnp.float32),
    )
    query_low = query_grad.reshape(token_count, feature_total).astype(jnp.bfloat16)
    key_low = key_sum.reshape(token_count, feature_total).astype(jnp.bfloat16)
    value_low = value_sum.reshape(token_count, feature_total).astype(jnp.bfloat16)
    query_weight_grad = jnp.einsum(
        "nd,ne->de", flat_tokens, query_low, preferred_element_type=jnp.float32
    )
    key_weight_grad = jnp.einsum(
        "nd,ne->de", flat_tokens, key_low, preferred_element_type=jnp.float32
    )
    value_weight_grad = jnp.einsum(
        "nd,ne->de", flat_tokens, value_low, preferred_element_type=jnp.float32
    )
    query_bias_grad = jnp.sum(query_low, axis=0, dtype=jnp.float32)
    value_bias_gradient = jnp.sum(value_low, axis=0, dtype=jnp.float32)
    tokens_grad = (
        jnp.einsum("ne,de->nd", query_low, back_query, preferred_element_type=jnp.float32)
        + jnp.einsum("ne,de->nd", key_low, back_key, preferred_element_type=jnp.float32)
        + jnp.einsum("ne,de->nd", value_low, back_value, preferred_element_type=jnp.float32)
        + first_grad
    )
    tokens_grad = tokens_grad.astype(jnp.bfloat16).reshape(seq_count, row_count, feature_total)
    matrix_grads = reduce_grads(
        query_weight_grad,
        key_weight_grad,
        value_weight_grad,
        out_weight_grad,
        up_weight_grad,
        down_weight_grad,
    )
    totals = lax.psum(
        (
            partial_stats,
            query_bias_grad,
            value_bias_gradient,
            out_bias_grad,
            attn_gain_grad,
            attn_shift_grad,
            up_bias_grad,
            down_bias_grad,
            feed_gain_grad,
            feed_shift_grad,
        ),
        ("dp", "seq"),
    )
    stream_rms = jnp.sqrt(totals[0][:3] / totals[0][3])
    return (
        mixed,
        tokens_grad,
        matrix_grads[0],
        matrix_grads[1],
        matrix_grads[2],
        matrix_grads[3],
        matrix_grads[4],
        matrix_grads[5],
        totals[1],
        totals[2],
        totals[3],
        totals[4],
        totals[5],
        totals[6],
        totals[7],
        totals[8],
        totals[9],
        stream_rms,
    )


def swap(value, axis):
    return lax.ppermute(value, axis, [(0, 1), (1, 0)])


def both(value, axis):
    return jnp.concatenate([value, swap(value, axis)], axis=0)


def in_order(own, other, index, axis=0):
    return jnp.where(
        index == 0, jnp.stack([own, other], axis=axis), jnp.stack([other, own], axis=axis)
    )


def pick(values, index, axis):
    return lax.dynamic_index_in_dim(values, index, axis, keepdims=False)


def add(left, right):
    return (left.astype(jnp.float32) + right.astype(jnp.float32)).astype(jnp.bfloat16)


def fold(values, axis, dim):
    index = lax.axis_index(axis)
    return add(pick(values, index, dim), swap(pick(values, 1 - index, dim), axis))


NEXT = [(0, 1), (1, 0), (2, 3), (3, 2)]
CROSS = [(0, 2), (2, 0), (1, 3), (3, 1)]


def fold_cross(pairs):
    upper = lax.axis_index("z") // 2
    return add(pick(pairs, upper, 0), lax.ppermute(pick(pairs, 1 - upper, 0), "z", CROSS))


def fold_line(values):
    odd = lax.axis_index("z") % 2
    pairs = values.reshape((2, 2) + values.shape[1:])
    sent = lax.ppermute(pick(pairs, 1 - odd, 1), "z", NEXT)
    return fold_cross(add(pick(pairs, odd, 1), sent))


def line_cross(value):
    return lax.ppermute(value, "z", CROSS)


def line_next(pair):
    return lax.ppermute(pair, "z", NEXT)


def gather_square(own, way):
    beside, below = swap(own, "x"), swap(own, "s")
    across = swap(below, "x") if way == "x" else swap(beside, "s")
    return [own, beside, below, across]


def fold_columns(total):
    half = lax.axis_index("s")
    return add(columns_of(total, half), swap(columns_of(total, 1 - half), "s"))


def halve(values, axis, dim):
    index = lax.axis_index(axis) % 2
    return pick(values, index, dim), pick(values, 1 - index, dim)


def line_parts(values):
    return halve(values.reshape((2, 2) + values.shape[1:]), "z", 1)


def scatter_top(send, keep):
    total = add(keep, swap(send, "s"))
    total = total.reshape((4, 2) + total.shape[1:])
    return fold_line(fold(total, "x", 1))


def grad_block(left_t, right, got=None):
    total = product(left_t, right, 1, 0)
    if got is not None:
        total = total + got.astype(jnp.float32)
    return total.astype(jnp.bfloat16)


def columns_of(right, index):
    columns = right.shape[-1] // 2
    return lax.dynamic_slice_in_dim(right, index * columns, columns, right.ndim - 1)


PAIR = 2 * HD
LIMIT = 10 * 1024 * 1024


def kernel_params(steps):
    return pltpu.CompilerParams(
        dimension_semantics=("arbitrary",) * steps, vmem_limit_bytes=LIMIT
    )


def product(left, right, left_dim, right_dim):
    return lax.dot_general(
        left, right, (((left_dim,), (right_dim,)), ((), ())), preferred_element_type=jnp.float32
    )


def key_bias(facts_ref, slots):
    place = lax.broadcasted_iota(jnp.int32, (slots, 1), 0) + facts_ref[2]
    place = jnp.where(place >= slots, place - slots, place)
    return jnp.where(place < facts_ref[pl.program_id(0)], 0.0, -1e30)


def head_lanes(value, head):
    lane = lax.broadcasted_iota(jnp.int32, value.shape, 1)
    return jnp.where((lane >= HD) == (head == 1), value, jnp.zeros_like(value))


def turned(value):
    return value.astype(jnp.float32).T


def attend_kernel(facts_ref, query_ref, key_ref, value_ref, out_ref, total_ref):
    slots = key_ref.shape[0]
    bias = key_bias(facts_ref, slots)
    query = query_ref[...] * jnp.bfloat16(0.125)
    key = key_ref[...]
    value_t = turned(value_ref[...]).astype(jnp.bfloat16)
    outs = []
    for head in range(2):
        scores = product(key, head_lanes(query, head), 1, 1) + bias
        peak = jnp.max(scores, axis=0, keepdims=True)
        weight = jnp.exp(scores - peak)
        total = jnp.sum(weight, axis=0, keepdims=True)
        part = product(value_t[head * HD : (head + 1) * HD], weight.astype(jnp.bfloat16), 1, 0)
        outs.append(part * (1.0 / total))
        total_ref[0, 0, head : head + 1, :] = peak + jnp.log(total)
    out_ref[...] = jnp.concatenate(outs, axis=0).T.astype(jnp.bfloat16)


def attend_back_kernel(
    facts_ref, query_ref, key_ref, value_ref, grad_ref, total_ref, low_ref, sums_ref
):
    slots = key_ref.shape[0]
    bias = key_bias(facts_ref, slots)
    query = query_ref[...] * jnp.bfloat16(0.125)
    key = key_ref[...]
    value = value_ref[...]
    grad = grad_ref[...]
    key_t = turned(key).astype(jnp.bfloat16)
    lane = lax.broadcasted_iota(jnp.int32, (slots, PAIR), 1)
    query_parts, key_parts, value_parts = [], [], []
    for head in range(2):
        scores = product(key, head_lanes(query, head), 1, 1) + bias
        soft = jnp.exp(scores - total_ref[0, 0, head : head + 1, :])
        value_parts.append(product(soft.astype(jnp.bfloat16), grad, 1, 0))
        change = product(value, head_lanes(grad, head), 1, 1)
        inner = jnp.sum(soft * change, axis=0, keepdims=True)
        change = (soft * (change - inner)).astype(jnp.bfloat16)
        key_parts.append(product(change, query, 1, 0))
        query_parts.append(product(key_t[head * HD : (head + 1) * HD], change, 1, 0))
    pair = pl.program_id(1)
    groups = low_ref.shape[1] // 3
    query_low = (jnp.concatenate(query_parts, axis=0) * 0.125).T
    key_low = jnp.where(lane < HD, key_parts[0], key_parts[1])
    value_low = jnp.where(lane < HD, value_parts[0], value_parts[1])
    for place, part in enumerate((query_low, key_low, value_low)):
        start = pl.multiple_of(place * groups + pair * PAIR, PAIR)
        low = part.astype(jnp.bfloat16)
        low_ref[:, pl.ds(start, PAIR)] = low
        sums_ref[0, :, pl.ds(start, PAIR)] = jnp.sum(
            low.astype(jnp.float32), axis=0, keepdims=True
        )


def attention_specs(slots, pairs):
    def at(part):
        return pl.BlockSpec(
            (slots, PAIR), lambda b, g, p, *_: (b, g * 3 * pairs + part * pairs + p)
        )

    heads = pl.BlockSpec((slots, PAIR), lambda b, g, p, *_: (b, g * pairs + p))
    totals = pl.BlockSpec((1, 1, 2, slots), lambda b, g, p, *_: (b, g * pairs + p, 0, 0))
    return [at(0), at(1), at(2)], heads, totals


def attend(facts, projected, slots, wait=()):
    pairs = projected.shape[1] // (6 * PAIR)
    inputs, heads, totals = attention_specs(slots, pairs)
    rows = projected.shape[0]
    return call(
        attend_kernel,
        "attend",
        (2, 2, pairs),
        inputs,
        [heads, totals],
        [
            like((rows, 2 * pairs * PAIR), jnp.bfloat16),
            like((2, 2 * pairs, 2, slots), jnp.float32),
        ],
        facts,
        projected,
        projected,
        projected,
        wait=wait,
    )


def attend_back(facts, projected, heads_grad, totals_in, slots, own, wait=(), through=()):
    pairs = projected.shape[1] // (6 * PAIR)

    def group(facts_ref):
        return facts_ref[3] if own else 1 - facts_ref[3]

    def at(part):
        return pl.BlockSpec(
            (slots, PAIR), lambda b, p, f: (b, group(f) * 3 * pairs + part * pairs + p)
        )

    heads = pl.BlockSpec((slots, PAIR), lambda b, p, f: (b, group(f) * pairs + p))
    totals = pl.BlockSpec((1, 1, 2, slots), lambda b, p, f: (b, group(f) * pairs + p, 0, 0))
    width = 3 * pairs * PAIR
    return call(
        attend_back_kernel,
        "attend_back",
        (2, pairs),
        [at(0), at(1), at(2), heads, totals],
        [
            pl.BlockSpec((slots, width), lambda b, p, f: (b, 0)),
            pl.BlockSpec((1, 1, width), lambda b, p, f: (b, 0, 0)),
        ],
        [
            like((2 * slots, width), jnp.bfloat16),
            like((2, 1, width), jnp.float32),
        ],
        facts,
        projected,
        projected,
        projected,
        heads_grad,
        totals_in,
        wait=wait,
        through=through,
    )


def call(kernel, name, grid, inputs, outputs, shapes, facts, *args, wait=(), scratch=(), through=(), into=()):
    single = not isinstance(outputs, list)
    outputs, shapes = ([outputs], [shapes]) if single else (outputs, shapes)
    wait = tuple(into) + tuple(wait)
    count, held, passed = len(args), len(wait) + len(through), len(through)
    last = count + held + len(outputs)

    def body(facts_ref, *refs):
        kernel(facts_ref, *refs[:count], *refs[count + held : last], *refs[last + passed + 1 :])
        for place in range(facts.shape[0]):
            refs[last + passed][place] = facts_ref[place]

    results = pl.pallas_call(
        body,
        grid_spec=pltpu.PrefetchScalarGridSpec(
            num_scalar_prefetch=1,
            grid=grid,
            in_specs=list(inputs) + [pl.BlockSpec(memory_space=pl.ANY)] * held,
            out_specs=list(outputs)
            + [pl.BlockSpec(memory_space=pl.ANY)] * passed
            + [pl.BlockSpec(memory_space=pltpu.SMEM)],
            scratch_shapes=list(scratch),
        ),
        out_shape=list(shapes)
        + [like(value.shape, value.dtype) for value in through]
        + [like(facts.shape, jnp.int32)],
        input_output_aliases={
            **{1 + count + i: i for i in range(len(into))},
            **{1 + count + len(wait) + i: len(outputs) + i for i in range(passed)},
        },
        compiler_params=kernel_params(len(grid)),
        name=name,
    )(facts, *args, *wait, *through)
    values = tuple(results[:-1])
    return (values[0] if single and not passed else values), results[-1]


def block(shape, *index):
    def at(*grid_and_facts):
        return tuple(entry(*grid_and_facts) if callable(entry) else entry for entry in index)

    return pl.BlockSpec(shape, at)


def whole(array):
    zeros = (0,) * array.ndim
    return pl.BlockSpec(array.shape, lambda *_: zeros)


def first(i, *_):
    return i


def like(shape, dtype):
    return jax.ShapeDtypeStruct(shape, dtype)


def rows_in_order(facts_ref, own, beside):
    even = facts_ref[4] == 0
    pieces = []
    for z in range(4):
        pieces += [jnp.where(even, own[z], beside[z]), jnp.where(even, beside[z], own[z])]
    return jnp.concatenate(pieces, axis=0)


def near_or_far(facts_ref, refs, near):
    own, beside, below, across = [ref[...] for ref in refs]
    return rows_in_order(
        facts_ref, jnp.where(near, own, below), jnp.where(near, beside, across)
    )


def square_columns(parts, wide, steps):
    shape = parts[0].shape[:2] + (wide,)
    near = block(shape, 0, 0, lambda i, *_: jnp.minimum(i, steps - 1))
    far = block(shape, 0, 0, lambda i, *_: jnp.maximum(i - steps, 0))
    return [near, near, far, far]


def half_at(i, facts, steps):
    return jnp.where(i < steps, facts[3], 1 - facts[3])


def gate_kernel(facts_ref):
    del facts_ref


def gate(facts, through, wait):
    return call(gate_kernel, "gate", (1,), [], [], [], facts, wait=wait, through=through)


def stack_kernel(own_at, facts_ref, own_ref, other_ref, out_ref):
    own = facts_ref[own_at] == pl.program_id(0)
    value = jnp.where(own, own_ref[...], other_ref[...])
    out_ref[...] = value.reshape(out_ref.shape)


def stack_pair(facts, own, other, wait=(), through=()):
    rows, columns = own.shape
    return call(
        partial(stack_kernel, 6),
        "stack",
        (2,),
        [whole(own), whole(other)],
        block((1, rows, columns), first, 0, 0),
        like((2, rows, columns), own.dtype),
        facts,
        own,
        other,
        wait=wait,
        through=through,
    )


def stack_line(facts, own, other, wait=()):
    _, rows, columns = own.shape
    line, facts = call(
        partial(stack_kernel, 7),
        "stack_line",
        (2,),
        [whole(own), whole(other)],
        block((2, 1, rows, columns), 0, first, 0, 0),
        like((2, 2, rows, columns), own.dtype),
        facts,
        own,
        other,
        wait=wait,
    )
    return line.reshape(4, rows, columns), facts


def turn_kernel(facts_ref, *refs):
    for i in range(2):
        refs[4 + i][...] = jnp.concatenate([refs[2 * i][...].T, refs[2 * i + 1][...].T], axis=1)


def turn_all_kernel(facts_ref, rows_ref, out_ref):
    out_ref[...] = rows_ref[...].T


def turn_all(facts, values, wait=()):
    count, width = values.shape
    step = width // 4
    return call(
        turn_all_kernel,
        "turn_all",
        (4,),
        [block((count, step), 0, first)],
        block((step, count), first, 0),
        like((width, count), values.dtype),
        facts,
        values,
        wait=wait,
    )


def turn(facts, values, others, rows, wait=()):
    count, width = values.shape
    half = width // 2
    out = block((rows, 2 * count), first, 0)
    shape = like((half, 2 * count), values.dtype)
    own = block((count, rows), 0, lambda i, f: 2 * i + f[4])
    other = block((count, rows), 0, lambda i, f: 2 * i + 1 - f[4])
    return call(
        turn_kernel,
        "turn",
        (half // rows,),
        [own, own, other, other],
        [out, out],
        [shape, shape],
        facts,
        values,
        others,
        values,
        others,
        wait=wait,
    )


def project_kernel(facts_ref, rows_ref, bias_ref, *refs):
    parts, (out_ref, in_ref, rest_ref) = refs[:4], refs[4:]
    step = pl.program_id(0)
    weight = near_or_far(facts_ref, parts, step < 4)

    @pl.when(step % 4 < 3)
    def _():
        in_ref[...] = weight
        value = product(rows_ref[...], weight, 1, 0) + bias_ref[...]
        out_ref[...] = value.astype(jnp.bfloat16)

    @pl.when(step % 4 == 3)
    def _():
        chips, count, wide = rest_ref.shape
        pairs = weight.reshape(chips, 2, count, wide // 2)
        rest_ref[...] = jnp.concatenate([pairs[:, 0], pairs[:, 1]], axis=2)


def project(facts, rows, bias, parts, wait=()):
    count, width = rows.shape
    wide = parts[0].shape[2] // 4

    def column(i, f):
        return half_at(i, f, 4) * 3 + jnp.minimum(i % 4, 2)

    out = block((count, wide), 0, column)
    rest = (8, parts[0].shape[1] // 2, 2 * wide)
    return call(
        project_kernel,
        "project",
        (8,),
        [whole(rows), block((1, wide), 0, column)] + square_columns(parts, wide, 4),
        [out, block((width, wide), 0, column), block(rest, 0, 0, lambda i, f: half_at(i, f, 4))],
        [
            like((count, 6 * wide), jnp.bfloat16),
            like((width, 6 * wide), jnp.bfloat16),
            like(rest[:2] + (4 * wide,), jnp.bfloat16),
        ],
        facts,
        rows,
        bias[None],
        *parts,
        wait=wait,
    )


def valid_rows(facts_ref, count, slots):
    place = lax.broadcasted_iota(jnp.int32, (count, 1), 0) + pl.program_id(0) * count + facts_ref[2]
    place = jnp.where(place >= slots, place - slots, place)
    return (place < facts_ref[0]).astype(jnp.float32)


def add_rows(sums_ref, rows):
    total = jnp.concatenate([jnp.sum(part, axis=0, keepdims=True) for part in rows], axis=0)
    total = jnp.concatenate([total, jnp.zeros((8 - len(rows), total.shape[1]), jnp.float32)], axis=0)

    @pl.when(pl.program_id(0) == 0)
    def _():
        sums_ref[...] = total

    @pl.when(pl.program_id(0) > 0)
    def _():
        sums_ref[...] += total


def mean_of(values):
    return jnp.mean(values, axis=-1, keepdims=True)


def attend_out_kernel(
    slots, facts_ref, own_ref, other_ref, own_weight_ref, other_weight_ref, tokens_ref, vectors_ref,
    hat_ref, rstd_ref, low_ref, sums_ref,
):
    branch = (
        product(own_ref[...], own_weight_ref[...], 1, 0)
        + product(other_ref[...], other_weight_ref[...], 1, 0)
        + vectors_ref[0:1]
    )
    tokens = tokens_ref[...].astype(jnp.float32)
    total = tokens + branch
    centered = total - mean_of(total)
    rstd = lax.rsqrt(mean_of(centered * centered) + 1e-05)
    hat = centered * rstd
    hat_ref[...] = hat
    rstd_ref[...] = rstd
    low_ref[...] = (hat * vectors_ref[1:2] + vectors_ref[2:3]).astype(jnp.bfloat16)
    valid = valid_rows(facts_ref, tokens.shape[0], slots)
    add_rows(sums_ref, [valid * tokens * tokens, valid * branch * branch])


def attend_out(facts, own, other, own_weight, other_weight, tokens, vectors, wait=()):
    slots, width = tokens.shape
    step = slots // 4
    rows = lambda array: block((step, array.shape[1]), first, 0)
    return call(
        partial(attend_out_kernel, slots),
        "attend_out",
        (4,),
        [rows(own), rows(other), whole(own_weight), whole(other_weight), rows(tokens), whole(vectors)],
        [block((step, width), first, 0), block((step, 1), first, 0), block((step, width), first, 0), block((8, width), 0, 0)],
        [
            like((slots, width), jnp.float32),
            like((slots, 1), jnp.float32),
            like((slots, width), jnp.bfloat16),
            like((8, width), jnp.float32),
        ],
        facts,
        own,
        other,
        own_weight,
        other_weight,
        tokens,
        vectors,
        wait=wait,
    )


def up_kernel(facts_ref, rows_ref, others_ref, bias_ref, *refs):
    parts, (act_ref, slope_ref, turned_ref, weight_ref) = refs[:4], refs[4:]
    weight = near_or_far(facts_ref, parts, pl.program_id(0) < 4)
    weight_ref[...] = weight
    pre_act = [product(ref[...], weight, 1, 0) for ref in (rows_ref, others_ref)]
    pre_act = jnp.concatenate(pre_act, axis=0) + bias_ref[...]
    below = 0.5 + 0.5 * lax.erf(pre_act * 0.7071067811865476)
    act = (pre_act * below).astype(jnp.bfloat16)
    act_ref[...] = act
    turned_ref[...] = act.T
    slope = below + pre_act * (0.3989422804014327 * jnp.exp(-0.5 * pre_act * pre_act))
    slope_ref[...] = slope.astype(jnp.bfloat16)


def feed_up(facts, rows, others, bias, parts, wait=()):
    count, width = 2 * rows.shape[0], rows.shape[1]
    units = bias.shape[0]
    wide = units // 8

    def column(i, f):
        return half_at(i, f, 4) * 4 + i % 4

    shape = like((count, units), jnp.bfloat16)
    out = block((count, wide), 0, column)
    return call(
        up_kernel,
        "feed_up",
        (8,),
        [whole(rows), whole(others), block((1, wide), 0, column)] + square_columns(parts, wide, 4),
        [out, out, block((wide, count), column, 0), block((width, wide), 0, column)],
        [
            shape,
            shape,
            like((units, count), jnp.bfloat16),
            like((width, units), jnp.bfloat16),
        ],
        facts,
        rows,
        others,
        bias[None],
        *parts,
        wait=wait,
    )


def down_kernel(facts_ref, rows_ref, *refs):
    parts, (weight_ref, out_ref, total_ref) = refs[:4], refs[4:]
    step = pl.program_id(0)
    own, beside, below, across = [ref[0] for ref in parts]
    even, left = facts_ref[4] == 0, facts_ref[3] == 0
    for x in range(2):
        mine = jnp.where(even, own, beside) if x == 0 else jnp.where(even, beside, own)
        theirs = jnp.where(even, below, across) if x == 0 else jnp.where(even, across, below)
        weight_ref[x] = jnp.concatenate(
            [jnp.where(left, mine, theirs), jnp.where(left, theirs, mine)], axis=1
        )
    weight = weight_ref[...].reshape(rows_ref.shape[1], out_ref.shape[1])
    value = product(rows_ref[...], weight, 1, 0)

    @pl.when(step == 0)
    def _():
        total_ref[...] = value

    @pl.when(step > 0)
    def _():
        total_ref[...] += value

    @pl.when(step == 3)
    def _():
        out_ref[...] = total_ref[...].astype(jnp.bfloat16)


def feed_down(facts, rows, parts, wait=()):
    count, units = rows.shape
    _, block_rows, half_width = parts[0].shape
    width = 2 * half_width
    shape = (1,) + parts[0].shape[1:]
    return call(
        down_kernel,
        "feed_down",
        (4,),
        [block((count // 2, units // 4), 1, first)] + [block(shape, first, 0, 0)] * 4,
        [block((2, block_rows, width), first, 0, 0), block((count // 2, width), 0, 0)],
        [like((8, block_rows, width), jnp.bfloat16), like((count // 2, width), jnp.bfloat16)],
        facts,
        rows,
        *parts,
        scratch=[pltpu.VMEM((count // 2, width), jnp.float32)],
        wait=wait,
    )


def second_norm_kernel(
    slots, facts_ref, part_ref, other_ref, hat_ref, cotangent_ref, vectors_ref,
    mixed_ref, grad_ref, low_ref, sums_ref,
):
    branch = part_ref[...] + other_ref[...].astype(jnp.float32) + vectors_ref[0:1]
    hidden = hat_ref[...] * vectors_ref[1:2] + vectors_ref[2:3]
    gain = vectors_ref[3:4]
    total = hidden + branch
    centered = total - mean_of(total)
    rstd = lax.rsqrt(mean_of(centered * centered) + 1e-05)
    hat = centered * rstd
    mixed_ref[...] = (hat * gain + vectors_ref[4:5]).astype(jnp.bfloat16)
    valid = valid_rows(facts_ref, branch.shape[0], slots)
    grad = cotangent_ref[...].astype(jnp.float32) * valid
    scaled = grad * gain
    result = rstd * (scaled - mean_of(scaled) - hat * mean_of(scaled * hat))
    low = result.astype(jnp.bfloat16)
    grad_ref[...] = result
    low_ref[...] = low
    add_rows(sums_ref, [low.astype(jnp.float32), grad * hat, grad, valid * branch * branch])


def second_norm(facts, part, other, hat, cotangent, vectors, wait=()):
    slots, width = part.shape
    step = slots // 4
    rows = block((step, width), first, 0)
    return call(
        partial(second_norm_kernel, slots),
        "second_norm",
        (4,),
        [rows, rows, rows, rows, whole(vectors)],
        [rows, rows, rows, block((8, width), 0, 0)],
        [
            like((slots, width), jnp.bfloat16),
            like((slots, width), jnp.float32),
            like((slots, width), jnp.bfloat16),
            like((8, width), jnp.float32),
        ],
        facts,
        part,
        other,
        hat,
        cotangent,
        vectors,
        wait=wait,
    )


def first_norm_kernel(
    facts_ref, part_ref, other_ref, second_ref, hat_ref, rstd_ref, vectors_ref,
    grad_ref, low_ref, sums_ref,
):
    grad = part_ref[...] + other_ref[...].astype(jnp.float32) + second_ref[...]
    hat = hat_ref[...]
    scaled = grad * vectors_ref[1:2]
    result = rstd_ref[...] * (scaled - mean_of(scaled) - hat * mean_of(scaled * hat))
    low = result.astype(jnp.bfloat16)
    grad_ref[...] = result
    low_ref[...] = low
    add_rows(sums_ref, [low.astype(jnp.float32), grad * hat, grad])


def first_norm(facts, part, other, second, hat, rstd, vectors, wait=()):
    slots, width = part.shape
    step = slots // 4
    rows = block((step, width), first, 0)
    return call(
        first_norm_kernel,
        "first_norm",
        (4,),
        [rows, rows, rows, rows, block((step, 1), first, 0), whole(vectors)],
        [rows, rows, block((8, width), 0, 0)],
        [
            like((slots, width), jnp.float32),
            like((slots, width), jnp.bfloat16),
            like((8, width), jnp.float32),
        ],
        facts,
        part,
        other,
        second,
        hat,
        rstd,
        vectors,
        wait=wait,
    )


def act_grad_kernel(facts_ref, rows_ref, weight_ref, slope_ref, out_ref, sums_ref):
    total = product(rows_ref[...], weight_ref[...], 1, 1)
    grad = total.astype(jnp.bfloat16).astype(jnp.float32) * slope_ref[...].astype(jnp.float32)
    low = grad.astype(jnp.bfloat16)
    out_ref[...] = low
    sums_ref[...] = jnp.sum(low.astype(jnp.float32), axis=0, keepdims=True)


def act_grad(facts, rows, weight, slope, wait=()):
    count, units = slope.shape
    step = units // 8
    out = block((count, step), 0, first)
    return call(
        act_grad_kernel,
        "act_grad",
        (8,),
        [whole(rows), block((step, rows.shape[1]), first, 0), out],
        [out, block((1, step), 0, first)],
        [like((count, units), jnp.bfloat16), like((1, units), jnp.float32)],
        facts,
        rows,
        weight,
        slope,
        wait=wait,
    )


def tokens_grad_kernel(facts_ref, mine_ref, theirs_ref, weight_ref, out_ref, sent_ref):
    wide = mine_ref.shape[1]
    slots = out_ref.shape[0]
    half = facts_ref[3]
    mine = weight_ref[:, pl.ds(pl.multiple_of(half * wide, 128), wide)]
    theirs = weight_ref[:, pl.ds(pl.multiple_of((1 - half) * wide, 128), wide)]
    total = product(mine_ref[...], mine, 1, 1) + product(theirs_ref[...], theirs, 1, 1)
    out_ref[...] = total[:slots]
    sent_ref[...] = total[slots:].astype(sent_ref.dtype)


def tokens_grad(facts, mine, theirs, weight, wait=(), through=()):
    count, columns = mine.shape
    width = weight.shape[0]
    step = width // 4
    out = block((count // 2, step), 0, first)
    return call(
        tokens_grad_kernel,
        "tokens_grad",
        (4,),
        [whole(mine), whole(theirs), block((step, 2 * columns), first, 0)],
        [out, out],
        [
            like((count // 2, width), jnp.float32),
            like((count // 2, width), jnp.bfloat16),
        ],
        facts,
        mine,
        theirs,
        weight,
        wait=wait,
        through=through,
    )


def add_parts_kernel(facts_ref, own_ref, got_ref, kept_ref, sent_ref):
    step = pl.program_id(0)
    total = own_ref[...].astype(jnp.float32) + got_ref[...].astype(jnp.float32)
    total = total.astype(jnp.bfloat16)

    @pl.when(step < 2)
    def _():
        sent_ref[...] = total

    @pl.when(step >= 2)
    def _():
        kept_ref[...] = total


def add_last_kernel(facts_ref, own_ref, got_ref, kept_ref, sent_ref):
    total = own_ref[0].astype(jnp.float32) + got_ref[0].astype(jnp.float32)
    total = total.astype(jnp.bfloat16)

    @pl.when(pl.program_id(0) == 0)
    def _():
        sent_ref[...] = total

    @pl.when(pl.program_id(0) == 1)
    def _():
        kept_ref[...] = total


def add_last(facts, own, got, wait=(), through=()):
    _, rows, columns = own.shape
    part = block((1, rows, columns), lambda i, f: jnp.where(i == 0, 1 - f[6], f[6]), 0, 0)
    shape = like((rows, columns), jnp.bfloat16)
    out = block((rows, columns), 0, 0)
    return call(
        add_last_kernel,
        "add_last",
        (2,),
        [part, part],
        [out, out],
        [shape, shape],
        facts,
        own,
        got,
        wait=wait,
        through=through,
    )


def add_parts(facts, own, got, wait=(), through=()):
    _, rows, columns = own.shape
    shape = (1, rows, columns)
    part = block(shape, lambda i, f: 2 * (i % 2) + jnp.where(i < 2, 1 - f[7], f[7]), 0, 0)
    half = like((2, rows, columns), jnp.bfloat16)
    return call(
        add_parts_kernel,
        "add_parts",
        (4,),
        [part, part],
        [
            block(shape, lambda i, *_: jnp.maximum(i - 2, 0), 0, 0),
            block(shape, lambda i, *_: jnp.minimum(i, 1), 0, 0),
        ],
        [half, half],
        facts,
        own,
        got,
        wait=wait,
        through=through,
    )


def alternate(value, width, offset):
    starts = range(offset * width, value.shape[1], 2 * width)
    return jnp.concatenate([value[:, start : start + width] for start in starts], axis=1)


def deal_kernel(unit_block, core_ref, query_ref, key_ref, value_ref, up_ref, *refs):
    first_core = core_ref[0] == 0
    near = [ref[...] for ref in (query_ref, key_ref, value_ref)]
    even = jnp.concatenate([alternate(value, HD, 0) for value in near], axis=1)
    odd = jnp.concatenate([alternate(value, HD, 1) for value in near], axis=1)
    up = up_ref[...]
    up_even, up_odd = alternate(up, unit_block, 0), alternate(up, unit_block, 1)
    refs[0][...] = jnp.where(first_core, even, odd)
    refs[1][...] = jnp.where(first_core, odd, even)
    refs[2][...] = jnp.where(first_core, up_even, up_odd)
    refs[3][...] = jnp.where(first_core, up_odd, up_even)


def deal(core, query, key, value, up, unit_block):
    near = like((query.shape[0], 3 * query.shape[1] // 2), jnp.bfloat16)
    half = like((up.shape[0], up.shape[1] // 2), jnp.bfloat16)
    shapes = [near, near, half, half]
    return call(
        partial(deal_kernel, unit_block),
        "deal",
        (1,),
        [whole(value) for value in (query, key, value, up)],
        [whole(shape) for shape in shapes],
        shapes,
        core,
        query,
        key,
        value,
        up,
    )


def lay_out_kernel(core_ref, near_ref, near_got_ref, out_ref, up_ref, up_got_ref, *refs):
    first_core = core_ref[0] == 0
    near, near_got, up, up_got = [
        ref[...] for ref in (near_ref, near_got_ref, up_ref, up_got_ref)
    ]
    out = out_ref[...]
    wide = out.shape[1] // 2
    near_rows = jnp.concatenate(
        [jnp.where(first_core, near, near_got), jnp.where(first_core, near_got, near)], axis=0
    )
    out_rows = jnp.concatenate([out[:, :wide], out[:, wide:]], axis=0)
    refs[0][...] = jnp.concatenate([near_rows, out_rows], axis=1)
    refs[1][...] = jnp.concatenate(
        [jnp.where(first_core, up, up_got), jnp.where(first_core, up_got, up)], axis=0
    )


def lay_out(core, near, near_got, out, up, up_got):
    rows = 2 * near.shape[0]
    shapes = [
        like((rows, near.shape[1] + out.shape[1] // 2), jnp.bfloat16),
        like((rows, up.shape[1]), jnp.bfloat16),
    ]
    arrays = (near, near_got, out, up, up_got)
    return call(
        lay_out_kernel,
        "lay_out",
        (1,),
        [whole(value) for value in arrays],
        [whole(shape) for shape in shapes],
        shapes,
        core,
        *arrays,
    )[0]


def split_body(
    tokens,
    lengths,
    cotangent,
    query_weight,
    key_weight,
    value_weight,
    out_weight,
    up_weight,
    down_weight,
    query_bias,
    value_bias,
    out_bias,
    attn_gain,
    attn_shift,
    up_bias,
    down_bias,
    feed_gain,
    feed_shift,
):
    core = lax.axis_index("c")
    half = lax.axis_index("s")
    row_count, width = tokens.shape[1:]
    slots = 2 * row_count
    unit_block = down_weight.shape[0]
    units = up_bias.shape[0] // 2
    cols = width // 2
    wide = cols // 2

    def to_sequence(values):
        return jnp.concatenate([pick(values, half, 0), swap(pick(values, 1 - half, 0), "s")], axis=0)

    def from_sequence(values):
        return in_order(values[:row_count], swap(values[row_count:], "s"), half)

    place = jnp.stack([core]).astype(jnp.int32)
    (near_kept, near_sent, up_kept, up_sent), place = deal(
        place, query_weight, key_weight, value_weight, up_weight, unit_block
    )
    near_mine, up_mine = lay_out(
        place, near_kept, swap(near_sent, "c"), out_weight, up_kept, swap(up_sent, "c")
    )
    rows, up_cols = up_mine.shape
    line = lax.axis_index("z")
    length_own = lax.dynamic_slice_in_dim(lengths, half, 1, 0)
    facts = jnp.concatenate(
        [
            both(length_own, "c"),
            jnp.stack(
                [
                    half * row_count,
                    half,
                    lax.axis_index("x"),
                    jnp.int32(0),
                    line // 2,
                    line % 2,
                ]
            ).astype(jnp.int32),
        ]
    )
    tokens_own = to_sequence(tokens)
    cotangent_own = to_sequence(cotangent)
    (near, up_mine, down_mine), facts = stack_pair(
        facts,
        near_mine,
        line_cross(near_mine),
        wait=(tokens_own,),
        through=(up_mine, down_weight),
    )
    near, facts = stack_line(facts, near, line_next(near), wait=(cotangent_own,))
    near_parts = gather_square(near, "x")
    up_pairs, facts = stack_pair(facts, up_mine, line_cross(up_mine), wait=(near,))
    tokens_both = both(tokens_own, "c")
    up_part, facts = stack_line(
        facts, up_pairs, line_next(up_pairs), wait=(near_parts[1], near_parts[2])
    )
    up_parts = gather_square(up_part, "s")
    down_pairs, facts = stack_pair(facts, down_mine, line_cross(down_mine), wait=(up_part,))
    def halves_of(vector, size):
        return pick(vector.reshape(-1, 2, size), core, 1).reshape(-1)

    query_part = halves_of(query_bias, HD).reshape(2, wide)
    value_part = halves_of(value_bias, HD).reshape(2, wide)
    in_bias = jnp.stack([query_part, jnp.zeros_like(query_part), value_part], axis=1).reshape(-1)
    down_part, facts = stack_line(facts, down_pairs, line_next(down_pairs))
    down_parts = gather_square(down_part, "x")
    (projected, in_weight, out_own), facts = project(
        facts, tokens_both, in_bias, near_parts, wait=(down_part, up_parts[2])
    )
    out_own = out_own.reshape(cols, width)
    out_other = swap(out_own, "c")
    (heads_out, totals), facts = attend(facts, projected, slots)
    heads_other = swap(heads_out[slots:], "c")
    vectors = jnp.stack(
        [out_bias, attn_gain, attn_shift, down_bias, feed_gain, feed_shift, out_bias, out_bias]
    )
    (first_hat, first_rstd, hidden_low, first_sums), facts = attend_out(
        facts,
        heads_out,
        heads_other,
        out_own,
        out_other,
        tokens_own,
        vectors,
        wait=(up_parts[1], down_parts[2]),
    )
    tokens_t, facts = turn_all(facts, tokens_both, wait=(hidden_low,))
    (hidden_low,), facts = gate(facts, (hidden_low,), (up_parts[3], down_parts[1]))
    hidden_from = swap(hidden_low, "c")
    (activation, slope, act_t, up_all), facts = feed_up(
        facts, hidden_low, hidden_from, halves_of(up_bias, unit_block), up_parts
    )
    hidden_turned, facts = turn(facts, hidden_low, hidden_from, rows, wait=(act_t,))
    (down_all, feed_sent), facts = feed_down(facts, activation, down_parts)
    down_all = down_all.reshape(units, width)
    feed_other = swap(feed_sent, "c")
    feed_part = product(activation[:slots], down_all, 1, 0)
    feed_vectors = jnp.stack(
        [down_bias, attn_gain, attn_shift, feed_gain, feed_shift, out_bias, out_bias, out_bias]
    )
    (mixed, second_grad, feed_low, second_sums), facts = second_norm(
        facts, feed_part, feed_other, first_hat, cotangent_own, feed_vectors
    )

    feed_both = both(feed_low, "c")
    feed_mine, feed_theirs = columns_of(feed_both, half), columns_of(feed_both, 1 - half)
    down_sent = grad_block(act_t, feed_theirs)
    down_got = swap(down_sent, "s")
    (pre_grad, up_bias_grad), facts = act_grad(
        facts, feed_both, down_all, slope, wait=(down_sent,)
    )
    hidden_sent = product(pre_grad[slots:], up_all, 1, 1).astype(jnp.bfloat16)
    hidden_other = swap(hidden_sent, "c")
    hidden_own_t, hidden_other_t = hidden_turned
    up_sent = grad_block(hidden_other_t, pre_grad)
    up_got = swap(up_sent, "x")
    hidden_part = product(pre_grad[:slots], up_all, 1, 1)
    (first_grad, attn_low, third_sums), facts = first_norm(
        facts,
        hidden_part,
        hidden_other,
        second_grad,
        first_hat,
        first_rstd,
        vectors,
        wait=(up_sent,),
    )
    grad_sent = product(attn_low, out_other, 1, 1).astype(jnp.bfloat16)
    grad_other = swap(grad_sent, "c")
    grad_own = product(attn_low, out_own, 1, 1).astype(jnp.bfloat16)
    out_sent = product(heads_other, attn_low, 0, 0).astype(jnp.bfloat16)
    out_got = swap(out_sent, "c")
    heads_grad = jnp.concatenate([grad_own, grad_other], axis=0)
    (theirs_low, theirs_sums), facts = attend_back(
        facts, projected, heads_grad, totals, slots, False, wait=(out_sent,)
    )
    in_sent = grad_block(tokens_t, theirs_low)
    in_got = swap(in_sent, "s")
    down_total = grad_block(act_t, feed_mine, down_got)
    down_kept, down_sent = halve(down_total.reshape(4, 2, unit_block, cols), "x", 1)
    down_got = swap(down_sent, "x")
    out_grad = grad_block(heads_out[:slots].T, attn_low, out_got)
    out_line = out_grad.reshape((4, 2 * out_weight.shape[0], width))
    out_kept, out_sent = line_parts(out_line)
    out_got = lax.ppermute(out_sent, "z", NEXT)
    (mine_low, mine_sums), facts = attend_back(
        facts, projected, heads_grad, totals, slots, True, wait=(in_sent, out_sent, down_sent)
    )
    up_total = grad_block(hidden_own_t, pre_grad, up_got).reshape(4, rows, 2 * up_cols)
    up_kept, up_sent = columns_of(up_total, half), columns_of(up_total, 1 - half)
    up_got = swap(up_sent, "s")
    out_total = add(out_kept, out_got)
    valid_count = length_own[0].astype(jnp.float32) * width
    stats = jnp.stack(
        [jnp.sum(first_sums[0]), jnp.sum(first_sums[1]), jnp.sum(second_sums[3]), valid_count]
    )
    mine_sums, theirs_sums = jnp.sum(mine_sums, axis=(0, 1)), jnp.sum(theirs_sums, axis=(0, 1))
    late = in_order(mine_sums, theirs_sums, half)
    sums = jnp.concatenate(
        [
            second_sums[:3].reshape(-1),
            third_sums[:3].reshape(-1),
            jnp.pad(stats, (0, 124)),
            up_bias_grad[0],
            late[:, :wide].reshape(-1),
            late[:, 2 * wide :].reshape(-1),
        ]
    )
    sums = sums + lax.ppermute(sums, "z", NEXT)
    (tokens_part, tokens_sent), facts = tokens_grad(
        facts,
        mine_low,
        theirs_low,
        in_weight,
        wait=(up_sent, out_total, sums),
    )
    in_total = grad_block(tokens_t, mine_low, in_got)
    in_kept, in_sent = halve(in_total.reshape(4, 2, rows, 3 * wide), "x", 1)
    in_got = swap(in_sent, "x")
    tokens_other = swap(tokens_sent, "c")
    (down_pairs, down_next), facts = add_parts(
        facts, down_kept, down_got, wait=(in_sent, tokens_part)
    )
    down_got = lax.ppermute(down_next, "z", NEXT)
    upper = lax.axis_index("z") // 2
    out_kept, out_sent = pick(out_total, upper, 0), pick(out_total, 1 - upper, 0)
    out_kept = add(out_kept, lax.ppermute(out_sent, "z", CROSS))
    (in_pairs, in_next), facts = add_parts(
        facts, in_kept, in_got, wait=(down_next, out_kept)
    )
    in_got = lax.ppermute(in_next, "z", NEXT)
    (down_kept, down_sent), facts = add_last(facts, down_pairs, down_got, wait=(in_next,))
    (up_pairs, up_next), facts = add_parts(facts, up_kept, up_got, wait=(down_sent,))
    up_got = lax.ppermute(up_next, "z", NEXT)
    (in_kept, in_sent, out_kept, sums), facts = add_last(
        facts, in_pairs, in_got, wait=(up_next,), through=(out_kept, sums)
    )
    sums = sums + swap(sums, "x")
    sums = sums + swap(sums, "s")
    (up_kept, up_sent, sums, mixed), facts = add_last(
        facts, up_pairs, up_got, wait=(in_sent,), through=(sums, mixed)
    )
    in_sum = add(in_kept, lax.ppermute(in_sent, "z", CROSS))
    tokens_grad_sum = tokens_part + tokens_other.astype(jnp.float32) + first_grad
    tokens_grad_sum = from_sequence(tokens_grad_sum.astype(jnp.bfloat16))
    mixed = in_order(mixed[:row_count], swap(mixed[row_count:], "s"), half)
    down_sum = add(down_kept, lax.ppermute(down_sent, "z", CROSS))
    up_sum = add(up_kept, lax.ppermute(up_sent, "z", CROSS))
    out_sum = fold_columns(fold(out_kept.reshape(2, out_weight.shape[0], width), "x", 0))

    sums = sums + lax.ppermute(sums, "z", CROSS)
    both_sums = in_order(sums, swap(sums, "c"), core)
    count = 6 * width + 128
    shared = both_sums[0, :count] + both_sums[1, :count]
    down_bias_grad, feed_gain_grad, feed_shift_grad, out_bias_grad, attn_gain_grad, attn_shift_grad = [
        shared[i * width : (i + 1) * width] for i in range(6)
    ]
    stats = shared[6 * width : 6 * width + 4]

    def interleave(start, size, block_size):
        sums = both_sums[:, start : start + size].reshape(2, -1, block_size)
        return sums.transpose(1, 0, 2).reshape(-1)

    up_bias_grad = interleave(count, units, unit_block)
    query_bias_grad = interleave(count + units, cols, HD)
    value_bias_gradient = interleave(count + units + cols, cols, HD)
    stream_rms = jnp.sqrt(stats[:3] / stats[3])

    def give_back(total):
        total = total.reshape((2, rows // 2) + total.shape[1:])
        return pick(total, core, 0), swap(pick(total, 1 - core, 0), "c")

    up_shares = give_back(up_sum)
    in_shares = give_back(in_sum)
    down_weight_grad = down_sum.astype(jnp.float32)
    out_weight_grad = out_sum.astype(jnp.float32)

    def merge(shares, start, size, block):
        one, two = [
            share[:, start : start + size].reshape(rows // 2, -1, block) for share in shares
        ]
        first = jnp.where(core == 0, one, two)
        second = jnp.where(core == 0, two, one)
        return jnp.stack([first, second], axis=2).reshape(rows // 2, -1).astype(jnp.float32)

    query_weight_grad = merge(in_shares, 0, wide, HD)
    key_weight_grad = merge(in_shares, wide, wide, HD)
    value_weight_grad = merge(in_shares, 2 * wide, wide, HD)
    up_weight_grad = merge(up_shares, 0, up_cols, unit_block)
    return (
        mixed,
        tokens_grad_sum,
        query_weight_grad,
        key_weight_grad,
        value_weight_grad,
        out_weight_grad,
        up_weight_grad,
        down_weight_grad,
        query_bias_grad,
        value_bias_gradient,
        out_bias_grad,
        attn_gain_grad,
        attn_shift_grad,
        up_bias_grad,
        down_bias_grad,
        feed_gain_grad,
        feed_shift_grad,
        stream_rms,
    )


def solution(mesh):
    devices = mesh.devices
    dp_count, seq_count = devices.shape
    split = seq_count == 2 and dp_count == 16
    if split:
        inner = jax.sharding.Mesh(devices.reshape(4, 2, 2, seq_count), ("z", "x", "c", "s"))
        dp, seq, body = ("z", "x", "c"), "s", split_body
    else:
        inner, dp, seq, body = mesh, "dp", "seq", general_body
    weights = (P(dp, seq),) * 6
    vectors = (P(),) * 9
    rows = P(dp, seq, None)
    in_specs = (rows, P(dp), rows) + weights + vectors
    out_specs = (rows, rows) + weights + vectors + (P(),)
    return jax.shard_map(body, mesh=inner, in_specs=in_specs, out_specs=out_specs, check_vma=False)
```
